32 devices in a mesh: dp: 16 (over z, x, core), mp: 2 (over y).
Axes of the slice: x: 2, y: 2, z: 4, core: 2. Of those that a mesh axis runs over, the one named last changes fastest.
Arguments:
- tokens: bfloat16 [16384, 768], P('dp'), may hold values from -6 to 6
- mix_blend: float32 [16], P('dp'), may hold values from 0.2 to 0.8
- partner: int32 [16], replicated, may hold values from 0 to 15, as said below
- clip_ids: int32 [16, 1024], P('dp'), may hold values from 0 to 7, never falling along the last dimension, each value on 1 to 256 neighbouring positions
- gain_one: float32 [768], replicated, may hold values from 0.1 to 1.9
- shift_one: float32 [768], replicated, may hold values from -3 to 3
- qkv_weight: bfloat16 [768, 3, 768], P(None, None, 'mp'), may hold values from -0.21875 to 0.21875
- qv_bias: float32 [2, 768], P(None, 'mp'), may hold values from -3 to 3
- proj_weight: bfloat16 [768, 768], P('mp'), may hold values from -1.75 to 1.75
- proj_bias: float32 [768], replicated, may hold values from -3 to 3
- gain_two: float32 [768], replicated, may hold values from 0.1 to 1.9
- shift_two: float32 [768], replicated, may hold values from -3 to 3
- in_weight: bfloat16 [768, 3072], P(None, 'mp'), may hold values from -0.21875 to 0.21875
- in_bias: float32 [3072], P('mp'), may hold values from -3 to 3
- out_weight: bfloat16 [3072, 768], P('mp'), may hold values from -0.109375 to 0.109375
- out_bias: float32 [768], replicated, may hold values from -3 to 3
- cotangent: bfloat16 [16384, 768], P('dp'), may hold values from -6 to 6
Outputs:
- block_out: bfloat16 [16384, 768], P('dp')
- grad_tokens: bfloat16 [16384, 768], P('dp')
- grad_gain_one: float32 [768], P('dp')
- grad_shift_one: float32 [768], P('dp')
- grad_qkv_weight: float32 [768, 3, 768], P('dp', None, 'mp')
- grad_qv_bias: float32 [2, 768], P(None, ('mp', 'dp'))
- grad_proj_weight: float32 [768, 768], P('mp', 'dp')
- grad_proj_bias: float32 [768], P('dp')
- grad_gain_two: float32 [768], P('dp')
- grad_shift_two: float32 [768], P('dp')
- grad_in_weight: float32 [768, 3072], P('dp', 'mp')
- grad_in_bias: float32 [3072], P(('mp', 'dp'))
- grad_out_weight: float32 [3072, 768], P('mp', 'dp')
- grad_out_bias: float32 [768], P('dp')
The draws below stay inside these ranges and needn't reach their ends.
Inputs may be any that keep to these rules, and one draw needn't show every extreme that they name: partner is a permutation of the 16 sequences in which no sequence is its own partner. `clip_ids`: within a sequence the clip ids never fall; a clip holds at most 256 tokens.
All inputs are finite; a program needn't handle non-finite values.
Results may differ from the reference program's by a relative error of at most 0.017.
Values may be sent and summed in bfloat16 or wider, within the bound.
No kernel may reach another device: no remote copies, remote signals or barrier semaphores. Data moves between devices by JAX's collectives and lax.ppermute only.
A program may use at most 192 MiB of HBM per device.

```python
import math
import jax
import jax.numpy as jnp
import numpy as np
from jax import lax

D = 768
HEADS = 12
HEAD_DIM = 64
FF = 3072
SEQLEN = 1024
CLIPS = 8
SEQS = 16
TOKENS = 16384


def draw_partner(key, part):
    key = jax.random.fold_in(key, 11)
    order = jax.random.permutation(key, SEQS).astype(jnp.int32)
    return jnp.zeros((SEQS,), jnp.int32).at[order].set(jnp.roll(order, -1))


def strengthened(drawn, own_key, source, target, blocks, factor):
    def block_of(dim):
        return (jnp.arange(drawn.shape[dim]) // (drawn.shape[dim] // blocks)).reshape((-1,) + (1,) * (drawn.ndim - 1 - dim))

    near = jax.random.permutation(own_key, blocks)[block_of(target)]
    far = (block_of(target) + blocks // 2) % blocks
    return jnp.where((block_of(source) == near) | (block_of(source) == far), factor * drawn, drawn)


def block_scale(key, extent, pieces, smallest, largest):
    gain = 1.0
    for position, parts in pieces:
        steps = jax.random.uniform(jax.random.fold_in(jax.random.fold_in(key, 6), position), (parts,), jnp.float32, smallest / len(pieces), largest / len(pieces))
        gain = gain * jnp.repeat(jnp.exp(steps), extent[position] // parts).reshape((-1,) + (1,) * (len(extent) - 1 - position))
    return gain


def profile(amount, total, most, lean):
    loads = [(1 << 20) // math.isqrt(rank ** lean) + 1 for rank in range(2, amount + 1)]
    rest, counts = total - most - (amount - 1), [1] * (amount - 1)
    while rest > 0:
        movable = [i for i in range(amount - 1) if counts[i] < most]
        mass, remaining = sum([loads[i] for i in movable]), rest
        for i in movable:
            more = min(most - counts[i], max(1, remaining * loads[i] // mass), rest)
            counts[i] = counts[i] + more
            rest = rest - more
    return np.array([most] + counts)


def uneven(stream_key, number_of, total, reach, slope):
    if number_of == 2:
        one = jax.random.randint(stream_key, (), max(1, total - reach), min(reach, total - 1) + 1)
        return jnp.stack([one, total - one])
    sizes = jnp.asarray(profile(number_of, total, reach, slope), jnp.int32)
    pairs = (number_of - 1) // 2
    source_of, sink = sizes[1:1 + 2 * pairs:2], sizes[2:2 + 2 * pairs:2]
    room = jnp.minimum(source_of - 1, reach - sink)
    shifted = jax.random.randint(jax.random.fold_in(stream_key, 1), (pairs,), 0, 1 << 20) % (room + 1)
    sizes = sizes.at[1:1 + 2 * pairs:2].set(source_of - shifted).at[2:2 + 2 * pairs:2].set(sink + shifted)
    return sizes[jax.random.permutation(jax.random.fold_in(stream_key, 2), number_of)]


def noise(own_key, dims, width, most, split=(), held_as=jnp.bfloat16):
    values = jax.random.normal(own_key, dims, jnp.float32) * width
    if len(split) > 0:
        values = block_scale(own_key, dims, split, -0.22, 0.18) * values
    return jnp.clip(values, min=-most, max=most).astype(held_as)


def heavy_noise(rng, dims, scale, most, cuts, heavy, kind=jnp.bfloat16):
    entries = scale * jax.random.normal(rng, dims, jnp.float32)
    if cuts:
        entries = entries * block_scale(rng, dims, cuts, -0.22, 0.18)
    return jnp.clip(strengthened(entries, jax.random.fold_in(rng, 3), *heavy), -most, most).astype(kind)


def setup_inputs(seed: int = 0) -> dict:
    seeds = jax.random.split(jax.random.key(seed), 18)
    return {
        "tokens": heavy_noise(seeds[0], (TOKENS, D), 1.0, 6.0, ((0, 16),), (0, 1, 16, 2.0)),
        "mix_blend": jnp.clip(0.2 + 0.6 * jax.random.uniform(seeds[1], (SEQS,), jnp.float32) ** block_scale(seeds[1], (SEQS,), ((0, 16),), -0.2, 0.2), 0.2, 0.8),
        "partner": draw_partner(jax.random.fold_in(seeds[17], 71), 0),
        "clip_ids": jax.vmap(lambda own: jnp.searchsorted(jnp.cumsum(uneven(own, CLIPS, SEQLEN, SEQLEN // 4, 1)), jnp.arange(SEQLEN), side="right"))(jax.random.split(seeds[3], SEQS)).reshape((SEQS, SEQLEN)).astype(jnp.int32),
        "gain_one": jnp.clip(1.0 + 0.18 * jax.random.normal(seeds[4], (D,), jnp.float32), 0.1, 1.9),
        "shift_one": noise(seeds[5], (D,), 0.5, 3.0, (), jnp.float32),
        "qkv_weight": noise(seeds[6], (D, 3, HEADS * HEAD_DIM), D ** -0.5, 0.21875, ((2, 2),)),
        "qv_bias": noise(seeds[7], (2, HEADS * HEAD_DIM), 0.5, 3.0, ((1, 2),), jnp.float32),
        "proj_weight": noise(seeds[8], (HEADS * HEAD_DIM, D), (D // 64) ** -0.5, 1.75, ((0, 2),)),
        "proj_bias": noise(seeds[9], (D,), 0.5, 3.0, (), jnp.float32),
        "gain_two": jnp.clip(1.0 + 0.18 * jax.random.normal(seeds[10], (D,), jnp.float32), 0.1, 1.9),
        "shift_two": noise(seeds[11], (D,), 0.5, 3.0, (), jnp.float32),
        "in_weight": noise(seeds[12], (D, FF), D ** -0.5, 0.21875, ((1, 2),)),
        "in_bias": noise(seeds[13], (FF,), 0.5, 3.0, ((0, 2),), jnp.float32),
        "out_weight": noise(seeds[14], (FF, D), FF ** -0.5, 0.109375, ((0, 2),)),
        "out_bias": noise(seeds[15], (D,), 0.5, 3.0, (), jnp.float32),
        "cotangent": heavy_noise(seeds[16], (TOKENS, D), 1.0, 6.0, ((0, 16),), (0, 1, 16, 2.0)),
    }


@jax.custom_vjp
def low(v):
    return lax.optimization_barrier(v.astype(jnp.bfloat16)).astype(jnp.float32)

@jax.custom_vjp
def low_back(v):
    return v

def low_keep(v):
    return (low(v), None)

def low_pass(kept, grad):
    return (grad,)

def back_keep(v):
    return (v, None)

def back_low(kept, grad):
    return (low(grad),)
low.defvjp(low_keep, low_pass)
low_back.defvjp(back_keep, back_low)
NORM_EPS = 1e-06
NEG_FILL = -1e+30
HIGH_PREC = lax.Precision.HIGHEST

def layer_norm(vector, gain_vec, shift_vec):
    centred = vector - lax.optimization_barrier(jnp.mean(vector, axis=-1, keepdims=True))
    spread = lax.optimization_barrier(jnp.mean(centred * centred, axis=-1, keepdims=True))
    return centred * lax.rsqrt(spread + NORM_EPS) * gain_vec + shift_vec

def gelu_exact(vector):
    return jax.nn.gelu(vector, approximate=False)

def encode_one(mixed_rows, segment, params):
    gain_one, shift_one, qkv_weight, qv_bias, proj_weight, proj_bias, gain_two, shift_two, in_weight, in_bias, out_weight, out_bias = params
    seq_rows = mixed_rows.shape[0]
    full_width = qkv_weight.shape[2]
    num_heads = full_width // HEAD_DIM
    normed_one = low(layer_norm(mixed_rows, gain_one, shift_one))
    projected = low_back(jnp.dot(normed_one, qkv_weight.reshape(D, 3 * full_width), precision=HIGH_PREC))
    projected = projected.reshape(seq_rows, 3, full_width)
    queries = low(projected[:, 0] + qv_bias[0]).reshape(seq_rows, num_heads, HEAD_DIM)
    key_vecs = low(projected[:, 1]).reshape(seq_rows, num_heads, HEAD_DIM)
    value_vecs = low(projected[:, 2] + qv_bias[1]).reshape(seq_rows, num_heads, HEAD_DIM)
    raw_scores = jnp.einsum('qhd,khd->hqk', queries, key_vecs, precision=HIGH_PREC)
    scores = low_back(raw_scores) * HEAD_DIM ** (-0.5)
    allowed = (segment[:, None] == segment[None, :])[None]
    scores = jnp.where(allowed, scores, NEG_FILL)
    row_max = lax.optimization_barrier(jnp.max(scores, axis=-1, keepdims=True))
    exp_scores = jnp.exp(scores - row_max)
    probs = low(exp_scores / lax.optimization_barrier(jnp.sum(exp_scores, axis=-1, keepdims=True)))
    attended = jnp.einsum('hqk,khd->qhd', probs, value_vecs, precision=HIGH_PREC).reshape(seq_rows, full_width)
    attended = low(low_back(attended))
    hidden = mixed_rows + low_back(jnp.dot(attended, proj_weight, precision=HIGH_PREC)) + proj_bias
    normed_two = low(layer_norm(hidden, gain_two, shift_two))
    pre_act = low_back(jnp.dot(normed_two, in_weight, precision=HIGH_PREC)) + in_bias
    activated = low(gelu_exact(pre_act))
    return hidden + low_back(jnp.dot(activated, out_weight, precision=HIGH_PREC)) + out_bias

def reference(tokens, mix_blend, partner, clip_ids, gain_one, shift_one, qkv_weight, qv_bias, proj_weight, proj_bias, gain_two, shift_two, in_weight, in_bias, out_weight, out_bias, cotangent):
    params = (gain_one, shift_one, qkv_weight.astype(jnp.float32), qv_bias, proj_weight.astype(jnp.float32), proj_bias, gain_two, shift_two, in_weight.astype(jnp.float32), in_bias, out_weight.astype(jnp.float32), out_bias)
    source = tokens.astype(jnp.float32)
    encode = jax.checkpoint(encode_one)

    def forward(source_rows, weights_all):
        sequences = source_rows.reshape(SEQS, SEQLEN, D)
        blend_col = mix_blend[:, None, None]
        mixed_all = blend_col * sequences + (1.0 - blend_col) * sequences[partner]

        def scan_step(carried, sliced):
            return (carried, encode(sliced[0], sliced[1], weights_all))
        _, encoded = lax.scan(scan_step, jnp.int32(0), (mixed_all, clip_ids))
        return encoded.reshape(TOKENS, D)
    block_out, pullback = jax.vjp(forward, source, params)
    grad_source, grads = pullback(cotangent.astype(jnp.float32))
    grad_gain_one, grad_shift_one, grad_qkv_weight, grad_qv_bias, grad_proj_weight, grad_proj_bias, grad_gain_two, grad_shift_two, grad_in_weight, grad_in_bias, grad_out_weight, grad_out_bias = grads
    return (block_out.astype(jnp.bfloat16), grad_source.astype(jnp.bfloat16), grad_gain_one, grad_shift_one, grad_qkv_weight, grad_qv_bias, grad_proj_weight, grad_proj_bias, grad_gain_two, grad_shift_two, grad_in_weight, grad_in_bias, grad_out_weight, grad_out_bias)
```

```python
import functools

import jax
import jax.numpy as jnp
from jax import lax
from jax.experimental import pallas as pl
from jax.experimental.pallas import tpu as pltpu
from jax.sharding import PartitionSpec as P

HEAD_DIM = 64
NORM_EPS = 1e-06
NEG_FILL = -1e30
SCORE_SCALE = HEAD_DIM ** (-0.5)
MAX_CLIP = 256
LANES = 128
F32 = jnp.float32
BF16 = jnp.bfloat16
MIB = 1 << 20


def nn(left, right):
    return lax.dot_general(left, right, (((1,), (0,)), ((), ())), preferred_element_type=F32)


def nt(left, right):
    return lax.dot_general(left, right, (((1,), (1,)), ((), ())), preferred_element_type=F32)


def vmem():
    return pl.BlockSpec(memory_space=pltpu.VMEM)


def smem():
    return pl.BlockSpec(memory_space=pltpu.SMEM)


def params(mib):
    return pltpu.CompilerParams(vmem_limit_bytes=mib * MIB)


def shape(dims, dtype):
    return jax.ShapeDtypeStruct(dims, dtype)


def row_stats(vector):
    mean = jnp.mean(vector, axis=-1, keepdims=True)
    centred = vector - mean
    spread = jnp.mean(centred * centred, axis=-1, keepdims=True)
    return centred, lax.rsqrt(spread + NORM_EPS)


def fold_rows(block):
    rows, width = block.shape
    return jnp.sum(block.reshape(rows // 8, 8, width), axis=0)


def pick_kernel(count, partner, source, picked, sems):
    def start(i, carry):
        pltpu.make_async_copy(source.at[partner[i]], picked.at[i], sems.at[i]).start()
        return carry

    def finish(i, carry):
        pltpu.make_async_copy(source.at[partner[i]], picked.at[i], sems.at[i]).wait()
        return carry

    lax.fori_loop(0, count, start, 0)
    lax.fori_loop(0, count, finish, 0)


def pick(source, partner):
    count = partner.shape[0]
    return pl.pallas_call(
        functools.partial(pick_kernel, count),
        out_shape=shape(source.shape, source.dtype),
        in_specs=[smem(), pl.BlockSpec(memory_space=pl.ANY)],
        out_specs=pl.BlockSpec(memory_space=pl.ANY),
        scratch_shapes=[pltpu.SemaphoreType.DMA((count,))],
        name="pick",
    )(partner, source)


def attention_kernel(
    blend, halves, tok, own, oth, seg_row, seg_col, gain, shift, w3, bq, bv, wp,
    mixed, n1, q, k, v, att, lse, part,
    vt, att_t, seg_b, bias,
):
    rows, width = tok.shape
    local = wp.shape[0]
    half_rows = rows // 2
    ratio = blend[0]
    blk = 64

    for src, half in ((own, halves[0]), (oth, halves[1])):

        def mix(i, carry, src=src, half=half):
            here = pl.ds(pl.multiple_of(half * half_rows + i * blk, blk), blk)
            there = pl.ds(pl.multiple_of(i * blk, blk), blk)
            blended = ratio * tok[here, :].astype(F32) + (1.0 - ratio) * src[there, :].astype(F32)
            mixed[here, :] = blended
            centred, inv = row_stats(blended)
            n1[here, :] = (centred * inv * gain[...] + shift[...]).astype(BF16)
            seg_b[here, :] = jnp.broadcast_to(seg_col[here, :], (blk, LANES))
            return carry

        lax.fori_loop(0, half_rows // blk, mix, 0)

    big = 256
    for i in range(rows // big):
        here = pl.ds(i * big, big)
        normed = n1[here, :]
        queries = (nn(normed, w3[0]) + bq[...]).astype(BF16).astype(F32)
        q[here, :] = (queries * SCORE_SCALE).astype(BF16)
        k[here, :] = nn(normed, w3[1]).astype(BF16)
        values = (nn(normed, w3[2]) + bv[...]).astype(BF16)
        v[here, :] = values
        vt[:, here] = values.T

    window = min(rows, LANES + 2 * MAX_CLIP)
    lane = lax.broadcasted_iota(jnp.int32, (LANES, LANES), 1)
    sides = [(lane // HEAD_DIM == e).astype(BF16) for e in range(2)]

    def attend(j, carry):
        here = pl.ds(pl.multiple_of(j * LANES, LANES), LANES)
        first = pl.multiple_of(jnp.clip(j * LANES - MAX_CLIP, 0, rows - window), LANES)
        keys = pl.ds(first, window)
        bias[...] = jnp.where(seg_b[keys, :] == seg_row[:, here], 0.0, NEG_FILL)
        for h in range(local // HEAD_DIM):
            pair = pl.ds((h // 2) * LANES, LANES)
            query = q[here, pair] * sides[h % 2]
            scores = nt(k[keys, pair], query) + bias[...]
            top = jnp.max(scores, axis=0, keepdims=True)
            grown = jnp.exp(scores - top)
            total = jnp.sum(grown, axis=0, keepdims=True)
            head = pl.ds(h * HEAD_DIM, HEAD_DIM)
            out = nn(vt[head, keys], grown.astype(BF16)) / total
            att_t[head, here] = out.astype(BF16)
            lse[pl.ds(h, 1), here] = top + jnp.log(total)
        return carry

    lax.fori_loop(0, rows // LANES, attend, 0)

    for i in range(rows // big):
        here = pl.ds(i * big, big)
        block = att_t[:, here].T
        att[here, :] = block
        part[here, :] = nn(block, wp[...]).astype(BF16)


def attention(blend, halves, tok, own, oth, segment, gain, shift, w3, bq, bv, wp):
    rows, width = tok.shape
    local = wp.shape[0]
    heads = local // HEAD_DIM
    window = min(rows, LANES + 2 * MAX_CLIP)
    return pl.pallas_call(
        attention_kernel,
        out_shape=(
            shape((rows, width), F32),
            shape((rows, width), BF16),
            shape((rows, local), BF16),
            shape((rows, local), BF16),
            shape((rows, local), BF16),
            shape((rows, local), BF16),
            shape((heads, rows), F32),
            shape((rows, width), BF16),
        ),
        in_specs=[smem(), smem()] + [vmem()] * 11,
        out_specs=[vmem()] * 8,
        scratch_shapes=[
            pltpu.VMEM((local, rows), BF16),
            pltpu.VMEM((local, rows), BF16),
            pltpu.VMEM((rows, LANES), jnp.int32),
            pltpu.VMEM((window, LANES), F32),
        ],
        compiler_params=params(48),
        cost_estimate=pl.CostEstimate(
            flops=2 * rows * width * local * 4 + 4 * rows * window * local * 4,
            bytes_accessed=24 * MIB,
            transcendentals=rows * window * heads,
        ),
        name="attention",
    )(
        blend, halves, tok, own, oth, segment[None, :], segment[:, None],
        gain[None, :], shift[None, :], w3, bq[None, :], bv[None, :], wp,
    )


def feed_kernel(
    mixed, p_own, p_oth, pb, gain, shift, cot, w_in, b_in, w_out,
    hidden, n2, act, gp, part, gn_part, g_bin, g_bout,
    acc_o, acc_g,
):
    step = pl.program_id(0)
    rows, width = mixed.shape
    units = w_in.shape[1]

    @pl.when(step == 0)
    def _():
        blk = 64
        g_bout[...] = jnp.zeros_like(g_bout)

        def norm(i, carry):
            here = pl.ds(pl.multiple_of(i * blk, blk), blk)
            attn = p_own[here, :].astype(F32) + p_oth[here, :].astype(F32)
            total = mixed[here, :] + attn + pb[...]
            hidden[here, :] = total
            centred, inv = row_stats(total)
            n2[here, :] = (centred * inv * gain[...] + shift[...]).astype(BF16)
            g_bout[...] += fold_rows(cot[here, :].astype(F32))
            return carry

        lax.fori_loop(0, rows // blk, norm, 0)
        acc_o[...] = jnp.zeros_like(acc_o)
        acc_g[...] = jnp.zeros_like(acc_g)

    big = 256
    sub = 32
    sums = jnp.zeros((8, units), F32)
    for i in range(rows // big):
        here = pl.ds(i * big, big)
        pre_all = nn(n2[here, :], w_in[...])
        grad_all = nt(cot[here, :], w_out[...])
        for s in range(big // sub):
            rng = slice(s * sub, s * sub + sub)
            pre = pre_all[rng] + b_in[...]
            cdf = 0.5 * (1.0 + lax.erf(pre * (0.5**0.5)))
            pdf = jnp.exp(-0.5 * pre * pre) * 0.3989422804014327
            grad = grad_all[rng] * (cdf + pre * pdf)
            sums += fold_rows(grad)
            spot = pl.ds(i * big + s * sub, sub)
            act[spot, :] = (pre * cdf).astype(BF16)
            gp[spot, :] = grad.astype(BF16)
        acc_o[here, :] += nn(act[here, :], w_out[...])
        acc_g[here, :] += nt(gp[here, :], w_in[...])
    g_bin[...] = sums

    @pl.when(step == pl.num_programs(0) - 1)
    def _():
        part[...] = acc_o[...].astype(BF16)
        gn_part[...] = acc_g[...].astype(BF16)


def feed(mixed, p_own, p_oth, pb, gain, shift, cot, w_in, b_in, w_out):
    rows, width = mixed.shape
    units = w_in.shape[1]
    chunk = 256

    def whole(dims):
        return pl.BlockSpec(dims, lambda j: (0, 0), pipeline_mode=pl.Buffered(1))

    def columns(lines):
        return pl.BlockSpec((lines, chunk), lambda j: (0, j))

    tall = whole((rows, width))
    flat = whole((1, width))
    return pl.pallas_call(
        feed_kernel,
        grid=(units // chunk,),
        out_shape=(
            shape((rows, width), F32),
            shape((rows, width), BF16),
            shape((rows, units), BF16),
            shape((rows, units), BF16),
            shape((rows, width), BF16),
            shape((rows, width), BF16),
            shape((8, units), F32),
            shape((8, width), F32),
        ),
        in_specs=[
            tall, tall, tall, flat, flat, flat, tall,
            columns(width), columns(1), pl.BlockSpec((chunk, width), lambda j: (j, 0)),
        ],
        out_specs=[
            tall, tall, columns(rows), columns(rows), tall, tall, columns(8), whole((8, width)),
        ],
        scratch_shapes=[pltpu.VMEM((rows, width), F32), pltpu.VMEM((rows, width), F32)],
        compiler_params=params(48),
        cost_estimate=pl.CostEstimate(
            flops=2 * rows * width * units * 4,
            bytes_accessed=24 * MIB,
            transcendentals=2 * rows * units,
        ),
        name="feed",
    )(
        mixed, p_own, p_oth, pb[None, :], gain[None, :], shift[None, :], cot,
        w_in, b_in[None, :], w_out,
    )


def transpose_into(target, source):
    rows = source.shape[0]
    big = 256
    for i in range(rows // big):
        here = pl.ds(i * big, big)
        target[:, here] = source[here, :].T


def outer_kernel(firsts, *refs):
    count = len(firsts)
    lefts, rights = refs[:count], refs[count : 2 * count]
    out, turned = refs[2 * count], refs[2 * count + 1]
    step = pl.program_id(0)
    big = 256
    for n, first in enumerate(firsts):

        @pl.when(step == first)
        def _(n=n):
            transpose_into(turned, lefts[n])

        last = firsts[n + 1] if n + 1 < count else 1 << 20

        @pl.when((step >= first) & (step < last))
        def _(n=n):
            for i in range(out.shape[0] // big):
                here = pl.ds(i * big, big)
                out[here, :] = nn(turned[here, :], rights[n][...]).astype(BF16)


def outer(*pairs):
    chunk = 384
    rows, width = pairs[0][0].shape
    steps = [right.shape[1] // chunk for _, right in pairs]
    firsts = [sum(steps[:n]) for n in range(len(steps))]
    total = sum(steps)

    def right_spec(first, count):
        return pl.BlockSpec(
            (rows, chunk), lambda j: (0, jnp.clip(j - first, 0, count - 1))
        )

    left_spec = pl.BlockSpec((rows, width), lambda j: (0, 0), pipeline_mode=pl.Buffered(1))
    return pl.pallas_call(
        functools.partial(outer_kernel, firsts),
        grid=(total,),
        out_shape=shape((width, total * chunk), BF16),
        in_specs=[left_spec] * len(pairs)
        + [right_spec(first, count) for first, count in zip(firsts, steps)],
        out_specs=pl.BlockSpec((width, chunk), lambda j: (0, j)),
        scratch_shapes=[pltpu.VMEM((width, rows), BF16)],
        compiler_params=params(32),
        cost_estimate=pl.CostEstimate(
            flops=2 * rows * width * total * chunk,
            bytes_accessed=8 * MIB,
            transcendentals=0,
        ),
        name="outer",
    )(*[left for left, _ in pairs], *[right for _, right in pairs])


def attention_back_kernel(
    hidden, cot, g_own, g_oth, gain, seg_row, seg_col, wp, q, k, v, lse, w3,
    gh, gh_low, gproj, part, sums, g_qv,
    d_out, kt, dq_t, dk, dv, seg_b, bias,
):
    rows, width = hidden.shape
    local = wp.shape[0]
    blk = 64
    sums[...] = jnp.zeros_like(sums)

    def norm(i, carry):
        here = pl.ds(pl.multiple_of(i * blk, blk), blk)
        grad = g_own[here, :].astype(F32) + g_oth[here, :].astype(F32)
        centred, inv = row_stats(hidden[here, :])
        normed = centred * inv
        scaled = grad * gain[...]
        mean_one = jnp.mean(scaled, axis=-1, keepdims=True)
        mean_two = jnp.mean(scaled * normed, axis=-1, keepdims=True)
        back = cot[here, :].astype(F32) + inv * (scaled - mean_one - normed * mean_two)
        gh[here, :] = back
        gh_low[here, :] = back.astype(BF16)
        sums[0] += fold_rows(grad * normed)
        sums[1] += fold_rows(grad)
        sums[2] += fold_rows(back)
        seg_b[here, :] = jnp.broadcast_to(seg_col[here, :], (blk, LANES))
        return carry

    lax.fori_loop(0, rows // blk, norm, 0)

    big = 256
    for i in range(rows // big):
        here = pl.ds(i * big, big)
        d_out[here, :] = nt(gh_low[here, :], wp[...]).astype(BF16)
        kt[:, here] = k[here, :].T
    dk[...] = jnp.zeros_like(dk)
    dv[...] = jnp.zeros_like(dv)

    window = min(rows, LANES + 2 * MAX_CLIP)
    lane = lax.broadcasted_iota(jnp.int32, (LANES, LANES), 1)
    sides = [(lane // HEAD_DIM == e).astype(BF16) for e in range(2)]

    def attend(j, carry):
        here = pl.ds(pl.multiple_of(j * LANES, LANES), LANES)
        first = pl.multiple_of(jnp.clip(j * LANES - MAX_CLIP, 0, rows - window), LANES)
        keys = pl.ds(first, window)
        bias[...] = jnp.where(seg_b[keys, :] == seg_row[:, here], 0.0, NEG_FILL)
        for p in range(local // LANES):
            pair = pl.ds(p * LANES, LANES)
            key_block, value_block = k[keys, pair], v[keys, pair]
            probs_two, grads_two, queries_two, outs_two = [], [], [], []
            for e in range(2):
                h = 2 * p + e
                head = pl.ds(h * HEAD_DIM, HEAD_DIM)
                query = q[here, pair] * sides[e]
                grad_out = d_out[here, pair] * sides[e]
                scores = nt(key_block, query) + bias[...]
                probs = jnp.exp(scores - lse[pl.ds(h, 1), here])
                weighted = probs * nt(value_block, grad_out)
                inner = jnp.sum(weighted, axis=0, keepdims=True)
                grads = (weighted - probs * inner).astype(BF16)
                dq_t[head, here] = nn(kt[head, keys], grads) * SCORE_SCALE
                probs_two.append(probs.astype(BF16))
                grads_two.append(grads)
                queries_two.append(query)
                outs_two.append(grad_out)
            both = jnp.concatenate(grads_two, axis=1)
            dk[keys, pair] += nn(both, jnp.concatenate(queries_two, axis=0))
            both = jnp.concatenate(probs_two, axis=1)
            dv[keys, pair] += nn(both, jnp.concatenate(outs_two, axis=0))
        return carry

    lax.fori_loop(0, rows // LANES, attend, 0)

    q_sum = jnp.zeros((8, local), F32)
    v_sum = jnp.zeros((8, local), F32)
    for i in range(rows // big):
        here = pl.ds(i * big, big)
        grad_q, grad_k, grad_v = dq_t[:, here].T, dk[here, :], dv[here, :]
        q_sum += fold_rows(grad_q)
        v_sum += fold_rows(grad_v)
        low_q, low_k, low_v = grad_q.astype(BF16), grad_k.astype(BF16), grad_v.astype(BF16)
        gproj[here, pl.ds(0, local)] = low_q
        gproj[here, pl.ds(local, local)] = low_k
        gproj[here, pl.ds(2 * local, local)] = low_v
        part[here, :] = (nt(low_q, w3[0]) + nt(low_k, w3[1]) + nt(low_v, w3[2])).astype(BF16)
    g_qv[0] = q_sum
    g_qv[1] = v_sum


def attention_back(hidden, cot, g_own, g_oth, gain, segment, wp, q, k, v, lse, w3):
    rows, width = hidden.shape
    local = wp.shape[0]
    heads = local // HEAD_DIM
    window = min(rows, LANES + 2 * MAX_CLIP)
    return pl.pallas_call(
        attention_back_kernel,
        out_shape=(
            shape((rows, width), F32),
            shape((rows, width), BF16),
            shape((rows, 3 * local), BF16),
            shape((rows, width), BF16),
            shape((3, 8, width), F32),
            shape((2, 8, local), F32),
        ),
        in_specs=[vmem()] * 13,
        out_specs=[vmem()] * 6,
        scratch_shapes=[
            pltpu.VMEM((rows, local), BF16),
            pltpu.VMEM((local, rows), BF16),
            pltpu.VMEM((local, rows), F32),
            pltpu.VMEM((rows, local), F32),
            pltpu.VMEM((rows, local), F32),
            pltpu.VMEM((rows, LANES), jnp.int32),
            pltpu.VMEM((window, LANES), F32),
        ],
        compiler_params=params(48),
        cost_estimate=pl.CostEstimate(
            flops=2 * rows * width * local * 4 + 10 * rows * window * local * 4,
            bytes_accessed=24 * MIB,
            transcendentals=rows * window * heads,
        ),
        name="attention_back",
    )(
        hidden, cot, g_own, g_oth, gain[None, :], segment[None, :], segment[:, None],
        wp, q, k, v, lse, w3,
    )


def mixed_back_kernel(blend, mixed, gh, g_own, g_oth, gain, outgoing, kept, sums):
    ratio = blend[0]

    @pl.when(pl.program_id(0) == 0)
    def _():
        sums[...] = jnp.zeros_like(sums)

    blk = 64
    rows = mixed.shape[0]
    for i in range(rows // blk):
        here = pl.ds(i * blk, blk)
        grad = g_own[here, :].astype(F32) + g_oth[here, :].astype(F32)
        centred, inv = row_stats(mixed[here, :])
        normed = centred * inv
        scaled = grad * gain[...]
        mean_one = jnp.mean(scaled, axis=-1, keepdims=True)
        mean_two = jnp.mean(scaled * normed, axis=-1, keepdims=True)
        back = gh[here, :] + inv * (scaled - mean_one - normed * mean_two)
        outgoing[here, :] = ((1.0 - ratio) * back).astype(BF16)
        kept[here, :] = (ratio * back).astype(BF16)
        sums[0] += fold_rows(grad * normed)
        sums[1] += fold_rows(grad)


def mixed_back(blend, mixed, gh, g_own, g_oth, gain):
    rows, width = mixed.shape
    block = 128
    strip = pl.BlockSpec((block, width), lambda i: (i, 0))
    flat = pl.BlockSpec((1, width), lambda i: (0, 0))
    return pl.pallas_call(
        mixed_back_kernel,
        grid=(rows // block,),
        out_shape=(
            shape((rows, width), BF16),
            shape((rows, width), BF16),
            shape((2, 8, width), F32),
        ),
        in_specs=[smem(), strip, strip, strip, strip, flat],
        out_specs=[strip, strip, pl.BlockSpec((2, 8, width), lambda i: (0, 0, 0))],
        compiler_params=params(32),
        cost_estimate=pl.CostEstimate(
            flops=20 * rows * width, bytes_accessed=12 * MIB, transcendentals=0
        ),
        name="mixed_back",
    )(blend, mixed, gh, g_own, g_oth, gain[None, :])


def shards(
    tokens,
    mix_blend,
    partner,
    clip_ids,
    gain_one,
    shift_one,
    qkv_weight,
    qv_bias,
    proj_weight,
    proj_bias,
    gain_two,
    shift_two,
    in_weight,
    in_bias,
    out_weight,
    out_bias,
    cotangent,
):
    rows, width = tokens.shape
    dp_count = lax.axis_size("dp")
    both = ("dp", "mp")
    bits = dp_count.bit_length() - 1
    seq = lax.axis_index("dp")
    mp = lax.axis_index("mp")
    core = lax.rem(seq, 2)
    home = core == mp
    all_dp = range(dp_count)

    def joint(d, m):
        return 2 * d + m

    core_swap = [(d, d ^ 1) for d in all_dp]
    chip_share = [(joint(d, d & 1), joint(d ^ 1, d & 1)) for d in all_dp]
    home_to_pair = [(joint(d, d & 1), joint(d, 1 - (d & 1))) for d in all_dp]
    pair_to_home = [(joint(d, 1 - (d & 1)), joint(d, d & 1)) for d in all_dp]
    weight_move = home_to_pair + [
        (joint(d, 1 - (d & 1)), joint(d ^ 1, 1 - (d & 1))) for d in all_dp
    ]

    def swap(value):
        return lax.ppermute(value, "dp", core_swap)

    def chip_value(value):
        return jnp.where(home, value, lax.ppermute(value, both, chip_share))

    def half_weight(value):
        return lax.ppermute(value, both, weight_move)

    piece = rows // (2 * 2 * dp_count)
    sent = tokens.reshape(2, dp_count, 2, piece, width)
    sent = lax.dynamic_index_in_dim(sent, mp, 2, keepdims=False)
    spread = lax.all_to_all(sent.transpose(1, 0, 2, 3), "dp", 0, 0, tiled=True)
    chosen = pick(spread, partner).reshape(dp_count // 2, 2, 2, piece, width)
    partner_own = lax.all_to_all(
        chosen.transpose(0, 2, 1, 3, 4).reshape(2 * dp_count, piece, width),
        both,
        0,
        0,
        tiled=True,
    ).reshape(rows // 2, width)
    partner_oth = swap(partner_own)

    w3 = half_weight(qkv_weight.transpose(1, 0, 2))
    qv_half = half_weight(qv_bias)
    wp = half_weight(proj_weight)
    w_in = half_weight(in_weight)
    b_in = half_weight(in_bias)
    w_out = half_weight(out_weight)

    tok = chip_value(tokens)
    cot = chip_value(cotangent)
    blend = chip_value(mix_blend)
    segment = chip_value(clip_ids)[0]
    halves = jnp.stack([core, 1 - core]).astype(jnp.int32)

    mixed, n1, q, k, v, att, lse, attn_part = attention(
        blend, halves, tok, partner_own, partner_oth, segment, gain_one, shift_one,
        w3, qv_half[0], qv_half[1], wp,
    )
    hidden, n2, act, gp, out_part, gn2_part, g_bin, g_bout = feed(
        mixed, attn_part, swap(attn_part), proj_bias, gain_two, shift_two, cot, w_in, b_in, w_out
    )
    gn2_oth = swap(gn2_part)
    out_oth = swap(out_part)
    g_in = outer((n2, gp))
    g_out = outer((cot, act))
    block = (hidden + (out_part.astype(F32) + out_oth.astype(F32)) + out_bias).astype(BF16)
    block_out = jnp.where(home, block, lax.ppermute(block, both, home_to_pair))

    gh, gh_low, gproj, gn1_part, sums_two, g_qv = attention_back(
        hidden, cot, gn2_part, gn2_oth, gain_two, segment, wp, q, k, v, lse, w3
    )
    g_attn = outer((n1, gproj), (gh_low, att))
    outgoing, kept, sums_one = mixed_back(blend, mixed, gh, gn1_part, swap(gn1_part), gain_one)

    leaving = lax.dynamic_index_in_dim(
        outgoing.reshape(2, 2 * dp_count, piece, width), core, 0, keepdims=False
    )
    back = lax.all_to_all(leaving, both, 0, 0, tiled=True)
    back = back.reshape(dp_count // 2, 2, 2, piece, width).transpose(0, 2, 1, 3, 4)
    back = back.reshape(dp_count, 2, piece, width)
    ids = jnp.arange(dp_count, dtype=jnp.int32)
    source_of = jnp.sum(
        jnp.where(partner[:, None] == ids[None, :], ids[:, None], 0), axis=0, dtype=jnp.int32
    )
    returning = pick(back, source_of)
    returning = jnp.broadcast_to(
        returning[:, None], (dp_count, 2, 2, piece, width)
    ).reshape(2 * dp_count, 2, piece, width)
    returned = lax.all_to_all(returning, both, 0, 0, tiled=True)
    returned = returned.transpose(1, 0, 2, 3).reshape(rows, width)
    kept = jnp.where(home, kept, lax.ppermute(kept, both, home_to_pair))
    grad_tokens = (kept.astype(F32) + returned.astype(F32)).astype(BF16)

    def pair_step(value):
        extra = lax.ppermute(value, both, pair_to_home)
        return (value.astype(F32) + extra.astype(F32)).astype(BF16)

    def core_step(value):
        axis = value.ndim - 3
        given = lax.ppermute(
            lax.dynamic_index_in_dim(value, 1 - core, axis, keepdims=False), both, chip_share
        )
        held = lax.dynamic_index_in_dim(value, core, axis, keepdims=False)
        return jnp.where(home, held, given)

    def bit_step(value, axis, bit):
        mine = (seq >> bit) & 1
        moved = lax.ppermute(
            lax.dynamic_index_in_dim(value, 1 - mine, axis, keepdims=False),
            "dp",
            [(d, d ^ (1 << bit)) for d in all_dp],
        )
        held = lax.dynamic_index_in_dim(value, mine, axis, keepdims=False)
        return (held.astype(F32) + moved.astype(F32)).astype(BF16)

    def scatter(value, first):
        value = value.reshape((2,) * bits + (width // dp_count, value.shape[1]))
        left = list(range(bits - 1, 0, -1))
        if first == "bit":
            value = bit_step(value, left.index(1), 1)
            left.remove(1)
        value = core_step(pair_step(value))
        while left:
            bit = left[-1]
            value = bit_step(value, left.index(bit), bit)
            left.remove(bit)
        return value.astype(F32)

    sum_in = scatter(g_in, "pair")
    sum_out = scatter(g_out, "bit")
    sum_attn = scatter(g_attn, "pair")
    local = width // 2
    sum_qkv = sum_attn[:, : 3 * local].reshape(-1, 3, local)
    sum_proj = sum_attn[:, 3 * local :].T

    first_core = (core == 0).astype(F32)

    def folded(value):
        return jnp.sum(value, axis=-2)

    def spread_half(vector):
        zero = jnp.zeros_like(vector)
        low = jnp.where(core == 0, vector, zero)
        return jnp.concatenate([low, vector - low], axis=-1).reshape(-1)

    g_qv_sum = folded(g_qv)
    packed = jnp.concatenate(
        [
            (first_core * folded(sums_one)).reshape(-1),
            (first_core * folded(sums_two)).reshape(-1),
            first_core * folded(g_bout),
            spread_half(folded(g_bin)),
            spread_half(g_qv_sum[0]),
            spread_half(g_qv_sum[1]),
        ]
    )
    packed = lax.psum(packed, both)
    small = width // dp_count

    def part_of(offset, size):
        return lax.dynamic_slice(packed, (offset,), (size,))

    plain = [part_of(i * width + seq * small, small) for i in range(6)]
    units = in_bias.shape[0]
    tail = 6 * width
    sum_bin = part_of(tail + mp * units + seq * (units // dp_count), units // dp_count)
    tail = tail + 2 * units
    sum_qv = jnp.stack(
        [
            part_of(tail + i * width + mp * local + seq * (local // dp_count), local // dp_count)
            for i in range(2)
        ]
    )
    return (
        block_out,
        grad_tokens,
        plain[0],
        plain[1],
        sum_qkv,
        sum_qv,
        sum_proj,
        plain[4],
        plain[2],
        plain[3],
        sum_in,
        sum_bin,
        sum_out.T,
        plain[5],
    )


def solution(mesh):
    return jax.shard_map(
        shards,
        mesh=mesh,
        in_specs=(
            P("dp", None),
            P("dp"),
            P(),
            P("dp", None),
            P(),
            P(),
            P(None, None, "mp"),
            P(None, "mp"),
            P("mp", None),
            P(),
            P(),
            P(),
            P(None, "mp"),
            P("mp"),
            P("mp", None),
            P(),
            P("dp", None),
        ),
        out_specs=(
            P("dp", None),
            P("dp", None),
            P("dp"),
            P("dp"),
            P("dp", None, "mp"),
            P(None, ("mp", "dp")),
            P("mp", "dp"),
            P("dp"),
            P("dp"),
            P("dp"),
            P("dp", "mp"),
            P(("mp", "dp")),
            P("mp", "dp"),
            P("dp"),
        ),
        check_vma=False,
    )
```

```python
import functools

import jax
import jax.numpy as jnp
from jax import lax
from jax.experimental import pallas as pl
from jax.experimental.pallas import tpu as pltpu
from jax.sharding import PartitionSpec as P

HEAD_DIM = 64
NORM_EPS = 1e-06
NEG_FILL = -1e30
SCORE_SCALE = HEAD_DIM ** (-0.5)
MAX_CLIP = 256
LANES = 128
F32 = jnp.float32
BF16 = jnp.bfloat16
MIB = 1 << 20
SMALL = pl.CostEstimate(flops=1 << 20, bytes_accessed=1 << 20, transcendentals=0)


def nn(left, right):
    return lax.dot_general(left, right, (((1,), (0,)), ((), ())), preferred_element_type=F32)


def nt(left, right):
    return lax.dot_general(left, right, (((1,), (1,)), ((), ())), preferred_element_type=F32)


def vmem():
    return pl.BlockSpec(memory_space=pltpu.VMEM)


def anywhere():
    return pl.BlockSpec(memory_space=pl.ANY)


def smem():
    return pl.BlockSpec(memory_space=pltpu.SMEM)


def params(mib):
    return pltpu.CompilerParams(vmem_limit_bytes=mib * MIB)


def shape(dims, dtype):
    return jax.ShapeDtypeStruct(dims, dtype)


def row_stats(vector):
    mean = jnp.mean(vector, axis=-1, keepdims=True)
    centred = vector - mean
    spread = jnp.mean(centred * centred, axis=-1, keepdims=True)
    return centred, lax.rsqrt(spread + NORM_EPS)


def fold_rows(block):
    rows, width = block.shape
    return jnp.sum(block.reshape(rows // 8, 8, width), axis=0)


def pick_kernel(index, source, *refs):
    picked = refs[-1]

    def move(i, carry):
        picked[i] = source[index[i]]
        return carry

    lax.fori_loop(0, picked.shape[0], move, 0, unroll=4)


def pick(source, index, *after):
    dims = index.shape + source.shape[1:]
    return pl.pallas_call(
        pick_kernel,
        out_shape=shape(dims, source.dtype),
        in_specs=[smem(), vmem()] + [anywhere()] * len(after),
        out_specs=vmem(),
        compiler_params=params(16),
        cost_estimate=SMALL,
        name="pick",
    )(index, source, *after)


def attention_kernel(
    blend, halves, tok, own, oth, seg_row, seg_col, gain, shift, w3, bq, bv, wp,
    mixed, n1, q, k, v, att, lse, part,
    vt, att_t, seg_b, bias,
):
    rows, width = tok.shape
    local = wp.shape[0]
    half_rows = rows // 2
    ratio = blend[0]
    blk = 64

    for src, half in ((own, halves[0]), (oth, halves[1])):

        def mix(i, carry, src=src, half=half):
            here = pl.ds(pl.multiple_of(half * half_rows + i * blk, blk), blk)
            there = pl.ds(pl.multiple_of(i * blk, blk), blk)
            blended = ratio * tok[here, :].astype(F32) + (1.0 - ratio) * src[there, :].astype(F32)
            mixed[here, :] = blended
            centred, inv = row_stats(blended)
            n1[here, :] = (centred * inv * gain[...] + shift[...]).astype(BF16)
            seg_b[here, :] = jnp.broadcast_to(seg_col[here, :], (blk, LANES))
            return carry

        lax.fori_loop(0, half_rows // blk, mix, 0)

    big = 256
    for i in range(rows // big):
        here = pl.ds(i * big, big)
        normed = n1[here, :]
        queries = (nn(normed, w3[0]) + bq[...]).astype(BF16).astype(F32)
        q[here, :] = (queries * SCORE_SCALE).astype(BF16)
        k[here, :] = nn(normed, w3[1]).astype(BF16)
        values = (nn(normed, w3[2]) + bv[...]).astype(BF16)
        v[here, :] = values
        vt[:, here] = values.T

    window = min(rows, LANES + 2 * MAX_CLIP)
    lane = lax.broadcasted_iota(jnp.int32, (LANES, LANES), 1)
    sides = [(lane // HEAD_DIM == e).astype(BF16) for e in range(2)]

    def attend(j, carry):
        here = pl.ds(pl.multiple_of(j * LANES, LANES), LANES)
        first = pl.multiple_of(jnp.clip(j * LANES - MAX_CLIP, 0, rows - window), LANES)
        keys = pl.ds(first, window)
        bias[...] = jnp.where(seg_b[keys, :] == seg_row[:, here], 0.0, NEG_FILL)
        for h in range(local // HEAD_DIM):
            pair = pl.ds((h // 2) * LANES, LANES)
            query = q[here, pair] * sides[h % 2]
            scores = nt(k[keys, pair], query) + bias[...]
            top = jnp.max(scores, axis=0, keepdims=True)
            grown = jnp.exp(scores - top)
            total = jnp.sum(grown, axis=0, keepdims=True)
            head = pl.ds(h * HEAD_DIM, HEAD_DIM)
            out = nn(vt[head, keys], grown.astype(BF16)) / total
            att_t[head, here] = out.astype(BF16)
            lse[pl.ds(h, 1), here] = top + jnp.log(total)
        return carry

    lax.fori_loop(0, rows // LANES, attend, 0)

    for i in range(rows // big):
        here = pl.ds(i * big, big)
        block = att_t[:, here].T
        att[here, :] = block
        part[here, :] = nn(block, wp[...]).astype(BF16)


def attention(blend, halves, tok, own, oth, segment, gain, shift, w3, bq, bv, wp):
    rows, width = tok.shape
    local = wp.shape[0]
    heads = local // HEAD_DIM
    window = min(rows, LANES + 2 * MAX_CLIP)
    return pl.pallas_call(
        attention_kernel,
        out_shape=(
            shape((rows, width), F32),
            shape((rows, width), BF16),
            shape((rows, local), BF16),
            shape((rows, local), BF16),
            shape((rows, local), BF16),
            shape((rows, local), BF16),
            shape((heads, rows), F32),
            shape((rows, width), BF16),
        ),
        in_specs=[smem(), smem()] + [vmem()] * 11,
        out_specs=[vmem()] * 8,
        scratch_shapes=[
            pltpu.VMEM((local, rows), BF16),
            pltpu.VMEM((local, rows), BF16),
            pltpu.VMEM((rows, LANES), jnp.int32),
            pltpu.VMEM((window, LANES), F32),
        ],
        compiler_params=params(48),
        cost_estimate=SMALL,
        name="attention",
    )(
        blend, halves, tok, own, oth, segment[None, :], segment[:, None],
        gain[None, :], shift[None, :], w3, bq[None, :], bv[None, :], wp,
    )


ERFC_SLOPE = 0.47
ERFC_COEFFS = (
    0.2663094668265691,
    0.2480096137831850,
    0.3362712657560771,
    -0.1262288063821733,
    0.6076790117752645,
    -0.4204702410368928,
    0.0884296765518492,
)


def gelu_parts(pre):
    bell = jnp.exp(pre * pre * -0.5)
    t = 1.0 / (1.0 + jnp.abs(pre) * (ERFC_SLOPE * 0.5**0.5))
    poly = 0.5 * ERFC_COEFFS[-1]
    for coeff in ERFC_COEFFS[-2::-1]:
        poly = poly * t + 0.5 * coeff
    tail = poly * t * bell
    cdf = jnp.where(pre >= 0, 1.0 - tail, tail)
    return pre * cdf, cdf + pre * bell * 0.3989422804014327


def transpose_into(target, source):
    rows = source.shape[0]
    big = 256
    for i in range(rows // big):
        here = pl.ds(i * big, big)
        target[:, here] = source[here, :].T


def feed_kernel(
    mixed, p_own, p_oth, pb, gain, shift, cot, cot_t, w_in, b_in, w_out,
    hidden, part, gn_part, g_in, g_out, g_bin, g_bout,
    n2, n2_t, act, gp, acc_o, acc_g,
):
    step = pl.program_id(0)
    rows, width = mixed.shape
    units = w_in.shape[1]

    @pl.when(step == 0)
    def _():
        blk = 64
        g_bout[...] = jnp.zeros_like(g_bout)

        def norm(i, carry):
            here = pl.ds(pl.multiple_of(i * blk, blk), blk)
            attn = p_own[here, :].astype(F32) + p_oth[here, :].astype(F32)
            total = mixed[here, :] + attn + pb[...]
            hidden[here, :] = total
            centred, inv = row_stats(total)
            n2[here, :] = (centred * inv * gain[...] + shift[...]).astype(BF16)
            g_bout[...] += fold_rows(cot[here, :].astype(F32))
            return carry

        lax.fori_loop(0, rows // blk, norm, 0)
        transpose_into(n2_t, n2)
        acc_o[...] = jnp.zeros_like(acc_o)
        acc_g[...] = jnp.zeros_like(acc_g)

    big = 256
    sub = 16
    sums = jnp.zeros((8, units), F32)
    for i in range(rows // big):
        here = pl.ds(i * big, big)
        pre_all = nn(n2[here, :], w_in[...])
        grad_all = nt(cot[here, :], w_out[...])
        for s in range(big // sub):
            rng = slice(s * sub, s * sub + sub)
            value, slope = gelu_parts(pre_all[rng] + b_in[...])
            grad = grad_all[rng] * slope
            sums += fold_rows(grad)
            spot = pl.ds(i * big + s * sub, sub)
            act[spot, :] = value.astype(BF16)
            gp[spot, :] = grad.astype(BF16)
        acc_o[here, :] += nn(act[here, :], w_out[...])
        acc_g[here, :] += nt(gp[here, :], w_in[...])
    g_bin[...] = sums
    for i in range(width // big):
        here = pl.ds(i * big, big)
        g_in[here, :] = nn(n2_t[here, :], gp[...]).astype(BF16)
        g_out[here, :] = nn(cot_t[here, :], act[...]).astype(BF16)

    @pl.when(step == pl.num_programs(0) - 1)
    def _():
        part[...] = acc_o[...].astype(BF16)
        gn_part[...] = acc_g[...].astype(BF16)


def feed(mixed, p_own, p_oth, pb, gain, shift, cot, cot_t, w_in, b_in, w_out):
    rows, width = mixed.shape
    units = w_in.shape[1]
    chunk = 512

    def whole(dims):
        return pl.BlockSpec(dims, lambda j: (0, 0), pipeline_mode=pl.Buffered(1))

    def columns(lines):
        return pl.BlockSpec((lines, chunk), lambda j: (0, j))

    tall = whole((rows, width))
    flat = whole((1, width))
    return pl.pallas_call(
        feed_kernel,
        grid=(units // chunk,),
        out_shape=(
            shape((rows, width), F32),
            shape((rows, width), BF16),
            shape((rows, width), BF16),
            shape((width, units), BF16),
            shape((width, units), BF16),
            shape((8, units), F32),
            shape((8, width), F32),
        ),
        in_specs=[
            tall, tall, tall, flat, flat, flat, tall, whole((width, rows)),
            columns(width), columns(1), pl.BlockSpec((chunk, width), lambda j: (j, 0)),
        ],
        out_specs=[
            tall, tall, tall, columns(width), columns(width), columns(8), whole((8, width)),
        ],
        scratch_shapes=[
            pltpu.VMEM((rows, width), BF16),
            pltpu.VMEM((width, rows), BF16),
            pltpu.VMEM((rows, chunk), BF16),
            pltpu.VMEM((rows, chunk), BF16),
            pltpu.VMEM((rows, width), F32),
            pltpu.VMEM((rows, width), F32),
        ],
        compiler_params=params(50),
        cost_estimate=SMALL,
        name="feed",
    )(
        mixed, p_own, p_oth, pb[None, :], gain[None, :], shift[None, :], cot, cot_t,
        w_in, b_in[None, :], w_out,
    )


def outer_kernel(firsts, *refs):
    count = len(firsts)
    lefts, rights = refs[:count], refs[count : 2 * count]
    out, turned = refs[2 * count], refs[2 * count + 1]
    step = pl.program_id(0)
    big = 256
    for n, first in enumerate(firsts):

        @pl.when(step == first)
        def _(n=n):
            transpose_into(turned, lefts[n])

        last = firsts[n + 1] if n + 1 < count else 1 << 20

        @pl.when((step >= first) & (step < last))
        def _(n=n):
            for i in range(out.shape[0] // big):
                here = pl.ds(i * big, big)
                out[here, :] = nn(turned[here, :], rights[n][...]).astype(BF16)


def outer(*pairs):
    chunk = 384
    rows, width = pairs[0][0].shape
    steps = [right.shape[1] // chunk for _, right in pairs]
    firsts = [sum(steps[:n]) for n in range(len(steps))]
    total = sum(steps)

    def right_spec(first, count):
        return pl.BlockSpec(
            (rows, chunk), lambda j: (0, jnp.clip(j - first, 0, count - 1))
        )

    left_spec = pl.BlockSpec((rows, width), lambda j: (0, 0), pipeline_mode=pl.Buffered(1))
    return pl.pallas_call(
        functools.partial(outer_kernel, firsts),
        grid=(total,),
        out_shape=shape((width, total * chunk), BF16),
        in_specs=[left_spec] * len(pairs)
        + [right_spec(first, count) for first, count in zip(firsts, steps)],
        out_specs=pl.BlockSpec((width, chunk), lambda j: (0, j)),
        scratch_shapes=[pltpu.VMEM((width, rows), BF16)],
        compiler_params=params(32),
        cost_estimate=SMALL,
        name="outer",
    )(*[left for left, _ in pairs], *[right for _, right in pairs])


def attention_back_kernel(
    hidden, cot, g_own, g_oth, gain, seg_row, seg_col, wp, q, k, v, lse, w3,
    gh, gh_low, gproj, part, sums, g_qv,
    d_out, kt, dq_t, dk, dv, seg_b, bias,
):
    rows, width = hidden.shape
    local = wp.shape[0]
    blk = 64
    sums[...] = jnp.zeros_like(sums)

    def norm(i, carry):
        here = pl.ds(pl.multiple_of(i * blk, blk), blk)
        grad = g_own[here, :].astype(F32) + g_oth[here, :].astype(F32)
        centred, inv = row_stats(hidden[here, :])
        normed = centred * inv
        scaled = grad * gain[...]
        mean_one = jnp.mean(scaled, axis=-1, keepdims=True)
        mean_two = jnp.mean(scaled * normed, axis=-1, keepdims=True)
        back = cot[here, :].astype(F32) + inv * (scaled - mean_one - normed * mean_two)
        gh[here, :] = back
        gh_low[here, :] = back.astype(BF16)
        sums[0] += fold_rows(grad * normed)
        sums[1] += fold_rows(grad)
        sums[2] += fold_rows(back)
        seg_b[here, :] = jnp.broadcast_to(seg_col[here, :], (blk, LANES))
        return carry

    lax.fori_loop(0, rows // blk, norm, 0)

    big = 256
    for i in range(rows // big):
        here = pl.ds(i * big, big)
        d_out[here, :] = nt(gh_low[here, :], wp[...]).astype(BF16)
        kt[:, here] = k[here, :].T
    dk[...] = jnp.zeros_like(dk)
    dv[...] = jnp.zeros_like(dv)

    window = min(rows, LANES + 2 * MAX_CLIP)
    lane = lax.broadcasted_iota(jnp.int32, (LANES, LANES), 1)
    sides = [(lane // HEAD_DIM == e).astype(BF16) for e in range(2)]

    def attend(j, carry):
        here = pl.ds(pl.multiple_of(j * LANES, LANES), LANES)
        first = pl.multiple_of(jnp.clip(j * LANES - MAX_CLIP, 0, rows - window), LANES)
        keys = pl.ds(first, window)
        bias[...] = jnp.where(seg_b[keys, :] == seg_row[:, here], 0.0, NEG_FILL)
        for p in range(local // LANES):
            pair = pl.ds(p * LANES, LANES)
            key_block, value_block = k[keys, pair], v[keys, pair]
            probs_two, grads_two, queries_two, outs_two = [], [], [], []
            for e in range(2):
                h = 2 * p + e
                head = pl.ds(h * HEAD_DIM, HEAD_DIM)
                query = q[here, pair] * sides[e]
                grad_out = d_out[here, pair] * sides[e]
                scores = nt(key_block, query) + bias[...]
                probs = jnp.exp(scores - lse[pl.ds(h, 1), here])
                weighted = probs * nt(value_block, grad_out)
                inner = jnp.sum(weighted, axis=0, keepdims=True)
                grads = (weighted - probs * inner).astype(BF16)
                dq_t[head, here] = nn(kt[head, keys], grads) * SCORE_SCALE
                probs_two.append(probs.astype(BF16))
                grads_two.append(grads)
                queries_two.append(query)
                outs_two.append(grad_out)
            both = jnp.concatenate(grads_two, axis=1)
            dk[keys, pair] += nn(both, jnp.concatenate(queries_two, axis=0))
            both = jnp.concatenate(probs_two, axis=1)
            dv[keys, pair] += nn(both, jnp.concatenate(outs_two, axis=0))
        return carry

    lax.fori_loop(0, rows // LANES, attend, 0)

    q_sum = jnp.zeros((8, local), F32)
    v_sum = jnp.zeros((8, local), F32)
    for i in range(rows // big):
        here = pl.ds(i * big, big)
        grad_q, grad_k, grad_v = dq_t[:, here].T, dk[here, :], dv[here, :]
        q_sum += fold_rows(grad_q)
        v_sum += fold_rows(grad_v)
        low_q, low_k, low_v = grad_q.astype(BF16), grad_k.astype(BF16), grad_v.astype(BF16)
        gproj[here, pl.ds(0, local)] = low_q
        gproj[here, pl.ds(local, local)] = low_k
        gproj[here, pl.ds(2 * local, local)] = low_v
        part[here, :] = (nt(low_q, w3[0]) + nt(low_k, w3[1]) + nt(low_v, w3[2])).astype(BF16)
    g_qv[0] = q_sum
    g_qv[1] = v_sum


def attention_back(hidden, cot, g_own, g_oth, gain, segment, wp, q, k, v, lse, w3):
    rows, width = hidden.shape
    local = wp.shape[0]
    heads = local // HEAD_DIM
    window = min(rows, LANES + 2 * MAX_CLIP)
    return pl.pallas_call(
        attention_back_kernel,
        out_shape=(
            shape((rows, width), F32),
            shape((rows, width), BF16),
            shape((rows, 3 * local), BF16),
            shape((rows, width), BF16),
            shape((3, 8, width), F32),
            shape((2, 8, local), F32),
        ),
        in_specs=[vmem()] * 13,
        out_specs=[vmem()] * 6,
        scratch_shapes=[
            pltpu.VMEM((rows, local), BF16),
            pltpu.VMEM((local, rows), BF16),
            pltpu.VMEM((local, rows), F32),
            pltpu.VMEM((rows, local), F32),
            pltpu.VMEM((rows, local), F32),
            pltpu.VMEM((rows, LANES), jnp.int32),
            pltpu.VMEM((window, LANES), F32),
        ],
        compiler_params=params(48),
        cost_estimate=SMALL,
        name="attention_back",
    )(
        hidden, cot, g_own, g_oth, gain[None, :], segment[None, :], segment[:, None],
        wp, q, k, v, lse, w3,
    )


def mixed_back_kernel(blend, mixed, gh, g_own, g_oth, gain, *refs):
    outgoing, kept, sums = refs[-3:]
    ratio = blend[0]

    @pl.when(pl.program_id(0) == 0)
    def _():
        sums[...] = jnp.zeros_like(sums)

    blk = 64
    rows = mixed.shape[0]
    for i in range(rows // blk):
        here = pl.ds(i * blk, blk)
        grad = g_own[here, :].astype(F32) + g_oth[here, :].astype(F32)
        centred, inv = row_stats(mixed[here, :])
        normed = centred * inv
        scaled = grad * gain[...]
        mean_one = jnp.mean(scaled, axis=-1, keepdims=True)
        mean_two = jnp.mean(scaled * normed, axis=-1, keepdims=True)
        back = gh[here, :] + inv * (scaled - mean_one - normed * mean_two)
        outgoing[here, :] = ((1.0 - ratio) * back).astype(BF16)
        kept[here, :] = (ratio * back).astype(BF16)
        sums[0] += fold_rows(grad * normed)
        sums[1] += fold_rows(grad)


def mixed_back(blend, mixed, gh, g_own, g_oth, gain, *before):
    rows, width = mixed.shape
    block = 128
    strip = pl.BlockSpec((block, width), lambda i: (i, 0))
    flat = pl.BlockSpec((1, width), lambda i: (0, 0))
    return pl.pallas_call(
        mixed_back_kernel,
        grid=(rows // block,),
        out_shape=(
            shape((rows, width), BF16),
            shape((rows, width), BF16),
            shape((2, 8, width), F32),
        ),
        in_specs=[smem(), strip, strip, strip, strip, flat] + [anywhere()] * len(before),
        out_specs=[strip, strip, pl.BlockSpec((2, 8, width), lambda i: (0, 0, 0))],
        compiler_params=params(32),
        cost_estimate=SMALL,
        name="mixed_back",
    )(blend, mixed, gh, g_own, g_oth, gain[None, :], *before)


def shards(
    tokens,
    mix_blend,
    partner,
    clip_ids,
    gain_one,
    shift_one,
    qkv_weight,
    qv_bias,
    proj_weight,
    proj_bias,
    gain_two,
    shift_two,
    in_weight,
    in_bias,
    out_weight,
    out_bias,
    cotangent,
):
    rows, width = tokens.shape
    dp_count = lax.axis_size("dp")
    both = ("dp", "mp")
    bits = dp_count.bit_length() - 1
    seq = lax.axis_index("dp")
    mp = lax.axis_index("mp")
    core = lax.rem(seq, 2)
    home = core == mp
    all_dp = range(dp_count)

    def joint(d, m):
        return 2 * d + m

    core_swap = [(d, d ^ 1) for d in all_dp]
    chip_share = [(joint(d, d & 1), joint(d ^ 1, d & 1)) for d in all_dp]
    home_to_pair = [(joint(d, d & 1), joint(d, 1 - (d & 1))) for d in all_dp]
    pair_to_home = [(joint(d, 1 - (d & 1)), joint(d, d & 1)) for d in all_dp]
    weight_move = home_to_pair + [
        (joint(d, 1 - (d & 1)), joint(d ^ 1, 1 - (d & 1))) for d in all_dp
    ]

    def swap(value):
        return lax.ppermute(value, "dp", core_swap)

    def chip_value(value):
        return jnp.where(home, value, lax.ppermute(value, both, chip_share))

    def after(value, *others):
        return lax.optimization_barrier((value,) + others)[0]

    def half_weight(value):
        return lax.ppermute(value, both, weight_move)

    seq_small = chip_value(jnp.concatenate([mix_blend, clip_ids[0].astype(F32)]))
    blend = seq_small[:1]
    segment = seq_small[1:].astype(jnp.int32)
    local = proj_weight.shape[0]
    units = in_bias.shape[0]
    half_small = jnp.concatenate([qv_bias.reshape(-1), in_bias])
    half_small = jnp.where(home, half_small, lax.ppermute(half_small, both, home_to_pair))
    bq, bv = half_small[:local], half_small[local : 2 * local]
    b_in = half_small[2 * local :]

    w3 = half_weight(qkv_weight.transpose(1, 0, 2))

    ids = jnp.arange(2 * dp_count, dtype=jnp.int32)
    piece = rows // (2 * 2 * dp_count)
    sent = tokens.reshape(2, dp_count, 2, piece, width)
    sent = lax.dynamic_index_in_dim(sent, mp, 2, keepdims=False)
    spread = lax.all_to_all(sent.transpose(1, 0, 2, 3), "dp", 0, 0, tiled=True)
    wanted = partner[(ids // 4) * 2 + ids % 2] * 2 + (ids // 2) % 2
    chosen = pick(spread.reshape(2 * dp_count, piece, width), wanted, w3)
    partner_own = lax.all_to_all(chosen, both, 0, 0, tiled=True).reshape(rows // 2, width)
    partner_oth = swap(partner_own)

    wp = half_weight(proj_weight)
    w_in = half_weight(in_weight)
    w_out = half_weight(out_weight)

    tok = chip_value(tokens)
    cot = chip_value(cotangent)
    halves = jnp.stack([core, 1 - core]).astype(jnp.int32)

    mixed, n1, q, k, v, att, lse, attn_part = attention(
        blend, halves, tok, partner_own, partner_oth, segment, gain_one, shift_one,
        w3, bq, bv, wp,
    )
    hidden, out_part, gn2_part, g_in, g_out, g_bin, g_bout = feed(
        mixed, attn_part, swap(attn_part), proj_bias, gain_two, shift_two, cot, cot.T,
        w_in, b_in, w_out,
    )
    gn2_oth = swap(gn2_part)

    across = lax.rem(seq // 2, 2)
    pair_and_core = pair_to_home + [(joint(d, d & 1), joint(d ^ 1, d & 1)) for d in all_dp]
    pair_diagonal = [(joint(d, 1 - (d & 1)), joint(d ^ 1, d & 1)) for d in all_dp]

    def taken(value, index, axis):
        return lax.dynamic_index_in_dim(value, index, axis, keepdims=False)

    def total(*terms):
        return sum(term.astype(F32) for term in terms)

    def send_across(value):
        value = value.reshape(dp_count // 4, 2, 2, width // dp_count, -1)
        got = lax.ppermute(taken(value, 1 - across, 1), "dp", [(d, d ^ 2) for d in all_dp])
        return taken(value, across, 1), got

    def send_pair(value):
        one = lax.ppermute(taken(value, jnp.where(home, 1 - core, core), 1), both, pair_and_core)
        two = lax.ppermute(taken(value, 1 - core, 1), both, pair_diagonal)
        held = taken(value, core, 1)
        return jnp.where(home, held, jnp.zeros_like(held)), one, two

    def send_far(value, shift, radix):
        value = value.reshape((-1, radix) + value.shape[1:])
        spot = lax.rem(seq >> shift, radix)
        got = [
            lax.ppermute(
                taken(value, spot ^ flip, 1), "dp", [(d, d ^ (flip << shift)) for d in all_dp]
            )
            for flip in range(1, radix)
        ]
        return [taken(value, spot, 1)] + got

    def far(value, *others):
        shift = 2
        while shift < bits:
            radix = min(4, dp_count >> shift)
            terms = send_far(value, shift, radix)
            value = total(terms[0], *after(terms[1:], *others))
            shift += radix.bit_length() - 1
            if shift < bits:
                value = value.astype(BF16)
        return value.reshape(value.shape[-2:])

    in_held, in_got = send_across(g_in)
    out_held, out_got = send_across(g_out)
    gh, gh_low, gproj, gn1_part, sums_two, g_qv = attention_back(
        hidden, cot, gn2_part, gn2_oth, gain_two, segment, wp, q, k, v, lse, w3
    )
    in_value = total(in_held, after(in_got, gn1_part)).astype(BF16)
    in_terms = send_pair(in_value)
    outgoing, kept, sums_one = mixed_back(
        blend, mixed, gh, gn1_part, swap(gn1_part), gain_one, in_value
    )

    leaving = lax.dynamic_index_in_dim(
        outgoing.reshape(2, 2 * dp_count, piece, width), core, 0, keepdims=False
    )
    back = lax.all_to_all(leaving, both, 0, 0, tiled=True)
    g_attn = outer((n1, gproj), (after(gh_low, leaving), att))
    out_value = total(out_held, after(out_got, leaving)).astype(BF16)
    out_terms = send_pair(out_value)
    in_value = total(in_terms[0], *after(in_terms[1:], leaving)).astype(BF16)

    part_rows = width // dp_count
    wide = jnp.concatenate(
        [jnp.sum(sums_one, axis=1), jnp.sum(sums_two, axis=1), jnp.sum(g_bout, axis=0)[None]]
    )
    short = jnp.concatenate(
        [
            vectors.reshape(-1, dp_count, vectors.shape[-1] // dp_count)
            .transpose(1, 0, 2)
            .reshape(dp_count, -1)
            for vectors in (wide, jnp.sum(g_bin, axis=0), jnp.sum(g_qv, axis=1))
        ],
        axis=1,
    )
    short_size = short.shape[1]
    short = jnp.pad(short, ((0, 0), (0, part_rows * LANES - short_size))).astype(BF16)
    g_attn = jnp.concatenate([g_attn, short.reshape(width, LANES)], axis=1)
    attn_held, attn_got = send_across(g_attn)

    source_of = jnp.sum(
        jnp.where(partner[:, None] == ids[None, :dp_count], ids[:dp_count, None], 0),
        axis=0,
        dtype=jnp.int32,
    )
    source = source_of[ids // 2]
    wanted = (source // 2) * 4 + (ids % 2) * 2 + source % 2
    returning = pick(back, wanted, in_value, out_value)
    returned = lax.all_to_all(
        returning.reshape(dp_count, 2, piece, width), "dp", 0, 0, tiled=True
    )
    kept = kept.reshape(2, dp_count, 2, piece, width)
    kept_got = lax.ppermute(taken(kept, 1 - mp, 2), both, home_to_pair)
    kept = jnp.where(home, taken(kept, mp, 2), kept_got)
    mine = (kept.astype(F32) + returned.transpose(1, 0, 2, 3).astype(F32)).astype(BF16)
    other = lax.ppermute(mine, "mp", [(0, 1), (1, 0)])
    first = mp == 0
    grad_tokens = jnp.stack(
        [jnp.where(first, mine, other), jnp.where(first, other, mine)], axis=2
    ).reshape(rows, width)

    out_oth = after(swap(out_part), leaving)
    block = (hidden + (out_part.astype(F32) + out_oth.astype(F32)) + out_bias).astype(BF16)
    block_out = jnp.where(home, block, lax.ppermute(block, both, home_to_pair))

    out_value = total(out_terms[0], *after(out_terms[1:], returned)).astype(BF16)
    attn_value = total(attn_held, after(attn_got, returned)).astype(BF16)
    attn_terms = send_pair(attn_value)
    attn_value = total(*attn_terms).astype(BF16)
    sum_in = far(in_value, returned)
    sum_out = far(out_value)
    sum_attn = far(attn_value)
    sum_qkv = sum_attn[:, : 3 * local].reshape(-1, 3, local)
    sum_proj = sum_attn[:, 3 * local : 4 * local].T
    short = sum_attn[:, 4 * local :].reshape(-1)[:short_size]
    plain = short[: 6 * part_rows].reshape(6, part_rows)
    sum_bin = short[6 * part_rows : 6 * part_rows + units // dp_count]
    sum_qv = short[6 * part_rows + units // dp_count :].reshape(2, -1)
    return (
        block_out,
        grad_tokens,
        plain[0],
        plain[1],
        sum_qkv,
        sum_qv,
        sum_proj,
        plain[4],
        plain[2],
        plain[3],
        sum_in,
        sum_bin,
        sum_out.T,
        plain[5],
    )


def solution(mesh):
    return jax.shard_map(
        shards,
        mesh=mesh,
        in_specs=(
            P("dp", None),
            P("dp"),
            P(),
            P("dp", None),
            P(),
            P(),
            P(None, None, "mp"),
            P(None, "mp"),
            P("mp", None),
            P(),
            P(),
            P(),
            P(None, "mp"),
            P("mp"),
            P("mp", None),
            P(),
            P("dp", None),
        ),
        out_specs=(
            P("dp", None),
            P("dp", None),
            P("dp"),
            P("dp"),
            P("dp", None, "mp"),
            P(None, ("mp", "dp")),
            P("mp", "dp"),
            P("dp"),
            P("dp"),
            P("dp"),
            P("dp", "mp"),
            P(("mp", "dp")),
            P("mp", "dp"),
            P("dp"),
        ),
        check_vma=False,
    )
```

```python
import functools

import jax
import jax.numpy as jnp
from jax import lax
from jax.experimental import pallas as pl
from jax.experimental.pallas import tpu as pltpu
from jax.sharding import PartitionSpec as P

HEAD_DIM = 64
NORM_EPS = 1e-06
NEG_FILL = -1e30
SCORE_SCALE = HEAD_DIM ** (-0.5)
MAX_CLIP = 256
LANES = 128
F32 = jnp.float32
BF16 = jnp.bfloat16
MIB = 1 << 20
SMALL = pl.CostEstimate(flops=1 << 20, bytes_accessed=1 << 20, transcendentals=0)


def nn(left, right):
    return lax.dot_general(left, right, (((1,), (0,)), ((), ())), preferred_element_type=F32)


def nt(left, right):
    return lax.dot_general(left, right, (((1,), (1,)), ((), ())), preferred_element_type=F32)


def vmem():
    return pl.BlockSpec(memory_space=pltpu.VMEM)


def anywhere():
    return pl.BlockSpec(memory_space=pl.ANY)


def smem():
    return pl.BlockSpec(memory_space=pltpu.SMEM)


def params(mib):
    return pltpu.CompilerParams(vmem_limit_bytes=mib * MIB)


def shape(dims, dtype):
    return jax.ShapeDtypeStruct(dims, dtype)


def row_stats(vector):
    mean = jnp.mean(vector, axis=-1, keepdims=True)
    centred = vector - mean
    spread = jnp.mean(centred * centred, axis=-1, keepdims=True)
    return centred, lax.rsqrt(spread + NORM_EPS)


def fold_rows(block):
    rows, width = block.shape
    return jnp.sum(block.reshape(rows // 8, 8, width), axis=0)


def pick_kernel(index, source, *refs):
    picked = refs[-1]

    def move(i, carry):
        picked[i] = source[index[i]]
        return carry

    lax.fori_loop(0, picked.shape[0], move, 0, unroll=4)


def pick(source, index, *after):
    dims = index.shape + source.shape[1:]
    return pl.pallas_call(
        pick_kernel,
        out_shape=shape(dims, source.dtype),
        in_specs=[smem(), vmem()] + [anywhere()] * len(after),
        out_specs=vmem(),
        compiler_params=params(4),
        cost_estimate=SMALL,
        name="pick",
    )(index, source, *after)


def attention_kernel(
    blend, halves, tok, own, oth, seg_row, seg_col, gain, shift, w3, bq, bv, wp, *refs
):
    mixed, n1, q, k, v, att, lse, part, vt, att_t, seg_b, bias = refs[-12:]
    rows, width = tok.shape
    local = wp.shape[0]
    half_rows = rows // 2
    ratio = blend[0]
    blk = 32

    for src, half in ((own, halves[0]), (oth, halves[1])):

        def mix(i, carry, src=src, half=half):
            here = pl.ds(pl.multiple_of(half * half_rows + i * blk, blk), blk)
            there = pl.ds(pl.multiple_of(i * blk, blk), blk)
            blended = ratio * tok[here, :].astype(F32) + (1.0 - ratio) * src[there, :].astype(F32)
            mixed[here, :] = blended
            centred, inv = row_stats(blended)
            n1[here, :] = (centred * inv * gain[...] + shift[...]).astype(BF16)
            seg_b[here, :] = jnp.broadcast_to(seg_col[here, :], (blk, LANES))
            return carry

        lax.fori_loop(0, half_rows // blk, mix, 0, unroll=4)

    big = 256
    for i in range(rows // big):
        here = pl.ds(i * big, big)
        normed = n1[here, :]
        queries = (nn(normed, w3[0]) + bq[...]).astype(BF16).astype(F32)
        q[here, :] = (queries * SCORE_SCALE).astype(BF16)
        k[here, :] = nn(normed, w3[1]).astype(BF16)
        values = (nn(normed, w3[2]) + bv[...]).astype(BF16)
        v[here, :] = values
        vt[:, here] = values.T

    window = min(rows, LANES + 2 * MAX_CLIP)
    lane = lax.broadcasted_iota(jnp.int32, (LANES, LANES), 1)
    sides = [(lane // HEAD_DIM == e).astype(BF16) for e in range(2)]

    def attend(j, carry):
        here = pl.ds(pl.multiple_of(j * LANES, LANES), LANES)
        first = pl.multiple_of(jnp.clip(j * LANES - MAX_CLIP, 0, rows - window), LANES)
        keys = pl.ds(first, window)
        bias[...] = jnp.where(seg_b[keys, :] == seg_row[:, here], 0.0, NEG_FILL)
        for h in range(local // HEAD_DIM):
            pair = pl.ds((h // 2) * LANES, LANES)
            query = q[here, pair] * sides[h % 2]
            scores = nt(k[keys, pair], query) + bias[...]
            top = jnp.max(scores, axis=0, keepdims=True)
            grown = jnp.exp(scores - top)
            total = jnp.sum(grown, axis=0, keepdims=True)
            head = pl.ds(h * HEAD_DIM, HEAD_DIM)
            out = nn(vt[head, keys], grown.astype(BF16)) / total
            att_t[head, here] = out.astype(BF16)
            lse[pl.ds(h, 1), here] = top + jnp.log(total)
        return carry

    lax.fori_loop(0, rows // LANES, attend, 0)

    for i in range(rows // big):
        here = pl.ds(i * big, big)
        block = att_t[:, here].T
        att[here, :] = block
        part[here, :] = nn(block, wp[...]).astype(BF16)


def attention(blend, halves, tok, own, oth, segment, gain, shift, w3, bq, bv, wp, *before):
    rows, width = tok.shape
    local = wp.shape[0]
    heads = local // HEAD_DIM
    window = min(rows, LANES + 2 * MAX_CLIP)
    return pl.pallas_call(
        attention_kernel,
        out_shape=(
            shape((rows, width), F32),
            shape((rows, width), BF16),
            shape((rows, local), BF16),
            shape((rows, local), BF16),
            shape((rows, local), BF16),
            shape((rows, local), BF16),
            shape((heads, rows), F32),
            shape((rows, width), BF16),
        ),
        in_specs=[smem(), smem()] + [vmem()] * 11 + [anywhere()] * len(before),
        out_specs=[vmem()] * 8,
        scratch_shapes=[
            pltpu.VMEM((local, rows), BF16),
            pltpu.VMEM((local, rows), BF16),
            pltpu.VMEM((rows, LANES), jnp.int32),
            pltpu.VMEM((window, LANES), F32),
        ],
        compiler_params=params(24),
        cost_estimate=SMALL,
        name="attention",
    )(
        blend, halves, tok, own, oth, segment[None, :], segment[:, None],
        gain[None, :], shift[None, :], w3, bq[None, :], bv[None, :], wp, *before,
    )


ERFC_SLOPE = 0.47
ERFC_COEFFS = (
    0.2663094668265691,
    0.2480096137831850,
    0.3362712657560771,
    -0.1262288063821733,
    0.6076790117752645,
    -0.4204702410368928,
    0.0884296765518492,
)


def gelu_parts(pre):
    bell = jnp.exp(pre * pre * -0.5)
    t = 1.0 / (1.0 + jnp.abs(pre) * (ERFC_SLOPE * 0.5**0.5))
    poly = 0.5 * ERFC_COEFFS[-1]
    for coeff in ERFC_COEFFS[-2::-1]:
        poly = poly * t + 0.5 * coeff
    tail = poly * t * bell
    cdf = jnp.where(pre >= 0, 1.0 - tail, tail)
    return pre * cdf, cdf + pre * bell * 0.3989422804014327


def transpose_into(target, source):
    rows = source.shape[0]
    big = 256
    for i in range(rows // big):
        here = pl.ds(i * big, big)
        target[:, here] = source[here, :].T


def feed_kernel(
    mixed, p_own, p_oth, pb, gain, shift, cot, cot_t, w_in, b_in, w_out,
    hidden, part, gn_part, g_in, g_out, g_bin, g_bout,
    n2, n2_t, act, gp, acc_o, acc_g,
):
    step = pl.program_id(0)
    rows, width = mixed.shape
    units = w_in.shape[1]

    @pl.when(step == 0)
    def _():
        blk = 32
        g_bout[...] = jnp.zeros_like(g_bout)

        def norm(i, carry):
            here = pl.ds(pl.multiple_of(i * blk, blk), blk)
            attn = p_own[here, :].astype(F32) + p_oth[here, :].astype(F32)
            total = mixed[here, :] + attn + pb[...]
            hidden[here, :] = total
            centred, inv = row_stats(total)
            n2[here, :] = (centred * inv * gain[...] + shift[...]).astype(BF16)
            g_bout[...] += fold_rows(cot[here, :].astype(F32))
            return carry

        lax.fori_loop(0, rows // blk, norm, 0, unroll=4)
        transpose_into(n2_t, n2)
        acc_o[...] = jnp.zeros_like(acc_o)
        acc_g[...] = jnp.zeros_like(acc_g)

    big = 256
    sub = 16
    sums = jnp.zeros((8, units), F32)
    for i in range(rows // big):
        here = pl.ds(i * big, big)
        pre_all = nn(n2[here, :], w_in[...])
        grad_all = nt(cot[here, :], w_out[...])
        for s in range(big // sub):
            rng = slice(s * sub, s * sub + sub)
            value, slope = gelu_parts(pre_all[rng] + b_in[...])
            grad = grad_all[rng] * slope
            sums += fold_rows(grad)
            spot = pl.ds(i * big + s * sub, sub)
            act[spot, :] = value.astype(BF16)
            gp[spot, :] = grad.astype(BF16)
        acc_o[here, :] += nn(act[here, :], w_out[...])
        acc_g[here, :] += nt(gp[here, :], w_in[...])
    g_bin[...] = sums
    for i in range(width // big):
        here = pl.ds(i * big, big)
        g_in[here, :] = nn(n2_t[here, :], gp[...]).astype(BF16)
        g_out[here, :] = nn(cot_t[here, :], act[...]).astype(BF16)

    @pl.when(step == pl.num_programs(0) - 1)
    def _():
        part[...] = acc_o[...].astype(BF16)
        gn_part[...] = acc_g[...].astype(BF16)


def feed(mixed, p_own, p_oth, pb, gain, shift, cot, cot_t, w_in, b_in, w_out):
    rows, width = mixed.shape
    units = w_in.shape[1]
    chunk = 512

    def whole(dims):
        return pl.BlockSpec(dims, lambda j: (0, 0), pipeline_mode=pl.Buffered(1))

    def columns(lines):
        return pl.BlockSpec((lines, chunk), lambda j: (0, j))

    tall = whole((rows, width))
    flat = whole((1, width))
    return pl.pallas_call(
        feed_kernel,
        grid=(units // chunk,),
        out_shape=(
            shape((rows, width), F32),
            shape((rows, width), BF16),
            shape((rows, width), BF16),
            shape((width, units), BF16),
            shape((width, units), BF16),
            shape((8, units), F32),
            shape((8, width), F32),
        ),
        in_specs=[
            tall, tall, tall, flat, flat, flat, tall, whole((width, rows)),
            columns(width), columns(1), pl.BlockSpec((chunk, width), lambda j: (j, 0)),
        ],
        out_specs=[
            tall, tall, tall, columns(width), columns(width), columns(8), whole((8, width)),
        ],
        scratch_shapes=[
            pltpu.VMEM((rows, width), BF16),
            pltpu.VMEM((width, rows), BF16),
            pltpu.VMEM((rows, chunk), BF16),
            pltpu.VMEM((rows, chunk), BF16),
            pltpu.VMEM((rows, width), F32),
            pltpu.VMEM((rows, width), F32),
        ],
        compiler_params=params(30),
        cost_estimate=SMALL,
        name="feed",
    )(
        mixed, p_own, p_oth, pb[None, :], gain[None, :], shift[None, :], cot, cot_t,
        w_in, b_in[None, :], w_out,
    )


def outer_kernel(firsts, *refs):
    count = len(firsts)
    lefts, rights = refs[:count], refs[count : 2 * count]
    out, turned = refs[2 * count], refs[2 * count + 1]
    step = pl.program_id(0)
    big = 256
    for n, first in enumerate(firsts):

        @pl.when(step == first)
        def _(n=n):
            transpose_into(turned, lefts[n])

        last = firsts[n + 1] if n + 1 < count else 1 << 20

        @pl.when((step >= first) & (step < last))
        def _(n=n):
            for i in range(out.shape[0] // big):
                here = pl.ds(i * big, big)
                out[here, :] = nn(turned[here, :], rights[n][...]).astype(BF16)


def outer(*pairs):
    chunk = 384
    rows, width = pairs[0][0].shape
    steps = [right.shape[1] // chunk for _, right in pairs]
    firsts = [sum(steps[:n]) for n in range(len(steps))]
    total = sum(steps)

    def right_spec(first, count):
        return pl.BlockSpec(
            (rows, chunk), lambda j: (0, jnp.clip(j - first, 0, count - 1))
        )

    left_spec = pl.BlockSpec((rows, width), lambda j: (0, 0), pipeline_mode=pl.Buffered(1))
    return pl.pallas_call(
        functools.partial(outer_kernel, firsts),
        grid=(total,),
        out_shape=shape((width, total * chunk), BF16),
        in_specs=[left_spec] * len(pairs)
        + [right_spec(first, count) for first, count in zip(firsts, steps)],
        out_specs=pl.BlockSpec((width, chunk), lambda j: (0, j)),
        scratch_shapes=[pltpu.VMEM((width, rows), BF16)],
        compiler_params=params(10),
        cost_estimate=SMALL,
        name="outer",
    )(*[left for left, _ in pairs], *[right for _, right in pairs])


def attention_back_kernel(
    hidden, cot, g_own, g_oth, gain, seg_row, seg_col, wp, q, k, v, lse, w3,
    gh, gh_low, gproj, part, sums, g_qv,
    d_out, kt, dq_t, dk, dv, seg_b, bias,
):
    rows, width = hidden.shape
    local = wp.shape[0]
    blk = 32
    sums[...] = jnp.zeros_like(sums)

    def norm(i, carry):
        here = pl.ds(pl.multiple_of(i * blk, blk), blk)
        grad = g_own[here, :].astype(F32) + g_oth[here, :].astype(F32)
        centred, inv = row_stats(hidden[here, :])
        normed = centred * inv
        scaled = grad * gain[...]
        mean_one = jnp.mean(scaled, axis=-1, keepdims=True)
        mean_two = jnp.mean(scaled * normed, axis=-1, keepdims=True)
        back = cot[here, :].astype(F32) + inv * (scaled - mean_one - normed * mean_two)
        gh[here, :] = back
        gh_low[here, :] = back.astype(BF16)
        sums[0] += fold_rows(grad * normed)
        sums[1] += fold_rows(grad)
        sums[2] += fold_rows(back)
        seg_b[here, :] = jnp.broadcast_to(seg_col[here, :], (blk, LANES))
        return carry

    lax.fori_loop(0, rows // blk, norm, 0, unroll=4)

    big = 256
    for i in range(rows // big):
        here = pl.ds(i * big, big)
        d_out[here, :] = nt(gh_low[here, :], wp[...]).astype(BF16)
        kt[:, here] = k[here, :].T
    dk[...] = jnp.zeros_like(dk)
    dv[...] = jnp.zeros_like(dv)

    window = min(rows, LANES + 2 * MAX_CLIP)
    lane = lax.broadcasted_iota(jnp.int32, (LANES, LANES), 1)
    sides = [(lane // HEAD_DIM == e).astype(BF16) for e in range(2)]

    def attend(j, carry):
        here = pl.ds(pl.multiple_of(j * LANES, LANES), LANES)
        first = pl.multiple_of(jnp.clip(j * LANES - MAX_CLIP, 0, rows - window), LANES)
        keys = pl.ds(first, window)
        bias[...] = jnp.where(seg_b[keys, :] == seg_row[:, here], 0.0, NEG_FILL)
        for p in range(local // LANES):
            pair = pl.ds(p * LANES, LANES)
            key_block, value_block = k[keys, pair], v[keys, pair]
            probs_two, grads_two, queries_two, outs_two = [], [], [], []
            for e in range(2):
                h = 2 * p + e
                head = pl.ds(h * HEAD_DIM, HEAD_DIM)
                query = q[here, pair] * sides[e]
                grad_out = d_out[here, pair] * sides[e]
                scores = nt(key_block, query) + bias[...]
                probs = jnp.exp(scores - lse[pl.ds(h, 1), here])
                weighted = probs * nt(value_block, grad_out)
                inner = jnp.sum(weighted, axis=0, keepdims=True)
                grads = (weighted - probs * inner).astype(BF16)
                dq_t[head, here] = nn(kt[head, keys], grads) * SCORE_SCALE
                probs_two.append(probs.astype(BF16))
                grads_two.append(grads)
                queries_two.append(query)
                outs_two.append(grad_out)
            both = jnp.concatenate(grads_two, axis=1)
            dk[keys, pair] += nn(both, jnp.concatenate(queries_two, axis=0))
            both = jnp.concatenate(probs_two, axis=1)
            dv[keys, pair] += nn(both, jnp.concatenate(outs_two, axis=0))
        return carry

    lax.fori_loop(0, rows // LANES, attend, 0)

    q_sum = jnp.zeros((8, local), F32)
    v_sum = jnp.zeros((8, local), F32)
    for i in range(rows // big):
        here = pl.ds(i * big, big)
        grad_q, grad_k, grad_v = dq_t[:, here].T, dk[here, :], dv[here, :]
        q_sum += fold_rows(grad_q)
        v_sum += fold_rows(grad_v)
        low_q, low_k, low_v = grad_q.astype(BF16), grad_k.astype(BF16), grad_v.astype(BF16)
        gproj[here, pl.ds(0, local)] = low_q
        gproj[here, pl.ds(local, local)] = low_k
        gproj[here, pl.ds(2 * local, local)] = low_v
        part[here, :] = (nt(low_q, w3[0]) + nt(low_k, w3[1]) + nt(low_v, w3[2])).astype(BF16)
    g_qv[0] = q_sum
    g_qv[1] = v_sum


def attention_back(hidden, cot, g_own, g_oth, gain, segment, wp, q, k, v, lse, w3):
    rows, width = hidden.shape
    local = wp.shape[0]
    heads = local // HEAD_DIM
    window = min(rows, LANES + 2 * MAX_CLIP)
    return pl.pallas_call(
        attention_back_kernel,
        out_shape=(
            shape((rows, width), F32),
            shape((rows, width), BF16),
            shape((rows, 3 * local), BF16),
            shape((rows, width), BF16),
            shape((3, 8, width), F32),
            shape((2, 8, local), F32),
        ),
        in_specs=[vmem()] * 13,
        out_specs=[vmem()] * 6,
        scratch_shapes=[
            pltpu.VMEM((rows, local), BF16),
            pltpu.VMEM((local, rows), BF16),
            pltpu.VMEM((local, rows), F32),
            pltpu.VMEM((rows, local), F32),
            pltpu.VMEM((rows, local), F32),
            pltpu.VMEM((rows, LANES), jnp.int32),
            pltpu.VMEM((window, LANES), F32),
        ],
        compiler_params=params(24),
        cost_estimate=SMALL,
        name="attention_back",
    )(
        hidden, cot, g_own, g_oth, gain[None, :], segment[None, :], segment[:, None],
        wp, q, k, v, lse, w3,
    )


def mixed_back_kernel(blend, mixed, gh, g_own, g_oth, gain, *refs):
    outgoing, kept, sums = refs[-3:]
    ratio = blend[0]

    @pl.when(pl.program_id(0) == 0)
    def _():
        sums[...] = jnp.zeros_like(sums)

    blk = 32
    rows = mixed.shape[0]
    for i in range(rows // blk):
        here = pl.ds(i * blk, blk)
        grad = g_own[here, :].astype(F32) + g_oth[here, :].astype(F32)
        centred, inv = row_stats(mixed[here, :])
        normed = centred * inv
        scaled = grad * gain[...]
        mean_one = jnp.mean(scaled, axis=-1, keepdims=True)
        mean_two = jnp.mean(scaled * normed, axis=-1, keepdims=True)
        back = gh[here, :] + inv * (scaled - mean_one - normed * mean_two)
        outgoing[here, :] = ((1.0 - ratio) * back).astype(BF16)
        kept[here, :] = (ratio * back).astype(BF16)
        sums[0] += fold_rows(grad * normed)
        sums[1] += fold_rows(grad)


def mixed_back(blend, mixed, gh, g_own, g_oth, gain, *before):
    rows, width = mixed.shape
    block = 128
    strip = pl.BlockSpec((block, width), lambda i: (i, 0))
    flat = pl.BlockSpec((1, width), lambda i: (0, 0))
    return pl.pallas_call(
        mixed_back_kernel,
        grid=(rows // block,),
        out_shape=(
            shape((rows, width), BF16),
            shape((rows, width), BF16),
            shape((2, 8, width), F32),
        ),
        in_specs=[smem(), strip, strip, strip, strip, flat] + [anywhere()] * len(before),
        out_specs=[strip, strip, pl.BlockSpec((2, 8, width), lambda i: (0, 0, 0))],
        compiler_params=params(8),
        cost_estimate=SMALL,
        name="mixed_back",
    )(blend, mixed, gh, g_own, g_oth, gain[None, :], *before)


def shards(
    tokens,
    mix_blend,
    partner,
    clip_ids,
    gain_one,
    shift_one,
    qkv_weight,
    qv_bias,
    proj_weight,
    proj_bias,
    gain_two,
    shift_two,
    in_weight,
    in_bias,
    out_weight,
    out_bias,
    cotangent,
):
    rows, width = tokens.shape
    dp_count = lax.axis_size("dp")
    both = ("dp", "mp")
    bits = dp_count.bit_length() - 1
    seq = lax.axis_index("dp")
    mp = lax.axis_index("mp")
    core = lax.rem(seq, 2)
    home = core == mp
    all_dp = range(dp_count)

    def joint(d, m):
        return 2 * d + m

    core_swap = [(d, d ^ 1) for d in all_dp]
    chip_share = [(joint(d, d & 1), joint(d ^ 1, d & 1)) for d in all_dp]
    home_to_pair = [(joint(d, d & 1), joint(d, 1 - (d & 1))) for d in all_dp]
    pair_to_home = [(joint(d, 1 - (d & 1)), joint(d, d & 1)) for d in all_dp]
    weight_move = home_to_pair + [
        (joint(d, 1 - (d & 1)), joint(d ^ 1, 1 - (d & 1))) for d in all_dp
    ]

    def swap(value):
        return lax.ppermute(value, "dp", core_swap)

    def chip_value(value):
        return jnp.where(home, value, lax.ppermute(value, both, chip_share))

    def after(value, *others):
        return lax.optimization_barrier((value,) + others)[0]

    def half_weight(value):
        return lax.ppermute(value, both, weight_move)

    seq_small = chip_value(jnp.concatenate([mix_blend, clip_ids[0].astype(F32)]))
    blend = seq_small[:1]
    segment = seq_small[1:].astype(jnp.int32)
    local = proj_weight.shape[0]
    units = in_bias.shape[0]
    half_small = jnp.concatenate([qv_bias.reshape(-1), in_bias])
    half_small = jnp.where(home, half_small, lax.ppermute(half_small, both, home_to_pair))
    bq, bv = half_small[:local], half_small[local : 2 * local]
    b_in = half_small[2 * local :]

    w3 = half_weight(qkv_weight.transpose(1, 0, 2))
    wp = half_weight(proj_weight)

    ids = jnp.arange(2 * dp_count, dtype=jnp.int32)
    piece = rows // (2 * 2 * dp_count)
    sent = tokens.reshape(2, dp_count, 2, piece, width)
    sent = lax.dynamic_index_in_dim(sent, mp, 2, keepdims=False)
    spread = lax.all_to_all(sent.transpose(1, 0, 2, 3), "dp", 0, 0, tiled=True)
    wanted = partner[(ids // 4) * 2 + ids % 2] * 2 + (ids // 2) % 2
    chosen = pick(spread.reshape(2 * dp_count, piece, width), wanted, w3, wp, half_small)
    partner_own = lax.all_to_all(chosen, both, 0, 0, tiled=True).reshape(rows // 2, width)
    partner_oth = swap(partner_own)

    w_in = half_weight(in_weight)
    w_out = half_weight(out_weight)

    tok = chip_value(tokens)
    cot = chip_value(cotangent)
    halves = jnp.stack([core, 1 - core]).astype(jnp.int32)

    mixed, n1, q, k, v, att, lse, attn_part = attention(
        blend, halves, tok, partner_own, partner_oth, segment, gain_one, shift_one,
        w3, bq, bv, wp, w_in,
    )
    hidden, out_part, gn2_part, g_in, g_out, g_bin, g_bout = feed(
        mixed, attn_part, swap(attn_part), proj_bias, gain_two, shift_two, cot, cot.T,
        w_in, b_in, w_out,
    )
    gn2_oth = swap(gn2_part)

    across = lax.rem(seq // 2, 2)
    pair_and_core = pair_to_home + [(joint(d, d & 1), joint(d ^ 1, d & 1)) for d in all_dp]
    pair_diagonal = [(joint(d, 1 - (d & 1)), joint(d ^ 1, d & 1)) for d in all_dp]

    def taken(value, index, axis):
        return lax.dynamic_index_in_dim(value, index, axis, keepdims=False)

    def total(*terms):
        return sum(term.astype(F32) for term in terms)

    def send_across(value):
        value = value.reshape(dp_count // 4, 2, 2, width // dp_count, -1)
        got = lax.ppermute(taken(value, 1 - across, 1), "dp", [(d, d ^ 2) for d in all_dp])
        return taken(value, across, 1), got

    def send_pair(value):
        one = lax.ppermute(taken(value, jnp.where(home, 1 - core, core), 1), both, pair_and_core)
        two = lax.ppermute(taken(value, 1 - core, 1), both, pair_diagonal)
        held = taken(value, core, 1)
        return jnp.where(home, held, jnp.zeros_like(held)), one, two

    def send_far(value, shift, radix):
        value = value.reshape((-1, radix) + value.shape[1:])
        spot = lax.rem(seq >> shift, radix)
        got = [
            lax.ppermute(
                taken(value, spot ^ flip, 1), "dp", [(d, d ^ (flip << shift)) for d in all_dp]
            )
            for flip in range(1, radix)
        ]
        return [taken(value, spot, 1)] + got

    def far(value, *others):
        shift = 2
        while shift < bits:
            radix = min(4, dp_count >> shift)
            terms = send_far(value, shift, radix)
            value = total(terms[0], *after(terms[1:], *others))
            shift += radix.bit_length() - 1
            if shift < bits:
                value = value.astype(BF16)
        return value.reshape(value.shape[-2:])

    in_held, in_got = send_across(g_in)
    gh, gh_low, gproj, gn1_part, sums_two, g_qv = attention_back(
        hidden, cot, gn2_part, gn2_oth, gain_two, segment, wp, q, k, v, lse, w3
    )
    in_value = total(in_held, after(in_got, gn1_part)).astype(BF16)
    in_terms = send_pair(in_value)
    outgoing, kept, sums_one = mixed_back(
        blend, mixed, gh, gn1_part, swap(gn1_part), gain_one, in_value
    )

    leaving = lax.dynamic_index_in_dim(
        outgoing.reshape(2, 2 * dp_count, piece, width), core, 0, keepdims=False
    )
    back = lax.all_to_all(leaving, both, 0, 0, tiled=True)
    g_attn = outer((n1, gproj), (after(gh_low, leaving), att))
    out_held, out_got = send_across(after(g_out, leaving))
    out_value = total(out_held, out_got).astype(BF16)
    out_terms = send_pair(out_value)
    in_value = total(in_terms[0], *after(in_terms[1:], leaving)).astype(BF16)

    part_rows = width // dp_count
    wide = jnp.concatenate(
        [jnp.sum(sums_one, axis=1), jnp.sum(sums_two, axis=1), jnp.sum(g_bout, axis=0)[None]]
    )
    short = jnp.concatenate(
        [
            vectors.reshape(-1, dp_count, vectors.shape[-1] // dp_count)
            .transpose(1, 0, 2)
            .reshape(dp_count, -1)
            for vectors in (wide, jnp.sum(g_bin, axis=0), jnp.sum(g_qv, axis=1))
        ],
        axis=1,
    )
    short_size = short.shape[1]
    short = jnp.pad(short, ((0, 0), (0, part_rows * LANES - short_size))).astype(BF16)
    g_attn = jnp.concatenate([g_attn, short.reshape(width, LANES)], axis=1)
    attn_held, attn_got = send_across(g_attn)

    source_of = jnp.sum(
        jnp.where(partner[:, None] == ids[None, :dp_count], ids[:dp_count, None], 0),
        axis=0,
        dtype=jnp.int32,
    )
    source = source_of[ids // 2]
    wanted = (source // 2) * 4 + (ids % 2) * 2 + source % 2
    returning = pick(back, wanted, in_value, out_value, g_attn)
    returned = lax.all_to_all(
        returning.reshape(dp_count, 2, piece, width), "dp", 0, 0, tiled=True
    )
    kept = kept.reshape(2, dp_count, 2, piece, width)
    kept_got = lax.ppermute(taken(kept, 1 - mp, 2), both, home_to_pair)
    kept = jnp.where(home, taken(kept, mp, 2), kept_got)
    mine = (kept.astype(F32) + returned.transpose(1, 0, 2, 3).astype(F32)).astype(BF16)
    other = lax.ppermute(mine, "mp", [(0, 1), (1, 0)])
    first = mp == 0
    grad_tokens = jnp.stack(
        [jnp.where(first, mine, other), jnp.where(first, other, mine)], axis=2
    ).reshape(rows, width)

    out_oth = after(swap(out_part), leaving)
    block = (hidden + (out_part.astype(F32) + out_oth.astype(F32)) + out_bias).astype(BF16)
    block_out = jnp.where(home, block, lax.ppermute(block, both, home_to_pair))

    out_value = total(out_terms[0], *after(out_terms[1:], returned)).astype(BF16)
    attn_value = total(attn_held, after(attn_got, returned)).astype(BF16)
    attn_terms = send_pair(attn_value)
    attn_value = total(*attn_terms).astype(BF16)
    sum_in = far(in_value, returned)
    sum_out = far(out_value)
    sum_attn = far(attn_value)
    sum_qkv = sum_attn[:, : 3 * local].reshape(-1, 3, local)
    sum_proj = sum_attn[:, 3 * local : 4 * local].T
    short = sum_attn[:, 4 * local :].reshape(-1)[:short_size]
    plain = short[: 6 * part_rows].reshape(6, part_rows)
    sum_bin = short[6 * part_rows : 6 * part_rows + units // dp_count]
    sum_qv = short[6 * part_rows + units // dp_count :].reshape(2, -1)
    return (
        block_out,
        grad_tokens,
        plain[0],
        plain[1],
        sum_qkv,
        sum_qv,
        sum_proj,
        plain[4],
        plain[2],
        plain[3],
        sum_in,
        sum_bin,
        sum_out.T,
        plain[5],
    )


def solution(mesh):
    return jax.shard_map(
        shards,
        mesh=mesh,
        in_specs=(
            P("dp", None),
            P("dp"),
            P(),
            P("dp", None),
            P(),
            P(),
            P(None, None, "mp"),
            P(None, "mp"),
            P("mp", None),
            P(),
            P(),
            P(),
            P(None, "mp"),
            P("mp"),
            P("mp", None),
            P(),
            P("dp", None),
        ),
        out_specs=(
            P("dp", None),
            P("dp", None),
            P("dp"),
            P("dp"),
            P("dp", None, "mp"),
            P(None, ("mp", "dp")),
            P("mp", "dp"),
            P("dp"),
            P("dp"),
            P("dp"),
            P("dp", "mp"),
            P(("mp", "dp")),
            P("mp", "dp"),
            P("dp"),
        ),
        check_vma=False,
    )
```

```python
import functools

import jax
import jax.numpy as jnp
from jax import lax
from jax.experimental import pallas as pl
from jax.experimental.pallas import tpu as pltpu
from jax.sharding import PartitionSpec as P

HEAD_DIM = 64
NORM_EPS = 1e-06
NEG_FILL = -1e30
SCORE_SCALE = HEAD_DIM ** (-0.5)
MAX_CLIP = 256
LANES = 128
F32 = jnp.float32
BF16 = jnp.bfloat16
MIB = 1 << 20
SMALL = pl.CostEstimate(flops=1 << 20, bytes_accessed=1 << 20, transcendentals=0)


def nn(left, right):
    return lax.dot_general(left, right, (((1,), (0,)), ((), ())), preferred_element_type=F32)


def nt(left, right):
    return lax.dot_general(left, right, (((1,), (1,)), ((), ())), preferred_element_type=F32)


def vmem():
    return pl.BlockSpec(memory_space=pltpu.VMEM)


def hbm():
    return pl.BlockSpec(memory_space=pltpu.HBM)


def smem():
    return pl.BlockSpec(memory_space=pltpu.SMEM)


def params(mib):
    return pltpu.CompilerParams(vmem_limit_bytes=mib * MIB)


def shape(dims, dtype):
    return jax.ShapeDtypeStruct(dims, dtype)


def row_stats(vector):
    mean = jnp.mean(vector, axis=-1, keepdims=True)
    centred = vector - mean
    spread = jnp.mean(centred * centred, axis=-1, keepdims=True)
    return centred, lax.rsqrt(spread + NORM_EPS)


def fold_rows(block):
    rows, width = block.shape
    return jnp.sum(block.reshape(rows // 8, 8, width), axis=0)


def pick_kernel(index, source, *refs):
    picked = refs[-1]

    def move(i, carry):
        picked[i] = source[index[i]]
        return carry

    lax.fori_loop(0, picked.shape[0], move, 0, unroll=4)


def pick(source, index, *after):
    dims = index.shape + source.shape[1:]
    return pl.pallas_call(
        pick_kernel,
        out_shape=shape(dims, source.dtype),
        in_specs=[smem(), vmem()] + [hbm()] * len(after),
        out_specs=vmem(),
        compiler_params=params(16),
        cost_estimate=SMALL,
        name="pick",
    )(index, source, *after)


def move(source, target, sem):
    return pltpu.make_async_copy(source, target, sem)


def spread_clips(seg_row, seg_b):
    for i in range(seg_b.shape[0] // LANES):
        here = pl.ds(i * LANES, LANES)
        seg_b[here, :] = jnp.broadcast_to(seg_row[:, here], (LANES, LANES)).T


def key_window(j, rows):
    window = min(rows, LANES + 2 * MAX_CLIP)
    here = pl.ds(pl.multiple_of(j * LANES, LANES), LANES)
    first = pl.multiple_of(jnp.clip(j * LANES - MAX_CLIP, 0, rows - window), LANES)
    return here, pl.ds(first, window)


def set_bias(bias, seg_b, seg_row, here, keys):
    filled = jnp.where(seg_b[keys, :] == seg_row[:, here], 0.0, NEG_FILL)
    bias[:, pl.ds(0, LANES)] = filled
    bias[:, pl.ds(LANES, LANES)] = filled


def two_heads(block):
    lane = lax.broadcasted_iota(jnp.int32, block.shape, 1)
    return jnp.concatenate(
        [block * (lane // HEAD_DIM == e).astype(BF16) for e in range(2)], axis=0
    )


def attention_kernel(
    blend, flags, seg_row, gain, shift, bq, bv, tok, own, oth, w3, wp, *refs
):
    mixed, n1, q, k, v, att, part, lse = refs[-28:-20]
    (
        tok_v, own_v, oth_v, w3_v, wp_v, mixed_v, n1_v, q_v, k_v, v_v, att_v, part_v,
        vt, att_t, seg_b, bias, ones, in_sems, out_sems, part_sems,
    ) = refs[-20:]
    rows, width = tok.shape
    local = wp.shape[0]
    half_rows = rows // 2
    ratio = blend[0]
    blk = 32
    big = 256

    loads = [
        move(source, target, in_sems.at[n])
        for n, (source, target) in enumerate(
            [(tok, tok_v), (own, own_v), (oth, oth_v), (w3, w3_v), (wp, wp_v)]
        )
    ]
    for load in loads:
        load.start()
    stores = [
        move(source, target, out_sems.at[n])
        for n, (source, target) in enumerate(
            [(mixed_v, mixed), (n1_v, n1), (q_v, q), (k_v, k), (v_v, v)]
        )
    ]
    ones[...] = jnp.ones_like(ones)
    spread_clips(seg_row, seg_b)

    loads[0].wait()
    for n, src, half in ((1, own_v, flags[0]), (2, oth_v, 1 - flags[0])):
        loads[n].wait()

        def mix(i, carry, src=src, half=half):
            here = pl.ds(pl.multiple_of(half * half_rows + i * blk, blk), blk)
            there = pl.ds(pl.multiple_of(i * blk, blk), blk)
            blended = ratio * tok_v[here, :].astype(F32) + (1.0 - ratio) * src[there, :].astype(F32)
            mixed_v[here, :] = blended
            centred, inv = row_stats(blended)
            n1_v[here, :] = (centred * inv * gain[...] + shift[...]).astype(BF16)
            return carry

        lax.fori_loop(0, half_rows // blk, mix, 0, unroll=4)
    for store in stores[:2]:
        store.start()

    loads[3].wait()
    for i in range(rows // big):
        here = pl.ds(i * big, big)
        normed = n1_v[here, :]
        queries = (nn(normed, w3_v[0]) + bq[...]).astype(BF16).astype(F32)
        q_v[here, :] = (queries * SCORE_SCALE).astype(BF16)
        k_v[here, :] = nn(normed, w3_v[1]).astype(BF16)
        values = (nn(normed, w3_v[2]) + bv[...]).astype(BF16)
        v_v[here, :] = values
        vt[:, here] = values.T
    for store in stores[2:]:
        store.start()

    def attend(j, carry):
        here, keys = key_window(j, rows)
        set_bias(bias, seg_b, seg_row, here, keys)
        for p in range(local // LANES):
            pair = pl.ds(p * LANES, LANES)
            scores = nt(k_v[keys, pair], two_heads(q_v[here, pair])) + bias[...]
            top = jnp.max(scores, axis=0, keepdims=True)
            grown = jnp.exp(scores - top).astype(BF16)
            total = nn(ones[...], grown)[:1]
            out = (nn(vt[pair, keys], grown) / total).astype(BF16)
            logs = top + jnp.log(total)
            for e in range(2):
                lanes = slice(e * LANES, e * LANES + LANES)
                head = slice(e * HEAD_DIM, e * HEAD_DIM + HEAD_DIM)
                att_t[pl.ds(p * LANES + e * HEAD_DIM, HEAD_DIM), here] = out[head, lanes]
                lse[pl.ds(2 * p + e, 1), here] = logs[:, lanes]
        return carry

    lax.fori_loop(0, rows // LANES, attend, 0)

    loads[4].wait()
    last = []
    for i in range(rows // big):
        here = pl.ds(i * big, big)
        block = att_t[:, here].T
        att_v[here, :] = block
        part_v[here, :] = nn(block, wp_v[...]).astype(BF16)
        last.append(move(part_v.at[here, :], part.at[here, :], part_sems.at[i]))
        last[-1].start()
    last.append(move(att_v, att, out_sems.at[5]))
    last[-1].start()
    for store in stores + last:
        store.wait()


def attention(blend, flags, tok, own, oth, segment, gain, shift, w3, bq, bv, wp, *before):
    rows, width = tok.shape
    local = wp.shape[0]
    window = min(rows, LANES + 2 * MAX_CLIP)
    thin = shape((rows, local), BF16)
    tall = shape((rows, width), BF16)
    return pl.pallas_call(
        attention_kernel,
        out_shape=(
            shape((rows, width), F32), tall, thin, thin, thin, thin, tall,
            shape((local // HEAD_DIM, rows), F32),
        ),
        in_specs=[smem(), smem()] + [vmem()] * 5 + [hbm()] * 5 + [hbm()] * len(before),
        out_specs=[hbm()] * 7 + [vmem()],
        scratch_shapes=[
            pltpu.VMEM((rows, width), BF16),
            pltpu.VMEM((rows // 2, width), BF16),
            pltpu.VMEM((rows // 2, width), BF16),
            pltpu.VMEM(w3.shape, BF16),
            pltpu.VMEM(wp.shape, BF16),
            pltpu.VMEM((rows, width), F32),
            pltpu.VMEM((rows, width), BF16),
            pltpu.VMEM((rows, local), BF16),
            pltpu.VMEM((rows, local), BF16),
            pltpu.VMEM((rows, local), BF16),
            pltpu.VMEM((rows, local), BF16),
            pltpu.VMEM((rows, width), BF16),
            pltpu.VMEM((local, rows), BF16),
            pltpu.VMEM((local, rows), BF16),
            pltpu.VMEM((rows, LANES), F32),
            pltpu.VMEM((window, 2 * LANES), F32),
            pltpu.VMEM((16, window), BF16),
            pltpu.SemaphoreType.DMA((5,)),
            pltpu.SemaphoreType.DMA((6,)),
            pltpu.SemaphoreType.DMA((rows // 256,)),
        ],
        compiler_params=params(60),
        cost_estimate=SMALL,
        name="attention",
    )(
        blend, flags, segment[None, :], gain[None, :], shift[None, :], bq[None, :], bv[None, :],
        tok, own, oth, w3, wp, *before,
    )


ERFC_SLOPE = 0.47
ERFC_COEFFS = (
    0.2663094668265691,
    0.2480096137831850,
    0.3362712657560771,
    -0.1262288063821733,
    0.6076790117752645,
    -0.4204702410368928,
    0.0884296765518492,
)


def gelu_parts(pre):
    bell = jnp.exp(pre * pre * -0.5)
    t = 1.0 / (1.0 + jnp.abs(pre) * (ERFC_SLOPE * 0.5**0.5))
    poly = 0.5 * ERFC_COEFFS[-1]
    for coeff in ERFC_COEFFS[-2::-1]:
        poly = poly * t + 0.5 * coeff
    tail = poly * t * bell
    cdf = jnp.where(pre >= 0, 1.0 - tail, tail)
    return pre * cdf, cdf + pre * bell * 0.3989422804014327


def turn_into(target, source, blocks):
    rows = source.shape[0]
    big = 256
    for i in range(rows // big):
        here = pl.ds(i * big, big)
        turned = source[here, :].T
        for start, place, count in blocks:
            target[pl.ds(place, count), here] = turned[start : start + count]


def lead_blocks(width, lead_rows):
    runs = width // lead_rows
    return [
        (run * lead_rows, ((run % 2) * (runs // 2) + run // 2) * lead_rows, lead_rows)
        for run in range(runs)
    ]


def feed_kernel(
    lead_rows, flags, pb, gain, shift, b_in, mixed, p_own, p_oth, cot, cot_t,
    w_in, w_in_one, w_in_two, w_out, w_out_one, w_out_two,
    hidden, part, gn_part, in_keep, in_send, out_keep, out_send, g_bin, g_bout,
    mixed_v, own_v, oth_v, cot_v, cot_tv, w_in_v, w_out_v, n2, n2_t, act, gp, acc_o, acc_g,
    g_in, g_out, in_sems, turn_sems, weight_sems, out_sems, grad_sems,
):
    rows, width = mixed.shape
    units = w_in.shape[1]
    chunk = act.shape[1]
    blk = 32
    big = 256
    sub = 16
    blocks = lead_blocks(width, lead_rows)
    home = flags[1] == 1
    across = flags[2]

    loads = [
        move(source, target, in_sems.at[n])
        for n, (source, target) in enumerate(
            [(mixed, mixed_v), (p_own, own_v), (p_oth, oth_v), (cot, cot_v)]
        )
    ]
    for load in loads:
        load.start()

    weights = []
    for n, (whole, one, two, target) in enumerate(
        [(w_in, w_in_one, w_in_two, w_in_v), (w_out, w_out_one, w_out_two, w_out_v)]
    ):
        half = whole.shape[0] // 2
        for m, (got, place) in enumerate([(one, across), (two, 1 - across)]):
            spot = pl.ds(pl.multiple_of(place * half, half), half)
            sem = weight_sems.at[2 * n + m]

            @pl.when(home)
            def _(whole=whole, target=target, spot=spot, sem=sem):
                move(whole.at[spot, :], target.at[spot, :], sem).start()

            @pl.when(jnp.logical_not(home))
            def _(got=got, target=target, spot=spot, sem=sem):
                move(got, target.at[spot, :], sem).start()

            weights.append(move(whole.at[spot, :], target.at[spot, :], sem))
    turns = [
        move(cot_t.at[pl.ds(start, count), :], cot_tv.at[pl.ds(place, count), :], turn_sems.at[n])
        for n, (start, place, count) in enumerate(blocks)
    ]
    for turn in turns:
        turn.start()

    g_bout[...] = jnp.zeros_like(g_bout)
    for load in loads:
        load.wait()

    def norm(i, carry):
        here = pl.ds(pl.multiple_of(i * blk, blk), blk)
        attn = own_v[here, :].astype(F32) + oth_v[here, :].astype(F32)
        total = mixed_v[here, :] + attn + pb[...]
        mixed_v[here, :] = total
        centred, inv = row_stats(total)
        n2[here, :] = (centred * inv * gain[...] + shift[...]).astype(BF16)
        g_bout[...] += fold_rows(cot_v[here, :].astype(F32))
        return carry

    lax.fori_loop(0, rows // blk, norm, 0, unroll=4)
    stores = [move(mixed_v, hidden, out_sems.at[0])]
    stores[0].start()
    turn_into(n2_t, n2, blocks)
    for weight in weights:
        weight.wait()
    for turn in turns:
        turn.wait()

    def step(j, carry):
        units_here = pl.ds(pl.multiple_of(j * chunk, chunk), chunk)
        sums = jnp.zeros((8, chunk), F32)
        for i in range(rows // big):
            here = pl.ds(i * big, big)
            pre_all = nn(n2[here, :], w_in_v[:, units_here])
            grad_all = nt(cot_v[here, :], w_out_v[units_here, :])
            for s in range(big // sub):
                rng = slice(s * sub, s * sub + sub)
                value, slope = gelu_parts(pre_all[rng] + b_in[:, units_here])
                grad = grad_all[rng] * slope
                sums += fold_rows(grad)
                spot = pl.ds(i * big + s * sub, sub)
                act[spot, :] = value.astype(BF16)
                gp[spot, :] = grad.astype(BF16)
            more_o = nn(act[here, :], w_out_v[units_here, :])
            more_g = nt(gp[here, :], w_in_v[:, units_here])

            @pl.when(j == 0)
            def _(here=here, more_o=more_o, more_g=more_g):
                acc_o[here, :] = more_o
                acc_g[here, :] = more_g

            @pl.when(j > 0)
            def _(here=here, more_o=more_o, more_g=more_g):
                acc_o[here, :] += more_o
                acc_g[here, :] += more_g

        g_bin[:, units_here] = sums
        half = width // 2
        for x in range(2):
            side = pl.ds(x * half, half)
            g_in[j, x] = nn(n2_t[side, :], gp[...]).astype(BF16)
            g_out[j, x] = nn(cot_tv[side, :], act[...]).astype(BF16)
        for n, (buf, keep, send) in enumerate(
            [(g_in, in_keep, in_send), (g_out, out_keep, out_send)]
        ):
            move(buf.at[j, across], keep.at[:, units_here], grad_sems.at[j, 2 * n]).start()
            move(buf.at[j, 1 - across], send.at[:, units_here], grad_sems.at[j, 2 * n + 1]).start()
        return carry

    steps = units // chunk
    lax.fori_loop(0, steps, step, 0)
    for i in range(rows // big):
        here = pl.ds(i * big, big)
        own_v[here, :] = acc_o[here, :].astype(BF16)
        oth_v[here, :] = acc_g[here, :].astype(BF16)
    for n, (source, target) in enumerate([(oth_v, gn_part), (own_v, part)]):
        stores.append(move(source, target, out_sems.at[1 + n]))
        stores[-1].start()
    for j in range(steps):
        units_here = pl.ds(j * chunk, chunk)
        for n, (buf, keep, send) in enumerate(
            [(g_in, in_keep, in_send), (g_out, out_keep, out_send)]
        ):
            stores.append(move(buf.at[j, 0], keep.at[:, units_here], grad_sems.at[j, 2 * n]))
            stores.append(move(buf.at[j, 1], send.at[:, units_here], grad_sems.at[j, 2 * n + 1]))
    for store in stores:
        store.wait()


def feed(
    lead_rows, flags, pb, gain, shift, b_in, mixed, p_own, p_oth, cot, cot_t,
    w_in, w_in_one, w_in_two, w_out, w_out_one, w_out_two,
):
    rows, width = mixed.shape
    units = w_in.shape[1]
    chunk = 512
    steps = units // chunk
    tall = shape((rows, width), BF16)
    grad = shape((width // 2, units), BF16)
    return pl.pallas_call(
        functools.partial(feed_kernel, lead_rows),
        out_shape=(
            shape((rows, width), F32), tall, tall, grad, grad, grad, grad,
            shape((8, units), F32), shape((8, width), F32),
        ),
        in_specs=[smem()] + [vmem()] * 4 + [hbm()] * 11,
        out_specs=[hbm()] * 7 + [vmem()] * 2,
        scratch_shapes=[
            pltpu.VMEM((rows, width), F32),
            pltpu.VMEM((rows, width), BF16),
            pltpu.VMEM((rows, width), BF16),
            pltpu.VMEM((rows, width), BF16),
            pltpu.VMEM((width, rows), BF16),
            pltpu.VMEM(w_in.shape, BF16),
            pltpu.VMEM(w_out.shape, BF16),
            pltpu.VMEM((rows, width), BF16),
            pltpu.VMEM((width, rows), BF16),
            pltpu.VMEM((rows, chunk), BF16),
            pltpu.VMEM((rows, chunk), BF16),
            pltpu.VMEM((rows, width), F32),
            pltpu.VMEM((rows, width), F32),
            pltpu.VMEM((steps, 2, width // 2, chunk), BF16),
            pltpu.VMEM((steps, 2, width // 2, chunk), BF16),
            pltpu.SemaphoreType.DMA((4,)),
            pltpu.SemaphoreType.DMA((width // lead_rows,)),
            pltpu.SemaphoreType.DMA((4,)),
            pltpu.SemaphoreType.DMA((3,)),
            pltpu.SemaphoreType.DMA((steps, 4)),
        ],
        compiler_params=params(60),
        cost_estimate=SMALL,
        name="feed",
    )(
        flags, pb[None, :], gain[None, :], shift[None, :], b_in[None, :],
        mixed, p_own, p_oth, cot, cot_t,
        w_in, w_in_one, w_in_two, w_out, w_out_one, w_out_two,
    )


def outer_kernel(
    lead_rows, flags, n1, gproj, gh_low, att, short,
    keep, send,
    n1_v, gproj_v, gh_v, att_v, turned, out, in_sems, short_sems, out_sems,
):
    width = n1.shape[1]
    local = att.shape[1]
    half = width // 2
    across = flags[2]
    blocks = lead_blocks(width, lead_rows)
    loads = [
        move(source, target, in_sems.at[n])
        for n, (source, target) in enumerate(
            [(n1, n1_v), (gproj, gproj_v), (gh_low, gh_v), (att, att_v)]
        )
    ]
    per_half = len(blocks) // 2
    for n, (start, place, count) in enumerate(blocks):
        loads.append(
            move(
                short.at[pl.ds(start, count), :],
                out.at[n % 2, pl.ds(place % half, count), pl.ds(4 * local, LANES)],
                short_sems.at[n],
            )
        )
    for load in loads:
        load.start()
    loads[0].wait()
    turn_into(turned, n1_v, blocks)
    loads[1].wait()
    for part in range(4):
        if part == 3:
            loads[2].wait()
            turn_into(turned, gh_v, blocks)
            loads[3].wait()
        right = att_v[...] if part == 3 else gproj_v[:, pl.ds(part * local, local)]
        for x in range(2):
            out[x, :, pl.ds(part * local, local)] = nn(
                turned[pl.ds(x * half, half), :], right
            ).astype(BF16)
    for load in loads[4:]:
        load.wait()
    stores = [
        move(out.at[1 - across], send, out_sems.at[0]),
        move(out.at[across], keep, out_sems.at[1]),
    ]
    for store in stores:
        store.start()
    for store in stores:
        store.wait()


def outer(lead_rows, flags, n1, gproj, gh_low, att, short):
    rows, width = n1.shape
    local = att.shape[1]
    half = shape((width // 2, 4 * local + LANES), BF16)
    return pl.pallas_call(
        functools.partial(outer_kernel, lead_rows),
        out_shape=(half, half),
        in_specs=[smem()] + [hbm()] * 5,
        out_specs=[hbm()] * 2,
        scratch_shapes=[
            pltpu.VMEM((rows, width), BF16),
            pltpu.VMEM((rows, 3 * local), BF16),
            pltpu.VMEM((rows, width), BF16),
            pltpu.VMEM((rows, local), BF16),
            pltpu.VMEM((width, rows), BF16),
            pltpu.VMEM((2,) + half.shape, BF16),
            pltpu.SemaphoreType.DMA((4,)),
            pltpu.SemaphoreType.DMA((width // lead_rows,)),
            pltpu.SemaphoreType.DMA((2,)),
        ],
        compiler_params=params(60),
        cost_estimate=SMALL,
        name="outer",
    )(flags, n1, gproj, gh_low, att, short)


def attention_back_kernel(
    gain, seg_row, lse, hidden, g_own, g_oth, cot, wp, att, k, q, v, w3,
    gh, gh_low, gproj, part, sums, g_qv,
    hidden_v, own_v, oth_v, cot_v, wp_v, att_v, k_v, q_v, v_v, w3_v, low_v, gproj_v, part_v,
    d_out, kt, dq_t, dk, dv, delta, seg_b, bias, in_sems, out_sems, last_sems,
):
    rows, width = hidden.shape
    local = wp.shape[0]
    blk = 32
    big = 256
    loads = [
        move(source, target, in_sems.at[n])
        for n, (source, target) in enumerate(
            [
                (hidden, hidden_v), (g_own, own_v), (g_oth, oth_v), (cot, cot_v), (wp, wp_v),
                (att, att_v), (k, k_v), (q, q_v), (v, v_v), (w3, w3_v),
            ]
        )
    ]
    for load in loads:
        load.start()
    sums[...] = jnp.zeros_like(sums)
    dk[...] = jnp.zeros_like(dk)
    dv[...] = jnp.zeros_like(dv)
    spread_clips(seg_row, seg_b)
    for load in loads[:4]:
        load.wait()

    def norm(i, carry):
        here = pl.ds(pl.multiple_of(i * blk, blk), blk)
        grad = own_v[here, :].astype(F32) + oth_v[here, :].astype(F32)
        centred, inv = row_stats(hidden_v[here, :])
        normed = centred * inv
        scaled = grad * gain[...]
        mean_one = jnp.mean(scaled, axis=-1, keepdims=True)
        mean_two = jnp.mean(scaled * normed, axis=-1, keepdims=True)
        back = cot_v[here, :].astype(F32) + inv * (scaled - mean_one - normed * mean_two)
        hidden_v[here, :] = back
        low_v[here, :] = back.astype(BF16)
        sums[0] += fold_rows(grad * normed)
        sums[1] += fold_rows(grad)
        sums[2] += fold_rows(back)
        return carry

    lax.fori_loop(0, rows // blk, norm, 0, unroll=4)
    stores = [move(hidden_v, gh, out_sems.at[0]), move(low_v, gh_low, out_sems.at[1])]
    for store in stores:
        store.start()

    for load in loads[4:7]:
        load.wait()
    heads = local // HEAD_DIM
    lane = lax.broadcasted_iota(jnp.int32, (delta.shape[0], local), 1)
    row = lax.broadcasted_iota(jnp.int32, (delta.shape[0], local), 0)
    of_head = (lane // HEAD_DIM == row).astype(BF16)
    for i in range(rows // big):
        here = pl.ds(i * big, big)
        grad_out = nt(low_v[here, :], wp_v[...]).astype(BF16)
        d_out[here, :] = grad_out
        product = grad_out.astype(F32) * att_v[here, :].astype(F32)
        coarse = product.astype(BF16)
        fine = (product - coarse.astype(F32)).astype(BF16)
        delta[:, here] = nt(of_head, coarse) + nt(of_head, fine)
        kt[:, here] = k_v[here, :].T
    for load in loads[7:9]:
        load.wait()

    def attend(j, carry):
        here, keys = key_window(j, rows)
        set_bias(bias, seg_b, seg_row, here, keys)
        for p in range(heads // 2):
            pair = pl.ds(p * LANES, LANES)
            query = two_heads(q_v[here, pair])
            grad_out = two_heads(d_out[here, pair])
            tops = jnp.concatenate([lse[pl.ds(2 * p + e, 1), here] for e in range(2)], axis=1)
            inner = jnp.concatenate([delta[pl.ds(2 * p + e, 1), here] for e in range(2)], axis=1)
            scores = nt(k_v[keys, pair], query) + bias[...]
            probs = jnp.exp(scores - tops)
            grads = (probs * (nt(v_v[keys, pair], grad_out) - inner)).astype(BF16)
            dv[keys, pair] += nn(probs.astype(BF16), grad_out)
            dk[keys, pair] += nn(grads, query)
            grad_q = nn(kt[pair, keys], grads) * SCORE_SCALE
            for e in range(2):
                lanes = slice(e * LANES, e * LANES + LANES)
                head = slice(e * HEAD_DIM, e * HEAD_DIM + HEAD_DIM)
                dq_t[pl.ds(p * LANES + e * HEAD_DIM, HEAD_DIM), here] = grad_q[head, lanes]
        return carry

    lax.fori_loop(0, rows // LANES, attend, 0)

    loads[9].wait()
    q_sum = jnp.zeros((8, local), F32)
    v_sum = jnp.zeros((8, local), F32)
    for i in range(rows // big):
        here = pl.ds(i * big, big)
        grad_q, grad_k, grad_v = dq_t[:, here].T, dk[here, :], dv[here, :]
        q_sum += fold_rows(grad_q)
        v_sum += fold_rows(grad_v)
        lows = [grad.astype(BF16) for grad in (grad_q, grad_k, grad_v)]
        total = sum(nt(low, w3_v[n]) for n, low in enumerate(lows))
        part_v[here, :] = total.astype(BF16)
        for n, low in enumerate(lows):
            gproj_v[here, pl.ds(n * local, local)] = low
        for n, (source, target) in enumerate([(part_v, part), (gproj_v, gproj)]):
            stores.append(move(source.at[here, :], target.at[here, :], last_sems.at[i, n]))
            stores[-1].start()
    g_qv[0] = q_sum
    g_qv[1] = v_sum
    for store in stores:
        store.wait()


def attention_back(hidden, cot, g_own, g_oth, gain, segment, wp, att, q, k, v, lse, w3):
    rows, width = hidden.shape
    local = wp.shape[0]
    window = min(rows, LANES + 2 * MAX_CLIP)
    tall, thin = pltpu.VMEM((rows, width), BF16), pltpu.VMEM((rows, local), BF16)
    return pl.pallas_call(
        attention_back_kernel,
        out_shape=(
            shape((rows, width), F32),
            shape((rows, width), BF16),
            shape((rows, 3 * local), BF16),
            shape((rows, width), BF16),
            shape((3, 8, width), F32),
            shape((2, 8, local), F32),
        ),
        in_specs=[vmem()] * 3 + [hbm()] * 10,
        out_specs=[hbm()] * 4 + [vmem()] * 2,
        scratch_shapes=[
            pltpu.VMEM((rows, width), F32),
            tall, tall, tall,
            pltpu.VMEM(wp.shape, BF16),
            thin, thin, thin, thin,
            pltpu.VMEM(w3.shape, BF16),
            tall,
            pltpu.VMEM((rows, 3 * local), BF16),
            tall,
            thin,
            pltpu.VMEM((local, rows), BF16),
            pltpu.VMEM((local, rows), F32),
            pltpu.VMEM((rows, local), F32),
            pltpu.VMEM((rows, local), F32),
            pltpu.VMEM((8, rows), F32),
            pltpu.VMEM((rows, LANES), F32),
            pltpu.VMEM((window, 2 * LANES), F32),
            pltpu.SemaphoreType.DMA((10,)),
            pltpu.SemaphoreType.DMA((2,)),
            pltpu.SemaphoreType.DMA((rows // 256, 2)),
        ],
        compiler_params=params(60),
        cost_estimate=SMALL,
        name="attention_back",
    )(
        gain[None, :], segment[None, :], lse,
        hidden, g_own, g_oth, cot, wp, att, k, q, v, w3,
    )


def mixed_back_kernel(blend, mixed, gh, g_own, g_oth, gain, *refs):
    outgoing, kept, sums = refs[-3:]
    ratio = blend[0]

    @pl.when(pl.program_id(0) == 0)
    def _():
        sums[...] = jnp.zeros_like(sums)

    blk = 32
    rows = mixed.shape[0]
    for i in range(rows // blk):
        here = pl.ds(i * blk, blk)
        grad = g_own[here, :].astype(F32) + g_oth[here, :].astype(F32)
        centred, inv = row_stats(mixed[here, :])
        normed = centred * inv
        scaled = grad * gain[...]
        mean_one = jnp.mean(scaled, axis=-1, keepdims=True)
        mean_two = jnp.mean(scaled * normed, axis=-1, keepdims=True)
        back = gh[here, :] + inv * (scaled - mean_one - normed * mean_two)
        outgoing[here, :] = ((1.0 - ratio) * back).astype(BF16)
        kept[here, :] = (ratio * back).astype(BF16)
        sums[0] += fold_rows(grad * normed)
        sums[1] += fold_rows(grad)


def mixed_back(blend, mixed, gh, g_own, g_oth, gain, *before):
    rows, width = mixed.shape
    block = 128
    strip = pl.BlockSpec((block, width), lambda i: (i, 0))
    flat = pl.BlockSpec((1, width), lambda i: (0, 0))
    return pl.pallas_call(
        mixed_back_kernel,
        grid=(rows // block,),
        out_shape=(
            shape((rows, width), BF16),
            shape((rows, width), BF16),
            shape((2, 8, width), F32),
        ),
        in_specs=[smem(), strip, strip, strip, strip, flat] + [hbm()] * len(before),
        out_specs=[strip, strip, pl.BlockSpec((2, 8, width), lambda i: (0, 0, 0))],
        compiler_params=params(60),
        cost_estimate=SMALL,
        name="mixed_back",
    )(blend, mixed, gh, g_own, g_oth, gain[None, :], *before)


def shards(
    tokens,
    mix_blend,
    partner,
    clip_ids,
    gain_one,
    shift_one,
    qkv_weight,
    qv_bias,
    proj_weight,
    proj_bias,
    gain_two,
    shift_two,
    in_weight,
    in_bias,
    out_weight,
    out_bias,
    cotangent,
):
    rows, width = tokens.shape
    dp_count = lax.axis_size("dp")
    both = ("dp", "mp")
    bits = dp_count.bit_length() - 1
    seq = lax.axis_index("dp")
    mp = lax.axis_index("mp")
    core = lax.rem(seq, 2)
    home = core == mp
    all_dp = range(dp_count)

    def joint(d, m):
        return 2 * d + m

    core_swap = [(d, d ^ 1) for d in all_dp]
    home_to_pair = [(joint(d, d & 1), joint(d, 1 - (d & 1))) for d in all_dp]
    pair_to_home = [(joint(d, 1 - (d & 1)), joint(d, d & 1)) for d in all_dp]
    weight_move = home_to_pair + [
        (joint(d, 1 - (d & 1)), joint(d ^ 1, 1 - (d & 1))) for d in all_dp
    ]

    def swap(value):
        return lax.ppermute(value, "dp", core_swap)

    def chip_value(value):
        return jnp.where(home, value, swap(value))

    def after(value, *others):
        return lax.optimization_barrier((value,) + others)[0]

    def half_weight(value):
        return lax.ppermute(value, both, weight_move)

    part_rows = width // dp_count
    lead = min(n for n in range(1, bits) if (part_rows << n) % 16 == 0)
    lead_rows = part_rows << lead
    across = lax.rem(seq >> lead, 2)
    flags = jnp.stack([core, home.astype(jnp.int32), across]).astype(jnp.int32)

    def taken(value, index, axis):
        return lax.dynamic_index_in_dim(value, index, axis, keepdims=False)

    seq_small = chip_value(jnp.concatenate([mix_blend, clip_ids[0].astype(F32)]))
    blend, segment = seq_small[:1], seq_small[1:]
    local = proj_weight.shape[0]
    units = in_bias.shape[0]
    half_small = jnp.concatenate([qv_bias.reshape(-1), in_bias])
    half_small = jnp.where(home, half_small, half_weight(half_small))
    bq, bv = half_small[:local], half_small[local : 2 * local]
    b_in = half_small[2 * local :]

    w3 = half_weight(qkv_weight.transpose(1, 0, 2))
    wp = half_weight(proj_weight)

    def two_way(value):
        halves = value.reshape(2, value.shape[0] // 2, value.shape[1])
        one = half_weight(taken(halves, across, 0))
        moves = [(joint(d, 1 - (d & 1)), joint(d ^ (1 << lead), 1 - (d & 1))) for d in all_dp]
        return value, one, lax.ppermute(one, both, moves)

    ids = jnp.arange(2 * dp_count, dtype=jnp.int32)
    piece = rows // (2 * 2 * dp_count)
    sent = tokens.reshape(2, dp_count, 2, piece, width)
    sent = lax.dynamic_index_in_dim(sent, mp, 2, keepdims=False)
    spread = lax.all_to_all(sent.transpose(1, 0, 2, 3), "dp", 0, 0, tiled=True)
    wanted = partner[(ids // 4) * 2 + ids % 2] * 2 + (ids // 2) % 2
    chosen = pick(spread.reshape(2 * dp_count, piece, width), wanted, w3, wp, half_small)
    partner_own = lax.all_to_all(chosen, both, 0, 0, tiled=True).reshape(rows // 2, width)
    partner_oth = swap(partner_own)

    w_in = two_way(in_weight)
    w_out = two_way(out_weight)

    tok = chip_value(tokens)
    cot = chip_value(cotangent)
    cot_t = cot.T
    mixed, n1, q, k, v, att, attn_part, lse = attention(
        blend, flags, tok, partner_own, partner_oth, segment, gain_one, shift_one,
        w3, bq, bv, wp, w_in[1], w_out[1], cot_t,
    )
    hidden, out_part, gn2_part, in_keep, in_send, out_keep, out_send, g_bin, g_bout = feed(
        lead_rows, flags, proj_bias, gain_two, shift_two, b_in,
        mixed, attn_part, swap(attn_part), cot, cot_t, *w_in, *w_out,
    )
    gn2_oth = swap(gn2_part)

    high, mid = dp_count >> (lead + 1), 1 << (lead - 1)
    pair_and_core = pair_to_home + [(joint(d, d & 1), joint(d ^ 1, d & 1)) for d in all_dp]
    pair_diagonal = [(joint(d, 1 - (d & 1)), joint(d ^ 1, d & 1)) for d in all_dp]

    def total(*terms):
        return sum(term.astype(F32) for term in terms)

    def send_across(value):
        return lax.ppermute(value, "dp", [(d, d ^ (1 << lead)) for d in all_dp])

    def send_pair(value):
        value = value.reshape(high, mid, 2, part_rows, -1)
        one = lax.ppermute(taken(value, jnp.where(home, 1 - core, core), 2), both, pair_and_core)
        two = lax.ppermute(taken(value, 1 - core, 2), both, pair_diagonal)
        held = taken(value, core, 2)
        return jnp.where(home, held, jnp.zeros_like(held)), one, two

    def far(value, *others):
        for shift, left in ((1, mid), (lead + 1, high)):
            while left > 1:
                radix = min(4, left)
                left //= radix
                value = value.reshape((-1, left, radix) + value.shape[-2:]).astype(BF16)
                spot = lax.rem(seq >> shift, radix)
                got = [
                    lax.ppermute(
                        taken(value, spot ^ flip, 2),
                        "dp",
                        [(d, d ^ (flip << shift)) for d in all_dp],
                    )
                    for flip in range(1, radix)
                ]
                value = total(taken(value, spot, 2), *after(got, *others))
                shift += radix.bit_length() - 1
        return value.reshape(value.shape[-2:])

    in_got = send_across(in_send)
    gh, gh_low, gproj, gn1_part, sums_two, g_qv = attention_back(
        hidden, cot, gn2_part, gn2_oth, gain_two, segment, wp, att, q, k, v, lse, w3
    )
    in_value = total(in_keep, after(in_got, gn1_part)).astype(BF16)
    in_terms = send_pair(in_value)
    outgoing, kept, sums_one = mixed_back(
        blend, mixed, gh, gn1_part, swap(gn1_part), gain_one, in_value
    )

    leaving = lax.dynamic_index_in_dim(
        outgoing.reshape(2, 2 * dp_count, piece, width), core, 0, keepdims=False
    )
    back = lax.all_to_all(leaving, both, 0, 0, tiled=True)
    out_got = send_across(after(out_send, leaving))

    wide = jnp.concatenate(
        [jnp.sum(sums_one, axis=1), jnp.sum(sums_two, axis=1), jnp.sum(g_bout, axis=0)[None]]
    )
    short = jnp.concatenate(
        [
            vectors.reshape(-1, dp_count, vectors.shape[-1] // dp_count)
            .transpose(1, 0, 2)
            .reshape(dp_count, -1)
            for vectors in (wide, jnp.sum(g_bin, axis=0), jnp.sum(g_qv, axis=1))
        ],
        axis=1,
    )
    short_size = short.shape[1]
    short = jnp.pad(short, ((0, 0), (0, part_rows * LANES - short_size))).astype(BF16)
    attn_keep, attn_send = outer(
        lead_rows, flags, n1, gproj, after(gh_low, leaving), att, short.reshape(width, LANES)
    )
    attn_got = send_across(attn_send)
    out_value = total(out_keep, out_got).astype(BF16)
    out_terms = send_pair(out_value)
    in_value = total(in_terms[0], *after(in_terms[1:], leaving)).astype(BF16)

    source_of = jnp.sum(
        jnp.where(partner[:, None] == ids[None, :dp_count], ids[:dp_count, None], 0),
        axis=0,
        dtype=jnp.int32,
    )
    source = source_of[ids // 2]
    wanted = (source // 2) * 4 + (ids % 2) * 2 + source % 2
    returning = pick(back, wanted, in_value, out_value, attn_send)
    returned = lax.all_to_all(
        returning.reshape(dp_count, 2, piece, width), "dp", 0, 0, tiled=True
    )
    kept = kept.reshape(2, dp_count, 2, piece, width)
    kept_got = half_weight(taken(kept, 1 - mp, 2))
    kept = jnp.where(home, taken(kept, mp, 2), kept_got)
    mine = (kept.astype(F32) + returned.transpose(1, 0, 2, 3).astype(F32)).astype(BF16)
    other = lax.ppermute(mine, "mp", [(0, 1), (1, 0)])
    first = mp == 0
    grad_tokens = jnp.stack(
        [jnp.where(first, mine, other), jnp.where(first, other, mine)], axis=2
    ).reshape(rows, width)

    out_oth = after(swap(out_part), leaving)
    block = (hidden + (out_part.astype(F32) + out_oth.astype(F32)) + out_bias).astype(BF16)
    block_out = jnp.where(home, block, half_weight(block))

    out_value = total(out_terms[0], *after(out_terms[1:], returned)).astype(BF16)
    attn_value = total(attn_keep, after(attn_got, returned)).astype(BF16)
    attn_terms = send_pair(attn_value)
    attn_value = total(*attn_terms).astype(BF16)
    sum_in = far(in_value, returned)
    sum_out = far(out_value)
    sum_attn = far(attn_value)
    sum_qkv = sum_attn[:, : 3 * local].reshape(-1, 3, local)
    sum_proj = sum_attn[:, 3 * local : 4 * local].T
    short = sum_attn[:, 4 * local :].reshape(-1)[:short_size]
    plain = short[: 6 * part_rows].reshape(6, part_rows)
    sum_bin = short[6 * part_rows : 6 * part_rows + units // dp_count]
    sum_qv = short[6 * part_rows + units // dp_count :].reshape(2, -1)
    return (
        block_out,
        grad_tokens,
        plain[0],
        plain[1],
        sum_qkv,
        sum_qv,
        sum_proj,
        plain[4],
        plain[2],
        plain[3],
        sum_in,
        sum_bin,
        sum_out.T,
        plain[5],
    )


def solution(mesh):
    return jax.shard_map(
        shards,
        mesh=mesh,
        in_specs=(
            P("dp", None),
            P("dp"),
            P(),
            P("dp", None),
            P(),
            P(),
            P(None, None, "mp"),
            P(None, "mp"),
            P("mp", None),
            P(),
            P(),
            P(),
            P(None, "mp"),
            P("mp"),
            P("mp", None),
            P(),
            P("dp", None),
        ),
        out_specs=(
            P("dp", None),
            P("dp", None),
            P("dp"),
            P("dp"),
            P("dp", None, "mp"),
            P(None, ("mp", "dp")),
            P("mp", "dp"),
            P("dp"),
            P("dp"),
            P("dp"),
            P("dp", "mp"),
            P(("mp", "dp")),
            P("mp", "dp"),
            P("dp"),
        ),
        check_vma=False,
    )
```

```python
import functools

import jax
import jax.numpy as jnp
from jax import lax
from jax.experimental import pallas as pl
from jax.experimental.pallas import tpu as pltpu
from jax.sharding import PartitionSpec as P

HEAD_DIM = 64
NORM_EPS = 1e-06
NEG_FILL = -1e30
SCORE_SCALE = HEAD_DIM ** (-0.5)
MAX_CLIP = 256
LANES = 128
F32 = jnp.float32
BF16 = jnp.bfloat16
MIB = 1 << 20
SMALL = pl.CostEstimate(flops=1 << 20, bytes_accessed=1 << 20, transcendentals=0)


def nn(left, right):
    return lax.dot_general(left, right, (((1,), (0,)), ((), ())), preferred_element_type=F32)


def nt(left, right):
    return lax.dot_general(left, right, (((1,), (1,)), ((), ())), preferred_element_type=F32)


def vmem():
    return pl.BlockSpec(memory_space=pltpu.VMEM)


def hbm():
    return pl.BlockSpec(memory_space=pltpu.HBM)


def smem():
    return pl.BlockSpec(memory_space=pltpu.SMEM)


def params(mib):
    return pltpu.CompilerParams(vmem_limit_bytes=mib * MIB)


def shape(dims, dtype):
    return jax.ShapeDtypeStruct(dims, dtype)


def row_stats(vector):
    mean = jnp.mean(vector, axis=-1, keepdims=True)
    centred = vector - mean
    spread = jnp.mean(centred * centred, axis=-1, keepdims=True)
    return centred, lax.rsqrt(spread + NORM_EPS)


def fold_rows(block):
    rows, width = block.shape
    return jnp.sum(block.reshape(rows // 8, 8, width), axis=0)


def pick_kernel(index, source, *refs):
    picked = refs[-1]

    def move(i, carry):
        picked[i] = source[index[i]]
        return carry

    lax.fori_loop(0, picked.shape[0], move, 0, unroll=4)


def pick(source, index, *after):
    dims = index.shape + source.shape[1:]
    return pl.pallas_call(
        pick_kernel,
        out_shape=shape(dims, source.dtype),
        in_specs=[smem(), vmem()] + [hbm()] * len(after),
        out_specs=vmem(),
        compiler_params=params(16),
        cost_estimate=SMALL,
        name="pick",
    )(index, source, *after)


def move(source, target, sem):
    return pltpu.make_async_copy(source, target, sem)


PARTS = 4


def part_moves(pairs, sems):
    moves = []
    for c in range(PARTS):
        row = []
        for n, (source, target) in enumerate(pairs):
            count = source.shape[0] // PARTS
            here = pl.ds(c * count, count)
            row.append(move(source.at[here, :], target.at[here, :], sems.at[n, c]))
        moves.append(row)
    return moves


def start_all(moves):
    for one in moves:
        one.start()


def wait_all(moves):
    for one in moves:
        one.wait()


def interleave(*streams):
    order = sorted(
        ((n + 0.5) / len(stream), which, n)
        for which, stream in enumerate(streams)
        for n in range(len(stream))
    )
    for _, which, n in order:
        streams[which][n]()


def spread_clips(seg_row, seg_b):
    for i in range(seg_b.shape[0] // LANES):
        here = pl.ds(i * LANES, LANES)
        seg_b[here, :] = jnp.broadcast_to(seg_row[:, here], (LANES, LANES)).T


def key_window(j, rows):
    window = min(rows, LANES + 2 * MAX_CLIP)
    here = pl.ds(pl.multiple_of(j * LANES, LANES), LANES)
    first = pl.multiple_of(jnp.clip(j * LANES - MAX_CLIP, 0, rows - window), LANES)
    return here, pl.ds(first, window)


def set_bias(bias, seg_b, seg_row, here, keys):
    filled = jnp.where(seg_b[keys, :] == seg_row[:, here], 0.0, NEG_FILL)
    bias[:, pl.ds(0, LANES)] = filled
    bias[:, pl.ds(LANES, LANES)] = filled


def two_heads(block):
    lane = lax.broadcasted_iota(jnp.int32, block.shape, 1)
    return jnp.concatenate(
        [block * (lane // HEAD_DIM == e).astype(BF16) for e in range(2)], axis=0
    )


def attention_kernel(
    blend, flags, seg_row, gain, shift, bq, bv, tok, own, oth, w3, wp, *refs
):
    mixed, n1, q, k, v, att, part, lse = refs[-29:-21]
    (
        tok_v, own_v, oth_v, w3_v, wp_v, mixed_v, n1_v, q_v, k_v, v_v, att_v, part_v,
        vt, att_t, seg_b, bias, ones, raw, in_sems, half_sems, out_sems,
    ) = refs[-21:]
    rows, width = tok.shape
    local = wp.shape[0]
    half_rows = rows // 2
    ratio = blend[0]
    blk = 32
    big = 256

    loads = [
        move(source, target, in_sems.at[n])
        for n, (source, target) in enumerate([(tok, tok_v), (w3, w3_v), (wp, wp_v)])
    ]
    halves = part_moves([(own, own_v), (oth, oth_v)], half_sems)
    loads[0].start()
    for part_of in halves:
        start_all(part_of)
    start_all(loads[1:])
    early = [
        move(source, target, out_sems.at[n])
        for n, (source, target) in enumerate(
            [(mixed_v, mixed), (n1_v, n1), (q_v, q), (k_v, k), (v_v, v)]
        )
    ]
    ones[...] = jnp.ones_like(ones)
    spread_clips(seg_row, seg_b)

    loads[0].wait()
    steps = half_rows // PARTS // blk
    for n, src, half in ((0, own_v, flags[0]), (1, oth_v, 1 - flags[0])):
        for c in range(PARTS):
            halves[c][n].wait()

            def mix(i, carry, src=src, half=half, c=c):
                low = (c * steps + i) * blk
                here = pl.ds(pl.multiple_of(half * half_rows + low, blk), blk)
                there = pl.ds(pl.multiple_of(low, blk), blk)
                mine, other = tok_v[here, :].astype(F32), src[there, :].astype(F32)
                blended = ratio * mine + (1.0 - ratio) * other
                mixed_v[here, :] = blended
                centred, inv = row_stats(blended)
                n1_v[here, :] = (centred * inv * gain[...] + shift[...]).astype(BF16)
                return carry

            lax.fori_loop(0, steps, mix, 0, unroll=True)
    start_all(early[:2])

    loads[1].wait()
    for i in range(rows // big):
        here = pl.ds(i * big, big)
        normed = n1_v[here, :]
        queries = (nn(normed, w3_v[0]) + bq[...]).astype(BF16).astype(F32)
        q_v[here, :] = (queries * SCORE_SCALE).astype(BF16)
        k_v[here, :] = nn(normed, w3_v[1]).astype(BF16)
        values = (nn(normed, w3_v[2]) + bv[...]).astype(BF16)
        v_v[here, :] = values
        vt[:, here] = values.T
    start_all(early[2:])

    pairs = local // LANES
    window = bias.shape[0]
    strip = 128

    def attend(j, carry):
        here, keys = key_window(j, rows)
        first = pl.multiple_of(keys.start, LANES)
        set_bias(bias, seg_b, seg_row, here, keys)
        tops = {}

        def make_scores(p):
            pair = pl.ds(p * LANES, LANES)
            query = two_heads(q_v[here, pair])
            slot = p % 2

            def strip_of(n):
                def run():
                    some = pl.ds(pl.multiple_of(first + n * strip, strip), strip)
                    at = pl.ds(n * strip, strip)
                    scores = nt(k_v[some, pair], query) + bias[at, :]
                    raw[slot, at, :] = scores
                    top = jnp.max(scores.reshape(strip // 8, 8, 2 * LANES), axis=0)
                    tops[p] = jnp.maximum(tops[p], top) if p in tops else top

                return run

            return [strip_of(n) for n in range(window // strip)]

        def make_output(p):
            pair = pl.ds(p * LANES, LANES)
            slot = p % 2
            state = {}

            def begin():
                state["top"] = jnp.max(tops[p], axis=0, keepdims=True)
                state["out"] = jnp.zeros((LANES, 2 * LANES), F32)
                state["total"] = jnp.zeros((16, 2 * LANES), F32)

            def strip_of(n):
                def run():
                    some = pl.ds(pl.multiple_of(first + n * strip, strip), strip)
                    at = pl.ds(n * strip, strip)
                    grown = jnp.exp(raw[slot, at, :] - state["top"]).astype(BF16)
                    state["total"] += nn(ones[:, at], grown)
                    state["out"] += nn(vt[pair, some], grown)

                return run

            def end():
                total = state["total"][:1]
                out = (state["out"] / total).astype(BF16)
                logs = state["top"] + jnp.log(total)
                for e in range(2):
                    lanes = slice(e * LANES, e * LANES + LANES)
                    head = slice(e * HEAD_DIM, e * HEAD_DIM + HEAD_DIM)
                    att_t[pl.ds(p * LANES + e * HEAD_DIM, HEAD_DIM), here] = out[head, lanes]
                    lse[pl.ds(2 * p + e, 1), here] = logs[:, lanes]

            return [begin] + [strip_of(n) for n in range(window // strip)] + [end]

        interleave(make_scores(0))
        for p in range(pairs):
            interleave(make_output(p), make_scores(p + 1) if p + 1 < pairs else [])
        return carry

    lax.fori_loop(0, rows // LANES, attend, 0)

    loads[2].wait()
    last = []
    for i in range(rows // big):
        here = pl.ds(i * big, big)
        block = att_t[:, here].T
        att_v[here, :] = block
        part_v[here, :] = nn(block, wp_v[...]).astype(BF16)
        last.append(move(part_v.at[here, :], part.at[here, :], out_sems.at[6 + i]))
        last[-1].start()
    last.append(move(att_v, att, out_sems.at[5]))
    last[-1].start()
    wait_all(early + last)


def attention(blend, flags, tok, own, oth, segment, gain, shift, w3, bq, bv, wp, *before):
    rows, width = tok.shape
    local = wp.shape[0]
    window = min(rows, LANES + 2 * MAX_CLIP)
    thin = shape((rows, local), BF16)
    tall = shape((rows, width), BF16)
    return pl.pallas_call(
        attention_kernel,
        out_shape=(
            shape((rows, width), F32), tall, thin, thin, thin, thin, tall,
            shape((local // HEAD_DIM, rows), F32),
        ),
        in_specs=[smem(), smem()] + [vmem()] * 5 + [hbm()] * 5 + [hbm()] * len(before),
        out_specs=[hbm()] * 7 + [vmem()],
        scratch_shapes=[
            pltpu.VMEM((rows, width), BF16),
            pltpu.VMEM((rows // 2, width), BF16),
            pltpu.VMEM((rows // 2, width), BF16),
            pltpu.VMEM(w3.shape, BF16),
            pltpu.VMEM(wp.shape, BF16),
            pltpu.VMEM((rows, width), F32),
            pltpu.VMEM((rows, width), BF16),
            pltpu.VMEM((rows, local), BF16),
            pltpu.VMEM((rows, local), BF16),
            pltpu.VMEM((rows, local), BF16),
            pltpu.VMEM((rows, local), BF16),
            pltpu.VMEM((rows, width), BF16),
            pltpu.VMEM((local, rows), BF16),
            pltpu.VMEM((local, rows), BF16),
            pltpu.VMEM((rows, LANES), F32),
            pltpu.VMEM((window, 2 * LANES), F32),
            pltpu.VMEM((16, window), BF16),
            pltpu.VMEM((2, window, 2 * LANES), F32),
            pltpu.SemaphoreType.DMA((3,)),
            pltpu.SemaphoreType.DMA((2, PARTS)),
            pltpu.SemaphoreType.DMA((6 + rows // 256,)),
        ],
        compiler_params=params(60),
        cost_estimate=SMALL,
        name="attention",
    )(
        blend, flags, segment[None, :], gain[None, :], shift[None, :], bq[None, :], bv[None, :],
        tok, own, oth, w3, wp, *before,
    )


ERFC_SLOPE = 0.47
ERFC_COEFFS = (
    0.2663094668265691,
    0.2480096137831850,
    0.3362712657560771,
    -0.1262288063821733,
    0.6076790117752645,
    -0.4204702410368928,
    0.0884296765518492,
)


def gelu_parts(pre):
    bell = jnp.exp(pre * pre * -0.5)
    t = 1.0 / (1.0 + jnp.abs(pre) * (ERFC_SLOPE * 0.5**0.5))
    poly = 0.5 * ERFC_COEFFS[-1]
    for coeff in ERFC_COEFFS[-2::-1]:
        poly = poly * t + 0.5 * coeff
    tail = poly * t * bell
    cdf = jnp.where(pre >= 0, 1.0 - tail, tail)
    return pre * cdf, cdf + pre * bell * 0.3989422804014327


def turn_into(target, source, blocks):
    rows = source.shape[0]
    big = 256
    for i in range(rows // big):
        here = pl.ds(i * big, big)
        turned = source[here, :].T
        for start, place, count in blocks:
            target[pl.ds(place, count), here] = turned[start : start + count]


def lead_blocks(width, lead_rows):
    runs = width // lead_rows
    return [
        (run * lead_rows, ((run % 2) * (runs // 2) + run // 2) * lead_rows, lead_rows)
        for run in range(runs)
    ]


def feed_kernel(
    in_rows, out_rows, flags, pb, gain, shift, b_in, mixed, p_own, p_oth, cot, cot_t,
    w_in, w_out, w_out_one, w_out_two,
    hidden, part, gn_part, in_keep, in_send, out_keep, out_send, g_bin, g_bout,
    mixed_v, own_v, oth_v, cot_v, cot_tv, w_in_v, w_out_v, n2, n2_t, act, gp, acc_o, acc_g,
    pre_s, grad_s, g_in, g_out, in_sems, turn_sems, weight_sems, out_sems, grad_sems,
):
    rows, width = mixed.shape
    units = w_in.shape[1]
    chunk = act.shape[2]
    blk = 32
    big = 256
    sub = 32
    home = flags[1] == 1
    across = flags[2]
    kept_out = jnp.where(home, flags[0], 1 - flags[0]) if in_rows != out_rows else across
    sides = (across, kept_out)

    loads = part_moves(
        [(mixed, mixed_v), (p_own, own_v), (p_oth, oth_v), (cot, cot_v)], in_sems
    )
    for part_of in loads:
        start_all(part_of)

    weights = [move(w_in, w_in_v, weight_sems.at[0])]
    weights[0].start()
    half = w_out.shape[0] // 2
    for n, (got, place) in enumerate([(w_out_one, across), (w_out_two, 1 - across)]):
        spot = pl.ds(pl.multiple_of(place * half, half), half)
        sem = weight_sems.at[1 + n]
        weights.append(move(w_out.at[spot, :], w_out_v.at[spot, :], sem))

        @pl.when(home)
        def _(spot=spot, sem=sem):
            move(w_out.at[spot, :], w_out_v.at[spot, :], sem).start()

        @pl.when(jnp.logical_not(home))
        def _(got=got, spot=spot, sem=sem):
            move(got, w_out_v.at[spot, :], sem).start()

    turns = [
        move(cot_t.at[pl.ds(start, count), :], cot_tv.at[pl.ds(place, count), :], turn_sems.at[n])
        for n, (start, place, count) in enumerate(lead_blocks(width, out_rows))
    ]
    start_all(turns)

    g_bout[...] = jnp.zeros_like(g_bout)
    acc_o[...] = jnp.zeros_like(acc_o)
    acc_g[...] = jnp.zeros_like(acc_g)
    steps = rows // PARTS // blk
    for c in range(PARTS):
        wait_all(loads[c])

        def norm(i, carry, c=c):
            here = pl.ds(pl.multiple_of((c * steps + i) * blk, blk), blk)
            attn = own_v[here, :].astype(F32) + oth_v[here, :].astype(F32)
            total = mixed_v[here, :] + attn + pb[...]
            mixed_v[here, :] = total
            centred, inv = row_stats(total)
            n2[here, :] = (centred * inv * gain[...] + shift[...]).astype(BF16)
            g_bout[...] += fold_rows(cot_v[here, :].astype(F32))
            return carry

        lax.fori_loop(0, steps, norm, 0, unroll=4)
    stores = [move(mixed_v, hidden, out_sems.at[0])]
    stores[0].start()
    turn_into(n2_t, n2, lead_blocks(width, in_rows))
    wait_all(weights + turns)

    spans = [slice(n, n + big) for n in range(0, chunk, big)]
    row_blocks = rows // big

    def here_of(i):
        return pl.ds(i * big, big)

    def first_products(j, i):
        def run_in(span):
            def run():
                cols = pl.ds(j * chunk + span.start, big)
                pre_s[i % 2, :, span] = nn(n2[here_of(i), :], w_in_v[:, cols])

            return run

        def run_out(span):
            def run():
                cols = pl.ds(j * chunk + span.start, big)
                grad_s[i % 2, :, span] = nt(cot_v[here_of(i), :], w_out_v[cols, :])

            return run

        return [make(span) for span in spans for make in (run_in, run_out)]

    def gelu_of(j, i, sums):
        def run_at(r, span):
            def run():
                rng = slice(r * sub, r * sub + sub)
                bias = b_in[:, pl.ds(j * chunk + span.start, big)]
                value, slope = gelu_parts(pre_s[i % 2, rng, span] + bias)
                grad = grad_s[i % 2, rng, span] * slope
                sums[span.start] += fold_rows(grad)
                spot = pl.ds(i * big + r * sub, sub)
                act[j % 2, spot, span] = value.astype(BF16)
                gp[j % 2, spot, span] = grad.astype(BF16)

            return run

        return [run_at(r, span) for r in range(big // sub) for span in spans]

    def second_products(j, i):
        units_here = pl.ds(j * chunk, chunk)

        def run_out(n):
            def run():
                cols = pl.ds(n * big, big)
                acc_o[here_of(i), cols] += nn(act[j % 2, here_of(i), :], w_out_v[units_here, cols])

            return run

        def run_in(n):
            def run():
                cols = pl.ds(n * big, big)
                acc_g[here_of(i), cols] += nt(gp[j % 2, here_of(i), :], w_in_v[cols, units_here])

            return run

        return [make(n) for n in range(width // big) for make in (run_out, run_in)]

    quarter = width // 4

    def weight_grads(j):
        def run_of(turned, right, out, n, span):
            def run():
                side, at = divmod(n, 2)
                lines = pl.ds(n * quarter, quarter)
                out[j, side, pl.ds(at * quarter, quarter), span] = nn(
                    turned[lines, :], right[j % 2, :, span]
                ).astype(BF16)

            return run

        return [
            run_of(turned, right, out, n, span)
            for turned, right, out in ((n2_t, gp, g_in), (cot_tv, act, g_out))
            for n in range(4)
            for span in spans
        ]

    def send_grads(j):
        units_here = pl.ds(j * chunk, chunk)
        for n, (buf, keep, send) in enumerate(
            [(g_in, in_keep, in_send), (g_out, out_keep, out_send)]
        ):
            for m, (side, target) in enumerate([(sides[n], keep), (1 - sides[n], send)]):
                stores.append(
                    move(buf.at[j, side], target.at[:, units_here], grad_sems.at[j, 2 * n + m])
                )
                stores[-1].start()

    chunks = units // chunk
    todo = [(j, i) for j in range(chunks) for i in range(row_blocks)]
    interleave(first_products(*todo[0]))
    waiting = []
    for n, (j, i) in enumerate(todo):
        if i == 0:
            sums = {span.start: jnp.zeros((8, big), F32) for span in spans}
        ahead = first_products(*todo[n + 1]) if n + 1 < len(todo) else []
        share = -(-len(waiting) // (row_blocks - i))
        late, waiting = waiting[:share], waiting[share:]
        interleave(gelu_of(j, i, sums), ahead + late)
        if i == row_blocks - 1:
            if j > 0:
                send_grads(j - 1)
            waiting = weight_grads(j)
            for span in spans:
                g_bin[:, pl.ds(j * chunk + span.start, big)] = sums[span.start]
        waiting = second_products(j, i) + waiting
    interleave(waiting)
    for i in range(row_blocks):
        here = here_of(i)
        oth_v[here, :] = acc_g[here, :].astype(BF16)
        own_v[here, :] = acc_o[here, :].astype(BF16)
    for n, (source, target) in enumerate([(oth_v, gn_part), (own_v, part)]):
        stores.append(move(source, target, out_sems.at[1 + n]))
        stores[-1].start()
    send_grads(chunks - 1)
    wait_all(stores)


def feed(
    in_rows, out_rows, flags, pb, gain, shift, b_in, mixed, p_own, p_oth, cot, cot_t,
    w_in, w_out, w_out_one, w_out_two,
):
    rows, width = mixed.shape
    units = w_in.shape[1]
    chunk = 512
    steps = units // chunk
    tall = shape((rows, width), BF16)
    grad = shape((width // 2, units), BF16)
    return pl.pallas_call(
        functools.partial(feed_kernel, in_rows, out_rows),
        out_shape=(
            shape((rows, width), F32), tall, tall, grad, grad, grad, grad,
            shape((8, units), F32), shape((8, width), F32),
        ),
        in_specs=[smem()] + [vmem()] * 4 + [hbm()] * 9,
        out_specs=[hbm()] * 7 + [vmem()] * 2,
        scratch_shapes=[
            pltpu.VMEM((rows, width), F32),
            pltpu.VMEM((rows, width), BF16),
            pltpu.VMEM((rows, width), BF16),
            pltpu.VMEM((rows, width), BF16),
            pltpu.VMEM((width, rows), BF16),
            pltpu.VMEM(w_in.shape, BF16),
            pltpu.VMEM(w_out.shape, BF16),
            pltpu.VMEM((rows, width), BF16),
            pltpu.VMEM((width, rows), BF16),
            pltpu.VMEM((2, rows, chunk), BF16),
            pltpu.VMEM((2, rows, chunk), BF16),
            pltpu.VMEM((rows, width), F32),
            pltpu.VMEM((rows, width), F32),
            pltpu.VMEM((2, 256, chunk), F32),
            pltpu.VMEM((2, 256, chunk), F32),
            pltpu.VMEM((steps, 2, width // 2, chunk), BF16),
            pltpu.VMEM((steps, 2, width // 2, chunk), BF16),
            pltpu.SemaphoreType.DMA((4, PARTS)),
            pltpu.SemaphoreType.DMA((width // out_rows,)),
            pltpu.SemaphoreType.DMA((3,)),
            pltpu.SemaphoreType.DMA((3,)),
            pltpu.SemaphoreType.DMA((steps, 4)),
        ],
        compiler_params=params(60),
        cost_estimate=SMALL,
        name="feed",
    )(
        flags, pb[None, :], gain[None, :], shift[None, :], b_in[None, :],
        mixed, p_own, p_oth, cot, cot_t,
        w_in, w_out, w_out_one, w_out_two,
    )


def attention_back_kernel(
    lead_rows, flags, gain, seg_row, lse, hidden, g_own, g_oth, cot, wp, att, k, q, v, w3, n1,
    gh, part, keep, send, sums, g_qv,
    hidden_v, own_v, oth_v, cot_v, wp_v, att_v, k_v, q_v, v_v, w3_v, n1_v, low_v, part_v,
    d_out, kt, dq_t, dk, dv, delta, seg_b, bias, raw, raw_g, low_p, low_g, n1_t, gh_t, grad_v, out,
    in_sems, row_sems, out_sems,
):
    rows, width = hidden.shape
    local = wp.shape[0]
    blk = 32
    big = 256
    blocks = lead_blocks(width, lead_rows)
    across = flags[2]
    row_loads = part_moves(
        [(hidden, hidden_v), (g_own, own_v), (g_oth, oth_v), (cot, cot_v)], row_sems
    )
    for part_of in row_loads:
        start_all(part_of)
    loads = [
        move(source, target, in_sems.at[n])
        for n, (source, target) in enumerate(
            [(wp, wp_v), (att, att_v), (k, k_v), (q, q_v), (v, v_v), (w3, w3_v), (n1, n1_v)]
        )
    ]
    start_all(loads)
    sums[...] = jnp.zeros_like(sums)
    dk[...] = jnp.zeros_like(dk)
    dv[...] = jnp.zeros_like(dv)
    spread_clips(seg_row, seg_b)

    steps = rows // PARTS // blk
    for c in range(PARTS):
        wait_all(row_loads[c])

        def norm(i, carry, c=c):
            here = pl.ds(pl.multiple_of((c * steps + i) * blk, blk), blk)
            grad = own_v[here, :].astype(F32) + oth_v[here, :].astype(F32)
            centred, inv = row_stats(hidden_v[here, :])
            normed = centred * inv
            scaled = grad * gain[...]
            mean_one = jnp.mean(scaled, axis=-1, keepdims=True)
            mean_two = jnp.mean(scaled * normed, axis=-1, keepdims=True)
            back = cot_v[here, :].astype(F32) + inv * (scaled - mean_one - normed * mean_two)
            hidden_v[here, :] = back
            low_v[here, :] = back.astype(BF16)
            sums[0] += fold_rows(grad * normed)
            sums[1] += fold_rows(grad)
            sums[2] += fold_rows(back)
            return carry

        lax.fori_loop(0, steps, norm, 0, unroll=4)
    stores = [move(hidden_v, gh, out_sems.at[0])]
    stores[0].start()

    wait_all(loads[:3])
    heads = local // HEAD_DIM
    lane = lax.broadcasted_iota(jnp.int32, (delta.shape[0], local), 1)
    row = lax.broadcasted_iota(jnp.int32, (delta.shape[0], local), 0)
    of_head = (lane // HEAD_DIM == row).astype(BF16)
    for i in range(rows // big):
        here = pl.ds(i * big, big)
        grad_out = nt(low_v[here, :], wp_v[...]).astype(BF16)
        d_out[here, :] = grad_out
        product = grad_out.astype(F32) * att_v[here, :].astype(F32)
        coarse = product.astype(BF16)
        fine = (product - coarse.astype(F32)).astype(BF16)
        delta[:, here] = nt(of_head, coarse) + nt(of_head, fine)
        kt[:, here] = k_v[here, :].T
    wait_all(loads[3:])

    pairs = heads // 2
    window = bias.shape[0]
    strip = 128
    strips = window // strip

    def attend(j, carry):
        here, keys = key_window(j, rows)
        first = pl.multiple_of(keys.start, LANES)
        set_bias(bias, seg_b, seg_row, here, keys)
        blocks_two = {}

        def two(p):
            if p not in blocks_two:
                pair = pl.ds(p * LANES, LANES)
                blocks_two[p] = (two_heads(q_v[here, pair]), two_heads(d_out[here, pair]))
            return blocks_two[p]

        def at_strip(n):
            return (
                pl.ds(pl.multiple_of(first + n * strip, strip), strip),
                pl.ds(n * strip, strip),
            )

        def products(p):
            pair = pl.ds(p * LANES, LANES)

            def scores(n):
                def run():
                    some, at = at_strip(n)
                    raw[p % 2, at, :] = nt(k_v[some, pair], two(p)[0])

                return run

            def grads(n):
                def run():
                    some, at = at_strip(n)
                    raw_g[p % 2, at, :] = nt(v_v[some, pair], two(p)[1])

                return run

            return [make(n) for n in range(strips) for make in (scores, grads)]

        def softmax_back(p):
            tops = jnp.concatenate([lse[pl.ds(2 * p + e, 1), here] for e in range(2)], axis=1)
            inner = jnp.concatenate([delta[pl.ds(2 * p + e, 1), here] for e in range(2)], axis=1)
            half = strip // 2

            def run_at(n):
                def run():
                    at = pl.ds(n * half, half)
                    probs = jnp.exp(raw[p % 2, at, :] + bias[at, :] - tops)
                    low_p[p % 2, at, :] = probs.astype(BF16)
                    low_g[p % 2, at, :] = (probs * (raw_g[p % 2, at, :] - inner)).astype(BF16)

                return run

            return [run_at(n) for n in range(2 * strips)]

        def sums_of(p):
            pair = pl.ds(p * LANES, LANES)

            def keys_of(n):
                def run():
                    some, at = at_strip(n)
                    dk[some, pair] += nn(low_g[p % 2, at, :], two(p)[0])

                return run

            def values_of(n):
                def run():
                    some, at = at_strip(n)
                    dv[some, pair] += nn(low_p[p % 2, at, :], two(p)[1])

                return run

            def queries():
                grad_q = nn(kt[pair, keys], low_g[p % 2]) * SCORE_SCALE
                for e in range(2):
                    lanes = slice(e * LANES, e * LANES + LANES)
                    head = slice(e * HEAD_DIM, e * HEAD_DIM + HEAD_DIM)
                    dq_t[pl.ds(p * LANES + e * HEAD_DIM, HEAD_DIM), here] = grad_q[head, lanes]

            return [make(n) for n in range(strips) for make in (keys_of, values_of)] + [queries]

        def turns():
            for target, source in ((n1_t, n1_v), (gh_t, low_v)):
                turned = source[here, :].T
                for start, place, count in blocks:
                    target[pl.ds(place, count), here] = turned[start : start + count]

        interleave(products(0), [turns])
        for p in range(pairs):
            matrix = (products(p + 1) if p + 1 < pairs else []) + (sums_of(p - 1) if p else [])
            interleave(softmax_back(p), matrix)
        interleave(sums_of(pairs - 1))
        return carry

    lax.fori_loop(0, rows // LANES, attend, 0)

    q_sum = jnp.zeros((8, local), F32)
    v_sum = jnp.zeros((8, local), F32)
    for i in range(rows // big):
        here = pl.ds(i * big, big)
        grad_q, grad_k, grad_val = dq_t[:, here].T, dk[here, :], dv[here, :]
        q_sum += fold_rows(grad_q)
        v_sum += fold_rows(grad_val)
        lows = [grad.astype(BF16) for grad in (grad_q, grad_k, grad_val)]
        total = sum(nt(low, w3_v[n]) for n, low in enumerate(lows))
        part_v[here, :] = total.astype(BF16)
        for n, low in enumerate(lows):
            grad_v[here, pl.ds(n * local, local)] = low
        stores.append(move(part_v.at[here, :], part.at[here, :], out_sems.at[1 + i]))
        stores[-1].start()
    g_qv[0] = q_sum
    g_qv[1] = v_sum
    half = width // 2
    for side in range(2):
        lines = pl.ds(side * half, half)
        for n in range(3):
            cols = pl.ds(n * local, local)
            out[side, :, cols] = nn(n1_t[lines, :], grad_v[:, cols]).astype(BF16)
        out[side, :, pl.ds(3 * local, local)] = nn(gh_t[lines, :], att_v[...]).astype(BF16)
    base = 1 + rows // big
    for n, (side, target) in enumerate([(1 - across, send), (across, keep)]):
        stores.append(move(out.at[side], target, out_sems.at[base + n]))
        stores[-1].start()
    wait_all(stores)


def attention_back(
    lead_rows, flags, hidden, cot, g_own, g_oth, gain, segment, wp, att, q, k, v, lse, w3, n1
):
    rows, width = hidden.shape
    local = wp.shape[0]
    window = min(rows, LANES + 2 * MAX_CLIP)
    tall, thin = pltpu.VMEM((rows, width), BF16), pltpu.VMEM((rows, local), BF16)
    turned = pltpu.VMEM((width, rows), BF16)
    half = (width // 2, 4 * local)
    return pl.pallas_call(
        functools.partial(attention_back_kernel, lead_rows),
        out_shape=(
            shape((rows, width), F32),
            shape((rows, width), BF16),
            shape(half, BF16),
            shape(half, BF16),
            shape((3, 8, width), F32),
            shape((2, 8, local), F32),
        ),
        in_specs=[smem()] + [vmem()] * 3 + [hbm()] * 11,
        out_specs=[hbm()] * 4 + [vmem()] * 2,
        scratch_shapes=[
            pltpu.VMEM((rows, width), F32),
            tall, tall, tall,
            pltpu.VMEM(wp.shape, BF16),
            thin, thin, thin, thin,
            pltpu.VMEM(w3.shape, BF16),
            tall, tall, tall,
            thin,
            pltpu.VMEM((local, rows), BF16),
            pltpu.VMEM((local, rows), F32),
            pltpu.VMEM((rows, local), F32),
            pltpu.VMEM((rows, local), F32),
            pltpu.VMEM((8, rows), F32),
            pltpu.VMEM((rows, LANES), F32),
            pltpu.VMEM((window, 2 * LANES), F32),
            pltpu.VMEM((2, window, 2 * LANES), F32),
            pltpu.VMEM((2, window, 2 * LANES), F32),
            pltpu.VMEM((2, window, 2 * LANES), BF16),
            pltpu.VMEM((2, window, 2 * LANES), BF16),
            turned, turned,
            pltpu.VMEM((rows, 3 * local), BF16),
            pltpu.VMEM((2,) + half, BF16),
            pltpu.SemaphoreType.DMA((7,)),
            pltpu.SemaphoreType.DMA((4, PARTS)),
            pltpu.SemaphoreType.DMA((3 + rows // 256,)),
        ],
        compiler_params=params(60),
        cost_estimate=SMALL,
        name="attention_back",
    )(
        flags, gain[None, :], segment[None, :], lse,
        hidden, g_own, g_oth, cot, wp, att, k, q, v, w3, n1,
    )


def mixed_back_kernel(blend, gain, mixed, gh, g_own, g_oth, *refs):
    outgoing, kept, sums = refs[-11:-8]
    mixed_v, gh_v, own_v, oth_v, leave_v, kept_v, in_sems, out_sems = refs[-8:]
    ratio = blend[0]
    rows = mixed.shape[0]
    blk = 32
    loads = part_moves([(mixed, mixed_v), (gh, gh_v), (g_own, own_v), (g_oth, oth_v)], in_sems)
    stores = part_moves([(leave_v, outgoing), (kept_v, kept)], out_sems)
    for part_of in loads:
        start_all(part_of)
    sums[...] = jnp.zeros_like(sums)
    steps = rows // PARTS // blk
    for c in range(PARTS):
        wait_all(loads[c])

        def norm(i, carry, c=c):
            here = pl.ds(pl.multiple_of((c * steps + i) * blk, blk), blk)
            grad = own_v[here, :].astype(F32) + oth_v[here, :].astype(F32)
            centred, inv = row_stats(mixed_v[here, :])
            normed = centred * inv
            scaled = grad * gain[...]
            mean_one = jnp.mean(scaled, axis=-1, keepdims=True)
            mean_two = jnp.mean(scaled * normed, axis=-1, keepdims=True)
            back = gh_v[here, :] + inv * (scaled - mean_one - normed * mean_two)
            leave_v[here, :] = ((1.0 - ratio) * back).astype(BF16)
            kept_v[here, :] = (ratio * back).astype(BF16)
            sums[0] += fold_rows(grad * normed)
            sums[1] += fold_rows(grad)
            return carry

        lax.fori_loop(0, steps, norm, 0, unroll=4)
        start_all(stores[c])
    for part_of in stores:
        wait_all(part_of)


def mixed_back(blend, mixed, gh, g_own, g_oth, gain, *before):
    rows, width = mixed.shape
    wide, tall = pltpu.VMEM((rows, width), F32), pltpu.VMEM((rows, width), BF16)
    return pl.pallas_call(
        mixed_back_kernel,
        out_shape=(
            shape((rows, width), BF16),
            shape((rows, width), BF16),
            shape((2, 8, width), F32),
        ),
        in_specs=[smem(), vmem()] + [hbm()] * (4 + len(before)),
        out_specs=[hbm(), hbm(), vmem()],
        scratch_shapes=[
            wide, wide, tall, tall, tall, tall,
            pltpu.SemaphoreType.DMA((4, PARTS)),
            pltpu.SemaphoreType.DMA((2, PARTS)),
        ],
        compiler_params=params(60),
        cost_estimate=SMALL,
        name="mixed_back",
    )(blend, gain[None, :], mixed, gh, g_own, g_oth, *before)


def shards(
    tokens,
    mix_blend,
    partner,
    clip_ids,
    gain_one,
    shift_one,
    qkv_weight,
    qv_bias,
    proj_weight,
    proj_bias,
    gain_two,
    shift_two,
    in_weight,
    in_bias,
    out_weight,
    out_bias,
    cotangent,
):
    rows, width = tokens.shape
    dp_count = lax.axis_size("dp")
    both = ("dp", "mp")
    bits = dp_count.bit_length() - 1
    seq = lax.axis_index("dp")
    mp = lax.axis_index("mp")
    core = lax.rem(seq, 2)
    home = core == mp
    all_dp = range(dp_count)

    def joint(d, m):
        return 2 * d + m

    core_swap = [(d, d ^ 1) for d in all_dp]
    home_to_pair = [(joint(d, d & 1), joint(d, 1 - (d & 1))) for d in all_dp]
    pair_to_home = [(joint(d, 1 - (d & 1)), joint(d, d & 1)) for d in all_dp]
    weight_move = home_to_pair + [
        (joint(d, 1 - (d & 1)), joint(d ^ 1, 1 - (d & 1))) for d in all_dp
    ]

    def swap(value):
        return lax.ppermute(value, "dp", core_swap)

    def chip_value(value):
        return jnp.where(home, value, swap(value))

    def after(value, *others):
        return lax.optimization_barrier((value,) + others)[0]

    def half_weight(value):
        return lax.ppermute(value, both, weight_move)

    part_rows = width // dp_count
    lead = min(n for n in range(1, bits) if (part_rows << n) % 16 == 0)
    lead_rows = part_rows << lead
    across = lax.rem(seq >> lead, 2)
    flags = jnp.stack([core, home.astype(jnp.int32), across]).astype(jnp.int32)

    def taken(value, index, axis):
        return lax.dynamic_index_in_dim(value, index, axis, keepdims=False)

    seq_small = chip_value(jnp.concatenate([mix_blend, clip_ids[0].astype(F32)]))
    blend, segment = seq_small[:1], seq_small[1:]
    local = proj_weight.shape[0]
    units = in_bias.shape[0]
    half_small = jnp.concatenate([qv_bias.reshape(-1), in_bias])
    half_small = jnp.where(home, half_small, half_weight(half_small))
    bq, bv = half_small[:local], half_small[local : 2 * local]
    b_in = half_small[2 * local :]

    w3 = half_weight(qkv_weight.transpose(1, 0, 2))
    wp = half_weight(proj_weight)

    def two_way(value):
        halves = value.reshape(2, value.shape[0] // 2, value.shape[1])
        one = half_weight(taken(halves, across, 0))
        moves = [(joint(d, 1 - (d & 1)), joint(d ^ (1 << lead), 1 - (d & 1))) for d in all_dp]
        return value, one, lax.ppermute(one, both, moves)

    ids = jnp.arange(2 * dp_count, dtype=jnp.int32)
    piece = rows // (2 * 2 * dp_count)
    sent = tokens.reshape(2, dp_count, 2, piece, width)
    sent = lax.dynamic_index_in_dim(sent, mp, 2, keepdims=False)
    spread = lax.all_to_all(sent.transpose(1, 0, 2, 3), "dp", 0, 0, tiled=True)
    wanted = partner[(ids // 4) * 2 + ids % 2] * 2 + (ids // 2) % 2
    chosen = pick(spread.reshape(2 * dp_count, piece, width), wanted, w3, wp, half_small)
    partner_own = lax.all_to_all(chosen, both, 0, 0, tiled=True).reshape(rows // 2, width)
    partner_oth = swap(partner_own)

    w_out = two_way(out_weight)
    w_in = half_weight(in_weight)

    tok = chip_value(tokens)
    cot = chip_value(cotangent)
    cot_t = cot.T
    mixed, n1, q, k, v, att, attn_part, lse = attention(
        blend, flags, tok, partner_own, partner_oth, segment, gain_one, shift_one,
        w3, bq, bv, wp, w_out[2], cot_t,
    )
    pair_first = part_rows % 16 == 0
    hidden, out_part, gn2_part, in_keep, in_send, out_keep, out_send, g_bin, g_bout = feed(
        lead_rows, part_rows if pair_first else lead_rows, flags, proj_bias, gain_two, shift_two, b_in,
        mixed, attn_part, swap(attn_part), cot, cot_t, w_in, *w_out,
    )
    gn2_oth = swap(gn2_part)

    high, mid = dp_count >> (lead + 1), 1 << (lead - 1)
    pair_and_core = pair_to_home + [(joint(d, d & 1), joint(d ^ 1, d & 1)) for d in all_dp]
    pair_diagonal = [(joint(d, 1 - (d & 1)), joint(d ^ 1, d & 1)) for d in all_dp]

    def total(*terms):
        return sum(term.astype(F32) for term in terms)

    def send_across(value):
        return lax.ppermute(value, "dp", [(d, d ^ (1 << lead)) for d in all_dp])

    def send_pair(value):
        value = value.reshape(high, mid, 2, part_rows, -1)
        one = lax.ppermute(taken(value, jnp.where(home, 1 - core, core), 2), both, pair_and_core)
        two = lax.ppermute(taken(value, 1 - core, 2), both, pair_diagonal)
        held = taken(value, core, 2)
        return jnp.where(home, held, jnp.zeros_like(held)), one, two

    def far(value, *others):
        for shift, left in ((1, mid), (lead + 1, high)):
            while left > 1:
                radix = min(4, left)
                left //= radix
                value = value.reshape((-1, left, radix) + value.shape[-2:]).astype(BF16)
                spot = lax.rem(seq >> shift, radix)
                got = [
                    lax.ppermute(
                        taken(value, spot ^ flip, 2),
                        "dp",
                        [(d, d ^ (flip << shift)) for d in all_dp],
                    )
                    for flip in range(1, radix)
                ]
                value = total(taken(value, spot, 2), *after(got, *others))
                shift += radix.bit_length() - 1
        return value.reshape(value.shape[-2:])

    in_got = send_across(in_send)
    if pair_first:
        out_got = [
            lax.ppermute(out_send, both, pair_and_core),
            lax.ppermute(out_keep, both, pair_diagonal),
        ]
        out_keep = jnp.where(home, out_keep, jnp.zeros_like(out_keep))
    else:
        out_got = [send_across(out_send)]
    gh, gn1_part, attn_keep, attn_send, sums_two, g_qv = attention_back(
        lead_rows, flags, hidden, cot, gn2_part, gn2_oth, gain_two, segment, wp, att, q, k, v, lse,
        w3, n1,
    )
    attn_got = send_across(attn_send)
    gn1_oth = swap(after(gn1_part, in_got, *out_got))
    outgoing, kept, sums_one = mixed_back(blend, mixed, gh, gn1_part, gn1_oth, gain_one)

    leaving = lax.dynamic_index_in_dim(
        outgoing.reshape(2, 2 * dp_count, piece, width), core, 0, keepdims=False
    )
    back = lax.all_to_all(leaving, both, 0, 0, tiled=True)
    in_terms = send_pair(total(in_keep, after(in_got, leaving)).astype(BF16))
    attn_terms = send_pair(total(attn_keep, after(attn_got, leaving)).astype(BF16))
    out_value = total(out_keep, *after(out_got, leaving)).astype(BF16)
    if pair_first:
        out_value = out_value.reshape(high, 2, mid, part_rows, units)
        out_terms = (
            taken(out_value, across, 1), send_across(taken(out_value, 1 - across, 1))
        )
    else:
        out_terms = send_pair(out_value)
    in_value = total(*after(in_terms, leaving)).astype(BF16)

    out_oth = swap(after(out_part, leaving))
    block = (hidden + (out_part.astype(F32) + out_oth.astype(F32)) + out_bias).astype(BF16)
    block_got = half_weight(block)
    block_out = jnp.where(home, block, block_got)

    source_of = jnp.sum(
        jnp.where(partner[:, None] == ids[None, :dp_count], ids[:dp_count, None], 0),
        axis=0,
        dtype=jnp.int32,
    )
    source = source_of[ids // 2]
    wanted = (source // 2) * 4 + (ids % 2) * 2 + source % 2
    returning = pick(back, wanted, in_value, block)
    returned = lax.all_to_all(
        returning.reshape(dp_count, 2, piece, width), "dp", 0, 0, tiled=True
    )
    returned = after(returned, block_got)
    kept = kept.reshape(2, dp_count, 2, piece, width)
    kept_got = half_weight(after(taken(kept, 1 - mp, 2), returning))
    kept = jnp.where(home, taken(kept, mp, 2), kept_got)
    mine = (kept.astype(F32) + returned.transpose(1, 0, 2, 3).astype(F32)).astype(BF16)
    other = lax.ppermute(mine, "mp", [(0, 1), (1, 0)])
    first = mp == 0
    grad_tokens = jnp.stack(
        [jnp.where(first, mine, other), jnp.where(first, other, mine)], axis=2
    ).reshape(rows, width)

    out_value = total(*after(out_terms, kept_got)).astype(BF16)
    attn_value = total(*after(attn_terms, kept_got)).astype(BF16)
    sum_in = far(in_value, returned)
    sum_out = far(out_value, returned)
    sum_attn = far(attn_value, returned)
    sum_qkv = sum_attn[:, : 3 * local].reshape(-1, 3, local)
    sum_proj = sum_attn[:, 3 * local :].T

    wide = jnp.concatenate(
        [jnp.sum(sums_one, axis=1), jnp.sum(sums_two, axis=1), jnp.sum(g_bout, axis=0)[None]]
    )
    wide = jnp.where(core == 0, wide, 0.0).reshape(6, dp_count, 1, part_rows)
    wide = jnp.broadcast_to(wide, (6, dp_count, 2, part_rows)).transpose(1, 2, 0, 3)
    to_half = jnp.arange(2) == core

    def half_terms(vectors):
        terms = vectors.reshape(vectors.shape[0], dp_count, 1, -1)
        terms = jnp.where(to_half[None, None, :, None], terms, 0.0)
        return terms.transpose(1, 2, 0, 3).reshape(dp_count, 2, -1)

    short = jnp.concatenate(
        [
            wide.reshape(dp_count, 2, -1),
            half_terms(jnp.sum(g_bin, axis=0)[None]),
            half_terms(jnp.sum(g_qv, axis=1)),
        ],
        axis=-1,
    ).reshape(2 * dp_count, -1)
    short = lax.all_to_all(after(short, returned), both, 0, 0, tiled=True)
    short = jnp.sum(short, axis=0)
    plain = short[: 6 * part_rows].reshape(6, part_rows)
    sum_bin = short[6 * part_rows : 6 * part_rows + units // dp_count]
    sum_qv = short[6 * part_rows + units // dp_count :].reshape(2, -1)
    return (
        block_out,
        grad_tokens,
        plain[0],
        plain[1],
        sum_qkv,
        sum_qv,
        sum_proj,
        plain[4],
        plain[2],
        plain[3],
        sum_in,
        sum_bin,
        sum_out.T,
        plain[5],
    )


def solution(mesh):
    return jax.shard_map(
        shards,
        mesh=mesh,
        in_specs=(
            P("dp", None),
            P("dp"),
            P(),
            P("dp", None),
            P(),
            P(),
            P(None, None, "mp"),
            P(None, "mp"),
            P("mp", None),
            P(),
            P(),
            P(),
            P(None, "mp"),
            P("mp"),
            P("mp", None),
            P(),
            P("dp", None),
        ),
        out_specs=(
            P("dp", None),
            P("dp", None),
            P("dp"),
            P("dp"),
            P("dp", None, "mp"),
            P(None, ("mp", "dp")),
            P("mp", "dp"),
            P("dp"),
            P("dp"),
            P("dp"),
            P("dp", "mp"),
            P(("mp", "dp")),
            P("mp", "dp"),
            P("dp"),
        ),
        check_vma=False,
    )
```

```python
import functools

import jax
import jax.numpy as jnp
from jax import lax
from jax.experimental import pallas as pl
from jax.experimental.pallas import tpu as pltpu
from jax.sharding import PartitionSpec as P

HEAD_DIM = 64
NORM_EPS = 1e-06
NEG_FILL = -1e30
SCORE_SCALE = HEAD_DIM ** (-0.5)
MAX_CLIP = 256
LANES = 128
F32 = jnp.float32
BF16 = jnp.bfloat16
MIB = 1 << 20
SMALL = pl.CostEstimate(flops=1 << 20, bytes_accessed=1 << 20, transcendentals=0)


def nn(left, right):
    return lax.dot_general(left, right, (((1,), (0,)), ((), ())), preferred_element_type=F32)


def nt(left, right):
    return lax.dot_general(left, right, (((1,), (1,)), ((), ())), preferred_element_type=F32)


def vmem():
    return pl.BlockSpec(memory_space=pltpu.VMEM)


def hbm():
    return pl.BlockSpec(memory_space=pltpu.HBM)


def smem():
    return pl.BlockSpec(memory_space=pltpu.SMEM)


def params(mib):
    return pltpu.CompilerParams(vmem_limit_bytes=mib * MIB)


def shape(dims, dtype):
    return jax.ShapeDtypeStruct(dims, dtype)


def row_stats(vector):
    mean = jnp.mean(vector, axis=-1, keepdims=True)
    centred = vector - mean
    spread = jnp.mean(centred * centred, axis=-1, keepdims=True)
    return centred, lax.rsqrt(spread + NORM_EPS)


def fold_rows(block):
    rows, width = block.shape
    return jnp.sum(block.reshape(rows // 8, 8, width), axis=0)


def pick_kernel(index, source, *refs):
    picked = refs[-1]

    def move(i, carry):
        picked[i] = source[index[i]]
        return carry

    lax.fori_loop(0, picked.shape[0], move, 0, unroll=4)


def pick(source, index, *after):
    dims = index.shape + source.shape[1:]
    return pl.pallas_call(
        pick_kernel,
        out_shape=shape(dims, source.dtype),
        in_specs=[smem(), vmem()] + [hbm()] * len(after),
        out_specs=vmem(),
        compiler_params=params(16),
        cost_estimate=SMALL,
        name="pick",
    )(index, source, *after)


def move(source, target, sem):
    return pltpu.make_async_copy(source, target, sem)


PARTS = 4


def part_moves(pairs, sems):
    moves = []
    for c in range(PARTS):
        row = []
        for n, (source, target) in enumerate(pairs):
            count = source.shape[0] // PARTS
            here = pl.ds(c * count, count)
            row.append(move(source.at[here, :], target.at[here, :], sems.at[n, c]))
        moves.append(row)
    return moves


def start_all(moves):
    for one in moves:
        one.start()


def wait_all(moves):
    for one in moves:
        one.wait()


def interleave(*streams):
    order = sorted(
        ((n + 0.5) / len(stream), which, n)
        for which, stream in enumerate(streams)
        for n in range(len(stream))
    )
    for _, which, n in order:
        streams[which][n]()


def spread_clips(seg_row, seg_b):
    for i in range(seg_b.shape[0] // LANES):
        here = pl.ds(i * LANES, LANES)
        seg_b[here, :] = jnp.broadcast_to(seg_row[:, here], (LANES, LANES)).T


def key_window(j, rows):
    window = min(rows, LANES + 2 * MAX_CLIP)
    here = pl.ds(pl.multiple_of(j * LANES, LANES), LANES)
    first = pl.multiple_of(jnp.clip(j * LANES - MAX_CLIP, 0, rows - window), LANES)
    return here, pl.ds(first, window)


def set_bias(bias, seg_b, seg_row, here, keys):
    filled = jnp.where(seg_b[keys, :] == seg_row[:, here], 0.0, NEG_FILL)
    bias[:, pl.ds(0, LANES)] = filled
    bias[:, pl.ds(LANES, LANES)] = filled


def two_heads(block):
    lane = lax.broadcasted_iota(jnp.int32, block.shape, 1)
    return jnp.concatenate(
        [block * (lane // HEAD_DIM == e).astype(BF16) for e in range(2)], axis=0
    )


def attention_kernel(
    blend, flags, seg_row, vecs, biases, tok, own, oth, w3, wp, *refs
):
    mixed, n1, q, k, v, att, part, lse = refs[-28:-20]
    (
        tok_v, own_v, oth_v, w3_v, wp_v, mixed_v, n1_v, q_v, k_v, v_v, att_v, part_v,
        vt, att_t, seg_b, bias, ones, in_sems, half_sems, out_sems,
    ) = refs[-20:]
    rows, width = tok.shape
    local = wp.shape[0]
    half_rows = rows // 2
    ratio = blend[0]
    blk = 32
    big = 256

    loads = [
        move(source, target, in_sems.at[n])
        for n, (source, target) in enumerate([(tok, tok_v), (w3, w3_v), (wp, wp_v)])
    ]
    halves = part_moves([(own, own_v), (oth, oth_v)], half_sems)
    loads[0].start()
    for part_of in halves:
        start_all(part_of)
    start_all(loads[1:])
    early = [
        move(source, target, out_sems.at[n])
        for n, (source, target) in enumerate(
            [(mixed_v, mixed), (n1_v, n1), (q_v, q), (k_v, k), (v_v, v)]
        )
    ]
    ones[...] = jnp.ones_like(ones)
    spread_clips(seg_row, seg_b)

    loads[0].wait()
    steps = half_rows // PARTS // blk
    for n, src, half in ((0, own_v, flags[0]), (1, oth_v, 1 - flags[0])):
        for c in range(PARTS):
            halves[c][n].wait()

            def mix(i, carry, src=src, half=half, c=c):
                low = (c * steps + i) * blk
                here = pl.ds(pl.multiple_of(half * half_rows + low, blk), blk)
                there = pl.ds(pl.multiple_of(low, blk), blk)
                mine, other = tok_v[here, :].astype(F32), src[there, :].astype(F32)
                blended = ratio * mine + (1.0 - ratio) * other
                mixed_v[here, :] = blended
                centred, inv = row_stats(blended)
                n1_v[here, :] = (centred * inv * vecs[0:1, :] + vecs[1:2, :]).astype(BF16)
                return carry

            lax.fori_loop(0, steps, mix, 0, unroll=True)
    start_all(early[:2])

    loads[1].wait()
    for i in range(rows // big):
        here = pl.ds(i * big, big)
        normed = n1_v[here, :]
        queries = (nn(normed, w3_v[0]) + biases[0:1, :local]).astype(BF16).astype(F32)
        q_v[here, :] = (queries * SCORE_SCALE).astype(BF16)
        k_v[here, :] = nn(normed, w3_v[1]).astype(BF16)
        values = (nn(normed, w3_v[2]) + biases[0:1, local:]).astype(BF16)
        v_v[here, :] = values
        vt[:, here] = values.T
    start_all(early[2:])

    def attend(j, carry):
        here, keys = key_window(j, rows)
        set_bias(bias, seg_b, seg_row, here, keys)
        for p in range(local // LANES):
            pair = pl.ds(p * LANES, LANES)
            scores = nt(k_v[keys, pair], two_heads(q_v[here, pair])) + bias[...]
            top = jnp.max(scores, axis=0, keepdims=True)
            grown = jnp.exp(scores - top).astype(BF16)
            total = nn(ones[...], grown)[:1]
            out = (nn(vt[pair, keys], grown) / total).astype(BF16)
            logs = top + jnp.log(total)
            for e in range(2):
                lanes = slice(e * LANES, e * LANES + LANES)
                head = slice(e * HEAD_DIM, e * HEAD_DIM + HEAD_DIM)
                att_t[pl.ds(p * LANES + e * HEAD_DIM, HEAD_DIM), here] = out[head, lanes]
                lse[pl.ds(2 * p + e, 1), here] = logs[:, lanes]
        return carry

    lax.fori_loop(0, rows // LANES, attend, 0)

    loads[2].wait()
    last = []
    for i in range(rows // big):
        here = pl.ds(i * big, big)
        block = att_t[:, here].T
        att_v[here, :] = block
        part_v[here, :] = nn(block, wp_v[...]).astype(BF16)
        last.append(move(part_v.at[here, :], part.at[here, :], out_sems.at[6 + i]))
        last[-1].start()
    last.append(move(att_v, att, out_sems.at[5]))
    last[-1].start()
    wait_all(early + last)


def attention(blend, flags, segment, vecs, biases, tok, own, oth, w3, wp, *before):
    rows, width = tok.shape
    local = wp.shape[0]
    window = min(rows, LANES + 2 * MAX_CLIP)
    thin = shape((rows, local), BF16)
    tall = shape((rows, width), BF16)
    return pl.pallas_call(
        attention_kernel,
        out_shape=(
            shape((rows, width), F32), tall, thin, thin, thin, thin, tall,
            shape((local // HEAD_DIM, rows), F32),
        ),
        in_specs=[smem(), smem()] + [vmem()] * 3 + [hbm()] * (5 + len(before)),
        out_specs=[hbm()] * 7 + [vmem()],
        scratch_shapes=[
            pltpu.VMEM((rows, width), BF16),
            pltpu.VMEM((rows // 2, width), BF16),
            pltpu.VMEM((rows // 2, width), BF16),
            pltpu.VMEM(w3.shape, BF16),
            pltpu.VMEM(wp.shape, BF16),
            pltpu.VMEM((rows, width), F32),
            pltpu.VMEM((rows, width), BF16),
            pltpu.VMEM((rows, local), BF16),
            pltpu.VMEM((rows, local), BF16),
            pltpu.VMEM((rows, local), BF16),
            pltpu.VMEM((rows, local), BF16),
            pltpu.VMEM((rows, width), BF16),
            pltpu.VMEM((local, rows), BF16),
            pltpu.VMEM((local, rows), BF16),
            pltpu.VMEM((rows, LANES), F32),
            pltpu.VMEM((window, 2 * LANES), F32),
            pltpu.VMEM((16, window), BF16),
            pltpu.SemaphoreType.DMA((3,)),
            pltpu.SemaphoreType.DMA((2, PARTS)),
            pltpu.SemaphoreType.DMA((6 + rows // 256,)),
        ],
        compiler_params=params(60),
        cost_estimate=SMALL,
        name="attention",
    )(
        blend, flags, segment, vecs, biases, tok, own, oth, w3, wp, *before,
    )


ERFC_SLOPE = 0.47
ERFC_COEFFS = (
    0.2663094668265691,
    0.2480096137831850,
    0.3362712657560771,
    -0.1262288063821733,
    0.6076790117752645,
    -0.4204702410368928,
    0.0884296765518492,
)


def gelu_parts(pre):
    bell = jnp.exp(pre * pre * -0.5)
    t = 1.0 / (1.0 + jnp.abs(pre) * (ERFC_SLOPE * 0.5**0.5))
    poly = 0.5 * ERFC_COEFFS[-1]
    for coeff in ERFC_COEFFS[-2::-1]:
        poly = poly * t + 0.5 * coeff
    tail = poly * t * bell
    cdf = jnp.where(pre >= 0, 1.0 - tail, tail)
    return pre * cdf, cdf + pre * bell * 0.3989422804014327


def turn_into(target, source, blocks):
    rows = source.shape[0]
    big = 256
    for i in range(rows // big):
        here = pl.ds(i * big, big)
        turned = source[here, :].T
        for start, place, count in blocks:
            target[pl.ds(place, count), here] = turned[start : start + count]


def lead_blocks(width, lead_rows):
    runs = width // lead_rows
    return [
        (run * lead_rows, ((run % 2) * (runs // 2) + run // 2) * lead_rows, lead_rows)
        for run in range(runs)
    ]


def feed_kernel(
    in_rows, out_rows, flags, vecs, biases, mixed, p_own, p_oth, cot, cot_t,
    w_in, w_out, w_out_one, w_out_two,
    hidden, part, gn_part, in_keep, in_send, out_keep, out_send, g_bin, g_bout,
    mixed_v, own_v, oth_v, cot_v, cot_tv, w_in_v, w_out_v, n2, n2_t, act, gp,
    g_in, g_out, in_sems, turn_sems, weight_sems, out_sems, grad_sems,
):
    rows, width = mixed.shape
    units = w_in.shape[1]
    blk = 32
    big = 256
    sub = 16
    home = flags[1] == 1
    across = flags[2]
    kept_out = jnp.where(home, flags[0], 1 - flags[0]) if in_rows != out_rows else across
    sides = (across, kept_out)

    loads = part_moves(
        [(mixed, mixed_v), (p_own, own_v), (p_oth, oth_v), (cot, cot_v)], in_sems
    )
    for part_of in loads:
        start_all(part_of)

    weights = [move(w_in, w_in_v, weight_sems.at[0])]
    weights[0].start()
    half = w_out.shape[0] // 2
    for n, (got, place) in enumerate([(w_out_one, across), (w_out_two, 1 - across)]):
        spot = pl.ds(pl.multiple_of(place * half, half), half)
        sem = weight_sems.at[1 + n]
        weights.append(move(w_out.at[spot, :], w_out_v.at[spot, :], sem))

        @pl.when(home)
        def _(spot=spot, sem=sem):
            move(w_out.at[spot, :], w_out_v.at[spot, :], sem).start()

        @pl.when(jnp.logical_not(home))
        def _(got=got, spot=spot, sem=sem):
            move(got, w_out_v.at[spot, :], sem).start()

    turns = [
        move(cot_t.at[pl.ds(start, count), :], cot_tv.at[pl.ds(place, count), :], turn_sems.at[n])
        for n, (start, place, count) in enumerate(lead_blocks(width, out_rows))
    ]
    start_all(turns)

    g_bout[...] = jnp.zeros_like(g_bout)
    steps = rows // PARTS // blk
    for c in range(PARTS):
        wait_all(loads[c])

        def norm(i, carry, c=c):
            here = pl.ds(pl.multiple_of((c * steps + i) * blk, blk), blk)
            attn = own_v[here, :].astype(F32) + oth_v[here, :].astype(F32)
            total = mixed_v[here, :] + attn + vecs[4:5, :]
            mixed_v[here, :] = total
            centred, inv = row_stats(total)
            n2[here, :] = (centred * inv * vecs[2:3, :] + vecs[3:4, :]).astype(BF16)
            g_bout[...] += fold_rows(cot_v[here, :].astype(F32))
            return carry

        lax.fori_loop(0, steps, norm, 0, unroll=4)
    stores = [move(mixed_v, hidden, out_sems.at[0, 0])]
    stores[0].start()
    turn_into(n2_t, n2, lead_blocks(width, in_rows))
    wait_all(weights)

    sums = [jnp.zeros((8, width), F32) for _ in range(units // width)]
    for i in range(rows // big):
        here = pl.ds(i * big, big)
        for j in range(units // width):
            cols = pl.ds(j * width, width)
            pre_all = nn(n2[here, :], w_in_v[:, cols])
            grad_all = nt(cot_v[here, :], w_out_v[cols, :])
            for s in range(big // sub):
                rng = slice(s * sub, s * sub + sub)
                value, slope = gelu_parts(pre_all[rng] + biases[1 + j : 2 + j, :])
                grad = grad_all[rng] * slope
                sums[j] += fold_rows(grad)
                spot = pl.ds(i * big + s * sub, sub)
                act[spot, cols] = value.astype(BF16)
                gp[spot, cols] = grad.astype(BF16)
        oth_v[here, :] = nt(gp[here, :], w_in_v[...]).astype(BF16)
        own_v[here, :] = nn(act[here, :], w_out_v[...]).astype(BF16)
        for n, (source, target) in enumerate([(oth_v, gn_part), (own_v, part)]):
            stores.append(move(source.at[here, :], target.at[here, :], out_sems.at[1 + n, i]))
            stores[-1].start()
    for j in range(units // width):
        g_bin[:, pl.ds(j * width, width)] = sums[j]

    wait_all(turns)
    half = width // 2
    for n, (turned, right, buf, keep, send) in enumerate(
        [(n2_t, gp, g_in, in_keep, in_send), (cot_tv, act, g_out, out_keep, out_send)]
    ):
        for side in range(2):
            lines = pl.ds(side * half, half)
            for j in range(units // width):
                cols = pl.ds(j * width, width)
                buf[side, :, cols] = nn(turned[lines, :], right[:, cols]).astype(BF16)
        for m, (side, target) in enumerate([(1 - sides[n], send), (sides[n], keep)]):
            stores.append(move(buf.at[side], target, grad_sems.at[n, m]))
            stores[-1].start()
    wait_all(stores)


def feed(
    in_rows, out_rows, flags, vecs, biases, mixed, p_own, p_oth, cot, cot_t,
    w_in, w_out, w_out_one, w_out_two,
):
    rows, width = mixed.shape
    units = w_in.shape[1]
    tall = shape((rows, width), BF16)
    grad = shape((width // 2, units), BF16)
    return pl.pallas_call(
        functools.partial(feed_kernel, in_rows, out_rows),
        out_shape=(
            shape((rows, width), F32), tall, tall, grad, grad, grad, grad,
            shape((8, units), F32), shape((8, width), F32),
        ),
        in_specs=[smem()] + [vmem()] * 2 + [hbm()] * 9,
        out_specs=[hbm()] * 7 + [vmem()] * 2,
        scratch_shapes=[
            pltpu.VMEM((rows, width), F32),
            pltpu.VMEM((rows, width), BF16),
            pltpu.VMEM((rows, width), BF16),
            pltpu.VMEM((rows, width), BF16),
            pltpu.VMEM((width, rows), BF16),
            pltpu.VMEM(w_in.shape, BF16),
            pltpu.VMEM(w_out.shape, BF16),
            pltpu.VMEM((rows, width), BF16),
            pltpu.VMEM((width, rows), BF16),
            pltpu.VMEM((rows, units), BF16),
            pltpu.VMEM((rows, units), BF16),
            pltpu.VMEM((2, width // 2, units), BF16),
            pltpu.VMEM((2, width // 2, units), BF16),
            pltpu.SemaphoreType.DMA((4, PARTS)),
            pltpu.SemaphoreType.DMA((width // out_rows,)),
            pltpu.SemaphoreType.DMA((3,)),
            pltpu.SemaphoreType.DMA((3, rows // 256)),
            pltpu.SemaphoreType.DMA((2, 2)),
        ],
        compiler_params=params(60),
        cost_estimate=SMALL,
        name="feed",
    )(
        flags, vecs, biases, mixed, p_own, p_oth, cot, cot_t,
        w_in, w_out, w_out_one, w_out_two,
    )


def attention_back_kernel(
    lead_rows, flags, vecs, seg_row, lse, hidden, g_own, g_oth, cot, wp, att, k, q, v, w3, n1,
    gh, part, keep, send, sums, g_qv,
    hidden_v, own_v, oth_v, cot_v, wp_v, att_v, k_v, q_v, v_v, w3_v, n1_v, low_v, part_v,
    d_out, kt, dq_t, dk, dv, delta, seg_b, bias, raw, raw_g, low_p, low_g, n1_t, gh_t, grad_v, out,
    in_sems, row_sems, out_sems,
):
    rows, width = hidden.shape
    local = wp.shape[0]
    blk = 32
    big = 256
    blocks = lead_blocks(width, lead_rows)
    across = flags[2]
    row_loads = part_moves(
        [(hidden, hidden_v), (g_own, own_v), (g_oth, oth_v), (cot, cot_v)], row_sems
    )
    for part_of in row_loads:
        start_all(part_of)
    loads = [
        move(source, target, in_sems.at[n])
        for n, (source, target) in enumerate(
            [(wp, wp_v), (att, att_v), (k, k_v), (q, q_v), (v, v_v), (w3, w3_v), (n1, n1_v)]
        )
    ]
    start_all(loads)
    sums[...] = jnp.zeros_like(sums)
    dk[...] = jnp.zeros_like(dk)
    dv[...] = jnp.zeros_like(dv)
    spread_clips(seg_row, seg_b)

    steps = rows // PARTS // blk
    for c in range(PARTS):
        wait_all(row_loads[c])

        def norm(i, carry, c=c):
            here = pl.ds(pl.multiple_of((c * steps + i) * blk, blk), blk)
            grad = own_v[here, :].astype(F32) + oth_v[here, :].astype(F32)
            centred, inv = row_stats(hidden_v[here, :])
            normed = centred * inv
            scaled = grad * vecs[2:3, :]
            mean_one = jnp.mean(scaled, axis=-1, keepdims=True)
            mean_two = jnp.mean(scaled * normed, axis=-1, keepdims=True)
            back = cot_v[here, :].astype(F32) + inv * (scaled - mean_one - normed * mean_two)
            hidden_v[here, :] = back
            low_v[here, :] = back.astype(BF16)
            sums[0] += fold_rows(grad * normed)
            sums[1] += fold_rows(grad)
            sums[2] += fold_rows(back)
            return carry

        lax.fori_loop(0, steps, norm, 0, unroll=4)
    stores = [move(hidden_v, gh, out_sems.at[0])]
    stores[0].start()

    wait_all(loads[:3])
    heads = local // HEAD_DIM
    lane = lax.broadcasted_iota(jnp.int32, (delta.shape[0], local), 1)
    row = lax.broadcasted_iota(jnp.int32, (delta.shape[0], local), 0)
    of_head = (lane // HEAD_DIM == row).astype(BF16)
    for i in range(rows // big):
        here = pl.ds(i * big, big)
        grad_out = nt(low_v[here, :], wp_v[...]).astype(BF16)
        d_out[here, :] = grad_out
        product = grad_out.astype(F32) * att_v[here, :].astype(F32)
        coarse = product.astype(BF16)
        fine = (product - coarse.astype(F32)).astype(BF16)
        delta[:, here] = nt(of_head, coarse) + nt(of_head, fine)
        kt[:, here] = k_v[here, :].T
    wait_all(loads[3:])

    pairs = heads // 2
    window = bias.shape[0]
    strip = 128
    strips = window // strip

    def attend(j, carry):
        here, keys = key_window(j, rows)
        first = pl.multiple_of(keys.start, LANES)
        set_bias(bias, seg_b, seg_row, here, keys)
        blocks_two = {}

        def two(p):
            if p not in blocks_two:
                pair = pl.ds(p * LANES, LANES)
                blocks_two[p] = (two_heads(q_v[here, pair]), two_heads(d_out[here, pair]))
            return blocks_two[p]

        def at_strip(n):
            return (
                pl.ds(pl.multiple_of(first + n * strip, strip), strip),
                pl.ds(n * strip, strip),
            )

        def products(p):
            pair = pl.ds(p * LANES, LANES)

            def scores(n):
                def run():
                    some, at = at_strip(n)
                    raw[p % 2, at, :] = nt(k_v[some, pair], two(p)[0])

                return run

            def grads(n):
                def run():
                    some, at = at_strip(n)
                    raw_g[p % 2, at, :] = nt(v_v[some, pair], two(p)[1])

                return run

            return [make(n) for n in range(strips) for make in (scores, grads)]

        def softmax_back(p):
            tops = jnp.concatenate([lse[pl.ds(2 * p + e, 1), here] for e in range(2)], axis=1)
            inner = jnp.concatenate([delta[pl.ds(2 * p + e, 1), here] for e in range(2)], axis=1)
            half = strip // 2

            def run_at(n):
                def run():
                    at = pl.ds(n * half, half)
                    probs = jnp.exp(raw[p % 2, at, :] + bias[at, :] - tops)
                    low_p[p % 2, at, :] = probs.astype(BF16)
                    low_g[p % 2, at, :] = (probs * (raw_g[p % 2, at, :] - inner)).astype(BF16)

                return run

            return [run_at(n) for n in range(2 * strips)]

        def sums_of(p):
            pair = pl.ds(p * LANES, LANES)

            def keys_of(n):
                def run():
                    some, at = at_strip(n)
                    dk[some, pair] += nn(low_g[p % 2, at, :], two(p)[0])

                return run

            def values_of(n):
                def run():
                    some, at = at_strip(n)
                    dv[some, pair] += nn(low_p[p % 2, at, :], two(p)[1])

                return run

            def queries():
                grad_q = nn(kt[pair, keys], low_g[p % 2]) * SCORE_SCALE
                for e in range(2):
                    lanes = slice(e * LANES, e * LANES + LANES)
                    head = slice(e * HEAD_DIM, e * HEAD_DIM + HEAD_DIM)
                    dq_t[pl.ds(p * LANES + e * HEAD_DIM, HEAD_DIM), here] = grad_q[head, lanes]

            return [make(n) for n in range(strips) for make in (keys_of, values_of)] + [queries]

        def turns():
            for target, source in ((n1_t, n1_v), (gh_t, low_v)):
                turned = source[here, :].T
                for start, place, count in blocks:
                    target[pl.ds(place, count), here] = turned[start : start + count]

        interleave(products(0), [turns])
        for p in range(pairs):
            matrix = (products(p + 1) if p + 1 < pairs else []) + (sums_of(p - 1) if p else [])
            interleave(softmax_back(p), matrix)
        interleave(sums_of(pairs - 1))
        return carry

    lax.fori_loop(0, rows // LANES, attend, 0)

    q_sum = jnp.zeros((8, local), F32)
    v_sum = jnp.zeros((8, local), F32)
    for i in range(rows // big):
        here = pl.ds(i * big, big)
        grad_q, grad_k, grad_val = dq_t[:, here].T, dk[here, :], dv[here, :]
        q_sum += fold_rows(grad_q)
        v_sum += fold_rows(grad_val)
        lows = [grad.astype(BF16) for grad in (grad_q, grad_k, grad_val)]
        total = sum(nt(low, w3_v[n]) for n, low in enumerate(lows))
        part_v[here, :] = total.astype(BF16)
        for n, low in enumerate(lows):
            grad_v[here, pl.ds(n * local, local)] = low
        stores.append(move(part_v.at[here, :], part.at[here, :], out_sems.at[1 + i]))
        stores[-1].start()
    g_qv[0] = q_sum
    g_qv[1] = v_sum
    half = width // 2
    for side in range(2):
        lines = pl.ds(side * half, half)
        for n in range(3):
            cols = pl.ds(n * local, local)
            out[side, :, cols] = nn(n1_t[lines, :], grad_v[:, cols]).astype(BF16)
        out[side, :, pl.ds(3 * local, local)] = nn(gh_t[lines, :], att_v[...]).astype(BF16)
    base = 1 + rows // big
    for n, (side, target) in enumerate([(1 - across, send), (across, keep)]):
        stores.append(move(out.at[side], target, out_sems.at[base + n]))
        stores[-1].start()
    wait_all(stores)


def attention_back(
    lead_rows, flags, vecs, segment, hidden, cot, g_own, g_oth, wp, att, q, k, v, lse, w3, n1
):
    rows, width = hidden.shape
    local = wp.shape[0]
    window = min(rows, LANES + 2 * MAX_CLIP)
    tall, thin = pltpu.VMEM((rows, width), BF16), pltpu.VMEM((rows, local), BF16)
    turned = pltpu.VMEM((width, rows), BF16)
    half = (width // 2, 4 * local)
    return pl.pallas_call(
        functools.partial(attention_back_kernel, lead_rows),
        out_shape=(
            shape((rows, width), F32),
            shape((rows, width), BF16),
            shape(half, BF16),
            shape(half, BF16),
            shape((3, 8, width), F32),
            shape((2, 8, local), F32),
        ),
        in_specs=[smem()] + [vmem()] * 3 + [hbm()] * 11,
        out_specs=[hbm()] * 4 + [vmem()] * 2,
        scratch_shapes=[
            pltpu.VMEM((rows, width), F32),
            tall, tall, tall,
            pltpu.VMEM(wp.shape, BF16),
            thin, thin, thin, thin,
            pltpu.VMEM(w3.shape, BF16),
            tall, tall, tall,
            thin,
            pltpu.VMEM((local, rows), BF16),
            pltpu.VMEM((local, rows), F32),
            pltpu.VMEM((rows, local), F32),
            pltpu.VMEM((rows, local), F32),
            pltpu.VMEM((8, rows), F32),
            pltpu.VMEM((rows, LANES), F32),
            pltpu.VMEM((window, 2 * LANES), F32),
            pltpu.VMEM((2, window, 2 * LANES), F32),
            pltpu.VMEM((2, window, 2 * LANES), F32),
            pltpu.VMEM((2, window, 2 * LANES), BF16),
            pltpu.VMEM((2, window, 2 * LANES), BF16),
            turned, turned,
            pltpu.VMEM((rows, 3 * local), BF16),
            pltpu.VMEM((2,) + half, BF16),
            pltpu.SemaphoreType.DMA((7,)),
            pltpu.SemaphoreType.DMA((4, PARTS)),
            pltpu.SemaphoreType.DMA((3 + rows // 256,)),
        ],
        compiler_params=params(60),
        cost_estimate=SMALL,
        name="attention_back",
    )(
        flags, vecs, segment, lse,
        hidden, g_own, g_oth, cot, wp, att, k, q, v, w3, n1,
    )


def mixed_back_kernel(blend, vecs, mixed, gh, g_own, g_oth, *refs):
    outgoing, kept, sums = refs[-11:-8]
    mixed_v, gh_v, own_v, oth_v, leave_v, kept_v, in_sems, out_sems = refs[-8:]
    ratio = blend[0]
    rows = mixed.shape[0]
    blk = 32
    loads = part_moves([(mixed, mixed_v), (gh, gh_v), (g_own, own_v), (g_oth, oth_v)], in_sems)
    stores = part_moves([(leave_v, outgoing), (kept_v, kept)], out_sems)
    for part_of in loads:
        start_all(part_of)
    sums[...] = jnp.zeros_like(sums)
    steps = rows // PARTS // blk
    for c in range(PARTS):
        wait_all(loads[c])

        def norm(i, carry, c=c):
            here = pl.ds(pl.multiple_of((c * steps + i) * blk, blk), blk)
            grad = own_v[here, :].astype(F32) + oth_v[here, :].astype(F32)
            centred, inv = row_stats(mixed_v[here, :])
            normed = centred * inv
            scaled = grad * vecs[0:1, :]
            mean_one = jnp.mean(scaled, axis=-1, keepdims=True)
            mean_two = jnp.mean(scaled * normed, axis=-1, keepdims=True)
            back = gh_v[here, :] + inv * (scaled - mean_one - normed * mean_two)
            leave_v[here, :] = ((1.0 - ratio) * back).astype(BF16)
            kept_v[here, :] = (ratio * back).astype(BF16)
            sums[0] += fold_rows(grad * normed)
            sums[1] += fold_rows(grad)
            return carry

        lax.fori_loop(0, steps, norm, 0, unroll=4)
        start_all(stores[c])
    for part_of in stores:
        wait_all(part_of)


def mixed_back(blend, vecs, mixed, gh, g_own, g_oth, *before):
    rows, width = mixed.shape
    wide, tall = pltpu.VMEM((rows, width), F32), pltpu.VMEM((rows, width), BF16)
    return pl.pallas_call(
        mixed_back_kernel,
        out_shape=(
            shape((rows, width), BF16),
            shape((rows, width), BF16),
            shape((2, 8, width), F32),
        ),
        in_specs=[smem(), vmem()] + [hbm()] * (4 + len(before)),
        out_specs=[hbm(), hbm(), vmem()],
        scratch_shapes=[
            wide, wide, tall, tall, tall, tall,
            pltpu.SemaphoreType.DMA((4, PARTS)),
            pltpu.SemaphoreType.DMA((2, PARTS)),
        ],
        compiler_params=params(60),
        cost_estimate=SMALL,
        name="mixed_back",
    )(blend, vecs, mixed, gh, g_own, g_oth, *before)


def shards(
    tokens,
    mix_blend,
    partner,
    clip_ids,
    gain_one,
    shift_one,
    qkv_weight,
    qv_bias,
    proj_weight,
    proj_bias,
    gain_two,
    shift_two,
    in_weight,
    in_bias,
    out_weight,
    out_bias,
    cotangent,
):
    rows, width = tokens.shape
    dp_count = lax.axis_size("dp")
    both = ("dp", "mp")
    bits = dp_count.bit_length() - 1
    seq = lax.axis_index("dp")
    mp = lax.axis_index("mp")
    core = lax.rem(seq, 2)
    home = core == mp
    all_dp = range(dp_count)

    def joint(d, m):
        return 2 * d + m

    core_swap = [(d, d ^ 1) for d in all_dp]
    home_to_pair = [(joint(d, d & 1), joint(d, 1 - (d & 1))) for d in all_dp]
    pair_to_home = [(joint(d, 1 - (d & 1)), joint(d, d & 1)) for d in all_dp]
    weight_move = home_to_pair + [
        (joint(d, 1 - (d & 1)), joint(d ^ 1, 1 - (d & 1))) for d in all_dp
    ]

    def swap(value):
        return lax.ppermute(value, "dp", core_swap)

    def chip_value(value):
        return jnp.where(home, value, swap(value))

    def after(value, *others):
        return lax.optimization_barrier((value,) + others)[0]

    def half_weight(value):
        return lax.ppermute(value, both, weight_move)

    part_rows = width // dp_count
    lead = min(n for n in range(1, bits) if (part_rows << n) % 16 == 0)
    lead_rows = part_rows << lead
    across = lax.rem(seq >> lead, 2)
    flags = jnp.stack([core, home.astype(jnp.int32), across]).astype(jnp.int32)

    def taken(value, index, axis):
        return lax.dynamic_index_in_dim(value, index, axis, keepdims=False)

    seq_small = chip_value(jnp.concatenate([mix_blend, clip_ids[0].astype(F32)]))
    blend, segment = seq_small[:1], seq_small[1:].reshape(1, rows)
    local = proj_weight.shape[0]
    units = in_bias.shape[0]
    half_small = jnp.concatenate([qv_bias.reshape(-1), in_bias])
    half_small = jnp.where(home, half_small, half_weight(half_small))
    biases = half_small.reshape(-1, width)
    vecs = jnp.stack([gain_one, shift_one, gain_two, shift_two, proj_bias])

    w3 = half_weight(qkv_weight.transpose(1, 0, 2))
    wp = half_weight(proj_weight)

    def two_way(value):
        halves = value.reshape(2, value.shape[0] // 2, value.shape[1])
        one = half_weight(taken(halves, across, 0))
        moves = [(joint(d, 1 - (d & 1)), joint(d ^ (1 << lead), 1 - (d & 1))) for d in all_dp]
        return value, one, lax.ppermute(one, both, moves)

    ids = jnp.arange(2 * dp_count, dtype=jnp.int32)
    piece = rows // (2 * 2 * dp_count)
    sent = tokens.reshape(2, dp_count, 2, piece, width)
    sent = lax.dynamic_index_in_dim(sent, mp, 2, keepdims=False)
    spread = lax.all_to_all(sent.transpose(1, 0, 2, 3), "dp", 0, 0, tiled=True)
    wanted = partner[(ids // 4) * 2 + ids % 2] * 2 + (ids // 2) % 2
    chosen = pick(spread.reshape(2 * dp_count, piece, width), wanted, w3, wp, half_small)
    partner_own = lax.all_to_all(chosen, both, 0, 0, tiled=True).reshape(rows // 2, width)
    w_out = two_way(out_weight)
    w_in = half_weight(after(in_weight, w_out[1]))

    tok = chip_value(tokens)
    cot = chip_value(cotangent)
    cot_t = cot.T
    partner_oth = swap(after(partner_own, tok, cot_t, vecs))

    mixed, n1, q, k, v, att, attn_part, lse = attention(
        blend, flags, segment, vecs, biases, tok, partner_own, partner_oth, w3, wp, w_out[2]
    )
    pair_first = part_rows % 16 == 0
    hidden, out_part, gn2_part, in_keep, in_send, out_keep, out_send, g_bin, g_bout = feed(
        lead_rows, part_rows if pair_first else lead_rows, flags, vecs, biases,
        mixed, attn_part, swap(attn_part), cot, cot_t, w_in, *w_out,
    )
    gn2_oth = swap(gn2_part)

    high, mid = dp_count >> (lead + 1), 1 << (lead - 1)
    pair_and_core = pair_to_home + [(joint(d, d & 1), joint(d ^ 1, d & 1)) for d in all_dp]
    pair_diagonal = [(joint(d, 1 - (d & 1)), joint(d ^ 1, d & 1)) for d in all_dp]

    def total(*terms):
        return sum(term.astype(F32) for term in terms)

    def send_across(value):
        return lax.ppermute(value, "dp", [(d, d ^ (1 << lead)) for d in all_dp])

    def send_pair(value):
        value = value.reshape(high, mid, 2, part_rows, -1)
        one = lax.ppermute(taken(value, jnp.where(home, 1 - core, core), 2), both, pair_and_core)
        two = lax.ppermute(taken(value, 1 - core, 2), both, pair_diagonal)
        held = taken(value, core, 2)
        return jnp.where(home, held, jnp.zeros_like(held)), one, two

    def far(value, *others):
        for shift, left in ((1, mid), (lead + 1, high)):
            while left > 1:
                radix = min(4, left)
                left //= radix
                value = value.reshape((-1, left, radix) + value.shape[-2:]).astype(BF16)
                spot = lax.rem(seq >> shift, radix)
                got = [
                    lax.ppermute(
                        taken(value, spot ^ flip, 2),
                        "dp",
                        [(d, d ^ (flip << shift)) for d in all_dp],
                    )
                    for flip in range(1, radix)
                ]
                value = total(taken(value, spot, 2), *after(got, *others))
                shift += radix.bit_length() - 1
        return value.reshape(value.shape[-2:])

    in_got = send_across(in_send)
    if pair_first:
        out_got = [
            lax.ppermute(out_send, both, pair_and_core),
            lax.ppermute(out_keep, both, pair_diagonal),
        ]
        out_keep = jnp.where(home, out_keep, jnp.zeros_like(out_keep))
    else:
        out_got = [send_across(out_send)]
    gh, gn1_part, attn_keep, attn_send, sums_two, g_qv = attention_back(
        lead_rows, flags, vecs, segment, hidden, cot, gn2_part, gn2_oth, wp, att, q, k, v, lse,
        w3, n1,
    )
    attn_got = send_across(attn_send)
    gn1_oth = swap(after(gn1_part, in_got, *out_got))
    in_terms = send_pair(total(in_keep, in_got).astype(BF16))
    outgoing, kept, sums_one = mixed_back(blend, vecs, mixed, gh, gn1_part, gn1_oth)

    leaving = taken(outgoing.reshape(2, 2, dp_count, piece, width), core, 1)
    leaving = leaving.transpose(1, 0, 2, 3).reshape(2 * dp_count, piece, width)
    back = lax.all_to_all(leaving, both, 0, 0, tiled=True)

    attn_value = total(attn_keep, after(attn_got, leaving)).astype(BF16)
    attn_terms = send_pair(attn_value)
    out_value = total(out_keep, *after(out_got, leaving)).astype(BF16)
    if pair_first:
        out_value = out_value.reshape(high, 2, mid, part_rows, units)
        out_terms = (taken(out_value, across, 1), send_across(taken(out_value, 1 - across, 1)))
    else:
        out_terms = send_pair(out_value)
    sum_in = far(total(*after(in_terms, leaving)))
    out_oth = swap(after(out_part, leaving))
    block = (hidden + (out_part.astype(F32) + out_oth.astype(F32)) + out_bias).astype(BF16)
    block_got = half_weight(block)
    block_out = jnp.where(home, block, block_got)

    source_of = jnp.sum(
        jnp.where(partner[:, None] == ids[None, :dp_count], ids[:dp_count, None], 0),
        axis=0,
        dtype=jnp.int32,
    )
    source = source_of[ids // 2]
    wanted = (source // 2) * 4 + (ids % 2) * 2 + source % 2
    returning = pick(back, wanted, sum_in, block, attn_value)
    returned = lax.all_to_all(
        returning.reshape(dp_count, 2, piece, width), "dp", 0, 0, tiled=True
    )
    kept = kept.reshape(2, rows // 2, width)
    kept_got = half_weight(taken(kept, 1 - mp, 0))
    returned = after(returned, block_got)
    kept = jnp.where(home, taken(kept, mp, 0), kept_got)
    returned = returned.transpose(1, 0, 2, 3).reshape(rows // 2, width)
    mine = (kept.astype(F32) + returned.astype(F32)).astype(BF16)
    other = lax.ppermute(mine, "mp", [(0, 1), (1, 0)])
    grad_tokens = jnp.where(
        jnp.arange(2)[:, None, None] == mp, mine[None], other[None]
    ).reshape(rows, width)

    sum_out = far(total(*after(out_terms, mine)))
    sum_attn = far(total(*after(attn_terms, mine)))
    sum_qkv = sum_attn[:, : 3 * local].reshape(-1, 3, local)
    sum_proj = sum_attn[:, 3 * local :].T

    wide = jnp.concatenate(
        [jnp.sum(sums_one, axis=1), jnp.sum(sums_two, axis=1), jnp.sum(g_bout, axis=0)[None]]
    )
    wide = jnp.where(core == 0, wide, 0.0).reshape(6, dp_count, 1, part_rows)
    wide = jnp.broadcast_to(wide, (6, dp_count, 2, part_rows)).transpose(1, 2, 0, 3)
    to_half = jnp.arange(2) == core

    def half_terms(vectors):
        terms = vectors.reshape(vectors.shape[0], dp_count, 1, -1)
        terms = jnp.where(to_half[None, None, :, None], terms, 0.0)
        return terms.transpose(1, 2, 0, 3).reshape(dp_count, 2, -1)

    short = jnp.concatenate(
        [
            wide.reshape(dp_count, 2, -1),
            half_terms(jnp.sum(g_bin, axis=0)[None]),
            half_terms(jnp.sum(g_qv, axis=1)),
        ],
        axis=-1,
    ).reshape(2 * dp_count, -1)
    short = lax.all_to_all(after(short, mine), both, 0, 0, tiled=True)
    short = jnp.sum(short, axis=0)
    plain = short[: 6 * part_rows].reshape(6, part_rows)
    sum_bin = short[6 * part_rows : 6 * part_rows + units // dp_count]
    sum_qv = short[6 * part_rows + units // dp_count :].reshape(2, -1)
    return (
        block_out,
        grad_tokens,
        plain[0],
        plain[1],
        sum_qkv,
        sum_qv,
        sum_proj,
        plain[4],
        plain[2],
        plain[3],
        sum_in,
        sum_bin,
        sum_out.T,
        plain[5],
    )


def solution(mesh):
    return jax.shard_map(
        shards,
        mesh=mesh,
        in_specs=(
            P("dp", None),
            P("dp"),
            P(),
            P("dp", None),
            P(),
            P(),
            P(None, None, "mp"),
            P(None, "mp"),
            P("mp", None),
            P(),
            P(),
            P(),
            P(None, "mp"),
            P("mp"),
            P("mp", None),
            P(),
            P("dp", None),
        ),
        out_specs=(
            P("dp", None),
            P("dp", None),
            P("dp"),
            P("dp"),
            P("dp", None, "mp"),
            P(None, ("mp", "dp")),
            P("mp", "dp"),
            P("dp"),
            P("dp"),
            P("dp"),
            P("dp", "mp"),
            P(("mp", "dp")),
            P("mp", "dp"),
            P("dp"),
        ),
        check_vma=False,
    )
```

```python
import functools

import jax
import jax.numpy as jnp
from jax import lax
from jax.experimental import pallas as pl
from jax.experimental.pallas import tpu as pltpu
from jax.sharding import PartitionSpec as P

HEAD_DIM = 64
NORM_EPS = 1e-06
NEG_FILL = -1e30
SCORE_SCALE = HEAD_DIM ** (-0.5)
MAX_CLIP = 256
LANES = 128
F32 = jnp.float32
BF16 = jnp.bfloat16
MIB = 1 << 20
SMALL = pl.CostEstimate(flops=1 << 20, bytes_accessed=1 << 20, transcendentals=0)


def nn(left, right):
    return lax.dot_general(left, right, (((1,), (0,)), ((), ())), preferred_element_type=F32)


def nt(left, right):
    return lax.dot_general(left, right, (((1,), (1,)), ((), ())), preferred_element_type=F32)


def vmem():
    return pl.BlockSpec(memory_space=pltpu.VMEM)


def hbm():
    return pl.BlockSpec(memory_space=pltpu.HBM)


def anywhere():
    return pl.BlockSpec(memory_space=pl.ANY)


def smem():
    return pl.BlockSpec(memory_space=pltpu.SMEM)


def params(mib):
    return pltpu.CompilerParams(vmem_limit_bytes=mib * MIB)


def shape(dims, dtype):
    return jax.ShapeDtypeStruct(dims, dtype)


def row_stats(vector):
    mean = jnp.mean(vector, axis=-1, keepdims=True)
    centred = vector - mean
    spread = jnp.mean(centred * centred, axis=-1, keepdims=True)
    return centred, lax.rsqrt(spread + NORM_EPS)


def on_lanes(column):
    return jnp.broadcast_to(column, (column.shape[0], LANES))


def wide_rsqrt(inv, here, width):
    return jnp.concatenate([inv[here, :]] * (width // LANES), axis=1)


def row_sum(block):
    return jnp.sum(block, axis=0, keepdims=True)


def fold_rows(block):
    rows, width = block.shape
    return jnp.sum(block.reshape(rows // 8, 8, width), axis=0)


def pick_kernel(index, source, *refs):
    picked = refs[-1]

    def move(i, carry):
        picked[i] = source[index[i]]
        return carry

    lax.fori_loop(0, picked.shape[0], move, 0, unroll=4)


def pick(source, index, *after):
    dims = index.shape + source.shape[1:]
    return pl.pallas_call(
        pick_kernel,
        out_shape=shape(dims, source.dtype),
        in_specs=[smem(), vmem()] + [hbm()] * len(after),
        out_specs=vmem(),
        compiler_params=params(16),
        cost_estimate=SMALL,
        name="pick",
    )(index, source, *after)


def move(source, target, sem):
    return pltpu.make_async_copy(source, target, sem)


PARTS = 4


def part_moves(pairs, sems):
    moves = []
    for c in range(PARTS):
        row = []
        for n, (source, target) in enumerate(pairs):
            count = source.shape[0] // PARTS
            here = pl.ds(c * count, count)
            row.append(move(source.at[here, :], target.at[here, :], sems.at[n, c]))
        moves.append(row)
    return moves


def start_all(moves):
    for one in moves:
        one.start()


def wait_all(moves):
    for one in moves:
        one.wait()


def interleave(*streams):
    order = sorted(
        ((n + 0.5) / len(stream), which, n)
        for which, stream in enumerate(streams)
        for n in range(len(stream))
    )
    for _, which, n in order:
        streams[which][n]()


def spread_clips(seg_row, seg_b):
    for i in range(seg_b.shape[0] // LANES):
        here = pl.ds(i * LANES, LANES)
        seg_b[here, :] = jnp.broadcast_to(seg_row[:, here], (LANES, LANES)).T


def key_window(j, rows):
    window = min(rows, LANES + 2 * MAX_CLIP)
    here = pl.ds(pl.multiple_of(j * LANES, LANES), LANES)
    first = pl.multiple_of(jnp.clip(j * LANES - MAX_CLIP, 0, rows - window), LANES)
    return here, pl.ds(first, window)


def set_bias(bias, seg_b, seg_row, here, keys):
    filled = jnp.where(seg_b[keys, :] == seg_row[:, here], 0.0, NEG_FILL)
    bias[:, pl.ds(0, LANES)] = filled
    bias[:, pl.ds(LANES, LANES)] = filled


def two_heads(block):
    lane = lax.broadcasted_iota(jnp.int32, block.shape, 1)
    return jnp.concatenate(
        [block * (lane // HEAD_DIM == e).astype(BF16) for e in range(2)], axis=0
    )


def attention_kernel(
    blend, flags, seg_row, vecs, biases, tok, own, oth, w3, wp, *refs
):
    mixed, n1, normed, inv, q, k, v, att, part, lse = refs[-32:-22]
    (
        tok_v, own_v, oth_v, w3_v, wp_v, mixed_v, n1_v, q_v, k_v, v_v, att_v, part_v,
        vt, att_t, seg_b, bias, ones, normed_v, inv_v, in_sems, half_sems, out_sems,
    ) = refs[-22:]
    rows, width = tok.shape
    local = wp.shape[0]
    half_rows = rows // 2
    ratio = blend[0]
    blk = 32
    big = 256

    loads = [
        move(source, target, in_sems.at[n])
        for n, (source, target) in enumerate([(tok, tok_v), (w3, w3_v), (wp, wp_v)])
    ]
    halves = part_moves([(own, own_v), (oth, oth_v)], half_sems)
    loads[0].start()
    for part_of in halves:
        start_all(part_of)
    start_all(loads[1:])
    early = [
        move(source, target, out_sems.at[n])
        for n, (source, target) in enumerate(
            [
                (mixed_v, mixed), (n1_v, n1), (normed_v, normed), (inv_v, inv),
                (q_v, q), (k_v, k), (v_v, v),
            ]
        )
    ]
    ones[...] = jnp.ones_like(ones)
    spread_clips(seg_row, seg_b)

    loads[0].wait()
    steps = half_rows // PARTS // blk
    for n, src, half in ((0, own_v, flags[0]), (1, oth_v, 1 - flags[0])):
        for c in range(PARTS):
            halves[c][n].wait()

            def mix(i, carry, src=src, half=half, c=c):
                low = (c * steps + i) * blk
                here = pl.ds(pl.multiple_of(half * half_rows + low, blk), blk)
                there = pl.ds(pl.multiple_of(low, blk), blk)
                mine, other = tok_v[here, :].astype(F32), src[there, :].astype(F32)
                blended = ratio * mine + (1.0 - ratio) * other
                mixed_v[here, :] = blended
                centred, scale = row_stats(blended)
                inv_v[here, :] = on_lanes(scale)
                plain = centred * scale
                normed_v[here, :] = plain.astype(BF16)
                n1_v[here, :] = (plain * vecs[0:1, :] + vecs[1:2, :]).astype(BF16)
                return carry

            lax.fori_loop(0, steps, mix, 0, unroll=True)
    start_all(early[:4])

    loads[1].wait()
    for i in range(rows // big):
        here = pl.ds(i * big, big)
        rows_in = n1_v[here, :]
        queries = (nn(rows_in, w3_v[0]) + biases[0:1, :local]).astype(BF16).astype(F32)
        q_v[here, :] = (queries * SCORE_SCALE).astype(BF16)
        k_v[here, :] = nn(rows_in, w3_v[1]).astype(BF16)
        values = (nn(rows_in, w3_v[2]) + biases[0:1, local:]).astype(BF16)
        v_v[here, :] = values
        vt[:, here] = values.T
    start_all(early[4:])

    def attend(j, carry):
        here, keys = key_window(j, rows)
        set_bias(bias, seg_b, seg_row, here, keys)
        for p in range(local // LANES):
            pair = pl.ds(p * LANES, LANES)
            scores = nt(k_v[keys, pair], two_heads(q_v[here, pair])) + bias[...]
            top = jnp.max(scores, axis=0, keepdims=True)
            grown = jnp.exp(scores - top).astype(BF16)
            total = nn(ones[...], grown)[:1]
            out = (nn(vt[pair, keys], grown) / total).astype(BF16)
            logs = top + jnp.log(total)
            for e in range(2):
                lanes = slice(e * LANES, e * LANES + LANES)
                head = slice(e * HEAD_DIM, e * HEAD_DIM + HEAD_DIM)
                att_t[pl.ds(p * LANES + e * HEAD_DIM, HEAD_DIM), here] = out[head, lanes]
                lse[pl.ds(2 * p + e, 1), here] = logs[:, lanes]
        return carry

    lax.fori_loop(0, rows // LANES, attend, 0)

    loads[2].wait()
    last = []
    for i in range(rows // big):
        here = pl.ds(i * big, big)
        block = att_t[:, here].T
        att_v[here, :] = block
        part_v[here, :] = nn(block, wp_v[...]).astype(BF16)
        last.append(move(part_v.at[here, :], part.at[here, :], out_sems.at[8 + i]))
        last[-1].start()
    last.append(move(att_v, att, out_sems.at[7]))
    last[-1].start()
    wait_all(early + last)


def attention(blend, flags, segment, vecs, biases, tok, own, oth, w3, wp, *before):
    rows, width = tok.shape
    local = wp.shape[0]
    window = min(rows, LANES + 2 * MAX_CLIP)
    thin = shape((rows, local), BF16)
    tall = shape((rows, width), BF16)
    return pl.pallas_call(
        attention_kernel,
        out_shape=(
            shape((rows, width), F32), tall, tall, shape((rows, LANES), F32),
            thin, thin, thin, thin, tall, shape((local // HEAD_DIM, rows), F32),
        ),
        in_specs=[smem(), smem()] + [vmem()] * 3 + [anywhere()] * 3 + [hbm()] * (2 + len(before)),
        out_specs=[hbm()] * 9 + [vmem()],
        scratch_shapes=[
            pltpu.VMEM((rows, width), BF16),
            pltpu.VMEM((rows // 2, width), BF16),
            pltpu.VMEM((rows // 2, width), BF16),
            pltpu.VMEM(w3.shape, BF16),
            pltpu.VMEM(wp.shape, BF16),
            pltpu.VMEM((rows, width), F32),
            pltpu.VMEM((rows, width), BF16),
            pltpu.VMEM((rows, local), BF16),
            pltpu.VMEM((rows, local), BF16),
            pltpu.VMEM((rows, local), BF16),
            pltpu.VMEM((rows, local), BF16),
            pltpu.VMEM((rows, width), BF16),
            pltpu.VMEM((local, rows), BF16),
            pltpu.VMEM((local, rows), BF16),
            pltpu.VMEM((rows, LANES), F32),
            pltpu.VMEM((window, 2 * LANES), F32),
            pltpu.VMEM((16, window), BF16),
            pltpu.VMEM((rows, width), BF16),
            pltpu.VMEM((rows, LANES), F32),
            pltpu.SemaphoreType.DMA((3,)),
            pltpu.SemaphoreType.DMA((2, PARTS)),
            pltpu.SemaphoreType.DMA((8 + rows // 256,)),
        ],
        compiler_params=params(60),
        cost_estimate=SMALL,
        name="attention",
    )(
        blend, flags, segment, vecs, biases, tok, own, oth, w3, wp, *before,
    )


ERFC_SLOPE = 0.47
ERFC_COEFFS = (
    0.2663094668265691,
    0.2480096137831850,
    0.3362712657560771,
    -0.1262288063821733,
    0.6076790117752645,
    -0.4204702410368928,
    0.0884296765518492,
)


def gelu_parts(pre):
    bell = jnp.exp(pre * pre * -0.5)
    t = 1.0 / (1.0 + jnp.abs(pre) * (ERFC_SLOPE * 0.5**0.5))
    poly = 0.5 * ERFC_COEFFS[-1]
    for coeff in ERFC_COEFFS[-2::-1]:
        poly = poly * t + 0.5 * coeff
    tail = poly * t * bell
    cdf = jnp.where(pre >= 0, 1.0 - tail, tail)
    return pre * cdf, cdf + pre * bell * 0.3989422804014327


def turn_into(target, source, blocks):
    rows = source.shape[0]
    big = 256
    for i in range(rows // big):
        here = pl.ds(i * big, big)
        turned = source[here, :].T
        for start, place, count in blocks:
            target[pl.ds(place, count), here] = turned[start : start + count]


def lead_blocks(width, lead_rows):
    runs = width // lead_rows
    return [
        (run * lead_rows, ((run % 2) * (runs // 2) + run // 2) * lead_rows, lead_rows)
        for run in range(runs)
    ]


def feed_kernel(
    in_rows, out_rows, flags, vecs, biases, mixed, p_own, p_oth, cot, cot_t,
    w_in, w_out, w_out_one, w_out_two,
    hidden, part, gn_part, in_keep, in_send, out_keep, out_send, normed, inv, g_bin, g_bout,
    mixed_v, own_v, oth_v, cot_v, cot_tv, w_in_v, w_out_v, n2, n2_t, act, gp,
    g_in, g_out, normed_v, inv_v, in_sems, turn_sems, weight_sems, out_sems, grad_sems,
):
    rows, width = mixed.shape
    units = w_in.shape[1]
    blk = 32
    big = 256
    sub = 16
    home = flags[1] == 1
    across = flags[2]
    kept_out = jnp.where(home, flags[0], 1 - flags[0]) if in_rows != out_rows else across
    sides = (across, kept_out)

    loads = part_moves(
        [(mixed, mixed_v), (p_own, own_v), (p_oth, oth_v), (cot, cot_v)], in_sems
    )
    for part_of in loads:
        start_all(part_of)

    weights = [move(w_in, w_in_v, weight_sems.at[0])]
    weights[0].start()
    half = w_out.shape[0] // 2
    for n, (got, place) in enumerate([(w_out_one, across), (w_out_two, 1 - across)]):
        spot = pl.ds(pl.multiple_of(place * half, half), half)
        sem = weight_sems.at[1 + n]
        weights.append(move(w_out.at[spot, :], w_out_v.at[spot, :], sem))

        @pl.when(home)
        def _(spot=spot, sem=sem):
            move(w_out.at[spot, :], w_out_v.at[spot, :], sem).start()

        @pl.when(jnp.logical_not(home))
        def _(got=got, spot=spot, sem=sem):
            move(got, w_out_v.at[spot, :], sem).start()

    turns = [
        move(cot_t.at[pl.ds(start, count), :], cot_tv.at[pl.ds(place, count), :], turn_sems.at[n])
        for n, (start, place, count) in enumerate(lead_blocks(width, out_rows))
    ]
    start_all(turns)

    g_bout[...] = jnp.zeros_like(g_bout)
    steps = rows // PARTS // blk
    for c in range(PARTS):
        wait_all(loads[c])

        def norm(i, carry, c=c):
            here = pl.ds(pl.multiple_of((c * steps + i) * blk, blk), blk)
            attn = own_v[here, :].astype(F32) + oth_v[here, :].astype(F32)
            total = mixed_v[here, :] + attn + vecs[4:5, :]
            mixed_v[here, :] = total
            centred, scale = row_stats(total)
            inv_v[here, :] = on_lanes(scale)
            plain = centred * scale
            normed_v[here, :] = plain.astype(BF16)
            n2[here, :] = (plain * vecs[2:3, :] + vecs[3:4, :]).astype(BF16)
            g_bout[...] += fold_rows(cot_v[here, :].astype(F32))
            return carry

        lax.fori_loop(0, steps, norm, 0, unroll=4)
    stores = [
        move(source, target, out_sems.at[0, n])
        for n, (source, target) in enumerate(
            [(mixed_v, hidden), (normed_v, normed), (inv_v, inv)]
        )
    ]
    start_all(stores)
    turn_into(n2_t, n2, lead_blocks(width, in_rows))
    wait_all(weights)

    sums = [jnp.zeros((8, width), F32) for _ in range(units // width)]
    for i in range(rows // big):
        here = pl.ds(i * big, big)
        for j in range(units // width):
            cols = pl.ds(j * width, width)
            pre_all = nn(n2[here, :], w_in_v[:, cols])
            grad_all = nt(cot_v[here, :], w_out_v[cols, :])
            for s in range(big // sub):
                rng = slice(s * sub, s * sub + sub)
                value, slope = gelu_parts(pre_all[rng] + biases[1 + j : 2 + j, :])
                grad = grad_all[rng] * slope
                sums[j] += fold_rows(grad)
                spot = pl.ds(i * big + s * sub, sub)
                act[spot, cols] = value.astype(BF16)
                gp[spot, cols] = grad.astype(BF16)
        oth_v[here, :] = nt(gp[here, :], w_in_v[...]).astype(BF16)
        own_v[here, :] = nn(act[here, :], w_out_v[...]).astype(BF16)
        for n, (source, target) in enumerate([(oth_v, gn_part), (own_v, part)]):
            stores.append(move(source.at[here, :], target.at[here, :], out_sems.at[1 + n, i]))
            stores[-1].start()
    for j in range(units // width):
        g_bin[:, pl.ds(j * width, width)] = sums[j]

    wait_all(turns)
    half = width // 2
    for n, (turned, right, buf, keep, send) in enumerate(
        [(n2_t, gp, g_in, in_keep, in_send), (cot_tv, act, g_out, out_keep, out_send)]
    ):
        for side in range(2):
            lines = pl.ds(side * half, half)
            for j in range(units // width):
                cols = pl.ds(j * width, width)
                buf[side, :, cols] = nn(turned[lines, :], right[:, cols]).astype(BF16)
        for m, (side, target) in enumerate([(1 - sides[n], send), (sides[n], keep)]):
            stores.append(move(buf.at[side], target, grad_sems.at[n, m]))
            stores[-1].start()
    wait_all(stores)


def feed(
    in_rows, out_rows, flags, vecs, biases, mixed, p_own, p_oth, cot, cot_t,
    w_in, w_out, w_out_one, w_out_two,
):
    rows, width = mixed.shape
    units = w_in.shape[1]
    tall = shape((rows, width), BF16)
    grad = shape((width // 2, units), BF16)
    return pl.pallas_call(
        functools.partial(feed_kernel, in_rows, out_rows),
        out_shape=(
            shape((rows, width), F32), tall, tall, grad, grad, grad, grad,
            tall, shape((rows, LANES), F32), shape((8, units), F32), shape((8, width), F32),
        ),
        in_specs=[smem()] + [vmem()] * 2 + [hbm()] * 2 + [anywhere()] + [hbm()] * 6,
        out_specs=[hbm()] * 9 + [vmem()] * 2,
        scratch_shapes=[
            pltpu.VMEM((rows, width), F32),
            pltpu.VMEM((rows, width), BF16),
            pltpu.VMEM((rows, width), BF16),
            pltpu.VMEM((rows, width), BF16),
            pltpu.VMEM((width, rows), BF16),
            pltpu.VMEM(w_in.shape, BF16),
            pltpu.VMEM(w_out.shape, BF16),
            pltpu.VMEM((rows, width), BF16),
            pltpu.VMEM((width, rows), BF16),
            pltpu.VMEM((rows, units), BF16),
            pltpu.VMEM((rows, units), BF16),
            pltpu.VMEM((2, width // 2, units), BF16),
            pltpu.VMEM((2, width // 2, units), BF16),
            pltpu.VMEM((rows, width), BF16),
            pltpu.VMEM((rows, LANES), F32),
            pltpu.SemaphoreType.DMA((4, PARTS)),
            pltpu.SemaphoreType.DMA((width // out_rows,)),
            pltpu.SemaphoreType.DMA((3,)),
            pltpu.SemaphoreType.DMA((3, rows // 256)),
            pltpu.SemaphoreType.DMA((2, 2)),
        ],
        compiler_params=params(60),
        cost_estimate=SMALL,
        name="feed",
    )(
        flags, vecs, biases, mixed, p_own, p_oth, cot, cot_t,
        w_in, w_out, w_out_one, w_out_two,
    )


def attention_back_kernel(
    lead_rows, flags, vecs, seg_row, lse, g_bin, g_bout, g_own, g_oth, cot, normed, inv,
    wp, att, k, q, v, w3, n1, normed_one,
    gh, part, keep, send, short,
    gh_v, own_v, oth_v, cot_v, normed_v, inv_v, wp_v, att_v, k_v, q_v, v_v, w3_v, n1_v, one_v, low_v, part_v,
    sums, d_out, kt, dq_t, dk, dv, delta, seg_b, bias, raw, raw_g, low_p, low_g, n1_t, gh_t, grad_v, out,
    in_sems, row_sems, out_sems,
):
    rows, width = cot.shape
    local = wp.shape[0]
    blk = 32
    big = 256
    blocks = lead_blocks(width, lead_rows)
    across = flags[2]
    row_loads = part_moves(
        [(g_own, own_v), (g_oth, oth_v), (cot, cot_v), (normed, normed_v), (inv, inv_v)],
        row_sems,
    )
    for part_of in row_loads:
        start_all(part_of)
    loads = [
        move(source, target, in_sems.at[n])
        for n, (source, target) in enumerate(
            [
                (wp, wp_v), (att, att_v), (k, k_v), (q, q_v), (v, v_v), (w3, w3_v), (n1, n1_v),
                (normed_one, one_v),
            ]
        )
    ]
    start_all(loads)
    sums[...] = jnp.zeros_like(sums)
    dk[...] = jnp.zeros_like(dk)
    dv[...] = jnp.zeros_like(dv)
    spread_clips(seg_row, seg_b)

    steps = rows // PARTS // blk
    for c in range(PARTS):
        wait_all(row_loads[c])

        def norm(i, carry, c=c):
            here = pl.ds(pl.multiple_of((c * steps + i) * blk, blk), blk)
            grad = own_v[here, :].astype(F32) + oth_v[here, :].astype(F32)
            plain = normed_v[here, :].astype(F32)
            scaled = grad * vecs[2:3, :]
            mean_one = jnp.mean(scaled, axis=-1, keepdims=True)
            mean_two = jnp.mean(scaled * plain, axis=-1, keepdims=True)
            scale = wide_rsqrt(inv_v, here, width)
            back = cot_v[here, :].astype(F32) + scale * (scaled - mean_one - plain * mean_two)
            gh_v[here, :] = back
            low_v[here, :] = back.astype(BF16)
            sums[0] += fold_rows(grad * plain)
            sums[1] += fold_rows(grad)
            sums[2] += fold_rows(back)
            return carry

        lax.fori_loop(0, steps, norm, 0, unroll=4)
    stores = [move(gh_v, gh, out_sems.at[0])]
    stores[0].start()

    wait_all(loads[:3])
    heads = local // HEAD_DIM
    lane = lax.broadcasted_iota(jnp.int32, (delta.shape[0], local), 1)
    row = lax.broadcasted_iota(jnp.int32, (delta.shape[0], local), 0)
    of_head = (lane // HEAD_DIM == row).astype(BF16)
    for i in range(rows // big):
        here = pl.ds(i * big, big)
        grad_out = nt(low_v[here, :], wp_v[...]).astype(BF16)
        d_out[here, :] = grad_out
        product = grad_out.astype(F32) * att_v[here, :].astype(F32)
        coarse = product.astype(BF16)
        fine = (product - coarse.astype(F32)).astype(BF16)
        delta[:, here] = nt(of_head, coarse) + nt(of_head, fine)
        kt[:, here] = k_v[here, :].T
    wait_all(loads[3:])

    pairs = heads // 2
    window = bias.shape[0]
    strip = 128
    strips = window // strip

    def attend(j, carry):
        here, keys = key_window(j, rows)
        first = pl.multiple_of(keys.start, LANES)
        set_bias(bias, seg_b, seg_row, here, keys)
        blocks_two = {}

        def two(p):
            if p not in blocks_two:
                pair = pl.ds(p * LANES, LANES)
                blocks_two[p] = (two_heads(q_v[here, pair]), two_heads(d_out[here, pair]))
            return blocks_two[p]

        def at_strip(n):
            return (
                pl.ds(pl.multiple_of(first + n * strip, strip), strip),
                pl.ds(n * strip, strip),
            )

        def products(p):
            pair = pl.ds(p * LANES, LANES)

            def scores(n):
                def run():
                    some, at = at_strip(n)
                    raw[p % 2, at, :] = nt(k_v[some, pair], two(p)[0])

                return run

            def grads(n):
                def run():
                    some, at = at_strip(n)
                    raw_g[p % 2, at, :] = nt(v_v[some, pair], two(p)[1])

                return run

            return [make(n) for n in range(strips) for make in (scores, grads)]

        def softmax_back(p):
            tops = jnp.concatenate([lse[pl.ds(2 * p + e, 1), here] for e in range(2)], axis=1)
            inner = jnp.concatenate([delta[pl.ds(2 * p + e, 1), here] for e in range(2)], axis=1)
            half = strip // 2

            def run_at(n):
                def run():
                    at = pl.ds(n * half, half)
                    probs = jnp.exp(raw[p % 2, at, :] + bias[at, :] - tops)
                    low_p[p % 2, at, :] = probs.astype(BF16)
                    low_g[p % 2, at, :] = (probs * (raw_g[p % 2, at, :] - inner)).astype(BF16)

                return run

            return [run_at(n) for n in range(2 * strips)]

        def sums_of(p):
            pair = pl.ds(p * LANES, LANES)

            def keys_of(n):
                def run():
                    some, at = at_strip(n)
                    dk[some, pair] += nn(low_g[p % 2, at, :], two(p)[0])

                return run

            def values_of(n):
                def run():
                    some, at = at_strip(n)
                    dv[some, pair] += nn(low_p[p % 2, at, :], two(p)[1])

                return run

            def queries():
                grad_q = nn(kt[pair, keys], low_g[p % 2]) * SCORE_SCALE
                for e in range(2):
                    lanes = slice(e * LANES, e * LANES + LANES)
                    head = slice(e * HEAD_DIM, e * HEAD_DIM + HEAD_DIM)
                    dq_t[pl.ds(p * LANES + e * HEAD_DIM, HEAD_DIM), here] = grad_q[head, lanes]

            return [make(n) for n in range(strips) for make in (keys_of, values_of)] + [queries]

        def turns():
            for target, source in ((n1_t, n1_v), (gh_t, low_v)):
                turned = source[here, :].T
                for start, place, count in blocks:
                    target[pl.ds(place, count), here] = turned[start : start + count]

        interleave(products(0), [turns])
        for p in range(pairs):
            matrix = (products(p + 1) if p + 1 < pairs else []) + (sums_of(p - 1) if p else [])
            interleave(softmax_back(p), matrix)
        interleave(sums_of(pairs - 1))
        return carry

    lax.fori_loop(0, rows // LANES, attend, 0)

    q_sum = jnp.zeros((8, local), F32)
    v_sum = jnp.zeros((8, local), F32)
    gain_sum = jnp.zeros((8, width), F32)
    shift_sum = jnp.zeros((8, width), F32)
    for i in range(rows // big):
        here = pl.ds(i * big, big)
        grad_q, grad_k, grad_val = dq_t[:, here].T, dk[here, :], dv[here, :]
        q_sum += fold_rows(grad_q)
        v_sum += fold_rows(grad_val)
        lows = [grad.astype(BF16) for grad in (grad_q, grad_k, grad_val)]
        total = sum(nt(low, w3_v[n]) for n, low in enumerate(lows))
        part_v[here, :] = total.astype(BF16)
        gain_sum += fold_rows(total * one_v[here, :].astype(F32))
        shift_sum += fold_rows(total)
        for n, low in enumerate(lows):
            grad_v[here, pl.ds(n * local, local)] = low
        stores.append(move(part_v.at[here, :], part.at[here, :], out_sems.at[1 + i]))
        stores[-1].start()
    units = g_bin.shape[1]
    qv_sum = jnp.concatenate([q_sum, v_sum], axis=1)
    listed = [gain_sum, shift_sum, sums[0], sums[1], sums[2], g_bout[...], qv_sum]
    listed += [g_bin[:, pl.ds(n, width)] for n in range(0, units, width)]
    for n, block in enumerate(listed):
        short[pl.ds(n, 1), :] = row_sum(block)
    half = width // 2
    for side in range(2):
        lines = pl.ds(side * half, half)
        for n in range(3):
            cols = pl.ds(n * local, local)
            out[side, :, cols] = nn(n1_t[lines, :], grad_v[:, cols]).astype(BF16)
        out[side, :, pl.ds(3 * local, local)] = nn(gh_t[lines, :], att_v[...]).astype(BF16)
    base = 1 + rows // big
    for n, (side, target) in enumerate([(1 - across, send), (across, keep)]):
        stores.append(move(out.at[side], target, out_sems.at[base + n]))
        stores[-1].start()
    wait_all(stores)


def attention_back(
    lead_rows, flags, vecs, segment, lse, g_bin, g_bout, g_own, g_oth, cot, normed, inv,
    wp, att, k, q, v, w3, n1, normed_one,
):
    rows, width = cot.shape
    local = wp.shape[0]
    window = min(rows, LANES + 2 * MAX_CLIP)
    tall, thin = pltpu.VMEM((rows, width), BF16), pltpu.VMEM((rows, local), BF16)
    turned = pltpu.VMEM((width, rows), BF16)
    half = (width // 2, 4 * local)
    return pl.pallas_call(
        functools.partial(attention_back_kernel, lead_rows),
        out_shape=(
            shape((rows, width), F32),
            shape((rows, width), BF16),
            shape(half, BF16),
            shape(half, BF16),
            shape((7 + g_bin.shape[1] // width, width), F32),
        ),
        in_specs=[smem()] + [vmem()] * 5 + [hbm()] + [anywhere()] + [hbm()] * 11,
        out_specs=[hbm()] * 4 + [vmem()],
        scratch_shapes=[
            pltpu.VMEM((rows, width), F32),
            tall, tall, tall, tall,
            pltpu.VMEM((rows, LANES), F32),
            pltpu.VMEM(wp.shape, BF16),
            thin, thin, thin, thin,
            pltpu.VMEM(w3.shape, BF16),
            tall, tall, tall, tall,
            pltpu.VMEM((3, 8, width), F32),
            thin,
            pltpu.VMEM((local, rows), BF16),
            pltpu.VMEM((local, rows), F32),
            pltpu.VMEM((rows, local), F32),
            pltpu.VMEM((rows, local), F32),
            pltpu.VMEM((8, rows), F32),
            pltpu.VMEM((rows, LANES), F32),
            pltpu.VMEM((window, 2 * LANES), F32),
            pltpu.VMEM((2, window, 2 * LANES), F32),
            pltpu.VMEM((2, window, 2 * LANES), F32),
            pltpu.VMEM((2, window, 2 * LANES), BF16),
            pltpu.VMEM((2, window, 2 * LANES), BF16),
            turned, turned,
            pltpu.VMEM((rows, 3 * local), BF16),
            pltpu.VMEM((2,) + half, BF16),
            pltpu.SemaphoreType.DMA((8,)),
            pltpu.SemaphoreType.DMA((5, PARTS)),
            pltpu.SemaphoreType.DMA((3 + rows // 256,)),
        ],
        compiler_params=params(60),
        cost_estimate=SMALL,
        name="attention_back",
    )(
        flags, vecs, segment, lse, g_bin, g_bout, g_own, g_oth, cot, normed, inv,
        wp, att, k, q, v, w3, n1, normed_one,
    )


def mixed_back_kernel(blend, vecs, gh, g_own, g_oth, normed, inv, outgoing, kept, *refs):
    gh_v, own_v, oth_v, normed_v, inv_v, leave_v, kept_v, in_sems, out_sems = refs
    ratio = blend[0]
    rows, width = gh.shape
    blk = 32
    loads = part_moves(
        [(gh, gh_v), (g_own, own_v), (g_oth, oth_v), (normed, normed_v), (inv, inv_v)], in_sems
    )
    stores = part_moves([(leave_v, outgoing), (kept_v, kept)], out_sems)
    for part_of in loads:
        start_all(part_of)
    steps = rows // PARTS // blk
    for c in range(PARTS):
        wait_all(loads[c])

        def norm(i, carry, c=c):
            here = pl.ds(pl.multiple_of((c * steps + i) * blk, blk), blk)
            grad = own_v[here, :].astype(F32) + oth_v[here, :].astype(F32)
            plain = normed_v[here, :].astype(F32)
            scaled = grad * vecs[0:1, :]
            mean_one = jnp.mean(scaled, axis=-1, keepdims=True)
            mean_two = jnp.mean(scaled * plain, axis=-1, keepdims=True)
            scale = wide_rsqrt(inv_v, here, width)
            back = gh_v[here, :] + scale * (scaled - mean_one - plain * mean_two)
            leave_v[here, :] = ((1.0 - ratio) * back).astype(BF16)
            kept_v[here, :] = (ratio * back).astype(BF16)
            return carry

        lax.fori_loop(0, steps, norm, 0, unroll=4)
        start_all(stores[c])
    for part_of in stores:
        wait_all(part_of)


def mixed_back(blend, vecs, gh, g_own, g_oth, normed, inv):
    rows, width = gh.shape
    tall = pltpu.VMEM((rows, width), BF16)
    return pl.pallas_call(
        mixed_back_kernel,
        out_shape=(shape((rows, width), BF16), shape((rows, width), BF16)),
        in_specs=[smem(), vmem()] + [hbm()] * 2 + [anywhere()] + [hbm()] * 2,
        out_specs=[hbm(), hbm()],
        scratch_shapes=[
            pltpu.VMEM((rows, width), F32),
            tall, tall, tall, pltpu.VMEM((rows, LANES), F32), tall, tall,
            pltpu.SemaphoreType.DMA((5, PARTS)),
            pltpu.SemaphoreType.DMA((2, PARTS)),
        ],
        compiler_params=params(60),
        cost_estimate=SMALL,
        name="mixed_back",
    )(blend, vecs, gh, g_own, g_oth, normed, inv)


def shards(
    tokens,
    mix_blend,
    partner,
    clip_ids,
    gain_one,
    shift_one,
    qkv_weight,
    qv_bias,
    proj_weight,
    proj_bias,
    gain_two,
    shift_two,
    in_weight,
    in_bias,
    out_weight,
    out_bias,
    cotangent,
):
    rows, width = tokens.shape
    dp_count = lax.axis_size("dp")
    both = ("dp", "mp")
    bits = dp_count.bit_length() - 1
    seq = lax.axis_index("dp")
    mp = lax.axis_index("mp")
    core = lax.rem(seq, 2)
    home = core == mp
    all_dp = range(dp_count)

    def joint(d, m):
        return 2 * d + m

    core_swap = [(d, d ^ 1) for d in all_dp]
    home_to_pair = [(joint(d, d & 1), joint(d, 1 - (d & 1))) for d in all_dp]
    pair_to_home = [(joint(d, 1 - (d & 1)), joint(d, d & 1)) for d in all_dp]
    weight_move = home_to_pair + [
        (joint(d, 1 - (d & 1)), joint(d ^ 1, 1 - (d & 1))) for d in all_dp
    ]

    def swap(value):
        return lax.ppermute(value, "dp", core_swap)

    def chip_value(value):
        return jnp.where(home, value, swap(value))

    def after(value, *others):
        return lax.optimization_barrier((value,) + others)[0]

    def half_weight(value):
        return lax.ppermute(value, both, weight_move)

    part_rows = width // dp_count
    lead = min(n for n in range(1, bits) if (part_rows << n) % 16 == 0)
    lead_rows = part_rows << lead
    across = lax.rem(seq >> lead, 2)
    flags = jnp.stack([core, home.astype(jnp.int32), across]).astype(jnp.int32)

    def taken(value, index, axis):
        return lax.dynamic_index_in_dim(value, index, axis, keepdims=False)

    seq_small = chip_value(jnp.concatenate([mix_blend, clip_ids[0].astype(F32)]))
    blend, segment = seq_small[:1], seq_small[1:].reshape(1, rows)
    local = proj_weight.shape[0]
    units = in_bias.shape[0]
    half_small = jnp.concatenate([qv_bias.reshape(-1), in_bias])
    half_small = jnp.where(home, half_small, half_weight(half_small))
    biases = half_small.reshape(-1, width)
    vecs = jnp.stack([gain_one, shift_one, gain_two, shift_two, proj_bias])

    w3 = half_weight(qkv_weight.transpose(1, 0, 2))
    wp = half_weight(proj_weight)

    def two_way(value):
        halves = value.reshape(2, value.shape[0] // 2, value.shape[1])
        one = half_weight(taken(halves, across, 0))
        moves = [(joint(d, 1 - (d & 1)), joint(d ^ (1 << lead), 1 - (d & 1))) for d in all_dp]
        return value, one, lax.ppermute(one, both, moves)

    ids = jnp.arange(2 * dp_count, dtype=jnp.int32)
    piece = rows // (2 * 2 * dp_count)
    sent = tokens.reshape(2, dp_count, 2, piece, width)
    sent = lax.dynamic_index_in_dim(sent, mp, 2, keepdims=False)
    spread = lax.all_to_all(sent.transpose(1, 0, 2, 3), "dp", 0, 0, tiled=True)
    wanted = partner[(ids // 4) * 2 + ids % 2] * 2 + (ids // 2) % 2
    source_of = jnp.sum(
        jnp.where(partner[:, None] == ids[None, :dp_count], ids[:dp_count, None], 0),
        axis=0,
        dtype=jnp.int32,
    )
    source = source_of[ids // 2]
    wanted_back = (source // 2) * 4 + (ids % 2) * 2 + source % 2
    chosen = pick(spread.reshape(2 * dp_count, piece, width), wanted, w3, wp, half_small)
    partner_own = lax.all_to_all(chosen, both, 0, 0, tiled=True).reshape(rows // 2, width)
    w_out = two_way(out_weight)
    w_in = half_weight(after(in_weight, w_out[1]))

    tok = chip_value(tokens)
    cot = chip_value(cotangent)
    cot_t = cot.T
    partner_oth = swap(after(partner_own, tok, cot, vecs, segment, wanted_back))

    mixed, n1, normed_one, inv_one, q, k, v, att, attn_part, lse = attention(
        blend, flags, segment, vecs, biases, tok, partner_own, partner_oth, w3, wp, w_out[2], cot_t
    )
    pair_first = part_rows % 16 == 0
    fed = feed(
        lead_rows, part_rows if pair_first else lead_rows, flags, vecs, biases,
        mixed, attn_part, swap(attn_part), cot, cot_t, w_in, *w_out,
    )
    hidden, out_part, gn2_part, in_keep, in_send, out_keep, out_send = fed[:7]
    normed_two, inv_two, g_bin, g_bout = fed[7:]
    gn2_oth = swap(gn2_part)

    high, mid = dp_count >> (lead + 1), 1 << (lead - 1)
    pair_and_core = pair_to_home + [(joint(d, d & 1), joint(d ^ 1, d & 1)) for d in all_dp]
    pair_diagonal = [(joint(d, 1 - (d & 1)), joint(d ^ 1, d & 1)) for d in all_dp]

    def total(*terms):
        return sum(term.astype(F32) for term in terms)

    def send_across(value):
        return lax.ppermute(value, "dp", [(d, d ^ (1 << lead)) for d in all_dp])

    def send_pair(value):
        value = value.reshape(high, mid, 2, part_rows, -1)
        one = lax.ppermute(taken(value, jnp.where(home, 1 - core, core), 2), both, pair_and_core)
        two = lax.ppermute(taken(value, 1 - core, 2), both, pair_diagonal)
        held = taken(value, core, 2)
        return jnp.where(home, held, jnp.zeros_like(held)), one, two

    def far(value, *others):
        for shift, left in ((1, mid), (lead + 1, high)):
            while left > 1:
                radix = min(4, left)
                left //= radix
                value = value.reshape((-1, left, radix) + value.shape[-2:]).astype(BF16)
                spot = lax.rem(seq >> shift, radix)
                got = [
                    lax.ppermute(
                        taken(value, spot ^ flip, 2),
                        "dp",
                        [(d, d ^ (flip << shift)) for d in all_dp],
                    )
                    for flip in range(1, radix)
                ]
                value = total(taken(value, spot, 2), *after(got, *others))
                shift += radix.bit_length() - 1
        return value.reshape(value.shape[-2:])

    in_got = send_across(in_send)
    if pair_first:
        out_got = [
            lax.ppermute(out_send, both, pair_and_core),
            lax.ppermute(out_keep, both, pair_diagonal),
        ]
        out_keep = jnp.where(home, out_keep, jnp.zeros_like(out_keep))
    else:
        out_got = [send_across(out_send)]
    gh, gn1_part, attn_keep, attn_send, short = attention_back(
        lead_rows, flags, vecs, segment, lse, g_bin, g_bout, gn2_part, gn2_oth, cot,
        normed_two, inv_two, wp, att, k, q, v, w3, n1, normed_one,
    )
    attn_got = send_across(attn_send)
    gn1_oth = swap(after(gn1_part, in_got, *out_got))
    outgoing, kept = mixed_back(blend, vecs, gh, gn1_part, gn1_oth, normed_one, inv_one)

    leaving = taken(outgoing.reshape(2, 2, dp_count, piece, width), core, 1)
    leaving = leaving.transpose(1, 0, 2, 3).reshape(2 * dp_count, piece, width)
    back = lax.all_to_all(leaving, both, 0, 0, tiled=True)

    in_terms = send_pair(total(in_keep, after(in_got, leaving)).astype(BF16))
    attn_value = total(attn_keep, after(attn_got, leaving)).astype(BF16)
    attn_terms = send_pair(attn_value)
    out_value = total(out_keep, *after(out_got, leaving)).astype(BF16)
    if pair_first:
        out_value = out_value.reshape(high, 2, mid, part_rows, units)
        out_terms = (taken(out_value, across, 1), send_across(taken(out_value, 1 - across, 1)))
    else:
        out_terms = send_pair(out_value)
    out_oth = swap(after(out_part, leaving))
    block = (hidden + (out_part.astype(F32) + out_oth.astype(F32)) + out_bias).astype(BF16)

    kept = kept.reshape(2, rows // 2, width)
    passed = jnp.concatenate([block, taken(kept, 1 - mp, 0)], axis=0)
    passed_got = half_weight(passed)

    returning = pick(back, wanted_back, passed, attn_value)
    returned = lax.all_to_all(
        returning.reshape(dp_count, 2, piece, width), "dp", 0, 0, tiled=True
    )
    returned = after(returned, passed_got)
    block_out = jnp.where(home, block, passed_got[:rows])
    kept = jnp.where(home, taken(kept, mp, 0), passed_got[rows:])
    returned = returned.transpose(1, 0, 2, 3).reshape(rows // 2, width)
    mine = (kept.astype(F32) + returned.astype(F32)).astype(BF16)
    other = lax.ppermute(mine, "mp", [(0, 1), (1, 0)])
    grad_tokens = jnp.where(
        jnp.arange(2)[:, None, None] == mp, mine[None], other[None]
    ).reshape(rows, width)

    short = after(short, returning)
    counts = jnp.where((core == 0) | (jnp.arange(6) < 2), 1.0, 0.0).astype(F32)
    wide = (short[:6] * counts[:, None]).reshape(6, dp_count, 1, part_rows)
    wide = jnp.broadcast_to(wide, (6, dp_count, 2, part_rows)).transpose(1, 2, 0, 3)
    to_half = (jnp.arange(2) == core)[None, :, None]

    def half_terms(vectors):
        terms = vectors.reshape(vectors.shape[0], dp_count, -1).transpose(1, 0, 2)
        return jnp.where(to_half, terms.reshape(dp_count, 1, -1), 0.0)

    short = jnp.concatenate(
        [
            wide.reshape(dp_count, 2, -1),
            half_terms(short[6].reshape(2, local)),
            half_terms(short[7:].reshape(1, units)),
        ],
        axis=-1,
    ).reshape(2 * dp_count, -1)

    values = [
        total(*after(terms, mine)).reshape(high * mid, part_rows, -1).astype(BF16)
        for terms in (in_terms, out_terms, attn_terms)
    ]
    summed = far(jnp.concatenate(values, axis=2))
    sum_in, sum_out, sum_attn = summed[:, :units], summed[:, units : 2 * units], summed[:, 2 * units :]
    short = lax.all_to_all(after(short, mine), both, 0, 0, tiled=True)
    short = jnp.sum(after(short, summed), axis=0)
    sum_qkv = sum_attn[:, : 3 * local].reshape(-1, 3, local)
    sum_proj = sum_attn[:, 3 * local :].T

    plain = short[: 6 * part_rows].reshape(6, part_rows)
    sum_qv = short[6 * part_rows : 6 * part_rows + width // dp_count].reshape(2, -1)
    sum_bin = short[6 * part_rows + width // dp_count :]
    return (
        block_out,
        grad_tokens,
        plain[0],
        plain[1],
        sum_qkv,
        sum_qv,
        sum_proj,
        plain[4],
        plain[2],
        plain[3],
        sum_in,
        sum_bin,
        sum_out.T,
        plain[5],
    )


def solution(mesh):
    return jax.shard_map(
        shards,
        mesh=mesh,
        in_specs=(
            P("dp", None),
            P("dp"),
            P(),
            P("dp", None),
            P(),
            P(),
            P(None, None, "mp"),
            P(None, "mp"),
            P("mp", None),
            P(),
            P(),
            P(),
            P(None, "mp"),
            P("mp"),
            P("mp", None),
            P(),
            P("dp", None),
        ),
        out_specs=(
            P("dp", None),
            P("dp", None),
            P("dp"),
            P("dp"),
            P("dp", None, "mp"),
            P(None, ("mp", "dp")),
            P("mp", "dp"),
            P("dp"),
            P("dp"),
            P("dp"),
            P("dp", "mp"),
            P(("mp", "dp")),
            P("mp", "dp"),
            P("dp"),
        ),
        check_vma=False,
    )
```

```python
import functools

import jax
import jax.numpy as jnp
from jax import lax
from jax.experimental import pallas as pl
from jax.experimental.pallas import tpu as pltpu
from jax.sharding import PartitionSpec as P

HEAD_DIM = 64
NORM_EPS = 1e-06
NEG_FILL = -1e30
SCORE_SCALE = HEAD_DIM ** (-0.5)
MAX_CLIP = 256
LANES = 128
F32 = jnp.float32
BF16 = jnp.bfloat16
MIB = 1 << 20
SMALL = pl.CostEstimate(flops=1 << 20, bytes_accessed=1 << 20, transcendentals=0)


def nn(left, right):
    return lax.dot_general(left, right, (((1,), (0,)), ((), ())), preferred_element_type=F32)


def nt(left, right):
    return lax.dot_general(left, right, (((1,), (1,)), ((), ())), preferred_element_type=F32)


def vmem():
    return pl.BlockSpec(memory_space=pltpu.VMEM)


def hbm():
    return pl.BlockSpec(memory_space=pltpu.HBM)


def anywhere():
    return pl.BlockSpec(memory_space=pl.ANY)


def smem():
    return pl.BlockSpec(memory_space=pltpu.SMEM)


def params(mib):
    return pltpu.CompilerParams(vmem_limit_bytes=mib * MIB)


def shape(dims, dtype):
    return jax.ShapeDtypeStruct(dims, dtype)


def row_stats(vector):
    mean = jnp.mean(vector, axis=-1, keepdims=True)
    centred = vector - mean
    spread = jnp.mean(centred * centred, axis=-1, keepdims=True)
    return centred, lax.rsqrt(spread + NORM_EPS)


def on_lanes(column):
    return jnp.broadcast_to(column, (column.shape[0], LANES))


def wide_rsqrt(inv, here, width):
    return jnp.concatenate([inv[here, :]] * (width // LANES), axis=1)


def row_sum(block):
    return jnp.sum(block, axis=0, keepdims=True)


def fold_rows(block):
    rows, width = block.shape
    return jnp.sum(block.reshape(rows // 8, 8, width), axis=0)


def pick_kernel(index, source, *refs):
    picked = refs[-1]

    def move(i, carry):
        picked[i] = source[index[i]]
        return carry

    lax.fori_loop(0, picked.shape[0], move, 0, unroll=4)


def pick(source, index, *after):
    dims = index.shape + source.shape[1:]
    return pl.pallas_call(
        pick_kernel,
        out_shape=shape(dims, source.dtype),
        in_specs=[smem(), vmem()] + [hbm()] * len(after),
        out_specs=vmem(),
        compiler_params=params(16),
        cost_estimate=SMALL,
        name="pick",
    )(index, source, *after)


def move(source, target, sem):
    return pltpu.make_async_copy(source, target, sem)


PARTS = 4


def part_moves(pairs, sems):
    moves = []
    for c in range(PARTS):
        row = []
        for n, (source, target) in enumerate(pairs):
            count = source.shape[0] // PARTS
            here = pl.ds(c * count, count)
            row.append(move(source.at[here, :], target.at[here, :], sems.at[n, c]))
        moves.append(row)
    return moves


def start_all(moves):
    for one in moves:
        one.start()


def wait_all(moves):
    for one in moves:
        one.wait()


def interleave(*streams):
    order = sorted(
        ((n + 0.5) / len(stream), which, n)
        for which, stream in enumerate(streams)
        for n in range(len(stream))
    )
    for _, which, n in order:
        streams[which][n]()


def spread_clips(seg_row, seg_b):
    for i in range(seg_b.shape[0] // LANES):
        here = pl.ds(i * LANES, LANES)
        seg_b[here, :] = jnp.broadcast_to(seg_row[:, here], (LANES, LANES)).T


def key_window(j, rows):
    window = min(rows, LANES + 2 * MAX_CLIP)
    here = pl.ds(pl.multiple_of(j * LANES, LANES), LANES)
    first = pl.multiple_of(jnp.clip(j * LANES - MAX_CLIP, 0, rows - window), LANES)
    return here, pl.ds(first, window)


def set_bias(bias, seg_b, seg_row, here, keys):
    filled = jnp.where(seg_b[keys, :] == seg_row[:, here], 0.0, NEG_FILL)
    bias[:, pl.ds(0, LANES)] = filled
    bias[:, pl.ds(LANES, LANES)] = filled


def two_heads(block):
    lane = lax.broadcasted_iota(jnp.int32, block.shape, 1)
    return jnp.concatenate(
        [block * (lane // HEAD_DIM == e).astype(BF16) for e in range(2)], axis=0
    )


def attention_kernel(
    blend, flags, seg_row, vecs, biases, tok, own, oth, w3, wp, *refs
):
    mixed, n1, normed, inv, q, k, v, att, part, lse = refs[-32:-22]
    (
        tok_v, own_v, oth_v, w3_v, wp_v, mixed_v, n1_v, q_v, k_v, v_v, att_v, part_v,
        vt, att_t, seg_b, bias, ones, normed_v, inv_v, in_sems, half_sems, out_sems,
    ) = refs[-22:]
    rows, width = tok.shape
    local = wp.shape[0]
    half_rows = rows // 2
    ratio = blend[0]
    blk = 32
    big = 256

    loads = [
        move(source, target, in_sems.at[n])
        for n, (source, target) in enumerate([(tok, tok_v), (w3, w3_v), (wp, wp_v)])
    ]
    halves = part_moves([(own, own_v), (oth, oth_v)], half_sems)
    loads[0].start()
    for part_of in halves:
        start_all(part_of)
    start_all(loads[1:])
    early = [
        move(source, target, out_sems.at[n])
        for n, (source, target) in enumerate(
            [
                (mixed_v, mixed), (n1_v, n1), (normed_v, normed), (inv_v, inv),
                (q_v, q), (k_v, k), (v_v, v),
            ]
        )
    ]
    ones[...] = jnp.ones_like(ones)
    spread_clips(seg_row, seg_b)

    loads[0].wait()
    steps = half_rows // PARTS // blk
    for n, src, half in ((0, own_v, flags[0]), (1, oth_v, 1 - flags[0])):
        for c in range(PARTS):
            halves[c][n].wait()

            def mix(i, carry, src=src, half=half, c=c):
                low = (c * steps + i) * blk
                here = pl.ds(pl.multiple_of(half * half_rows + low, blk), blk)
                there = pl.ds(pl.multiple_of(low, blk), blk)
                mine, other = tok_v[here, :].astype(F32), src[there, :].astype(F32)
                blended = ratio * mine + (1.0 - ratio) * other
                mixed_v[here, :] = blended
                centred, scale = row_stats(blended)
                inv_v[here, :] = on_lanes(scale)
                plain = centred * scale
                normed_v[here, :] = plain.astype(BF16)
                n1_v[here, :] = (plain * vecs[0:1, :] + vecs[1:2, :]).astype(BF16)
                return carry

            lax.fori_loop(0, steps, mix, 0, unroll=True)
    start_all(early[:4])

    loads[1].wait()
    for i in range(rows // big):
        here = pl.ds(i * big, big)
        rows_in = n1_v[here, :]
        queries = (nn(rows_in, w3_v[0]) + biases[0:1, :local]).astype(BF16).astype(F32)
        q_v[here, :] = (queries * SCORE_SCALE).astype(BF16)
        k_v[here, :] = nn(rows_in, w3_v[1]).astype(BF16)
        values = (nn(rows_in, w3_v[2]) + biases[0:1, local:]).astype(BF16)
        v_v[here, :] = values
        vt[:, here] = values.T
    start_all(early[4:])

    def attend(j, carry):
        here, keys = key_window(j, rows)
        set_bias(bias, seg_b, seg_row, here, keys)
        for p in range(local // LANES):
            pair = pl.ds(p * LANES, LANES)
            scores = nt(k_v[keys, pair], two_heads(q_v[here, pair])) + bias[...]
            top = jnp.max(scores, axis=0, keepdims=True)
            grown = jnp.exp(scores - top).astype(BF16)
            total = nn(ones[...], grown)[:1]
            out = (nn(vt[pair, keys], grown) / total).astype(BF16)
            logs = top + jnp.log(total)
            for e in range(2):
                lanes = slice(e * LANES, e * LANES + LANES)
                head = slice(e * HEAD_DIM, e * HEAD_DIM + HEAD_DIM)
                att_t[pl.ds(p * LANES + e * HEAD_DIM, HEAD_DIM), here] = out[head, lanes]
                lse[pl.ds(2 * p + e, 1), here] = logs[:, lanes]
        return carry

    lax.fori_loop(0, rows // LANES, attend, 0)

    loads[2].wait()
    last = []
    for i in range(rows // big):
        here = pl.ds(i * big, big)
        block = att_t[:, here].T
        att_v[here, :] = block
        part_v[here, :] = nn(block, wp_v[...]).astype(BF16)
        last.append(move(part_v.at[here, :], part.at[here, :], out_sems.at[8 + i]))
        last[-1].start()
    last.append(move(att_v, att, out_sems.at[7]))
    last[-1].start()
    wait_all(early + last)


def attention(blend, flags, segment, vecs, biases, tok, own, oth, w3, wp, *before):
    rows, width = tok.shape
    local = wp.shape[0]
    window = min(rows, LANES + 2 * MAX_CLIP)
    thin = shape((rows, local), BF16)
    tall = shape((rows, width), BF16)
    return pl.pallas_call(
        attention_kernel,
        out_shape=(
            shape((rows, width), F32), tall, tall, shape((rows, LANES), F32),
            thin, thin, thin, thin, tall, shape((local // HEAD_DIM, rows), F32),
        ),
        in_specs=[smem(), smem()] + [vmem()] * 3 + [anywhere()] * 3 + [hbm()] * (2 + len(before)),
        out_specs=[hbm()] * 9 + [vmem()],
        scratch_shapes=[
            pltpu.VMEM((rows, width), BF16),
            pltpu.VMEM((rows // 2, width), BF16),
            pltpu.VMEM((rows // 2, width), BF16),
            pltpu.VMEM(w3.shape, BF16),
            pltpu.VMEM(wp.shape, BF16),
            pltpu.VMEM((rows, width), F32),
            pltpu.VMEM((rows, width), BF16),
            pltpu.VMEM((rows, local), BF16),
            pltpu.VMEM((rows, local), BF16),
            pltpu.VMEM((rows, local), BF16),
            pltpu.VMEM((rows, local), BF16),
            pltpu.VMEM((rows, width), BF16),
            pltpu.VMEM((local, rows), BF16),
            pltpu.VMEM((local, rows), BF16),
            pltpu.VMEM((rows, LANES), F32),
            pltpu.VMEM((window, 2 * LANES), F32),
            pltpu.VMEM((16, window), BF16),
            pltpu.VMEM((rows, width), BF16),
            pltpu.VMEM((rows, LANES), F32),
            pltpu.SemaphoreType.DMA((3,)),
            pltpu.SemaphoreType.DMA((2, PARTS)),
            pltpu.SemaphoreType.DMA((8 + rows // 256,)),
        ],
        compiler_params=params(60),
        cost_estimate=SMALL,
        name="attention",
    )(
        blend, flags, segment, vecs, biases, tok, own, oth, w3, wp, *before,
    )


ERFC_SLOPE = 0.47
ERFC_COEFFS = (
    0.2663094668265691,
    0.2480096137831850,
    0.3362712657560771,
    -0.1262288063821733,
    0.6076790117752645,
    -0.4204702410368928,
    0.0884296765518492,
)


def gelu_parts(pre):
    bell = jnp.exp(pre * pre * -0.5)
    t = 1.0 / (1.0 + jnp.abs(pre) * (ERFC_SLOPE * 0.5**0.5))
    poly = 0.5 * ERFC_COEFFS[-1]
    for coeff in ERFC_COEFFS[-2::-1]:
        poly = poly * t + 0.5 * coeff
    tail = poly * t * bell
    cdf = jnp.where(pre >= 0, 1.0 - tail, tail)
    return pre * cdf, cdf + pre * bell * 0.3989422804014327


def turn_into(target, source, blocks):
    rows = source.shape[0]
    big = 256
    for i in range(rows // big):
        here = pl.ds(i * big, big)
        turned = source[here, :].T
        for start, place, count in blocks:
            target[pl.ds(place, count), here] = turned[start : start + count]


def lead_blocks(width, lead_rows):
    runs = width // lead_rows
    return [
        (run * lead_rows, ((run % 2) * (runs // 2) + run // 2) * lead_rows, lead_rows)
        for run in range(runs)
    ]


def feed_kernel(
    in_rows, out_rows, flags, vecs, biases, mixed, p_own, p_oth, cot, cot_t,
    w_in, w_out, w_out_one, w_out_two,
    hidden, part, gn_part, in_keep, in_send, out_keep, out_send, normed, inv, g_bin, g_bout,
    mixed_v, own_v, oth_v, cot_v, cot_tv, w_in_v, w_out_v, n2, n2_t, act, gp,
    g_in, g_out, normed_v, inv_v, in_sems, turn_sems, weight_sems, out_sems, grad_sems,
):
    rows, width = mixed.shape
    units = w_in.shape[1]
    blk = 32
    big = 256
    sub = 16
    home = flags[1] == 1
    across = flags[2]
    kept_out = jnp.where(home, flags[0], 1 - flags[0]) if in_rows != out_rows else across
    sides = (across, kept_out)

    loads = part_moves(
        [(mixed, mixed_v), (p_own, own_v), (p_oth, oth_v), (cot, cot_v)], in_sems
    )
    for part_of in loads:
        start_all(part_of)

    weights = [move(w_in, w_in_v, weight_sems.at[0])]
    weights[0].start()
    half = w_out.shape[0] // 2
    for n, (got, place) in enumerate([(w_out_one, across), (w_out_two, 1 - across)]):
        spot = pl.ds(pl.multiple_of(place * half, half), half)
        sem = weight_sems.at[1 + n]
        weights.append(move(w_out.at[spot, :], w_out_v.at[spot, :], sem))

        @pl.when(home)
        def _(spot=spot, sem=sem):
            move(w_out.at[spot, :], w_out_v.at[spot, :], sem).start()

        @pl.when(jnp.logical_not(home))
        def _(got=got, spot=spot, sem=sem):
            move(got, w_out_v.at[spot, :], sem).start()

    turns = [
        move(cot_t.at[pl.ds(start, count), :], cot_tv.at[pl.ds(place, count), :], turn_sems.at[n])
        for n, (start, place, count) in enumerate(lead_blocks(width, out_rows))
    ]
    start_all(turns)

    g_bout[...] = jnp.zeros_like(g_bout)
    steps = rows // PARTS // blk
    for c in range(PARTS):
        wait_all(loads[c])

        def norm(i, carry, c=c):
            here = pl.ds(pl.multiple_of((c * steps + i) * blk, blk), blk)
            attn = own_v[here, :].astype(F32) + oth_v[here, :].astype(F32)
            total = mixed_v[here, :] + attn + vecs[4:5, :]
            mixed_v[here, :] = total
            centred, scale = row_stats(total)
            inv_v[here, :] = on_lanes(scale)
            plain = centred * scale
            normed_v[here, :] = plain.astype(BF16)
            n2[here, :] = (plain * vecs[2:3, :] + vecs[3:4, :]).astype(BF16)
            g_bout[...] += fold_rows(cot_v[here, :].astype(F32))
            return carry

        lax.fori_loop(0, steps, norm, 0, unroll=4)
    stores = [
        move(source, target, out_sems.at[0, n])
        for n, (source, target) in enumerate(
            [(mixed_v, hidden), (normed_v, normed), (inv_v, inv)]
        )
    ]
    start_all(stores)
    turn_into(n2_t, n2, lead_blocks(width, in_rows))
    wait_all(weights)

    sums = [jnp.zeros((8, width), F32) for _ in range(units // width)]
    for i in range(rows // big):
        here = pl.ds(i * big, big)
        for j in range(units // width):
            cols = pl.ds(j * width, width)
            pre_all = nn(n2[here, :], w_in_v[:, cols])
            grad_all = nt(cot_v[here, :], w_out_v[cols, :])
            for s in range(big // sub):
                rng = slice(s * sub, s * sub + sub)
                value, slope = gelu_parts(pre_all[rng] + biases[1 + j : 2 + j, :])
                grad = grad_all[rng] * slope
                sums[j] += fold_rows(grad)
                spot = pl.ds(i * big + s * sub, sub)
                act[spot, cols] = value.astype(BF16)
                gp[spot, cols] = grad.astype(BF16)
        oth_v[here, :] = nt(gp[here, :], w_in_v[...]).astype(BF16)
        own_v[here, :] = nn(act[here, :], w_out_v[...]).astype(BF16)
        for n, (source, target) in enumerate([(oth_v, gn_part), (own_v, part)]):
            stores.append(move(source.at[here, :], target.at[here, :], out_sems.at[1 + n, i]))
            stores[-1].start()
    for j in range(units // width):
        g_bin[:, pl.ds(j * width, width)] = sums[j]

    wait_all(turns)
    half = width // 2
    for n, (turned, right, buf, keep, send) in enumerate(
        [(n2_t, gp, g_in, in_keep, in_send), (cot_tv, act, g_out, out_keep, out_send)]
    ):
        for side in range(2):
            lines = pl.ds(side * half, half)
            for j in range(units // width):
                cols = pl.ds(j * width, width)
                buf[side, :, cols] = nn(turned[lines, :], right[:, cols]).astype(BF16)
        for m, (side, target) in enumerate([(1 - sides[n], send), (sides[n], keep)]):
            stores.append(move(buf.at[side], target, grad_sems.at[n, m]))
            stores[-1].start()
    wait_all(stores)


def feed(
    in_rows, out_rows, flags, vecs, biases, mixed, p_own, p_oth, cot, cot_t,
    w_in, w_out, w_out_one, w_out_two,
):
    rows, width = mixed.shape
    units = w_in.shape[1]
    tall = shape((rows, width), BF16)
    grad = shape((width // 2, units), BF16)
    return pl.pallas_call(
        functools.partial(feed_kernel, in_rows, out_rows),
        out_shape=(
            shape((rows, width), F32), tall, tall, grad, grad, grad, grad,
            tall, shape((rows, LANES), F32), shape((8, units), F32), shape((8, width), F32),
        ),
        in_specs=[smem()] + [vmem()] * 2 + [hbm()] * 2 + [anywhere()] + [hbm()] * 6,
        out_specs=[hbm()] * 9 + [vmem()] * 2,
        scratch_shapes=[
            pltpu.VMEM((rows, width), F32),
            pltpu.VMEM((rows, width), BF16),
            pltpu.VMEM((rows, width), BF16),
            pltpu.VMEM((rows, width), BF16),
            pltpu.VMEM((width, rows), BF16),
            pltpu.VMEM(w_in.shape, BF16),
            pltpu.VMEM(w_out.shape, BF16),
            pltpu.VMEM((rows, width), BF16),
            pltpu.VMEM((width, rows), BF16),
            pltpu.VMEM((rows, units), BF16),
            pltpu.VMEM((rows, units), BF16),
            pltpu.VMEM((2, width // 2, units), BF16),
            pltpu.VMEM((2, width // 2, units), BF16),
            pltpu.VMEM((rows, width), BF16),
            pltpu.VMEM((rows, LANES), F32),
            pltpu.SemaphoreType.DMA((4, PARTS)),
            pltpu.SemaphoreType.DMA((width // out_rows,)),
            pltpu.SemaphoreType.DMA((3,)),
            pltpu.SemaphoreType.DMA((3, rows // 256)),
            pltpu.SemaphoreType.DMA((2, 2)),
        ],
        compiler_params=params(60),
        cost_estimate=SMALL,
        name="feed",
    )(
        flags, vecs, biases, mixed, p_own, p_oth, cot, cot_t,
        w_in, w_out, w_out_one, w_out_two,
    )


def attention_back_kernel(
    lead_rows, flags, vecs, seg_row, lse, g_bin, g_bout, g_own, g_oth, cot, normed, inv,
    wp, att, k, q, v, w3, n1, normed_one, hidden, out_own, out_oth,
    gh, part, keep, send, block_out, short,
    hidden_v, gh_v, own_v, oth_v, cot_v, normed_v, inv_v, wp_v, att_v, k_v, q_v, v_v, w3_v, n1_v, one_v, low_v, part_v,
    sums, d_out, kt, dq_t, dk, dv, delta, seg_b, bias, raw, raw_g, low_p, low_g, n1_t, gh_t, grad_v, out,
    in_sems, row_sems, out_sems, last_sems,
):
    rows, width = cot.shape
    local = wp.shape[0]
    blk = 32
    big = 256
    blocks = lead_blocks(width, lead_rows)
    across = flags[2]
    row_loads = part_moves(
        [(g_own, own_v), (g_oth, oth_v), (cot, cot_v), (normed, normed_v), (inv, inv_v)],
        row_sems,
    )
    for part_of in row_loads:
        start_all(part_of)
    loads = [
        move(source, target, in_sems.at[n])
        for n, (source, target) in enumerate(
            [
                (wp, wp_v), (att, att_v), (k, k_v), (q, q_v), (v, v_v), (w3, w3_v), (n1, n1_v),
                (normed_one, one_v), (hidden, hidden_v),
            ]
        )
    ]
    start_all(loads)
    sums[...] = jnp.zeros_like(sums)
    dk[...] = jnp.zeros_like(dk)
    dv[...] = jnp.zeros_like(dv)
    spread_clips(seg_row, seg_b)

    steps = rows // PARTS // blk
    for c in range(PARTS):
        wait_all(row_loads[c])

        def norm(i, carry, c=c):
            here = pl.ds(pl.multiple_of((c * steps + i) * blk, blk), blk)
            grad = own_v[here, :].astype(F32) + oth_v[here, :].astype(F32)
            plain = normed_v[here, :].astype(F32)
            scaled = grad * vecs[2:3, :]
            mean_one = jnp.mean(scaled, axis=-1, keepdims=True)
            mean_two = jnp.mean(scaled * plain, axis=-1, keepdims=True)
            scale = wide_rsqrt(inv_v, here, width)
            back = cot_v[here, :].astype(F32) + scale * (scaled - mean_one - plain * mean_two)
            gh_v[here, :] = back
            low_v[here, :] = back.astype(BF16)
            sums[0] += fold_rows(grad * plain)
            sums[1] += fold_rows(grad)
            sums[2] += fold_rows(back)
            return carry

        lax.fori_loop(0, steps, norm, 0, unroll=4)
    stores = [move(gh_v, gh, out_sems.at[0])]
    stores[0].start()
    late = [
        move(source, target, in_sems.at[len(loads) + n])
        for n, (source, target) in enumerate([(out_own, own_v), (out_oth, oth_v)])
    ]
    start_all(late)

    wait_all(loads[:3])
    heads = local // HEAD_DIM
    lane = lax.broadcasted_iota(jnp.int32, (delta.shape[0], local), 1)
    row = lax.broadcasted_iota(jnp.int32, (delta.shape[0], local), 0)
    of_head = (lane // HEAD_DIM == row).astype(BF16)
    for i in range(rows // big):
        here = pl.ds(i * big, big)
        grad_out = nt(low_v[here, :], wp_v[...]).astype(BF16)
        d_out[here, :] = grad_out
        product = grad_out.astype(F32) * att_v[here, :].astype(F32)
        coarse = product.astype(BF16)
        fine = (product - coarse.astype(F32)).astype(BF16)
        delta[:, here] = nt(of_head, coarse) + nt(of_head, fine)
        kt[:, here] = k_v[here, :].T
    wait_all(loads[3:])

    pairs = heads // 2
    window = bias.shape[0]
    strip = 128
    strips = window // strip

    def attend(j, carry):
        here, keys = key_window(j, rows)
        first = pl.multiple_of(keys.start, LANES)
        set_bias(bias, seg_b, seg_row, here, keys)
        blocks_two = {}

        def two(p):
            if p not in blocks_two:
                pair = pl.ds(p * LANES, LANES)
                blocks_two[p] = (two_heads(q_v[here, pair]), two_heads(d_out[here, pair]))
            return blocks_two[p]

        def at_strip(n):
            return (
                pl.ds(pl.multiple_of(first + n * strip, strip), strip),
                pl.ds(n * strip, strip),
            )

        def products(p):
            pair = pl.ds(p * LANES, LANES)

            def scores(n):
                def run():
                    some, at = at_strip(n)
                    raw[p % 2, at, :] = nt(k_v[some, pair], two(p)[0])

                return run

            def grads(n):
                def run():
                    some, at = at_strip(n)
                    raw_g[p % 2, at, :] = nt(v_v[some, pair], two(p)[1])

                return run

            return [make(n) for n in range(strips) for make in (scores, grads)]

        def softmax_back(p):
            tops = jnp.concatenate([lse[pl.ds(2 * p + e, 1), here] for e in range(2)], axis=1)
            inner = jnp.concatenate([delta[pl.ds(2 * p + e, 1), here] for e in range(2)], axis=1)
            half = strip // 2

            def run_at(n):
                def run():
                    at = pl.ds(n * half, half)
                    probs = jnp.exp(raw[p % 2, at, :] + bias[at, :] - tops)
                    low_p[p % 2, at, :] = probs.astype(BF16)
                    low_g[p % 2, at, :] = (probs * (raw_g[p % 2, at, :] - inner)).astype(BF16)

                return run

            return [run_at(n) for n in range(2 * strips)]

        def sums_of(p):
            pair = pl.ds(p * LANES, LANES)

            def keys_of(n):
                def run():
                    some, at = at_strip(n)
                    dk[some, pair] += nn(low_g[p % 2, at, :], two(p)[0])

                return run

            def values_of(n):
                def run():
                    some, at = at_strip(n)
                    dv[some, pair] += nn(low_p[p % 2, at, :], two(p)[1])

                return run

            def queries():
                grad_q = nn(kt[pair, keys], low_g[p % 2]) * SCORE_SCALE
                for e in range(2):
                    lanes = slice(e * LANES, e * LANES + LANES)
                    head = slice(e * HEAD_DIM, e * HEAD_DIM + HEAD_DIM)
                    dq_t[pl.ds(p * LANES + e * HEAD_DIM, HEAD_DIM), here] = grad_q[head, lanes]

            return [make(n) for n in range(strips) for make in (keys_of, values_of)] + [queries]

        def turns():
            for target, source in ((n1_t, n1_v), (gh_t, low_v)):
                turned = source[here, :].T
                for start, place, count in blocks:
                    target[pl.ds(place, count), here] = turned[start : start + count]

        interleave(products(0), [turns])
        for p in range(pairs):
            matrix = (products(p + 1) if p + 1 < pairs else []) + (sums_of(p - 1) if p else [])
            interleave(softmax_back(p), matrix)
        interleave(sums_of(pairs - 1))
        return carry

    lax.fori_loop(0, rows // LANES, attend, 0)

    wait_all(late)
    q_sum = jnp.zeros((8, local), F32)
    v_sum = jnp.zeros((8, local), F32)
    gain_sum = jnp.zeros((8, width), F32)
    shift_sum = jnp.zeros((8, width), F32)
    for i in range(rows // big):
        here = pl.ds(i * big, big)
        grad_q, grad_k, grad_val = dq_t[:, here].T, dk[here, :], dv[here, :]
        q_sum += fold_rows(grad_q)
        v_sum += fold_rows(grad_val)
        lows = [grad.astype(BF16) for grad in (grad_q, grad_k, grad_val)]
        total = sum(nt(low, w3_v[n]) for n, low in enumerate(lows))
        part_v[here, :] = total.astype(BF16)
        gain_sum += fold_rows(total * one_v[here, :].astype(F32))
        shift_sum += fold_rows(total)
        for n, low in enumerate(lows):
            grad_v[here, pl.ds(n * local, local)] = low
        fed = own_v[here, :].astype(F32) + oth_v[here, :].astype(F32)
        cot_v[here, :] = (hidden_v[here, :] + fed + vecs[5:6, :]).astype(BF16)
        for n, (source, target) in enumerate([(part_v, part), (cot_v, block_out)]):
            stores.append(move(source.at[here, :], target.at[here, :], last_sems.at[n, i]))
            stores[-1].start()
    units = g_bin.shape[1]
    qv_sum = jnp.concatenate([q_sum, v_sum], axis=1)
    listed = [gain_sum, shift_sum, sums[0], sums[1], sums[2], g_bout[...], qv_sum]
    listed += [g_bin[:, pl.ds(n, width)] for n in range(0, units, width)]
    for n, block in enumerate(listed):
        short[pl.ds(n, 1), :] = row_sum(block)
    half = width // 2
    for side in range(2):
        lines = pl.ds(side * half, half)
        for n in range(3):
            cols = pl.ds(n * local, local)
            out[side, :, cols] = nn(n1_t[lines, :], grad_v[:, cols]).astype(BF16)
        out[side, :, pl.ds(3 * local, local)] = nn(gh_t[lines, :], att_v[...]).astype(BF16)
    for n, (side, target) in enumerate([(1 - across, send), (across, keep)]):
        stores.append(move(out.at[side], target, out_sems.at[1 + n]))
        stores[-1].start()
    wait_all(stores)


def attention_back(
    lead_rows, flags, vecs, segment, lse, g_bin, g_bout, g_own, g_oth, cot, normed, inv,
    wp, att, k, q, v, w3, n1, normed_one, hidden, out_own, out_oth,
):
    rows, width = cot.shape
    local = wp.shape[0]
    window = min(rows, LANES + 2 * MAX_CLIP)
    tall, thin = pltpu.VMEM((rows, width), BF16), pltpu.VMEM((rows, local), BF16)
    turned = pltpu.VMEM((width, rows), BF16)
    half = (width // 2, 4 * local)
    return pl.pallas_call(
        functools.partial(attention_back_kernel, lead_rows),
        out_shape=(
            shape((rows, width), F32),
            shape((rows, width), BF16),
            shape(half, BF16),
            shape(half, BF16),
            shape((rows, width), BF16),
            shape((7 + g_bin.shape[1] // width, width), F32),
        ),
        in_specs=[smem()] + [vmem()] * 5 + [hbm()] + [anywhere()] + [hbm()] * 13 + [anywhere()],
        out_specs=[hbm()] * 5 + [vmem()],
        scratch_shapes=[
            pltpu.VMEM((rows, width), F32),
            pltpu.VMEM((rows, width), F32),
            tall, tall, tall, tall,
            pltpu.VMEM((rows, LANES), F32),
            pltpu.VMEM(wp.shape, BF16),
            thin, thin, thin, thin,
            pltpu.VMEM(w3.shape, BF16),
            tall, tall, tall, tall,
            pltpu.VMEM((3, 8, width), F32),
            thin,
            pltpu.VMEM((local, rows), BF16),
            pltpu.VMEM((local, rows), F32),
            pltpu.VMEM((rows, local), F32),
            pltpu.VMEM((rows, local), F32),
            pltpu.VMEM((8, rows), F32),
            pltpu.VMEM((rows, LANES), F32),
            pltpu.VMEM((window, 2 * LANES), F32),
            pltpu.VMEM((2, window, 2 * LANES), F32),
            pltpu.VMEM((2, window, 2 * LANES), F32),
            pltpu.VMEM((2, window, 2 * LANES), BF16),
            pltpu.VMEM((2, window, 2 * LANES), BF16),
            turned, turned,
            pltpu.VMEM((rows, 3 * local), BF16),
            pltpu.VMEM((2,) + half, BF16),
            pltpu.SemaphoreType.DMA((11,)),
            pltpu.SemaphoreType.DMA((5, PARTS)),
            pltpu.SemaphoreType.DMA((3,)),
            pltpu.SemaphoreType.DMA((2, rows // 256)),
        ],
        compiler_params=params(60),
        cost_estimate=SMALL,
        name="attention_back",
    )(
        flags, vecs, segment, lse, g_bin, g_bout, g_own, g_oth, cot, normed, inv,
        wp, att, k, q, v, w3, n1, normed_one, hidden, out_own, out_oth,
    )


def mixed_back_kernel(blend, vecs, gh, g_own, g_oth, normed, inv, outgoing, kept, *refs):
    gh_v, own_v, oth_v, normed_v, inv_v, leave_v, kept_v, in_sems, out_sems = refs
    ratio = blend[0]
    rows, width = gh.shape
    blk = 32
    loads = part_moves(
        [(gh, gh_v), (g_own, own_v), (g_oth, oth_v), (normed, normed_v), (inv, inv_v)], in_sems
    )
    stores = part_moves([(leave_v, outgoing), (kept_v, kept)], out_sems)
    for part_of in loads:
        start_all(part_of)
    steps = rows // PARTS // blk
    for c in range(PARTS):
        wait_all(loads[c])

        def norm(i, carry, c=c):
            here = pl.ds(pl.multiple_of((c * steps + i) * blk, blk), blk)
            grad = own_v[here, :].astype(F32) + oth_v[here, :].astype(F32)
            plain = normed_v[here, :].astype(F32)
            scaled = grad * vecs[0:1, :]
            mean_one = jnp.mean(scaled, axis=-1, keepdims=True)
            mean_two = jnp.mean(scaled * plain, axis=-1, keepdims=True)
            scale = wide_rsqrt(inv_v, here, width)
            back = gh_v[here, :] + scale * (scaled - mean_one - plain * mean_two)
            leave_v[here, :] = ((1.0 - ratio) * back).astype(BF16)
            kept_v[here, :] = (ratio * back).astype(BF16)
            return carry

        lax.fori_loop(0, steps, norm, 0, unroll=4)
        start_all(stores[c])
    for part_of in stores:
        wait_all(part_of)


def mixed_back(blend, vecs, gh, g_own, g_oth, normed, inv):
    rows, width = gh.shape
    tall = pltpu.VMEM((rows, width), BF16)
    return pl.pallas_call(
        mixed_back_kernel,
        out_shape=(shape((rows, width), BF16), shape((rows, width), BF16)),
        in_specs=[smem(), vmem()] + [hbm()] * 2 + [anywhere()] + [hbm()] * 2,
        out_specs=[hbm(), hbm()],
        scratch_shapes=[
            pltpu.VMEM((rows, width), F32),
            tall, tall, tall, pltpu.VMEM((rows, LANES), F32), tall, tall,
            pltpu.SemaphoreType.DMA((5, PARTS)),
            pltpu.SemaphoreType.DMA((2, PARTS)),
        ],
        compiler_params=params(60),
        cost_estimate=SMALL,
        name="mixed_back",
    )(blend, vecs, gh, g_own, g_oth, normed, inv)


def shards(
    tokens,
    mix_blend,
    partner,
    clip_ids,
    gain_one,
    shift_one,
    qkv_weight,
    qv_bias,
    proj_weight,
    proj_bias,
    gain_two,
    shift_two,
    in_weight,
    in_bias,
    out_weight,
    out_bias,
    cotangent,
):
    rows, width = tokens.shape
    dp_count = lax.axis_size("dp")
    both = ("dp", "mp")
    bits = dp_count.bit_length() - 1
    seq = lax.axis_index("dp")
    mp = lax.axis_index("mp")
    core = lax.rem(seq, 2)
    home = core == mp
    all_dp = range(dp_count)

    def joint(d, m):
        return 2 * d + m

    core_swap = [(d, d ^ 1) for d in all_dp]
    home_to_pair = [(joint(d, d & 1), joint(d, 1 - (d & 1))) for d in all_dp]
    pair_to_home = [(joint(d, 1 - (d & 1)), joint(d, d & 1)) for d in all_dp]
    weight_move = home_to_pair + [
        (joint(d, 1 - (d & 1)), joint(d ^ 1, 1 - (d & 1))) for d in all_dp
    ]

    def swap(value):
        return lax.ppermute(value, "dp", core_swap)

    def chip_value(value):
        return jnp.where(home, value, swap(value))

    def after(value, *others):
        return lax.optimization_barrier((value,) + others)[0]

    def half_weight(value):
        return lax.ppermute(value, both, weight_move)

    part_rows = width // dp_count
    lead = min(n for n in range(1, bits) if (part_rows << n) % 16 == 0)
    lead_rows = part_rows << lead
    across = lax.rem(seq >> lead, 2)
    flags = jnp.stack([core, home.astype(jnp.int32), across]).astype(jnp.int32)

    def taken(value, index, axis):
        return lax.dynamic_index_in_dim(value, index, axis, keepdims=False)

    seq_small = chip_value(jnp.concatenate([mix_blend, clip_ids[0].astype(F32)]))
    blend, segment = seq_small[:1], seq_small[1:].reshape(1, rows)
    local = proj_weight.shape[0]
    units = in_bias.shape[0]
    half_small = jnp.concatenate([qv_bias.reshape(-1), in_bias])
    half_small = jnp.where(home, half_small, half_weight(half_small))
    biases = half_small.reshape(-1, width)
    vecs = jnp.stack([gain_one, shift_one, gain_two, shift_two, proj_bias, out_bias])

    w3 = half_weight(qkv_weight.transpose(1, 0, 2))
    wp = half_weight(proj_weight)

    def two_way(value):
        halves = value.reshape(2, value.shape[0] // 2, value.shape[1])
        one = half_weight(taken(halves, across, 0))
        moves = [(joint(d, 1 - (d & 1)), joint(d ^ (1 << lead), 1 - (d & 1))) for d in all_dp]
        return value, one, lax.ppermute(one, both, moves)

    ids = jnp.arange(2 * dp_count, dtype=jnp.int32)
    piece = rows // (2 * 2 * dp_count)
    sent = tokens.reshape(2, dp_count, 2, piece, width)
    sent = lax.dynamic_index_in_dim(sent, mp, 2, keepdims=False)
    spread = lax.all_to_all(sent.transpose(1, 0, 2, 3), "dp", 0, 0, tiled=True)
    wanted = partner[(ids // 4) * 2 + ids % 2] * 2 + (ids // 2) % 2
    source_of = jnp.sum(
        jnp.where(partner[:, None] == ids[None, :dp_count], ids[:dp_count, None], 0),
        axis=0,
        dtype=jnp.int32,
    )
    source = source_of[ids // 2]
    wanted_back = (source // 2) * 4 + (ids % 2) * 2 + source % 2
    chosen = pick(spread.reshape(2 * dp_count, piece, width), wanted, w3, wp, half_small)
    partner_own = lax.all_to_all(chosen, both, 0, 0, tiled=True).reshape(rows // 2, width)
    w_out = two_way(out_weight)
    w_in = half_weight(after(in_weight, w_out[1]))

    tok = chip_value(tokens)
    cot = chip_value(cotangent)
    cot_t = cot.T
    partner_oth = swap(after(partner_own, tok, cot, vecs, segment, wanted_back))

    mixed, n1, normed_one, inv_one, q, k, v, att, attn_part, lse = attention(
        blend, flags, segment, vecs, biases, tok, partner_own, partner_oth, w3, wp, w_out[2], cot_t
    )
    pair_first = part_rows % 16 == 0
    fed = feed(
        lead_rows, part_rows if pair_first else lead_rows, flags, vecs, biases,
        mixed, attn_part, swap(attn_part), cot, cot_t, w_in, *w_out,
    )
    hidden, out_part, gn2_part, in_keep, in_send, out_keep, out_send = fed[:7]
    normed_two, inv_two, g_bin, g_bout = fed[7:]
    gn2_oth = swap(gn2_part)

    high, mid = dp_count >> (lead + 1), 1 << (lead - 1)
    pair_and_core = pair_to_home + [(joint(d, d & 1), joint(d ^ 1, d & 1)) for d in all_dp]
    pair_diagonal = [(joint(d, 1 - (d & 1)), joint(d ^ 1, d & 1)) for d in all_dp]

    def total(*terms):
        return sum(term.astype(F32) for term in terms)

    def send_across(value):
        return lax.ppermute(value, "dp", [(d, d ^ (1 << lead)) for d in all_dp])

    def send_pair(value):
        value = value.reshape(high, mid, 2, part_rows, -1)
        one = lax.ppermute(taken(value, jnp.where(home, 1 - core, core), 2), both, pair_and_core)
        two = lax.ppermute(taken(value, 1 - core, 2), both, pair_diagonal)
        held = taken(value, core, 2)
        return jnp.where(home, held, jnp.zeros_like(held)), one, two

    def far(value, *others):
        for shift, left in ((1, mid), (lead + 1, high)):
            while left > 1:
                radix = min(4, left)
                left //= radix
                value = value.reshape((-1, left, radix) + value.shape[-2:]).astype(BF16)
                spot = lax.rem(seq >> shift, radix)
                got = [
                    lax.ppermute(
                        taken(value, spot ^ flip, 2),
                        "dp",
                        [(d, d ^ (flip << shift)) for d in all_dp],
                    )
                    for flip in range(1, radix)
                ]
                value = total(taken(value, spot, 2), *after(got, *others))
                shift += radix.bit_length() - 1
        return value.reshape(value.shape[-2:])

    in_got = send_across(in_send)
    if pair_first:
        out_got = [
            lax.ppermute(out_send, both, pair_and_core),
            lax.ppermute(out_keep, both, pair_diagonal),
        ]
        out_keep = jnp.where(home, out_keep, jnp.zeros_like(out_keep))
    else:
        out_got = [send_across(out_send)]
    gh, gn1_part, attn_keep, attn_send, block, short = attention_back(
        lead_rows, flags, vecs, segment, lse, g_bin, g_bout, gn2_part, gn2_oth, cot,
        normed_two, inv_two, wp, att, k, q, v, w3, n1, normed_one, hidden, out_part, swap(out_part),
    )
    block_got = half_weight(block)
    block_out = jnp.where(home, block, block_got)
    attn_got = send_across(attn_send)
    gn1_oth = swap(after(gn1_part, in_got, *out_got))
    in_terms = send_pair(total(in_keep, in_got).astype(BF16))
    outgoing, kept = mixed_back(blend, vecs, gh, gn1_part, gn1_oth, normed_one, inv_one)

    leaving = taken(outgoing.reshape(2, 2, dp_count, piece, width), core, 1)
    leaving = leaving.transpose(1, 0, 2, 3).reshape(2 * dp_count, piece, width)
    back = lax.all_to_all(leaving, both, 0, 0, tiled=True)

    out_value = total(out_keep, *after(out_got, leaving)).astype(BF16)
    if pair_first:
        out_value = out_value.reshape(high, 2, mid, part_rows, units)
        out_terms = (taken(out_value, across, 1), send_across(taken(out_value, 1 - across, 1)))
    else:
        out_terms = send_pair(out_value)
    kept = kept.reshape(2, rows // 2, width)
    kept_got = half_weight(taken(kept, 1 - mp, 0))

    def side_by_side(*groups):
        values = [total(*terms).reshape(high * mid, part_rows, -1) for terms in groups]
        return jnp.concatenate(values, axis=2).astype(BF16)

    feed_value = side_by_side(after(in_terms, leaving), after(out_terms, leaving))

    returning = pick(back, wanted_back, feed_value)
    attn_terms = send_pair(total(attn_keep, after(attn_got, returning)).astype(BF16))
    returned = lax.all_to_all(
        returning.reshape(dp_count, 2, piece, width), "dp", 0, 0, tiled=True
    )
    returned = after(returned, kept_got)
    kept = jnp.where(home, taken(kept, mp, 0), kept_got)
    returned = returned.transpose(1, 0, 2, 3).reshape(rows // 2, width)
    mine = (kept.astype(F32) + returned.astype(F32)).astype(BF16)
    other = lax.ppermute(mine, "mp", [(0, 1), (1, 0)])
    grad_tokens = jnp.where(
        jnp.arange(2)[:, None, None] == mp, mine[None], other[None]
    ).reshape(rows, width)

    short = after(short, returning)
    counts = jnp.where((core == 0) | (jnp.arange(6) < 2), 1.0, 0.0).astype(F32)
    wide = (short[:6] * counts[:, None]).reshape(6, dp_count, 1, part_rows)
    wide = jnp.broadcast_to(wide, (6, dp_count, 2, part_rows)).transpose(1, 2, 0, 3)
    to_half = (jnp.arange(2) == core)[None, :, None]

    def half_terms(vectors):
        terms = vectors.reshape(vectors.shape[0], dp_count, -1).transpose(1, 0, 2)
        return jnp.where(to_half, terms.reshape(dp_count, 1, -1), 0.0)

    short = jnp.concatenate(
        [
            wide.reshape(dp_count, 2, -1),
            half_terms(short[6].reshape(2, local)),
            half_terms(short[7:].reshape(1, units)),
        ],
        axis=-1,
    ).reshape(2 * dp_count, -1)

    sum_feed = far(feed_value, mine)
    sum_in, sum_out = sum_feed[:, :units], sum_feed[:, units:]
    sum_attn = far(side_by_side(after(attn_terms, mine)))
    short = lax.all_to_all(after(short, mine), both, 0, 0, tiled=True)
    short = jnp.sum(after(short, sum_attn), axis=0)
    sum_qkv = sum_attn[:, : 3 * local].reshape(-1, 3, local)
    sum_proj = sum_attn[:, 3 * local :].T

    plain = short[: 6 * part_rows].reshape(6, part_rows)
    sum_qv = short[6 * part_rows : 6 * part_rows + width // dp_count].reshape(2, -1)
    sum_bin = short[6 * part_rows + width // dp_count :]
    return (
        block_out,
        grad_tokens,
        plain[0],
        plain[1],
        sum_qkv,
        sum_qv,
        sum_proj,
        plain[4],
        plain[2],
        plain[3],
        sum_in,
        sum_bin,
        sum_out.T,
        plain[5],
    )


def solution(mesh):
    return jax.shard_map(
        shards,
        mesh=mesh,
        in_specs=(
            P("dp", None),
            P("dp"),
            P(),
            P("dp", None),
            P(),
            P(),
            P(None, None, "mp"),
            P(None, "mp"),
            P("mp", None),
            P(),
            P(),
            P(),
            P(None, "mp"),
            P("mp"),
            P("mp", None),
            P(),
            P("dp", None),
        ),
        out_specs=(
            P("dp", None),
            P("dp", None),
            P("dp"),
            P("dp"),
            P("dp", None, "mp"),
            P(None, ("mp", "dp")),
            P("mp", "dp"),
            P("dp"),
            P("dp"),
            P("dp"),
            P("dp", "mp"),
            P(("mp", "dp")),
            P("mp", "dp"),
            P("dp"),
        ),
        check_vma=False,
    )
```

```python
import functools

import jax
import jax.numpy as jnp
from jax import lax
from jax.experimental import pallas as pl
from jax.experimental.pallas import tpu as pltpu
from jax.sharding import PartitionSpec as P

HEAD_DIM = 64
NORM_EPS = 1e-06
NEG_FILL = -1e30
SCORE_SCALE = HEAD_DIM ** (-0.5)
MAX_CLIP = 256
LANES = 128
F32 = jnp.float32
BF16 = jnp.bfloat16
MIB = 1 << 20
SMALL = pl.CostEstimate(flops=1 << 20, bytes_accessed=1 << 20, transcendentals=0)


def nn(left, right):
    return lax.dot_general(left, right, (((1,), (0,)), ((), ())), preferred_element_type=F32)


def nt(left, right):
    return lax.dot_general(left, right, (((1,), (1,)), ((), ())), preferred_element_type=F32)


def vmem():
    return pl.BlockSpec(memory_space=pltpu.VMEM)


def hbm():
    return pl.BlockSpec(memory_space=pltpu.HBM)


def anywhere():
    return pl.BlockSpec(memory_space=pl.ANY)


def smem():
    return pl.BlockSpec(memory_space=pltpu.SMEM)


def params(mib):
    return pltpu.CompilerParams(vmem_limit_bytes=mib * MIB)


def shape(dims, dtype):
    return jax.ShapeDtypeStruct(dims, dtype)


def row_stats(vector):
    mean = jnp.mean(vector, axis=-1, keepdims=True)
    centred = vector - mean
    spread = jnp.mean(centred * centred, axis=-1, keepdims=True)
    return centred, lax.rsqrt(spread + NORM_EPS)


def on_lanes(column):
    return jnp.broadcast_to(column, (column.shape[0], LANES))


def wide_rsqrt(inv, here, width):
    return jnp.concatenate([inv[here, :]] * (width // LANES), axis=1)


def row_sum(block):
    return jnp.sum(block, axis=0, keepdims=True)


def fold_rows(block):
    rows, width = block.shape
    return jnp.sum(block.reshape(rows // 8, 8, width), axis=0)


def pick_kernel(index, source, *refs):
    picked = refs[-1]

    def move(i, carry):
        picked[i] = source[index[i]]
        return carry

    lax.fori_loop(0, picked.shape[0], move, 0, unroll=4)


def pick(source, index, *after):
    dims = index.shape + source.shape[1:]
    return pl.pallas_call(
        pick_kernel,
        out_shape=shape(dims, source.dtype),
        in_specs=[smem(), vmem()] + [hbm()] * len(after),
        out_specs=vmem(),
        compiler_params=params(16),
        cost_estimate=SMALL,
        name="pick",
    )(index, source, *after)


def move(source, target, sem):
    return pltpu.make_async_copy(source, target, sem)


PARTS = 4


def part_moves(pairs, sems):
    moves = []
    for c in range(PARTS):
        row = []
        for n, (source, target) in enumerate(pairs):
            count = source.shape[0] // PARTS
            here = pl.ds(c * count, count)
            row.append(move(source.at[here, :], target.at[here, :], sems.at[n, c]))
        moves.append(row)
    return moves


def start_all(moves):
    for one in moves:
        one.start()


def wait_all(moves):
    for one in moves:
        one.wait()


def interleave(*streams):
    order = sorted(
        ((n + 0.5) / len(stream), which, n)
        for which, stream in enumerate(streams)
        for n in range(len(stream))
    )
    for _, which, n in order:
        streams[which][n]()


def spread_clips(seg_row, seg_b):
    for i in range(seg_b.shape[0] // LANES):
        here = pl.ds(i * LANES, LANES)
        seg_b[here, :] = jnp.broadcast_to(seg_row[:, here], (LANES, LANES)).T


def key_window(j, rows):
    window = min(rows, LANES + 2 * MAX_CLIP)
    here = pl.ds(pl.multiple_of(j * LANES, LANES), LANES)
    first = pl.multiple_of(jnp.clip(j * LANES - MAX_CLIP, 0, rows - window), LANES)
    return here, pl.ds(first, window)


def set_bias(bias, seg_b, seg_row, here, keys):
    filled = jnp.where(seg_b[keys, :] == seg_row[:, here], 0.0, NEG_FILL)
    bias[:, pl.ds(0, LANES)] = filled
    bias[:, pl.ds(LANES, LANES)] = filled


def two_heads(block):
    lane = lax.broadcasted_iota(jnp.int32, block.shape, 1)
    return jnp.concatenate(
        [block * (lane // HEAD_DIM == e).astype(BF16) for e in range(2)], axis=0
    )


def attention_kernel(
    blend, flags, seg_row, vecs, biases, tok, own, oth, w3, wp, *refs
):
    mixed, n1, normed, inv, q, k, v, att, part, lse = refs[-32:-22]
    (
        tok_v, own_v, oth_v, w3_v, wp_v, mixed_v, n1_v, q_v, k_v, v_v, att_v, part_v,
        vt, att_t, seg_b, bias, ones, normed_v, inv_v, in_sems, half_sems, out_sems,
    ) = refs[-22:]
    rows, width = tok.shape
    local = wp.shape[0]
    half_rows = rows // 2
    ratio = blend[0]
    blk = 32
    big = 256

    loads = [
        move(source, target, in_sems.at[n])
        for n, (source, target) in enumerate([(tok, tok_v), (w3, w3_v), (wp, wp_v)])
    ]
    halves = part_moves([(own, own_v), (oth, oth_v)], half_sems)
    loads[0].start()
    for part_of in halves:
        start_all(part_of)
    start_all(loads[1:])
    early = [
        move(source, target, out_sems.at[n])
        for n, (source, target) in enumerate(
            [
                (mixed_v, mixed), (n1_v, n1), (normed_v, normed), (inv_v, inv),
                (q_v, q), (k_v, k), (v_v, v),
            ]
        )
    ]
    ones[...] = jnp.ones_like(ones)
    spread_clips(seg_row, seg_b)

    loads[0].wait()
    steps = half_rows // PARTS // blk
    for n, src, half in ((0, own_v, flags[0]), (1, oth_v, 1 - flags[0])):
        for c in range(PARTS):
            halves[c][n].wait()

            def mix(i, carry, src=src, half=half, c=c):
                low = (c * steps + i) * blk
                here = pl.ds(pl.multiple_of(half * half_rows + low, blk), blk)
                there = pl.ds(pl.multiple_of(low, blk), blk)
                mine, other = tok_v[here, :].astype(F32), src[there, :].astype(F32)
                blended = ratio * mine + (1.0 - ratio) * other
                mixed_v[here, :] = blended
                centred, scale = row_stats(blended)
                inv_v[here, :] = on_lanes(scale)
                plain = centred * scale
                normed_v[here, :] = plain.astype(BF16)
                n1_v[here, :] = (plain * vecs[0:1, :] + vecs[1:2, :]).astype(BF16)
                return carry

            lax.fori_loop(0, steps, mix, 0, unroll=2)
    start_all(early[:4])

    loads[1].wait()
    def project(i, carry):
        here = pl.ds(pl.multiple_of(i * big, big), big)
        rows_in = n1_v[here, :]
        queries = (nn(rows_in, w3_v[0]) + biases[0:1, :local]).astype(BF16).astype(F32)
        q_v[here, :] = (queries * SCORE_SCALE).astype(BF16)
        k_v[here, :] = nn(rows_in, w3_v[1]).astype(BF16)
        values = (nn(rows_in, w3_v[2]) + biases[0:1, local:]).astype(BF16)
        v_v[here, :] = values
        vt[:, here] = values.T
        return carry

    lax.fori_loop(0, rows // big, project, 0)
    start_all(early[4:])

    def attend(j, carry):
        here, keys = key_window(j, rows)
        set_bias(bias, seg_b, seg_row, here, keys)
        for p in range(local // LANES):
            pair = pl.ds(p * LANES, LANES)
            scores = nt(k_v[keys, pair], two_heads(q_v[here, pair])) + bias[...]
            top = jnp.max(scores, axis=0, keepdims=True)
            grown = jnp.exp(scores - top).astype(BF16)
            total = nn(ones[...], grown)[:1]
            out = (nn(vt[pair, keys], grown) / total).astype(BF16)
            logs = top + jnp.log(total)
            for e in range(2):
                lanes = slice(e * LANES, e * LANES + LANES)
                head = slice(e * HEAD_DIM, e * HEAD_DIM + HEAD_DIM)
                att_t[pl.ds(p * LANES + e * HEAD_DIM, HEAD_DIM), here] = out[head, lanes]
                lse[pl.ds(2 * p + e, 1), here] = logs[:, lanes]
        return carry

    lax.fori_loop(0, rows // LANES, attend, 0)

    loads[2].wait()
    def finish(i, carry):
        here = pl.ds(pl.multiple_of(i * big, big), big)
        block = att_t[:, here].T
        att_v[here, :] = block
        part_v[here, :] = nn(block, wp_v[...]).astype(BF16)
        move(part_v.at[here, :], part.at[here, :], out_sems.at[8 + i]).start()
        return carry

    lax.fori_loop(0, rows // big, finish, 0)
    last = [
        move(part_v.at[pl.ds(i * big, big), :], part.at[pl.ds(i * big, big), :], out_sems.at[8 + i])
        for i in range(rows // big)
    ]
    last.append(move(att_v, att, out_sems.at[7]))
    last[-1].start()
    wait_all(early + last)


def attention(blend, flags, segment, vecs, biases, tok, own, oth, w3, wp, *before):
    rows, width = tok.shape
    local = wp.shape[0]
    window = min(rows, LANES + 2 * MAX_CLIP)
    thin = shape((rows, local), BF16)
    tall = shape((rows, width), BF16)
    return pl.pallas_call(
        attention_kernel,
        out_shape=(
            shape((rows, width), F32), tall, tall, shape((rows, LANES), F32),
            thin, thin, thin, thin, tall, shape((local // HEAD_DIM, rows), F32),
        ),
        in_specs=[smem(), smem()] + [vmem()] * 3 + [anywhere()] * 3 + [hbm()] * (2 + len(before)),
        out_specs=[hbm()] * 9 + [vmem()],
        scratch_shapes=[
            pltpu.VMEM((rows, width), BF16),
            pltpu.VMEM((rows // 2, width), BF16),
            pltpu.VMEM((rows // 2, width), BF16),
            pltpu.VMEM(w3.shape, BF16),
            pltpu.VMEM(wp.shape, BF16),
            pltpu.VMEM((rows, width), F32),
            pltpu.VMEM((rows, width), BF16),
            pltpu.VMEM((rows, local), BF16),
            pltpu.VMEM((rows, local), BF16),
            pltpu.VMEM((rows, local), BF16),
            pltpu.VMEM((rows, local), BF16),
            pltpu.VMEM((rows, width), BF16),
            pltpu.VMEM((local, rows), BF16),
            pltpu.VMEM((local, rows), BF16),
            pltpu.VMEM((rows, LANES), F32),
            pltpu.VMEM((window, 2 * LANES), F32),
            pltpu.VMEM((16, window), BF16),
            pltpu.VMEM((rows, width), BF16),
            pltpu.VMEM((rows, LANES), F32),
            pltpu.SemaphoreType.DMA((3,)),
            pltpu.SemaphoreType.DMA((2, PARTS)),
            pltpu.SemaphoreType.DMA((8 + rows // 256,)),
        ],
        compiler_params=params(60),
        cost_estimate=SMALL,
        name="attention",
    )(
        blend, flags, segment, vecs, biases, tok, own, oth, w3, wp, *before,
    )


ERFC_SLOPE = 0.47
ERFC_COEFFS = (
    0.2663094668265691,
    0.2480096137831850,
    0.3362712657560771,
    -0.1262288063821733,
    0.6076790117752645,
    -0.4204702410368928,
    0.0884296765518492,
)


def gelu_parts(pre):
    bell = jnp.exp(pre * pre * -0.5)
    t = 1.0 / (1.0 + jnp.abs(pre) * (ERFC_SLOPE * 0.5**0.5))
    poly = 0.5 * ERFC_COEFFS[-1]
    for coeff in ERFC_COEFFS[-2::-1]:
        poly = poly * t + 0.5 * coeff
    tail = poly * t * bell
    cdf = jnp.where(pre >= 0, 1.0 - tail, tail)
    return pre * cdf, cdf + pre * bell * 0.3989422804014327


def turn_into(target, source, blocks):
    rows = source.shape[0]
    big = 256
    for i in range(rows // big):
        here = pl.ds(i * big, big)
        turned = source[here, :].T
        for start, place, count in blocks:
            target[pl.ds(place, count), here] = turned[start : start + count]


def lead_blocks(width, lead_rows):
    runs = width // lead_rows
    return [
        (run * lead_rows, ((run % 2) * (runs // 2) + run // 2) * lead_rows, lead_rows)
        for run in range(runs)
    ]


def feed_kernel(
    in_rows, out_rows, flags, vecs, biases, mixed, p_own, p_oth, cot, cot_t,
    w_in, w_out, w_out_one, w_out_two,
    hidden, part, gn_part, in_keep, in_send, out_keep, out_send, normed, inv, g_bin, g_bout,
    mixed_v, own_v, oth_v, cot_v, cot_tv, w_in_v, w_out_v, n2, n2_t, act, gp,
    g_in, g_out, normed_v, inv_v, in_sems, turn_sems, weight_sems, out_sems, grad_sems,
):
    rows, width = mixed.shape
    units = w_in.shape[1]
    blk = 32
    big = 256
    sub = 16
    home = flags[1] == 1
    across = flags[2]
    kept_out = jnp.where(home, flags[0], 1 - flags[0]) if in_rows != out_rows else across
    sides = (across, kept_out)

    loads = part_moves(
        [(mixed, mixed_v), (p_own, own_v), (p_oth, oth_v), (cot, cot_v)], in_sems
    )
    for part_of in loads:
        start_all(part_of)

    weights = [move(w_in, w_in_v, weight_sems.at[0])]
    weights[0].start()
    half = w_out.shape[0] // 2
    for n, (got, place) in enumerate([(w_out_one, across), (w_out_two, 1 - across)]):
        spot = pl.ds(pl.multiple_of(place * half, half), half)
        sem = weight_sems.at[1 + n]
        weights.append(move(w_out.at[spot, :], w_out_v.at[spot, :], sem))

        @pl.when(home)
        def _(spot=spot, sem=sem):
            move(w_out.at[spot, :], w_out_v.at[spot, :], sem).start()

        @pl.when(jnp.logical_not(home))
        def _(got=got, spot=spot, sem=sem):
            move(got, w_out_v.at[spot, :], sem).start()

    turns = [
        move(cot_t.at[pl.ds(start, count), :], cot_tv.at[pl.ds(place, count), :], turn_sems.at[n])
        for n, (start, place, count) in enumerate(lead_blocks(width, out_rows))
    ]
    start_all(turns)

    g_bout[...] = jnp.zeros_like(g_bout)
    steps = rows // PARTS // blk
    for c in range(PARTS):
        wait_all(loads[c])

        def norm(i, carry, c=c):
            here = pl.ds(pl.multiple_of((c * steps + i) * blk, blk), blk)
            attn = own_v[here, :].astype(F32) + oth_v[here, :].astype(F32)
            total = mixed_v[here, :] + attn + vecs[4:5, :]
            mixed_v[here, :] = total
            centred, scale = row_stats(total)
            inv_v[here, :] = on_lanes(scale)
            plain = centred * scale
            normed_v[here, :] = plain.astype(BF16)
            n2[here, :] = (plain * vecs[2:3, :] + vecs[3:4, :]).astype(BF16)
            g_bout[...] += fold_rows(cot_v[here, :].astype(F32))
            return carry

        lax.fori_loop(0, steps, norm, 0, unroll=2)
    stores = [
        move(source, target, out_sems.at[0, n])
        for n, (source, target) in enumerate(
            [(mixed_v, hidden), (normed_v, normed), (inv_v, inv)]
        )
    ]
    start_all(stores)
    turn_into(n2_t, n2, lead_blocks(width, in_rows))
    wait_all(weights)

    g_bin[...] = jnp.zeros_like(g_bin)

    def row_block(i, carry):
        here = pl.ds(pl.multiple_of(i * big, big), big)
        for j in range(units // width):
            cols = pl.ds(j * width, width)
            pre_all = nn(n2[here, :], w_in_v[:, cols])
            grad_all = nt(cot_v[here, :], w_out_v[cols, :])
            sums = jnp.zeros((8, width), F32)
            for s in range(big // sub):
                rng = slice(s * sub, s * sub + sub)
                value, slope = gelu_parts(pre_all[rng] + biases[1 + j : 2 + j, :])
                grad = grad_all[rng] * slope
                sums += fold_rows(grad)
                spot = pl.ds(pl.multiple_of(i * big + s * sub, sub), sub)
                act[spot, cols] = value.astype(BF16)
                gp[spot, cols] = grad.astype(BF16)
            g_bin[:, cols] += sums
        oth_v[here, :] = nt(gp[here, :], w_in_v[...]).astype(BF16)
        own_v[here, :] = nn(act[here, :], w_out_v[...]).astype(BF16)
        for n, (source, target) in enumerate([(oth_v, gn_part), (own_v, part)]):
            move(source.at[here, :], target.at[here, :], out_sems.at[1 + n, i]).start()
        return carry

    lax.fori_loop(0, rows // big, row_block, 0)
    for i in range(rows // big):
        here = pl.ds(i * big, big)
        for n, (source, target) in enumerate([(oth_v, gn_part), (own_v, part)]):
            stores.append(move(source.at[here, :], target.at[here, :], out_sems.at[1 + n, i]))

    wait_all(turns)
    half = width // 2
    for n, (turned, right, buf, keep, send) in enumerate(
        [(n2_t, gp, g_in, in_keep, in_send), (cot_tv, act, g_out, out_keep, out_send)]
    ):
        for side in range(2):
            lines = pl.ds(side * half, half)
            for j in range(units // width):
                cols = pl.ds(j * width, width)
                buf[side, :, cols] = nn(turned[lines, :], right[:, cols]).astype(BF16)
        for m, (side, target) in enumerate([(1 - sides[n], send), (sides[n], keep)]):
            stores.append(move(buf.at[side], target, grad_sems.at[n, m]))
            stores[-1].start()
    wait_all(stores)


def feed(
    in_rows, out_rows, flags, vecs, biases, mixed, p_own, p_oth, cot, cot_t,
    w_in, w_out, w_out_one, w_out_two,
):
    rows, width = mixed.shape
    units = w_in.shape[1]
    tall = shape((rows, width), BF16)
    grad = shape((width // 2, units), BF16)
    return pl.pallas_call(
        functools.partial(feed_kernel, in_rows, out_rows),
        out_shape=(
            shape((rows, width), F32), tall, tall, grad, grad, grad, grad,
            tall, shape((rows, LANES), F32), shape((8, units), F32), shape((8, width), F32),
        ),
        in_specs=[smem()] + [vmem()] * 2 + [hbm()] * 2 + [anywhere()] + [hbm()] * 6,
        out_specs=[hbm()] * 9 + [vmem()] * 2,
        scratch_shapes=[
            pltpu.VMEM((rows, width), F32),
            pltpu.VMEM((rows, width), BF16),
            pltpu.VMEM((rows, width), BF16),
            pltpu.VMEM((rows, width), BF16),
            pltpu.VMEM((width, rows), BF16),
            pltpu.VMEM(w_in.shape, BF16),
            pltpu.VMEM(w_out.shape, BF16),
            pltpu.VMEM((rows, width), BF16),
            pltpu.VMEM((width, rows), BF16),
            pltpu.VMEM((rows, units), BF16),
            pltpu.VMEM((rows, units), BF16),
            pltpu.VMEM((2, width // 2, units), BF16),
            pltpu.VMEM((2, width // 2, units), BF16),
            pltpu.VMEM((rows, width), BF16),
            pltpu.VMEM((rows, LANES), F32),
            pltpu.SemaphoreType.DMA((4, PARTS)),
            pltpu.SemaphoreType.DMA((width // out_rows,)),
            pltpu.SemaphoreType.DMA((3,)),
            pltpu.SemaphoreType.DMA((3, rows // 256)),
            pltpu.SemaphoreType.DMA((2, 2)),
        ],
        compiler_params=params(60),
        cost_estimate=SMALL,
        name="feed",
    )(
        flags, vecs, biases, mixed, p_own, p_oth, cot, cot_t,
        w_in, w_out, w_out_one, w_out_two,
    )


def attention_back_kernel(
    lead_rows, flags, vecs, seg_row, lse, g_bin, g_bout, g_own, g_oth, cot, normed, inv,
    wp, att, k, q, v, w3, n1, normed_one,
    gh, part, keep, send, short,
    gh_v, own_v, oth_v, cot_v, normed_v, inv_v, wp_v, att_v, k_v, q_v, v_v, w3_v, n1_v, one_v, low_v, part_v,
    sums, tails, d_out, kt, dq_t, dk, dv, delta, seg_b, bias, raw, raw_g, low_p, low_g, n1_t, gh_t, grad_v, out,
    in_sems, row_sems, out_sems, last_sems,
):
    rows, width = cot.shape
    local = wp.shape[0]
    blk = 32
    big = 256
    blocks = lead_blocks(width, lead_rows)
    across = flags[2]
    row_loads = part_moves(
        [(g_own, own_v), (g_oth, oth_v), (cot, cot_v), (normed, normed_v), (inv, inv_v)],
        row_sems,
    )
    for part_of in row_loads:
        start_all(part_of)
    loads = [
        move(source, target, in_sems.at[n])
        for n, (source, target) in enumerate(
            [
                (wp, wp_v), (att, att_v), (k, k_v), (q, q_v), (v, v_v), (w3, w3_v), (n1, n1_v),
                (normed_one, one_v),
            ]
        )
    ]
    start_all(loads)
    sums[...] = jnp.zeros_like(sums)
    dk[...] = jnp.zeros_like(dk)
    dv[...] = jnp.zeros_like(dv)
    spread_clips(seg_row, seg_b)

    steps = rows // PARTS // blk
    for c in range(PARTS):
        wait_all(row_loads[c])

        def norm(i, carry, c=c):
            here = pl.ds(pl.multiple_of((c * steps + i) * blk, blk), blk)
            grad = own_v[here, :].astype(F32) + oth_v[here, :].astype(F32)
            plain = normed_v[here, :].astype(F32)
            scaled = grad * vecs[2:3, :]
            mean_one = jnp.mean(scaled, axis=-1, keepdims=True)
            mean_two = jnp.mean(scaled * plain, axis=-1, keepdims=True)
            scale = wide_rsqrt(inv_v, here, width)
            back = cot_v[here, :].astype(F32) + scale * (scaled - mean_one - plain * mean_two)
            gh_v[here, :] = back
            low_v[here, :] = back.astype(BF16)
            sums[0] += fold_rows(grad * plain)
            sums[1] += fold_rows(grad)
            sums[2] += fold_rows(back)
            return carry

        lax.fori_loop(0, steps, norm, 0, unroll=2)
    stores = [move(gh_v, gh, out_sems.at[0])]
    stores[0].start()

    wait_all(loads[:3])
    heads = local // HEAD_DIM
    lane = lax.broadcasted_iota(jnp.int32, (delta.shape[0], local), 1)
    row = lax.broadcasted_iota(jnp.int32, (delta.shape[0], local), 0)
    of_head = (lane // HEAD_DIM == row).astype(BF16)

    def project(i, carry):
        here = pl.ds(pl.multiple_of(i * big, big), big)
        grad_out = nt(low_v[here, :], wp_v[...]).astype(BF16)
        d_out[here, :] = grad_out
        product = grad_out.astype(F32) * att_v[here, :].astype(F32)
        coarse = product.astype(BF16)
        fine = (product - coarse.astype(F32)).astype(BF16)
        delta[:, here] = nt(of_head, coarse) + nt(of_head, fine)
        kt[:, here] = k_v[here, :].T
        return carry

    lax.fori_loop(0, rows // big, project, 0)
    wait_all(loads[3:])

    pairs = heads // 2
    window = bias.shape[0]
    strip = 128
    strips = window // strip

    def attend(j, carry):
        here, keys = key_window(j, rows)
        first = pl.multiple_of(keys.start, LANES)
        set_bias(bias, seg_b, seg_row, here, keys)
        blocks_two = {}

        def two(p):
            if p not in blocks_two:
                pair = pl.ds(p * LANES, LANES)
                blocks_two[p] = (two_heads(q_v[here, pair]), two_heads(d_out[here, pair]))
            return blocks_two[p]

        def at_strip(n):
            return (
                pl.ds(pl.multiple_of(first + n * strip, strip), strip),
                pl.ds(n * strip, strip),
            )

        def products(p):
            pair = pl.ds(p * LANES, LANES)

            def scores(n):
                def run():
                    some, at = at_strip(n)
                    raw[p % 2, at, :] = nt(k_v[some, pair], two(p)[0])

                return run

            def grads(n):
                def run():
                    some, at = at_strip(n)
                    raw_g[p % 2, at, :] = nt(v_v[some, pair], two(p)[1])

                return run

            return [make(n) for n in range(strips) for make in (scores, grads)]

        def softmax_back(p):
            tops = jnp.concatenate([lse[pl.ds(2 * p + e, 1), here] for e in range(2)], axis=1)
            inner = jnp.concatenate([delta[pl.ds(2 * p + e, 1), here] for e in range(2)], axis=1)
            half = strip // 2

            def run_at(n):
                def run():
                    at = pl.ds(n * half, half)
                    probs = jnp.exp(raw[p % 2, at, :] + bias[at, :] - tops)
                    low_p[p % 2, at, :] = probs.astype(BF16)
                    low_g[p % 2, at, :] = (probs * (raw_g[p % 2, at, :] - inner)).astype(BF16)

                return run

            return [run_at(n) for n in range(2 * strips)]

        def sums_of(p):
            pair = pl.ds(p * LANES, LANES)

            def keys_of(n):
                def run():
                    some, at = at_strip(n)
                    dk[some, pair] += nn(low_g[p % 2, at, :], two(p)[0])

                return run

            def values_of(n):
                def run():
                    some, at = at_strip(n)
                    dv[some, pair] += nn(low_p[p % 2, at, :], two(p)[1])

                return run

            def queries():
                grad_q = nn(kt[pair, keys], low_g[p % 2]) * SCORE_SCALE
                for e in range(2):
                    lanes = slice(e * LANES, e * LANES + LANES)
                    head = slice(e * HEAD_DIM, e * HEAD_DIM + HEAD_DIM)
                    dq_t[pl.ds(p * LANES + e * HEAD_DIM, HEAD_DIM), here] = grad_q[head, lanes]

            return [make(n) for n in range(strips) for make in (keys_of, values_of)] + [queries]

        def turns():
            for target, source in ((n1_t, n1_v), (gh_t, low_v)):
                turned = source[here, :].T
                for start, place, count in blocks:
                    target[pl.ds(place, count), here] = turned[start : start + count]

        interleave(products(0), [turns])
        for p in range(pairs):
            matrix = (products(p + 1) if p + 1 < pairs else []) + (sums_of(p - 1) if p else [])
            interleave(softmax_back(p), matrix)
        interleave(sums_of(pairs - 1))
        return carry

    lax.fori_loop(0, rows // LANES, attend, 0)

    tails[...] = jnp.zeros_like(tails)

    def finish(i, carry):
        here = pl.ds(pl.multiple_of(i * big, big), big)
        grad_q, grad_k, grad_val = dq_t[:, here].T, dk[here, :], dv[here, :]
        tails[2, :, pl.ds(0, local)] += fold_rows(grad_q)
        tails[2, :, pl.ds(local, local)] += fold_rows(grad_val)
        lows = [grad.astype(BF16) for grad in (grad_q, grad_k, grad_val)]
        total = sum(nt(low, w3_v[n]) for n, low in enumerate(lows))
        part_v[here, :] = total.astype(BF16)
        tails[0] += fold_rows(total * one_v[here, :].astype(F32))
        tails[1] += fold_rows(total)
        for n, low in enumerate(lows):
            grad_v[here, pl.ds(n * local, local)] = low
        move(part_v.at[here, :], part.at[here, :], last_sems.at[i]).start()
        return carry

    lax.fori_loop(0, rows // big, finish, 0)
    for i in range(rows // big):
        here = pl.ds(i * big, big)
        stores.append(move(part_v.at[here, :], part.at[here, :], last_sems.at[i]))
    units = g_bin.shape[1]
    listed = [tails[0], tails[1], sums[0], sums[1], sums[2], g_bout[...], tails[2]]
    listed += [g_bin[:, pl.ds(n, width)] for n in range(0, units, width)]
    for n, block in enumerate(listed):
        short[pl.ds(n, 1), :] = row_sum(block)
    half = width // 2
    for side in range(2):
        lines = pl.ds(side * half, half)
        for n in range(3):
            cols = pl.ds(n * local, local)
            out[side, :, cols] = nn(n1_t[lines, :], grad_v[:, cols]).astype(BF16)
        out[side, :, pl.ds(3 * local, local)] = nn(gh_t[lines, :], att_v[...]).astype(BF16)
    for n, (side, target) in enumerate([(1 - across, send), (across, keep)]):
        stores.append(move(out.at[side], target, out_sems.at[1 + n]))
        stores[-1].start()
    wait_all(stores)


def attention_back(
    lead_rows, flags, vecs, segment, lse, g_bin, g_bout, g_own, g_oth, cot, normed, inv,
    wp, att, k, q, v, w3, n1, normed_one,
):
    rows, width = cot.shape
    local = wp.shape[0]
    window = min(rows, LANES + 2 * MAX_CLIP)
    tall, thin = pltpu.VMEM((rows, width), BF16), pltpu.VMEM((rows, local), BF16)
    turned = pltpu.VMEM((width, rows), BF16)
    half = (width // 2, 4 * local)
    return pl.pallas_call(
        functools.partial(attention_back_kernel, lead_rows),
        out_shape=(
            shape((rows, width), F32),
            shape((rows, width), BF16),
            shape(half, BF16),
            shape(half, BF16),
            shape((7 + g_bin.shape[1] // width, width), F32),
        ),
        in_specs=[smem()] + [vmem()] * 5 + [hbm()] + [anywhere()] + [hbm()] * 11,
        out_specs=[hbm()] * 4 + [vmem()],
        scratch_shapes=[
            pltpu.VMEM((rows, width), F32),
            tall, tall, tall, tall,
            pltpu.VMEM((rows, LANES), F32),
            pltpu.VMEM(wp.shape, BF16),
            thin, thin, thin, thin,
            pltpu.VMEM(w3.shape, BF16),
            tall, tall, tall, tall,
            pltpu.VMEM((3, 8, width), F32),
            pltpu.VMEM((3, 8, width), F32),
            thin,
            pltpu.VMEM((local, rows), BF16),
            pltpu.VMEM((local, rows), F32),
            pltpu.VMEM((rows, local), F32),
            pltpu.VMEM((rows, local), F32),
            pltpu.VMEM((8, rows), F32),
            pltpu.VMEM((rows, LANES), F32),
            pltpu.VMEM((window, 2 * LANES), F32),
            pltpu.VMEM((2, window, 2 * LANES), F32),
            pltpu.VMEM((2, window, 2 * LANES), F32),
            pltpu.VMEM((2, window, 2 * LANES), BF16),
            pltpu.VMEM((2, window, 2 * LANES), BF16),
            turned, turned,
            pltpu.VMEM((rows, 3 * local), BF16),
            pltpu.VMEM((2,) + half, BF16),
            pltpu.SemaphoreType.DMA((8,)),
            pltpu.SemaphoreType.DMA((5, PARTS)),
            pltpu.SemaphoreType.DMA((3,)),
            pltpu.SemaphoreType.DMA((rows // 256,)),
        ],
        compiler_params=params(60),
        cost_estimate=SMALL,
        name="attention_back",
    )(
        flags, vecs, segment, lse, g_bin, g_bout, g_own, g_oth, cot, normed, inv,
        wp, att, k, q, v, w3, n1, normed_one,
    )


def mixed_back_kernel(blend, vecs, gh, g_own, g_oth, normed, inv, outgoing, kept, *refs):
    gh_v, own_v, oth_v, normed_v, inv_v, leave_v, kept_v, in_sems, out_sems = refs
    ratio = blend[0]
    rows, width = gh.shape
    blk = 32
    loads = part_moves(
        [(gh, gh_v), (g_own, own_v), (g_oth, oth_v), (normed, normed_v), (inv, inv_v)], in_sems
    )
    stores = part_moves([(leave_v, outgoing), (kept_v, kept)], out_sems)
    for part_of in loads:
        start_all(part_of)
    steps = rows // PARTS // blk
    for c in range(PARTS):
        wait_all(loads[c])

        def norm(i, carry, c=c):
            here = pl.ds(pl.multiple_of((c * steps + i) * blk, blk), blk)
            grad = own_v[here, :].astype(F32) + oth_v[here, :].astype(F32)
            plain = normed_v[here, :].astype(F32)
            scaled = grad * vecs[0:1, :]
            mean_one = jnp.mean(scaled, axis=-1, keepdims=True)
            mean_two = jnp.mean(scaled * plain, axis=-1, keepdims=True)
            scale = wide_rsqrt(inv_v, here, width)
            back = gh_v[here, :] + scale * (scaled - mean_one - plain * mean_two)
            leave_v[here, :] = ((1.0 - ratio) * back).astype(BF16)
            kept_v[here, :] = (ratio * back).astype(BF16)
            return carry

        lax.fori_loop(0, steps, norm, 0, unroll=2)
        start_all(stores[c])
    for part_of in stores:
        wait_all(part_of)


def mixed_back(blend, vecs, gh, g_own, g_oth, normed, inv):
    rows, width = gh.shape
    tall = pltpu.VMEM((rows, width), BF16)
    return pl.pallas_call(
        mixed_back_kernel,
        out_shape=(shape((rows, width), BF16), shape((rows, width), BF16)),
        in_specs=[smem(), vmem()] + [hbm()] * 2 + [anywhere()] + [hbm()] * 2,
        out_specs=[hbm(), hbm()],
        scratch_shapes=[
            pltpu.VMEM((rows, width), F32),
            tall, tall, tall, pltpu.VMEM((rows, LANES), F32), tall, tall,
            pltpu.SemaphoreType.DMA((5, PARTS)),
            pltpu.SemaphoreType.DMA((2, PARTS)),
        ],
        compiler_params=params(60),
        cost_estimate=SMALL,
        name="mixed_back",
    )(blend, vecs, gh, g_own, g_oth, normed, inv)


def shards(
    tokens,
    mix_blend,
    partner,
    clip_ids,
    gain_one,
    shift_one,
    qkv_weight,
    qv_bias,
    proj_weight,
    proj_bias,
    gain_two,
    shift_two,
    in_weight,
    in_bias,
    out_weight,
    out_bias,
    cotangent,
):
    rows, width = tokens.shape
    dp_count = lax.axis_size("dp")
    both = ("dp", "mp")
    bits = dp_count.bit_length() - 1
    seq = lax.axis_index("dp")
    mp = lax.axis_index("mp")
    core = lax.rem(seq, 2)
    home = core == mp
    all_dp = range(dp_count)

    def joint(d, m):
        return 2 * d + m

    core_swap = [(d, d ^ 1) for d in all_dp]
    home_to_pair = [(joint(d, d & 1), joint(d, 1 - (d & 1))) for d in all_dp]
    pair_to_home = [(joint(d, 1 - (d & 1)), joint(d, d & 1)) for d in all_dp]
    weight_move = home_to_pair + [
        (joint(d, 1 - (d & 1)), joint(d ^ 1, 1 - (d & 1))) for d in all_dp
    ]

    def swap(value):
        return lax.ppermute(value, "dp", core_swap)

    def chip_value(value):
        return jnp.where(home, value, swap(value))

    def after(value, *others):
        return lax.optimization_barrier((value,) + others)[0]

    def half_weight(value):
        return lax.ppermute(value, both, weight_move)

    part_rows = width // dp_count
    lead = min(n for n in range(1, bits) if (part_rows << n) % 16 == 0)
    lead_rows = part_rows << lead
    across = lax.rem(seq >> lead, 2)
    flags = jnp.stack([core, home.astype(jnp.int32), across]).astype(jnp.int32)

    def taken(value, index, axis):
        return lax.dynamic_index_in_dim(value, index, axis, keepdims=False)

    seq_small = chip_value(jnp.concatenate([mix_blend, clip_ids[0].astype(F32)]))
    blend, segment = seq_small[:1], seq_small[1:].reshape(1, rows)
    local = proj_weight.shape[0]
    units = in_bias.shape[0]
    half_small = jnp.concatenate([qv_bias.reshape(-1), in_bias])
    half_small = jnp.where(home, half_small, half_weight(half_small))
    biases = half_small.reshape(-1, width)
    vecs = jnp.stack([gain_one, shift_one, gain_two, shift_two, proj_bias])

    w3 = half_weight(qkv_weight.transpose(1, 0, 2))
    wp = half_weight(proj_weight)

    def two_way(value):
        halves = value.reshape(2, value.shape[0] // 2, value.shape[1])
        one = half_weight(taken(halves, across, 0))
        moves = [(joint(d, 1 - (d & 1)), joint(d ^ (1 << lead), 1 - (d & 1))) for d in all_dp]
        return value, one, lax.ppermute(one, both, moves)

    ids = jnp.arange(2 * dp_count, dtype=jnp.int32)
    piece = rows // (2 * 2 * dp_count)
    sent = tokens.reshape(2, dp_count, 2, piece, width)
    sent = lax.dynamic_index_in_dim(sent, mp, 2, keepdims=False)
    spread = lax.all_to_all(sent.transpose(1, 0, 2, 3), "dp", 0, 0, tiled=True)
    wanted = partner[(ids // 4) * 2 + ids % 2] * 2 + (ids // 2) % 2
    source_of = jnp.sum(
        jnp.where(partner[:, None] == ids[None, :dp_count], ids[:dp_count, None], 0),
        axis=0,
        dtype=jnp.int32,
    )
    source = source_of[ids // 2]
    wanted_back = (source // 2) * 4 + (ids % 2) * 2 + source % 2
    chosen = pick(spread.reshape(2 * dp_count, piece, width), wanted, w3, wp, half_small)
    partner_own = lax.all_to_all(chosen, both, 0, 0, tiled=True).reshape(rows // 2, width)
    w_out = two_way(out_weight)
    w_in = half_weight(after(in_weight, w_out[1]))

    tok = chip_value(tokens)
    cot = chip_value(cotangent)
    cot_t = cot.T
    partner_oth = swap(after(partner_own, tok, cot, vecs, segment, wanted_back))

    mixed, n1, normed_one, inv_one, q, k, v, att, attn_part, lse = attention(
        blend, flags, segment, vecs, biases, tok, partner_own, partner_oth, w3, wp, w_out[2], cot_t
    )
    pair_first = part_rows % 16 == 0
    fed = feed(
        lead_rows, part_rows if pair_first else lead_rows, flags, vecs, biases,
        mixed, attn_part, swap(attn_part), cot, cot_t, w_in, *w_out,
    )
    hidden, out_part, gn2_part, in_keep, in_send, out_keep, out_send = fed[:7]
    normed_two, inv_two, g_bin, g_bout = fed[7:]
    gn2_oth = swap(gn2_part)

    high, mid = dp_count >> (lead + 1), 1 << (lead - 1)
    pair_and_core = pair_to_home + [(joint(d, d & 1), joint(d ^ 1, d & 1)) for d in all_dp]
    pair_diagonal = [(joint(d, 1 - (d & 1)), joint(d ^ 1, d & 1)) for d in all_dp]

    def total(*terms):
        return sum(term.astype(F32) for term in terms)

    def send_across(value):
        return lax.ppermute(value, "dp", [(d, d ^ (1 << lead)) for d in all_dp])

    def send_pair(value):
        value = value.reshape(high, mid, 2, part_rows, -1)
        one = lax.ppermute(taken(value, jnp.where(home, 1 - core, core), 2), both, pair_and_core)
        two = lax.ppermute(taken(value, 1 - core, 2), both, pair_diagonal)
        held = taken(value, core, 2)
        return jnp.where(home, held, jnp.zeros_like(held)), one, two

    def far(value, *others):
        for shift, left in ((1, mid), (lead + 1, high)):
            while left > 1:
                radix = min(4, left)
                left //= radix
                value = value.reshape((-1, left, radix) + value.shape[-2:]).astype(BF16)
                spot = lax.rem(seq >> shift, radix)
                got = [
                    lax.ppermute(
                        taken(value, spot ^ flip, 2),
                        "dp",
                        [(d, d ^ (flip << shift)) for d in all_dp],
                    )
                    for flip in range(1, radix)
                ]
                value = total(taken(value, spot, 2), *after(got, *others))
                shift += radix.bit_length() - 1
        return value.reshape(value.shape[-2:])

    in_got = send_across(in_send)
    if pair_first:
        out_got = [
            lax.ppermute(out_send, both, pair_and_core),
            lax.ppermute(out_keep, both, pair_diagonal),
        ]
        out_keep = jnp.where(home, out_keep, jnp.zeros_like(out_keep))
    else:
        out_got = [send_across(out_send)]
    gh, gn1_part, attn_keep, attn_send, short = attention_back(
        lead_rows, flags, vecs, segment, lse, g_bin, g_bout, gn2_part, gn2_oth, cot,
        normed_two, inv_two, wp, att, k, q, v, w3, n1, normed_one,
    )
    attn_got = send_across(attn_send)
    gn1_oth = swap(after(gn1_part, in_got, *out_got))
    in_terms = send_pair(total(in_keep, in_got).astype(BF16))
    outgoing, kept = mixed_back(blend, vecs, gh, gn1_part, gn1_oth, normed_one, inv_one)

    leaving = taken(outgoing.reshape(2, 2, dp_count, piece, width), core, 1)
    leaving = leaving.transpose(1, 0, 2, 3).reshape(2 * dp_count, piece, width)
    back = lax.all_to_all(leaving, both, 0, 0, tiled=True)

    in_value = total(*after(in_terms, leaving)).astype(BF16)
    out_value = total(out_keep, *after(out_got, in_value)).astype(BF16)
    if pair_first:
        out_value = out_value.reshape(high, 2, mid, part_rows, units)
        out_terms = (taken(out_value, across, 1), send_across(taken(out_value, 1 - across, 1)))
    else:
        out_terms = send_pair(out_value)
    out_oth = swap(after(out_part, leaving))
    block = (hidden + (out_part.astype(F32) + out_oth.astype(F32)) + out_bias).astype(BF16)
    block_got = half_weight(block)
    block_out = jnp.where(home, block, block_got)
    kept = kept.reshape(2, rows // 2, width)
    kept_away = taken(kept, 1 - mp, 0)

    def side_by_side(*groups):
        values = [total(*terms).reshape(high * mid, part_rows, -1) for terms in groups]
        return jnp.concatenate(values, axis=2).astype(BF16)


    returning = pick(back, wanted_back, in_value, block, kept_away)
    attn_value = total(attn_keep, after(attn_got, returning)).astype(BF16)
    attn_terms = send_pair(attn_value)
    returned = lax.all_to_all(
        returning.reshape(dp_count, 2, piece, width), "dp", 0, 0, tiled=True
    )
    kept_got = half_weight(after(kept_away, returning))
    returned = after(returned, kept_got, block_got)
    kept = jnp.where(home, taken(kept, mp, 0), kept_got)
    returned = returned.transpose(1, 0, 2, 3).reshape(rows // 2, width)
    mine = (kept.astype(F32) + returned.astype(F32)).astype(BF16)
    other = lax.ppermute(mine, "mp", [(0, 1), (1, 0)])
    grad_tokens = jnp.where(
        jnp.arange(2)[:, None, None] == mp, mine[None], other[None]
    ).reshape(rows, width)

    short = after(short, returning)
    counts = jnp.where((core == 0) | (jnp.arange(6) < 2), 1.0, 0.0).astype(F32)
    wide = (short[:6] * counts[:, None]).reshape(6, dp_count, 1, part_rows)
    wide = jnp.broadcast_to(wide, (6, dp_count, 2, part_rows)).transpose(1, 2, 0, 3)
    to_half = (jnp.arange(2) == core)[None, :, None]

    def half_terms(vectors):
        terms = vectors.reshape(vectors.shape[0], dp_count, -1).transpose(1, 0, 2)
        return jnp.where(to_half, terms.reshape(dp_count, 1, -1), 0.0)

    short = jnp.concatenate(
        [
            wide.reshape(dp_count, 2, -1),
            half_terms(short[6].reshape(2, local)),
            half_terms(short[7:].reshape(1, units)),
        ],
        axis=-1,
    ).reshape(2 * dp_count, -1)

    feed_value = side_by_side([in_value], after(out_terms, kept_got))
    sum_feed = far(feed_value, mine)
    sum_attn = far(side_by_side(after(attn_terms, feed_value)), mine)
    short = lax.all_to_all(after(short, mine), both, 0, 0, tiled=True)
    short = jnp.sum(short, axis=0)
    sum_feed = after(sum_feed, short)
    sum_in, sum_out = sum_feed[:, :units], sum_feed[:, units:]
    sum_qkv = sum_attn[:, : 3 * local].reshape(-1, 3, local)
    sum_proj = sum_attn[:, 3 * local :].T

    plain = short[: 6 * part_rows].reshape(6, part_rows)
    sum_qv = short[6 * part_rows : 6 * part_rows + width // dp_count].reshape(2, -1)
    sum_bin = short[6 * part_rows + width // dp_count :]
    return (
        block_out,
        grad_tokens,
        plain[0],
        plain[1],
        sum_qkv,
        sum_qv,
        sum_proj,
        plain[4],
        plain[2],
        plain[3],
        sum_in,
        sum_bin,
        sum_out.T,
        plain[5],
    )


def solution(mesh):
    return jax.shard_map(
        shards,
        mesh=mesh,
        in_specs=(
            P("dp", None),
            P("dp"),
            P(),
            P("dp", None),
            P(),
            P(),
            P(None, None, "mp"),
            P(None, "mp"),
            P("mp", None),
            P(),
            P(),
            P(),
            P(None, "mp"),
            P("mp"),
            P("mp", None),
            P(),
            P("dp", None),
        ),
        out_specs=(
            P("dp", None),
            P("dp", None),
            P("dp"),
            P("dp"),
            P("dp", None, "mp"),
            P(None, ("mp", "dp")),
            P("mp", "dp"),
            P("dp"),
            P("dp"),
            P("dp"),
            P("dp", "mp"),
            P(("mp", "dp")),
            P("mp", "dp"),
            P("dp"),
        ),
        check_vma=False,
    )
```

```python
import functools

import jax
import jax.numpy as jnp
from jax import lax
from jax.experimental import pallas as pl
from jax.experimental.pallas import tpu as pltpu
from jax.sharding import PartitionSpec as P

HEAD_DIM = 64
NORM_EPS = 1e-06
NEG_FILL = -1e30
SCORE_SCALE = HEAD_DIM ** (-0.5)
MAX_CLIP = 256
LANES = 128
F32 = jnp.float32
BF16 = jnp.bfloat16
MIB = 1 << 20
SMALL = pl.CostEstimate(flops=1 << 20, bytes_accessed=1 << 20, transcendentals=0)


def nn(left, right):
    return lax.dot_general(left, right, (((1,), (0,)), ((), ())), preferred_element_type=F32)


def nt(left, right):
    return lax.dot_general(left, right, (((1,), (1,)), ((), ())), preferred_element_type=F32)


def vmem():
    return pl.BlockSpec(memory_space=pltpu.VMEM)


def hbm():
    return pl.BlockSpec(memory_space=pltpu.HBM)


def anywhere():
    return pl.BlockSpec(memory_space=pl.ANY)


def smem():
    return pl.BlockSpec(memory_space=pltpu.SMEM)


def params(mib):
    return pltpu.CompilerParams(vmem_limit_bytes=mib * MIB)


def shape(dims, dtype):
    return jax.ShapeDtypeStruct(dims, dtype)


def row_stats(vector):
    mean = jnp.mean(vector, axis=-1, keepdims=True)
    centred = vector - mean
    spread = jnp.mean(centred * centred, axis=-1, keepdims=True)
    return centred, lax.rsqrt(spread + NORM_EPS)


def on_lanes(column):
    return jnp.broadcast_to(column, (column.shape[0], LANES))


def wide_rsqrt(inv, here, width):
    return jnp.concatenate([inv[here, :]] * (width // LANES), axis=1)


def row_sum(block):
    return jnp.sum(block, axis=0, keepdims=True)


def fold_rows(block):
    rows, width = block.shape
    return jnp.sum(block.reshape(rows // 8, 8, width), axis=0)


def pick_kernel(index, source, *refs):
    picked = refs[-1]

    def move(i, carry):
        picked[i] = source[index[i]]
        return carry

    lax.fori_loop(0, picked.shape[0], move, 0, unroll=4)


def pick(source, index, *after):
    dims = index.shape + source.shape[1:]
    return pl.pallas_call(
        pick_kernel,
        out_shape=shape(dims, source.dtype),
        in_specs=[smem(), vmem()] + [hbm()] * len(after),
        out_specs=vmem(),
        compiler_params=params(16),
        cost_estimate=SMALL,
        name="pick",
    )(index, source, *after)


def move(source, target, sem):
    return pltpu.make_async_copy(source, target, sem)


PARTS = 4


def part_moves(pairs, sems):
    moves = []
    for c in range(PARTS):
        row = []
        for n, (source, target) in enumerate(pairs):
            count = source.shape[0] // PARTS
            here = pl.ds(c * count, count)
            row.append(move(source.at[here, :], target.at[here, :], sems.at[n, c]))
        moves.append(row)
    return moves


def start_all(moves):
    for one in moves:
        one.start()


def wait_all(moves):
    for one in moves:
        one.wait()


def interleave(*streams):
    order = sorted(
        ((n + 0.5) / len(stream), which, n)
        for which, stream in enumerate(streams)
        for n in range(len(stream))
    )
    for _, which, n in order:
        streams[which][n]()


def spread_clips(seg_row, seg_b):
    for i in range(seg_b.shape[0] // LANES):
        here = pl.ds(i * LANES, LANES)
        seg_b[here, :] = jnp.broadcast_to(seg_row[:, here], (LANES, LANES)).T


def key_window(j, rows):
    window = min(rows, LANES + 2 * MAX_CLIP)
    here = pl.ds(pl.multiple_of(j * LANES, LANES), LANES)
    first = pl.multiple_of(jnp.clip(j * LANES - MAX_CLIP, 0, rows - window), LANES)
    return here, pl.ds(first, window)


def set_bias(bias, seg_b, seg_row, here, keys):
    filled = jnp.where(seg_b[keys, :] == seg_row[:, here], 0.0, NEG_FILL)
    bias[:, pl.ds(0, LANES)] = filled
    bias[:, pl.ds(LANES, LANES)] = filled


def two_heads(block):
    lane = lax.broadcasted_iota(jnp.int32, block.shape, 1)
    return jnp.concatenate(
        [block * (lane // HEAD_DIM == e).astype(BF16) for e in range(2)], axis=0
    )


def attention_kernel(
    blend, flags, seg_row, vecs, biases, tok, own, oth, w3, wp, *refs
):
    mixed, n1, normed, inv, q, k, v, att, part, lse = refs[-32:-22]
    (
        tok_v, own_v, oth_v, w3_v, wp_v, mixed_v, n1_v, q_v, k_v, v_v, att_v, part_v,
        vt, att_t, seg_b, bias, ones, normed_v, inv_v, in_sems, half_sems, out_sems,
    ) = refs[-22:]
    rows, width = tok.shape
    local = wp.shape[0]
    half_rows = rows // 2
    ratio = blend[0]
    blk = 32
    big = 256

    loads = [
        move(source, target, in_sems.at[n])
        for n, (source, target) in enumerate([(tok, tok_v), (w3, w3_v), (wp, wp_v)])
    ]
    halves = part_moves([(own, own_v), (oth, oth_v)], half_sems)
    loads[0].start()
    for part_of in halves:
        start_all(part_of)
    start_all(loads[1:])
    early = [
        move(source, target, out_sems.at[n])
        for n, (source, target) in enumerate(
            [
                (mixed_v, mixed), (n1_v, n1), (normed_v, normed), (inv_v, inv),
                (q_v, q), (k_v, k), (v_v, v),
            ]
        )
    ]
    ones[...] = jnp.ones_like(ones)
    spread_clips(seg_row, seg_b)

    loads[0].wait()
    steps = half_rows // PARTS // blk
    for n, src, half in ((0, own_v, flags[0]), (1, oth_v, 1 - flags[0])):
        for c in range(PARTS):
            halves[c][n].wait()

            def mix(i, carry, src=src, half=half, c=c):
                low = (c * steps + i) * blk
                here = pl.ds(pl.multiple_of(half * half_rows + low, blk), blk)
                there = pl.ds(pl.multiple_of(low, blk), blk)
                mine, other = tok_v[here, :].astype(F32), src[there, :].astype(F32)
                blended = ratio * mine + (1.0 - ratio) * other
                mixed_v[here, :] = blended
                centred, scale = row_stats(blended)
                inv_v[here, :] = on_lanes(scale)
                plain = centred * scale
                normed_v[here, :] = plain.astype(BF16)
                n1_v[here, :] = (plain * vecs[0:1, :] + vecs[1:2, :]).astype(BF16)
                return carry

            lax.fori_loop(0, steps, mix, 0, unroll=True)
    start_all(early[:4])

    loads[1].wait()
    for i in range(rows // big):
        here = pl.ds(i * big, big)
        rows_in = n1_v[here, :]
        queries = (nn(rows_in, w3_v[0]) + biases[0:1, :local]).astype(BF16).astype(F32)
        q_v[here, :] = (queries * SCORE_SCALE).astype(BF16)
        k_v[here, :] = nn(rows_in, w3_v[1]).astype(BF16)
        values = (nn(rows_in, w3_v[2]) + biases[0:1, local:]).astype(BF16)
        v_v[here, :] = values
        vt[:, here] = values.T
    start_all(early[4:])

    def attend(j, carry):
        here, keys = key_window(j, rows)
        set_bias(bias, seg_b, seg_row, here, keys)
        for p in range(local // LANES):
            pair = pl.ds(p * LANES, LANES)
            scores = nt(k_v[keys, pair], two_heads(q_v[here, pair])) + bias[...]
            top = jnp.max(scores, axis=0, keepdims=True)
            grown = jnp.exp(scores - top).astype(BF16)
            total = nn(ones[...], grown)[:1]
            out = (nn(vt[pair, keys], grown) / total).astype(BF16)
            logs = top + jnp.log(total)
            for e in range(2):
                lanes = slice(e * LANES, e * LANES + LANES)
                head = slice(e * HEAD_DIM, e * HEAD_DIM + HEAD_DIM)
                att_t[pl.ds(p * LANES + e * HEAD_DIM, HEAD_DIM), here] = out[head, lanes]
                lse[pl.ds(2 * p + e, 1), here] = logs[:, lanes]
        return carry

    lax.fori_loop(0, rows // LANES, attend, 0)

    loads[2].wait()
    last = []
    for i in range(rows // big):
        here = pl.ds(i * big, big)
        block = att_t[:, here].T
        att_v[here, :] = block
        part_v[here, :] = nn(block, wp_v[...]).astype(BF16)
        last.append(move(part_v.at[here, :], part.at[here, :], out_sems.at[8 + i]))
        last[-1].start()
    last.append(move(att_v, att, out_sems.at[7]))
    last[-1].start()
    wait_all(early + last)


def attention(blend, flags, segment, vecs, biases, tok, own, oth, w3, wp, *before):
    rows, width = tok.shape
    local = wp.shape[0]
    window = min(rows, LANES + 2 * MAX_CLIP)
    thin = shape((rows, local), BF16)
    tall = shape((rows, width), BF16)
    return pl.pallas_call(
        attention_kernel,
        out_shape=(
            shape((rows, width), F32), tall, tall, shape((rows, LANES), F32),
            thin, thin, thin, thin, tall, shape((local // HEAD_DIM, rows), F32),
        ),
        in_specs=[smem(), smem()] + [vmem()] * 3 + [anywhere()] * 3 + [hbm()] * (2 + len(before)),
        out_specs=[hbm()] * 9 + [vmem()],
        scratch_shapes=[
            pltpu.VMEM((rows, width), BF16),
            pltpu.VMEM((rows // 2, width), BF16),
            pltpu.VMEM((rows // 2, width), BF16),
            pltpu.VMEM(w3.shape, BF16),
            pltpu.VMEM(wp.shape, BF16),
            pltpu.VMEM((rows, width), F32),
            pltpu.VMEM((rows, width), BF16),
            pltpu.VMEM((rows, local), BF16),
            pltpu.VMEM((rows, local), BF16),
            pltpu.VMEM((rows, local), BF16),
            pltpu.VMEM((rows, local), BF16),
            pltpu.VMEM((rows, width), BF16),
            pltpu.VMEM((local, rows), BF16),
            pltpu.VMEM((local, rows), BF16),
            pltpu.VMEM((rows, LANES), F32),
            pltpu.VMEM((window, 2 * LANES), F32),
            pltpu.VMEM((16, window), BF16),
            pltpu.VMEM((rows, width), BF16),
            pltpu.VMEM((rows, LANES), F32),
            pltpu.SemaphoreType.DMA((3,)),
            pltpu.SemaphoreType.DMA((2, PARTS)),
            pltpu.SemaphoreType.DMA((8 + rows // 256,)),
        ],
        compiler_params=params(60),
        cost_estimate=SMALL,
        name="attention",
    )(
        blend, flags, segment, vecs, biases, tok, own, oth, w3, wp, *before,
    )


ERFC_SLOPE = 0.47
ERFC_COEFFS = (
    0.2663094668265691,
    0.2480096137831850,
    0.3362712657560771,
    -0.1262288063821733,
    0.6076790117752645,
    -0.4204702410368928,
    0.0884296765518492,
)


def gelu_parts(pre):
    bell = jnp.exp(pre * pre * -0.5)
    t = 1.0 / (1.0 + jnp.abs(pre) * (ERFC_SLOPE * 0.5**0.5))
    poly = 0.5 * ERFC_COEFFS[-1]
    for coeff in ERFC_COEFFS[-2::-1]:
        poly = poly * t + 0.5 * coeff
    tail = poly * t * bell
    cdf = jnp.where(pre >= 0, 1.0 - tail, tail)
    return pre * cdf, cdf + pre * bell * 0.3989422804014327


def turn_into(target, source, blocks):
    rows = source.shape[0]
    big = 256
    for i in range(rows // big):
        here = pl.ds(i * big, big)
        turned = source[here, :].T
        for start, place, count in blocks:
            target[pl.ds(place, count), here] = turned[start : start + count]


def lead_blocks(width, lead_rows):
    runs = width // lead_rows
    return [
        (run * lead_rows, ((run % 2) * (runs // 2) + run // 2) * lead_rows, lead_rows)
        for run in range(runs)
    ]


def feed_kernel(
    in_rows, out_rows, flags, vecs, biases, mixed, p_own, p_oth, cot, cot_t,
    w_in, w_out, w_out_one, w_out_two,
    hidden, part, gn_part, in_keep, in_send, out_keep, out_send, normed, inv, g_bin, g_bout,
    mixed_v, own_v, oth_v, cot_v, cot_tv, w_in_v, w_out_v, n2, n2_t, act, gp,
    g_in, g_out, normed_v, inv_v, in_sems, turn_sems, weight_sems, out_sems, grad_sems,
):
    rows, width = mixed.shape
    units = w_in.shape[1]
    blk = 32
    big = 256
    sub = 16
    home = flags[1] == 1
    across = flags[2]
    kept_out = jnp.where(home, flags[0], 1 - flags[0]) if in_rows != out_rows else across
    sides = (across, kept_out)

    loads = part_moves(
        [(mixed, mixed_v), (p_own, own_v), (p_oth, oth_v), (cot, cot_v)], in_sems
    )
    for part_of in loads:
        start_all(part_of)

    weights = [move(w_in, w_in_v, weight_sems.at[0])]
    weights[0].start()
    half = w_out.shape[0] // 2
    for n, (got, place) in enumerate([(w_out_one, across), (w_out_two, 1 - across)]):
        spot = pl.ds(pl.multiple_of(place * half, half), half)
        sem = weight_sems.at[1 + n]
        weights.append(move(w_out.at[spot, :], w_out_v.at[spot, :], sem))

        @pl.when(home)
        def _(spot=spot, sem=sem):
            move(w_out.at[spot, :], w_out_v.at[spot, :], sem).start()

        @pl.when(jnp.logical_not(home))
        def _(got=got, spot=spot, sem=sem):
            move(got, w_out_v.at[spot, :], sem).start()

    turns = [
        move(cot_t.at[pl.ds(start, count), :], cot_tv.at[pl.ds(place, count), :], turn_sems.at[n])
        for n, (start, place, count) in enumerate(lead_blocks(width, out_rows))
    ]
    start_all(turns)

    g_bout[...] = jnp.zeros_like(g_bout)
    steps = rows // PARTS // blk
    for c in range(PARTS):
        wait_all(loads[c])

        def norm(i, carry, c=c):
            here = pl.ds(pl.multiple_of((c * steps + i) * blk, blk), blk)
            attn = own_v[here, :].astype(F32) + oth_v[here, :].astype(F32)
            total = mixed_v[here, :] + attn + vecs[4:5, :]
            mixed_v[here, :] = total
            centred, scale = row_stats(total)
            inv_v[here, :] = on_lanes(scale)
            plain = centred * scale
            normed_v[here, :] = plain.astype(BF16)
            n2[here, :] = (plain * vecs[2:3, :] + vecs[3:4, :]).astype(BF16)
            g_bout[...] += fold_rows(cot_v[here, :].astype(F32))
            return carry

        lax.fori_loop(0, steps, norm, 0, unroll=4)
    stores = [
        move(source, target, out_sems.at[0, n])
        for n, (source, target) in enumerate(
            [(mixed_v, hidden), (normed_v, normed), (inv_v, inv)]
        )
    ]
    start_all(stores)
    turn_into(n2_t, n2, lead_blocks(width, in_rows))
    wait_all(weights)

    g_bin[...] = jnp.zeros_like(g_bin)

    def row_block(i, carry):
        here = pl.ds(pl.multiple_of(i * big, big), big)
        for j in range(units // width):
            cols = pl.ds(j * width, width)
            pre_all = nn(n2[here, :], w_in_v[:, cols])
            grad_all = nt(cot_v[here, :], w_out_v[cols, :])
            sums = jnp.zeros((8, width), F32)
            for s in range(big // sub):
                rng = slice(s * sub, s * sub + sub)
                value, slope = gelu_parts(pre_all[rng] + biases[1 + j : 2 + j, :])
                grad = grad_all[rng] * slope
                sums += fold_rows(grad)
                spot = pl.ds(pl.multiple_of(i * big + s * sub, sub), sub)
                act[spot, cols] = value.astype(BF16)
                gp[spot, cols] = grad.astype(BF16)
            g_bin[:, cols] += sums
        oth_v[here, :] = nt(gp[here, :], w_in_v[...]).astype(BF16)
        own_v[here, :] = nn(act[here, :], w_out_v[...]).astype(BF16)
        for n, (source, target) in enumerate([(oth_v, gn_part), (own_v, part)]):
            move(source.at[here, :], target.at[here, :], out_sems.at[1 + n, i]).start()
        return carry

    lax.fori_loop(0, rows // big, row_block, 0)
    for i in range(rows // big):
        here = pl.ds(i * big, big)
        for n, (source, target) in enumerate([(oth_v, gn_part), (own_v, part)]):
            stores.append(move(source.at[here, :], target.at[here, :], out_sems.at[1 + n, i]))

    wait_all(turns)
    half = width // 2
    for n, (turned, right, buf, keep, send) in enumerate(
        [(n2_t, gp, g_in, in_keep, in_send), (cot_tv, act, g_out, out_keep, out_send)]
    ):
        for side in range(2):
            lines = pl.ds(side * half, half)
            for j in range(units // width):
                cols = pl.ds(j * width, width)
                buf[side, :, cols] = nn(turned[lines, :], right[:, cols]).astype(BF16)
        for m, (side, target) in enumerate([(1 - sides[n], send), (sides[n], keep)]):
            stores.append(move(buf.at[side], target, grad_sems.at[n, m]))
            stores[-1].start()
    wait_all(stores)


def feed(
    in_rows, out_rows, flags, vecs, biases, mixed, p_own, p_oth, cot, cot_t,
    w_in, w_out, w_out_one, w_out_two,
):
    rows, width = mixed.shape
    units = w_in.shape[1]
    tall = shape((rows, width), BF16)
    grad = shape((width // 2, units), BF16)
    return pl.pallas_call(
        functools.partial(feed_kernel, in_rows, out_rows),
        out_shape=(
            shape((rows, width), F32), tall, tall, grad, grad, grad, grad,
            tall, shape((rows, LANES), F32), shape((8, units), F32), shape((8, width), F32),
        ),
        in_specs=[smem()] + [vmem()] * 2 + [hbm()] * 2 + [anywhere()] + [hbm()] * 6,
        out_specs=[hbm()] * 9 + [vmem()] * 2,
        scratch_shapes=[
            pltpu.VMEM((rows, width), F32),
            pltpu.VMEM((rows, width), BF16),
            pltpu.VMEM((rows, width), BF16),
            pltpu.VMEM((rows, width), BF16),
            pltpu.VMEM((width, rows), BF16),
            pltpu.VMEM(w_in.shape, BF16),
            pltpu.VMEM(w_out.shape, BF16),
            pltpu.VMEM((rows, width), BF16),
            pltpu.VMEM((width, rows), BF16),
            pltpu.VMEM((rows, units), BF16),
            pltpu.VMEM((rows, units), BF16),
            pltpu.VMEM((2, width // 2, units), BF16),
            pltpu.VMEM((2, width // 2, units), BF16),
            pltpu.VMEM((rows, width), BF16),
            pltpu.VMEM((rows, LANES), F32),
            pltpu.SemaphoreType.DMA((4, PARTS)),
            pltpu.SemaphoreType.DMA((width // out_rows,)),
            pltpu.SemaphoreType.DMA((3,)),
            pltpu.SemaphoreType.DMA((3, rows // 256)),
            pltpu.SemaphoreType.DMA((2, 2)),
        ],
        compiler_params=params(60),
        cost_estimate=SMALL,
        name="feed",
    )(
        flags, vecs, biases, mixed, p_own, p_oth, cot, cot_t,
        w_in, w_out, w_out_one, w_out_two,
    )


def attention_back_kernel(
    lead_rows, by_core, flags, vecs, seg_row, lse, g_bin, g_bout, g_own, g_oth, cot, normed, inv,
    wp, att, k, q, v, w3, n1, normed_one,
    gh, part, keep, send, short,
    gh_v, own_v, oth_v, cot_v, normed_v, inv_v, wp_v, att_v, k_v, q_v, v_v, w3_v, n1_v, one_v, low_v, part_v,
    sums, tails, d_out, kt, dq_t, dk, dv, delta, seg_b, bias, raw, raw_g, low_p, low_g, n1_t, gh_t, grad_v, out,
    in_sems, row_sems, out_sems, last_sems,
):
    rows, width = cot.shape
    local = wp.shape[0]
    blk = 32
    big = 256
    blocks = lead_blocks(width, lead_rows)
    kept_side = jnp.where(flags[1] == 1, flags[0], 1 - flags[0]) if by_core else flags[2]
    row_loads = part_moves(
        [(g_own, own_v), (g_oth, oth_v), (cot, cot_v), (normed, normed_v), (inv, inv_v)],
        row_sems,
    )
    for part_of in row_loads:
        start_all(part_of)
    loads = [
        move(source, target, in_sems.at[n])
        for n, (source, target) in enumerate(
            [
                (wp, wp_v), (att, att_v), (k, k_v), (q, q_v), (v, v_v), (w3, w3_v), (n1, n1_v),
                (normed_one, one_v),
            ]
        )
    ]
    start_all(loads)
    sums[...] = jnp.zeros_like(sums)
    dk[...] = jnp.zeros_like(dk)
    dv[...] = jnp.zeros_like(dv)
    spread_clips(seg_row, seg_b)

    steps = rows // PARTS // blk
    for c in range(PARTS):
        wait_all(row_loads[c])

        def norm(i, carry, c=c):
            here = pl.ds(pl.multiple_of((c * steps + i) * blk, blk), blk)
            grad = own_v[here, :].astype(F32) + oth_v[here, :].astype(F32)
            plain = normed_v[here, :].astype(F32)
            scaled = grad * vecs[2:3, :]
            mean_one = jnp.mean(scaled, axis=-1, keepdims=True)
            mean_two = jnp.mean(scaled * plain, axis=-1, keepdims=True)
            scale = wide_rsqrt(inv_v, here, width)
            back = cot_v[here, :].astype(F32) + scale * (scaled - mean_one - plain * mean_two)
            gh_v[here, :] = back
            low_v[here, :] = back.astype(BF16)
            sums[0] += fold_rows(grad * plain)
            sums[1] += fold_rows(grad)
            sums[2] += fold_rows(back)
            return carry

        lax.fori_loop(0, steps, norm, 0, unroll=2)
    stores = [move(gh_v, gh, out_sems.at[0])]
    stores[0].start()

    wait_all(loads[:3])
    heads = local // HEAD_DIM
    lane = lax.broadcasted_iota(jnp.int32, (delta.shape[0], local), 1)
    row = lax.broadcasted_iota(jnp.int32, (delta.shape[0], local), 0)
    of_head = (lane // HEAD_DIM == row).astype(BF16)

    def project(i, carry):
        here = pl.ds(pl.multiple_of(i * big, big), big)
        grad_out = nt(low_v[here, :], wp_v[...]).astype(BF16)
        d_out[here, :] = grad_out
        product = grad_out.astype(F32) * att_v[here, :].astype(F32)
        coarse = product.astype(BF16)
        fine = (product - coarse.astype(F32)).astype(BF16)
        delta[:, here] = nt(of_head, coarse) + nt(of_head, fine)
        kt[:, here] = k_v[here, :].T
        return carry

    lax.fori_loop(0, rows // big, project, 0)
    wait_all(loads[3:])

    pairs = heads // 2
    window = bias.shape[0]
    strip = 128
    strips = window // strip

    def attend(j, carry):
        here, keys = key_window(j, rows)
        first = pl.multiple_of(keys.start, LANES)
        set_bias(bias, seg_b, seg_row, here, keys)
        blocks_two = {}

        def two(p):
            if p not in blocks_two:
                pair = pl.ds(p * LANES, LANES)
                blocks_two[p] = (two_heads(q_v[here, pair]), two_heads(d_out[here, pair]))
            return blocks_two[p]

        def at_strip(n):
            return (
                pl.ds(pl.multiple_of(first + n * strip, strip), strip),
                pl.ds(n * strip, strip),
            )

        def products(p):
            pair = pl.ds(p * LANES, LANES)

            def scores(n):
                def run():
                    some, at = at_strip(n)
                    raw[p % 2, at, :] = nt(k_v[some, pair], two(p)[0])

                return run

            def grads(n):
                def run():
                    some, at = at_strip(n)
                    raw_g[p % 2, at, :] = nt(v_v[some, pair], two(p)[1])

                return run

            return [make(n) for n in range(strips) for make in (scores, grads)]

        def softmax_back(p):
            tops = jnp.concatenate([lse[pl.ds(2 * p + e, 1), here] for e in range(2)], axis=1)
            inner = jnp.concatenate([delta[pl.ds(2 * p + e, 1), here] for e in range(2)], axis=1)
            half = strip // 2

            def run_at(n):
                def run():
                    at = pl.ds(n * half, half)
                    probs = jnp.exp(raw[p % 2, at, :] + bias[at, :] - tops)
                    low_p[p % 2, at, :] = probs.astype(BF16)
                    low_g[p % 2, at, :] = (probs * (raw_g[p % 2, at, :] - inner)).astype(BF16)

                return run

            return [run_at(n) for n in range(2 * strips)]

        def sums_of(p):
            pair = pl.ds(p * LANES, LANES)

            def keys_of(n):
                def run():
                    some, at = at_strip(n)
                    dk[some, pair] += nn(low_g[p % 2, at, :], two(p)[0])

                return run

            def values_of(n):
                def run():
                    some, at = at_strip(n)
                    dv[some, pair] += nn(low_p[p % 2, at, :], two(p)[1])

                return run

            def queries():
                grad_q = nn(kt[pair, keys], low_g[p % 2]) * SCORE_SCALE
                for e in range(2):
                    lanes = slice(e * LANES, e * LANES + LANES)
                    head = slice(e * HEAD_DIM, e * HEAD_DIM + HEAD_DIM)
                    dq_t[pl.ds(p * LANES + e * HEAD_DIM, HEAD_DIM), here] = grad_q[head, lanes]

            return [make(n) for n in range(strips) for make in (keys_of, values_of)] + [queries]

        def turns():
            for target, source in ((n1_t, n1_v), (gh_t, low_v)):
                turned = source[here, :].T
                for start, place, count in blocks:
                    target[pl.ds(place, count), here] = turned[start : start + count]

        interleave(products(0), [turns])
        for p in range(pairs):
            matrix = (products(p + 1) if p + 1 < pairs else []) + (sums_of(p - 1) if p else [])
            interleave(softmax_back(p), matrix)
        interleave(sums_of(pairs - 1))
        return carry

    lax.fori_loop(0, rows // LANES, attend, 0)

    tails[...] = jnp.zeros_like(tails)

    def finish(i, carry):
        here = pl.ds(pl.multiple_of(i * big, big), big)
        grad_q, grad_k, grad_val = dq_t[:, here].T, dk[here, :], dv[here, :]
        tails[2, :, pl.ds(0, local)] += fold_rows(grad_q)
        tails[2, :, pl.ds(local, local)] += fold_rows(grad_val)
        lows = [grad.astype(BF16) for grad in (grad_q, grad_k, grad_val)]
        total = sum(nt(low, w3_v[n]) for n, low in enumerate(lows))
        part_v[here, :] = total.astype(BF16)
        tails[0] += fold_rows(total * one_v[here, :].astype(F32))
        tails[1] += fold_rows(total)
        for n, low in enumerate(lows):
            grad_v[here, pl.ds(n * local, local)] = low
        move(part_v.at[here, :], part.at[here, :], last_sems.at[i]).start()
        return carry

    lax.fori_loop(0, rows // big, finish, 0)
    for i in range(rows // big):
        here = pl.ds(i * big, big)
        stores.append(move(part_v.at[here, :], part.at[here, :], last_sems.at[i]))
    units = g_bin.shape[1]
    listed = [tails[0], tails[1], sums[0], sums[1], sums[2], g_bout[...], tails[2]]
    listed += [g_bin[:, pl.ds(n, width)] for n in range(0, units, width)]
    for n, block in enumerate(listed):
        short[pl.ds(n, 1), :] = row_sum(block)
    half = width // 2
    for side in range(2):
        lines = pl.ds(side * half, half)
        for n in range(3):
            cols = pl.ds(n * local, local)
            out[side, :, cols] = nn(n1_t[lines, :], grad_v[:, cols]).astype(BF16)
        out[side, :, pl.ds(3 * local, local)] = nn(gh_t[lines, :], att_v[...]).astype(BF16)
    for n, (side, target) in enumerate([(1 - kept_side, send), (kept_side, keep)]):
        stores.append(move(out.at[side], target, out_sems.at[1 + n]))
        stores[-1].start()
    wait_all(stores)


def attention_back(
    lead_rows, by_core, flags, vecs, segment, lse, g_bin, g_bout, g_own, g_oth, cot, normed, inv,
    wp, att, k, q, v, w3, n1, normed_one,
):
    rows, width = cot.shape
    local = wp.shape[0]
    window = min(rows, LANES + 2 * MAX_CLIP)
    tall, thin = pltpu.VMEM((rows, width), BF16), pltpu.VMEM((rows, local), BF16)
    turned = pltpu.VMEM((width, rows), BF16)
    half = (width // 2, 4 * local)
    return pl.pallas_call(
        functools.partial(attention_back_kernel, lead_rows, by_core),
        out_shape=(
            shape((rows, width), F32),
            shape((rows, width), BF16),
            shape(half, BF16),
            shape(half, BF16),
            shape((7 + g_bin.shape[1] // width, width), F32),
        ),
        in_specs=[smem()] + [vmem()] * 5 + [hbm()] + [anywhere()] + [hbm()] * 11,
        out_specs=[hbm()] * 4 + [vmem()],
        scratch_shapes=[
            pltpu.VMEM((rows, width), F32),
            tall, tall, tall, tall,
            pltpu.VMEM((rows, LANES), F32),
            pltpu.VMEM(wp.shape, BF16),
            thin, thin, thin, thin,
            pltpu.VMEM(w3.shape, BF16),
            tall, tall, tall, tall,
            pltpu.VMEM((3, 8, width), F32),
            pltpu.VMEM((3, 8, width), F32),
            thin,
            pltpu.VMEM((local, rows), BF16),
            pltpu.VMEM((local, rows), F32),
            pltpu.VMEM((rows, local), F32),
            pltpu.VMEM((rows, local), F32),
            pltpu.VMEM((8, rows), F32),
            pltpu.VMEM((rows, LANES), F32),
            pltpu.VMEM((window, 2 * LANES), F32),
            pltpu.VMEM((2, window, 2 * LANES), F32),
            pltpu.VMEM((2, window, 2 * LANES), F32),
            pltpu.VMEM((2, window, 2 * LANES), BF16),
            pltpu.VMEM((2, window, 2 * LANES), BF16),
            turned, turned,
            pltpu.VMEM((rows, 3 * local), BF16),
            pltpu.VMEM((2,) + half, BF16),
            pltpu.SemaphoreType.DMA((8,)),
            pltpu.SemaphoreType.DMA((5, PARTS)),
            pltpu.SemaphoreType.DMA((3,)),
            pltpu.SemaphoreType.DMA((rows // 256,)),
        ],
        compiler_params=params(60),
        cost_estimate=SMALL,
        name="attention_back",
    )(
        flags, vecs, segment, lse, g_bin, g_bout, g_own, g_oth, cot, normed, inv,
        wp, att, k, q, v, w3, n1, normed_one,
    )


def mixed_back_kernel(blend, vecs, gh, g_own, g_oth, normed, inv, outgoing, kept, *refs):
    gh_v, own_v, oth_v, normed_v, inv_v, leave_v, kept_v, in_sems, out_sems = refs
    ratio = blend[0]
    rows, width = gh.shape
    blk = 32
    loads = part_moves(
        [(gh, gh_v), (g_own, own_v), (g_oth, oth_v), (normed, normed_v), (inv, inv_v)], in_sems
    )
    stores = part_moves([(leave_v, outgoing), (kept_v, kept)], out_sems)
    for part_of in loads:
        start_all(part_of)
    steps = rows // PARTS // blk
    for c in range(PARTS):
        wait_all(loads[c])

        def norm(i, carry, c=c):
            here = pl.ds(pl.multiple_of((c * steps + i) * blk, blk), blk)
            grad = own_v[here, :].astype(F32) + oth_v[here, :].astype(F32)
            plain = normed_v[here, :].astype(F32)
            scaled = grad * vecs[0:1, :]
            mean_one = jnp.mean(scaled, axis=-1, keepdims=True)
            mean_two = jnp.mean(scaled * plain, axis=-1, keepdims=True)
            scale = wide_rsqrt(inv_v, here, width)
            back = gh_v[here, :] + scale * (scaled - mean_one - plain * mean_two)
            leave_v[here, :] = ((1.0 - ratio) * back).astype(BF16)
            kept_v[here, :] = (ratio * back).astype(BF16)
            return carry

        lax.fori_loop(0, steps, norm, 0, unroll=4)
        start_all(stores[c])
    for part_of in stores:
        wait_all(part_of)


def mixed_back(blend, vecs, gh, g_own, g_oth, normed, inv):
    rows, width = gh.shape
    tall = pltpu.VMEM((rows, width), BF16)
    return pl.pallas_call(
        mixed_back_kernel,
        out_shape=(shape((rows, width), BF16), shape((rows, width), BF16)),
        in_specs=[smem(), vmem()] + [hbm()] * 2 + [anywhere()] + [hbm()] * 2,
        out_specs=[hbm(), hbm()],
        scratch_shapes=[
            pltpu.VMEM((rows, width), F32),
            tall, tall, tall, pltpu.VMEM((rows, LANES), F32), tall, tall,
            pltpu.SemaphoreType.DMA((5, PARTS)),
            pltpu.SemaphoreType.DMA((2, PARTS)),
        ],
        compiler_params=params(60),
        cost_estimate=SMALL,
        name="mixed_back",
    )(blend, vecs, gh, g_own, g_oth, normed, inv)


def shards(
    tokens,
    mix_blend,
    partner,
    clip_ids,
    gain_one,
    shift_one,
    qkv_weight,
    qv_bias,
    proj_weight,
    proj_bias,
    gain_two,
    shift_two,
    in_weight,
    in_bias,
    out_weight,
    out_bias,
    cotangent,
):
    rows, width = tokens.shape
    dp_count = lax.axis_size("dp")
    both = ("dp", "mp")
    bits = dp_count.bit_length() - 1
    seq = lax.axis_index("dp")
    mp = lax.axis_index("mp")
    core = lax.rem(seq, 2)
    home = core == mp
    all_dp = range(dp_count)

    def joint(d, m):
        return 2 * d + m

    core_swap = [(d, d ^ 1) for d in all_dp]
    home_to_pair = [(joint(d, d & 1), joint(d, 1 - (d & 1))) for d in all_dp]
    pair_to_home = [(joint(d, 1 - (d & 1)), joint(d, d & 1)) for d in all_dp]
    weight_move = home_to_pair + [
        (joint(d, 1 - (d & 1)), joint(d ^ 1, 1 - (d & 1))) for d in all_dp
    ]

    def swap(value):
        return lax.ppermute(value, "dp", core_swap)

    def chip_value(value):
        return jnp.where(home, value, swap(value))

    def after(value, *others):
        return lax.optimization_barrier((value,) + others)[0]

    def half_weight(value):
        return lax.ppermute(value, both, weight_move)

    part_rows = width // dp_count
    lead = min(n for n in range(1, bits) if (part_rows << n) % 16 == 0)
    lead_rows = part_rows << lead
    across = lax.rem(seq >> lead, 2)
    flags = jnp.stack([core, home.astype(jnp.int32), across]).astype(jnp.int32)

    def taken(value, index, axis):
        return lax.dynamic_index_in_dim(value, index, axis, keepdims=False)

    seq_small = chip_value(jnp.concatenate([mix_blend, clip_ids[0].astype(F32)]))
    blend, segment = seq_small[:1], seq_small[1:].reshape(1, rows)
    local = proj_weight.shape[0]
    units = in_bias.shape[0]
    half_small = jnp.concatenate([qv_bias.reshape(-1), in_bias])
    half_small = jnp.where(home, half_small, half_weight(half_small))
    biases = half_small.reshape(-1, width)
    vecs = jnp.stack([gain_one, shift_one, gain_two, shift_two, proj_bias])

    w3 = half_weight(qkv_weight.transpose(1, 0, 2))
    wp = half_weight(proj_weight)

    def two_way(value):
        halves = value.reshape(2, value.shape[0] // 2, value.shape[1])
        one = half_weight(taken(halves, across, 0))
        moves = [(joint(d, 1 - (d & 1)), joint(d ^ (1 << lead), 1 - (d & 1))) for d in all_dp]
        return value, one, lax.ppermute(one, both, moves)

    ids = jnp.arange(2 * dp_count, dtype=jnp.int32)
    piece = rows // (2 * 2 * dp_count)
    sent = tokens.reshape(2, dp_count, 2, piece, width)
    sent = lax.dynamic_index_in_dim(sent, mp, 2, keepdims=False)
    spread = lax.all_to_all(sent.transpose(1, 0, 2, 3), "dp", 0, 0, tiled=True)
    wanted = partner[(ids // 4) * 2 + ids % 2] * 2 + (ids // 2) % 2
    source_of = jnp.sum(
        jnp.where(partner[:, None] == ids[None, :dp_count], ids[:dp_count, None], 0),
        axis=0,
        dtype=jnp.int32,
    )
    source = source_of[ids // 2]
    wanted_back = (source // 2) * 4 + (ids % 2) * 2 + source % 2
    chosen = pick(spread.reshape(2 * dp_count, piece, width), wanted, w3, wp, half_small)
    partner_own = lax.all_to_all(chosen, both, 0, 0, tiled=True).reshape(rows // 2, width)
    w_out = two_way(out_weight)
    w_in = half_weight(after(in_weight, w_out[1]))

    tok = chip_value(tokens)
    cot = chip_value(cotangent)
    cot_t = cot.T
    partner_oth = swap(after(partner_own, tok, cot, vecs, segment, wanted_back))

    mixed, n1, normed_one, inv_one, q, k, v, att, attn_part, lse = attention(
        blend, flags, segment, vecs, biases, tok, partner_own, partner_oth, w3, wp, w_out[2], cot_t
    )
    pair_first = part_rows % 16 == 0
    fed = feed(
        lead_rows, part_rows if pair_first else lead_rows, flags, vecs, biases,
        mixed, attn_part, swap(attn_part), cot, cot_t, w_in, *w_out,
    )
    hidden, out_part, gn2_part, in_keep, in_send, out_keep, out_send = fed[:7]
    normed_two, inv_two, g_bin, g_bout = fed[7:]
    gn2_oth = swap(gn2_part)

    high, mid = dp_count >> (lead + 1), 1 << (lead - 1)
    pair_and_core = pair_to_home + [(joint(d, d & 1), joint(d ^ 1, d & 1)) for d in all_dp]
    pair_diagonal = [(joint(d, 1 - (d & 1)), joint(d ^ 1, d & 1)) for d in all_dp]

    def total(*terms):
        return sum(term.astype(F32) for term in terms)

    def send_across(value):
        return lax.ppermute(value, "dp", [(d, d ^ (1 << lead)) for d in all_dp])

    def send_pair(value):
        value = value.reshape(high, mid, 2, part_rows, -1)
        one = lax.ppermute(taken(value, jnp.where(home, 1 - core, core), 2), both, pair_and_core)
        two = lax.ppermute(taken(value, 1 - core, 2), both, pair_diagonal)
        held = taken(value, core, 2)
        return jnp.where(home, held, jnp.zeros_like(held)), one, two

    def far(value, *others):
        for shift, left in ((1, mid), (lead + 1, high)):
            while left > 1:
                radix = min(4, left)
                left //= radix
                value = value.reshape((-1, left, radix) + value.shape[-2:]).astype(BF16)
                spot = lax.rem(seq >> shift, radix)
                got = [
                    lax.ppermute(
                        taken(value, spot ^ flip, 2),
                        "dp",
                        [(d, d ^ (flip << shift)) for d in all_dp],
                    )
                    for flip in range(1, radix)
                ]
                value = total(taken(value, spot, 2), *after(got, *others))
                shift += radix.bit_length() - 1
        return value.reshape(value.shape[-2:])

    def send_first(keep, send):
        if not pair_first:
            return [keep, send_across(send)]
        one = lax.ppermute(send, both, pair_and_core)
        two = lax.ppermute(keep, both, pair_diagonal)
        return [jnp.where(home, keep, jnp.zeros_like(keep)), one, two]

    def send_second(value):
        if not pair_first:
            return send_pair(value)
        value = value.reshape(high, 2, mid, part_rows, -1)
        return taken(value, across, 1), send_across(taken(value, 1 - across, 1))

    in_got = send_across(in_send)
    out_first = send_first(out_keep, out_send)
    gh, gn1_part, attn_keep, attn_send, short = attention_back(
        part_rows if pair_first else lead_rows, pair_first, flags, vecs, segment, lse, g_bin, g_bout,
        gn2_part, gn2_oth, cot, normed_two, inv_two, wp, att, k, q, v, w3, n1, normed_one,
    )
    gn1_oth = swap(after(gn1_part, in_got, *out_first))
    attn_first = send_first(attn_keep, attn_send)
    out_terms = send_second(total(*after(out_first, gn1_part)).astype(BF16))
    outgoing, kept = mixed_back(blend, vecs, gh, gn1_part, gn1_oth, normed_one, inv_one)

    leaving = taken(outgoing.reshape(2, 2, dp_count, piece, width), core, 1)
    leaving = leaving.transpose(1, 0, 2, 3).reshape(2 * dp_count, piece, width)
    back = lax.all_to_all(leaving, both, 0, 0, tiled=True)

    in_terms = send_pair(total(in_keep, after(in_got, leaving)).astype(BF16))
    attn_terms = send_second(total(*after(attn_first, leaving)).astype(BF16))
    out_oth = swap(after(out_part, leaving))
    block = (hidden + (out_part.astype(F32) + out_oth.astype(F32)) + out_bias).astype(BF16)
    block_got = half_weight(block)
    block_out = jnp.where(home, block, block_got)
    kept = kept.reshape(2, rows // 2, width)
    kept_got = half_weight(taken(kept, 1 - mp, 0))

    def side_by_side(*groups):
        values = [total(*terms).reshape(high * mid, part_rows, -1) for terms in groups]
        return jnp.concatenate(values, axis=2).astype(BF16)

    feed_value = side_by_side(after(in_terms, leaving), after(out_terms, leaving))

    returning = pick(back, wanted_back, feed_value)
    returned = lax.all_to_all(
        returning.reshape(dp_count, 2, piece, width), "dp", 0, 0, tiled=True
    )
    returned = after(returned, kept_got, block_got)
    kept = jnp.where(home, taken(kept, mp, 0), kept_got)
    returned = returned.transpose(1, 0, 2, 3).reshape(rows // 2, width)
    mine = (kept.astype(F32) + returned.astype(F32)).astype(BF16)
    other = lax.ppermute(mine, "mp", [(0, 1), (1, 0)])
    grad_tokens = jnp.where(
        jnp.arange(2)[:, None, None] == mp, mine[None], other[None]
    ).reshape(rows, width)

    short = after(short, returning)
    counts = jnp.where((core == 0) | (jnp.arange(6) < 2), 1.0, 0.0).astype(F32)
    wide = (short[:6] * counts[:, None]).reshape(6, dp_count, 1, part_rows)
    wide = jnp.broadcast_to(wide, (6, dp_count, 2, part_rows)).transpose(1, 2, 0, 3)
    to_half = (jnp.arange(2) == core)[None, :, None]

    def half_terms(vectors):
        terms = vectors.reshape(vectors.shape[0], dp_count, -1).transpose(1, 0, 2)
        return jnp.where(to_half, terms.reshape(dp_count, 1, -1), 0.0)

    short = jnp.concatenate(
        [
            wide.reshape(dp_count, 2, -1),
            half_terms(short[6].reshape(2, local)),
            half_terms(short[7:].reshape(1, units)),
        ],
        axis=-1,
    ).reshape(2 * dp_count, -1)

    sum_feed = far(feed_value, mine)
    sum_in, sum_out = sum_feed[:, :units], sum_feed[:, units:]
    sum_attn = far(side_by_side(after(attn_terms, mine)))
    short = lax.all_to_all(after(short, mine), both, 0, 0, tiled=True)
    short = jnp.sum(after(short, sum_attn), axis=0)
    sum_qkv = sum_attn[:, : 3 * local].reshape(-1, 3, local)
    sum_proj = sum_attn[:, 3 * local :].T

    plain = short[: 6 * part_rows].reshape(6, part_rows)
    sum_qv = short[6 * part_rows : 6 * part_rows + width // dp_count].reshape(2, -1)
    sum_bin = short[6 * part_rows + width // dp_count :]
    return (
        block_out,
        grad_tokens,
        plain[0],
        plain[1],
        sum_qkv,
        sum_qv,
        sum_proj,
        plain[4],
        plain[2],
        plain[3],
        sum_in,
        sum_bin,
        sum_out.T,
        plain[5],
    )


def solution(mesh):
    return jax.shard_map(
        shards,
        mesh=mesh,
        in_specs=(
            P("dp", None),
            P("dp"),
            P(),
            P("dp", None),
            P(),
            P(),
            P(None, None, "mp"),
            P(None, "mp"),
            P("mp", None),
            P(),
            P(),
            P(),
            P(None, "mp"),
            P("mp"),
            P("mp", None),
            P(),
            P("dp", None),
        ),
        out_specs=(
            P("dp", None),
            P("dp", None),
            P("dp"),
            P("dp"),
            P("dp", None, "mp"),
            P(None, ("mp", "dp")),
            P("mp", "dp"),
            P("dp"),
            P("dp"),
            P("dp"),
            P("dp", "mp"),
            P(("mp", "dp")),
            P("mp", "dp"),
            P("dp"),
        ),
        check_vma=False,
    )
```

```python
import functools

import jax
import jax.numpy as jnp
from jax import lax
from jax.experimental import pallas as pl
from jax.experimental.pallas import tpu as pltpu
from jax.sharding import PartitionSpec as P

HEAD_DIM = 64
NORM_EPS = 1e-06
NEG_FILL = -1e30
SCORE_SCALE = HEAD_DIM ** (-0.5)
MAX_CLIP = 256
LANES = 128
F32 = jnp.float32
BF16 = jnp.bfloat16
MIB = 1 << 20
SMALL = pl.CostEstimate(flops=1 << 20, bytes_accessed=1 << 20, transcendentals=0)


def nn(left, right):
    return lax.dot_general(left, right, (((1,), (0,)), ((), ())), preferred_element_type=F32)


def nt(left, right):
    return lax.dot_general(left, right, (((1,), (1,)), ((), ())), preferred_element_type=F32)


def vmem():
    return pl.BlockSpec(memory_space=pltpu.VMEM)


def hbm():
    return pl.BlockSpec(memory_space=pltpu.HBM)


def anywhere():
    return pl.BlockSpec(memory_space=pl.ANY)


def smem():
    return pl.BlockSpec(memory_space=pltpu.SMEM)


def params(mib):
    return pltpu.CompilerParams(vmem_limit_bytes=mib * MIB)


def shape(dims, dtype):
    return jax.ShapeDtypeStruct(dims, dtype)


def row_stats(vector):
    mean = jnp.mean(vector, axis=-1, keepdims=True)
    centred = vector - mean
    spread = jnp.mean(centred * centred, axis=-1, keepdims=True)
    return centred, lax.rsqrt(spread + NORM_EPS)


def on_lanes(column):
    return jnp.broadcast_to(column, (column.shape[0], LANES))


def wide_rsqrt(inv, here, width):
    return jnp.concatenate([inv[here, :]] * (width // LANES), axis=1)


def row_sum(block):
    return jnp.sum(block, axis=0, keepdims=True)


def fold_rows(block):
    rows, width = block.shape
    return jnp.sum(block.reshape(rows // 8, 8, width), axis=0)


def pick_kernel(index, source, *refs):
    picked = refs[-1]

    def move(i, carry):
        picked[i] = source[index[i]]
        return carry

    lax.fori_loop(0, picked.shape[0], move, 0, unroll=4)


def pick(source, index, *after):
    dims = index.shape + source.shape[1:]
    return pl.pallas_call(
        pick_kernel,
        out_shape=shape(dims, source.dtype),
        in_specs=[smem(), vmem()] + [hbm()] * len(after),
        out_specs=vmem(),
        compiler_params=params(16),
        cost_estimate=SMALL,
        name="pick",
    )(index, source, *after)


def move(source, target, sem):
    return pltpu.make_async_copy(source, target, sem)


PARTS = 4


def part_moves(pairs, sems):
    moves = []
    for c in range(PARTS):
        row = []
        for n, (source, target) in enumerate(pairs):
            count = source.shape[0] // PARTS
            here = pl.ds(c * count, count)
            row.append(move(source.at[here, :], target.at[here, :], sems.at[n, c]))
        moves.append(row)
    return moves


def start_all(moves):
    for one in moves:
        one.start()


def wait_all(moves):
    for one in moves:
        one.wait()


def interleave(*streams):
    order = sorted(
        ((n + 0.5) / len(stream), which, n)
        for which, stream in enumerate(streams)
        for n in range(len(stream))
    )
    for _, which, n in order:
        streams[which][n]()


def spread_clips(seg_row, seg_b):
    for i in range(seg_b.shape[0] // LANES):
        here = pl.ds(i * LANES, LANES)
        seg_b[here, :] = jnp.broadcast_to(seg_row[:, here], (LANES, LANES)).T


def key_window(j, rows):
    window = min(rows, LANES + 2 * MAX_CLIP)
    here = pl.ds(pl.multiple_of(j * LANES, LANES), LANES)
    first = pl.multiple_of(jnp.clip(j * LANES - MAX_CLIP, 0, rows - window), LANES)
    return here, pl.ds(first, window)


def set_bias(bias, seg_b, seg_row, here, keys):
    filled = jnp.where(seg_b[keys, :] == seg_row[:, here], 0.0, NEG_FILL)
    bias[:, pl.ds(0, LANES)] = filled
    bias[:, pl.ds(LANES, LANES)] = filled


def two_heads(block):
    lane = lax.broadcasted_iota(jnp.int32, block.shape, 1)
    return jnp.concatenate(
        [block * (lane // HEAD_DIM == e).astype(BF16) for e in range(2)], axis=0
    )


def attention_kernel(
    blend, flags, seg_row, vecs, biases, tok, own, oth, w3, wp, *refs
):
    mixed, n1, normed, inv, q, k, v, att, part, lse = refs[-32:-22]
    (
        tok_v, own_v, oth_v, w3_v, wp_v, mixed_v, n1_v, q_v, k_v, v_v, att_v, part_v,
        vt, att_t, seg_b, bias, ones, normed_v, inv_v, in_sems, half_sems, out_sems,
    ) = refs[-22:]
    rows, width = tok.shape
    local = wp.shape[0]
    half_rows = rows // 2
    ratio = blend[0]
    blk = 32
    big = 256

    loads = [
        move(source, target, in_sems.at[n])
        for n, (source, target) in enumerate([(tok, tok_v), (w3, w3_v), (wp, wp_v)])
    ]
    halves = part_moves([(own, own_v), (oth, oth_v)], half_sems)
    loads[0].start()
    for part_of in halves:
        start_all(part_of)
    start_all(loads[1:])
    early = [
        move(source, target, out_sems.at[n])
        for n, (source, target) in enumerate(
            [
                (mixed_v, mixed), (n1_v, n1), (normed_v, normed), (inv_v, inv),
                (q_v, q), (k_v, k), (v_v, v),
            ]
        )
    ]
    ones[...] = jnp.ones_like(ones)
    spread_clips(seg_row, seg_b)

    loads[0].wait()
    steps = half_rows // PARTS // blk
    for n, src, half in ((0, own_v, flags[0]), (1, oth_v, 1 - flags[0])):
        for c in range(PARTS):
            halves[c][n].wait()

            def mix(i, carry, src=src, half=half, c=c):
                low = (c * steps + i) * blk
                here = pl.ds(pl.multiple_of(half * half_rows + low, blk), blk)
                there = pl.ds(pl.multiple_of(low, blk), blk)
                mine, other = tok_v[here, :].astype(F32), src[there, :].astype(F32)
                blended = ratio * mine + (1.0 - ratio) * other
                mixed_v[here, :] = blended
                centred, scale = row_stats(blended)
                inv_v[here, :] = on_lanes(scale)
                plain = centred * scale
                normed_v[here, :] = plain.astype(BF16)
                n1_v[here, :] = (plain * vecs[0:1, :] + vecs[1:2, :]).astype(BF16)
                return carry

            lax.fori_loop(0, steps, mix, 0, unroll=True)
    start_all(early[:4])

    loads[1].wait()
    for i in range(rows // big):
        here = pl.ds(i * big, big)
        rows_in = n1_v[here, :]
        queries = (nn(rows_in, w3_v[0]) + biases[0:1, :local]).astype(BF16).astype(F32)
        q_v[here, :] = (queries * SCORE_SCALE).astype(BF16)
        k_v[here, :] = nn(rows_in, w3_v[1]).astype(BF16)
        values = (nn(rows_in, w3_v[2]) + biases[0:1, local:]).astype(BF16)
        v_v[here, :] = values
        vt[:, here] = values.T
    start_all(early[4:])

    def attend(j, carry):
        here, keys = key_window(j, rows)
        set_bias(bias, seg_b, seg_row, here, keys)
        for p in range(local // LANES):
            pair = pl.ds(p * LANES, LANES)
            scores = nt(k_v[keys, pair], two_heads(q_v[here, pair])) + bias[...]
            top = jnp.max(scores, axis=0, keepdims=True)
            grown = jnp.exp(scores - top).astype(BF16)
            total = nn(ones[...], grown)[:1]
            out = (nn(vt[pair, keys], grown) / total).astype(BF16)
            logs = top + jnp.log(total)
            for e in range(2):
                lanes = slice(e * LANES, e * LANES + LANES)
                head = slice(e * HEAD_DIM, e * HEAD_DIM + HEAD_DIM)
                att_t[pl.ds(p * LANES + e * HEAD_DIM, HEAD_DIM), here] = out[head, lanes]
                lse[pl.ds(2 * p + e, 1), here] = logs[:, lanes]
        return carry

    lax.fori_loop(0, rows // LANES, attend, 0)

    loads[2].wait()
    last = []
    for i in range(rows // big):
        here = pl.ds(i * big, big)
        block = att_t[:, here].T
        att_v[here, :] = block
        part_v[here, :] = nn(block, wp_v[...]).astype(BF16)
        last.append(move(part_v.at[here, :], part.at[here, :], out_sems.at[8 + i]))
        last[-1].start()
    last.append(move(att_v, att, out_sems.at[7]))
    last[-1].start()
    wait_all(early + last)


def attention(blend, flags, segment, vecs, biases, tok, own, oth, w3, wp, *before):
    rows, width = tok.shape
    local = wp.shape[0]
    window = min(rows, LANES + 2 * MAX_CLIP)
    thin = shape((rows, local), BF16)
    tall = shape((rows, width), BF16)
    return pl.pallas_call(
        attention_kernel,
        out_shape=(
            shape((rows, width), F32), tall, tall, shape((rows, LANES), F32),
            thin, thin, thin, thin, tall, shape((local // HEAD_DIM, rows), F32),
        ),
        in_specs=[smem(), smem()] + [vmem()] * 3 + [anywhere()] * 3 + [hbm()] * (2 + len(before)),
        out_specs=[hbm()] * 9 + [vmem()],
        scratch_shapes=[
            pltpu.VMEM((rows, width), BF16),
            pltpu.VMEM((rows // 2, width), BF16),
            pltpu.VMEM((rows // 2, width), BF16),
            pltpu.VMEM(w3.shape, BF16),
            pltpu.VMEM(wp.shape, BF16),
            pltpu.VMEM((rows, width), F32),
            pltpu.VMEM((rows, width), BF16),
            pltpu.VMEM((rows, local), BF16),
            pltpu.VMEM((rows, local), BF16),
            pltpu.VMEM((rows, local), BF16),
            pltpu.VMEM((rows, local), BF16),
            pltpu.VMEM((rows, width), BF16),
            pltpu.VMEM((local, rows), BF16),
            pltpu.VMEM((local, rows), BF16),
            pltpu.VMEM((rows, LANES), F32),
            pltpu.VMEM((window, 2 * LANES), F32),
            pltpu.VMEM((16, window), BF16),
            pltpu.VMEM((rows, width), BF16),
            pltpu.VMEM((rows, LANES), F32),
            pltpu.SemaphoreType.DMA((3,)),
            pltpu.SemaphoreType.DMA((2, PARTS)),
            pltpu.SemaphoreType.DMA((8 + rows // 256,)),
        ],
        compiler_params=params(60),
        cost_estimate=SMALL,
        name="attention",
    )(
        blend, flags, segment, vecs, biases, tok, own, oth, w3, wp, *before,
    )


ERFC_SLOPE = 0.47
ERFC_COEFFS = (
    0.2663094668265691,
    0.2480096137831850,
    0.3362712657560771,
    -0.1262288063821733,
    0.6076790117752645,
    -0.4204702410368928,
    0.0884296765518492,
)


def gelu_parts(pre):
    bell = jnp.exp(pre * pre * -0.5)
    t = 1.0 / (1.0 + jnp.abs(pre) * (ERFC_SLOPE * 0.5**0.5))
    poly = 0.5 * ERFC_COEFFS[-1]
    for coeff in ERFC_COEFFS[-2::-1]:
        poly = poly * t + 0.5 * coeff
    tail = poly * t * bell
    cdf = jnp.where(pre >= 0, 1.0 - tail, tail)
    return pre * cdf, cdf + pre * bell * 0.3989422804014327


def turn_into(target, source, blocks):
    rows = source.shape[0]
    big = 256
    for i in range(rows // big):
        here = pl.ds(i * big, big)
        turned = source[here, :].T
        for start, place, count in blocks:
            target[pl.ds(place, count), here] = turned[start : start + count]


def lead_blocks(width, lead_rows):
    runs = width // lead_rows
    return [
        (run * lead_rows, ((run % 2) * (runs // 2) + run // 2) * lead_rows, lead_rows)
        for run in range(runs)
    ]


def feed_kernel(
    in_rows, out_rows, flags, vecs, biases, mixed, p_own, p_oth, cot, cot_t,
    w_in, w_out, w_out_one, w_out_two,
    hidden, part, gn_part, in_keep, in_send, out_keep, out_send, normed, inv, g_bin, g_bout,
    mixed_v, own_v, oth_v, cot_v, cot_tv, w_in_v, w_out_v, n2, n2_t, act, gp,
    g_in, g_out, normed_v, inv_v, in_sems, turn_sems, weight_sems, out_sems, grad_sems,
):
    rows, width = mixed.shape
    units = w_in.shape[1]
    blk = 32
    big = 256
    sub = 16
    home = flags[1] == 1
    across = flags[2]
    kept_out = jnp.where(home, flags[0], 1 - flags[0]) if in_rows != out_rows else across
    sides = (across, kept_out)

    loads = part_moves(
        [(mixed, mixed_v), (p_own, own_v), (p_oth, oth_v), (cot, cot_v)], in_sems
    )
    for part_of in loads:
        start_all(part_of)

    weights = [move(w_in, w_in_v, weight_sems.at[0])]
    weights[0].start()
    half = w_out.shape[0] // 2
    for n, (got, place) in enumerate([(w_out_one, across), (w_out_two, 1 - across)]):
        spot = pl.ds(pl.multiple_of(place * half, half), half)
        sem = weight_sems.at[1 + n]
        weights.append(move(w_out.at[spot, :], w_out_v.at[spot, :], sem))

        @pl.when(home)
        def _(spot=spot, sem=sem):
            move(w_out.at[spot, :], w_out_v.at[spot, :], sem).start()

        @pl.when(jnp.logical_not(home))
        def _(got=got, spot=spot, sem=sem):
            move(got, w_out_v.at[spot, :], sem).start()

    turns = [
        move(cot_t.at[pl.ds(start, count), :], cot_tv.at[pl.ds(place, count), :], turn_sems.at[n])
        for n, (start, place, count) in enumerate(lead_blocks(width, out_rows))
    ]
    start_all(turns)

    g_bout[...] = jnp.zeros_like(g_bout)
    steps = rows // PARTS // blk
    for c in range(PARTS):
        wait_all(loads[c])

        def norm(i, carry, c=c):
            here = pl.ds(pl.multiple_of((c * steps + i) * blk, blk), blk)
            attn = own_v[here, :].astype(F32) + oth_v[here, :].astype(F32)
            total = mixed_v[here, :] + attn + vecs[4:5, :]
            mixed_v[here, :] = total
            centred, scale = row_stats(total)
            inv_v[here, :] = on_lanes(scale)
            plain = centred * scale
            normed_v[here, :] = plain.astype(BF16)
            n2[here, :] = (plain * vecs[2:3, :] + vecs[3:4, :]).astype(BF16)
            g_bout[...] += fold_rows(cot_v[here, :].astype(F32))
            return carry

        lax.fori_loop(0, steps, norm, 0, unroll=4)
    stores = [
        move(source, target, out_sems.at[0, n])
        for n, (source, target) in enumerate(
            [(mixed_v, hidden), (normed_v, normed), (inv_v, inv)]
        )
    ]
    start_all(stores)
    turn_into(n2_t, n2, lead_blocks(width, in_rows))
    wait_all(weights)

    g_bin[...] = jnp.zeros_like(g_bin)

    def row_block(i, carry):
        here = pl.ds(pl.multiple_of(i * big, big), big)
        for j in range(units // width):
            cols = pl.ds(j * width, width)
            pre_all = nn(n2[here, :], w_in_v[:, cols])
            grad_all = nt(cot_v[here, :], w_out_v[cols, :])
            sums = jnp.zeros((8, width), F32)
            for s in range(big // sub):
                rng = slice(s * sub, s * sub + sub)
                value, slope = gelu_parts(pre_all[rng] + biases[1 + j : 2 + j, :])
                grad = grad_all[rng] * slope
                sums += fold_rows(grad)
                spot = pl.ds(pl.multiple_of(i * big + s * sub, sub), sub)
                act[spot, cols] = value.astype(BF16)
                gp[spot, cols] = grad.astype(BF16)
            g_bin[:, cols] += sums
        oth_v[here, :] = nt(gp[here, :], w_in_v[...]).astype(BF16)
        own_v[here, :] = nn(act[here, :], w_out_v[...]).astype(BF16)
        for n, (source, target) in enumerate([(oth_v, gn_part), (own_v, part)]):
            move(source.at[here, :], target.at[here, :], out_sems.at[1 + n, i]).start()
        return carry

    lax.fori_loop(0, rows // big, row_block, 0)
    for i in range(rows // big):
        here = pl.ds(i * big, big)
        for n, (source, target) in enumerate([(oth_v, gn_part), (own_v, part)]):
            stores.append(move(source.at[here, :], target.at[here, :], out_sems.at[1 + n, i]))

    wait_all(turns)
    half = width // 2
    for n, (turned, right, buf, keep, send) in enumerate(
        [(n2_t, gp, g_in, in_keep, in_send), (cot_tv, act, g_out, out_keep, out_send)]
    ):
        for side in range(2):
            lines = pl.ds(side * half, half)
            for j in range(units // width):
                cols = pl.ds(j * width, width)
                buf[side, :, cols] = nn(turned[lines, :], right[:, cols]).astype(BF16)
        for m, (side, target) in enumerate([(1 - sides[n], send), (sides[n], keep)]):
            stores.append(move(buf.at[side], target, grad_sems.at[n, m]))
            stores[-1].start()
    wait_all(stores)


def feed(
    in_rows, out_rows, flags, vecs, biases, mixed, p_own, p_oth, cot, cot_t,
    w_in, w_out, w_out_one, w_out_two,
):
    rows, width = mixed.shape
    units = w_in.shape[1]
    tall = shape((rows, width), BF16)
    grad = shape((width // 2, units), BF16)
    return pl.pallas_call(
        functools.partial(feed_kernel, in_rows, out_rows),
        out_shape=(
            shape((rows, width), F32), tall, tall, grad, grad, grad, grad,
            tall, shape((rows, LANES), F32), shape((8, units), F32), shape((8, width), F32),
        ),
        in_specs=[smem()] + [vmem()] * 2 + [hbm()] * 2 + [anywhere()] + [hbm()] * 6,
        out_specs=[hbm()] * 9 + [vmem()] * 2,
        scratch_shapes=[
            pltpu.VMEM((rows, width), F32),
            pltpu.VMEM((rows, width), BF16),
            pltpu.VMEM((rows, width), BF16),
            pltpu.VMEM((rows, width), BF16),
            pltpu.VMEM((width, rows), BF16),
            pltpu.VMEM(w_in.shape, BF16),
            pltpu.VMEM(w_out.shape, BF16),
            pltpu.VMEM((rows, width), BF16),
            pltpu.VMEM((width, rows), BF16),
            pltpu.VMEM((rows, units), BF16),
            pltpu.VMEM((rows, units), BF16),
            pltpu.VMEM((2, width // 2, units), BF16),
            pltpu.VMEM((2, width // 2, units), BF16),
            pltpu.VMEM((rows, width), BF16),
            pltpu.VMEM((rows, LANES), F32),
            pltpu.SemaphoreType.DMA((4, PARTS)),
            pltpu.SemaphoreType.DMA((width // out_rows,)),
            pltpu.SemaphoreType.DMA((3,)),
            pltpu.SemaphoreType.DMA((3, rows // 256)),
            pltpu.SemaphoreType.DMA((2, 2)),
        ],
        compiler_params=params(60),
        cost_estimate=SMALL,
        name="feed",
    )(
        flags, vecs, biases, mixed, p_own, p_oth, cot, cot_t,
        w_in, w_out, w_out_one, w_out_two,
    )


def attention_back_kernel(
    lead_rows, by_core, flags, vecs, seg_row, lse, g_bin, g_bout, g_own, g_oth, cot, normed, inv,
    wp, att, k, q, v, w3, n1, normed_one,
    gh, part, keep, send, short,
    gh_v, own_v, oth_v, cot_v, normed_v, inv_v, wp_v, att_v, k_v, q_v, v_v, w3_v, n1_v, one_v, low_v, part_v,
    sums, tails, d_out, kt, dq_t, dk, dv, delta, seg_b, bias, raw, raw_g, low_p, low_g, n1_t, gh_t, grad_v, out,
    in_sems, row_sems, out_sems, last_sems,
):
    rows, width = cot.shape
    local = wp.shape[0]
    blk = 32
    big = 256
    blocks = lead_blocks(width, lead_rows)
    kept_side = jnp.where(flags[1] == 1, flags[0], 1 - flags[0]) if by_core else flags[2]
    row_loads = part_moves(
        [(g_own, own_v), (g_oth, oth_v), (cot, cot_v), (normed, normed_v), (inv, inv_v)],
        row_sems,
    )
    for part_of in row_loads:
        start_all(part_of)
    loads = [
        move(source, target, in_sems.at[n])
        for n, (source, target) in enumerate(
            [
                (wp, wp_v), (att, att_v), (k, k_v), (q, q_v), (v, v_v), (w3, w3_v), (n1, n1_v),
                (normed_one, one_v),
            ]
        )
    ]
    start_all(loads)
    sums[...] = jnp.zeros_like(sums)
    dk[...] = jnp.zeros_like(dk)
    dv[...] = jnp.zeros_like(dv)
    spread_clips(seg_row, seg_b)

    steps = rows // PARTS // blk
    for c in range(PARTS):
        wait_all(row_loads[c])

        def norm(i, carry, c=c):
            here = pl.ds(pl.multiple_of((c * steps + i) * blk, blk), blk)
            grad = own_v[here, :].astype(F32) + oth_v[here, :].astype(F32)
            plain = normed_v[here, :].astype(F32)
            scaled = grad * vecs[2:3, :]
            mean_one = jnp.mean(scaled, axis=-1, keepdims=True)
            mean_two = jnp.mean(scaled * plain, axis=-1, keepdims=True)
            scale = wide_rsqrt(inv_v, here, width)
            back = cot_v[here, :].astype(F32) + scale * (scaled - mean_one - plain * mean_two)
            gh_v[here, :] = back
            low_v[here, :] = back.astype(BF16)
            sums[0] += fold_rows(grad * plain)
            sums[1] += fold_rows(grad)
            sums[2] += fold_rows(back)
            return carry

        lax.fori_loop(0, steps, norm, 0, unroll=2)
    stores = [move(gh_v, gh, out_sems.at[0])]
    stores[0].start()

    wait_all(loads[:3])
    heads = local // HEAD_DIM
    lane = lax.broadcasted_iota(jnp.int32, (delta.shape[0], local), 1)
    row = lax.broadcasted_iota(jnp.int32, (delta.shape[0], local), 0)
    of_head = (lane // HEAD_DIM == row).astype(BF16)

    def project(i, carry):
        here = pl.ds(pl.multiple_of(i * big, big), big)
        grad_out = nt(low_v[here, :], wp_v[...]).astype(BF16)
        d_out[here, :] = grad_out
        product = grad_out.astype(F32) * att_v[here, :].astype(F32)
        coarse = product.astype(BF16)
        fine = (product - coarse.astype(F32)).astype(BF16)
        delta[:, here] = nt(of_head, coarse) + nt(of_head, fine)
        kt[:, here] = k_v[here, :].T
        return carry

    lax.fori_loop(0, rows // big, project, 0)
    wait_all(loads[3:])

    pairs = heads // 2
    window = bias.shape[0]
    strip = 128
    strips = window // strip

    def attend(j, carry):
        here, keys = key_window(j, rows)
        first = pl.multiple_of(keys.start, LANES)
        set_bias(bias, seg_b, seg_row, here, keys)
        blocks_two = {}

        def two(p):
            if p not in blocks_two:
                pair = pl.ds(p * LANES, LANES)
                blocks_two[p] = (two_heads(q_v[here, pair]), two_heads(d_out[here, pair]))
            return blocks_two[p]

        def at_strip(n):
            return (
                pl.ds(pl.multiple_of(first + n * strip, strip), strip),
                pl.ds(n * strip, strip),
            )

        def products(p):
            pair = pl.ds(p * LANES, LANES)

            def scores(n):
                def run():
                    some, at = at_strip(n)
                    raw[p % 2, at, :] = nt(k_v[some, pair], two(p)[0])

                return run

            def grads(n):
                def run():
                    some, at = at_strip(n)
                    raw_g[p % 2, at, :] = nt(v_v[some, pair], two(p)[1])

                return run

            return [make(n) for n in range(strips) for make in (scores, grads)]

        def softmax_back(p):
            tops = jnp.concatenate([lse[pl.ds(2 * p + e, 1), here] for e in range(2)], axis=1)
            inner = jnp.concatenate([delta[pl.ds(2 * p + e, 1), here] for e in range(2)], axis=1)
            half = strip // 2

            def run_at(n):
                def run():
                    at = pl.ds(n * half, half)
                    probs = jnp.exp(raw[p % 2, at, :] + bias[at, :] - tops)
                    low_p[p % 2, at, :] = probs.astype(BF16)
                    low_g[p % 2, at, :] = (probs * (raw_g[p % 2, at, :] - inner)).astype(BF16)

                return run

            return [run_at(n) for n in range(2 * strips)]

        def sums_of(p):
            pair = pl.ds(p * LANES, LANES)

            def keys_of(n):
                def run():
                    some, at = at_strip(n)
                    dk[some, pair] += nn(low_g[p % 2, at, :], two(p)[0])

                return run

            def values_of(n):
                def run():
                    some, at = at_strip(n)
                    dv[some, pair] += nn(low_p[p % 2, at, :], two(p)[1])

                return run

            def queries():
                grad_q = nn(kt[pair, keys], low_g[p % 2]) * SCORE_SCALE
                for e in range(2):
                    lanes = slice(e * LANES, e * LANES + LANES)
                    head = slice(e * HEAD_DIM, e * HEAD_DIM + HEAD_DIM)
                    dq_t[pl.ds(p * LANES + e * HEAD_DIM, HEAD_DIM), here] = grad_q[head, lanes]

            return [make(n) for n in range(strips) for make in (keys_of, values_of)] + [queries]

        def turns():
            for target, source in ((n1_t, n1_v), (gh_t, low_v)):
                turned = source[here, :].T
                for start, place, count in blocks:
                    target[pl.ds(place, count), here] = turned[start : start + count]

        interleave(products(0), [turns])
        for p in range(pairs):
            matrix = (products(p + 1) if p + 1 < pairs else []) + (sums_of(p - 1) if p else [])
            interleave(softmax_back(p), matrix)
        interleave(sums_of(pairs - 1))
        return carry

    lax.fori_loop(0, rows // LANES, attend, 0)

    tails[...] = jnp.zeros_like(tails)

    def finish(i, carry):
        here = pl.ds(pl.multiple_of(i * big, big), big)
        grad_q, grad_k, grad_val = dq_t[:, here].T, dk[here, :], dv[here, :]
        tails[2, :, pl.ds(0, local)] += fold_rows(grad_q)
        tails[2, :, pl.ds(local, local)] += fold_rows(grad_val)
        lows = [grad.astype(BF16) for grad in (grad_q, grad_k, grad_val)]
        total = sum(nt(low, w3_v[n]) for n, low in enumerate(lows))
        part_v[here, :] = total.astype(BF16)
        tails[0] += fold_rows(total * one_v[here, :].astype(F32))
        tails[1] += fold_rows(total)
        for n, low in enumerate(lows):
            grad_v[here, pl.ds(n * local, local)] = low
        move(part_v.at[here, :], part.at[here, :], last_sems.at[i]).start()
        return carry

    lax.fori_loop(0, rows // big, finish, 0)
    for i in range(rows // big):
        here = pl.ds(i * big, big)
        stores.append(move(part_v.at[here, :], part.at[here, :], last_sems.at[i]))
    units = g_bin.shape[1]
    listed = [tails[0], tails[1], sums[0], sums[1], sums[2], g_bout[...], tails[2]]
    listed += [g_bin[:, pl.ds(n, width)] for n in range(0, units, width)]
    for n, block in enumerate(listed):
        short[pl.ds(n, 1), :] = row_sum(block)
    half = width // 2
    for side in range(2):
        lines = pl.ds(side * half, half)
        for n in range(3):
            cols = pl.ds(n * local, local)
            out[side, :, cols] = nn(n1_t[lines, :], grad_v[:, cols]).astype(BF16)
        out[side, :, pl.ds(3 * local, local)] = nn(gh_t[lines, :], att_v[...]).astype(BF16)
    for n, (side, target) in enumerate([(1 - kept_side, send), (kept_side, keep)]):
        stores.append(move(out.at[side], target, out_sems.at[1 + n]))
        stores[-1].start()
    wait_all(stores)


def attention_back(
    lead_rows, by_core, flags, vecs, segment, lse, g_bin, g_bout, g_own, g_oth, cot, normed, inv,
    wp, att, k, q, v, w3, n1, normed_one,
):
    rows, width = cot.shape
    local = wp.shape[0]
    window = min(rows, LANES + 2 * MAX_CLIP)
    tall, thin = pltpu.VMEM((rows, width), BF16), pltpu.VMEM((rows, local), BF16)
    turned = pltpu.VMEM((width, rows), BF16)
    half = (width // 2, 4 * local)
    return pl.pallas_call(
        functools.partial(attention_back_kernel, lead_rows, by_core),
        out_shape=(
            shape((rows, width), F32),
            shape((rows, width), BF16),
            shape(half, BF16),
            shape(half, BF16),
            shape((7 + g_bin.shape[1] // width, width), F32),
        ),
        in_specs=[smem()] + [vmem()] * 5 + [hbm()] + [anywhere()] + [hbm()] * 11,
        out_specs=[hbm()] * 4 + [vmem()],
        scratch_shapes=[
            pltpu.VMEM((rows, width), F32),
            tall, tall, tall, tall,
            pltpu.VMEM((rows, LANES), F32),
            pltpu.VMEM(wp.shape, BF16),
            thin, thin, thin, thin,
            pltpu.VMEM(w3.shape, BF16),
            tall, tall, tall, tall,
            pltpu.VMEM((3, 8, width), F32),
            pltpu.VMEM((3, 8, width), F32),
            thin,
            pltpu.VMEM((local, rows), BF16),
            pltpu.VMEM((local, rows), F32),
            pltpu.VMEM((rows, local), F32),
            pltpu.VMEM((rows, local), F32),
            pltpu.VMEM((8, rows), F32),
            pltpu.VMEM((rows, LANES), F32),
            pltpu.VMEM((window, 2 * LANES), F32),
            pltpu.VMEM((2, window, 2 * LANES), F32),
            pltpu.VMEM((2, window, 2 * LANES), F32),
            pltpu.VMEM((2, window, 2 * LANES), BF16),
            pltpu.VMEM((2, window, 2 * LANES), BF16),
            turned, turned,
            pltpu.VMEM((rows, 3 * local), BF16),
            pltpu.VMEM((2,) + half, BF16),
            pltpu.SemaphoreType.DMA((8,)),
            pltpu.SemaphoreType.DMA((5, PARTS)),
            pltpu.SemaphoreType.DMA((3,)),
            pltpu.SemaphoreType.DMA((rows // 256,)),
        ],
        compiler_params=params(60),
        cost_estimate=SMALL,
        name="attention_back",
    )(
        flags, vecs, segment, lse, g_bin, g_bout, g_own, g_oth, cot, normed, inv,
        wp, att, k, q, v, w3, n1, normed_one,
    )


def mixed_back_kernel(blend, vecs, gh, g_own, g_oth, normed, inv, outgoing, kept, *refs):
    gh_v, own_v, oth_v, normed_v, inv_v, leave_v, kept_v, in_sems, out_sems = refs
    ratio = blend[0]
    rows, width = gh.shape
    blk = 32
    loads = part_moves(
        [(gh, gh_v), (g_own, own_v), (g_oth, oth_v), (normed, normed_v), (inv, inv_v)], in_sems
    )
    stores = part_moves([(leave_v, outgoing), (kept_v, kept)], out_sems)
    for part_of in loads:
        start_all(part_of)
    steps = rows // PARTS // blk
    for c in range(PARTS):
        wait_all(loads[c])

        def norm(i, carry, c=c):
            here = pl.ds(pl.multiple_of((c * steps + i) * blk, blk), blk)
            grad = own_v[here, :].astype(F32) + oth_v[here, :].astype(F32)
            plain = normed_v[here, :].astype(F32)
            scaled = grad * vecs[0:1, :]
            mean_one = jnp.mean(scaled, axis=-1, keepdims=True)
            mean_two = jnp.mean(scaled * plain, axis=-1, keepdims=True)
            scale = wide_rsqrt(inv_v, here, width)
            back = gh_v[here, :] + scale * (scaled - mean_one - plain * mean_two)
            leave_v[here, :] = ((1.0 - ratio) * back).astype(BF16)
            kept_v[here, :] = (ratio * back).astype(BF16)
            return carry

        lax.fori_loop(0, steps, norm, 0, unroll=4)
        start_all(stores[c])
    for part_of in stores:
        wait_all(part_of)


def mixed_back(blend, vecs, gh, g_own, g_oth, normed, inv):
    rows, width = gh.shape
    tall = pltpu.VMEM((rows, width), BF16)
    return pl.pallas_call(
        mixed_back_kernel,
        out_shape=(shape((rows, width), BF16), shape((rows, width), BF16)),
        in_specs=[smem(), vmem()] + [hbm()] * 2 + [anywhere()] + [hbm()] * 2,
        out_specs=[hbm(), hbm()],
        scratch_shapes=[
            pltpu.VMEM((rows, width), F32),
            tall, tall, tall, pltpu.VMEM((rows, LANES), F32), tall, tall,
            pltpu.SemaphoreType.DMA((5, PARTS)),
            pltpu.SemaphoreType.DMA((2, PARTS)),
        ],
        compiler_params=params(60),
        cost_estimate=SMALL,
        name="mixed_back",
    )(blend, vecs, gh, g_own, g_oth, normed, inv)


def shards(
    tokens,
    mix_blend,
    partner,
    clip_ids,
    gain_one,
    shift_one,
    qkv_weight,
    qv_bias,
    proj_weight,
    proj_bias,
    gain_two,
    shift_two,
    in_weight,
    in_bias,
    out_weight,
    out_bias,
    cotangent,
):
    rows, width = tokens.shape
    dp_count = lax.axis_size("dp")
    both = ("dp", "mp")
    bits = dp_count.bit_length() - 1
    seq = lax.axis_index("dp")
    mp = lax.axis_index("mp")
    core = lax.rem(seq, 2)
    home = core == mp
    all_dp = range(dp_count)

    def joint(d, m):
        return 2 * d + m

    core_swap = [(d, d ^ 1) for d in all_dp]
    home_to_pair = [(joint(d, d & 1), joint(d, 1 - (d & 1))) for d in all_dp]
    pair_to_home = [(joint(d, 1 - (d & 1)), joint(d, d & 1)) for d in all_dp]
    weight_move = home_to_pair + [
        (joint(d, 1 - (d & 1)), joint(d ^ 1, 1 - (d & 1))) for d in all_dp
    ]

    def swap(value):
        return lax.ppermute(value, "dp", core_swap)

    def chip_value(value):
        return jnp.where(home, value, swap(value))

    def after(value, *others):
        return lax.optimization_barrier((value,) + others)[0]

    def half_weight(value):
        return lax.ppermute(value, both, weight_move)

    part_rows = width // dp_count
    lead = min(n for n in range(1, bits) if (part_rows << n) % 16 == 0)
    lead_rows = part_rows << lead
    across = lax.rem(seq >> lead, 2)
    flags = jnp.stack([core, home.astype(jnp.int32), across]).astype(jnp.int32)

    def taken(value, index, axis):
        return lax.dynamic_index_in_dim(value, index, axis, keepdims=False)

    seq_small = chip_value(jnp.concatenate([mix_blend, clip_ids[0].astype(F32)]))
    blend, segment = seq_small[:1], seq_small[1:].reshape(1, rows)
    local = proj_weight.shape[0]
    units = in_bias.shape[0]
    half_small = jnp.concatenate([qv_bias.reshape(-1), in_bias])
    half_small = jnp.where(home, half_small, half_weight(half_small))
    biases = half_small.reshape(-1, width)
    vecs = jnp.stack([gain_one, shift_one, gain_two, shift_two, proj_bias])

    w3 = half_weight(qkv_weight.transpose(1, 0, 2))
    wp = half_weight(proj_weight)

    def two_way(value):
        halves = value.reshape(2, value.shape[0] // 2, value.shape[1])
        one = half_weight(taken(halves, across, 0))
        moves = [(joint(d, 1 - (d & 1)), joint(d ^ (1 << lead), 1 - (d & 1))) for d in all_dp]
        return value, one, lax.ppermute(one, both, moves)

    ids = jnp.arange(2 * dp_count, dtype=jnp.int32)
    piece = rows // (2 * 2 * dp_count)
    sent = tokens.reshape(2, dp_count, 2, piece, width)
    sent = lax.dynamic_index_in_dim(sent, mp, 2, keepdims=False)
    spread = lax.all_to_all(sent.transpose(1, 0, 2, 3), "dp", 0, 0, tiled=True)
    wanted = partner[(ids // 4) * 2 + ids % 2] * 2 + (ids // 2) % 2
    source_of = jnp.sum(
        jnp.where(partner[:, None] == ids[None, :dp_count], ids[:dp_count, None], 0),
        axis=0,
        dtype=jnp.int32,
    )
    source = source_of[ids // 2]
    wanted_back = (source // 2) * 4 + (ids % 2) * 2 + source % 2
    chosen = pick(spread.reshape(2 * dp_count, piece, width), wanted, w3, wp, half_small)
    partner_own = lax.all_to_all(chosen, both, 0, 0, tiled=True).reshape(rows // 2, width)
    w_out = two_way(out_weight)
    w_in = half_weight(after(in_weight, w_out[1]))

    tok = chip_value(tokens)
    cot = chip_value(cotangent)
    cot_t = cot.T
    partner_oth = swap(after(partner_own, tok, cot, vecs, segment, wanted_back))

    mixed, n1, normed_one, inv_one, q, k, v, att, attn_part, lse = attention(
        blend, flags, segment, vecs, biases, tok, partner_own, partner_oth, w3, wp, w_out[2], cot_t
    )
    pair_first = part_rows % 16 == 0
    fed = feed(
        lead_rows, part_rows if pair_first else lead_rows, flags, vecs, biases,
        mixed, attn_part, swap(attn_part), cot, cot_t, w_in, *w_out,
    )
    hidden, out_part, gn2_part, in_keep, in_send, out_keep, out_send = fed[:7]
    normed_two, inv_two, g_bin, g_bout = fed[7:]
    gn2_oth = swap(gn2_part)

    high, mid = dp_count >> (lead + 1), 1 << (lead - 1)
    pair_and_core = pair_to_home + [(joint(d, d & 1), joint(d ^ 1, d & 1)) for d in all_dp]
    pair_diagonal = [(joint(d, 1 - (d & 1)), joint(d ^ 1, d & 1)) for d in all_dp]

    def total(*terms):
        return sum(term.astype(F32) for term in terms)

    def send_across(value):
        return lax.ppermute(value, "dp", [(d, d ^ (1 << lead)) for d in all_dp])

    def send_pair(value):
        value = value.reshape(high, mid, 2, part_rows, -1)
        one = lax.ppermute(taken(value, jnp.where(home, 1 - core, core), 2), both, pair_and_core)
        two = lax.ppermute(taken(value, 1 - core, 2), both, pair_diagonal)
        held = taken(value, core, 2)
        return jnp.where(home, held, jnp.zeros_like(held)), one, two

    def far(value, *others):
        for shift, left in ((1, mid), (lead + 1, high)):
            while left > 1:
                radix = min(4, left)
                left //= radix
                value = value.reshape((-1, left, radix) + value.shape[-2:]).astype(BF16)
                spot = lax.rem(seq >> shift, radix)
                got = [
                    lax.ppermute(
                        taken(value, spot ^ flip, 2),
                        "dp",
                        [(d, d ^ (flip << shift)) for d in all_dp],
                    )
                    for flip in range(1, radix)
                ]
                value = total(taken(value, spot, 2), *after(got, *others))
                shift += radix.bit_length() - 1
        return value.reshape(value.shape[-2:])

    def send_first(keep, send):
        if not pair_first:
            return [keep, send_across(send)]
        one = lax.ppermute(send, both, pair_and_core)
        two = lax.ppermute(keep, both, pair_diagonal)
        return [jnp.where(home, keep, jnp.zeros_like(keep)), one, two]

    def send_second(value):
        if not pair_first:
            return send_pair(value)
        value = value.reshape(high, 2, mid, part_rows, -1)
        return taken(value, across, 1), send_across(taken(value, 1 - across, 1))

    in_got = send_across(in_send)
    out_first = send_first(out_keep, out_send)
    gh, gn1_part, attn_keep, attn_send, short = attention_back(
        lead_rows, False, flags, vecs, segment, lse, g_bin, g_bout,
        gn2_part, gn2_oth, cot, normed_two, inv_two, wp, att, k, q, v, w3, n1, normed_one,
    )
    gn1_oth = swap(after(gn1_part, in_got, *out_first))
    attn_first = [attn_keep, send_across(attn_send)]
    outgoing, kept = mixed_back(blend, vecs, gh, gn1_part, gn1_oth, normed_one, inv_one)

    leaving = taken(outgoing.reshape(2, 2, dp_count, piece, width), core, 1)
    leaving = leaving.transpose(1, 0, 2, 3).reshape(2 * dp_count, piece, width)
    back = lax.all_to_all(leaving, both, 0, 0, tiled=True)

    in_value = total(in_keep, after(in_got, leaving)).astype(BF16)
    in_terms = send_pair(in_value)
    out_oth = swap(after(out_part, leaving))
    out_value = total(*after(out_first, in_value)).astype(BF16)
    out_terms = send_second(out_value)
    attn_value = total(*after(attn_first, out_value)).astype(BF16)
    attn_terms = send_pair(attn_value)
    block = hidden + (out_part.astype(F32) + after(out_oth, attn_value).astype(F32)) + out_bias
    block = block.astype(BF16)
    kept = kept.reshape(2, rows // 2, width)
    kept_got = half_weight(taken(kept, 1 - mp, 0))
    block_got = half_weight(block)

    def side_by_side(*groups):
        values = [total(*terms).reshape(high * mid, part_rows, -1) for terms in groups]
        return jnp.concatenate(values, axis=2).astype(BF16)

    returning = pick(back, wanted_back, block, attn_value)
    returned = lax.all_to_all(
        returning.reshape(dp_count, 2, piece, width), "dp", 0, 0, tiled=True
    )
    returned = after(returned, kept_got)
    kept = jnp.where(home, taken(kept, mp, 0), kept_got)
    returned = returned.transpose(1, 0, 2, 3).reshape(rows // 2, width)
    mine = (kept.astype(F32) + returned.astype(F32)).astype(BF16)
    other = lax.ppermute(mine, "mp", [(0, 1), (1, 0)])
    block_out = jnp.where(home, block, after(block_got, mine))
    grad_tokens = jnp.where(
        jnp.arange(2)[:, None, None] == mp, mine[None], other[None]
    ).reshape(rows, width)

    short = after(short, returning)
    counts = jnp.where((core == 0) | (jnp.arange(6) < 2), 1.0, 0.0).astype(F32)
    wide = (short[:6] * counts[:, None]).reshape(6, dp_count, 1, part_rows)
    wide = jnp.broadcast_to(wide, (6, dp_count, 2, part_rows)).transpose(1, 2, 0, 3)
    to_half = (jnp.arange(2) == core)[None, :, None]

    def half_terms(vectors):
        terms = vectors.reshape(vectors.shape[0], dp_count, -1).transpose(1, 0, 2)
        return jnp.where(to_half, terms.reshape(dp_count, 1, -1), 0.0)

    short = jnp.concatenate(
        [
            wide.reshape(dp_count, 2, -1),
            half_terms(short[6].reshape(2, local)),
            half_terms(short[7:].reshape(1, units)),
        ],
        axis=-1,
    ).reshape(2 * dp_count, -1)

    marker = swap(returning[0, :, :LANES])
    short = lax.all_to_all(after(short, mine), both, 0, 0, tiled=True)
    summed = far(
        side_by_side(*(after(terms, marker) for terms in (in_terms, out_terms, attn_terms))),
        mine,
    )
    sum_in, sum_out, sum_attn = (
        summed[:, :units], summed[:, units : 2 * units], summed[:, 2 * units :]
    )
    short = jnp.sum(short, axis=0)
    sum_qkv = sum_attn[:, : 3 * local].reshape(-1, 3, local)
    sum_proj = sum_attn[:, 3 * local :].T

    plain = short[: 6 * part_rows].reshape(6, part_rows)
    sum_qv = short[6 * part_rows : 6 * part_rows + width // dp_count].reshape(2, -1)
    sum_bin = short[6 * part_rows + width // dp_count :]
    return (
        block_out,
        grad_tokens,
        plain[0],
        plain[1],
        sum_qkv,
        sum_qv,
        sum_proj,
        plain[4],
        plain[2],
        plain[3],
        sum_in,
        sum_bin,
        sum_out.T,
        plain[5],
    )


def solution(mesh):
    return jax.shard_map(
        shards,
        mesh=mesh,
        in_specs=(
            P("dp", None),
            P("dp"),
            P(),
            P("dp", None),
            P(),
            P(),
            P(None, None, "mp"),
            P(None, "mp"),
            P("mp", None),
            P(),
            P(),
            P(),
            P(None, "mp"),
            P("mp"),
            P("mp", None),
            P(),
            P("dp", None),
        ),
        out_specs=(
            P("dp", None),
            P("dp", None),
            P("dp"),
            P("dp"),
            P("dp", None, "mp"),
            P(None, ("mp", "dp")),
            P("mp", "dp"),
            P("dp"),
            P("dp"),
            P("dp"),
            P("dp", "mp"),
            P(("mp", "dp")),
            P("mp", "dp"),
            P("dp"),
        ),
        check_vma=False,
    )
```

```python
import functools

import jax
import jax.numpy as jnp
from jax import lax
from jax.experimental import pallas as pl
from jax.experimental.pallas import tpu as pltpu
from jax.sharding import PartitionSpec as P

HEAD_DIM = 64
NORM_EPS = 1e-06
NEG_FILL = -1e30
SCORE_SCALE = HEAD_DIM ** (-0.5)
MAX_CLIP = 256
LANES = 128
F32 = jnp.float32
BF16 = jnp.bfloat16
MIB = 1 << 20
SMALL = pl.CostEstimate(flops=1 << 20, bytes_accessed=1 << 20, transcendentals=0)


def nn(left, right):
    return lax.dot_general(left, right, (((1,), (0,)), ((), ())), preferred_element_type=F32)


def nt(left, right):
    return lax.dot_general(left, right, (((1,), (1,)), ((), ())), preferred_element_type=F32)


def vmem():
    return pl.BlockSpec(memory_space=pltpu.VMEM)


def hbm():
    return pl.BlockSpec(memory_space=pltpu.HBM)


def anywhere():
    return pl.BlockSpec(memory_space=pl.ANY)


def smem():
    return pl.BlockSpec(memory_space=pltpu.SMEM)


def params(mib):
    return pltpu.CompilerParams(vmem_limit_bytes=mib * MIB)


def shape(dims, dtype):
    return jax.ShapeDtypeStruct(dims, dtype)


def row_stats(vector):
    mean = jnp.mean(vector, axis=-1, keepdims=True)
    centred = vector - mean
    spread = jnp.mean(centred * centred, axis=-1, keepdims=True)
    return centred, lax.rsqrt(spread + NORM_EPS)


def on_lanes(column):
    return jnp.broadcast_to(column, (column.shape[0], LANES))


def wide_rsqrt(inv, here, width):
    return jnp.concatenate([inv[here, :]] * (width // LANES), axis=1)


def row_sum(block):
    return jnp.sum(block, axis=0, keepdims=True)


def fold_rows(block):
    rows, width = block.shape
    return jnp.sum(block.reshape(rows // 8, 8, width), axis=0)


def pick_kernel(index, source, *refs):
    picked = refs[-1]

    def move(i, carry):
        picked[i] = source[index[i]]
        return carry

    lax.fori_loop(0, picked.shape[0], move, 0, unroll=4)


def pick(source, index, *after):
    dims = index.shape + source.shape[1:]
    return pl.pallas_call(
        pick_kernel,
        out_shape=shape(dims, source.dtype),
        in_specs=[smem(), vmem()] + [hbm()] * len(after),
        out_specs=vmem(),
        compiler_params=params(16),
        cost_estimate=SMALL,
        name="pick",
    )(index, source, *after)


def move(source, target, sem):
    return pltpu.make_async_copy(source, target, sem)


PARTS = 4


def part_moves(pairs, sems):
    moves = []
    for c in range(PARTS):
        row = []
        for n, (source, target) in enumerate(pairs):
            count = source.shape[0] // PARTS
            here = pl.ds(c * count, count)
            row.append(move(source.at[here, :], target.at[here, :], sems.at[n, c]))
        moves.append(row)
    return moves


def start_all(moves):
    for one in moves:
        one.start()


def wait_all(moves):
    for one in moves:
        one.wait()


def interleave(*streams):
    order = sorted(
        ((n + 0.5) / len(stream), which, n)
        for which, stream in enumerate(streams)
        for n in range(len(stream))
    )
    for _, which, n in order:
        streams[which][n]()


def spread_clips(seg_row, seg_b):
    for i in range(seg_b.shape[0] // LANES):
        here = pl.ds(i * LANES, LANES)
        seg_b[here, :] = jnp.broadcast_to(seg_row[:, here], (LANES, LANES)).T


def key_window(j, rows):
    window = min(rows, LANES + 2 * MAX_CLIP)
    here = pl.ds(pl.multiple_of(j * LANES, LANES), LANES)
    first = pl.multiple_of(jnp.clip(j * LANES - MAX_CLIP, 0, rows - window), LANES)
    return here, pl.ds(first, window)


def set_bias(bias, seg_b, seg_row, here, keys):
    filled = jnp.where(seg_b[keys, :] == seg_row[:, here], 0.0, NEG_FILL)
    bias[:, pl.ds(0, LANES)] = filled
    bias[:, pl.ds(LANES, LANES)] = filled


def two_heads(block):
    lane = lax.broadcasted_iota(jnp.int32, block.shape, 1)
    return jnp.concatenate(
        [block * (lane // HEAD_DIM == e).astype(BF16) for e in range(2)], axis=0
    )


def attention_kernel(
    blend, flags, seg_row, vecs, biases, tok, own, oth, w3, wp, *refs
):
    mixed, n1, normed, inv, q, k, v, att, part, lse = refs[-32:-22]
    (
        tok_v, own_v, oth_v, w3_v, wp_v, mixed_v, n1_v, q_v, k_v, v_v, att_v, part_v,
        vt, att_t, seg_b, bias, ones, normed_v, inv_v, in_sems, half_sems, out_sems,
    ) = refs[-22:]
    rows, width = tok.shape
    local = wp.shape[0]
    half_rows = rows // 2
    ratio = blend[0]
    blk = 32
    big = 256

    loads = [
        move(source, target, in_sems.at[n])
        for n, (source, target) in enumerate([(tok, tok_v), (w3, w3_v), (wp, wp_v)])
    ]
    halves = part_moves([(own, own_v), (oth, oth_v)], half_sems)
    loads[0].start()
    for part_of in halves:
        start_all(part_of)
    start_all(loads[1:])
    early = [
        move(source, target, out_sems.at[n])
        for n, (source, target) in enumerate(
            [
                (mixed_v, mixed), (n1_v, n1), (normed_v, normed), (inv_v, inv),
                (q_v, q), (k_v, k), (v_v, v),
            ]
        )
    ]
    ones[...] = jnp.ones_like(ones)
    spread_clips(seg_row, seg_b)

    loads[0].wait()
    steps = half_rows // PARTS // blk
    for n, src, half in ((0, own_v, flags[0]), (1, oth_v, 1 - flags[0])):
        for c in range(PARTS):
            halves[c][n].wait()

            def mix(i, carry, src=src, half=half, c=c):
                low = (c * steps + i) * blk
                here = pl.ds(pl.multiple_of(half * half_rows + low, blk), blk)
                there = pl.ds(pl.multiple_of(low, blk), blk)
                mine, other = tok_v[here, :].astype(F32), src[there, :].astype(F32)
                blended = ratio * mine + (1.0 - ratio) * other
                mixed_v[here, :] = blended
                centred, scale = row_stats(blended)
                inv_v[here, :] = on_lanes(scale)
                plain = centred * scale
                normed_v[here, :] = plain.astype(BF16)
                n1_v[here, :] = (plain * vecs[0:1, :] + vecs[1:2, :]).astype(BF16)
                return carry

            lax.fori_loop(0, steps, mix, 0, unroll=True)
    start_all(early[:4])

    loads[1].wait()
    for i in range(rows // big):
        here = pl.ds(i * big, big)
        rows_in = n1_v[here, :]
        queries = (nn(rows_in, w3_v[0]) + biases[0:1, :local]).astype(BF16).astype(F32)
        q_v[here, :] = (queries * SCORE_SCALE).astype(BF16)
        k_v[here, :] = nn(rows_in, w3_v[1]).astype(BF16)
        values = (nn(rows_in, w3_v[2]) + biases[0:1, local:]).astype(BF16)
        v_v[here, :] = values
        vt[:, here] = values.T
    start_all(early[4:])

    def attend(j, carry):
        here, keys = key_window(j, rows)
        set_bias(bias, seg_b, seg_row, here, keys)
        for p in range(local // LANES):
            pair = pl.ds(p * LANES, LANES)
            scores = nt(k_v[keys, pair], two_heads(q_v[here, pair])) + bias[...]
            top = jnp.max(scores, axis=0, keepdims=True)
            grown = jnp.exp(scores - top).astype(BF16)
            total = nn(ones[...], grown)[:1]
            out = (nn(vt[pair, keys], grown) / total).astype(BF16)
            logs = top + jnp.log(total)
            for e in range(2):
                lanes = slice(e * LANES, e * LANES + LANES)
                head = slice(e * HEAD_DIM, e * HEAD_DIM + HEAD_DIM)
                att_t[pl.ds(p * LANES + e * HEAD_DIM, HEAD_DIM), here] = out[head, lanes]
                lse[pl.ds(2 * p + e, 1), here] = logs[:, lanes]
        return carry

    lax.fori_loop(0, rows // LANES, attend, 0)

    loads[2].wait()
    last = []
    for i in range(rows // big):
        here = pl.ds(i * big, big)
        block = att_t[:, here].T
        att_v[here, :] = block
        part_v[here, :] = nn(block, wp_v[...]).astype(BF16)
        last.append(move(part_v.at[here, :], part.at[here, :], out_sems.at[8 + i]))
        last[-1].start()
    last.append(move(att_v, att, out_sems.at[7]))
    last[-1].start()
    wait_all(early + last)


def attention(blend, flags, segment, vecs, biases, tok, own, oth, w3, wp, *before):
    rows, width = tok.shape
    local = wp.shape[0]
    window = min(rows, LANES + 2 * MAX_CLIP)
    thin = shape((rows, local), BF16)
    tall = shape((rows, width), BF16)
    return pl.pallas_call(
        attention_kernel,
        out_shape=(
            shape((rows, width), F32), tall, tall, shape((rows, LANES), F32),
            thin, thin, thin, thin, tall, shape((local // HEAD_DIM, rows), F32),
        ),
        in_specs=[smem(), smem()] + [vmem()] * 3 + [anywhere()] * 3 + [hbm()] * (2 + len(before)),
        out_specs=[hbm()] * 9 + [vmem()],
        scratch_shapes=[
            pltpu.VMEM((rows, width), BF16),
            pltpu.VMEM((rows // 2, width), BF16),
            pltpu.VMEM((rows // 2, width), BF16),
            pltpu.VMEM(w3.shape, BF16),
            pltpu.VMEM(wp.shape, BF16),
            pltpu.VMEM((rows, width), F32),
            pltpu.VMEM((rows, width), BF16),
            pltpu.VMEM((rows, local), BF16),
            pltpu.VMEM((rows, local), BF16),
            pltpu.VMEM((rows, local), BF16),
            pltpu.VMEM((rows, local), BF16),
            pltpu.VMEM((rows, width), BF16),
            pltpu.VMEM((local, rows), BF16),
            pltpu.VMEM((local, rows), BF16),
            pltpu.VMEM((rows, LANES), F32),
            pltpu.VMEM((window, 2 * LANES), F32),
            pltpu.VMEM((16, window), BF16),
            pltpu.VMEM((rows, width), BF16),
            pltpu.VMEM((rows, LANES), F32),
            pltpu.SemaphoreType.DMA((3,)),
            pltpu.SemaphoreType.DMA((2, PARTS)),
            pltpu.SemaphoreType.DMA((8 + rows // 256,)),
        ],
        compiler_params=params(60),
        cost_estimate=SMALL,
        name="attention",
    )(
        blend, flags, segment, vecs, biases, tok, own, oth, w3, wp, *before,
    )


ERFC_SLOPE = 0.47
ERFC_COEFFS = (
    0.2663094668265691,
    0.2480096137831850,
    0.3362712657560771,
    -0.1262288063821733,
    0.6076790117752645,
    -0.4204702410368928,
    0.0884296765518492,
)


def gelu_parts(pre):
    bell = jnp.exp(pre * pre * -0.5)
    t = 1.0 / (1.0 + jnp.abs(pre) * (ERFC_SLOPE * 0.5**0.5))
    poly = 0.5 * ERFC_COEFFS[-1]
    for coeff in ERFC_COEFFS[-2::-1]:
        poly = poly * t + 0.5 * coeff
    tail = poly * t * bell
    cdf = jnp.where(pre >= 0, 1.0 - tail, tail)
    return pre * cdf, cdf + pre * bell * 0.3989422804014327


def turn_into(target, source, blocks):
    rows = source.shape[0]
    big = 256
    for i in range(rows // big):
        here = pl.ds(i * big, big)
        turned = source[here, :].T
        for start, place, count in blocks:
            target[pl.ds(place, count), here] = turned[start : start + count]


def lead_blocks(width, lead_rows):
    runs = width // lead_rows
    return [
        (run * lead_rows, ((run % 2) * (runs // 2) + run // 2) * lead_rows, lead_rows)
        for run in range(runs)
    ]


def feed_kernel(
    in_rows, out_rows, flags, vecs, biases, mixed, p_own, p_oth, cot, cot_t,
    w_in, w_out, w_out_one, w_out_two,
    hidden, part, gn_part, in_keep, in_send, out_keep, out_send, normed, inv, g_bin, g_bout,
    mixed_v, own_v, oth_v, cot_v, cot_tv, w_in_v, w_out_v, n2, n2_t, act, gp,
    g_in, g_out, normed_v, inv_v, in_sems, turn_sems, weight_sems, out_sems, grad_sems,
):
    rows, width = mixed.shape
    units = w_in.shape[1]
    blk = 32
    big = 256
    sub = 16
    home = flags[1] == 1
    across = flags[2]
    kept_out = jnp.where(home, flags[0], 1 - flags[0]) if in_rows != out_rows else across
    sides = (across, kept_out)

    loads = part_moves(
        [(mixed, mixed_v), (p_own, own_v), (p_oth, oth_v), (cot, cot_v)], in_sems
    )
    for part_of in loads:
        start_all(part_of)

    weights = [move(w_in, w_in_v, weight_sems.at[0])]
    weights[0].start()
    half = w_out.shape[0] // 2
    for n, (got, place) in enumerate([(w_out_one, across), (w_out_two, 1 - across)]):
        spot = pl.ds(pl.multiple_of(place * half, half), half)
        sem = weight_sems.at[1 + n]
        weights.append(move(w_out.at[spot, :], w_out_v.at[spot, :], sem))

        @pl.when(home)
        def _(spot=spot, sem=sem):
            move(w_out.at[spot, :], w_out_v.at[spot, :], sem).start()

        @pl.when(jnp.logical_not(home))
        def _(got=got, spot=spot, sem=sem):
            move(got, w_out_v.at[spot, :], sem).start()

    turns = [
        move(cot_t.at[pl.ds(start, count), :], cot_tv.at[pl.ds(place, count), :], turn_sems.at[n])
        for n, (start, place, count) in enumerate(lead_blocks(width, out_rows))
    ]
    start_all(turns)

    g_bout[...] = jnp.zeros_like(g_bout)
    steps = rows // PARTS // blk
    for c in range(PARTS):
        wait_all(loads[c])

        def norm(i, carry, c=c):
            here = pl.ds(pl.multiple_of((c * steps + i) * blk, blk), blk)
            attn = own_v[here, :].astype(F32) + oth_v[here, :].astype(F32)
            total = mixed_v[here, :] + attn + vecs[4:5, :]
            mixed_v[here, :] = total
            centred, scale = row_stats(total)
            inv_v[here, :] = on_lanes(scale)
            plain = centred * scale
            normed_v[here, :] = plain.astype(BF16)
            n2[here, :] = (plain * vecs[2:3, :] + vecs[3:4, :]).astype(BF16)
            g_bout[...] += fold_rows(cot_v[here, :].astype(F32))
            return carry

        lax.fori_loop(0, steps, norm, 0, unroll=4)
    stores = [
        move(source, target, out_sems.at[0, n])
        for n, (source, target) in enumerate(
            [(mixed_v, hidden), (normed_v, normed), (inv_v, inv)]
        )
    ]
    start_all(stores)
    turn_into(n2_t, n2, lead_blocks(width, in_rows))
    wait_all(weights)

    g_bin[...] = jnp.zeros_like(g_bin)

    def row_block(i, carry):
        here = pl.ds(pl.multiple_of(i * big, big), big)
        for j in range(units // width):
            cols = pl.ds(j * width, width)
            pre_all = nn(n2[here, :], w_in_v[:, cols])
            grad_all = nt(cot_v[here, :], w_out_v[cols, :])
            sums = jnp.zeros((8, width), F32)
            for s in range(big // sub):
                rng = slice(s * sub, s * sub + sub)
                value, slope = gelu_parts(pre_all[rng] + biases[1 + j : 2 + j, :])
                grad = grad_all[rng] * slope
                sums += fold_rows(grad)
                spot = pl.ds(pl.multiple_of(i * big + s * sub, sub), sub)
                act[spot, cols] = value.astype(BF16)
                gp[spot, cols] = grad.astype(BF16)
            g_bin[:, cols] += sums
        oth_v[here, :] = nt(gp[here, :], w_in_v[...]).astype(BF16)
        own_v[here, :] = nn(act[here, :], w_out_v[...]).astype(BF16)
        for n, (source, target) in enumerate([(oth_v, gn_part), (own_v, part)]):
            move(source.at[here, :], target.at[here, :], out_sems.at[1 + n, i]).start()
        return carry

    lax.fori_loop(0, rows // big, row_block, 0)
    for i in range(rows // big):
        here = pl.ds(i * big, big)
        for n, (source, target) in enumerate([(oth_v, gn_part), (own_v, part)]):
            stores.append(move(source.at[here, :], target.at[here, :], out_sems.at[1 + n, i]))

    wait_all(turns)
    half = width // 2
    for n, (turned, right, buf, keep, send) in enumerate(
        [(n2_t, gp, g_in, in_keep, in_send), (cot_tv, act, g_out, out_keep, out_send)]
    ):
        for side in range(2):
            lines = pl.ds(side * half, half)
            for j in range(units // width):
                cols = pl.ds(j * width, width)
                buf[side, :, cols] = nn(turned[lines, :], right[:, cols]).astype(BF16)
        for m, (side, target) in enumerate([(1 - sides[n], send), (sides[n], keep)]):
            stores.append(move(buf.at[side], target, grad_sems.at[n, m]))
            stores[-1].start()
    wait_all(stores)


def feed(
    in_rows, out_rows, flags, vecs, biases, mixed, p_own, p_oth, cot, cot_t,
    w_in, w_out, w_out_one, w_out_two,
):
    rows, width = mixed.shape
    units = w_in.shape[1]
    tall = shape((rows, width), BF16)
    grad = shape((width // 2, units), BF16)
    return pl.pallas_call(
        functools.partial(feed_kernel, in_rows, out_rows),
        out_shape=(
            shape((rows, width), F32), tall, tall, grad, grad, grad, grad,
            tall, shape((rows, LANES), F32), shape((8, units), F32), shape((8, width), F32),
        ),
        in_specs=[smem()] + [vmem()] * 2 + [hbm()] * 2 + [anywhere()] + [hbm()] * 6,
        out_specs=[hbm()] * 9 + [vmem()] * 2,
        scratch_shapes=[
            pltpu.VMEM((rows, width), F32),
            pltpu.VMEM((rows, width), BF16),
            pltpu.VMEM((rows, width), BF16),
            pltpu.VMEM((rows, width), BF16),
            pltpu.VMEM((width, rows), BF16),
            pltpu.VMEM(w_in.shape, BF16),
            pltpu.VMEM(w_out.shape, BF16),
            pltpu.VMEM((rows, width), BF16),
            pltpu.VMEM((width, rows), BF16),
            pltpu.VMEM((rows, units), BF16),
            pltpu.VMEM((rows, units), BF16),
            pltpu.VMEM((2, width // 2, units), BF16),
            pltpu.VMEM((2, width // 2, units), BF16),
            pltpu.VMEM((rows, width), BF16),
            pltpu.VMEM((rows, LANES), F32),
            pltpu.SemaphoreType.DMA((4, PARTS)),
            pltpu.SemaphoreType.DMA((width // out_rows,)),
            pltpu.SemaphoreType.DMA((3,)),
            pltpu.SemaphoreType.DMA((3, rows // 256)),
            pltpu.SemaphoreType.DMA((2, 2)),
        ],
        compiler_params=params(60),
        cost_estimate=SMALL,
        name="feed",
    )(
        flags, vecs, biases, mixed, p_own, p_oth, cot, cot_t,
        w_in, w_out, w_out_one, w_out_two,
    )


def attention_back_kernel(
    lead_rows, part_rows, flags, vecs, seg_row, lse, g_bin, g_bout, g_own, g_oth, cot, normed, inv,
    wp, att, k, q, v, w3, n1, normed_one,
    gh, part, keep, send, short,
    gh_v, own_v, oth_v, cot_v, normed_v, inv_v, wp_v, att_v, k_v, q_v, v_v, w3_v, n1_v, one_v, low_v, part_v,
    sums, tails, d_out, kt, dq_t, dk, dv, delta, seg_b, bias, raw, raw_g, low_p, low_g, n1_t, gh_t, grad_v, out,
    in_sems, row_sems, out_sems, last_sems,
):
    rows, width = cot.shape
    local = wp.shape[0]
    blk = 32
    big = 256
    blocks = lead_blocks(width, lead_rows)
    kept_side = flags[2]
    row_loads = part_moves(
        [(g_own, own_v), (g_oth, oth_v), (cot, cot_v), (normed, normed_v), (inv, inv_v)],
        row_sems,
    )
    for part_of in row_loads:
        start_all(part_of)
    loads = [
        move(source, target, in_sems.at[n])
        for n, (source, target) in enumerate(
            [
                (wp, wp_v), (att, att_v), (k, k_v), (q, q_v), (v, v_v), (w3, w3_v), (n1, n1_v),
                (normed_one, one_v),
            ]
        )
    ]
    start_all(loads)
    sums[...] = jnp.zeros_like(sums)
    dk[...] = jnp.zeros_like(dk)
    dv[...] = jnp.zeros_like(dv)
    spread_clips(seg_row, seg_b)

    steps = rows // PARTS // blk
    for c in range(PARTS):
        wait_all(row_loads[c])

        def norm(i, carry, c=c):
            here = pl.ds(pl.multiple_of((c * steps + i) * blk, blk), blk)
            grad = own_v[here, :].astype(F32) + oth_v[here, :].astype(F32)
            plain = normed_v[here, :].astype(F32)
            scaled = grad * vecs[2:3, :]
            mean_one = jnp.mean(scaled, axis=-1, keepdims=True)
            mean_two = jnp.mean(scaled * plain, axis=-1, keepdims=True)
            scale = wide_rsqrt(inv_v, here, width)
            back = cot_v[here, :].astype(F32) + scale * (scaled - mean_one - plain * mean_two)
            gh_v[here, :] = back
            low_v[here, :] = back.astype(BF16)
            sums[0] += fold_rows(grad * plain)
            sums[1] += fold_rows(grad)
            sums[2] += fold_rows(back)
            return carry

        lax.fori_loop(0, steps, norm, 0, unroll=2)
    stores = [move(gh_v, gh, out_sems.at[0])]
    stores[0].start()

    wait_all(loads[:3])
    heads = local // HEAD_DIM
    lane = lax.broadcasted_iota(jnp.int32, (delta.shape[0], local), 1)
    row = lax.broadcasted_iota(jnp.int32, (delta.shape[0], local), 0)
    of_head = (lane // HEAD_DIM == row).astype(BF16)

    def project(i, carry):
        here = pl.ds(pl.multiple_of(i * big, big), big)
        grad_out = nt(low_v[here, :], wp_v[...]).astype(BF16)
        d_out[here, :] = grad_out
        product = grad_out.astype(F32) * att_v[here, :].astype(F32)
        coarse = product.astype(BF16)
        fine = (product - coarse.astype(F32)).astype(BF16)
        delta[:, here] = nt(of_head, coarse) + nt(of_head, fine)
        kt[:, here] = k_v[here, :].T
        return carry

    lax.fori_loop(0, rows // big, project, 0)
    wait_all(loads[3:])

    pairs = heads // 2
    window = bias.shape[0]
    strip = 128
    strips = window // strip

    def attend(j, carry):
        here, keys = key_window(j, rows)
        first = pl.multiple_of(keys.start, LANES)
        set_bias(bias, seg_b, seg_row, here, keys)
        blocks_two = {}

        def two(p):
            if p not in blocks_two:
                pair = pl.ds(p * LANES, LANES)
                blocks_two[p] = (two_heads(q_v[here, pair]), two_heads(d_out[here, pair]))
            return blocks_two[p]

        def at_strip(n):
            return (
                pl.ds(pl.multiple_of(first + n * strip, strip), strip),
                pl.ds(n * strip, strip),
            )

        def products(p):
            pair = pl.ds(p * LANES, LANES)

            def scores(n):
                def run():
                    some, at = at_strip(n)
                    raw[p % 2, at, :] = nt(k_v[some, pair], two(p)[0])

                return run

            def grads(n):
                def run():
                    some, at = at_strip(n)
                    raw_g[p % 2, at, :] = nt(v_v[some, pair], two(p)[1])

                return run

            return [make(n) for n in range(strips) for make in (scores, grads)]

        def softmax_back(p):
            tops = jnp.concatenate([lse[pl.ds(2 * p + e, 1), here] for e in range(2)], axis=1)
            inner = jnp.concatenate([delta[pl.ds(2 * p + e, 1), here] for e in range(2)], axis=1)
            half = strip // 2

            def run_at(n):
                def run():
                    at = pl.ds(n * half, half)
                    probs = jnp.exp(raw[p % 2, at, :] + bias[at, :] - tops)
                    low_p[p % 2, at, :] = probs.astype(BF16)
                    low_g[p % 2, at, :] = (probs * (raw_g[p % 2, at, :] - inner)).astype(BF16)

                return run

            return [run_at(n) for n in range(2 * strips)]

        def sums_of(p):
            pair = pl.ds(p * LANES, LANES)

            def keys_of(n):
                def run():
                    some, at = at_strip(n)
                    dk[some, pair] += nn(low_g[p % 2, at, :], two(p)[0])

                return run

            def values_of(n):
                def run():
                    some, at = at_strip(n)
                    dv[some, pair] += nn(low_p[p % 2, at, :], two(p)[1])

                return run

            def queries():
                grad_q = nn(kt[pair, keys], low_g[p % 2]) * SCORE_SCALE
                for e in range(2):
                    lanes = slice(e * LANES, e * LANES + LANES)
                    head = slice(e * HEAD_DIM, e * HEAD_DIM + HEAD_DIM)
                    dq_t[pl.ds(p * LANES + e * HEAD_DIM, HEAD_DIM), here] = grad_q[head, lanes]

            return [make(n) for n in range(strips) for make in (keys_of, values_of)] + [queries]

        def turns():
            for target, source in ((n1_t, n1_v), (gh_t, low_v)):
                turned = source[here, :].T
                for start, place, count in blocks:
                    target[pl.ds(place, count), here] = turned[start : start + count]

        interleave(products(0), [turns])
        for p in range(pairs):
            matrix = (products(p + 1) if p + 1 < pairs else []) + (sums_of(p - 1) if p else [])
            interleave(softmax_back(p), matrix)
        interleave(sums_of(pairs - 1))
        return carry

    lax.fori_loop(0, rows // LANES, attend, 0)

    tails[...] = jnp.zeros_like(tails)

    def finish(i, carry):
        here = pl.ds(pl.multiple_of(i * big, big), big)
        grad_q, grad_k, grad_val = dq_t[:, here].T, dk[here, :], dv[here, :]
        tails[2, :, pl.ds(0, local)] += fold_rows(grad_q)
        tails[2, :, pl.ds(local, local)] += fold_rows(grad_val)
        lows = [grad.astype(BF16) for grad in (grad_q, grad_k, grad_val)]
        total = sum(nt(low, w3_v[n]) for n, low in enumerate(lows))
        part_v[here, :] = total.astype(BF16)
        tails[0] += fold_rows(total * one_v[here, :].astype(F32))
        tails[1] += fold_rows(total)
        for n, low in enumerate(lows):
            grad_v[here, pl.ds(n * local, local)] = low
        move(part_v.at[here, :], part.at[here, :], last_sems.at[i]).start()
        return carry

    lax.fori_loop(0, rows // big, finish, 0)
    for i in range(rows // big):
        here = pl.ds(i * big, big)
        stores.append(move(part_v.at[here, :], part.at[here, :], last_sems.at[i]))
    units = g_bin.shape[1]
    listed = [tails[0], tails[1], sums[0], sums[1], sums[2], g_bout[...], tails[2]]
    listed += [g_bin[:, pl.ds(n, width)] for n in range(0, units, width)]
    half = width // 2
    listed = [row_sum(block) for block in listed]
    for n, block in enumerate(listed):
        short[pl.ds(n, 1), :] = block
    if part_rows:
        sources = [
            (jnp.concatenate(listed[:6] + [jnp.zeros((2, width), F32)], axis=0), part_rows),
            (jnp.broadcast_to(listed[6][:, :local], (8, local)), local * part_rows // width),
            (jnp.broadcast_to(listed[6][:, local:], (8, local)), local * part_rows // width),
            (
                jnp.broadcast_to(jnp.concatenate(listed[7:], axis=1), (8, units)),
                units * part_rows // width,
            ),
        ]
        rest = jnp.zeros((part_rows - 8 * len(sources), LANES), F32)
        for start, place, count in blocks:
            for row in range(0, count, part_rows):
                d = (start + row) // part_rows
                parts = [
                    pltpu.roll(source, (source.shape[1] - d * size) % source.shape[1], 1)[:, :LANES]
                    for source, size in sources
                ]
                side, at = divmod(place + row, half)
                out[side, pl.ds(at, part_rows), pl.ds(4 * local, LANES)] = jnp.concatenate(
                    parts + [rest], axis=0
                ).astype(BF16)
    for side in range(2):
        lines = pl.ds(side * half, half)
        for n in range(3):
            cols = pl.ds(n * local, local)
            out[side, :, cols] = nn(n1_t[lines, :], grad_v[:, cols]).astype(BF16)
        out[side, :, pl.ds(3 * local, local)] = nn(gh_t[lines, :], att_v[...]).astype(BF16)
    for n, (side, target) in enumerate([(1 - kept_side, send), (kept_side, keep)]):
        stores.append(move(out.at[side], target, out_sems.at[1 + n]))
        stores[-1].start()
    wait_all(stores)


def attention_back(
    lead_rows, part_rows, flags, vecs, segment, lse, g_bin, g_bout, g_own, g_oth, cot, normed, inv,
    wp, att, k, q, v, w3, n1, normed_one,
):
    rows, width = cot.shape
    local = wp.shape[0]
    window = min(rows, LANES + 2 * MAX_CLIP)
    tall, thin = pltpu.VMEM((rows, width), BF16), pltpu.VMEM((rows, local), BF16)
    turned = pltpu.VMEM((width, rows), BF16)
    half = (width // 2, 4 * local + (LANES if part_rows else 0))
    return pl.pallas_call(
        functools.partial(attention_back_kernel, lead_rows, part_rows),
        out_shape=(
            shape((rows, width), F32),
            shape((rows, width), BF16),
            shape(half, BF16),
            shape(half, BF16),
            shape((7 + g_bin.shape[1] // width, width), F32),
        ),
        in_specs=[smem()] + [vmem()] * 5 + [hbm()] + [anywhere()] + [hbm()] * 11,
        out_specs=[hbm()] * 4 + [vmem()],
        scratch_shapes=[
            pltpu.VMEM((rows, width), F32),
            tall, tall, tall, tall,
            pltpu.VMEM((rows, LANES), F32),
            pltpu.VMEM(wp.shape, BF16),
            thin, thin, thin, thin,
            pltpu.VMEM(w3.shape, BF16),
            tall, tall, tall, tall,
            pltpu.VMEM((3, 8, width), F32),
            pltpu.VMEM((3, 8, width), F32),
            thin,
            pltpu.VMEM((local, rows), BF16),
            pltpu.VMEM((local, rows), F32),
            pltpu.VMEM((rows, local), F32),
            pltpu.VMEM((rows, local), F32),
            pltpu.VMEM((8, rows), F32),
            pltpu.VMEM((rows, LANES), F32),
            pltpu.VMEM((window, 2 * LANES), F32),
            pltpu.VMEM((2, window, 2 * LANES), F32),
            pltpu.VMEM((2, window, 2 * LANES), F32),
            pltpu.VMEM((2, window, 2 * LANES), BF16),
            pltpu.VMEM((2, window, 2 * LANES), BF16),
            turned, turned,
            pltpu.VMEM((rows, 3 * local), BF16),
            pltpu.VMEM((2,) + half, BF16),
            pltpu.SemaphoreType.DMA((8,)),
            pltpu.SemaphoreType.DMA((5, PARTS)),
            pltpu.SemaphoreType.DMA((3,)),
            pltpu.SemaphoreType.DMA((rows // 256,)),
        ],
        compiler_params=params(60),
        cost_estimate=SMALL,
        name="attention_back",
    )(
        flags, vecs, segment, lse, g_bin, g_bout, g_own, g_oth, cot, normed, inv,
        wp, att, k, q, v, w3, n1, normed_one,
    )


def mixed_back_kernel(blend, vecs, gh, g_own, g_oth, normed, inv, outgoing, kept, *refs):
    gh_v, own_v, oth_v, normed_v, inv_v, leave_v, kept_v, in_sems, out_sems = refs
    ratio = blend[0]
    rows, width = gh.shape
    blk = 32
    loads = part_moves(
        [(gh, gh_v), (g_own, own_v), (g_oth, oth_v), (normed, normed_v), (inv, inv_v)], in_sems
    )
    stores = part_moves([(leave_v, outgoing), (kept_v, kept)], out_sems)
    for part_of in loads:
        start_all(part_of)
    steps = rows // PARTS // blk
    for c in range(PARTS):
        wait_all(loads[c])

        def norm(i, carry, c=c):
            here = pl.ds(pl.multiple_of((c * steps + i) * blk, blk), blk)
            grad = own_v[here, :].astype(F32) + oth_v[here, :].astype(F32)
            plain = normed_v[here, :].astype(F32)
            scaled = grad * vecs[0:1, :]
            mean_one = jnp.mean(scaled, axis=-1, keepdims=True)
            mean_two = jnp.mean(scaled * plain, axis=-1, keepdims=True)
            scale = wide_rsqrt(inv_v, here, width)
            back = gh_v[here, :] + scale * (scaled - mean_one - plain * mean_two)
            leave_v[here, :] = ((1.0 - ratio) * back).astype(BF16)
            kept_v[here, :] = (ratio * back).astype(BF16)
            return carry

        lax.fori_loop(0, steps, norm, 0, unroll=4)
        start_all(stores[c])
    for part_of in stores:
        wait_all(part_of)


def mixed_back(blend, vecs, gh, g_own, g_oth, normed, inv):
    rows, width = gh.shape
    tall = pltpu.VMEM((rows, width), BF16)
    return pl.pallas_call(
        mixed_back_kernel,
        out_shape=(shape((rows, width), BF16), shape((rows, width), BF16)),
        in_specs=[smem(), vmem()] + [hbm()] * 2 + [anywhere()] + [hbm()] * 2,
        out_specs=[hbm(), hbm()],
        scratch_shapes=[
            pltpu.VMEM((rows, width), F32),
            tall, tall, tall, pltpu.VMEM((rows, LANES), F32), tall, tall,
            pltpu.SemaphoreType.DMA((5, PARTS)),
            pltpu.SemaphoreType.DMA((2, PARTS)),
        ],
        compiler_params=params(60),
        cost_estimate=SMALL,
        name="mixed_back",
    )(blend, vecs, gh, g_own, g_oth, normed, inv)


def shards(
    tokens,
    mix_blend,
    partner,
    clip_ids,
    gain_one,
    shift_one,
    qkv_weight,
    qv_bias,
    proj_weight,
    proj_bias,
    gain_two,
    shift_two,
    in_weight,
    in_bias,
    out_weight,
    out_bias,
    cotangent,
):
    rows, width = tokens.shape
    dp_count = lax.axis_size("dp")
    both = ("dp", "mp")
    bits = dp_count.bit_length() - 1
    seq = lax.axis_index("dp")
    mp = lax.axis_index("mp")
    core = lax.rem(seq, 2)
    home = core == mp
    all_dp = range(dp_count)

    def joint(d, m):
        return 2 * d + m

    core_swap = [(d, d ^ 1) for d in all_dp]
    home_to_pair = [(joint(d, d & 1), joint(d, 1 - (d & 1))) for d in all_dp]
    pair_to_home = [(joint(d, 1 - (d & 1)), joint(d, d & 1)) for d in all_dp]
    weight_move = home_to_pair + [
        (joint(d, 1 - (d & 1)), joint(d ^ 1, 1 - (d & 1))) for d in all_dp
    ]

    def swap(value):
        return lax.ppermute(value, "dp", core_swap)

    def chip_value(value):
        return jnp.where(home, value, swap(value))

    def after(value, *others):
        return lax.optimization_barrier((value,) + others)[0]

    def half_weight(value):
        return lax.ppermute(value, both, weight_move)

    part_rows = width // dp_count
    lead = min(n for n in range(1, bits) if (part_rows << n) % 16 == 0)
    lead_rows = part_rows << lead
    across = lax.rem(seq >> lead, 2)
    flags = jnp.stack([core, home.astype(jnp.int32), across]).astype(jnp.int32)

    def taken(value, index, axis):
        return lax.dynamic_index_in_dim(value, index, axis, keepdims=False)

    seq_small = chip_value(jnp.concatenate([mix_blend, clip_ids[0].astype(F32)]))
    blend, segment = seq_small[:1], seq_small[1:].reshape(1, rows)
    local = proj_weight.shape[0]
    units = in_bias.shape[0]
    half_small = jnp.concatenate([qv_bias.reshape(-1), in_bias])
    half_small = jnp.where(home, half_small, half_weight(half_small))
    biases = half_small.reshape(-1, width)
    vecs = jnp.stack([gain_one, shift_one, gain_two, shift_two, proj_bias])

    w3 = half_weight(qkv_weight.transpose(1, 0, 2))
    wp = half_weight(proj_weight)

    def two_way(value):
        halves = value.reshape(2, value.shape[0] // 2, value.shape[1])
        one = half_weight(taken(halves, across, 0))
        moves = [(joint(d, 1 - (d & 1)), joint(d ^ (1 << lead), 1 - (d & 1))) for d in all_dp]
        return value, one, lax.ppermute(one, both, moves)

    ids = jnp.arange(2 * dp_count, dtype=jnp.int32)
    piece = rows // (2 * 2 * dp_count)
    sent = tokens.reshape(2, dp_count, 2, piece, width)
    sent = lax.dynamic_index_in_dim(sent, mp, 2, keepdims=False)
    spread = lax.all_to_all(sent.transpose(1, 0, 2, 3), "dp", 0, 0, tiled=True)
    wanted = partner[(ids // 4) * 2 + ids % 2] * 2 + (ids // 2) % 2
    source_of = jnp.sum(
        jnp.where(partner[:, None] == ids[None, :dp_count], ids[:dp_count, None], 0),
        axis=0,
        dtype=jnp.int32,
    )
    source = source_of[ids // 2]
    wanted_back = (source // 2) * 4 + (ids % 2) * 2 + source % 2
    chosen = pick(spread.reshape(2 * dp_count, piece, width), wanted, w3, wp, half_small)
    partner_own = lax.all_to_all(chosen, both, 0, 0, tiled=True).reshape(rows // 2, width)
    w_out = two_way(out_weight)
    w_in = half_weight(after(in_weight, w_out[1]))

    tok = chip_value(tokens)
    cot = chip_value(cotangent)
    cot_t = cot.T
    partner_oth = swap(after(partner_own, tok, cot, vecs, segment, wanted_back))

    mixed, n1, normed_one, inv_one, q, k, v, att, attn_part, lse = attention(
        blend, flags, segment, vecs, biases, tok, partner_own, partner_oth, w3, wp, w_out[2], cot_t
    )
    pair_first = part_rows % 16 == 0
    fed = feed(
        lead_rows, part_rows if pair_first else lead_rows, flags, vecs, biases,
        mixed, attn_part, swap(attn_part), cot, cot_t, w_in, *w_out,
    )
    hidden, out_part, gn2_part, in_keep, in_send, out_keep, out_send = fed[:7]
    normed_two, inv_two, g_bin, g_bout = fed[7:]
    gn2_oth = swap(gn2_part)

    high, mid = dp_count >> (lead + 1), 1 << (lead - 1)
    pair_and_core = pair_to_home + [(joint(d, d & 1), joint(d ^ 1, d & 1)) for d in all_dp]
    pair_diagonal = [(joint(d, 1 - (d & 1)), joint(d ^ 1, d & 1)) for d in all_dp]

    def total(*terms):
        return sum(term.astype(F32) for term in terms)

    def send_across(value):
        return lax.ppermute(value, "dp", [(d, d ^ (1 << lead)) for d in all_dp])

    def send_pair(value):
        value = value.reshape(high, mid, 2, part_rows, -1)
        one = lax.ppermute(taken(value, jnp.where(home, 1 - core, core), 2), both, pair_and_core)
        two = lax.ppermute(taken(value, 1 - core, 2), both, pair_diagonal)
        held = taken(value, core, 2)
        return jnp.where(home, held, jnp.zeros_like(held)), one, two

    def far(value, *others):
        for shift, left in ((1, mid), (lead + 1, high)):
            while left > 1:
                radix = min(4, left)
                left //= radix
                value = value.reshape((-1, left, radix) + value.shape[-2:]).astype(BF16)
                spot = lax.rem(seq >> shift, radix)
                got = [
                    lax.ppermute(
                        taken(value, spot ^ flip, 2),
                        "dp",
                        [(d, d ^ (flip << shift)) for d in all_dp],
                    )
                    for flip in range(1, radix)
                ]
                value = total(taken(value, spot, 2), *after(got, *others))
                shift += radix.bit_length() - 1
        return value.reshape(value.shape[-2:])

    def send_first(keep, send):
        if not pair_first:
            return [keep, send_across(send)]
        one = lax.ppermute(send, both, pair_and_core)
        two = lax.ppermute(keep, both, pair_diagonal)
        return [jnp.where(home, keep, jnp.zeros_like(keep)), one, two]

    def send_second(value):
        if not pair_first:
            return send_pair(value)
        value = value.reshape(high, 2, mid, part_rows, -1)
        return taken(value, across, 1), send_across(taken(value, 1 - across, 1))

    in_got = send_across(in_send)
    out_first = send_first(out_keep, out_send)
    gh, gn1_part, attn_keep, attn_send, short = attention_back(
        lead_rows, part_rows if pair_first else 0, flags, vecs, segment, lse, g_bin, g_bout,
        gn2_part, gn2_oth, cot, normed_two, inv_two, wp, att, k, q, v, w3, n1, normed_one,
    )
    gn1_oth = swap(after(gn1_part, in_got, *out_first))
    attn_first = [attn_keep, send_across(attn_send)]
    outgoing, kept = mixed_back(blend, vecs, gh, gn1_part, gn1_oth, normed_one, inv_one)

    leaving = taken(outgoing.reshape(2, 2, dp_count, piece, width), core, 1)
    leaving = leaving.transpose(1, 0, 2, 3).reshape(2 * dp_count, piece, width)
    back = lax.all_to_all(leaving, both, 0, 0, tiled=True)

    in_value = total(in_keep, after(in_got, leaving)).astype(BF16)
    in_terms = send_pair(in_value)
    out_oth = swap(after(out_part, leaving))
    out_value = total(*after(out_first, in_value)).astype(BF16)
    out_terms = send_second(out_value)
    attn_value = total(*after(attn_first, out_value)).astype(BF16)
    attn_terms = send_pair(attn_value)
    block = hidden + (out_part.astype(F32) + after(out_oth, attn_value).astype(F32)) + out_bias
    block = block.astype(BF16)
    kept = kept.reshape(2, rows // 2, width)
    kept_got = half_weight(taken(kept, 1 - mp, 0))
    block_got = half_weight(block)

    def side_by_side(*groups):
        values = [total(*terms).reshape(high * mid, part_rows, -1) for terms in groups]
        return jnp.concatenate(values, axis=2).astype(BF16)

    returning = pick(back, wanted_back, block, attn_value)
    returned = lax.all_to_all(
        returning.reshape(dp_count, 2, piece, width), "dp", 0, 0, tiled=True
    )
    returned = after(returned, kept_got)
    kept = jnp.where(home, taken(kept, mp, 0), kept_got)
    returned = returned.transpose(1, 0, 2, 3).reshape(rows // 2, width)
    mine = (kept.astype(F32) + returned.astype(F32)).astype(BF16)
    other = lax.ppermute(mine, "mp", [(0, 1), (1, 0)])
    block_out = jnp.where(home, block, after(block_got, mine))
    grad_tokens = jnp.where(
        jnp.arange(2)[:, None, None] == mp, mine[None], other[None]
    ).reshape(rows, width)

    marker = swap(returning[0, :, :LANES])
    summed = far(
        side_by_side(*(after(terms, marker) for terms in (in_terms, out_terms, attn_terms))),
        mine,
    )
    summed = after(summed, other)
    sum_in, sum_out, sum_attn = (
        summed[:, :units], summed[:, units : 2 * units], summed[:, 2 * units :]
    )
    sum_qkv = sum_attn[:, : 3 * local].reshape(-1, 3, local)
    sum_proj = sum_attn[:, 3 * local : 4 * local].T
    quarter, eighth = local // dp_count, units // dp_count
    if pair_first:
        extra = sum_attn[:, 4 * local :]
        plain = extra[:6, :part_rows]
        ours = plain[:2] + lax.ppermute(plain[:2], "mp", [(0, 1), (1, 0)])
        plain = jnp.concatenate([ours, plain[2:]])
        sum_qv = jnp.stack([extra[8, :quarter], extra[16, :quarter]])
        sum_bin = extra[24, :eighth]
    else:
        counts = jnp.where((core == 0) | (jnp.arange(6) < 2), 1.0, 0.0).astype(F32)
        wide = (short[:6] * counts[:, None]).reshape(6, dp_count, 1, part_rows)
        wide = jnp.broadcast_to(wide, (6, dp_count, 2, part_rows)).transpose(1, 2, 0, 3)
        to_half = (jnp.arange(2) == core)[None, :, None]

        def half_terms(vectors):
            terms = vectors.reshape(vectors.shape[0], dp_count, -1).transpose(1, 0, 2)
            return jnp.where(to_half, terms.reshape(dp_count, 1, -1), 0.0)

        short = jnp.concatenate(
            [
                wide.reshape(dp_count, 2, -1),
                half_terms(short[6].reshape(2, local)),
                half_terms(short[7:].reshape(1, units)),
            ],
            axis=-1,
        ).reshape(2 * dp_count, -1)
        short = jnp.sum(lax.all_to_all(short, both, 0, 0, tiled=True), axis=0)
        plain = short[: 6 * part_rows].reshape(6, part_rows)
        sum_qv = short[6 * part_rows : 6 * part_rows + 2 * quarter].reshape(2, -1)
        sum_bin = short[6 * part_rows + 2 * quarter :]
    return (
        block_out,
        grad_tokens,
        plain[0],
        plain[1],
        sum_qkv,
        sum_qv,
        sum_proj,
        plain[4],
        plain[2],
        plain[3],
        sum_in,
        sum_bin,
        sum_out.T,
        plain[5],
    )


def solution(mesh):
    return jax.shard_map(
        shards,
        mesh=mesh,
        in_specs=(
            P("dp", None),
            P("dp"),
            P(),
            P("dp", None),
            P(),
            P(),
            P(None, None, "mp"),
            P(None, "mp"),
            P("mp", None),
            P(),
            P(),
            P(),
            P(None, "mp"),
            P("mp"),
            P("mp", None),
            P(),
            P("dp", None),
        ),
        out_specs=(
            P("dp", None),
            P("dp", None),
            P("dp"),
            P("dp"),
            P("dp", None, "mp"),
            P(None, ("mp", "dp")),
            P("mp", "dp"),
            P("dp"),
            P("dp"),
            P("dp"),
            P("dp", "mp"),
            P(("mp", "dp")),
            P("mp", "dp"),
            P("dp"),
        ),
        check_vma=False,
    )
```

```python
import functools

import jax
import jax.numpy as jnp
from jax import lax
from jax.experimental import pallas as pl
from jax.experimental.pallas import tpu as pltpu
from jax.sharding import PartitionSpec as P

HEAD_DIM = 64
NORM_EPS = 1e-06
NEG_FILL = -1e30
SCORE_SCALE = HEAD_DIM ** (-0.5)
MAX_CLIP = 256
LANES = 128
F32 = jnp.float32
BF16 = jnp.bfloat16
MIB = 1 << 20
SMALL = pl.CostEstimate(flops=1 << 20, bytes_accessed=1 << 20, transcendentals=0)


def nn(left, right):
    return lax.dot_general(left, right, (((1,), (0,)), ((), ())), preferred_element_type=F32)


def nt(left, right):
    return lax.dot_general(left, right, (((1,), (1,)), ((), ())), preferred_element_type=F32)


def vmem():
    return pl.BlockSpec(memory_space=pltpu.VMEM)


def hbm():
    return pl.BlockSpec(memory_space=pltpu.HBM)


def anywhere():
    return pl.BlockSpec(memory_space=pl.ANY)


def smem():
    return pl.BlockSpec(memory_space=pltpu.SMEM)


def params(mib):
    return pltpu.CompilerParams(vmem_limit_bytes=mib * MIB)


def shape(dims, dtype):
    return jax.ShapeDtypeStruct(dims, dtype)


def row_stats(vector):
    mean = jnp.mean(vector, axis=-1, keepdims=True)
    centred = vector - mean
    spread = jnp.mean(centred * centred, axis=-1, keepdims=True)
    return centred, lax.rsqrt(spread + NORM_EPS)


def on_lanes(column):
    return jnp.broadcast_to(column, (column.shape[0], LANES))


def wide_rsqrt(inv, here, width):
    return jnp.concatenate([inv[here, :]] * (width // LANES), axis=1)


def row_sum(block):
    return jnp.sum(block, axis=0, keepdims=True)


def fold_rows(block):
    rows, width = block.shape
    return jnp.sum(block.reshape(rows // 8, 8, width), axis=0)


def pick_kernel(index, source, *refs):
    picked = refs[-1]

    def move(i, carry):
        picked[i] = source[index[i]]
        return carry

    lax.fori_loop(0, picked.shape[0], move, 0, unroll=4)


def pick(source, index, *after):
    dims = index.shape + source.shape[1:]
    return pl.pallas_call(
        pick_kernel,
        out_shape=shape(dims, source.dtype),
        in_specs=[smem(), vmem()] + [hbm()] * len(after),
        out_specs=vmem(),
        compiler_params=params(16),
        cost_estimate=SMALL,
        name="pick",
    )(index, source, *after)


def move(source, target, sem):
    return pltpu.make_async_copy(source, target, sem)


PARTS = 4


def part_moves(pairs, sems):
    moves = []
    for c in range(PARTS):
        row = []
        for n, (source, target) in enumerate(pairs):
            count = source.shape[0] // PARTS
            here = pl.ds(c * count, count)
            row.append(move(source.at[here, :], target.at[here, :], sems.at[n, c]))
        moves.append(row)
    return moves


def start_all(moves):
    for one in moves:
        one.start()


def wait_all(moves):
    for one in moves:
        one.wait()


def interleave(*streams):
    order = sorted(
        ((n + 0.5) / len(stream), which, n)
        for which, stream in enumerate(streams)
        for n in range(len(stream))
    )
    for _, which, n in order:
        streams[which][n]()


def spread_clips(seg_row, seg_b):
    for i in range(seg_b.shape[0] // LANES):
        here = pl.ds(i * LANES, LANES)
        seg_b[here, :] = jnp.broadcast_to(seg_row[:, here], (LANES, LANES)).T


def key_window(j, rows):
    window = min(rows, LANES + 2 * MAX_CLIP)
    here = pl.ds(pl.multiple_of(j * LANES, LANES), LANES)
    first = pl.multiple_of(jnp.clip(j * LANES - MAX_CLIP, 0, rows - window), LANES)
    return here, pl.ds(first, window)


def set_bias(bias, seg_b, seg_row, here, keys):
    filled = jnp.where(seg_b[keys, :] == seg_row[:, here], 0.0, NEG_FILL)
    bias[:, pl.ds(0, LANES)] = filled
    bias[:, pl.ds(LANES, LANES)] = filled


def two_heads(block):
    lane = lax.broadcasted_iota(jnp.int32, block.shape, 1)
    return jnp.concatenate(
        [block * (lane // HEAD_DIM == e).astype(BF16) for e in range(2)], axis=0
    )


def attention_kernel(
    blend, flags, seg_row, vecs, biases, tok, own, oth, w3, wp, *refs
):
    mixed, n1, normed, inv, q, k, v, att, part, lse = refs[-32:-22]
    (
        tok_v, own_v, oth_v, w3_v, wp_v, mixed_v, n1_v, q_v, k_v, v_v, att_v, part_v,
        vt, att_t, seg_b, bias, ones, normed_v, inv_v, in_sems, half_sems, out_sems,
    ) = refs[-22:]
    rows, width = tok.shape
    local = wp.shape[0]
    half_rows = rows // 2
    ratio = blend[0]
    blk = 32
    big = 256

    loads = [
        move(source, target, in_sems.at[n])
        for n, (source, target) in enumerate([(tok, tok_v), (w3, w3_v), (wp, wp_v)])
    ]
    halves = part_moves([(own, own_v), (oth, oth_v)], half_sems)
    loads[0].start()
    for part_of in halves:
        start_all(part_of)
    start_all(loads[1:])
    early = [
        move(source, target, out_sems.at[n])
        for n, (source, target) in enumerate(
            [
                (mixed_v, mixed), (n1_v, n1), (normed_v, normed), (inv_v, inv),
                (q_v, q), (k_v, k), (v_v, v),
            ]
        )
    ]
    ones[...] = jnp.ones_like(ones)
    spread_clips(seg_row, seg_b)

    loads[0].wait()
    steps = half_rows // PARTS // blk
    for n, src, half in ((0, own_v, flags[0]), (1, oth_v, 1 - flags[0])):
        for c in range(PARTS):
            halves[c][n].wait()

            def mix(i, carry, src=src, half=half, c=c):
                low = (c * steps + i) * blk
                here = pl.ds(pl.multiple_of(half * half_rows + low, blk), blk)
                there = pl.ds(pl.multiple_of(low, blk), blk)
                mine, other = tok_v[here, :].astype(F32), src[there, :].astype(F32)
                blended = ratio * mine + (1.0 - ratio) * other
                mixed_v[here, :] = blended
                centred, scale = row_stats(blended)
                inv_v[here, :] = on_lanes(scale)
                plain = centred * scale
                normed_v[here, :] = plain.astype(BF16)
                n1_v[here, :] = (plain * vecs[0:1, :] + vecs[1:2, :]).astype(BF16)
                return carry

            lax.fori_loop(0, steps, mix, 0, unroll=True)
    start_all(early[:4])

    loads[1].wait()
    for i in range(rows // big):
        here = pl.ds(i * big, big)
        rows_in = n1_v[here, :]
        queries = (nn(rows_in, w3_v[0]) + biases[0:1, :local]).astype(BF16).astype(F32)
        q_v[here, :] = (queries * SCORE_SCALE).astype(BF16)
        k_v[here, :] = nn(rows_in, w3_v[1]).astype(BF16)
        values = (nn(rows_in, w3_v[2]) + biases[0:1, local:]).astype(BF16)
        v_v[here, :] = values
        vt[:, here] = values.T
    start_all(early[4:])

    def attend(j, carry):
        here, keys = key_window(j, rows)
        set_bias(bias, seg_b, seg_row, here, keys)
        for p in range(local // LANES):
            pair = pl.ds(p * LANES, LANES)
            scores = nt(k_v[keys, pair], two_heads(q_v[here, pair])) + bias[...]
            top = jnp.max(scores, axis=0, keepdims=True)
            grown = jnp.exp(scores - top).astype(BF16)
            total = nn(ones[...], grown)[:1]
            out = (nn(vt[pair, keys], grown) / total).astype(BF16)
            logs = top + jnp.log(total)
            for e in range(2):
                lanes = slice(e * LANES, e * LANES + LANES)
                head = slice(e * HEAD_DIM, e * HEAD_DIM + HEAD_DIM)
                att_t[pl.ds(p * LANES + e * HEAD_DIM, HEAD_DIM), here] = out[head, lanes]
                lse[pl.ds(2 * p + e, 1), here] = logs[:, lanes]
        return carry

    lax.fori_loop(0, rows // LANES, attend, 0)

    loads[2].wait()
    last = []
    for i in range(rows // big):
        here = pl.ds(i * big, big)
        block = att_t[:, here].T
        att_v[here, :] = block
        part_v[here, :] = nn(block, wp_v[...]).astype(BF16)
        last.append(move(part_v.at[here, :], part.at[here, :], out_sems.at[8 + i]))
        last[-1].start()
    last.append(move(att_v, att, out_sems.at[7]))
    last[-1].start()
    wait_all(early + last)


def attention(blend, flags, segment, vecs, biases, tok, own, oth, w3, wp, *before):
    rows, width = tok.shape
    local = wp.shape[0]
    window = min(rows, LANES + 2 * MAX_CLIP)
    thin = shape((rows, local), BF16)
    tall = shape((rows, width), BF16)
    return pl.pallas_call(
        attention_kernel,
        out_shape=(
            shape((rows, width), F32), tall, tall, shape((rows, LANES), F32),
            thin, thin, thin, thin, tall, shape((local // HEAD_DIM, rows), F32),
        ),
        in_specs=[smem(), smem()] + [vmem()] * 3 + [anywhere()] * 3 + [hbm()] * (2 + len(before)),
        out_specs=[hbm()] * 9 + [vmem()],
        scratch_shapes=[
            pltpu.VMEM((rows, width), BF16),
            pltpu.VMEM((rows // 2, width), BF16),
            pltpu.VMEM((rows // 2, width), BF16),
            pltpu.VMEM(w3.shape, BF16),
            pltpu.VMEM(wp.shape, BF16),
            pltpu.VMEM((rows, width), F32),
            pltpu.VMEM((rows, width), BF16),
            pltpu.VMEM((rows, local), BF16),
            pltpu.VMEM((rows, local), BF16),
            pltpu.VMEM((rows, local), BF16),
            pltpu.VMEM((rows, local), BF16),
            pltpu.VMEM((rows, width), BF16),
            pltpu.VMEM((local, rows), BF16),
            pltpu.VMEM((local, rows), BF16),
            pltpu.VMEM((rows, LANES), F32),
            pltpu.VMEM((window, 2 * LANES), F32),
            pltpu.VMEM((16, window), BF16),
            pltpu.VMEM((rows, width), BF16),
            pltpu.VMEM((rows, LANES), F32),
            pltpu.SemaphoreType.DMA((3,)),
            pltpu.SemaphoreType.DMA((2, PARTS)),
            pltpu.SemaphoreType.DMA((8 + rows // 256,)),
        ],
        compiler_params=params(60),
        cost_estimate=SMALL,
        name="attention",
    )(
        blend, flags, segment, vecs, biases, tok, own, oth, w3, wp, *before,
    )


ERFC_SLOPE = 0.47
ERFC_COEFFS = (
    0.2663094668265691,
    0.2480096137831850,
    0.3362712657560771,
    -0.1262288063821733,
    0.6076790117752645,
    -0.4204702410368928,
    0.0884296765518492,
)


def gelu_parts(pre):
    bell = jnp.exp(pre * pre * -0.5)
    t = 1.0 / (1.0 + jnp.abs(pre) * (ERFC_SLOPE * 0.5**0.5))
    poly = 0.5 * ERFC_COEFFS[-1]
    for coeff in ERFC_COEFFS[-2::-1]:
        poly = poly * t + 0.5 * coeff
    tail = poly * t * bell
    cdf = jnp.where(pre >= 0, 1.0 - tail, tail)
    return pre * cdf, cdf + pre * bell * 0.3989422804014327


def turn_into(target, source, blocks):
    rows = source.shape[0]
    big = 256
    for i in range(rows // big):
        here = pl.ds(i * big, big)
        turned = source[here, :].T
        for start, place, count in blocks:
            target[pl.ds(place, count), here] = turned[start : start + count]


def lead_blocks(width, lead_rows):
    runs = width // lead_rows
    return [
        (run * lead_rows, ((run % 2) * (runs // 2) + run // 2) * lead_rows, lead_rows)
        for run in range(runs)
    ]


def feed_kernel(
    in_rows, out_rows, flags, vecs, biases, mixed, p_own, p_oth, cot, cot_t,
    w_in, w_out, w_out_one, w_out_two,
    hidden, part, gn_part, in_keep, in_send, out_keep, out_send, normed, inv, g_bin, g_bout,
    mixed_v, own_v, oth_v, cot_v, cot_tv, w_in_v, w_out_v, n2, n2_t, act, gp,
    g_in, g_out, normed_v, inv_v, in_sems, turn_sems, weight_sems, out_sems, grad_sems,
):
    rows, width = mixed.shape
    units = w_in.shape[1]
    blk = 32
    big = 256
    sub = 16
    home = flags[1] == 1
    across = flags[2]
    kept_out = jnp.where(home, flags[0], 1 - flags[0]) if in_rows != out_rows else across
    sides = (across, kept_out)

    loads = part_moves(
        [(mixed, mixed_v), (p_own, own_v), (p_oth, oth_v), (cot, cot_v)], in_sems
    )
    for part_of in loads:
        start_all(part_of)

    weights = [move(w_in, w_in_v, weight_sems.at[0])]
    weights[0].start()
    half = w_out.shape[0] // 2
    for n, (got, place) in enumerate([(w_out_one, across), (w_out_two, 1 - across)]):
        spot = pl.ds(pl.multiple_of(place * half, half), half)
        sem = weight_sems.at[1 + n]
        weights.append(move(w_out.at[spot, :], w_out_v.at[spot, :], sem))

        @pl.when(home)
        def _(spot=spot, sem=sem):
            move(w_out.at[spot, :], w_out_v.at[spot, :], sem).start()

        @pl.when(jnp.logical_not(home))
        def _(got=got, spot=spot, sem=sem):
            move(got, w_out_v.at[spot, :], sem).start()

    turns = [
        move(cot_t.at[pl.ds(start, count), :], cot_tv.at[pl.ds(place, count), :], turn_sems.at[n])
        for n, (start, place, count) in enumerate(lead_blocks(width, out_rows))
    ]
    start_all(turns)

    g_bout[...] = jnp.zeros_like(g_bout)
    steps = rows // PARTS // blk
    for c in range(PARTS):
        wait_all(loads[c])

        def norm(i, carry, c=c):
            here = pl.ds(pl.multiple_of((c * steps + i) * blk, blk), blk)
            attn = own_v[here, :].astype(F32) + oth_v[here, :].astype(F32)
            total = mixed_v[here, :] + attn + vecs[4:5, :]
            mixed_v[here, :] = total
            centred, scale = row_stats(total)
            inv_v[here, :] = on_lanes(scale)
            plain = centred * scale
            normed_v[here, :] = plain.astype(BF16)
            n2[here, :] = (plain * vecs[2:3, :] + vecs[3:4, :]).astype(BF16)
            g_bout[...] += fold_rows(cot_v[here, :].astype(F32))
            return carry

        lax.fori_loop(0, steps, norm, 0, unroll=4)
    stores = [
        move(source, target, out_sems.at[0, n])
        for n, (source, target) in enumerate(
            [(mixed_v, hidden), (normed_v, normed), (inv_v, inv)]
        )
    ]
    start_all(stores)
    turn_into(n2_t, n2, lead_blocks(width, in_rows))
    wait_all(weights)

    g_bin[...] = jnp.zeros_like(g_bin)

    def row_block(i, carry):
        here = pl.ds(pl.multiple_of(i * big, big), big)
        for j in range(units // width):
            cols = pl.ds(j * width, width)
            pre_all = nn(n2[here, :], w_in_v[:, cols])
            grad_all = nt(cot_v[here, :], w_out_v[cols, :])
            sums = jnp.zeros((8, width), F32)
            for s in range(big // sub):
                rng = slice(s * sub, s * sub + sub)
                value, slope = gelu_parts(pre_all[rng] + biases[1 + j : 2 + j, :])
                grad = grad_all[rng] * slope
                sums += fold_rows(grad)
                spot = pl.ds(pl.multiple_of(i * big + s * sub, sub), sub)
                act[spot, cols] = value.astype(BF16)
                gp[spot, cols] = grad.astype(BF16)
            g_bin[:, cols] += sums
        oth_v[here, :] = nt(gp[here, :], w_in_v[...]).astype(BF16)
        own_v[here, :] = nn(act[here, :], w_out_v[...]).astype(BF16)
        for n, (source, target) in enumerate([(oth_v, gn_part), (own_v, part)]):
            move(source.at[here, :], target.at[here, :], out_sems.at[1 + n, i]).start()
        return carry

    lax.fori_loop(0, rows // big, row_block, 0)
    for i in range(rows // big):
        here = pl.ds(i * big, big)
        for n, (source, target) in enumerate([(oth_v, gn_part), (own_v, part)]):
            stores.append(move(source.at[here, :], target.at[here, :], out_sems.at[1 + n, i]))

    wait_all(turns)
    half = width // 2
    for n, (turned, right, buf, keep, send) in enumerate(
        [(n2_t, gp, g_in, in_keep, in_send), (cot_tv, act, g_out, out_keep, out_send)]
    ):
        for side in range(2):
            lines = pl.ds(side * half, half)
            for j in range(units // width):
                cols = pl.ds(j * width, width)
                buf[side, :, cols] = nn(turned[lines, :], right[:, cols]).astype(BF16)
        for m, (side, target) in enumerate([(1 - sides[n], send), (sides[n], keep)]):
            stores.append(move(buf.at[side], target, grad_sems.at[n, m]))
            stores[-1].start()
    wait_all(stores)


def feed(
    in_rows, out_rows, flags, vecs, biases, mixed, p_own, p_oth, cot, cot_t,
    w_in, w_out, w_out_one, w_out_two,
):
    rows, width = mixed.shape
    units = w_in.shape[1]
    tall = shape((rows, width), BF16)
    grad = shape((width // 2, units), BF16)
    return pl.pallas_call(
        functools.partial(feed_kernel, in_rows, out_rows),
        out_shape=(
            shape((rows, width), F32), tall, tall, grad, grad, grad, grad,
            tall, shape((rows, LANES), F32), shape((8, units), F32), shape((8, width), F32),
        ),
        in_specs=[smem()] + [vmem()] * 2 + [hbm()] * 2 + [anywhere()] + [hbm()] * 6,
        out_specs=[hbm()] * 9 + [vmem()] * 2,
        scratch_shapes=[
            pltpu.VMEM((rows, width), F32),
            pltpu.VMEM((rows, width), BF16),
            pltpu.VMEM((rows, width), BF16),
            pltpu.VMEM((rows, width), BF16),
            pltpu.VMEM((width, rows), BF16),
            pltpu.VMEM(w_in.shape, BF16),
            pltpu.VMEM(w_out.shape, BF16),
            pltpu.VMEM((rows, width), BF16),
            pltpu.VMEM((width, rows), BF16),
            pltpu.VMEM((rows, units), BF16),
            pltpu.VMEM((rows, units), BF16),
            pltpu.VMEM((2, width // 2, units), BF16),
            pltpu.VMEM((2, width // 2, units), BF16),
            pltpu.VMEM((rows, width), BF16),
            pltpu.VMEM((rows, LANES), F32),
            pltpu.SemaphoreType.DMA((4, PARTS)),
            pltpu.SemaphoreType.DMA((width // out_rows,)),
            pltpu.SemaphoreType.DMA((3,)),
            pltpu.SemaphoreType.DMA((3, rows // 256)),
            pltpu.SemaphoreType.DMA((2, 2)),
        ],
        compiler_params=params(60),
        cost_estimate=SMALL,
        name="feed",
    )(
        flags, vecs, biases, mixed, p_own, p_oth, cot, cot_t,
        w_in, w_out, w_out_one, w_out_two,
    )


def attention_back_kernel(
    lead_rows, part_rows, flags, vecs, seg_row, lse, g_bin, g_bout, g_own, g_oth, cot, normed, inv,
    wp, att, k, q, v, w3, n1, normed_one,
    gh, part, keep, send, short,
    gh_v, own_v, oth_v, cot_v, normed_v, inv_v, wp_v, att_v, k_v, q_v, v_v, w3_v, n1_v, one_v, low_v, part_v,
    sums, tails, d_out, kt, dq_t, dk, dv, delta, seg_b, bias, raw, raw_g, low_p, low_g, n1_t, gh_t, grad_v, out,
    in_sems, row_sems, out_sems, last_sems,
):
    rows, width = cot.shape
    local = wp.shape[0]
    blk = 32
    big = 256
    blocks = lead_blocks(width, lead_rows)
    kept_side = flags[2]
    row_loads = part_moves(
        [(g_own, own_v), (g_oth, oth_v), (cot, cot_v), (normed, normed_v), (inv, inv_v)],
        row_sems,
    )
    for part_of in row_loads:
        start_all(part_of)
    loads = [
        move(source, target, in_sems.at[n])
        for n, (source, target) in enumerate(
            [
                (wp, wp_v), (att, att_v), (k, k_v), (q, q_v), (v, v_v), (w3, w3_v), (n1, n1_v),
                (normed_one, one_v),
            ]
        )
    ]
    start_all(loads)
    sums[...] = jnp.zeros_like(sums)
    dk[...] = jnp.zeros_like(dk)
    dv[...] = jnp.zeros_like(dv)
    spread_clips(seg_row, seg_b)

    steps = rows // PARTS // blk
    for c in range(PARTS):
        wait_all(row_loads[c])

        def norm(i, carry, c=c):
            here = pl.ds(pl.multiple_of((c * steps + i) * blk, blk), blk)
            grad = own_v[here, :].astype(F32) + oth_v[here, :].astype(F32)
            plain = normed_v[here, :].astype(F32)
            scaled = grad * vecs[2:3, :]
            mean_one = jnp.mean(scaled, axis=-1, keepdims=True)
            mean_two = jnp.mean(scaled * plain, axis=-1, keepdims=True)
            scale = wide_rsqrt(inv_v, here, width)
            back = cot_v[here, :].astype(F32) + scale * (scaled - mean_one - plain * mean_two)
            gh_v[here, :] = back
            low_v[here, :] = back.astype(BF16)
            sums[0] += fold_rows(grad * plain)
            sums[1] += fold_rows(grad)
            sums[2] += fold_rows(back)
            return carry

        lax.fori_loop(0, steps, norm, 0, unroll=2)
    stores = [move(gh_v, gh, out_sems.at[0])]
    stores[0].start()

    wait_all(loads[:3])
    heads = local // HEAD_DIM
    lane = lax.broadcasted_iota(jnp.int32, (delta.shape[0], local), 1)
    row = lax.broadcasted_iota(jnp.int32, (delta.shape[0], local), 0)
    of_head = (lane // HEAD_DIM == row).astype(BF16)

    def project(i, carry):
        here = pl.ds(pl.multiple_of(i * big, big), big)
        grad_out = nt(low_v[here, :], wp_v[...]).astype(BF16)
        d_out[here, :] = grad_out
        product = grad_out.astype(F32) * att_v[here, :].astype(F32)
        coarse = product.astype(BF16)
        fine = (product - coarse.astype(F32)).astype(BF16)
        delta[:, here] = nt(of_head, coarse) + nt(of_head, fine)
        kt[:, here] = k_v[here, :].T
        return carry

    lax.fori_loop(0, rows // big, project, 0)
    wait_all(loads[3:])

    pairs = heads // 2
    window = bias.shape[0]
    strip = 128
    strips = window // strip

    def attend(j, carry):
        here, keys = key_window(j, rows)
        first = pl.multiple_of(keys.start, LANES)
        set_bias(bias, seg_b, seg_row, here, keys)
        blocks_two = {}

        def two(p):
            if p not in blocks_two:
                pair = pl.ds(p * LANES, LANES)
                blocks_two[p] = (two_heads(q_v[here, pair]), two_heads(d_out[here, pair]))
            return blocks_two[p]

        def at_strip(n):
            return (
                pl.ds(pl.multiple_of(first + n * strip, strip), strip),
                pl.ds(n * strip, strip),
            )

        def products(p):
            pair = pl.ds(p * LANES, LANES)

            def scores(n):
                def run():
                    some, at = at_strip(n)
                    raw[p % 2, at, :] = nt(k_v[some, pair], two(p)[0])

                return run

            def grads(n):
                def run():
                    some, at = at_strip(n)
                    raw_g[p % 2, at, :] = nt(v_v[some, pair], two(p)[1])

                return run

            return [make(n) for n in range(strips) for make in (scores, grads)]

        def softmax_back(p):
            tops = jnp.concatenate([lse[pl.ds(2 * p + e, 1), here] for e in range(2)], axis=1)
            inner = jnp.concatenate([delta[pl.ds(2 * p + e, 1), here] for e in range(2)], axis=1)
            half = strip // 2

            def run_at(n):
                def run():
                    at = pl.ds(n * half, half)
                    probs = jnp.exp(raw[p % 2, at, :] + bias[at, :] - tops)
                    low_p[p % 2, at, :] = probs.astype(BF16)
                    low_g[p % 2, at, :] = (probs * (raw_g[p % 2, at, :] - inner)).astype(BF16)

                return run

            return [run_at(n) for n in range(2 * strips)]

        def sums_of(p):
            pair = pl.ds(p * LANES, LANES)

            def keys_of(n):
                def run():
                    some, at = at_strip(n)
                    dk[some, pair] += nn(low_g[p % 2, at, :], two(p)[0])

                return run

            def values_of(n):
                def run():
                    some, at = at_strip(n)
                    dv[some, pair] += nn(low_p[p % 2, at, :], two(p)[1])

                return run

            def queries():
                grad_q = nn(kt[pair, keys], low_g[p % 2]) * SCORE_SCALE
                for e in range(2):
                    lanes = slice(e * LANES, e * LANES + LANES)
                    head = slice(e * HEAD_DIM, e * HEAD_DIM + HEAD_DIM)
                    dq_t[pl.ds(p * LANES + e * HEAD_DIM, HEAD_DIM), here] = grad_q[head, lanes]

            return [make(n) for n in range(strips) for make in (keys_of, values_of)] + [queries]

        def turns():
            for target, source in ((n1_t, n1_v), (gh_t, low_v)):
                turned = source[here, :].T
                for start, place, count in blocks:
                    target[pl.ds(place, count), here] = turned[start : start + count]

        interleave(products(0), [turns])
        for p in range(pairs):
            matrix = (products(p + 1) if p + 1 < pairs else []) + (sums_of(p - 1) if p else [])
            interleave(softmax_back(p), matrix)
        interleave(sums_of(pairs - 1))
        return carry

    lax.fori_loop(0, rows // LANES, attend, 0)

    tails[...] = jnp.zeros_like(tails)

    def finish(i, carry):
        here = pl.ds(pl.multiple_of(i * big, big), big)
        grad_q, grad_k, grad_val = dq_t[:, here].T, dk[here, :], dv[here, :]
        tails[2, :, pl.ds(0, local)] += fold_rows(grad_q)
        tails[2, :, pl.ds(local, local)] += fold_rows(grad_val)
        lows = [grad.astype(BF16) for grad in (grad_q, grad_k, grad_val)]
        total = sum(nt(low, w3_v[n]) for n, low in enumerate(lows))
        part_v[here, :] = total.astype(BF16)
        tails[0] += fold_rows(total * one_v[here, :].astype(F32))
        tails[1] += fold_rows(total)
        for n, low in enumerate(lows):
            grad_v[here, pl.ds(n * local, local)] = low
        move(part_v.at[here, :], part.at[here, :], last_sems.at[i]).start()
        return carry

    lax.fori_loop(0, rows // big, finish, 0)
    for i in range(rows // big):
        here = pl.ds(i * big, big)
        stores.append(move(part_v.at[here, :], part.at[here, :], last_sems.at[i]))
    units = g_bin.shape[1]
    listed = [tails[0], tails[1], sums[0], sums[1], sums[2], g_bout[...], tails[2]]
    listed += [g_bin[:, pl.ds(n, width)] for n in range(0, units, width)]
    half = width // 2
    listed = [row_sum(block) for block in listed]
    for n, block in enumerate(listed):
        short[pl.ds(n, 1), :] = block
    if part_rows:
        sources = [
            (jnp.concatenate(listed[:6] + [jnp.zeros((2, width), F32)], axis=0), part_rows),
            (jnp.broadcast_to(listed[6][:, :local], (8, local)), local * part_rows // width),
            (jnp.broadcast_to(listed[6][:, local:], (8, local)), local * part_rows // width),
            (
                jnp.broadcast_to(jnp.concatenate(listed[7:], axis=1), (8, units)),
                units * part_rows // width,
            ),
        ]
        rest = jnp.zeros((part_rows - 8 * len(sources), LANES), F32)
        for start, place, count in blocks:
            for row in range(0, count, part_rows):
                d = (start + row) // part_rows
                parts = [
                    pltpu.roll(source, (source.shape[1] - d * size) % source.shape[1], 1)[:, :LANES]
                    for source, size in sources
                ]
                side, at = divmod(place + row, half)
                out[side, pl.ds(at, part_rows), pl.ds(4 * local, LANES)] = jnp.concatenate(
                    parts + [rest], axis=0
                ).astype(BF16)
    for side in range(2):
        lines = pl.ds(side * half, half)
        for n in range(3):
            cols = pl.ds(n * local, local)
            out[side, :, cols] = nn(n1_t[lines, :], grad_v[:, cols]).astype(BF16)
        out[side, :, pl.ds(3 * local, local)] = nn(gh_t[lines, :], att_v[...]).astype(BF16)
    for n, (side, target) in enumerate([(1 - kept_side, send), (kept_side, keep)]):
        stores.append(move(out.at[side], target, out_sems.at[1 + n]))
        stores[-1].start()
    wait_all(stores)


def attention_back(
    lead_rows, part_rows, flags, vecs, segment, lse, g_bin, g_bout, g_own, g_oth, cot, normed, inv,
    wp, att, k, q, v, w3, n1, normed_one,
):
    rows, width = cot.shape
    local = wp.shape[0]
    window = min(rows, LANES + 2 * MAX_CLIP)
    tall, thin = pltpu.VMEM((rows, width), BF16), pltpu.VMEM((rows, local), BF16)
    turned = pltpu.VMEM((width, rows), BF16)
    half = (width // 2, 4 * local + (LANES if part_rows else 0))
    return pl.pallas_call(
        functools.partial(attention_back_kernel, lead_rows, part_rows),
        out_shape=(
            shape((rows, width), F32),
            shape((rows, width), BF16),
            shape(half, BF16),
            shape(half, BF16),
            shape((7 + g_bin.shape[1] // width, width), F32),
        ),
        in_specs=[smem()] + [vmem()] * 5 + [hbm()] + [anywhere()] + [hbm()] * 11,
        out_specs=[hbm()] * 4 + [vmem()],
        scratch_shapes=[
            pltpu.VMEM((rows, width), F32),
            tall, tall, tall, tall,
            pltpu.VMEM((rows, LANES), F32),
            pltpu.VMEM(wp.shape, BF16),
            thin, thin, thin, thin,
            pltpu.VMEM(w3.shape, BF16),
            tall, tall, tall, tall,
            pltpu.VMEM((3, 8, width), F32),
            pltpu.VMEM((3, 8, width), F32),
            thin,
            pltpu.VMEM((local, rows), BF16),
            pltpu.VMEM((local, rows), F32),
            pltpu.VMEM((rows, local), F32),
            pltpu.VMEM((rows, local), F32),
            pltpu.VMEM((8, rows), F32),
            pltpu.VMEM((rows, LANES), F32),
            pltpu.VMEM((window, 2 * LANES), F32),
            pltpu.VMEM((2, window, 2 * LANES), F32),
            pltpu.VMEM((2, window, 2 * LANES), F32),
            pltpu.VMEM((2, window, 2 * LANES), BF16),
            pltpu.VMEM((2, window, 2 * LANES), BF16),
            turned, turned,
            pltpu.VMEM((rows, 3 * local), BF16),
            pltpu.VMEM((2,) + half, BF16),
            pltpu.SemaphoreType.DMA((8,)),
            pltpu.SemaphoreType.DMA((5, PARTS)),
            pltpu.SemaphoreType.DMA((3,)),
            pltpu.SemaphoreType.DMA((rows // 256,)),
        ],
        compiler_params=params(60),
        cost_estimate=SMALL,
        name="attention_back",
    )(
        flags, vecs, segment, lse, g_bin, g_bout, g_own, g_oth, cot, normed, inv,
        wp, att, k, q, v, w3, n1, normed_one,
    )


def mixed_back_kernel(blend, vecs, gh, g_own, g_oth, normed, inv, outgoing, kept, *refs):
    gh_v, own_v, oth_v, normed_v, inv_v, leave_v, kept_v, in_sems, out_sems = refs
    ratio = blend[0]
    rows, width = gh.shape
    blk = 32
    loads = part_moves(
        [(gh, gh_v), (g_own, own_v), (g_oth, oth_v), (normed, normed_v), (inv, inv_v)], in_sems
    )
    stores = part_moves([(leave_v, outgoing), (kept_v, kept)], out_sems)
    for part_of in loads:
        start_all(part_of)
    steps = rows // PARTS // blk
    for c in range(PARTS):
        wait_all(loads[c])

        def norm(i, carry, c=c):
            here = pl.ds(pl.multiple_of((c * steps + i) * blk, blk), blk)
            grad = own_v[here, :].astype(F32) + oth_v[here, :].astype(F32)
            plain = normed_v[here, :].astype(F32)
            scaled = grad * vecs[0:1, :]
            mean_one = jnp.mean(scaled, axis=-1, keepdims=True)
            mean_two = jnp.mean(scaled * plain, axis=-1, keepdims=True)
            scale = wide_rsqrt(inv_v, here, width)
            back = gh_v[here, :] + scale * (scaled - mean_one - plain * mean_two)
            leave_v[here, :] = ((1.0 - ratio) * back).astype(BF16)
            kept_v[here, :] = (ratio * back).astype(BF16)
            return carry

        lax.fori_loop(0, steps, norm, 0, unroll=4)
        start_all(stores[c])
    for part_of in stores:
        wait_all(part_of)


def mixed_back(blend, vecs, gh, g_own, g_oth, normed, inv):
    rows, width = gh.shape
    tall = pltpu.VMEM((rows, width), BF16)
    return pl.pallas_call(
        mixed_back_kernel,
        out_shape=(shape((rows, width), BF16), shape((rows, width), BF16)),
        in_specs=[smem(), vmem()] + [hbm()] * 2 + [anywhere()] + [hbm()] * 2,
        out_specs=[hbm(), hbm()],
        scratch_shapes=[
            pltpu.VMEM((rows, width), F32),
            tall, tall, tall, pltpu.VMEM((rows, LANES), F32), tall, tall,
            pltpu.SemaphoreType.DMA((5, PARTS)),
            pltpu.SemaphoreType.DMA((2, PARTS)),
        ],
        compiler_params=params(60),
        cost_estimate=SMALL,
        name="mixed_back",
    )(blend, vecs, gh, g_own, g_oth, normed, inv)


def shards(
    tokens,
    mix_blend,
    partner,
    clip_ids,
    gain_one,
    shift_one,
    qkv_weight,
    qv_bias,
    proj_weight,
    proj_bias,
    gain_two,
    shift_two,
    in_weight,
    in_bias,
    out_weight,
    out_bias,
    cotangent,
):
    rows, width = tokens.shape
    dp_count = lax.axis_size("dp")
    both = ("dp", "mp")
    bits = dp_count.bit_length() - 1
    seq = lax.axis_index("dp")
    mp = lax.axis_index("mp")
    core = lax.rem(seq, 2)
    home = core == mp
    all_dp = range(dp_count)

    def joint(d, m):
        return 2 * d + m

    core_swap = [(d, d ^ 1) for d in all_dp]
    home_to_pair = [(joint(d, d & 1), joint(d, 1 - (d & 1))) for d in all_dp]
    pair_to_home = [(joint(d, 1 - (d & 1)), joint(d, d & 1)) for d in all_dp]
    weight_move = home_to_pair + [
        (joint(d, 1 - (d & 1)), joint(d ^ 1, 1 - (d & 1))) for d in all_dp
    ]

    def swap(value):
        return lax.ppermute(value, "dp", core_swap)

    def chip_value(value):
        return jnp.where(home, value, swap(value))

    def after(value, *others):
        return lax.optimization_barrier((value,) + others)[0]

    def half_weight(value):
        return lax.ppermute(value, both, weight_move)

    part_rows = width // dp_count
    lead = min(n for n in range(1, bits) if (part_rows << n) % 16 == 0)
    lead_rows = part_rows << lead
    across = lax.rem(seq >> lead, 2)
    flags = jnp.stack([core, home.astype(jnp.int32), across]).astype(jnp.int32)

    def taken(value, index, axis):
        return lax.dynamic_index_in_dim(value, index, axis, keepdims=False)

    seq_small = chip_value(jnp.concatenate([mix_blend, clip_ids[0].astype(F32)]))
    blend, segment = seq_small[:1], seq_small[1:].reshape(1, rows)
    local = proj_weight.shape[0]
    units = in_bias.shape[0]
    half_small = jnp.concatenate([qv_bias.reshape(-1), in_bias])
    half_small = jnp.where(home, half_small, half_weight(half_small))
    biases = half_small.reshape(-1, width)
    vecs = jnp.stack([gain_one, shift_one, gain_two, shift_two, proj_bias])

    w3 = half_weight(qkv_weight.transpose(1, 0, 2))
    wp = half_weight(proj_weight)

    def two_way(value):
        halves = value.reshape(2, value.shape[0] // 2, value.shape[1])
        one = half_weight(taken(halves, across, 0))
        moves = [(joint(d, 1 - (d & 1)), joint(d ^ (1 << lead), 1 - (d & 1))) for d in all_dp]
        return value, one, lax.ppermute(one, both, moves)

    ids = jnp.arange(2 * dp_count, dtype=jnp.int32)
    piece = rows // (2 * 2 * dp_count)
    sent = tokens.reshape(2, dp_count, 2, piece, width)
    sent = lax.dynamic_index_in_dim(sent, mp, 2, keepdims=False)
    spread = lax.all_to_all(sent.transpose(1, 0, 2, 3), "dp", 0, 0, tiled=True)
    wanted = partner[(ids // 4) * 2 + ids % 2] * 2 + (ids // 2) % 2
    source_of = jnp.sum(
        jnp.where(partner[:, None] == ids[None, :dp_count], ids[:dp_count, None], 0),
        axis=0,
        dtype=jnp.int32,
    )
    source = source_of[ids // 2]
    wanted_back = (source // 2) * 4 + (ids % 2) * 2 + source % 2
    chosen = pick(spread.reshape(2 * dp_count, piece, width), wanted, w3, wp, half_small)
    partner_own = lax.all_to_all(chosen, both, 0, 0, tiled=True).reshape(rows // 2, width)
    w_out = two_way(out_weight)
    w_in = half_weight(after(in_weight, w_out[1]))

    tok = chip_value(tokens)
    cot = chip_value(cotangent)
    cot_t = cot.T
    partner_oth = swap(after(partner_own, tok, cot, vecs, segment, wanted_back))

    mixed, n1, normed_one, inv_one, q, k, v, att, attn_part, lse = attention(
        blend, flags, segment, vecs, biases, tok, partner_own, partner_oth, w3, wp, w_out[2], cot_t
    )
    pair_first = part_rows % 16 == 0
    fed = feed(
        lead_rows, part_rows if pair_first else lead_rows, flags, vecs, biases,
        mixed, attn_part, swap(attn_part), cot, cot_t, w_in, *w_out,
    )
    hidden, out_part, gn2_part, in_keep, in_send, out_keep, out_send = fed[:7]
    normed_two, inv_two, g_bin, g_bout = fed[7:]
    gn2_oth = swap(gn2_part)

    high, mid = dp_count >> (lead + 1), 1 << (lead - 1)
    pair_and_core = pair_to_home + [(joint(d, d & 1), joint(d ^ 1, d & 1)) for d in all_dp]
    pair_diagonal = [(joint(d, 1 - (d & 1)), joint(d ^ 1, d & 1)) for d in all_dp]

    def total(*terms):
        return sum(term.astype(F32) for term in terms)

    def send_across(value):
        return lax.ppermute(value, "dp", [(d, d ^ (1 << lead)) for d in all_dp])

    def send_pair(value):
        value = value.reshape(high, mid, 2, part_rows, -1)
        one = lax.ppermute(taken(value, jnp.where(home, 1 - core, core), 2), both, pair_and_core)
        two = lax.ppermute(taken(value, 1 - core, 2), both, pair_diagonal)
        held = taken(value, core, 2)
        return jnp.where(home, held, jnp.zeros_like(held)), one, two

    def far(value, *others):
        for shift, left in ((1, mid), (lead + 1, high)):
            while left > 1:
                radix = min(4, left)
                left //= radix
                value = value.reshape((-1, left, radix) + value.shape[-2:]).astype(BF16)
                spot = lax.rem(seq >> shift, radix)
                got = [
                    lax.ppermute(
                        taken(value, spot ^ flip, 2),
                        "dp",
                        [(d, d ^ (flip << shift)) for d in all_dp],
                    )
                    for flip in range(1, radix)
                ]
                value = total(taken(value, spot, 2), *after(got, *others))
                shift += radix.bit_length() - 1
        return value.reshape(value.shape[-2:])

    def send_first(keep, send):
        if not pair_first:
            return [keep, send_across(send)]
        one = lax.ppermute(send, both, pair_and_core)
        two = lax.ppermute(keep, both, pair_diagonal)
        return [jnp.where(home, keep, jnp.zeros_like(keep)), one, two]

    def send_second(value):
        if not pair_first:
            return send_pair(value)
        value = value.reshape(high, 2, mid, part_rows, -1)
        return taken(value, across, 1), send_across(taken(value, 1 - across, 1))

    in_got = send_across(in_send)
    out_first = send_first(out_keep, out_send)
    gh, gn1_part, attn_keep, attn_send, short = attention_back(
        lead_rows, part_rows if pair_first else 0, flags, vecs, segment, lse, g_bin, g_bout,
        gn2_part, gn2_oth, cot, normed_two, inv_two, wp, att, k, q, v, w3, n1, normed_one,
    )
    gn1_oth = swap(after(gn1_part, in_got, *out_first))
    attn_first = [attn_keep, send_across(attn_send)]
    in_terms = send_pair(total(in_keep, in_got).astype(BF16))
    outgoing, kept = mixed_back(blend, vecs, gh, gn1_part, gn1_oth, normed_one, inv_one)

    leaving = taken(outgoing.reshape(2, 2, dp_count, piece, width), core, 1)
    leaving = leaving.transpose(1, 0, 2, 3).reshape(2 * dp_count, piece, width)
    back = lax.all_to_all(leaving, both, 0, 0, tiled=True)

    in_value = total(*after(in_terms, leaving)).astype(BF16)
    sum_in = far(in_value)
    out_oth = swap(after(out_part, leaving))
    out_value = total(*after(out_first, in_value)).astype(BF16)
    out_terms = send_second(out_value)
    attn_value = total(*after(attn_first, out_value)).astype(BF16)
    attn_terms = send_pair(attn_value)
    block = hidden + (out_part.astype(F32) + after(out_oth, attn_value).astype(F32)) + out_bias
    block = block.astype(BF16)
    kept = kept.reshape(2, rows // 2, width)
    kept_got = half_weight(taken(kept, 1 - mp, 0))
    block_got = half_weight(block)

    def side_by_side(*groups):
        values = [total(*terms).reshape(high * mid, part_rows, -1) for terms in groups]
        return jnp.concatenate(values, axis=2).astype(BF16)

    returning = pick(back, wanted_back, attn_value, sum_in)
    returned = lax.all_to_all(
        returning.reshape(dp_count, 2, piece, width), "dp", 0, 0, tiled=True
    )
    returned = after(returned, kept_got)
    kept = jnp.where(home, taken(kept, mp, 0), kept_got)
    returned = returned.transpose(1, 0, 2, 3).reshape(rows // 2, width)
    mine = (kept.astype(F32) + returned.astype(F32)).astype(BF16)
    other = lax.ppermute(mine, "mp", [(0, 1), (1, 0)])
    block_out = jnp.where(home, block, after(block_got, mine))
    grad_tokens = jnp.where(
        jnp.arange(2)[:, None, None] == mp, mine[None], other[None]
    ).reshape(rows, width)

    marker = swap(returning[0, :, :LANES])
    summed = far(
        side_by_side(*(after(terms, marker) for terms in (out_terms, attn_terms))),
        mine,
    )
    summed = after(summed, other)
    sum_out, sum_attn = summed[:, :units], summed[:, units:]
    sum_qkv = sum_attn[:, : 3 * local].reshape(-1, 3, local)
    sum_proj = sum_attn[:, 3 * local : 4 * local].T
    quarter, eighth = local // dp_count, units // dp_count
    if pair_first:
        extra = sum_attn[:, 4 * local :]
        plain = extra[:6, :part_rows]
        ours = plain[:2] + lax.ppermute(plain[:2], "mp", [(0, 1), (1, 0)])
        plain = jnp.concatenate([ours, plain[2:]])
        sum_qv = jnp.stack([extra[8, :quarter], extra[16, :quarter]])
        sum_bin = extra[24, :eighth]
    else:
        counts = jnp.where((core == 0) | (jnp.arange(6) < 2), 1.0, 0.0).astype(F32)
        wide = (short[:6] * counts[:, None]).reshape(6, dp_count, 1, part_rows)
        wide = jnp.broadcast_to(wide, (6, dp_count, 2, part_rows)).transpose(1, 2, 0, 3)
        to_half = (jnp.arange(2) == core)[None, :, None]

        def half_terms(vectors):
            terms = vectors.reshape(vectors.shape[0], dp_count, -1).transpose(1, 0, 2)
            return jnp.where(to_half, terms.reshape(dp_count, 1, -1), 0.0)

        short = jnp.concatenate(
            [
                wide.reshape(dp_count, 2, -1),
                half_terms(short[6].reshape(2, local)),
                half_terms(short[7:].reshape(1, units)),
            ],
            axis=-1,
        ).reshape(2 * dp_count, -1)
        short = jnp.sum(lax.all_to_all(short, both, 0, 0, tiled=True), axis=0)
        plain = short[: 6 * part_rows].reshape(6, part_rows)
        sum_qv = short[6 * part_rows : 6 * part_rows + 2 * quarter].reshape(2, -1)
        sum_bin = short[6 * part_rows + 2 * quarter :]
    return (
        block_out,
        grad_tokens,
        plain[0],
        plain[1],
        sum_qkv,
        sum_qv,
        sum_proj,
        plain[4],
        plain[2],
        plain[3],
        sum_in,
        sum_bin,
        sum_out.T,
        plain[5],
    )


def solution(mesh):
    return jax.shard_map(
        shards,
        mesh=mesh,
        in_specs=(
            P("dp", None),
            P("dp"),
            P(),
            P("dp", None),
            P(),
            P(),
            P(None, None, "mp"),
            P(None, "mp"),
            P("mp", None),
            P(),
            P(),
            P(),
            P(None, "mp"),
            P("mp"),
            P("mp", None),
            P(),
            P("dp", None),
        ),
        out_specs=(
            P("dp", None),
            P("dp", None),
            P("dp"),
            P("dp"),
            P("dp", None, "mp"),
            P(None, ("mp", "dp")),
            P("mp", "dp"),
            P("dp"),
            P("dp"),
            P("dp"),
            P("dp", "mp"),
            P(("mp", "dp")),
            P("mp", "dp"),
            P("dp"),
        ),
        check_vma=False,
    )
```

```python
import functools

import jax
import jax.numpy as jnp
from jax import lax
from jax.experimental import pallas as pl
from jax.experimental.pallas import tpu as pltpu
from jax.sharding import PartitionSpec as P

HEAD_DIM = 64
NORM_EPS = 1e-06
NEG_FILL = -1e30
SCORE_SCALE = HEAD_DIM ** (-0.5)
MAX_CLIP = 256
LANES = 128
F32 = jnp.float32
BF16 = jnp.bfloat16
MIB = 1 << 20
SMALL = pl.CostEstimate(flops=1 << 20, bytes_accessed=1 << 20, transcendentals=0)


def nn(left, right):
    return lax.dot_general(left, right, (((1,), (0,)), ((), ())), preferred_element_type=F32)


def nt(left, right):
    return lax.dot_general(left, right, (((1,), (1,)), ((), ())), preferred_element_type=F32)


def vmem():
    return pl.BlockSpec(memory_space=pltpu.VMEM)


def hbm():
    return pl.BlockSpec(memory_space=pltpu.HBM)


def anywhere():
    return pl.BlockSpec(memory_space=pl.ANY)


def smem():
    return pl.BlockSpec(memory_space=pltpu.SMEM)


def params(mib):
    return pltpu.CompilerParams(vmem_limit_bytes=mib * MIB)


def shape(dims, dtype):
    return jax.ShapeDtypeStruct(dims, dtype)


def row_stats(vector):
    mean = jnp.mean(vector, axis=-1, keepdims=True)
    centred = vector - mean
    spread = jnp.mean(centred * centred, axis=-1, keepdims=True)
    return centred, lax.rsqrt(spread + NORM_EPS)


def on_lanes(column):
    return jnp.broadcast_to(column, (column.shape[0], LANES))


def wide_rsqrt(inv, here, width):
    return jnp.concatenate([inv[here, :]] * (width // LANES), axis=1)


def row_sum(block):
    return jnp.sum(block, axis=0, keepdims=True)


def fold_rows(block):
    rows, width = block.shape
    return jnp.sum(block.reshape(rows // 8, 8, width), axis=0)


def pick_kernel(index, source, *refs):
    picked = refs[-1]

    def move(i, carry):
        picked[i] = source[index[i]]
        return carry

    lax.fori_loop(0, picked.shape[0], move, 0, unroll=4)


def pick(source, index, *after):
    dims = index.shape + source.shape[1:]
    return pl.pallas_call(
        pick_kernel,
        out_shape=shape(dims, source.dtype),
        in_specs=[smem(), vmem()] + [hbm()] * len(after),
        out_specs=vmem(),
        compiler_params=params(16),
        cost_estimate=SMALL,
        name="pick",
    )(index, source, *after)


def move(source, target, sem):
    return pltpu.make_async_copy(source, target, sem)


PARTS = 4


def part_moves(pairs, sems):
    moves = []
    for c in range(PARTS):
        row = []
        for n, (source, target) in enumerate(pairs):
            count = source.shape[0] // PARTS
            here = pl.ds(c * count, count)
            row.append(move(source.at[here, :], target.at[here, :], sems.at[n, c]))
        moves.append(row)
    return moves


def start_all(moves):
    for one in moves:
        one.start()


def wait_all(moves):
    for one in moves:
        one.wait()


def interleave(*streams):
    order = sorted(
        ((n + 0.5) / len(stream), which, n)
        for which, stream in enumerate(streams)
        for n in range(len(stream))
    )
    for _, which, n in order:
        streams[which][n]()


def spread_clips(seg_row, seg_b):
    for i in range(seg_b.shape[0] // LANES):
        here = pl.ds(i * LANES, LANES)
        seg_b[here, :] = jnp.broadcast_to(seg_row[:, here], (LANES, LANES)).T


def key_window(j, rows):
    window = min(rows, LANES + 2 * MAX_CLIP)
    here = pl.ds(pl.multiple_of(j * LANES, LANES), LANES)
    first = pl.multiple_of(jnp.clip(j * LANES - MAX_CLIP, 0, rows - window), LANES)
    return here, pl.ds(first, window)


def set_bias(bias, seg_b, seg_row, here, keys):
    filled = jnp.where(seg_b[keys, :] == seg_row[:, here], 0.0, NEG_FILL)
    bias[:, pl.ds(0, LANES)] = filled
    bias[:, pl.ds(LANES, LANES)] = filled


def two_heads(block):
    lane = lax.broadcasted_iota(jnp.int32, block.shape, 1)
    return jnp.concatenate(
        [block * (lane // HEAD_DIM == e).astype(BF16) for e in range(2)], axis=0
    )


def attention_kernel(
    blend, flags, seg_row, vecs, biases, tok, own, oth, w3, wp, *refs
):
    mixed, n1, normed, inv, q, k, v, att, part, lse = refs[-32:-22]
    (
        tok_v, own_v, oth_v, w3_v, wp_v, mixed_v, n1_v, q_v, k_v, v_v, att_v, part_v,
        vt, att_t, seg_b, bias, ones, normed_v, inv_v, in_sems, half_sems, out_sems,
    ) = refs[-22:]
    rows, width = tok.shape
    local = wp.shape[0]
    half_rows = rows // 2
    ratio = blend[0]
    blk = 32
    big = 256

    loads = [
        move(source, target, in_sems.at[n])
        for n, (source, target) in enumerate([(tok, tok_v), (w3, w3_v), (wp, wp_v)])
    ]
    halves = part_moves([(own, own_v), (oth, oth_v)], half_sems)
    loads[0].start()
    for part_of in halves:
        start_all(part_of)
    start_all(loads[1:])
    early = [
        move(source, target, out_sems.at[n])
        for n, (source, target) in enumerate(
            [
                (mixed_v, mixed), (n1_v, n1), (normed_v, normed), (inv_v, inv),
                (q_v, q), (k_v, k), (v_v, v),
            ]
        )
    ]
    ones[...] = jnp.ones_like(ones)
    spread_clips(seg_row, seg_b)

    loads[0].wait()
    steps = half_rows // PARTS // blk
    for n, src, half in ((0, own_v, flags[0]), (1, oth_v, 1 - flags[0])):
        for c in range(PARTS):
            halves[c][n].wait()

            def mix(i, carry, src=src, half=half, c=c):
                low = (c * steps + i) * blk
                here = pl.ds(pl.multiple_of(half * half_rows + low, blk), blk)
                there = pl.ds(pl.multiple_of(low, blk), blk)
                mine, other = tok_v[here, :].astype(F32), src[there, :].astype(F32)
                blended = ratio * mine + (1.0 - ratio) * other
                mixed_v[here, :] = blended
                centred, scale = row_stats(blended)
                inv_v[here, :] = on_lanes(scale)
                plain = centred * scale
                normed_v[here, :] = plain.astype(BF16)
                n1_v[here, :] = (plain * vecs[0:1, :] + vecs[1:2, :]).astype(BF16)
                return carry

            lax.fori_loop(0, steps, mix, 0, unroll=True)
    start_all(early[:4])

    loads[1].wait()
    for i in range(rows // big):
        here = pl.ds(i * big, big)
        rows_in = n1_v[here, :]
        queries = (nn(rows_in, w3_v[0]) + biases[0:1, :local]).astype(BF16).astype(F32)
        q_v[here, :] = (queries * SCORE_SCALE).astype(BF16)
        k_v[here, :] = nn(rows_in, w3_v[1]).astype(BF16)
        values = (nn(rows_in, w3_v[2]) + biases[0:1, local:]).astype(BF16)
        v_v[here, :] = values
        vt[:, here] = values.T
    start_all(early[4:])

    def attend(j, carry):
        here, keys = key_window(j, rows)
        set_bias(bias, seg_b, seg_row, here, keys)
        for p in range(local // LANES):
            pair = pl.ds(p * LANES, LANES)
            scores = nt(k_v[keys, pair], two_heads(q_v[here, pair])) + bias[...]
            top = jnp.max(scores, axis=0, keepdims=True)
            grown = jnp.exp(scores - top).astype(BF16)
            total = nn(ones[...], grown)[:1]
            out = (nn(vt[pair, keys], grown) / total).astype(BF16)
            logs = top + jnp.log(total)
            for e in range(2):
                lanes = slice(e * LANES, e * LANES + LANES)
                head = slice(e * HEAD_DIM, e * HEAD_DIM + HEAD_DIM)
                att_t[pl.ds(p * LANES + e * HEAD_DIM, HEAD_DIM), here] = out[head, lanes]
                lse[pl.ds(2 * p + e, 1), here] = logs[:, lanes]
        return carry

    lax.fori_loop(0, rows // LANES, attend, 0)

    loads[2].wait()
    last = []
    for i in range(rows // big):
        here = pl.ds(i * big, big)
        block = att_t[:, here].T
        att_v[here, :] = block
        part_v[here, :] = nn(block, wp_v[...]).astype(BF16)
        last.append(move(part_v.at[here, :], part.at[here, :], out_sems.at[8 + i]))
        last[-1].start()
    last.append(move(att_v, att, out_sems.at[7]))
    last[-1].start()
    wait_all(early + last)


def attention(blend, flags, segment, vecs, biases, tok, own, oth, w3, wp, *before):
    rows, width = tok.shape
    local = wp.shape[0]
    window = min(rows, LANES + 2 * MAX_CLIP)
    thin = shape((rows, local), BF16)
    tall = shape((rows, width), BF16)
    return pl.pallas_call(
        attention_kernel,
        out_shape=(
            shape((rows, width), F32), tall, tall, shape((rows, LANES), F32),
            thin, thin, thin, thin, tall, shape((local // HEAD_DIM, rows), F32),
        ),
        in_specs=[smem(), smem()] + [vmem()] * 3 + [anywhere()] * 3 + [hbm()] * (2 + len(before)),
        out_specs=[hbm()] * 9 + [vmem()],
        scratch_shapes=[
            pltpu.VMEM((rows, width), BF16),
            pltpu.VMEM((rows // 2, width), BF16),
            pltpu.VMEM((rows // 2, width), BF16),
            pltpu.VMEM(w3.shape, BF16),
            pltpu.VMEM(wp.shape, BF16),
            pltpu.VMEM((rows, width), F32),
            pltpu.VMEM((rows, width), BF16),
            pltpu.VMEM((rows, local), BF16),
            pltpu.VMEM((rows, local), BF16),
            pltpu.VMEM((rows, local), BF16),
            pltpu.VMEM((rows, local), BF16),
            pltpu.VMEM((rows, width), BF16),
            pltpu.VMEM((local, rows), BF16),
            pltpu.VMEM((local, rows), BF16),
            pltpu.VMEM((rows, LANES), F32),
            pltpu.VMEM((window, 2 * LANES), F32),
            pltpu.VMEM((16, window), BF16),
            pltpu.VMEM((rows, width), BF16),
            pltpu.VMEM((rows, LANES), F32),
            pltpu.SemaphoreType.DMA((3,)),
            pltpu.SemaphoreType.DMA((2, PARTS)),
            pltpu.SemaphoreType.DMA((8 + rows // 256,)),
        ],
        compiler_params=params(60),
        cost_estimate=SMALL,
        name="attention",
    )(
        blend, flags, segment, vecs, biases, tok, own, oth, w3, wp, *before,
    )


ERFC_SLOPE = 0.47
ERFC_COEFFS = (
    0.2663094668265691,
    0.2480096137831850,
    0.3362712657560771,
    -0.1262288063821733,
    0.6076790117752645,
    -0.4204702410368928,
    0.0884296765518492,
)


def gelu_parts(pre):
    bell = jnp.exp(pre * pre * -0.5)
    t = 1.0 / (1.0 + jnp.abs(pre) * (ERFC_SLOPE * 0.5**0.5))
    poly = 0.5 * ERFC_COEFFS[-1]
    for coeff in ERFC_COEFFS[-2::-1]:
        poly = poly * t + 0.5 * coeff
    tail = poly * t * bell
    cdf = jnp.where(pre >= 0, 1.0 - tail, tail)
    return pre * cdf, cdf + pre * bell * 0.3989422804014327


def turn_into(target, source, blocks):
    rows = source.shape[0]
    big = 256
    for i in range(rows // big):
        here = pl.ds(i * big, big)
        turned = source[here, :].T
        for start, place, count in blocks:
            target[pl.ds(place, count), here] = turned[start : start + count]


def lead_blocks(width, lead_rows):
    runs = width // lead_rows
    return [
        (run * lead_rows, ((run % 2) * (runs // 2) + run // 2) * lead_rows, lead_rows)
        for run in range(runs)
    ]


def feed_kernel(
    in_rows, out_rows, flags, vecs, biases, mixed, p_own, p_oth, cot, cot_t,
    w_in, w_out, w_out_one, w_out_two,
    hidden, part, gn_part, in_keep, in_send, out_keep, out_send, normed, inv, g_bin, g_bout,
    mixed_v, own_v, oth_v, cot_v, cot_tv, w_in_v, w_out_v, n2, n2_t, act, gp,
    g_in, g_out, normed_v, inv_v, in_sems, turn_sems, weight_sems, out_sems, grad_sems,
):
    rows, width = mixed.shape
    units = w_in.shape[1]
    blk = 32
    big = 256
    sub = 16
    home = flags[1] == 1
    across = flags[2]
    kept_out = jnp.where(home, flags[0], 1 - flags[0]) if in_rows != out_rows else across
    sides = (across, kept_out)

    loads = part_moves(
        [(mixed, mixed_v), (p_own, own_v), (p_oth, oth_v), (cot, cot_v)], in_sems
    )
    for part_of in loads:
        start_all(part_of)

    weights = [move(w_in, w_in_v, weight_sems.at[0])]
    weights[0].start()
    half = w_out.shape[0] // 2
    for n, (got, place) in enumerate([(w_out_one, across), (w_out_two, 1 - across)]):
        spot = pl.ds(pl.multiple_of(place * half, half), half)
        sem = weight_sems.at[1 + n]
        weights.append(move(w_out.at[spot, :], w_out_v.at[spot, :], sem))

        @pl.when(home)
        def _(spot=spot, sem=sem):
            move(w_out.at[spot, :], w_out_v.at[spot, :], sem).start()

        @pl.when(jnp.logical_not(home))
        def _(got=got, spot=spot, sem=sem):
            move(got, w_out_v.at[spot, :], sem).start()

    turns = [
        move(cot_t.at[pl.ds(start, count), :], cot_tv.at[pl.ds(place, count), :], turn_sems.at[n])
        for n, (start, place, count) in enumerate(lead_blocks(width, out_rows))
    ]
    start_all(turns)

    g_bout[...] = jnp.zeros_like(g_bout)
    steps = rows // PARTS // blk
    for c in range(PARTS):
        wait_all(loads[c])

        def norm(i, carry, c=c):
            here = pl.ds(pl.multiple_of((c * steps + i) * blk, blk), blk)
            attn = own_v[here, :].astype(F32) + oth_v[here, :].astype(F32)
            total = mixed_v[here, :] + attn + vecs[4:5, :]
            mixed_v[here, :] = total
            centred, scale = row_stats(total)
            inv_v[here, :] = on_lanes(scale)
            plain = centred * scale
            normed_v[here, :] = plain.astype(BF16)
            n2[here, :] = (plain * vecs[2:3, :] + vecs[3:4, :]).astype(BF16)
            g_bout[...] += fold_rows(cot_v[here, :].astype(F32))
            return carry

        lax.fori_loop(0, steps, norm, 0, unroll=4)
    stores = [
        move(source, target, out_sems.at[0, n])
        for n, (source, target) in enumerate(
            [(mixed_v, hidden), (normed_v, normed), (inv_v, inv)]
        )
    ]
    start_all(stores)
    turn_into(n2_t, n2, lead_blocks(width, in_rows))
    wait_all(weights)

    g_bin[...] = jnp.zeros_like(g_bin)

    def row_block(i, carry):
        here = pl.ds(pl.multiple_of(i * big, big), big)
        for j in range(units // width):
            cols = pl.ds(j * width, width)
            pre_all = nn(n2[here, :], w_in_v[:, cols])
            grad_all = nt(cot_v[here, :], w_out_v[cols, :])
            sums = jnp.zeros((8, width), F32)
            for s in range(big // sub):
                rng = slice(s * sub, s * sub + sub)
                value, slope = gelu_parts(pre_all[rng] + biases[1 + j : 2 + j, :])
                grad = grad_all[rng] * slope
                sums += fold_rows(grad)
                spot = pl.ds(pl.multiple_of(i * big + s * sub, sub), sub)
                act[spot, cols] = value.astype(BF16)
                gp[spot, cols] = grad.astype(BF16)
            g_bin[:, cols] += sums
        oth_v[here, :] = nt(gp[here, :], w_in_v[...]).astype(BF16)
        own_v[here, :] = nn(act[here, :], w_out_v[...]).astype(BF16)
        for n, (source, target) in enumerate([(oth_v, gn_part), (own_v, part)]):
            move(source.at[here, :], target.at[here, :], out_sems.at[1 + n, i]).start()
        return carry

    lax.fori_loop(0, rows // big, row_block, 0)
    for i in range(rows // big):
        here = pl.ds(i * big, big)
        for n, (source, target) in enumerate([(oth_v, gn_part), (own_v, part)]):
            stores.append(move(source.at[here, :], target.at[here, :], out_sems.at[1 + n, i]))

    wait_all(turns)
    half = width // 2
    for n, (turned, right, buf, keep, send) in enumerate(
        [(n2_t, gp, g_in, in_keep, in_send), (cot_tv, act, g_out, out_keep, out_send)]
    ):
        for side in range(2):
            lines = pl.ds(side * half, half)
            for j in range(units // width):
                cols = pl.ds(j * width, width)
                buf[side, :, cols] = nn(turned[lines, :], right[:, cols]).astype(BF16)
        for m, (side, target) in enumerate([(1 - sides[n], send), (sides[n], keep)]):
            stores.append(move(buf.at[side], target, grad_sems.at[n, m]))
            stores[-1].start()
    wait_all(stores)


def feed(
    in_rows, out_rows, flags, vecs, biases, mixed, p_own, p_oth, cot, cot_t,
    w_in, w_out, w_out_one, w_out_two,
):
    rows, width = mixed.shape
    units = w_in.shape[1]
    tall = shape((rows, width), BF16)
    grad = shape((width // 2, units), BF16)
    return pl.pallas_call(
        functools.partial(feed_kernel, in_rows, out_rows),
        out_shape=(
            shape((rows, width), F32), tall, tall, grad, grad, grad, grad,
            tall, shape((rows, LANES), F32), shape((8, units), F32), shape((8, width), F32),
        ),
        in_specs=[smem()] + [vmem()] * 2 + [hbm()] * 2 + [anywhere()] + [hbm()] * 6,
        out_specs=[hbm()] * 9 + [vmem()] * 2,
        scratch_shapes=[
            pltpu.VMEM((rows, width), F32),
            pltpu.VMEM((rows, width), BF16),
            pltpu.VMEM((rows, width), BF16),
            pltpu.VMEM((rows, width), BF16),
            pltpu.VMEM((width, rows), BF16),
            pltpu.VMEM(w_in.shape, BF16),
            pltpu.VMEM(w_out.shape, BF16),
            pltpu.VMEM((rows, width), BF16),
            pltpu.VMEM((width, rows), BF16),
            pltpu.VMEM((rows, units), BF16),
            pltpu.VMEM((rows, units), BF16),
            pltpu.VMEM((2, width // 2, units), BF16),
            pltpu.VMEM((2, width // 2, units), BF16),
            pltpu.VMEM((rows, width), BF16),
            pltpu.VMEM((rows, LANES), F32),
            pltpu.SemaphoreType.DMA((4, PARTS)),
            pltpu.SemaphoreType.DMA((width // out_rows,)),
            pltpu.SemaphoreType.DMA((3,)),
            pltpu.SemaphoreType.DMA((3, rows // 256)),
            pltpu.SemaphoreType.DMA((2, 2)),
        ],
        compiler_params=params(60),
        cost_estimate=SMALL,
        name="feed",
    )(
        flags, vecs, biases, mixed, p_own, p_oth, cot, cot_t,
        w_in, w_out, w_out_one, w_out_two,
    )


def attention_back_kernel(
    lead_rows, part_rows, flags, vecs, seg_row, lse, g_bin, g_bout, g_own, g_oth, cot, normed, inv,
    wp, att, k, q, v, w3, n1, normed_one,
    gh, part, keep, send, short,
    gh_v, own_v, oth_v, cot_v, normed_v, inv_v, wp_v, att_v, k_v, q_v, v_v, w3_v, n1_v, one_v, low_v, part_v,
    sums, tails, d_out, kt, dq_t, dk, dv, delta, seg_b, bias, raw, raw_g, low_p, low_g, n1_t, gh_t, grad_v, out,
    in_sems, row_sems, out_sems, last_sems,
):
    rows, width = cot.shape
    local = wp.shape[0]
    blk = 32
    big = 256
    blocks = lead_blocks(width, lead_rows)
    kept_side = flags[2]
    row_loads = part_moves(
        [(g_own, own_v), (g_oth, oth_v), (cot, cot_v), (normed, normed_v), (inv, inv_v)],
        row_sems,
    )
    for part_of in row_loads:
        start_all(part_of)
    loads = [
        move(source, target, in_sems.at[n])
        for n, (source, target) in enumerate(
            [
                (wp, wp_v), (att, att_v), (k, k_v), (q, q_v), (v, v_v), (w3, w3_v), (n1, n1_v),
                (normed_one, one_v),
            ]
        )
    ]
    start_all(loads)
    sums[...] = jnp.zeros_like(sums)
    dk[...] = jnp.zeros_like(dk)
    dv[...] = jnp.zeros_like(dv)
    spread_clips(seg_row, seg_b)

    steps = rows // PARTS // blk
    for c in range(PARTS):
        wait_all(row_loads[c])

        def norm(i, carry, c=c):
            here = pl.ds(pl.multiple_of((c * steps + i) * blk, blk), blk)
            grad = own_v[here, :].astype(F32) + oth_v[here, :].astype(F32)
            plain = normed_v[here, :].astype(F32)
            scaled = grad * vecs[2:3, :]
            mean_one = jnp.mean(scaled, axis=-1, keepdims=True)
            mean_two = jnp.mean(scaled * plain, axis=-1, keepdims=True)
            scale = wide_rsqrt(inv_v, here, width)
            back = cot_v[here, :].astype(F32) + scale * (scaled - mean_one - plain * mean_two)
            gh_v[here, :] = back
            low_v[here, :] = back.astype(BF16)
            sums[0] += fold_rows(grad * plain)
            sums[1] += fold_rows(grad)
            sums[2] += fold_rows(back)
            return carry

        lax.fori_loop(0, steps, norm, 0, unroll=2)
    stores = [move(gh_v, gh, out_sems.at[0])]
    stores[0].start()

    wait_all(loads[:3])
    heads = local // HEAD_DIM
    lane = lax.broadcasted_iota(jnp.int32, (delta.shape[0], local), 1)
    row = lax.broadcasted_iota(jnp.int32, (delta.shape[0], local), 0)
    of_head = (lane // HEAD_DIM == row).astype(BF16)

    def project(i, carry):
        here = pl.ds(pl.multiple_of(i * big, big), big)
        grad_out = nt(low_v[here, :], wp_v[...]).astype(BF16)
        d_out[here, :] = grad_out
        product = grad_out.astype(F32) * att_v[here, :].astype(F32)
        coarse = product.astype(BF16)
        fine = (product - coarse.astype(F32)).astype(BF16)
        delta[:, here] = nt(of_head, coarse) + nt(of_head, fine)
        kt[:, here] = k_v[here, :].T
        return carry

    lax.fori_loop(0, rows // big, project, 0)
    wait_all(loads[3:])

    pairs = heads // 2
    window = bias.shape[0]
    strip = 128
    strips = window // strip

    def attend(j, carry):
        here, keys = key_window(j, rows)
        first = pl.multiple_of(keys.start, LANES)
        set_bias(bias, seg_b, seg_row, here, keys)
        blocks_two = {}

        def two(p):
            if p not in blocks_two:
                pair = pl.ds(p * LANES, LANES)
                blocks_two[p] = (two_heads(q_v[here, pair]), two_heads(d_out[here, pair]))
            return blocks_two[p]

        def at_strip(n):
            return (
                pl.ds(pl.multiple_of(first + n * strip, strip), strip),
                pl.ds(n * strip, strip),
            )

        def products(p):
            pair = pl.ds(p * LANES, LANES)

            def scores(n):
                def run():
                    some, at = at_strip(n)
                    raw[p % 2, at, :] = nt(k_v[some, pair], two(p)[0])

                return run

            def grads(n):
                def run():
                    some, at = at_strip(n)
                    raw_g[p % 2, at, :] = nt(v_v[some, pair], two(p)[1])

                return run

            return [make(n) for n in range(strips) for make in (scores, grads)]

        def softmax_back(p):
            tops = jnp.concatenate([lse[pl.ds(2 * p + e, 1), here] for e in range(2)], axis=1)
            inner = jnp.concatenate([delta[pl.ds(2 * p + e, 1), here] for e in range(2)], axis=1)
            half = strip // 2

            def run_at(n):
                def run():
                    at = pl.ds(n * half, half)
                    probs = jnp.exp(raw[p % 2, at, :] + bias[at, :] - tops)
                    low_p[p % 2, at, :] = probs.astype(BF16)
                    low_g[p % 2, at, :] = (probs * (raw_g[p % 2, at, :] - inner)).astype(BF16)

                return run

            return [run_at(n) for n in range(2 * strips)]

        def sums_of(p):
            pair = pl.ds(p * LANES, LANES)

            def keys_of(n):
                def run():
                    some, at = at_strip(n)
                    dk[some, pair] += nn(low_g[p % 2, at, :], two(p)[0])

                return run

            def values_of(n):
                def run():
                    some, at = at_strip(n)
                    dv[some, pair] += nn(low_p[p % 2, at, :], two(p)[1])

                return run

            def queries():
                grad_q = nn(kt[pair, keys], low_g[p % 2]) * SCORE_SCALE
                for e in range(2):
                    lanes = slice(e * LANES, e * LANES + LANES)
                    head = slice(e * HEAD_DIM, e * HEAD_DIM + HEAD_DIM)
                    dq_t[pl.ds(p * LANES + e * HEAD_DIM, HEAD_DIM), here] = grad_q[head, lanes]

            return [make(n) for n in range(strips) for make in (keys_of, values_of)] + [queries]

        def turns():
            for target, source in ((n1_t, n1_v), (gh_t, low_v)):
                turned = source[here, :].T
                for start, place, count in blocks:
                    target[pl.ds(place, count), here] = turned[start : start + count]

        interleave(products(0), [turns])
        for p in range(pairs):
            matrix = (products(p + 1) if p + 1 < pairs else []) + (sums_of(p - 1) if p else [])
            interleave(softmax_back(p), matrix)
        interleave(sums_of(pairs - 1))
        return carry

    lax.fori_loop(0, rows // LANES, attend, 0)

    tails[...] = jnp.zeros_like(tails)

    def finish(i, carry):
        here = pl.ds(pl.multiple_of(i * big, big), big)
        grad_q, grad_k, grad_val = dq_t[:, here].T, dk[here, :], dv[here, :]
        tails[2, :, pl.ds(0, local)] += fold_rows(grad_q)
        tails[2, :, pl.ds(local, local)] += fold_rows(grad_val)
        lows = [grad.astype(BF16) for grad in (grad_q, grad_k, grad_val)]
        total = sum(nt(low, w3_v[n]) for n, low in enumerate(lows))
        part_v[here, :] = total.astype(BF16)
        tails[0] += fold_rows(total * one_v[here, :].astype(F32))
        tails[1] += fold_rows(total)
        for n, low in enumerate(lows):
            grad_v[here, pl.ds(n * local, local)] = low
        move(part_v.at[here, :], part.at[here, :], last_sems.at[i]).start()
        return carry

    lax.fori_loop(0, rows // big, finish, 0)
    for i in range(rows // big):
        here = pl.ds(i * big, big)
        stores.append(move(part_v.at[here, :], part.at[here, :], last_sems.at[i]))
    units = g_bin.shape[1]
    listed = [tails[0], tails[1], sums[0], sums[1], sums[2], g_bout[...], tails[2]]
    listed += [g_bin[:, pl.ds(n, width)] for n in range(0, units, width)]
    half = width // 2
    listed = [row_sum(block) for block in listed]
    for n, block in enumerate(listed):
        short[pl.ds(n, 1), :] = block
    if part_rows:
        sources = [
            (jnp.concatenate(listed[:6] + [jnp.zeros((2, width), F32)], axis=0), part_rows),
            (jnp.broadcast_to(listed[6][:, :local], (8, local)), local * part_rows // width),
            (jnp.broadcast_to(listed[6][:, local:], (8, local)), local * part_rows // width),
            (
                jnp.broadcast_to(jnp.concatenate(listed[7:], axis=1), (8, units)),
                units * part_rows // width,
            ),
        ]
        rest = jnp.zeros((part_rows - 8 * len(sources), LANES), F32)
        for start, place, count in blocks:
            for row in range(0, count, part_rows):
                d = (start + row) // part_rows
                parts = [
                    pltpu.roll(source, (source.shape[1] - d * size) % source.shape[1], 1)[:, :LANES]
                    for source, size in sources
                ]
                side, at = divmod(place + row, half)
                out[side, pl.ds(at, part_rows), pl.ds(4 * local, LANES)] = jnp.concatenate(
                    parts + [rest], axis=0
                ).astype(BF16)
    for side in range(2):
        lines = pl.ds(side * half, half)
        for n in range(3):
            cols = pl.ds(n * local, local)
            out[side, :, cols] = nn(n1_t[lines, :], grad_v[:, cols]).astype(BF16)
        out[side, :, pl.ds(3 * local, local)] = nn(gh_t[lines, :], att_v[...]).astype(BF16)
    for n, (side, target) in enumerate([(1 - kept_side, send), (kept_side, keep)]):
        stores.append(move(out.at[side], target, out_sems.at[1 + n]))
        stores[-1].start()
    wait_all(stores)


def attention_back(
    lead_rows, part_rows, flags, vecs, segment, lse, g_bin, g_bout, g_own, g_oth, cot, normed, inv,
    wp, att, k, q, v, w3, n1, normed_one,
):
    rows, width = cot.shape
    local = wp.shape[0]
    window = min(rows, LANES + 2 * MAX_CLIP)
    tall, thin = pltpu.VMEM((rows, width), BF16), pltpu.VMEM((rows, local), BF16)
    turned = pltpu.VMEM((width, rows), BF16)
    half = (width // 2, 4 * local + (LANES if part_rows else 0))
    return pl.pallas_call(
        functools.partial(attention_back_kernel, lead_rows, part_rows),
        out_shape=(
            shape((rows, width), F32),
            shape((rows, width), BF16),
            shape(half, BF16),
            shape(half, BF16),
            shape((7 + g_bin.shape[1] // width, width), F32),
        ),
        in_specs=[smem()] + [vmem()] * 5 + [hbm()] + [anywhere()] + [hbm()] * 11,
        out_specs=[hbm()] * 4 + [vmem()],
        scratch_shapes=[
            pltpu.VMEM((rows, width), F32),
            tall, tall, tall, tall,
            pltpu.VMEM((rows, LANES), F32),
            pltpu.VMEM(wp.shape, BF16),
            thin, thin, thin, thin,
            pltpu.VMEM(w3.shape, BF16),
            tall, tall, tall, tall,
            pltpu.VMEM((3, 8, width), F32),
            pltpu.VMEM((3, 8, width), F32),
            thin,
            pltpu.VMEM((local, rows), BF16),
            pltpu.VMEM((local, rows), F32),
            pltpu.VMEM((rows, local), F32),
            pltpu.VMEM((rows, local), F32),
            pltpu.VMEM((8, rows), F32),
            pltpu.VMEM((rows, LANES), F32),
            pltpu.VMEM((window, 2 * LANES), F32),
            pltpu.VMEM((2, window, 2 * LANES), F32),
            pltpu.VMEM((2, window, 2 * LANES), F32),
            pltpu.VMEM((2, window, 2 * LANES), BF16),
            pltpu.VMEM((2, window, 2 * LANES), BF16),
            turned, turned,
            pltpu.VMEM((rows, 3 * local), BF16),
            pltpu.VMEM((2,) + half, BF16),
            pltpu.SemaphoreType.DMA((8,)),
            pltpu.SemaphoreType.DMA((5, PARTS)),
            pltpu.SemaphoreType.DMA((3,)),
            pltpu.SemaphoreType.DMA((rows // 256,)),
        ],
        compiler_params=params(60),
        cost_estimate=SMALL,
        name="attention_back",
    )(
        flags, vecs, segment, lse, g_bin, g_bout, g_own, g_oth, cot, normed, inv,
        wp, att, k, q, v, w3, n1, normed_one,
    )


def mixed_back_kernel(blend, vecs, gh, g_own, g_oth, normed, inv, outgoing, kept, *refs):
    gh_v, own_v, oth_v, normed_v, inv_v, leave_v, kept_v, in_sems, out_sems = refs
    ratio = blend[0]
    rows, width = gh.shape
    blk = 32
    loads = part_moves(
        [(gh, gh_v), (g_own, own_v), (g_oth, oth_v), (normed, normed_v), (inv, inv_v)], in_sems
    )
    stores = part_moves([(leave_v, outgoing), (kept_v, kept)], out_sems)
    for part_of in loads:
        start_all(part_of)
    steps = rows // PARTS // blk
    for c in range(PARTS):
        wait_all(loads[c])

        def norm(i, carry, c=c):
            here = pl.ds(pl.multiple_of((c * steps + i) * blk, blk), blk)
            grad = own_v[here, :].astype(F32) + oth_v[here, :].astype(F32)
            plain = normed_v[here, :].astype(F32)
            scaled = grad * vecs[0:1, :]
            mean_one = jnp.mean(scaled, axis=-1, keepdims=True)
            mean_two = jnp.mean(scaled * plain, axis=-1, keepdims=True)
            scale = wide_rsqrt(inv_v, here, width)
            back = gh_v[here, :] + scale * (scaled - mean_one - plain * mean_two)
            leave_v[here, :] = ((1.0 - ratio) * back).astype(BF16)
            kept_v[here, :] = (ratio * back).astype(BF16)
            return carry

        lax.fori_loop(0, steps, norm, 0, unroll=4)
        start_all(stores[c])
    for part_of in stores:
        wait_all(part_of)


def mixed_back(blend, vecs, gh, g_own, g_oth, normed, inv):
    rows, width = gh.shape
    tall = pltpu.VMEM((rows, width), BF16)
    return pl.pallas_call(
        mixed_back_kernel,
        out_shape=(shape((rows, width), BF16), shape((rows, width), BF16)),
        in_specs=[smem(), vmem()] + [hbm()] * 2 + [anywhere()] + [hbm()] * 2,
        out_specs=[hbm(), hbm()],
        scratch_shapes=[
            pltpu.VMEM((rows, width), F32),
            tall, tall, tall, pltpu.VMEM((rows, LANES), F32), tall, tall,
            pltpu.SemaphoreType.DMA((5, PARTS)),
            pltpu.SemaphoreType.DMA((2, PARTS)),
        ],
        compiler_params=params(60),
        cost_estimate=SMALL,
        name="mixed_back",
    )(blend, vecs, gh, g_own, g_oth, normed, inv)


def shards(
    tokens,
    mix_blend,
    partner,
    clip_ids,
    gain_one,
    shift_one,
    qkv_weight,
    qv_bias,
    proj_weight,
    proj_bias,
    gain_two,
    shift_two,
    in_weight,
    in_bias,
    out_weight,
    out_bias,
    cotangent,
):
    rows, width = tokens.shape
    dp_count = lax.axis_size("dp")
    both = ("dp", "mp")
    bits = dp_count.bit_length() - 1
    seq = lax.axis_index("dp")
    mp = lax.axis_index("mp")
    core = lax.rem(seq, 2)
    home = core == mp
    all_dp = range(dp_count)

    def joint(d, m):
        return 2 * d + m

    core_swap = [(d, d ^ 1) for d in all_dp]
    home_to_pair = [(joint(d, d & 1), joint(d, 1 - (d & 1))) for d in all_dp]
    pair_to_home = [(joint(d, 1 - (d & 1)), joint(d, d & 1)) for d in all_dp]
    weight_move = home_to_pair + [
        (joint(d, 1 - (d & 1)), joint(d ^ 1, 1 - (d & 1))) for d in all_dp
    ]

    def swap(value):
        return lax.ppermute(value, "dp", core_swap)

    def chip_value(value):
        return jnp.where(home, value, swap(value))

    def after(value, *others):
        return lax.optimization_barrier((value,) + others)[0]

    def half_weight(value):
        return lax.ppermute(value, both, weight_move)

    part_rows = width // dp_count
    lead = min(n for n in range(1, bits) if (part_rows << n) % 16 == 0)
    lead_rows = part_rows << lead
    across = lax.rem(seq >> lead, 2)
    flags = jnp.stack([core, home.astype(jnp.int32), across]).astype(jnp.int32)

    def taken(value, index, axis):
        return lax.dynamic_index_in_dim(value, index, axis, keepdims=False)

    seq_small = chip_value(jnp.concatenate([mix_blend, clip_ids[0].astype(F32)]))
    blend, segment = seq_small[:1], seq_small[1:].reshape(1, rows)
    local = proj_weight.shape[0]
    units = in_bias.shape[0]
    half_small = jnp.concatenate([qv_bias.reshape(-1), in_bias])
    half_small = jnp.where(home, half_small, half_weight(half_small))
    biases = half_small.reshape(-1, width)
    vecs = jnp.stack([gain_one, shift_one, gain_two, shift_two, proj_bias])

    w3 = half_weight(qkv_weight.transpose(1, 0, 2))
    wp = half_weight(proj_weight)

    def two_way(value):
        halves = value.reshape(2, value.shape[0] // 2, value.shape[1])
        one = half_weight(taken(halves, across, 0))
        moves = [(joint(d, 1 - (d & 1)), joint(d ^ (1 << lead), 1 - (d & 1))) for d in all_dp]
        return value, one, lax.ppermute(one, both, moves)

    ids = jnp.arange(2 * dp_count, dtype=jnp.int32)
    piece = rows // (2 * 2 * dp_count)
    sent = tokens.reshape(2, dp_count, 2, piece, width)
    sent = lax.dynamic_index_in_dim(sent, mp, 2, keepdims=False)
    spread = lax.all_to_all(sent.transpose(1, 0, 2, 3), "dp", 0, 0, tiled=True)
    wanted = partner[(ids // 4) * 2 + ids % 2] * 2 + (ids // 2) % 2
    source_of = jnp.sum(
        jnp.where(partner[:, None] == ids[None, :dp_count], ids[:dp_count, None], 0),
        axis=0,
        dtype=jnp.int32,
    )
    source = source_of[ids // 2]
    wanted_back = (source // 2) * 4 + (ids % 2) * 2 + source % 2
    chosen = pick(spread.reshape(2 * dp_count, piece, width), wanted, w3, wp, half_small)
    partner_own = lax.all_to_all(chosen, both, 0, 0, tiled=True).reshape(rows // 2, width)
    w_out = two_way(out_weight)
    w_in = half_weight(after(in_weight, w_out[1]))

    tok = chip_value(tokens)
    cot = chip_value(cotangent)
    cot_t = cot.T
    partner_oth = swap(after(partner_own, tok, cot, vecs, segment, wanted_back))

    mixed, n1, normed_one, inv_one, q, k, v, att, attn_part, lse = attention(
        blend, flags, segment, vecs, biases, tok, partner_own, partner_oth, w3, wp, w_out[2], cot_t
    )
    pair_first = part_rows % 16 == 0
    fed = feed(
        lead_rows, part_rows if pair_first else lead_rows, flags, vecs, biases,
        mixed, attn_part, swap(attn_part), cot, cot_t, w_in, *w_out,
    )
    hidden, out_part, gn2_part, in_keep, in_send, out_keep, out_send = fed[:7]
    normed_two, inv_two, g_bin, g_bout = fed[7:]
    gn2_oth = swap(gn2_part)

    high, mid = dp_count >> (lead + 1), 1 << (lead - 1)
    pair_and_core = pair_to_home + [(joint(d, d & 1), joint(d ^ 1, d & 1)) for d in all_dp]
    pair_diagonal = [(joint(d, 1 - (d & 1)), joint(d ^ 1, d & 1)) for d in all_dp]

    def total(*terms):
        return sum(term.astype(F32) for term in terms)

    def send_across(value):
        return lax.ppermute(value, "dp", [(d, d ^ (1 << lead)) for d in all_dp])

    def send_pair(value):
        value = value.reshape(high, mid, 2, part_rows, -1)
        one = lax.ppermute(taken(value, jnp.where(home, 1 - core, core), 2), both, pair_and_core)
        two = lax.ppermute(taken(value, 1 - core, 2), both, pair_diagonal)
        held = taken(value, core, 2)
        return jnp.where(home, held, jnp.zeros_like(held)), one, two

    def far(value, *others):
        for shift, left in ((1, mid), (lead + 1, high)):
            while left > 1:
                radix = min(4, left)
                left //= radix
                value = value.reshape((-1, left, radix) + value.shape[-2:]).astype(BF16)
                spot = lax.rem(seq >> shift, radix)
                got = [
                    lax.ppermute(
                        taken(value, spot ^ flip, 2),
                        "dp",
                        [(d, d ^ (flip << shift)) for d in all_dp],
                    )
                    for flip in range(1, radix)
                ]
                value = total(taken(value, spot, 2), *after(got, *others))
                shift += radix.bit_length() - 1
        return value.reshape(value.shape[-2:])

    def send_first(keep, send):
        if not pair_first:
            return [keep, send_across(send)]
        one = lax.ppermute(send, both, pair_and_core)
        two = lax.ppermute(keep, both, pair_diagonal)
        return [jnp.where(home, keep, jnp.zeros_like(keep)), one, two]

    def send_second(value):
        if not pair_first:
            return send_pair(value)
        value = value.reshape(high, 2, mid, part_rows, -1)
        return taken(value, across, 1), send_across(taken(value, 1 - across, 1))

    in_got = send_across(in_send)
    out_first = send_first(out_keep, out_send)
    gh, gn1_part, attn_keep, attn_send, short = attention_back(
        lead_rows, part_rows if pair_first else 0, flags, vecs, segment, lse, g_bin, g_bout,
        gn2_part, gn2_oth, cot, normed_two, inv_two, wp, att, k, q, v, w3, n1, normed_one,
    )
    gn1_oth = swap(after(gn1_part, in_got, *out_first))
    attn_first = [attn_keep, send_across(attn_send)]
    in_terms = send_pair(total(in_keep, in_got).astype(BF16))
    outgoing, kept = mixed_back(blend, vecs, gh, gn1_part, gn1_oth, normed_one, inv_one)

    leaving = taken(outgoing.reshape(2, 2, dp_count, piece, width), core, 1)
    leaving = leaving.transpose(1, 0, 2, 3).reshape(2 * dp_count, piece, width)
    back = lax.all_to_all(leaving, both, 0, 0, tiled=True)

    in_value = total(*after(in_terms, leaving)).astype(BF16)
    sum_in = far(in_value)
    out_oth = swap(after(out_part, leaving))
    out_value = total(*after(out_first, in_value)).astype(BF16)
    out_terms = send_second(out_value)
    block = hidden + (out_part.astype(F32) + after(out_oth, out_value).astype(F32)) + out_bias
    block = block.astype(BF16)
    kept = kept.reshape(2, rows // 2, width)
    kept_away = taken(kept, 1 - mp, 0)
    kept_got = half_weight(kept_away)
    block_got = half_weight(block)

    returning = pick(back, wanted_back, sum_in, block, kept_got)
    returned = lax.all_to_all(
        returning.reshape(dp_count, 2, piece, width), "dp", 0, 0, tiled=True
    )
    returned = after(returned, kept_got, block_got)
    kept = jnp.where(home, taken(kept, mp, 0), kept_got)
    returned = returned.transpose(1, 0, 2, 3).reshape(rows // 2, width)
    mine = (kept.astype(F32) + returned.astype(F32)).astype(BF16)
    other = lax.ppermute(mine, "mp", [(0, 1), (1, 0)])
    block_out = jnp.where(home, block, block_got)
    grad_tokens = jnp.where(
        jnp.arange(2)[:, None, None] == mp, mine[None], other[None]
    ).reshape(rows, width)

    marker = swap(returning[0, :, :LANES])
    attn_terms = send_pair(total(*after(attn_first, marker)).astype(BF16))
    sum_out = far(total(*after(out_terms, marker)), mine)
    sum_attn = after(far(total(*after(attn_terms, mine))), other)
    sum_qkv = sum_attn[:, : 3 * local].reshape(-1, 3, local)
    sum_proj = sum_attn[:, 3 * local : 4 * local].T
    quarter, eighth = local // dp_count, units // dp_count
    if pair_first:
        extra = sum_attn[:, 4 * local :]
        plain = extra[:6, :part_rows]
        ours = plain[:2] + lax.ppermute(plain[:2], "mp", [(0, 1), (1, 0)])
        plain = jnp.concatenate([ours, plain[2:]])
        sum_qv = jnp.stack([extra[8, :quarter], extra[16, :quarter]])
        sum_bin = extra[24, :eighth]
    else:
        counts = jnp.where((core == 0) | (jnp.arange(6) < 2), 1.0, 0.0).astype(F32)
        wide = (short[:6] * counts[:, None]).reshape(6, dp_count, 1, part_rows)
        wide = jnp.broadcast_to(wide, (6, dp_count, 2, part_rows)).transpose(1, 2, 0, 3)
        to_half = (jnp.arange(2) == core)[None, :, None]

        def half_terms(vectors):
            terms = vectors.reshape(vectors.shape[0], dp_count, -1).transpose(1, 0, 2)
            return jnp.where(to_half, terms.reshape(dp_count, 1, -1), 0.0)

        short = jnp.concatenate(
            [
                wide.reshape(dp_count, 2, -1),
                half_terms(short[6].reshape(2, local)),
                half_terms(short[7:].reshape(1, units)),
            ],
            axis=-1,
        ).reshape(2 * dp_count, -1)
        short = jnp.sum(lax.all_to_all(short, both, 0, 0, tiled=True), axis=0)
        plain = short[: 6 * part_rows].reshape(6, part_rows)
        sum_qv = short[6 * part_rows : 6 * part_rows + 2 * quarter].reshape(2, -1)
        sum_bin = short[6 * part_rows + 2 * quarter :]
    return (
        block_out,
        grad_tokens,
        plain[0],
        plain[1],
        sum_qkv,
        sum_qv,
        sum_proj,
        plain[4],
        plain[2],
        plain[3],
        sum_in,
        sum_bin,
        sum_out.T,
        plain[5],
    )


def solution(mesh):
    return jax.shard_map(
        shards,
        mesh=mesh,
        in_specs=(
            P("dp", None),
            P("dp"),
            P(),
            P("dp", None),
            P(),
            P(),
            P(None, None, "mp"),
            P(None, "mp"),
            P("mp", None),
            P(),
            P(),
            P(),
            P(None, "mp"),
            P("mp"),
            P("mp", None),
            P(),
            P("dp", None),
        ),
        out_specs=(
            P("dp", None),
            P("dp", None),
            P("dp"),
            P("dp"),
            P("dp", None, "mp"),
            P(None, ("mp", "dp")),
            P("mp", "dp"),
            P("dp"),
            P("dp"),
            P("dp"),
            P("dp", "mp"),
            P(("mp", "dp")),
            P("mp", "dp"),
            P("dp"),
        ),
        check_vma=False,
    )
```

```python
import functools

import jax
import jax.numpy as jnp
from jax import lax
from jax.experimental import pallas as pl
from jax.experimental.pallas import tpu as pltpu
from jax.sharding import PartitionSpec as P

HEAD_DIM = 64
NORM_EPS = 1e-06
NEG_FILL = -1e30
SCORE_SCALE = HEAD_DIM ** (-0.5)
MAX_CLIP = 256
LANES = 128
F32 = jnp.float32
BF16 = jnp.bfloat16
MIB = 1 << 20
SMALL = pl.CostEstimate(flops=1 << 20, bytes_accessed=1 << 20, transcendentals=0)


def nn(left, right):
    return lax.dot_general(left, right, (((1,), (0,)), ((), ())), preferred_element_type=F32)


def nt(left, right):
    return lax.dot_general(left, right, (((1,), (1,)), ((), ())), preferred_element_type=F32)


def vmem():
    return pl.BlockSpec(memory_space=pltpu.VMEM)


def hbm():
    return pl.BlockSpec(memory_space=pltpu.HBM)


def anywhere():
    return pl.BlockSpec(memory_space=pl.ANY)


def smem():
    return pl.BlockSpec(memory_space=pltpu.SMEM)


def params(mib):
    return pltpu.CompilerParams(vmem_limit_bytes=mib * MIB)


def shape(dims, dtype):
    return jax.ShapeDtypeStruct(dims, dtype)


def row_stats(vector):
    mean = jnp.mean(vector, axis=-1, keepdims=True)
    centred = vector - mean
    spread = jnp.mean(centred * centred, axis=-1, keepdims=True)
    return centred, lax.rsqrt(spread + NORM_EPS)


def on_lanes(column):
    return jnp.broadcast_to(column, (column.shape[0], LANES))


def wide_rsqrt(inv, here, width):
    return jnp.concatenate([inv[here, :]] * (width // LANES), axis=1)


def row_sum(block):
    return jnp.sum(block, axis=0, keepdims=True)


def fold_rows(block):
    rows, width = block.shape
    return jnp.sum(block.reshape(rows // 8, 8, width), axis=0)


def pick_kernel(index, source, *refs):
    picked = refs[-1]

    def move(i, carry):
        picked[i] = source[index[i]]
        return carry

    lax.fori_loop(0, picked.shape[0], move, 0, unroll=4)


def pick(source, index, *after):
    dims = index.shape + source.shape[1:]
    return pl.pallas_call(
        pick_kernel,
        out_shape=shape(dims, source.dtype),
        in_specs=[smem(), vmem()] + [hbm()] * len(after),
        out_specs=vmem(),
        compiler_params=params(16),
        cost_estimate=SMALL,
        name="pick",
    )(index, source, *after)


def move(source, target, sem):
    return pltpu.make_async_copy(source, target, sem)


PARTS = 4


def part_moves(pairs, sems):
    moves = []
    for c in range(PARTS):
        row = []
        for n, (source, target) in enumerate(pairs):
            count = source.shape[0] // PARTS
            here = pl.ds(c * count, count)
            row.append(move(source.at[here, :], target.at[here, :], sems.at[n, c]))
        moves.append(row)
    return moves


def start_all(moves):
    for one in moves:
        one.start()


def wait_all(moves):
    for one in moves:
        one.wait()


def interleave(*streams):
    order = sorted(
        ((n + 0.5) / len(stream), which, n)
        for which, stream in enumerate(streams)
        for n in range(len(stream))
    )
    for _, which, n in order:
        streams[which][n]()


def spread_clips(seg_row, seg_b):
    for i in range(seg_b.shape[0] // LANES):
        here = pl.ds(i * LANES, LANES)
        seg_b[here, :] = jnp.broadcast_to(seg_row[:, here], (LANES, LANES)).T


def key_window(j, rows):
    window = min(rows, LANES + 2 * MAX_CLIP)
    here = pl.ds(pl.multiple_of(j * LANES, LANES), LANES)
    first = pl.multiple_of(jnp.clip(j * LANES - MAX_CLIP, 0, rows - window), LANES)
    return here, pl.ds(first, window)


def set_bias(bias, seg_b, seg_row, here, keys):
    filled = jnp.where(seg_b[keys, :] == seg_row[:, here], 0.0, NEG_FILL)
    bias[:, pl.ds(0, LANES)] = filled
    bias[:, pl.ds(LANES, LANES)] = filled


def two_heads(block):
    lane = lax.broadcasted_iota(jnp.int32, block.shape, 1)
    return jnp.concatenate(
        [block * (lane // HEAD_DIM == e).astype(BF16) for e in range(2)], axis=0
    )


def attention_kernel(
    blend, flags, seg_row, vecs, biases, tok, own, oth, w3, wp, *refs
):
    mixed, n1, normed, inv, q, k, v, att, part, lse = refs[-32:-22]
    (
        tok_v, own_v, oth_v, w3_v, wp_v, mixed_v, n1_v, q_v, k_v, v_v, att_v, part_v,
        vt, att_t, seg_b, bias, ones, normed_v, inv_v, in_sems, half_sems, out_sems,
    ) = refs[-22:]
    rows, width = tok.shape
    local = wp.shape[0]
    half_rows = rows // 2
    ratio = blend[0]
    blk = 32
    big = 512

    loads = [
        move(source, target, in_sems.at[n])
        for n, (source, target) in enumerate([(tok, tok_v), (w3, w3_v), (wp, wp_v)])
    ]
    halves = part_moves([(own, own_v), (oth, oth_v)], half_sems)
    loads[0].start()
    for part_of in halves:
        start_all(part_of)
    start_all(loads[1:])
    early = [
        move(source, target, out_sems.at[n])
        for n, (source, target) in enumerate(
            [
                (mixed_v, mixed), (n1_v, n1), (normed_v, normed), (inv_v, inv),
                (q_v, q), (k_v, k), (v_v, v),
            ]
        )
    ]
    ones[...] = jnp.ones_like(ones)
    spread_clips(seg_row, seg_b)

    loads[0].wait()
    steps = half_rows // PARTS // blk
    for n, src, half in ((0, own_v, flags[0]), (1, oth_v, 1 - flags[0])):
        for c in range(PARTS):
            halves[c][n].wait()

            def mix(i, carry, src=src, half=half, c=c):
                low = (c * steps + i) * blk
                here = pl.ds(pl.multiple_of(half * half_rows + low, blk), blk)
                there = pl.ds(pl.multiple_of(low, blk), blk)
                mine, other = tok_v[here, :].astype(F32), src[there, :].astype(F32)
                blended = ratio * mine + (1.0 - ratio) * other
                mixed_v[here, :] = blended
                centred, scale = row_stats(blended)
                inv_v[here, :] = on_lanes(scale)
                plain = centred * scale
                normed_v[here, :] = plain.astype(BF16)
                n1_v[here, :] = (plain * vecs[0:1, :] + vecs[1:2, :]).astype(BF16)
                return carry

            lax.fori_loop(0, steps, mix, 0, unroll=True)
    start_all(early[:4])

    loads[1].wait()
    for i in range(rows // big):
        here = pl.ds(i * big, big)
        rows_in = n1_v[here, :]
        queries = (nn(rows_in, w3_v[0]) + biases[0:1, :local]).astype(BF16).astype(F32)
        q_v[here, :] = (queries * SCORE_SCALE).astype(BF16)
        k_v[here, :] = nn(rows_in, w3_v[1]).astype(BF16)
        values = (nn(rows_in, w3_v[2]) + biases[0:1, local:]).astype(BF16)
        v_v[here, :] = values
        vt[:, here] = values.T
    start_all(early[4:])

    def attend(j, carry):
        here, keys = key_window(j, rows)
        set_bias(bias, seg_b, seg_row, here, keys)
        for p in range(local // LANES):
            pair = pl.ds(p * LANES, LANES)
            scores = nt(k_v[keys, pair], two_heads(q_v[here, pair])) + bias[...]
            top = jnp.max(scores, axis=0, keepdims=True)
            grown = jnp.exp(scores - top).astype(BF16)
            total = nn(ones[...], grown)[:1]
            out = (nn(vt[pair, keys], grown) / total).astype(BF16)
            logs = top + jnp.log(total)
            for e in range(2):
                lanes = slice(e * LANES, e * LANES + LANES)
                head = slice(e * HEAD_DIM, e * HEAD_DIM + HEAD_DIM)
                att_t[pl.ds(p * LANES + e * HEAD_DIM, HEAD_DIM), here] = out[head, lanes]
                lse[pl.ds(2 * p + e, 1), here] = logs[:, lanes]
        return carry

    lax.fori_loop(0, rows // LANES, attend, 0)

    loads[2].wait()
    last = []
    for i in range(rows // big):
        here = pl.ds(i * big, big)
        block = att_t[:, here].T
        att_v[here, :] = block
        part_v[here, :] = nn(block, wp_v[...]).astype(BF16)
        last.append(move(part_v.at[here, :], part.at[here, :], out_sems.at[8 + i]))
        last[-1].start()
    last.append(move(att_v, att, out_sems.at[7]))
    last[-1].start()
    wait_all(early + last)


def attention(blend, flags, segment, vecs, biases, tok, own, oth, w3, wp, *before):
    rows, width = tok.shape
    local = wp.shape[0]
    window = min(rows, LANES + 2 * MAX_CLIP)
    thin = shape((rows, local), BF16)
    tall = shape((rows, width), BF16)
    return pl.pallas_call(
        attention_kernel,
        out_shape=(
            shape((rows, width), F32), tall, tall, shape((rows, LANES), F32),
            thin, thin, thin, thin, tall, shape((local // HEAD_DIM, rows), F32),
        ),
        in_specs=[smem(), smem()] + [vmem()] * 3 + [anywhere()] * 3 + [hbm()] * (2 + len(before)),
        out_specs=[hbm()] * 9 + [vmem()],
        scratch_shapes=[
            pltpu.VMEM((rows, width), BF16),
            pltpu.VMEM((rows // 2, width), BF16),
            pltpu.VMEM((rows // 2, width), BF16),
            pltpu.VMEM(w3.shape, BF16),
            pltpu.VMEM(wp.shape, BF16),
            pltpu.VMEM((rows, width), F32),
            pltpu.VMEM((rows, width), BF16),
            pltpu.VMEM((rows, local), BF16),
            pltpu.VMEM((rows, local), BF16),
            pltpu.VMEM((rows, local), BF16),
            pltpu.VMEM((rows, local), BF16),
            pltpu.VMEM((rows, width), BF16),
            pltpu.VMEM((local, rows), BF16),
            pltpu.VMEM((local, rows), BF16),
            pltpu.VMEM((rows, LANES), F32),
            pltpu.VMEM((window, 2 * LANES), F32),
            pltpu.VMEM((16, window), BF16),
            pltpu.VMEM((rows, width), BF16),
            pltpu.VMEM((rows, LANES), F32),
            pltpu.SemaphoreType.DMA((3,)),
            pltpu.SemaphoreType.DMA((2, PARTS)),
            pltpu.SemaphoreType.DMA((8 + rows // 256,)),
        ],
        compiler_params=params(60),
        cost_estimate=SMALL,
        name="attention",
    )(
        blend, flags, segment, vecs, biases, tok, own, oth, w3, wp, *before,
    )


ERFC_SLOPE = 0.47
ERFC_COEFFS = (
    0.2663094668265691,
    0.2480096137831850,
    0.3362712657560771,
    -0.1262288063821733,
    0.6076790117752645,
    -0.4204702410368928,
    0.0884296765518492,
)


def gelu_parts(pre):
    bell = jnp.exp(pre * pre * -0.5)
    t = 1.0 / (1.0 + jnp.abs(pre) * (ERFC_SLOPE * 0.5**0.5))
    poly = 0.5 * ERFC_COEFFS[-1]
    for coeff in ERFC_COEFFS[-2::-1]:
        poly = poly * t + 0.5 * coeff
    tail = poly * t * bell
    cdf = jnp.where(pre >= 0, 1.0 - tail, tail)
    return pre * cdf, cdf + pre * bell * 0.3989422804014327


def turn_into(target, source, blocks):
    rows = source.shape[0]
    big = 256
    for i in range(rows // big):
        here = pl.ds(i * big, big)
        turned = source[here, :].T
        for start, place, count in blocks:
            target[pl.ds(place, count), here] = turned[start : start + count]


def lead_blocks(width, lead_rows):
    runs = width // lead_rows
    return [
        (run * lead_rows, ((run % 2) * (runs // 2) + run // 2) * lead_rows, lead_rows)
        for run in range(runs)
    ]


def feed_kernel(
    in_rows, out_rows, flags, vecs, biases, mixed, p_own, p_oth, cot, cot_t,
    w_in, w_out, w_out_one, w_out_two,
    hidden, part, gn_part, in_keep, in_send, out_keep, out_send, normed, inv, g_bin, g_bout,
    mixed_v, own_v, oth_v, cot_v, cot_tv, w_in_v, w_out_v, n2, n2_t, act, gp,
    pre_s, grad_s, g_in, g_out, normed_v, inv_v, in_sems, turn_sems, weight_sems, out_sems, grad_sems,
):
    rows, width = mixed.shape
    units = w_in.shape[1]
    blk = 32
    big = 512
    sub = 16
    home = flags[1] == 1
    across = flags[2]
    kept_out = jnp.where(home, flags[0], 1 - flags[0]) if in_rows != out_rows else across
    sides = (across, kept_out)

    loads = part_moves(
        [(mixed, mixed_v), (p_own, own_v), (p_oth, oth_v), (cot, cot_v)], in_sems
    )
    for part_of in loads:
        start_all(part_of)

    weights = [move(w_in, w_in_v, weight_sems.at[0])]
    weights[0].start()
    half = w_out.shape[0] // 2
    for n, (got, place) in enumerate([(w_out_one, across), (w_out_two, 1 - across)]):
        spot = pl.ds(pl.multiple_of(place * half, half), half)
        sem = weight_sems.at[1 + n]
        weights.append(move(w_out.at[spot, :], w_out_v.at[spot, :], sem))

        @pl.when(home)
        def _(spot=spot, sem=sem):
            move(w_out.at[spot, :], w_out_v.at[spot, :], sem).start()

        @pl.when(jnp.logical_not(home))
        def _(got=got, spot=spot, sem=sem):
            move(got, w_out_v.at[spot, :], sem).start()

    turns = [
        move(cot_t.at[pl.ds(start, count), :], cot_tv.at[pl.ds(place, count), :], turn_sems.at[n])
        for n, (start, place, count) in enumerate(lead_blocks(width, out_rows))
    ]
    start_all(turns)

    g_bout[...] = jnp.zeros_like(g_bout)
    steps = rows // PARTS // blk
    for c in range(PARTS):
        wait_all(loads[c])

        def norm(i, carry, c=c):
            here = pl.ds(pl.multiple_of((c * steps + i) * blk, blk), blk)
            attn = own_v[here, :].astype(F32) + oth_v[here, :].astype(F32)
            total = mixed_v[here, :] + attn + vecs[4:5, :]
            mixed_v[here, :] = total
            centred, scale = row_stats(total)
            inv_v[here, :] = on_lanes(scale)
            plain = centred * scale
            normed_v[here, :] = plain.astype(BF16)
            n2[here, :] = (plain * vecs[2:3, :] + vecs[3:4, :]).astype(BF16)
            g_bout[...] += fold_rows(cot_v[here, :].astype(F32))
            return carry

        lax.fori_loop(0, steps, norm, 0, unroll=4)
    stores = [
        move(source, target, out_sems.at[0, n])
        for n, (source, target) in enumerate(
            [(mixed_v, hidden), (normed_v, normed), (inv_v, inv)]
        )
    ]
    start_all(stores)
    turn_into(n2_t, n2, lead_blocks(width, in_rows))
    wait_all(weights)

    g_bin[...] = jnp.zeros_like(g_bin)

    def row_block(i, carry):
        here = pl.ds(pl.multiple_of(i * big, big), big)
        for j in range(units // width):
            cols = pl.ds(j * width, width)
            pre_s[...] = nn(n2[here, :], w_in_v[:, cols])
            grad_s[...] = nt(cot_v[here, :], w_out_v[cols, :])

            def activate(n, carry, j=j, cols=cols):
                rng = pl.ds(pl.multiple_of(n * sub, sub), sub)
                value, slope = gelu_parts(pre_s[rng, :] + biases[1 + j : 2 + j, :])
                grad = grad_s[rng, :] * slope
                g_bin[:, cols] += fold_rows(grad)
                spot = pl.ds(pl.multiple_of(i * big + n * sub, sub), sub)
                act[spot, cols] = value.astype(BF16)
                gp[spot, cols] = grad.astype(BF16)
                return carry

            lax.fori_loop(0, big // sub, activate, 0, unroll=4)
        oth_v[here, :] = nt(gp[here, :], w_in_v[...]).astype(BF16)
        own_v[here, :] = nn(act[here, :], w_out_v[...]).astype(BF16)
        for n, (source, target) in enumerate([(oth_v, gn_part), (own_v, part)]):
            move(source.at[here, :], target.at[here, :], out_sems.at[1 + n, i]).start()
        return carry

    lax.fori_loop(0, rows // big, row_block, 0)
    for i in range(rows // big):
        here = pl.ds(i * big, big)
        for n, (source, target) in enumerate([(oth_v, gn_part), (own_v, part)]):
            stores.append(move(source.at[here, :], target.at[here, :], out_sems.at[1 + n, i]))

    wait_all(turns)
    half = width // 2
    for n, (turned, right, buf, keep, send) in enumerate(
        [(n2_t, gp, g_in, in_keep, in_send), (cot_tv, act, g_out, out_keep, out_send)]
    ):
        for j in range(0, units, width // 2):
            cols = pl.ds(j, width // 2)
            product = nn(turned[...], right[:, cols]).astype(BF16)
            for side in range(2):
                buf[side, :, cols] = product[side * half : side * half + half]
        for m, (side, target) in enumerate([(1 - sides[n], send), (sides[n], keep)]):
            stores.append(move(buf.at[side], target, grad_sems.at[n, m]))
            stores[-1].start()
    wait_all(stores)


def feed(
    in_rows, out_rows, flags, vecs, biases, mixed, p_own, p_oth, cot, cot_t,
    w_in, w_out, w_out_one, w_out_two,
):
    rows, width = mixed.shape
    units = w_in.shape[1]
    tall = shape((rows, width), BF16)
    grad = shape((width // 2, units), BF16)
    return pl.pallas_call(
        functools.partial(feed_kernel, in_rows, out_rows),
        out_shape=(
            shape((rows, width), F32), tall, tall, grad, grad, grad, grad,
            tall, shape((rows, LANES), F32), shape((8, units), F32), shape((8, width), F32),
        ),
        in_specs=[smem()] + [vmem()] * 2 + [hbm()] * 2 + [anywhere()] + [hbm()] * 6,
        out_specs=[hbm()] * 9 + [vmem()] * 2,
        scratch_shapes=[
            pltpu.VMEM((rows, width), F32),
            pltpu.VMEM((rows, width), BF16),
            pltpu.VMEM((rows, width), BF16),
            pltpu.VMEM((rows, width), BF16),
            pltpu.VMEM((width, rows), BF16),
            pltpu.VMEM(w_in.shape, BF16),
            pltpu.VMEM(w_out.shape, BF16),
            pltpu.VMEM((rows, width), BF16),
            pltpu.VMEM((width, rows), BF16),
            pltpu.VMEM((rows, units), BF16),
            pltpu.VMEM((rows, units), BF16),
            pltpu.VMEM((512, width), F32),
            pltpu.VMEM((512, width), F32),
            pltpu.VMEM((2, width // 2, units), BF16),
            pltpu.VMEM((2, width // 2, units), BF16),
            pltpu.VMEM((rows, width), BF16),
            pltpu.VMEM((rows, LANES), F32),
            pltpu.SemaphoreType.DMA((4, PARTS)),
            pltpu.SemaphoreType.DMA((width // out_rows,)),
            pltpu.SemaphoreType.DMA((3,)),
            pltpu.SemaphoreType.DMA((3, rows // 256)),
            pltpu.SemaphoreType.DMA((2, 2)),
        ],
        compiler_params=params(60),
        cost_estimate=SMALL,
        name="feed",
    )(
        flags, vecs, biases, mixed, p_own, p_oth, cot, cot_t,
        w_in, w_out, w_out_one, w_out_two,
    )


def attention_back_kernel(
    lead_rows, part_rows, flags, vecs, seg_row, lse, g_bin, g_bout, g_own, g_oth, cot, normed, inv,
    wp, att, k, q, v, w3, n1, normed_one,
    gh, part, keep, send, short,
    gh_v, own_v, oth_v, cot_v, normed_v, inv_v, wp_v, att_v, k_v, q_v, v_v, w3_v, n1_v, one_v, low_v, part_v,
    sums, tails, d_out, kt, dq_t, dk, dv, delta, seg_b, bias, raw, raw_g, low_p, low_g, n1_t, gh_t, grad_v, out,
    in_sems, row_sems, out_sems, last_sems,
):
    rows, width = cot.shape
    local = wp.shape[0]
    blk = 32
    big = 256
    blocks = lead_blocks(width, lead_rows)
    kept_side = flags[2]
    row_loads = part_moves(
        [(g_own, own_v), (g_oth, oth_v), (cot, cot_v), (normed, normed_v), (inv, inv_v)],
        row_sems,
    )
    for part_of in row_loads:
        start_all(part_of)
    loads = [
        move(source, target, in_sems.at[n])
        for n, (source, target) in enumerate(
            [
                (wp, wp_v), (att, att_v), (k, k_v), (q, q_v), (v, v_v), (w3, w3_v), (n1, n1_v),
                (normed_one, one_v),
            ]
        )
    ]
    start_all(loads)
    sums[...] = jnp.zeros_like(sums)
    dk[...] = jnp.zeros_like(dk)
    dv[...] = jnp.zeros_like(dv)
    spread_clips(seg_row, seg_b)

    steps = rows // PARTS // blk
    for c in range(PARTS):
        wait_all(row_loads[c])

        def norm(i, carry, c=c):
            here = pl.ds(pl.multiple_of((c * steps + i) * blk, blk), blk)
            grad = own_v[here, :].astype(F32) + oth_v[here, :].astype(F32)
            plain = normed_v[here, :].astype(F32)
            scaled = grad * vecs[2:3, :]
            mean_one = jnp.mean(scaled, axis=-1, keepdims=True)
            mean_two = jnp.mean(scaled * plain, axis=-1, keepdims=True)
            scale = wide_rsqrt(inv_v, here, width)
            back = cot_v[here, :].astype(F32) + scale * (scaled - mean_one - plain * mean_two)
            gh_v[here, :] = back
            low_v[here, :] = back.astype(BF16)
            sums[0] += fold_rows(grad * plain)
            sums[1] += fold_rows(grad)
            sums[2] += fold_rows(back)
            return carry

        lax.fori_loop(0, steps, norm, 0, unroll=2)
    stores = [move(gh_v, gh, out_sems.at[0])]
    stores[0].start()

    wait_all(loads[:3])
    heads = local // HEAD_DIM
    lane = lax.broadcasted_iota(jnp.int32, (delta.shape[0], local), 1)
    row = lax.broadcasted_iota(jnp.int32, (delta.shape[0], local), 0)
    of_head = (lane // HEAD_DIM == row).astype(BF16)

    def project(i, carry):
        here = pl.ds(pl.multiple_of(i * big, big), big)
        grad_out = nt(low_v[here, :], wp_v[...]).astype(BF16)
        d_out[here, :] = grad_out
        product = grad_out.astype(F32) * att_v[here, :].astype(F32)
        coarse = product.astype(BF16)
        fine = (product - coarse.astype(F32)).astype(BF16)
        delta[:, here] = nt(of_head, coarse) + nt(of_head, fine)
        kt[:, here] = k_v[here, :].T
        return carry

    lax.fori_loop(0, rows // big, project, 0)
    wait_all(loads[3:])

    pairs = heads // 2
    window = bias.shape[0]
    strip = 128
    strips = window // strip

    def attend(j, carry):
        here, keys = key_window(j, rows)
        first = pl.multiple_of(keys.start, LANES)
        set_bias(bias, seg_b, seg_row, here, keys)
        blocks_two = {}

        def two(p):
            if p not in blocks_two:
                pair = pl.ds(p * LANES, LANES)
                blocks_two[p] = (two_heads(q_v[here, pair]), two_heads(d_out[here, pair]))
            return blocks_two[p]

        def at_strip(n):
            return (
                pl.ds(pl.multiple_of(first + n * strip, strip), strip),
                pl.ds(n * strip, strip),
            )

        def products(p):
            pair = pl.ds(p * LANES, LANES)

            def scores(n):
                def run():
                    some, at = at_strip(n)
                    raw[p % 2, at, :] = nt(k_v[some, pair], two(p)[0])

                return run

            def grads(n):
                def run():
                    some, at = at_strip(n)
                    raw_g[p % 2, at, :] = nt(v_v[some, pair], two(p)[1])

                return run

            return [make(n) for n in range(strips) for make in (scores, grads)]

        def softmax_back(p):
            tops = jnp.concatenate([lse[pl.ds(2 * p + e, 1), here] for e in range(2)], axis=1)
            inner = jnp.concatenate([delta[pl.ds(2 * p + e, 1), here] for e in range(2)], axis=1)
            half = strip // 2

            def run_at(n):
                def run():
                    at = pl.ds(n * half, half)
                    probs = jnp.exp(raw[p % 2, at, :] + bias[at, :] - tops)
                    low_p[p % 2, at, :] = probs.astype(BF16)
                    low_g[p % 2, at, :] = (probs * (raw_g[p % 2, at, :] - inner)).astype(BF16)

                return run

            return [run_at(n) for n in range(2 * strips)]

        def sums_of(p):
            pair = pl.ds(p * LANES, LANES)

            def keys_of(n):
                def run():
                    some, at = at_strip(n)
                    dk[some, pair] += nn(low_g[p % 2, at, :], two(p)[0])

                return run

            def values_of(n):
                def run():
                    some, at = at_strip(n)
                    dv[some, pair] += nn(low_p[p % 2, at, :], two(p)[1])

                return run

            def queries():
                grad_q = nn(kt[pair, keys], low_g[p % 2]) * SCORE_SCALE
                for e in range(2):
                    lanes = slice(e * LANES, e * LANES + LANES)
                    head = slice(e * HEAD_DIM, e * HEAD_DIM + HEAD_DIM)
                    dq_t[pl.ds(p * LANES + e * HEAD_DIM, HEAD_DIM), here] = grad_q[head, lanes]

            return [make(n) for n in range(strips) for make in (keys_of, values_of)] + [queries]

        def turns():
            for target, source in ((n1_t, n1_v), (gh_t, low_v)):
                turned = source[here, :].T
                for start, place, count in blocks:
                    target[pl.ds(place, count), here] = turned[start : start + count]

        interleave(products(0), [turns])
        for p in range(pairs):
            matrix = (products(p + 1) if p + 1 < pairs else []) + (sums_of(p - 1) if p else [])
            interleave(softmax_back(p), matrix)
        interleave(sums_of(pairs - 1))
        return carry

    lax.fori_loop(0, rows // LANES, attend, 0)

    tails[...] = jnp.zeros_like(tails)

    def finish(i, carry):
        here = pl.ds(pl.multiple_of(i * big, big), big)
        grad_q, grad_k, grad_val = dq_t[:, here].T, dk[here, :], dv[here, :]
        tails[2, :, pl.ds(0, local)] += fold_rows(grad_q)
        tails[2, :, pl.ds(local, local)] += fold_rows(grad_val)
        lows = [grad.astype(BF16) for grad in (grad_q, grad_k, grad_val)]
        total = sum(nt(low, w3_v[n]) for n, low in enumerate(lows))
        part_v[here, :] = total.astype(BF16)
        tails[0] += fold_rows(total * one_v[here, :].astype(F32))
        tails[1] += fold_rows(total)
        for n, low in enumerate(lows):
            grad_v[here, pl.ds(n * local, local)] = low
        move(part_v.at[here, :], part.at[here, :], last_sems.at[i]).start()
        return carry

    lax.fori_loop(0, rows // big, finish, 0)
    for i in range(rows // big):
        here = pl.ds(i * big, big)
        stores.append(move(part_v.at[here, :], part.at[here, :], last_sems.at[i]))
    units = g_bin.shape[1]
    listed = [tails[0], tails[1], sums[0], sums[1], sums[2], g_bout[...], tails[2]]
    listed += [g_bin[:, pl.ds(n, width)] for n in range(0, units, width)]
    half = width // 2
    listed = [row_sum(block) for block in listed]
    for n, block in enumerate(listed):
        short[pl.ds(n, 1), :] = block
    if part_rows:
        sources = [
            (jnp.concatenate(listed[:6] + [jnp.zeros((2, width), F32)], axis=0), part_rows),
            (jnp.broadcast_to(listed[6][:, :local], (8, local)), local * part_rows // width),
            (jnp.broadcast_to(listed[6][:, local:], (8, local)), local * part_rows // width),
            (
                jnp.broadcast_to(jnp.concatenate(listed[7:], axis=1), (8, units)),
                units * part_rows // width,
            ),
        ]
        rest = jnp.zeros((part_rows - 8 * len(sources), LANES), F32)
        for start, place, count in blocks:
            for row in range(0, count, part_rows):
                d = (start + row) // part_rows
                parts = [
                    pltpu.roll(source, (source.shape[1] - d * size) % source.shape[1], 1)[:, :LANES]
                    for source, size in sources
                ]
                side, at = divmod(place + row, half)
                out[side, pl.ds(at, part_rows), pl.ds(4 * local, LANES)] = jnp.concatenate(
                    parts + [rest], axis=0
                ).astype(BF16)
    for n in range(4):
        cols = pl.ds(n * local, local)
        product = nn(gh_t[...], att_v[...]) if n == 3 else nn(n1_t[...], grad_v[:, cols])
        for side in range(2):
            out[side, :, cols] = product[side * half : side * half + half].astype(BF16)
    for n, (side, target) in enumerate([(1 - kept_side, send), (kept_side, keep)]):
        stores.append(move(out.at[side], target, out_sems.at[1 + n]))
        stores[-1].start()
    wait_all(stores)


def attention_back(
    lead_rows, part_rows, flags, vecs, segment, lse, g_bin, g_bout, g_own, g_oth, cot, normed, inv,
    wp, att, k, q, v, w3, n1, normed_one,
):
    rows, width = cot.shape
    local = wp.shape[0]
    window = min(rows, LANES + 2 * MAX_CLIP)
    tall, thin = pltpu.VMEM((rows, width), BF16), pltpu.VMEM((rows, local), BF16)
    turned = pltpu.VMEM((width, rows), BF16)
    half = (width // 2, 4 * local + (LANES if part_rows else 0))
    return pl.pallas_call(
        functools.partial(attention_back_kernel, lead_rows, part_rows),
        out_shape=(
            shape((rows, width), F32),
            shape((rows, width), BF16),
            shape(half, BF16),
            shape(half, BF16),
            shape((7 + g_bin.shape[1] // width, width), F32),
        ),
        in_specs=[smem()] + [vmem()] * 5 + [hbm()] + [anywhere()] + [hbm()] * 11,
        out_specs=[hbm()] * 4 + [vmem()],
        scratch_shapes=[
            pltpu.VMEM((rows, width), F32),
            tall, tall, tall, tall,
            pltpu.VMEM((rows, LANES), F32),
            pltpu.VMEM(wp.shape, BF16),
            thin, thin, thin, thin,
            pltpu.VMEM(w3.shape, BF16),
            tall, tall, tall, tall,
            pltpu.VMEM((3, 8, width), F32),
            pltpu.VMEM((3, 8, width), F32),
            thin,
            pltpu.VMEM((local, rows), BF16),
            pltpu.VMEM((local, rows), F32),
            pltpu.VMEM((rows, local), F32),
            pltpu.VMEM((rows, local), F32),
            pltpu.VMEM((8, rows), F32),
            pltpu.VMEM((rows, LANES), F32),
            pltpu.VMEM((window, 2 * LANES), F32),
            pltpu.VMEM((2, window, 2 * LANES), F32),
            pltpu.VMEM((2, window, 2 * LANES), F32),
            pltpu.VMEM((2, window, 2 * LANES), BF16),
            pltpu.VMEM((2, window, 2 * LANES), BF16),
            turned, turned,
            pltpu.VMEM((rows, 3 * local), BF16),
            pltpu.VMEM((2,) + half, BF16),
            pltpu.SemaphoreType.DMA((8,)),
            pltpu.SemaphoreType.DMA((5, PARTS)),
            pltpu.SemaphoreType.DMA((3,)),
            pltpu.SemaphoreType.DMA((rows // 256,)),
        ],
        compiler_params=params(60),
        cost_estimate=SMALL,
        name="attention_back",
    )(
        flags, vecs, segment, lse, g_bin, g_bout, g_own, g_oth, cot, normed, inv,
        wp, att, k, q, v, w3, n1, normed_one,
    )


def mixed_back_kernel(blend, vecs, gh, g_own, g_oth, normed, inv, outgoing, kept, *refs):
    gh_v, own_v, oth_v, normed_v, inv_v, leave_v, kept_v, in_sems, out_sems = refs
    ratio = blend[0]
    rows, width = gh.shape
    blk = 32
    loads = part_moves(
        [(gh, gh_v), (g_own, own_v), (g_oth, oth_v), (normed, normed_v), (inv, inv_v)], in_sems
    )
    stores = part_moves([(leave_v, outgoing), (kept_v, kept)], out_sems)
    for part_of in loads:
        start_all(part_of)
    steps = rows // PARTS // blk
    for c in range(PARTS):
        wait_all(loads[c])

        def norm(i, carry, c=c):
            here = pl.ds(pl.multiple_of((c * steps + i) * blk, blk), blk)
            grad = own_v[here, :].astype(F32) + oth_v[here, :].astype(F32)
            plain = normed_v[here, :].astype(F32)
            scaled = grad * vecs[0:1, :]
            mean_one = jnp.mean(scaled, axis=-1, keepdims=True)
            mean_two = jnp.mean(scaled * plain, axis=-1, keepdims=True)
            scale = wide_rsqrt(inv_v, here, width)
            back = gh_v[here, :] + scale * (scaled - mean_one - plain * mean_two)
            leave_v[here, :] = ((1.0 - ratio) * back).astype(BF16)
            kept_v[here, :] = (ratio * back).astype(BF16)
            return carry

        lax.fori_loop(0, steps, norm, 0, unroll=4)
        start_all(stores[c])
    for part_of in stores:
        wait_all(part_of)


def mixed_back(blend, vecs, gh, g_own, g_oth, normed, inv):
    rows, width = gh.shape
    tall = pltpu.VMEM((rows, width), BF16)
    return pl.pallas_call(
        mixed_back_kernel,
        out_shape=(shape((rows, width), BF16), shape((rows, width), BF16)),
        in_specs=[smem(), vmem()] + [hbm()] * 2 + [anywhere()] + [hbm()] * 2,
        out_specs=[hbm(), hbm()],
        scratch_shapes=[
            pltpu.VMEM((rows, width), F32),
            tall, tall, tall, pltpu.VMEM((rows, LANES), F32), tall, tall,
            pltpu.SemaphoreType.DMA((5, PARTS)),
            pltpu.SemaphoreType.DMA((2, PARTS)),
        ],
        compiler_params=params(60),
        cost_estimate=SMALL,
        name="mixed_back",
    )(blend, vecs, gh, g_own, g_oth, normed, inv)


def shards(
    tokens,
    mix_blend,
    partner,
    clip_ids,
    gain_one,
    shift_one,
    qkv_weight,
    qv_bias,
    proj_weight,
    proj_bias,
    gain_two,
    shift_two,
    in_weight,
    in_bias,
    out_weight,
    out_bias,
    cotangent,
):
    rows, width = tokens.shape
    dp_count = lax.axis_size("dp")
    both = ("dp", "mp")
    bits = dp_count.bit_length() - 1
    seq = lax.axis_index("dp")
    mp = lax.axis_index("mp")
    core = lax.rem(seq, 2)
    home = core == mp
    all_dp = range(dp_count)

    def joint(d, m):
        return 2 * d + m

    core_swap = [(d, d ^ 1) for d in all_dp]
    home_to_pair = [(joint(d, d & 1), joint(d, 1 - (d & 1))) for d in all_dp]
    pair_to_home = [(joint(d, 1 - (d & 1)), joint(d, d & 1)) for d in all_dp]
    weight_move = home_to_pair + [
        (joint(d, 1 - (d & 1)), joint(d ^ 1, 1 - (d & 1))) for d in all_dp
    ]

    def swap(value):
        return lax.ppermute(value, "dp", core_swap)

    def chip_value(value):
        return jnp.where(home, value, swap(value))

    def after(value, *others):
        return lax.optimization_barrier((value,) + others)[0]

    def half_weight(value):
        return lax.ppermute(value, both, weight_move)

    part_rows = width // dp_count
    lead = min(n for n in range(1, bits) if (part_rows << n) % 16 == 0)
    lead_rows = part_rows << lead
    across = lax.rem(seq >> lead, 2)
    flags = jnp.stack([core, home.astype(jnp.int32), across]).astype(jnp.int32)

    def taken(value, index, axis):
        return lax.dynamic_index_in_dim(value, index, axis, keepdims=False)

    seq_small = chip_value(jnp.concatenate([mix_blend, clip_ids[0].astype(F32)]))
    blend, segment = seq_small[:1], seq_small[1:].reshape(1, rows)
    local = proj_weight.shape[0]
    units = in_bias.shape[0]
    half_small = jnp.concatenate([qv_bias.reshape(-1), in_bias])
    half_small = jnp.where(home, half_small, half_weight(half_small))
    biases = half_small.reshape(-1, width)
    vecs = jnp.stack([gain_one, shift_one, gain_two, shift_two, proj_bias])

    w3 = half_weight(qkv_weight.transpose(1, 0, 2))
    wp = half_weight(proj_weight)

    def two_way(value):
        halves = value.reshape(2, value.shape[0] // 2, value.shape[1])
        one = half_weight(taken(halves, across, 0))
        moves = [(joint(d, 1 - (d & 1)), joint(d ^ (1 << lead), 1 - (d & 1))) for d in all_dp]
        return value, one, lax.ppermute(one, both, moves)

    ids = jnp.arange(2 * dp_count, dtype=jnp.int32)
    piece = rows // (2 * 2 * dp_count)
    sent = tokens.reshape(2, dp_count, 2, piece, width)
    sent = lax.dynamic_index_in_dim(sent, mp, 2, keepdims=False)
    spread = lax.all_to_all(sent.transpose(1, 0, 2, 3), "dp", 0, 0, tiled=True)
    wanted = partner[(ids // 4) * 2 + ids % 2] * 2 + (ids // 2) % 2
    source_of = jnp.sum(
        jnp.where(partner[:, None] == ids[None, :dp_count], ids[:dp_count, None], 0),
        axis=0,
        dtype=jnp.int32,
    )
    source = source_of[ids // 2]
    wanted_back = (source // 2) * 4 + (ids % 2) * 2 + source % 2
    chosen = pick(spread.reshape(2 * dp_count, piece, width), wanted, w3, wp, half_small)
    partner_own = lax.all_to_all(chosen, both, 0, 0, tiled=True).reshape(rows // 2, width)
    w_out = two_way(out_weight)
    w_in = half_weight(after(in_weight, w_out[1]))

    tok = chip_value(tokens)
    cot = chip_value(cotangent)
    cot_t = cot.T
    partner_oth = swap(after(partner_own, tok, cot, vecs, segment, wanted_back))

    mixed, n1, normed_one, inv_one, q, k, v, att, attn_part, lse = attention(
        blend, flags, segment, vecs, biases, tok, partner_own, partner_oth, w3, wp, w_out[2], cot_t
    )
    pair_first = part_rows % 16 == 0
    fed = feed(
        lead_rows, part_rows if pair_first else lead_rows, flags, vecs, biases,
        mixed, attn_part, swap(attn_part), cot, cot_t, w_in, *w_out,
    )
    hidden, out_part, gn2_part, in_keep, in_send, out_keep, out_send = fed[:7]
    normed_two, inv_two, g_bin, g_bout = fed[7:]
    gn2_oth = swap(gn2_part)

    high, mid = dp_count >> (lead + 1), 1 << (lead - 1)
    pair_and_core = pair_to_home + [(joint(d, d & 1), joint(d ^ 1, d & 1)) for d in all_dp]
    pair_diagonal = [(joint(d, 1 - (d & 1)), joint(d ^ 1, d & 1)) for d in all_dp]

    def total(*terms):
        return sum(term.astype(F32) for term in terms)

    def send_across(value):
        return lax.ppermute(value, "dp", [(d, d ^ (1 << lead)) for d in all_dp])

    def send_pair(value):
        value = value.reshape(high, mid, 2, part_rows, -1)
        one = lax.ppermute(taken(value, jnp.where(home, 1 - core, core), 2), both, pair_and_core)
        two = lax.ppermute(taken(value, 1 - core, 2), both, pair_diagonal)
        held = taken(value, core, 2)
        return jnp.where(home, held, jnp.zeros_like(held)), one, two

    def far(value, *others):
        for shift, left in ((1, mid), (lead + 1, high)):
            while left > 1:
                radix = min(4, left)
                left //= radix
                value = value.reshape((-1, left, radix) + value.shape[-2:]).astype(BF16)
                spot = lax.rem(seq >> shift, radix)
                got = [
                    lax.ppermute(
                        taken(value, spot ^ flip, 2),
                        "dp",
                        [(d, d ^ (flip << shift)) for d in all_dp],
                    )
                    for flip in range(1, radix)
                ]
                value = total(taken(value, spot, 2), *after(got, *others))
                shift += radix.bit_length() - 1
        return value.reshape(value.shape[-2:])

    def send_first(keep, send):
        if not pair_first:
            return [keep, send_across(send)]
        one = lax.ppermute(send, both, pair_and_core)
        two = lax.ppermute(keep, both, pair_diagonal)
        return [jnp.where(home, keep, jnp.zeros_like(keep)), one, two]

    def send_second(value):
        if not pair_first:
            return send_pair(value)
        value = value.reshape(high, 2, mid, part_rows, -1)
        return taken(value, across, 1), send_across(taken(value, 1 - across, 1))

    in_got = send_across(in_send)
    out_first = send_first(out_keep, out_send)
    gh, gn1_part, attn_keep, attn_send, short = attention_back(
        lead_rows, part_rows if pair_first else 0, flags, vecs, segment, lse, g_bin, g_bout,
        gn2_part, gn2_oth, cot, normed_two, inv_two, wp, att, k, q, v, w3, n1, normed_one,
    )
    gn1_oth = swap(after(gn1_part, in_got, *out_first))
    attn_first = [attn_keep, send_across(attn_send)]
    in_terms = send_pair(total(in_keep, in_got).astype(BF16))
    outgoing, kept = mixed_back(blend, vecs, gh, gn1_part, gn1_oth, normed_one, inv_one)

    leaving = taken(outgoing.reshape(2, 2, dp_count, piece, width), core, 1)
    leaving = leaving.transpose(1, 0, 2, 3).reshape(2 * dp_count, piece, width)
    back = lax.all_to_all(leaving, both, 0, 0, tiled=True)

    in_value = total(*after(in_terms, leaving)).astype(BF16)
    sum_in = far(in_value)
    out_oth = swap(after(out_part, leaving))
    out_value = total(*after(out_first, in_value)).astype(BF16)
    out_terms = send_second(out_value)
    attn_value = total(*after(attn_first, out_value)).astype(BF16)
    attn_terms = send_pair(attn_value)
    block = hidden + (out_part.astype(F32) + after(out_oth, attn_value).astype(F32)) + out_bias
    block = block.astype(BF16)
    kept = kept.reshape(2, rows // 2, width)
    kept_got = half_weight(taken(kept, 1 - mp, 0))
    block_got = half_weight(block)

    def side_by_side(*groups):
        values = [total(*terms).reshape(high * mid, part_rows, -1) for terms in groups]
        return jnp.concatenate(values, axis=2).astype(BF16)

    returning = pick(back, wanted_back, attn_value, sum_in)
    returned = lax.all_to_all(
        returning.reshape(dp_count, 2, piece, width), "dp", 0, 0, tiled=True
    )
    returned = after(returned, kept_got)
    kept = jnp.where(home, taken(kept, mp, 0), kept_got)
    returned = returned.transpose(1, 0, 2, 3).reshape(rows // 2, width)
    mine = (kept.astype(F32) + returned.astype(F32)).astype(BF16)
    other = lax.ppermute(mine, "mp", [(0, 1), (1, 0)])
    block_out = jnp.where(home, block, after(block_got, mine))
    grad_tokens = jnp.where(
        jnp.arange(2)[:, None, None] == mp, mine[None], other[None]
    ).reshape(rows, width)

    marker = swap(returning[0, :, :LANES])
    summed = far(
        side_by_side(*(after(terms, marker) for terms in (out_terms, attn_terms))),
        mine,
    )
    sum_out, sum_attn = after(summed[:, :units], other), summed[:, units:]
    sum_qkv = sum_attn[:, : 3 * local].reshape(-1, 3, local)
    sum_proj = sum_attn[:, 3 * local : 4 * local].T
    quarter, eighth = local // dp_count, units // dp_count
    if pair_first:
        extra = sum_attn[:, 4 * local :]
        plain = extra[:6, :part_rows]
        ours = plain[:2] + lax.ppermute(plain[:2], "mp", [(0, 1), (1, 0)])
        plain = jnp.concatenate([ours, plain[2:]])
        sum_qv = jnp.stack([extra[8, :quarter], extra[16, :quarter]])
        sum_bin = extra[24, :eighth]
    else:
        counts = jnp.where((core == 0) | (jnp.arange(6) < 2), 1.0, 0.0).astype(F32)
        wide = (short[:6] * counts[:, None]).reshape(6, dp_count, 1, part_rows)
        wide = jnp.broadcast_to(wide, (6, dp_count, 2, part_rows)).transpose(1, 2, 0, 3)
        to_half = (jnp.arange(2) == core)[None, :, None]

        def half_terms(vectors):
            terms = vectors.reshape(vectors.shape[0], dp_count, -1).transpose(1, 0, 2)
            return jnp.where(to_half, terms.reshape(dp_count, 1, -1), 0.0)

        short = jnp.concatenate(
            [
                wide.reshape(dp_count, 2, -1),
                half_terms(short[6].reshape(2, local)),
                half_terms(short[7:].reshape(1, units)),
            ],
            axis=-1,
        ).reshape(2 * dp_count, -1)
        short = jnp.sum(lax.all_to_all(short, both, 0, 0, tiled=True), axis=0)
        plain = short[: 6 * part_rows].reshape(6, part_rows)
        sum_qv = short[6 * part_rows : 6 * part_rows + 2 * quarter].reshape(2, -1)
        sum_bin = short[6 * part_rows + 2 * quarter :]
    return (
        block_out,
        grad_tokens,
        plain[0],
        plain[1],
        sum_qkv,
        sum_qv,
        sum_proj,
        plain[4],
        plain[2],
        plain[3],
        sum_in,
        sum_bin,
        sum_out.T,
        plain[5],
    )


def solution(mesh):
    return jax.shard_map(
        shards,
        mesh=mesh,
        in_specs=(
            P("dp", None),
            P("dp"),
            P(),
            P("dp", None),
            P(),
            P(),
            P(None, None, "mp"),
            P(None, "mp"),
            P("mp", None),
            P(),
            P(),
            P(),
            P(None, "mp"),
            P("mp"),
            P("mp", None),
            P(),
            P("dp", None),
        ),
        out_specs=(
            P("dp", None),
            P("dp", None),
            P("dp"),
            P("dp"),
            P("dp", None, "mp"),
            P(None, ("mp", "dp")),
            P("mp", "dp"),
            P("dp"),
            P("dp"),
            P("dp"),
            P("dp", "mp"),
            P(("mp", "dp")),
            P("mp", "dp"),
            P("dp"),
        ),
        check_vma=False,
    )
```

```python
import functools

import jax
import jax.numpy as jnp
from jax import lax
from jax.experimental import pallas as pl
from jax.experimental.pallas import tpu as pltpu
from jax.sharding import PartitionSpec as P

HEAD_DIM = 64
NORM_EPS = 1e-06
NEG_FILL = -1e30
SCORE_SCALE = HEAD_DIM ** (-0.5)
MAX_CLIP = 256
LANES = 128
F32 = jnp.float32
BF16 = jnp.bfloat16
MIB = 1 << 20
SMALL = pl.CostEstimate(flops=1 << 20, bytes_accessed=1 << 20, transcendentals=0)


def nn(left, right):
    return lax.dot_general(left, right, (((1,), (0,)), ((), ())), preferred_element_type=F32)


def nt(left, right):
    return lax.dot_general(left, right, (((1,), (1,)), ((), ())), preferred_element_type=F32)


def vmem():
    return pl.BlockSpec(memory_space=pltpu.VMEM)


def hbm():
    return pl.BlockSpec(memory_space=pltpu.HBM)


def anywhere():
    return pl.BlockSpec(memory_space=pl.ANY)


def smem():
    return pl.BlockSpec(memory_space=pltpu.SMEM)


def params(mib):
    return pltpu.CompilerParams(vmem_limit_bytes=mib * MIB)


def shape(dims, dtype):
    return jax.ShapeDtypeStruct(dims, dtype)


def row_stats(vector):
    mean = jnp.mean(vector, axis=-1, keepdims=True)
    centred = vector - mean
    spread = jnp.mean(centred * centred, axis=-1, keepdims=True)
    return centred, lax.rsqrt(spread + NORM_EPS)


def on_lanes(column):
    return jnp.broadcast_to(column, (column.shape[0], LANES))


def wide_rsqrt(inv, here, width):
    return jnp.concatenate([inv[here, :]] * (width // LANES), axis=1)


def row_sum(block):
    return jnp.sum(block, axis=0, keepdims=True)


def fold_rows(block):
    rows, width = block.shape
    return jnp.sum(block.reshape(rows // 8, 8, width), axis=0)


def pick_kernel(index, source, *refs):
    picked = refs[-1]

    def move(i, carry):
        picked[i] = source[index[i]]
        return carry

    lax.fori_loop(0, picked.shape[0], move, 0, unroll=4)


def pick(source, index, *after):
    dims = index.shape + source.shape[1:]
    return pl.pallas_call(
        pick_kernel,
        out_shape=shape(dims, source.dtype),
        in_specs=[smem(), vmem()] + [hbm()] * len(after),
        out_specs=vmem(),
        compiler_params=params(16),
        cost_estimate=SMALL,
        name="pick",
    )(index, source, *after)


def move(source, target, sem):
    return pltpu.make_async_copy(source, target, sem)


PARTS = 4


def part_move(pairs, sems, c, first=0):
    moves = []
    for n, (source, target) in enumerate(pairs):
        count = source.shape[0] // PARTS
        here = pl.ds(pl.multiple_of(c * count, count), count)
        moves.append(move(source.at[here, :], target.at[here, :], sems.at[first + n, c]))
    return moves


def start_parts(pairs, sems):
    for c in range(PARTS):
        start_all(part_move(pairs, sems, c))


def row_parts(rows, blk, wait, body):
    steps = rows // PARTS // blk

    def part(c, carry):
        wait(c)

        def step(i, carry):
            body(pl.multiple_of((c * steps + i) * blk, blk))
            return carry

        return lax.fori_loop(0, steps, step, carry, unroll=4)

    lax.fori_loop(0, PARTS, part, 0)


def start_all(moves):
    for one in moves:
        one.start()


def wait_all(moves):
    for one in moves:
        one.wait()


def interleave(*streams):
    order = sorted(
        ((n + 0.5) / len(stream), which, n)
        for which, stream in enumerate(streams)
        for n in range(len(stream))
    )
    for _, which, n in order:
        streams[which][n]()


def spread_clips(seg_row, seg_b):
    for i in range(seg_b.shape[0] // LANES):
        here = pl.ds(i * LANES, LANES)
        seg_b[here, :] = jnp.broadcast_to(seg_row[:, here], (LANES, LANES)).T


def key_window(j, rows):
    window = min(rows, LANES + 2 * MAX_CLIP)
    here = pl.ds(pl.multiple_of(j * LANES, LANES), LANES)
    first = pl.multiple_of(jnp.clip(j * LANES - MAX_CLIP, 0, rows - window), LANES)
    return here, pl.ds(first, window)


def set_bias(bias, seg_b, seg_row, here, keys):
    filled = jnp.where(seg_b[keys, :] == seg_row[:, here], 0.0, NEG_FILL)
    bias[:, pl.ds(0, LANES)] = filled
    bias[:, pl.ds(LANES, LANES)] = filled


def two_heads(block):
    lane = lax.broadcasted_iota(jnp.int32, block.shape, 1)
    return jnp.concatenate(
        [block * (lane // HEAD_DIM == e).astype(BF16) for e in range(2)], axis=0
    )


def attention_kernel(
    blend, flags, seg_row, vecs, biases, tok, own, oth, w3, wp, *refs
):
    mixed, n1, normed, inv, q, k, v, att, part, lse = refs[-32:-22]
    (
        tok_v, own_v, oth_v, w3_v, wp_v, mixed_v, n1_v, q_v, k_v, v_v, att_v, part_v,
        vt, att_t, seg_b, bias, ones, normed_v, inv_v, in_sems, half_sems, out_sems,
    ) = refs[-22:]
    rows, width = tok.shape
    local = wp.shape[0]
    half_rows = rows // 2
    ratio = blend[0]
    blk = 32
    big = 256

    loads = [
        move(source, target, in_sems.at[n])
        for n, (source, target) in enumerate([(tok, tok_v), (w3, w3_v), (wp, wp_v)])
    ]
    halves = [(own, own_v), (oth, oth_v)]
    loads[0].start()
    start_parts(halves, half_sems)
    start_all(loads[1:])
    early = [
        move(source, target, out_sems.at[n])
        for n, (source, target) in enumerate(
            [
                (mixed_v, mixed), (n1_v, n1), (normed_v, normed), (inv_v, inv),
                (q_v, q), (k_v, k), (v_v, v),
            ]
        )
    ]
    ones[...] = jnp.ones_like(ones)
    spread_clips(seg_row, seg_b)

    loads[0].wait()
    for n, src, half in ((0, own_v, flags[0]), (1, oth_v, 1 - flags[0])):

        def mix(low, src=src, half=half):
            here = pl.ds(pl.multiple_of(half * half_rows + low, blk), blk)
            there = pl.ds(low, blk)
            mine, other = tok_v[here, :].astype(F32), src[there, :].astype(F32)
            blended = ratio * mine + (1.0 - ratio) * other
            mixed_v[here, :] = blended
            centred, scale = row_stats(blended)
            inv_v[here, :] = on_lanes(scale)
            plain = centred * scale
            normed_v[here, :] = plain.astype(BF16)
            n1_v[here, :] = (plain * vecs[0:1, :] + vecs[1:2, :]).astype(BF16)

        row_parts(
            half_rows, blk, lambda c, n=n: wait_all(part_move([halves[n]], half_sems, c, n)), mix
        )
    start_all(early[:4])

    loads[1].wait()
    for i in range(rows // big):
        here = pl.ds(i * big, big)
        rows_in = n1_v[here, :]
        queries = (nn(rows_in, w3_v[0]) + biases[0:1, :local]).astype(BF16).astype(F32)
        q_v[here, :] = (queries * SCORE_SCALE).astype(BF16)
        k_v[here, :] = nn(rows_in, w3_v[1]).astype(BF16)
        values = (nn(rows_in, w3_v[2]) + biases[0:1, local:]).astype(BF16)
        v_v[here, :] = values
        vt[:, here] = values.T
    start_all(early[4:])

    def attend(j, carry):
        here, keys = key_window(j, rows)
        set_bias(bias, seg_b, seg_row, here, keys)
        for p in range(local // LANES):
            pair = pl.ds(p * LANES, LANES)
            scores = nt(k_v[keys, pair], two_heads(q_v[here, pair])) + bias[...]
            top = jnp.max(scores, axis=0, keepdims=True)
            grown = jnp.exp(scores - top).astype(BF16)
            total = nn(ones[...], grown)[:1]
            out = (nn(vt[pair, keys], grown) / total).astype(BF16)
            logs = top + jnp.log(total)
            for e in range(2):
                lanes = slice(e * LANES, e * LANES + LANES)
                head = slice(e * HEAD_DIM, e * HEAD_DIM + HEAD_DIM)
                att_t[pl.ds(p * LANES + e * HEAD_DIM, HEAD_DIM), here] = out[head, lanes]
                lse[pl.ds(2 * p + e, 1), here] = logs[:, lanes]
        return carry

    lax.fori_loop(0, rows // LANES, attend, 0)

    loads[2].wait()
    last = []
    for i in range(rows // big):
        here = pl.ds(i * big, big)
        block = att_t[:, here].T
        att_v[here, :] = block
        part_v[here, :] = nn(block, wp_v[...]).astype(BF16)
        last.append(move(part_v.at[here, :], part.at[here, :], out_sems.at[8 + i]))
        last[-1].start()
    last.append(move(att_v, att, out_sems.at[7]))
    last[-1].start()
    wait_all(early + last)


def attention(blend, flags, segment, vecs, biases, tok, own, oth, w3, wp, *before):
    rows, width = tok.shape
    local = wp.shape[0]
    window = min(rows, LANES + 2 * MAX_CLIP)
    thin = shape((rows, local), BF16)
    tall = shape((rows, width), BF16)
    return pl.pallas_call(
        attention_kernel,
        out_shape=(
            shape((rows, width), F32), tall, tall, shape((rows, LANES), F32),
            thin, thin, thin, thin, tall, shape((local // HEAD_DIM, rows), F32),
        ),
        in_specs=[smem(), smem()] + [vmem()] * 3 + [anywhere()] * 3 + [hbm()] * (2 + len(before)),
        out_specs=[hbm()] * 9 + [vmem()],
        scratch_shapes=[
            pltpu.VMEM((rows, width), BF16),
            pltpu.VMEM((rows // 2, width), BF16),
            pltpu.VMEM((rows // 2, width), BF16),
            pltpu.VMEM(w3.shape, BF16),
            pltpu.VMEM(wp.shape, BF16),
            pltpu.VMEM((rows, width), F32),
            pltpu.VMEM((rows, width), BF16),
            pltpu.VMEM((rows, local), BF16),
            pltpu.VMEM((rows, local), BF16),
            pltpu.VMEM((rows, local), BF16),
            pltpu.VMEM((rows, local), BF16),
            pltpu.VMEM((rows, width), BF16),
            pltpu.VMEM((local, rows), BF16),
            pltpu.VMEM((local, rows), BF16),
            pltpu.VMEM((rows, LANES), F32),
            pltpu.VMEM((window, 2 * LANES), F32),
            pltpu.VMEM((16, window), BF16),
            pltpu.VMEM((rows, width), BF16),
            pltpu.VMEM((rows, LANES), F32),
            pltpu.SemaphoreType.DMA((3,)),
            pltpu.SemaphoreType.DMA((2, PARTS)),
            pltpu.SemaphoreType.DMA((8 + rows // 256,)),
        ],
        compiler_params=params(60),
        cost_estimate=SMALL,
        name="attention",
    )(
        blend, flags, segment, vecs, biases, tok, own, oth, w3, wp, *before,
    )


ERFC_SLOPE = 0.47
ERFC_COEFFS = (
    0.2663094668265691,
    0.2480096137831850,
    0.3362712657560771,
    -0.1262288063821733,
    0.6076790117752645,
    -0.4204702410368928,
    0.0884296765518492,
)


def gelu_parts(pre):
    bell = jnp.exp(pre * pre * -0.5)
    t = 1.0 / (1.0 + jnp.abs(pre) * (ERFC_SLOPE * 0.5**0.5))
    poly = 0.5 * ERFC_COEFFS[-1]
    for coeff in ERFC_COEFFS[-2::-1]:
        poly = poly * t + 0.5 * coeff
    tail = poly * t * bell
    cdf = jnp.where(pre >= 0, 1.0 - tail, tail)
    return pre * cdf, cdf + pre * bell * 0.3989422804014327


def turn_into(target, source, blocks):
    rows = source.shape[0]
    big = 256
    for i in range(rows // big):
        here = pl.ds(i * big, big)
        turned = source[here, :].T
        for start, place, count in blocks:
            target[pl.ds(place, count), here] = turned[start : start + count]


def lead_blocks(width, lead_rows):
    runs = width // lead_rows
    return [
        (run * lead_rows, ((run % 2) * (runs // 2) + run // 2) * lead_rows, lead_rows)
        for run in range(runs)
    ]


def feed_kernel(
    in_rows, out_rows, flags, vecs, biases, mixed, p_own, p_oth, cot, cot_t,
    w_in, w_out, w_out_one, w_out_two,
    hidden, part, gn_part, in_keep, in_send, out_keep, out_send, normed, inv, g_bin, g_bout,
    mixed_v, own_v, oth_v, cot_v, cot_tv, w_in_v, w_out_v, n2, n2_t, act, gp,
    g_in, g_out, normed_v, inv_v, in_sems, turn_sems, weight_sems, out_sems, grad_sems,
):
    rows, width = mixed.shape
    units = w_in.shape[1]
    blk = 32
    big = 256
    sub = 16
    home = flags[1] == 1
    across = flags[2]
    kept_out = jnp.where(home, flags[0], 1 - flags[0]) if in_rows != out_rows else across
    sides = (across, kept_out)

    loads = [(mixed, mixed_v), (p_own, own_v), (p_oth, oth_v), (cot, cot_v)]
    start_parts(loads, in_sems)

    weights = [move(w_in, w_in_v, weight_sems.at[0])]
    weights[0].start()
    half = w_out.shape[0] // 2
    for n, (got, place) in enumerate([(w_out_one, across), (w_out_two, 1 - across)]):
        spot = pl.ds(pl.multiple_of(place * half, half), half)
        sem = weight_sems.at[1 + n]
        weights.append(move(w_out.at[spot, :], w_out_v.at[spot, :], sem))

        @pl.when(home)
        def _(spot=spot, sem=sem):
            move(w_out.at[spot, :], w_out_v.at[spot, :], sem).start()

        @pl.when(jnp.logical_not(home))
        def _(got=got, spot=spot, sem=sem):
            move(got, w_out_v.at[spot, :], sem).start()

    turns = [
        move(cot_t.at[pl.ds(start, count), :], cot_tv.at[pl.ds(place, count), :], turn_sems.at[n])
        for n, (start, place, count) in enumerate(lead_blocks(width, out_rows))
    ]
    start_all(turns)

    g_bout[...] = jnp.zeros_like(g_bout)

    def norm(low):
        here = pl.ds(low, blk)
        attn = own_v[here, :].astype(F32) + oth_v[here, :].astype(F32)
        total = mixed_v[here, :] + attn + vecs[4:5, :]
        mixed_v[here, :] = total
        centred, scale = row_stats(total)
        inv_v[here, :] = on_lanes(scale)
        plain = centred * scale
        normed_v[here, :] = plain.astype(BF16)
        n2[here, :] = (plain * vecs[2:3, :] + vecs[3:4, :]).astype(BF16)
        g_bout[...] += fold_rows(cot_v[here, :].astype(F32))

    row_parts(rows, blk, lambda c: wait_all(part_move(loads, in_sems, c)), norm)
    stores = [
        move(source, target, out_sems.at[0, n])
        for n, (source, target) in enumerate(
            [(mixed_v, hidden), (normed_v, normed), (inv_v, inv)]
        )
    ]
    start_all(stores)
    turn_into(n2_t, n2, lead_blocks(width, in_rows))
    wait_all(weights)

    g_bin[...] = jnp.zeros_like(g_bin)

    def row_block(i):
        here = pl.ds(pl.multiple_of(i * big, big), big)
        for j in range(units // width):
            cols = pl.ds(j * width, width)
            pre_all = nn(n2[here, :], w_in_v[:, cols])
            grad_all = nt(cot_v[here, :], w_out_v[cols, :])
            sums = jnp.zeros((8, width), F32)
            for s in range(big // sub):
                rng = slice(s * sub, s * sub + sub)
                value, slope = gelu_parts(pre_all[rng] + biases[1 + j : 2 + j, :])
                grad = grad_all[rng] * slope
                sums += fold_rows(grad)
                spot = pl.ds(pl.multiple_of(i * big + s * sub, sub), sub)
                act[spot, cols] = value.astype(BF16)
                gp[spot, cols] = grad.astype(BF16)
            g_bin[:, cols] += sums
        oth_v[here, :] = nt(gp[here, :], w_in_v[...]).astype(BF16)
        own_v[here, :] = nn(act[here, :], w_out_v[...]).astype(BF16)
        for n, (source, target) in enumerate([(oth_v, gn_part), (own_v, part)]):
            move(source.at[here, :], target.at[here, :], out_sems.at[1 + n, i]).start()

    def two_blocks(i, carry):
        row_block(2 * i)
        row_block(2 * i + 1)
        return carry

    lax.fori_loop(0, rows // big // 2, two_blocks, 0)
    for i in range(rows // big):
        here = pl.ds(i * big, big)
        for n, (source, target) in enumerate([(oth_v, gn_part), (own_v, part)]):
            stores.append(move(source.at[here, :], target.at[here, :], out_sems.at[1 + n, i]))

    wait_all(turns)
    half = width // 2
    for n, (turned, right, buf, keep, send) in enumerate(
        [(n2_t, gp, g_in, in_keep, in_send), (cot_tv, act, g_out, out_keep, out_send)]
    ):
        for side in range(2):
            lines = pl.ds(side * half, half)
            for j in range(units // width):
                cols = pl.ds(j * width, width)
                buf[side, :, cols] = nn(turned[lines, :], right[:, cols]).astype(BF16)
        for m, (side, target) in enumerate([(1 - sides[n], send), (sides[n], keep)]):
            stores.append(move(buf.at[side], target, grad_sems.at[n, m]))
            stores[-1].start()
    wait_all(stores)


def feed(
    in_rows, out_rows, flags, vecs, biases, mixed, p_own, p_oth, cot, cot_t,
    w_in, w_out, w_out_one, w_out_two,
):
    rows, width = mixed.shape
    units = w_in.shape[1]
    tall = shape((rows, width), BF16)
    grad = shape((width // 2, units), BF16)
    return pl.pallas_call(
        functools.partial(feed_kernel, in_rows, out_rows),
        out_shape=(
            shape((rows, width), F32), tall, tall, grad, grad, grad, grad,
            tall, shape((rows, LANES), F32), shape((8, units), F32), shape((8, width), F32),
        ),
        in_specs=[smem()] + [vmem()] * 2 + [hbm()] * 2 + [anywhere()] + [hbm()] * 6,
        out_specs=[hbm()] * 9 + [vmem()] * 2,
        scratch_shapes=[
            pltpu.VMEM((rows, width), F32),
            pltpu.VMEM((rows, width), BF16),
            pltpu.VMEM((rows, width), BF16),
            pltpu.VMEM((rows, width), BF16),
            pltpu.VMEM((width, rows), BF16),
            pltpu.VMEM(w_in.shape, BF16),
            pltpu.VMEM(w_out.shape, BF16),
            pltpu.VMEM((rows, width), BF16),
            pltpu.VMEM((width, rows), BF16),
            pltpu.VMEM((rows, units), BF16),
            pltpu.VMEM((rows, units), BF16),
            pltpu.VMEM((2, width // 2, units), BF16),
            pltpu.VMEM((2, width // 2, units), BF16),
            pltpu.VMEM((rows, width), BF16),
            pltpu.VMEM((rows, LANES), F32),
            pltpu.SemaphoreType.DMA((4, PARTS)),
            pltpu.SemaphoreType.DMA((width // out_rows,)),
            pltpu.SemaphoreType.DMA((3,)),
            pltpu.SemaphoreType.DMA((3, rows // 256)),
            pltpu.SemaphoreType.DMA((2, 2)),
        ],
        compiler_params=params(60),
        cost_estimate=SMALL,
        name="feed",
    )(
        flags, vecs, biases, mixed, p_own, p_oth, cot, cot_t,
        w_in, w_out, w_out_one, w_out_two,
    )


def attention_back_kernel(
    lead_rows, part_rows, flags, vecs, seg_row, lse, g_bin, g_bout, g_own, g_oth, cot, normed, inv,
    wp, att, k, q, v, w3, n1, normed_one,
    gh, part, keep, send, short,
    gh_v, own_v, oth_v, cot_v, normed_v, inv_v, wp_v, att_v, k_v, q_v, v_v, w3_v, n1_v, one_v, low_v, part_v,
    sums, tails, d_out, kt, dq_t, dk, dv, delta, seg_b, bias, raw, raw_g, low_p, low_g, n1_t, gh_t, grad_v, out,
    in_sems, row_sems, out_sems, last_sems,
):
    rows, width = cot.shape
    local = wp.shape[0]
    blk = 32
    big = 256
    blocks = lead_blocks(width, lead_rows)
    kept_side = flags[2]
    row_loads = [(g_own, own_v), (g_oth, oth_v), (cot, cot_v), (normed, normed_v), (inv, inv_v)]
    start_parts(row_loads, row_sems)
    loads = [
        move(source, target, in_sems.at[n])
        for n, (source, target) in enumerate(
            [
                (wp, wp_v), (att, att_v), (k, k_v), (q, q_v), (v, v_v), (w3, w3_v), (n1, n1_v),
                (normed_one, one_v),
            ]
        )
    ]
    start_all(loads)
    sums[...] = jnp.zeros_like(sums)
    dk[...] = jnp.zeros_like(dk)
    dv[...] = jnp.zeros_like(dv)
    spread_clips(seg_row, seg_b)

    def norm(low):
        here = pl.ds(low, blk)
        grad = own_v[here, :].astype(F32) + oth_v[here, :].astype(F32)
        plain = normed_v[here, :].astype(F32)
        scaled = grad * vecs[2:3, :]
        mean_one = jnp.mean(scaled, axis=-1, keepdims=True)
        mean_two = jnp.mean(scaled * plain, axis=-1, keepdims=True)
        scale = wide_rsqrt(inv_v, here, width)
        back = cot_v[here, :].astype(F32) + scale * (scaled - mean_one - plain * mean_two)
        gh_v[here, :] = back
        low_v[here, :] = back.astype(BF16)
        sums[0] += fold_rows(grad * plain)
        sums[1] += fold_rows(grad)
        sums[2] += fold_rows(back)

    row_parts(rows, blk, lambda c: wait_all(part_move(row_loads, row_sems, c)), norm)
    stores = [move(gh_v, gh, out_sems.at[0])]
    stores[0].start()

    wait_all(loads[:3])
    heads = local // HEAD_DIM
    lane = lax.broadcasted_iota(jnp.int32, (delta.shape[0], local), 1)
    row = lax.broadcasted_iota(jnp.int32, (delta.shape[0], local), 0)
    of_head = (lane // HEAD_DIM == row).astype(BF16)

    def project(i, carry):
        here = pl.ds(pl.multiple_of(i * big, big), big)
        grad_out = nt(low_v[here, :], wp_v[...]).astype(BF16)
        d_out[here, :] = grad_out
        product = grad_out.astype(F32) * att_v[here, :].astype(F32)
        coarse = product.astype(BF16)
        fine = (product - coarse.astype(F32)).astype(BF16)
        delta[:, here] = nt(of_head, coarse) + nt(of_head, fine)
        kt[:, here] = k_v[here, :].T
        return carry

    lax.fori_loop(0, rows // big, project, 0)
    wait_all(loads[3:])

    pairs = heads // 2
    window = bias.shape[0]
    strip = 128
    strips = window // strip

    def attend(j, carry):
        here, keys = key_window(j, rows)
        first = pl.multiple_of(keys.start, LANES)
        set_bias(bias, seg_b, seg_row, here, keys)
        blocks_two = {}

        def two(p):
            if p not in blocks_two:
                pair = pl.ds(p * LANES, LANES)
                blocks_two[p] = (two_heads(q_v[here, pair]), two_heads(d_out[here, pair]))
            return blocks_two[p]

        def at_strip(n):
            return (
                pl.ds(pl.multiple_of(first + n * strip, strip), strip),
                pl.ds(n * strip, strip),
            )

        def products(p):
            pair = pl.ds(p * LANES, LANES)

            def scores(n):
                def run():
                    some, at = at_strip(n)
                    raw[p % 2, at, :] = nt(k_v[some, pair], two(p)[0])

                return run

            def grads(n):
                def run():
                    some, at = at_strip(n)
                    raw_g[p % 2, at, :] = nt(v_v[some, pair], two(p)[1])

                return run

            return [make(n) for n in range(strips) for make in (scores, grads)]

        def softmax_back(p):
            tops = jnp.concatenate([lse[pl.ds(2 * p + e, 1), here] for e in range(2)], axis=1)
            inner = jnp.concatenate([delta[pl.ds(2 * p + e, 1), here] for e in range(2)], axis=1)
            half = strip // 2

            def run_at(n):
                def run():
                    at = pl.ds(n * half, half)
                    probs = jnp.exp(raw[p % 2, at, :] + bias[at, :] - tops)
                    low_p[p % 2, at, :] = probs.astype(BF16)
                    low_g[p % 2, at, :] = (probs * (raw_g[p % 2, at, :] - inner)).astype(BF16)

                return run

            return [run_at(n) for n in range(2 * strips)]

        def sums_of(p):
            pair = pl.ds(p * LANES, LANES)

            def keys_of(n):
                def run():
                    some, at = at_strip(n)
                    dk[some, pair] += nn(low_g[p % 2, at, :], two(p)[0])

                return run

            def values_of(n):
                def run():
                    some, at = at_strip(n)
                    dv[some, pair] += nn(low_p[p % 2, at, :], two(p)[1])

                return run

            def queries():
                grad_q = nn(kt[pair, keys], low_g[p % 2]) * SCORE_SCALE
                for e in range(2):
                    lanes = slice(e * LANES, e * LANES + LANES)
                    head = slice(e * HEAD_DIM, e * HEAD_DIM + HEAD_DIM)
                    dq_t[pl.ds(p * LANES + e * HEAD_DIM, HEAD_DIM), here] = grad_q[head, lanes]

            return [make(n) for n in range(strips) for make in (keys_of, values_of)] + [queries]

        def turns():
            for target, source in ((n1_t, n1_v), (gh_t, low_v)):
                turned = source[here, :].T
                for start, place, count in blocks:
                    target[pl.ds(place, count), here] = turned[start : start + count]

        interleave(products(0), [turns])
        for p in range(pairs):
            matrix = (products(p + 1) if p + 1 < pairs else []) + (sums_of(p - 1) if p else [])
            interleave(softmax_back(p), matrix)
        interleave(sums_of(pairs - 1))
        return carry

    lax.fori_loop(0, rows // LANES, attend, 0)

    tails[...] = jnp.zeros_like(tails)

    def finish(i, carry):
        here = pl.ds(pl.multiple_of(i * big, big), big)
        grad_q, grad_k, grad_val = dq_t[:, here].T, dk[here, :], dv[here, :]
        tails[2, :, pl.ds(0, local)] += fold_rows(grad_q)
        tails[2, :, pl.ds(local, local)] += fold_rows(grad_val)
        lows = [grad.astype(BF16) for grad in (grad_q, grad_k, grad_val)]
        total = sum(nt(low, w3_v[n]) for n, low in enumerate(lows))
        part_v[here, :] = total.astype(BF16)
        tails[0] += fold_rows(total * one_v[here, :].astype(F32))
        tails[1] += fold_rows(total)
        for n, low in enumerate(lows):
            grad_v[here, pl.ds(n * local, local)] = low
        move(part_v.at[here, :], part.at[here, :], last_sems.at[i]).start()
        return carry

    lax.fori_loop(0, rows // big, finish, 0)
    for i in range(rows // big):
        here = pl.ds(i * big, big)
        stores.append(move(part_v.at[here, :], part.at[here, :], last_sems.at[i]))
    units = g_bin.shape[1]
    listed = [tails[0], tails[1], sums[0], sums[1], sums[2], g_bout[...], tails[2]]
    listed += [g_bin[:, pl.ds(n, width)] for n in range(0, units, width)]
    half = width // 2
    listed = [row_sum(block) for block in listed]
    for n, block in enumerate(listed):
        short[pl.ds(n, 1), :] = block
    if part_rows:
        sources = [
            (jnp.concatenate(listed[:6] + [jnp.zeros((2, width), F32)], axis=0), part_rows),
            (jnp.broadcast_to(listed[6][:, :local], (8, local)), local * part_rows // width),
            (jnp.broadcast_to(listed[6][:, local:], (8, local)), local * part_rows // width),
            (
                jnp.broadcast_to(jnp.concatenate(listed[7:], axis=1), (8, units)),
                units * part_rows // width,
            ),
        ]
        rest = jnp.zeros((part_rows - 8 * len(sources), LANES), F32)
        for start, place, count in blocks:
            for row in range(0, count, part_rows):
                d = (start + row) // part_rows
                parts = [
                    pltpu.roll(source, (source.shape[1] - d * size) % source.shape[1], 1)[:, :LANES]
                    for source, size in sources
                ]
                side, at = divmod(place + row, half)
                out[side, pl.ds(at, part_rows), pl.ds(4 * local, LANES)] = jnp.concatenate(
                    parts + [rest], axis=0
                ).astype(BF16)
    for side in range(2):
        lines = pl.ds(side * half, half)
        for n in range(3):
            cols = pl.ds(n * local, local)
            out[side, :, cols] = nn(n1_t[lines, :], grad_v[:, cols]).astype(BF16)
        out[side, :, pl.ds(3 * local, local)] = nn(gh_t[lines, :], att_v[...]).astype(BF16)
    for n, (side, target) in enumerate([(1 - kept_side, send), (kept_side, keep)]):
        stores.append(move(out.at[side], target, out_sems.at[1 + n]))
        stores[-1].start()
    wait_all(stores)


def attention_back(
    lead_rows, part_rows, flags, vecs, segment, lse, g_bin, g_bout, g_own, g_oth, cot, normed, inv,
    wp, att, k, q, v, w3, n1, normed_one,
):
    rows, width = cot.shape
    local = wp.shape[0]
    window = min(rows, LANES + 2 * MAX_CLIP)
    tall, thin = pltpu.VMEM((rows, width), BF16), pltpu.VMEM((rows, local), BF16)
    turned = pltpu.VMEM((width, rows), BF16)
    half = (width // 2, 4 * local + (LANES if part_rows else 0))
    return pl.pallas_call(
        functools.partial(attention_back_kernel, lead_rows, part_rows),
        out_shape=(
            shape((rows, width), F32),
            shape((rows, width), BF16),
            shape(half, BF16),
            shape(half, BF16),
            shape((7 + g_bin.shape[1] // width, width), F32),
        ),
        in_specs=[smem()] + [vmem()] * 5 + [hbm()] + [anywhere()] + [hbm()] * 11,
        out_specs=[hbm()] * 4 + [vmem()],
        scratch_shapes=[
            pltpu.VMEM((rows, width), F32),
            tall, tall, tall, tall,
            pltpu.VMEM((rows, LANES), F32),
            pltpu.VMEM(wp.shape, BF16),
            thin, thin, thin, thin,
            pltpu.VMEM(w3.shape, BF16),
            tall, tall, tall, tall,
            pltpu.VMEM((3, 8, width), F32),
            pltpu.VMEM((3, 8, width), F32),
            thin,
            pltpu.VMEM((local, rows), BF16),
            pltpu.VMEM((local, rows), F32),
            pltpu.VMEM((rows, local), F32),
            pltpu.VMEM((rows, local), F32),
            pltpu.VMEM((8, rows), F32),
            pltpu.VMEM((rows, LANES), F32),
            pltpu.VMEM((window, 2 * LANES), F32),
            pltpu.VMEM((2, window, 2 * LANES), F32),
            pltpu.VMEM((2, window, 2 * LANES), F32),
            pltpu.VMEM((2, window, 2 * LANES), BF16),
            pltpu.VMEM((2, window, 2 * LANES), BF16),
            turned, turned,
            pltpu.VMEM((rows, 3 * local), BF16),
            pltpu.VMEM((2,) + half, BF16),
            pltpu.SemaphoreType.DMA((8,)),
            pltpu.SemaphoreType.DMA((5, PARTS)),
            pltpu.SemaphoreType.DMA((3,)),
            pltpu.SemaphoreType.DMA((rows // 256,)),
        ],
        compiler_params=params(60),
        cost_estimate=SMALL,
        name="attention_back",
    )(
        flags, vecs, segment, lse, g_bin, g_bout, g_own, g_oth, cot, normed, inv,
        wp, att, k, q, v, w3, n1, normed_one,
    )


def mixed_back_kernel(blend, flags, vecs, gh, g_own, g_oth, normed, inv, outgoing, kept, *refs):
    gh_v, own_v, oth_v, normed_v, inv_v, leave_v, kept_v, in_sems, out_sems, leave_sems = refs
    ratio = blend[0]
    rows, width = gh.shape
    blk = 32
    piece = leave_v.shape[1]
    loads = [(gh, gh_v), (g_own, own_v), (g_oth, oth_v), (normed, normed_v), (inv, inv_v)]
    stores = [(kept_v, kept)]
    start_parts(loads, in_sems)

    def norm(low):
        here = pl.ds(low, blk)
        grad = own_v[here, :].astype(F32) + oth_v[here, :].astype(F32)
        plain = normed_v[here, :].astype(F32)
        scaled = grad * vecs[0:1, :]
        mean_one = jnp.mean(scaled, axis=-1, keepdims=True)
        mean_two = jnp.mean(scaled * plain, axis=-1, keepdims=True)
        scale = wide_rsqrt(inv_v, here, width)
        back = gh_v[here, :] + scale * (scaled - mean_one - plain * mean_two)
        leave = ((1.0 - ratio) * back).astype(BF16)
        leave_v[pl.ds(low // piece, blk // piece)] = leave.reshape(blk // piece, piece, width)
        kept_v[here, :] = (ratio * back).astype(BF16)

    row_parts(rows, blk, lambda c: wait_all(part_move(loads, in_sems, c)), norm)
    start_parts(stores, out_sems)
    if len(outgoing.shape) == 3:
        leaves = [move(leave_v, outgoing, leave_sems.at[0])]
    else:
        count = outgoing.shape[0]
        leaves = [
            move(
                leave_v.at[pl.ds(pl.multiple_of((2 * m + flags[0]) * count, count), count)],
                outgoing.at[:, m],
                leave_sems.at[m],
            )
            for m in range(2)
        ]
    start_all(leaves)
    for c in range(PARTS):
        wait_all(part_move(stores, out_sems, c))
    wait_all(leaves)


def mixed_back(piece, ordered, blend, flags, vecs, gh, g_own, g_oth, normed, inv):
    rows, width = gh.shape
    tall = pltpu.VMEM((rows, width), BF16)
    runs = rows // piece
    dims = (runs // 4, 2, piece, width) if ordered else (runs, piece, width)
    return pl.pallas_call(
        mixed_back_kernel,
        out_shape=(shape(dims, BF16), shape((rows, width), BF16)),
        in_specs=[smem(), smem(), vmem()] + [hbm()] * 2 + [anywhere()] + [hbm()] * 2,
        out_specs=[hbm(), hbm()],
        scratch_shapes=[
            pltpu.VMEM((rows, width), F32),
            tall, tall, tall, pltpu.VMEM((rows, LANES), F32),
            pltpu.VMEM((runs, piece, width), BF16),
            tall,
            pltpu.SemaphoreType.DMA((5, PARTS)),
            pltpu.SemaphoreType.DMA((1, PARTS)),
            pltpu.SemaphoreType.DMA((2,)),
        ],
        compiler_params=params(60),
        cost_estimate=SMALL,
        name="mixed_back",
    )(blend, flags, vecs, gh, g_own, g_oth, normed, inv)


def shards(
    tokens,
    mix_blend,
    partner,
    clip_ids,
    gain_one,
    shift_one,
    qkv_weight,
    qv_bias,
    proj_weight,
    proj_bias,
    gain_two,
    shift_two,
    in_weight,
    in_bias,
    out_weight,
    out_bias,
    cotangent,
):
    rows, width = tokens.shape
    dp_count = lax.axis_size("dp")
    both = ("dp", "mp")
    bits = dp_count.bit_length() - 1
    seq = lax.axis_index("dp")
    mp = lax.axis_index("mp")
    core = lax.rem(seq, 2)
    home = core == mp
    all_dp = range(dp_count)

    def joint(d, m):
        return 2 * d + m

    core_swap = [(d, d ^ 1) for d in all_dp]
    home_to_pair = [(joint(d, d & 1), joint(d, 1 - (d & 1))) for d in all_dp]
    pair_to_home = [(joint(d, 1 - (d & 1)), joint(d, d & 1)) for d in all_dp]
    weight_move = home_to_pair + [
        (joint(d, 1 - (d & 1)), joint(d ^ 1, 1 - (d & 1))) for d in all_dp
    ]

    def swap(value):
        return lax.ppermute(value, "dp", core_swap)

    def chip_value(value):
        return jnp.where(home, value, swap(value))

    def after(value, *others):
        return lax.optimization_barrier((value,) + others)[0]

    def half_weight(value):
        return lax.ppermute(value, both, weight_move)

    part_rows = width // dp_count
    lead = min(n for n in range(1, bits) if (part_rows << n) % 16 == 0)
    lead_rows = part_rows << lead
    across = lax.rem(seq >> lead, 2)
    flags = jnp.stack([core, home.astype(jnp.int32), across]).astype(jnp.int32)

    def taken(value, index, axis):
        return lax.dynamic_index_in_dim(value, index, axis, keepdims=False)

    seq_small = chip_value(jnp.concatenate([mix_blend, clip_ids[0].astype(F32)]))
    blend, segment = seq_small[:1], seq_small[1:].reshape(1, rows)
    local = proj_weight.shape[0]
    units = in_bias.shape[0]
    half_small = jnp.concatenate([qv_bias.reshape(-1), in_bias])
    half_small = jnp.where(home, half_small, half_weight(half_small))
    biases = half_small.reshape(-1, width)
    vecs = jnp.stack([gain_one, shift_one, gain_two, shift_two, proj_bias])

    w3 = half_weight(qkv_weight.transpose(1, 0, 2))
    wp = half_weight(proj_weight)

    def two_way(value):
        halves = value.reshape(2, value.shape[0] // 2, value.shape[1])
        one = half_weight(taken(halves, across, 0))
        moves = [(joint(d, 1 - (d & 1)), joint(d ^ (1 << lead), 1 - (d & 1))) for d in all_dp]
        return value, one, lax.ppermute(one, both, moves)

    ids = jnp.arange(2 * dp_count, dtype=jnp.int32)
    piece = rows // (2 * 2 * dp_count)
    sent = tokens.reshape(2, dp_count, 2, piece, width)
    sent = lax.dynamic_index_in_dim(sent, mp, 2, keepdims=False)
    spread = lax.all_to_all(sent.transpose(1, 0, 2, 3), "dp", 0, 0, tiled=True)
    wanted = partner[(ids // 4) * 2 + ids % 2] * 2 + (ids // 2) % 2
    source_of = jnp.sum(
        jnp.where(partner[:, None] == ids[None, :dp_count], ids[:dp_count, None], 0),
        axis=0,
        dtype=jnp.int32,
    )
    source = source_of[ids // 2]
    wanted_back = (source // 2) * 4 + (ids % 2) * 2 + source % 2
    chosen = pick(spread.reshape(2 * dp_count, piece, width), wanted, w3, wp, half_small)
    partner_own = lax.all_to_all(chosen, both, 0, 0, tiled=True).reshape(rows // 2, width)
    w_out = two_way(out_weight)
    w_in = half_weight(after(in_weight, w_out[1]))

    tok = chip_value(tokens)
    cot = chip_value(cotangent)
    cot_t = cot.T
    partner_oth = swap(after(partner_own, tok, cot, vecs, segment, wanted_back))

    mixed, n1, normed_one, inv_one, q, k, v, att, attn_part, lse = attention(
        blend, flags, segment, vecs, biases, tok, partner_own, partner_oth, w3, wp, w_out[2], cot_t
    )
    pair_first = part_rows % 16 == 0
    fed = feed(
        lead_rows, part_rows if pair_first else lead_rows, flags, vecs, biases,
        mixed, attn_part, swap(attn_part), cot, cot_t, w_in, *w_out,
    )
    hidden, out_part, gn2_part, in_keep, in_send, out_keep, out_send = fed[:7]
    normed_two, inv_two, g_bin, g_bout = fed[7:]
    gn2_oth = swap(gn2_part)

    high, mid = dp_count >> (lead + 1), 1 << (lead - 1)
    pair_and_core = pair_to_home + [(joint(d, d & 1), joint(d ^ 1, d & 1)) for d in all_dp]
    pair_diagonal = [(joint(d, 1 - (d & 1)), joint(d ^ 1, d & 1)) for d in all_dp]

    def total(*terms):
        return sum(term.astype(F32) for term in terms)

    def send_across(value):
        return lax.ppermute(value, "dp", [(d, d ^ (1 << lead)) for d in all_dp])

    def send_pair(value):
        value = value.reshape(high, mid, 2, part_rows, -1)
        one = lax.ppermute(taken(value, jnp.where(home, 1 - core, core), 2), both, pair_and_core)
        two = lax.ppermute(taken(value, 1 - core, 2), both, pair_diagonal)
        held = taken(value, core, 2)
        return jnp.where(home, held, jnp.zeros_like(held)), one, two

    def far(value, *others):
        for shift, left in ((1, mid), (lead + 1, high)):
            while left > 1:
                radix = min(4, left)
                left //= radix
                value = value.reshape((-1, left, radix) + value.shape[-2:]).astype(BF16)
                spot = lax.rem(seq >> shift, radix)
                got = [
                    lax.ppermute(
                        taken(value, spot ^ flip, 2),
                        "dp",
                        [(d, d ^ (flip << shift)) for d in all_dp],
                    )
                    for flip in range(1, radix)
                ]
                value = total(taken(value, spot, 2), *after(got, *others))
                shift += radix.bit_length() - 1
        return value.reshape(value.shape[-2:])

    def send_first(keep, send):
        if not pair_first:
            return [keep, send_across(send)]
        one = lax.ppermute(send, both, pair_and_core)
        two = lax.ppermute(keep, both, pair_diagonal)
        return [jnp.where(home, keep, jnp.zeros_like(keep)), one, two]

    def send_second(value):
        if not pair_first:
            return send_pair(value)
        value = value.reshape(high, 2, mid, part_rows, -1)
        return taken(value, across, 1), send_across(taken(value, 1 - across, 1))

    in_got = send_across(in_send)
    out_first = send_first(out_keep, out_send)
    gh, gn1_part, attn_keep, attn_send, short = attention_back(
        lead_rows, part_rows if pair_first else 0, flags, vecs, segment, lse, g_bin, g_bout,
        gn2_part, gn2_oth, cot, normed_two, inv_two, wp, att, k, q, v, w3, n1, normed_one,
    )
    gn1_oth = swap(after(gn1_part, in_got, *out_first))
    attn_first = [attn_keep, send_across(attn_send)]
    in_terms = send_pair(total(in_keep, in_got).astype(BF16))
    ordered = piece % 16 == 0
    outgoing, kept = mixed_back(
        piece if ordered else 16, ordered, blend, flags, vecs, gh, gn1_part, gn1_oth, normed_one, inv_one
    )

    if ordered:
        leaving = outgoing.reshape(2 * dp_count, piece, width)
    else:
        leaving = taken(outgoing.reshape(2, 2, dp_count, piece, width), core, 1)
        leaving = leaving.transpose(1, 0, 2, 3).reshape(2 * dp_count, piece, width)
    back = lax.all_to_all(leaving, both, 0, 0, tiled=True)

    in_value = total(*after(in_terms, leaving)).astype(BF16)
    sum_in = far(in_value)
    out_oth = swap(after(out_part, leaving))
    out_value = total(*after(out_first, in_value)).astype(BF16)
    out_terms = send_second(out_value)
    attn_value = total(*after(attn_first, out_value)).astype(BF16)
    attn_terms = send_pair(attn_value)
    block = hidden + (out_part.astype(F32) + after(out_oth, attn_value).astype(F32)) + out_bias
    block = block.astype(BF16)
    kept = kept.reshape(2, rows // 2, width)
    kept_got = half_weight(taken(kept, 1 - mp, 0))
    block_got = half_weight(block)

    def side_by_side(*groups):
        values = [total(*terms).reshape(high * mid, part_rows, -1) for terms in groups]
        return jnp.concatenate(values, axis=2).astype(BF16)

    returning = pick(back, wanted_back, attn_value, sum_in)
    returned = lax.all_to_all(
        returning.reshape(dp_count, 2, piece, width), "dp", 0, 0, tiled=True
    )
    returned = after(returned, kept_got)
    kept = jnp.where(home, taken(kept, mp, 0), kept_got)
    returned = returned.transpose(1, 0, 2, 3).reshape(rows // 2, width)
    mine = (kept.astype(F32) + returned.astype(F32)).astype(BF16)
    other = lax.ppermute(mine, "mp", [(0, 1), (1, 0)])
    block_out = jnp.where(home, block, after(block_got, mine))
    grad_tokens = jnp.where(
        jnp.arange(2)[:, None, None] == mp, mine[None], other[None]
    ).reshape(rows, width)

    marker = swap(returning[0, :, :LANES])
    summed = far(
        side_by_side(*(after(terms, marker) for terms in (out_terms, attn_terms))),
        mine,
    )
    sum_out, sum_attn = after(summed[:, :units], other), summed[:, units:]
    sum_qkv = sum_attn[:, : 3 * local].reshape(-1, 3, local)
    sum_proj = sum_attn[:, 3 * local : 4 * local].T
    quarter, eighth = local // dp_count, units // dp_count
    if pair_first:
        extra = sum_attn[:, 4 * local :]
        plain = extra[:6, :part_rows]
        ours = plain[:2] + lax.ppermute(plain[:2], "mp", [(0, 1), (1, 0)])
        plain = jnp.concatenate([ours, plain[2:]])
        sum_qv = jnp.stack([extra[8, :quarter], extra[16, :quarter]])
        sum_bin = extra[24, :eighth]
    else:
        counts = jnp.where((core == 0) | (jnp.arange(6) < 2), 1.0, 0.0).astype(F32)
        wide = (short[:6] * counts[:, None]).reshape(6, dp_count, 1, part_rows)
        wide = jnp.broadcast_to(wide, (6, dp_count, 2, part_rows)).transpose(1, 2, 0, 3)
        to_half = (jnp.arange(2) == core)[None, :, None]

        def half_terms(vectors):
            terms = vectors.reshape(vectors.shape[0], dp_count, -1).transpose(1, 0, 2)
            return jnp.where(to_half, terms.reshape(dp_count, 1, -1), 0.0)

        short = jnp.concatenate(
            [
                wide.reshape(dp_count, 2, -1),
                half_terms(short[6].reshape(2, local)),
                half_terms(short[7:].reshape(1, units)),
            ],
            axis=-1,
        ).reshape(2 * dp_count, -1)
        short = jnp.sum(lax.all_to_all(short, both, 0, 0, tiled=True), axis=0)
        plain = short[: 6 * part_rows].reshape(6, part_rows)
        sum_qv = short[6 * part_rows : 6 * part_rows + 2 * quarter].reshape(2, -1)
        sum_bin = short[6 * part_rows + 2 * quarter :]
    return (
        block_out,
        grad_tokens,
        plain[0],
        plain[1],
        sum_qkv,
        sum_qv,
        sum_proj,
        plain[4],
        plain[2],
        plain[3],
        sum_in,
        sum_bin,
        sum_out.T,
        plain[5],
    )


def solution(mesh):
    return jax.shard_map(
        shards,
        mesh=mesh,
        in_specs=(
            P("dp", None),
            P("dp"),
            P(),
            P("dp", None),
            P(),
            P(),
            P(None, None, "mp"),
            P(None, "mp"),
            P("mp", None),
            P(),
            P(),
            P(),
            P(None, "mp"),
            P("mp"),
            P("mp", None),
            P(),
            P("dp", None),
        ),
        out_specs=(
            P("dp", None),
            P("dp", None),
            P("dp"),
            P("dp"),
            P("dp", None, "mp"),
            P(None, ("mp", "dp")),
            P("mp", "dp"),
            P("dp"),
            P("dp"),
            P("dp"),
            P("dp", "mp"),
            P(("mp", "dp")),
            P("mp", "dp"),
            P("dp"),
        ),
        check_vma=False,
    )
```

```python
import functools

import jax
import jax.numpy as jnp
from jax import lax
from jax.experimental import pallas as pl
from jax.experimental.pallas import tpu as pltpu
from jax.sharding import PartitionSpec as P

HEAD_DIM = 64
NORM_EPS = 1e-06
NEG_FILL = -1e30
SCORE_SCALE = HEAD_DIM ** (-0.5)
MAX_CLIP = 256
LANES = 128
F32 = jnp.float32
BF16 = jnp.bfloat16
MIB = 1 << 20
SMALL = pl.CostEstimate(flops=1 << 20, bytes_accessed=1 << 20, transcendentals=0)


def nn(left, right):
    return lax.dot_general(left, right, (((1,), (0,)), ((), ())), preferred_element_type=F32)


def nt(left, right):
    return lax.dot_general(left, right, (((1,), (1,)), ((), ())), preferred_element_type=F32)


def vmem():
    return pl.BlockSpec(memory_space=pltpu.VMEM)


def hbm():
    return pl.BlockSpec(memory_space=pltpu.HBM)


def anywhere():
    return pl.BlockSpec(memory_space=pl.ANY)


def smem():
    return pl.BlockSpec(memory_space=pltpu.SMEM)


def params(mib):
    return pltpu.CompilerParams(vmem_limit_bytes=mib * MIB)


def shape(dims, dtype):
    return jax.ShapeDtypeStruct(dims, dtype)


def row_stats(vector):
    mean = jnp.mean(vector, axis=-1, keepdims=True)
    centred = vector - mean
    spread = jnp.mean(centred * centred, axis=-1, keepdims=True)
    return centred, lax.rsqrt(spread + NORM_EPS)


def on_lanes(column):
    return jnp.broadcast_to(column, (column.shape[0], LANES))


def wide_rsqrt(inv, here, width):
    return jnp.concatenate([inv[here, :]] * (width // LANES), axis=1)


def row_sum(block):
    return jnp.sum(block, axis=0, keepdims=True)


def fold_rows(block):
    rows, width = block.shape
    return jnp.sum(block.reshape(rows // 8, 8, width), axis=0)


def pick_kernel(index, source, *refs):
    picked = refs[-1]

    def move(i, carry):
        picked[i] = source[index[i]]
        return carry

    lax.fori_loop(0, picked.shape[0], move, 0, unroll=4)


def pick(source, index, *after):
    dims = index.shape + source.shape[1:]
    return pl.pallas_call(
        pick_kernel,
        out_shape=shape(dims, source.dtype),
        in_specs=[smem(), vmem()] + [hbm()] * len(after),
        out_specs=vmem(),
        compiler_params=params(16),
        cost_estimate=SMALL,
        name="pick",
    )(index, source, *after)


def move(source, target, sem):
    return pltpu.make_async_copy(source, target, sem)


PARTS = 4


def part_move(pairs, sems, c, first=0):
    moves = []
    for n, (source, target) in enumerate(pairs):
        count = source.shape[0] // PARTS
        here = pl.ds(pl.multiple_of(c * count, count), count)
        moves.append(move(source.at[here, :], target.at[here, :], sems.at[first + n, c]))
    return moves


def start_parts(pairs, sems):
    for c in range(PARTS):
        start_all(part_move(pairs, sems, c))


def row_parts(rows, blk, wait, body):
    steps = rows // PARTS // blk

    def part(c, carry):
        wait(c)

        def step(i, carry):
            body(pl.multiple_of((c * steps + i) * blk, blk))
            return carry

        return lax.fori_loop(0, steps, step, carry, unroll=4)

    lax.fori_loop(0, PARTS, part, 0)


def start_all(moves):
    for one in moves:
        one.start()


def wait_all(moves):
    for one in moves:
        one.wait()


def interleave(*streams):
    order = sorted(
        ((n + 0.5) / len(stream), which, n)
        for which, stream in enumerate(streams)
        for n in range(len(stream))
    )
    for _, which, n in order:
        streams[which][n]()


def spread_clips(seg_row, seg_b):
    for i in range(seg_b.shape[0] // LANES):
        here = pl.ds(i * LANES, LANES)
        seg_b[here, :] = jnp.broadcast_to(seg_row[:, here], (LANES, LANES)).T


def key_window(j, rows):
    window = min(rows, LANES + 2 * MAX_CLIP)
    here = pl.ds(pl.multiple_of(j * LANES, LANES), LANES)
    first = pl.multiple_of(jnp.clip(j * LANES - MAX_CLIP, 0, rows - window), LANES)
    return here, pl.ds(first, window)


def set_bias(bias, seg_b, seg_row, here, keys):
    filled = jnp.where(seg_b[keys, :] == seg_row[:, here], 0.0, NEG_FILL)
    bias[:, pl.ds(0, LANES)] = filled
    bias[:, pl.ds(LANES, LANES)] = filled


def two_heads(block):
    lane = lax.broadcasted_iota(jnp.int32, block.shape, 1)
    return jnp.concatenate(
        [block * (lane // HEAD_DIM == e).astype(BF16) for e in range(2)], axis=0
    )


def attention_kernel(
    blend, flags, seg_row, vecs, biases, tok, own, oth, w3, wp, *refs
):
    mixed, n1, normed, inv, q, k, v, att, part, lse = refs[-32:-22]
    (
        tok_v, own_v, oth_v, w3_v, wp_v, mixed_v, n1_v, q_v, k_v, v_v, att_v, part_v,
        vt, att_t, seg_b, bias, ones, normed_v, inv_v, in_sems, half_sems, out_sems,
    ) = refs[-22:]
    rows, width = tok.shape
    local = wp.shape[0]
    half_rows = rows // 2
    ratio = blend[0]
    blk = 32
    big = 256

    loads = [
        move(source, target, in_sems.at[n])
        for n, (source, target) in enumerate([(tok, tok_v), (w3, w3_v), (wp, wp_v)])
    ]
    halves = [(own, own_v), (oth, oth_v)]
    loads[0].start()
    start_parts(halves, half_sems)
    start_all(loads[1:])
    early = [
        move(source, target, out_sems.at[n])
        for n, (source, target) in enumerate(
            [
                (mixed_v, mixed), (n1_v, n1), (normed_v, normed), (inv_v, inv),
                (q_v, q), (k_v, k), (v_v, v),
            ]
        )
    ]
    ones[...] = jnp.ones_like(ones)
    spread_clips(seg_row, seg_b)

    loads[0].wait()
    for n, src, half in ((0, own_v, flags[0]), (1, oth_v, 1 - flags[0])):

        def mix(low, src=src, half=half):
            here = pl.ds(pl.multiple_of(half * half_rows + low, blk), blk)
            there = pl.ds(low, blk)
            mine, other = tok_v[here, :].astype(F32), src[there, :].astype(F32)
            blended = ratio * mine + (1.0 - ratio) * other
            mixed_v[here, :] = blended
            centred, scale = row_stats(blended)
            inv_v[here, :] = on_lanes(scale)
            plain = centred * scale
            normed_v[here, :] = plain.astype(BF16)
            n1_v[here, :] = (plain * vecs[0:1, :] + vecs[1:2, :]).astype(BF16)

        row_parts(
            half_rows, blk, lambda c, n=n: wait_all(part_move([halves[n]], half_sems, c, n)), mix
        )
    start_all(early[:4])

    loads[1].wait()
    for i in range(rows // big):
        here = pl.ds(i * big, big)
        rows_in = n1_v[here, :]
        queries = (nn(rows_in, w3_v[0]) + biases[0:1, :local]).astype(BF16).astype(F32)
        q_v[here, :] = (queries * SCORE_SCALE).astype(BF16)
        k_v[here, :] = nn(rows_in, w3_v[1]).astype(BF16)
        values = (nn(rows_in, w3_v[2]) + biases[0:1, local:]).astype(BF16)
        v_v[here, :] = values
        vt[:, here] = values.T
    start_all(early[4:])

    def attend(j, carry):
        here, keys = key_window(j, rows)
        set_bias(bias, seg_b, seg_row, here, keys)
        for p in range(local // LANES):
            pair = pl.ds(p * LANES, LANES)
            scores = nt(k_v[keys, pair], two_heads(q_v[here, pair])) + bias[...]
            top = jnp.max(scores, axis=0, keepdims=True)
            grown = jnp.exp(scores - top).astype(BF16)
            total = nn(ones[...], grown)[:1]
            out = (nn(vt[pair, keys], grown) / total).astype(BF16)
            logs = top + jnp.log(total)
            for e in range(2):
                lanes = slice(e * LANES, e * LANES + LANES)
                head = slice(e * HEAD_DIM, e * HEAD_DIM + HEAD_DIM)
                att_t[pl.ds(p * LANES + e * HEAD_DIM, HEAD_DIM), here] = out[head, lanes]
                lse[pl.ds(2 * p + e, 1), here] = logs[:, lanes]
        return carry

    lax.fori_loop(0, rows // LANES, attend, 0)

    loads[2].wait()
    last = []
    for i in range(rows // big):
        here = pl.ds(i * big, big)
        block = att_t[:, here].T
        att_v[here, :] = block
        part_v[here, :] = nn(block, wp_v[...]).astype(BF16)
        last.append(move(part_v.at[here, :], part.at[here, :], out_sems.at[8 + i]))
        last[-1].start()
    last.append(move(att_v, att, out_sems.at[7]))
    last[-1].start()
    wait_all(early + last)


def attention(blend, flags, segment, vecs, biases, tok, own, oth, w3, wp, *before):
    rows, width = tok.shape
    local = wp.shape[0]
    window = min(rows, LANES + 2 * MAX_CLIP)
    thin = shape((rows, local), BF16)
    tall = shape((rows, width), BF16)
    return pl.pallas_call(
        attention_kernel,
        out_shape=(
            shape((rows, width), F32), tall, tall, shape((rows, LANES), F32),
            thin, thin, thin, thin, tall, shape((local // HEAD_DIM, rows), F32),
        ),
        in_specs=[smem(), smem()] + [vmem()] * 3 + [anywhere()] * 3 + [hbm()] * (2 + len(before)),
        out_specs=[hbm()] * 9 + [vmem()],
        scratch_shapes=[
            pltpu.VMEM((rows, width), BF16),
            pltpu.VMEM((rows // 2, width), BF16),
            pltpu.VMEM((rows // 2, width), BF16),
            pltpu.VMEM(w3.shape, BF16),
            pltpu.VMEM(wp.shape, BF16),
            pltpu.VMEM((rows, width), F32),
            pltpu.VMEM((rows, width), BF16),
            pltpu.VMEM((rows, local), BF16),
            pltpu.VMEM((rows, local), BF16),
            pltpu.VMEM((rows, local), BF16),
            pltpu.VMEM((rows, local), BF16),
            pltpu.VMEM((rows, width), BF16),
            pltpu.VMEM((local, rows), BF16),
            pltpu.VMEM((local, rows), BF16),
            pltpu.VMEM((rows, LANES), F32),
            pltpu.VMEM((window, 2 * LANES), F32),
            pltpu.VMEM((16, window), BF16),
            pltpu.VMEM((rows, width), BF16),
            pltpu.VMEM((rows, LANES), F32),
            pltpu.SemaphoreType.DMA((3,)),
            pltpu.SemaphoreType.DMA((2, PARTS)),
            pltpu.SemaphoreType.DMA((8 + rows // 256,)),
        ],
        compiler_params=params(60),
        cost_estimate=SMALL,
        name="attention",
    )(
        blend, flags, segment, vecs, biases, tok, own, oth, w3, wp, *before,
    )


ERFC_SLOPE = 0.47
ERFC_COEFFS = (
    0.2663094668265691,
    0.2480096137831850,
    0.3362712657560771,
    -0.1262288063821733,
    0.6076790117752645,
    -0.4204702410368928,
    0.0884296765518492,
)


def gelu_parts(pre):
    bell = jnp.exp(pre * pre * -0.5)
    t = 1.0 / (1.0 + jnp.abs(pre) * (ERFC_SLOPE * 0.5**0.5))
    poly = 0.5 * ERFC_COEFFS[-1]
    for coeff in ERFC_COEFFS[-2::-1]:
        poly = poly * t + 0.5 * coeff
    tail = poly * t * bell
    cdf = jnp.where(pre >= 0, 1.0 - tail, tail)
    return pre * cdf, cdf + pre * bell * 0.3989422804014327


def turn_into(target, source, blocks):
    rows = source.shape[0]
    big = 256
    for i in range(rows // big):
        here = pl.ds(i * big, big)
        turned = source[here, :].T
        for start, place, count in blocks:
            target[pl.ds(place, count), here] = turned[start : start + count]


def lead_blocks(width, lead_rows):
    runs = width // lead_rows
    return [
        (run * lead_rows, ((run % 2) * (runs // 2) + run // 2) * lead_rows, lead_rows)
        for run in range(runs)
    ]


def feed_kernel(
    in_rows, out_rows, flags, vecs, biases, mixed, p_own, p_oth, cot, cot_t,
    w_in, w_out, w_out_one, w_out_two,
    hidden, part, gn_part, in_keep, in_send, out_keep, out_send, normed, inv, g_bin, g_bout,
    mixed_v, own_v, oth_v, cot_v, cot_tv, w_in_v, w_out_v, n2, n2_t, act, gp,
    g_in, g_out, normed_v, inv_v, in_sems, turn_sems, weight_sems, out_sems, grad_sems,
):
    rows, width = mixed.shape
    units = w_in.shape[1]
    blk = 32
    big = 256
    sub = 16
    home = flags[1] == 1
    across = flags[2]
    kept_out = jnp.where(home, flags[0], 1 - flags[0]) if in_rows != out_rows else across
    sides = (across, kept_out)

    loads = [(mixed, mixed_v), (p_own, own_v), (p_oth, oth_v), (cot, cot_v)]
    start_parts(loads, in_sems)

    weights = [move(w_in, w_in_v, weight_sems.at[0])]
    weights[0].start()
    half = w_out.shape[0] // 2
    for n, (got, place) in enumerate([(w_out_one, across), (w_out_two, 1 - across)]):
        spot = pl.ds(pl.multiple_of(place * half, half), half)
        sem = weight_sems.at[1 + n]
        weights.append(move(w_out.at[spot, :], w_out_v.at[spot, :], sem))

        @pl.when(home)
        def _(spot=spot, sem=sem):
            move(w_out.at[spot, :], w_out_v.at[spot, :], sem).start()

        @pl.when(jnp.logical_not(home))
        def _(got=got, spot=spot, sem=sem):
            move(got, w_out_v.at[spot, :], sem).start()

    turns = [
        move(cot_t.at[pl.ds(start, count), :], cot_tv.at[pl.ds(place, count), :], turn_sems.at[n])
        for n, (start, place, count) in enumerate(lead_blocks(width, out_rows))
    ]
    start_all(turns)

    g_bout[...] = jnp.zeros_like(g_bout)

    def norm(low):
        here = pl.ds(low, blk)
        attn = own_v[here, :].astype(F32) + oth_v[here, :].astype(F32)
        total = mixed_v[here, :] + attn + vecs[4:5, :]
        mixed_v[here, :] = total
        centred, scale = row_stats(total)
        inv_v[here, :] = on_lanes(scale)
        plain = centred * scale
        normed_v[here, :] = plain.astype(BF16)
        n2[here, :] = (plain * vecs[2:3, :] + vecs[3:4, :]).astype(BF16)
        g_bout[...] += fold_rows(cot_v[here, :].astype(F32))

    row_parts(rows, blk, lambda c: wait_all(part_move(loads, in_sems, c)), norm)
    stores = [
        move(source, target, out_sems.at[0, n])
        for n, (source, target) in enumerate(
            [(mixed_v, hidden), (normed_v, normed), (inv_v, inv)]
        )
    ]
    start_all(stores)
    turn_into(n2_t, n2, lead_blocks(width, in_rows))
    wait_all(weights)

    g_bin[...] = jnp.zeros_like(g_bin)

    def row_block(i):
        here = pl.ds(pl.multiple_of(i * big, big), big)
        for j in range(units // width):
            cols = pl.ds(j * width, width)
            pre_all = nn(n2[here, :], w_in_v[:, cols])
            grad_all = nt(cot_v[here, :], w_out_v[cols, :])
            sums = jnp.zeros((8, width), F32)
            for s in range(big // sub):
                rng = slice(s * sub, s * sub + sub)
                value, slope = gelu_parts(pre_all[rng] + biases[1 + j : 2 + j, :])
                grad = grad_all[rng] * slope
                sums += fold_rows(grad)
                spot = pl.ds(pl.multiple_of(i * big + s * sub, sub), sub)
                act[spot, cols] = value.astype(BF16)
                gp[spot, cols] = grad.astype(BF16)
            g_bin[:, cols] += sums
        oth_v[here, :] = nt(gp[here, :], w_in_v[...]).astype(BF16)
        own_v[here, :] = nn(act[here, :], w_out_v[...]).astype(BF16)
        for n, (source, target) in enumerate([(oth_v, gn_part), (own_v, part)]):
            move(source.at[here, :], target.at[here, :], out_sems.at[1 + n, i]).start()

    def two_blocks(i, carry):
        row_block(2 * i)
        row_block(2 * i + 1)
        return carry

    lax.fori_loop(0, rows // big // 2, two_blocks, 0)
    for i in range(rows // big):
        here = pl.ds(i * big, big)
        for n, (source, target) in enumerate([(oth_v, gn_part), (own_v, part)]):
            stores.append(move(source.at[here, :], target.at[here, :], out_sems.at[1 + n, i]))

    wait_all(turns)
    half = width // 2
    for n, (turned, right, buf, keep, send) in enumerate(
        [(n2_t, gp, g_in, in_keep, in_send), (cot_tv, act, g_out, out_keep, out_send)]
    ):
        for side in range(2):
            lines = pl.ds(side * half, half)
            for j in range(units // width):
                cols = pl.ds(j * width, width)
                buf[side, :, cols] = nn(turned[lines, :], right[:, cols]).astype(BF16)
        for m, (side, target) in enumerate([(1 - sides[n], send), (sides[n], keep)]):
            stores.append(move(buf.at[side], target, grad_sems.at[n, m]))
            stores[-1].start()
    wait_all(stores)


def feed(
    in_rows, out_rows, flags, vecs, biases, mixed, p_own, p_oth, cot, cot_t,
    w_in, w_out, w_out_one, w_out_two,
):
    rows, width = mixed.shape
    units = w_in.shape[1]
    tall = shape((rows, width), BF16)
    grad = shape((width // 2, units), BF16)
    return pl.pallas_call(
        functools.partial(feed_kernel, in_rows, out_rows),
        out_shape=(
            shape((rows, width), F32), tall, tall, grad, grad, grad, grad,
            tall, shape((rows, LANES), F32), shape((8, units), F32), shape((8, width), F32),
        ),
        in_specs=[smem()] + [vmem()] * 2 + [hbm()] * 2 + [anywhere()] + [hbm()] * 6,
        out_specs=[hbm()] * 9 + [vmem()] * 2,
        scratch_shapes=[
            pltpu.VMEM((rows, width), F32),
            pltpu.VMEM((rows, width), BF16),
            pltpu.VMEM((rows, width), BF16),
            pltpu.VMEM((rows, width), BF16),
            pltpu.VMEM((width, rows), BF16),
            pltpu.VMEM(w_in.shape, BF16),
            pltpu.VMEM(w_out.shape, BF16),
            pltpu.VMEM((rows, width), BF16),
            pltpu.VMEM((width, rows), BF16),
            pltpu.VMEM((rows, units), BF16),
            pltpu.VMEM((rows, units), BF16),
            pltpu.VMEM((2, width // 2, units), BF16),
            pltpu.VMEM((2, width // 2, units), BF16),
            pltpu.VMEM((rows, width), BF16),
            pltpu.VMEM((rows, LANES), F32),
            pltpu.SemaphoreType.DMA((4, PARTS)),
            pltpu.SemaphoreType.DMA((width // out_rows,)),
            pltpu.SemaphoreType.DMA((3,)),
            pltpu.SemaphoreType.DMA((3, rows // 256)),
            pltpu.SemaphoreType.DMA((2, 2)),
        ],
        compiler_params=params(60),
        cost_estimate=SMALL,
        name="feed",
    )(
        flags, vecs, biases, mixed, p_own, p_oth, cot, cot_t,
        w_in, w_out, w_out_one, w_out_two,
    )


def attention_back_kernel(
    lead_rows, part_rows, flags, vecs, seg_row, lse, g_bin, g_bout, g_own, g_oth, cot, normed, inv,
    wp, att, k, q, v, w3, n1, normed_one,
    gh, part, keep, send, short,
    gh_v, own_v, oth_v, cot_v, normed_v, inv_v, wp_v, att_v, k_v, q_v, v_v, w3_v, n1_v, one_v, low_v, part_v,
    sums, tails, d_out, kt, dq_t, dk, dv, delta, seg_b, bias, raw, raw_g, low_p, low_g, n1_t, gh_t, grad_v, out,
    in_sems, row_sems, out_sems, last_sems,
):
    rows, width = cot.shape
    local = wp.shape[0]
    blk = 32
    big = 256
    blocks = lead_blocks(width, lead_rows)
    kept_side = flags[2]
    row_loads = [(g_own, own_v), (g_oth, oth_v), (cot, cot_v), (normed, normed_v), (inv, inv_v)]
    start_parts(row_loads, row_sems)
    loads = [
        move(source, target, in_sems.at[n])
        for n, (source, target) in enumerate(
            [
                (wp, wp_v), (att, att_v), (k, k_v), (q, q_v), (v, v_v), (w3, w3_v), (n1, n1_v),
                (normed_one, one_v),
            ]
        )
    ]
    start_all(loads)
    sums[...] = jnp.zeros_like(sums)
    dk[...] = jnp.zeros_like(dk)
    dv[...] = jnp.zeros_like(dv)
    spread_clips(seg_row, seg_b)

    def norm(low):
        here = pl.ds(low, blk)
        grad = own_v[here, :].astype(F32) + oth_v[here, :].astype(F32)
        plain = normed_v[here, :].astype(F32)
        scaled = grad * vecs[2:3, :]
        mean_one = jnp.mean(scaled, axis=-1, keepdims=True)
        mean_two = jnp.mean(scaled * plain, axis=-1, keepdims=True)
        scale = wide_rsqrt(inv_v, here, width)
        back = cot_v[here, :].astype(F32) + scale * (scaled - mean_one - plain * mean_two)
        gh_v[here, :] = back
        low_v[here, :] = back.astype(BF16)
        sums[0] += fold_rows(grad * plain)
        sums[1] += fold_rows(grad)
        sums[2] += fold_rows(back)

    row_parts(rows, blk, lambda c: wait_all(part_move(row_loads, row_sems, c)), norm)
    stores = [move(gh_v, gh, out_sems.at[0])]
    stores[0].start()

    wait_all(loads[:3])
    heads = local // HEAD_DIM
    lane = lax.broadcasted_iota(jnp.int32, (delta.shape[0], local), 1)
    row = lax.broadcasted_iota(jnp.int32, (delta.shape[0], local), 0)
    of_head = (lane // HEAD_DIM == row).astype(BF16)

    def project(i, carry):
        here = pl.ds(pl.multiple_of(i * big, big), big)
        grad_out = nt(low_v[here, :], wp_v[...]).astype(BF16)
        d_out[here, :] = grad_out
        product = grad_out.astype(F32) * att_v[here, :].astype(F32)
        coarse = product.astype(BF16)
        fine = (product - coarse.astype(F32)).astype(BF16)
        delta[:, here] = nt(of_head, coarse) + nt(of_head, fine)
        kt[:, here] = k_v[here, :].T
        return carry

    lax.fori_loop(0, rows // big, project, 0)
    wait_all(loads[3:])

    pairs = heads // 2
    window = bias.shape[0]
    strip = 128
    strips = window // strip

    def attend(j, carry):
        here, keys = key_window(j, rows)
        first = pl.multiple_of(keys.start, LANES)
        set_bias(bias, seg_b, seg_row, here, keys)
        blocks_two = {}

        def two(p):
            if p not in blocks_two:
                pair = pl.ds(p * LANES, LANES)
                blocks_two[p] = (two_heads(q_v[here, pair]), two_heads(d_out[here, pair]))
            return blocks_two[p]

        def at_strip(n):
            return (
                pl.ds(pl.multiple_of(first + n * strip, strip), strip),
                pl.ds(n * strip, strip),
            )

        def products(p):
            pair = pl.ds(p * LANES, LANES)

            def scores(n):
                def run():
                    some, at = at_strip(n)
                    raw[p % 2, at, :] = nt(k_v[some, pair], two(p)[0])

                return run

            def grads(n):
                def run():
                    some, at = at_strip(n)
                    raw_g[p % 2, at, :] = nt(v_v[some, pair], two(p)[1])

                return run

            return [make(n) for n in range(strips) for make in (scores, grads)]

        def softmax_back(p):
            tops = jnp.concatenate([lse[pl.ds(2 * p + e, 1), here] for e in range(2)], axis=1)
            inner = jnp.concatenate([delta[pl.ds(2 * p + e, 1), here] for e in range(2)], axis=1)
            half = strip // 2

            def run_at(n):
                def run():
                    at = pl.ds(n * half, half)
                    probs = jnp.exp(raw[p % 2, at, :] + bias[at, :] - tops)
                    low_p[p % 2, at, :] = probs.astype(BF16)
                    low_g[p % 2, at, :] = (probs * (raw_g[p % 2, at, :] - inner)).astype(BF16)

                return run

            return [run_at(n) for n in range(2 * strips)]

        def sums_of(p):
            pair = pl.ds(p * LANES, LANES)

            def keys_of(n):
                def run():
                    some, at = at_strip(n)
                    dk[some, pair] += nn(low_g[p % 2, at, :], two(p)[0])

                return run

            def values_of(n):
                def run():
                    some, at = at_strip(n)
                    dv[some, pair] += nn(low_p[p % 2, at, :], two(p)[1])

                return run

            def queries():
                grad_q = nn(kt[pair, keys], low_g[p % 2]) * SCORE_SCALE
                for e in range(2):
                    lanes = slice(e * LANES, e * LANES + LANES)
                    head = slice(e * HEAD_DIM, e * HEAD_DIM + HEAD_DIM)
                    dq_t[pl.ds(p * LANES + e * HEAD_DIM, HEAD_DIM), here] = grad_q[head, lanes]

            return [make(n) for n in range(strips) for make in (keys_of, values_of)] + [queries]

        def turns():
            for target, source in ((n1_t, n1_v), (gh_t, low_v)):
                turned = source[here, :].T
                for start, place, count in blocks:
                    target[pl.ds(place, count), here] = turned[start : start + count]

        interleave(products(0), [turns])
        for p in range(pairs):
            matrix = (products(p + 1) if p + 1 < pairs else []) + (sums_of(p - 1) if p else [])
            interleave(softmax_back(p), matrix)
        interleave(sums_of(pairs - 1))
        return carry

    lax.fori_loop(0, rows // LANES, attend, 0)

    tails[...] = jnp.zeros_like(tails)

    def finish(i, carry):
        here = pl.ds(pl.multiple_of(i * big, big), big)
        grad_q, grad_k, grad_val = dq_t[:, here].T, dk[here, :], dv[here, :]
        tails[2, :, pl.ds(0, local)] += fold_rows(grad_q)
        tails[2, :, pl.ds(local, local)] += fold_rows(grad_val)
        lows = [grad.astype(BF16) for grad in (grad_q, grad_k, grad_val)]
        total = sum(nt(low, w3_v[n]) for n, low in enumerate(lows))
        part_v[here, :] = total.astype(BF16)
        tails[0] += fold_rows(total * one_v[here, :].astype(F32))
        tails[1] += fold_rows(total)
        for n, low in enumerate(lows):
            grad_v[here, pl.ds(n * local, local)] = low
        move(part_v.at[here, :], part.at[here, :], last_sems.at[i]).start()
        return carry

    lax.fori_loop(0, rows // big, finish, 0)
    for i in range(rows // big):
        here = pl.ds(i * big, big)
        stores.append(move(part_v.at[here, :], part.at[here, :], last_sems.at[i]))
    units = g_bin.shape[1]
    listed = [tails[0], tails[1], sums[0], sums[1], sums[2], g_bout[...], tails[2]]
    listed += [g_bin[:, pl.ds(n, width)] for n in range(0, units, width)]
    half = width // 2
    listed = [row_sum(block) for block in listed]
    for n, block in enumerate(listed):
        short[pl.ds(n, 1), :] = block
    if part_rows:
        sources = [
            (jnp.concatenate(listed[:6] + [jnp.zeros((2, width), F32)], axis=0), part_rows),
            (jnp.broadcast_to(listed[6][:, :local], (8, local)), local * part_rows // width),
            (jnp.broadcast_to(listed[6][:, local:], (8, local)), local * part_rows // width),
            (
                jnp.broadcast_to(jnp.concatenate(listed[7:], axis=1), (8, units)),
                units * part_rows // width,
            ),
        ]
        rest = jnp.zeros((part_rows - 8 * len(sources), LANES), F32)
        for start, place, count in blocks:
            for row in range(0, count, part_rows):
                d = (start + row) // part_rows
                parts = [
                    pltpu.roll(source, (source.shape[1] - d * size) % source.shape[1], 1)[:, :LANES]
                    for source, size in sources
                ]
                side, at = divmod(place + row, half)
                out[side, pl.ds(at, part_rows), pl.ds(4 * local, LANES)] = jnp.concatenate(
                    parts + [rest], axis=0
                ).astype(BF16)
    for side in range(2):
        lines = pl.ds(side * half, half)
        for n in range(3):
            cols = pl.ds(n * local, local)
            out[side, :, cols] = nn(n1_t[lines, :], grad_v[:, cols]).astype(BF16)
        out[side, :, pl.ds(3 * local, local)] = nn(gh_t[lines, :], att_v[...]).astype(BF16)
    for n, (side, target) in enumerate([(1 - kept_side, send), (kept_side, keep)]):
        stores.append(move(out.at[side], target, out_sems.at[1 + n]))
        stores[-1].start()
    wait_all(stores)


def attention_back(
    lead_rows, part_rows, flags, vecs, segment, lse, g_bin, g_bout, g_own, g_oth, cot, normed, inv,
    wp, att, k, q, v, w3, n1, normed_one,
):
    rows, width = cot.shape
    local = wp.shape[0]
    window = min(rows, LANES + 2 * MAX_CLIP)
    tall, thin = pltpu.VMEM((rows, width), BF16), pltpu.VMEM((rows, local), BF16)
    turned = pltpu.VMEM((width, rows), BF16)
    half = (width // 2, 4 * local + (LANES if part_rows else 0))
    return pl.pallas_call(
        functools.partial(attention_back_kernel, lead_rows, part_rows),
        out_shape=(
            shape((rows, width), F32),
            shape((rows, width), BF16),
            shape(half, BF16),
            shape(half, BF16),
            shape((7 + g_bin.shape[1] // width, width), F32),
        ),
        in_specs=[smem()] + [vmem()] * 5 + [hbm()] + [anywhere()] + [hbm()] * 11,
        out_specs=[hbm()] * 4 + [vmem()],
        scratch_shapes=[
            pltpu.VMEM((rows, width), F32),
            tall, tall, tall, tall,
            pltpu.VMEM((rows, LANES), F32),
            pltpu.VMEM(wp.shape, BF16),
            thin, thin, thin, thin,
            pltpu.VMEM(w3.shape, BF16),
            tall, tall, tall, tall,
            pltpu.VMEM((3, 8, width), F32),
            pltpu.VMEM((3, 8, width), F32),
            thin,
            pltpu.VMEM((local, rows), BF16),
            pltpu.VMEM((local, rows), F32),
            pltpu.VMEM((rows, local), F32),
            pltpu.VMEM((rows, local), F32),
            pltpu.VMEM((8, rows), F32),
            pltpu.VMEM((rows, LANES), F32),
            pltpu.VMEM((window, 2 * LANES), F32),
            pltpu.VMEM((2, window, 2 * LANES), F32),
            pltpu.VMEM((2, window, 2 * LANES), F32),
            pltpu.VMEM((2, window, 2 * LANES), BF16),
            pltpu.VMEM((2, window, 2 * LANES), BF16),
            turned, turned,
            pltpu.VMEM((rows, 3 * local), BF16),
            pltpu.VMEM((2,) + half, BF16),
            pltpu.SemaphoreType.DMA((8,)),
            pltpu.SemaphoreType.DMA((5, PARTS)),
            pltpu.SemaphoreType.DMA((3,)),
            pltpu.SemaphoreType.DMA((rows // 256,)),
        ],
        compiler_params=params(60),
        cost_estimate=SMALL,
        name="attention_back",
    )(
        flags, vecs, segment, lse, g_bin, g_bout, g_own, g_oth, cot, normed, inv,
        wp, att, k, q, v, w3, n1, normed_one,
    )


def mixed_back_kernel(blend, flags, vecs, gh, g_own, g_oth, normed, inv, outgoing, kept, *refs):
    gh_v, own_v, oth_v, normed_v, inv_v, leave_v, kept_v, in_sems, out_sems, leave_sems = refs
    ratio = blend[0]
    rows, width = gh.shape
    blk = 32
    piece = leave_v.shape[1]
    loads = [(gh, gh_v), (g_own, own_v), (g_oth, oth_v), (normed, normed_v), (inv, inv_v)]
    stores = [(kept_v, kept)]
    start_parts(loads, in_sems)

    def norm(low):
        here = pl.ds(low, blk)
        grad = own_v[here, :].astype(F32) + oth_v[here, :].astype(F32)
        plain = normed_v[here, :].astype(F32)
        scaled = grad * vecs[0:1, :]
        mean_one = jnp.mean(scaled, axis=-1, keepdims=True)
        mean_two = jnp.mean(scaled * plain, axis=-1, keepdims=True)
        scale = wide_rsqrt(inv_v, here, width)
        back = gh_v[here, :] + scale * (scaled - mean_one - plain * mean_two)
        leave = ((1.0 - ratio) * back).astype(BF16)
        leave_v[pl.ds(low // piece, blk // piece)] = leave.reshape(blk // piece, piece, width)
        kept_v[here, :] = (ratio * back).astype(BF16)

    row_parts(rows, blk, lambda c: wait_all(part_move(loads, in_sems, c)), norm)
    start_parts(stores, out_sems)
    if len(outgoing.shape) == 3:
        leaves = [move(leave_v, outgoing, leave_sems.at[0])]
    else:
        count = outgoing.shape[0]
        leaves = [
            move(
                leave_v.at[pl.ds(pl.multiple_of((2 * m + flags[0]) * count, count), count)],
                outgoing.at[:, m],
                leave_sems.at[m],
            )
            for m in range(2)
        ]
    start_all(leaves)
    for c in range(PARTS):
        wait_all(part_move(stores, out_sems, c))
    wait_all(leaves)


def mixed_back(piece, ordered, blend, flags, vecs, gh, g_own, g_oth, normed, inv):
    rows, width = gh.shape
    tall = pltpu.VMEM((rows, width), BF16)
    runs = rows // piece
    dims = (runs // 4, 2, piece, width) if ordered else (runs, piece, width)
    return pl.pallas_call(
        mixed_back_kernel,
        out_shape=(shape(dims, BF16), shape((rows, width), BF16)),
        in_specs=[smem(), smem(), vmem()] + [hbm()] * 2 + [anywhere()] + [hbm()] * 2,
        out_specs=[hbm(), hbm()],
        scratch_shapes=[
            pltpu.VMEM((rows, width), F32),
            tall, tall, tall, pltpu.VMEM((rows, LANES), F32),
            pltpu.VMEM((runs, piece, width), BF16),
            tall,
            pltpu.SemaphoreType.DMA((5, PARTS)),
            pltpu.SemaphoreType.DMA((1, PARTS)),
            pltpu.SemaphoreType.DMA((2,)),
        ],
        compiler_params=params(60),
        cost_estimate=SMALL,
        name="mixed_back",
    )(blend, flags, vecs, gh, g_own, g_oth, normed, inv)


def shards(
    tokens,
    mix_blend,
    partner,
    clip_ids,
    gain_one,
    shift_one,
    qkv_weight,
    qv_bias,
    proj_weight,
    proj_bias,
    gain_two,
    shift_two,
    in_weight,
    in_bias,
    out_weight,
    out_bias,
    cotangent,
):
    rows, width = tokens.shape
    dp_count = lax.axis_size("dp")
    both = ("dp", "mp")
    bits = dp_count.bit_length() - 1
    seq = lax.axis_index("dp")
    mp = lax.axis_index("mp")
    core = lax.rem(seq, 2)
    home = core == mp
    all_dp = range(dp_count)

    def joint(d, m):
        return 2 * d + m

    core_swap = [(d, d ^ 1) for d in all_dp]
    home_to_pair = [(joint(d, d & 1), joint(d, 1 - (d & 1))) for d in all_dp]
    pair_to_home = [(joint(d, 1 - (d & 1)), joint(d, d & 1)) for d in all_dp]
    weight_move = home_to_pair + [
        (joint(d, 1 - (d & 1)), joint(d ^ 1, 1 - (d & 1))) for d in all_dp
    ]

    def swap(value):
        return lax.ppermute(value, "dp", core_swap)

    def chip_value(value):
        return jnp.where(home, value, swap(value))

    def after(value, *others):
        return lax.optimization_barrier((value,) + others)[0]

    def half_weight(value):
        return lax.ppermute(value, both, weight_move)

    part_rows = width // dp_count
    lead = min(n for n in range(1, bits) if (part_rows << n) % 16 == 0)
    lead_rows = part_rows << lead
    across = lax.rem(seq >> lead, 2)
    flags = jnp.stack([core, home.astype(jnp.int32), across]).astype(jnp.int32)

    def taken(value, index, axis):
        return lax.dynamic_index_in_dim(value, index, axis, keepdims=False)

    seq_small = chip_value(jnp.concatenate([mix_blend, clip_ids[0].astype(F32)]))
    blend, segment = seq_small[:1], seq_small[1:].reshape(1, rows)
    local = proj_weight.shape[0]
    units = in_bias.shape[0]
    half_small = jnp.concatenate([qv_bias.reshape(-1), in_bias])
    half_small = jnp.where(home, half_small, half_weight(half_small))
    biases = half_small.reshape(-1, width)
    vecs = jnp.stack([gain_one, shift_one, gain_two, shift_two, proj_bias])

    w3 = half_weight(qkv_weight.transpose(1, 0, 2))
    wp = half_weight(proj_weight)

    def two_way(value):
        halves = value.reshape(2, value.shape[0] // 2, value.shape[1])
        one = half_weight(taken(halves, across, 0))
        moves = [(joint(d, 1 - (d & 1)), joint(d ^ (1 << lead), 1 - (d & 1))) for d in all_dp]
        return value, one, lax.ppermute(one, both, moves)

    ids = jnp.arange(2 * dp_count, dtype=jnp.int32)
    piece = rows // (2 * 2 * dp_count)
    sent = tokens.reshape(2, dp_count, 2, piece, width)
    sent = lax.dynamic_index_in_dim(sent, mp, 2, keepdims=False)
    spread = lax.all_to_all(sent.transpose(1, 0, 2, 3), "dp", 0, 0, tiled=True)
    wanted = partner[(ids // 4) * 2 + ids % 2] * 2 + (ids // 2) % 2
    source_of = jnp.sum(
        jnp.where(partner[:, None] == ids[None, :dp_count], ids[:dp_count, None], 0),
        axis=0,
        dtype=jnp.int32,
    )
    source = source_of[ids // 2]
    wanted_back = (source // 2) * 4 + (ids % 2) * 2 + source % 2
    chosen = pick(spread.reshape(2 * dp_count, piece, width), wanted, w3, wp, half_small)
    partner_own = lax.all_to_all(chosen, both, 0, 0, tiled=True).reshape(rows // 2, width)
    w_out = two_way(out_weight)
    w_in = half_weight(after(in_weight, w_out[1]))

    tok = chip_value(tokens)
    cot = chip_value(cotangent)
    cot_t = cot.T
    partner_oth = swap(after(partner_own, tok, cot, vecs, segment, wanted_back))

    mixed, n1, normed_one, inv_one, q, k, v, att, attn_part, lse = attention(
        blend, flags, segment, vecs, biases, tok, partner_own, partner_oth, w3, wp, w_out[2], cot_t
    )
    pair_first = part_rows % 16 == 0
    fed = feed(
        lead_rows, part_rows if pair_first else lead_rows, flags, vecs, biases,
        mixed, attn_part, swap(attn_part), cot, cot_t, w_in, *w_out,
    )
    hidden, out_part, gn2_part, in_keep, in_send, out_keep, out_send = fed[:7]
    normed_two, inv_two, g_bin, g_bout = fed[7:]
    gn2_oth = swap(gn2_part)

    high, mid = dp_count >> (lead + 1), 1 << (lead - 1)
    pair_and_core = pair_to_home + [(joint(d, d & 1), joint(d ^ 1, d & 1)) for d in all_dp]
    pair_diagonal = [(joint(d, 1 - (d & 1)), joint(d ^ 1, d & 1)) for d in all_dp]

    def total(*terms):
        return sum(term.astype(F32) for term in terms)

    def send_across(value):
        return lax.ppermute(value, "dp", [(d, d ^ (1 << lead)) for d in all_dp])

    def send_pair(value):
        value = value.reshape(high, mid, 2, part_rows, -1)
        one = lax.ppermute(taken(value, jnp.where(home, 1 - core, core), 2), both, pair_and_core)
        two = lax.ppermute(taken(value, 1 - core, 2), both, pair_diagonal)
        held = taken(value, core, 2)
        return jnp.where(home, held, jnp.zeros_like(held)), one, two

    def far(value, *others):
        for shift, left in ((1, mid), (lead + 1, high)):
            while left > 1:
                radix = min(4, left)
                left //= radix
                value = value.reshape((-1, left, radix) + value.shape[-2:]).astype(BF16)
                spot = lax.rem(seq >> shift, radix)
                got = [
                    lax.ppermute(
                        taken(value, spot ^ flip, 2),
                        "dp",
                        [(d, d ^ (flip << shift)) for d in all_dp],
                    )
                    for flip in range(1, radix)
                ]
                value = total(taken(value, spot, 2), *after(got, *others))
                shift += radix.bit_length() - 1
        return value.reshape(value.shape[-2:])

    def send_first(keep, send):
        if not pair_first:
            return [keep, send_across(send)]
        one = lax.ppermute(send, both, pair_and_core)
        two = lax.ppermute(keep, both, pair_diagonal)
        return [jnp.where(home, keep, jnp.zeros_like(keep)), one, two]

    def send_second(value):
        if not pair_first:
            return send_pair(value) + (value,)
        value = value.reshape(high, 2, mid, part_rows, -1)
        away = taken(value, 1 - across, 1)
        return taken(value, across, 1), send_across(away), away

    in_got = send_across(in_send)
    out_first = send_first(out_keep, out_send)
    gh, gn1_part, attn_keep, attn_send, short = attention_back(
        lead_rows, part_rows if pair_first else 0, flags, vecs, segment, lse, g_bin, g_bout,
        gn2_part, gn2_oth, cot, normed_two, inv_two, wp, att, k, q, v, w3, n1, normed_one,
    )
    gn1_oth = swap(after(gn1_part, in_got, *out_first))
    attn_first = [attn_keep, send_across(attn_send)]
    in_terms = send_pair(total(in_keep, in_got).astype(BF16))
    ordered = piece % 16 == 0
    outgoing, kept = mixed_back(
        piece if ordered else 16, ordered, blend, flags, vecs, gh, gn1_part, gn1_oth, normed_one, inv_one
    )

    if ordered:
        leaving = outgoing.reshape(2 * dp_count, piece, width)
    else:
        leaving = taken(outgoing.reshape(2, 2, dp_count, piece, width), core, 1)
        leaving = leaving.transpose(1, 0, 2, 3).reshape(2 * dp_count, piece, width)
    back = lax.all_to_all(leaving, both, 0, 0, tiled=True)

    in_value = total(*after(in_terms, leaving)).astype(BF16)
    sum_in = far(in_value)
    out_oth = swap(after(out_part, leaving))
    out_value = total(*after(out_first, in_value)).astype(BF16)
    *out_terms, out_away = send_second(out_value)
    attn_value = total(*after(attn_first, out_away)).astype(BF16)
    attn_terms = send_pair(attn_value)
    block = hidden + (out_part.astype(F32) + after(out_oth, attn_value).astype(F32)) + out_bias
    block = block.astype(BF16)
    kept = kept.reshape(2, rows // 2, width)
    kept_got = half_weight(taken(kept, 1 - mp, 0))
    block_got = half_weight(block)

    def side_by_side(*groups):
        values = [total(*terms).reshape(high * mid, part_rows, -1) for terms in groups]
        return jnp.concatenate(values, axis=2).astype(BF16)

    returning = pick(back, wanted_back, attn_value, sum_in)
    returned = lax.all_to_all(
        returning.reshape(dp_count, 2, piece, width), "dp", 0, 0, tiled=True
    )
    returned = after(returned, kept_got)
    kept = jnp.where(home, taken(kept, mp, 0), kept_got)
    returned = returned.transpose(1, 0, 2, 3).reshape(rows // 2, width)
    mine = (kept.astype(F32) + returned.astype(F32)).astype(BF16)
    other = lax.ppermute(mine, "mp", [(0, 1), (1, 0)])
    block_out = jnp.where(home, block, after(block_got, mine))
    grad_tokens = jnp.where(
        jnp.arange(2)[:, None, None] == mp, mine[None], other[None]
    ).reshape(rows, width)

    marker = swap(returning[0, :, :LANES])
    summed = far(
        side_by_side(*(after(terms, marker) for terms in (out_terms, attn_terms))),
        mine,
    )
    sum_out, sum_attn = after(summed[:, :units], other), summed[:, units:]
    sum_qkv = sum_attn[:, : 3 * local].reshape(-1, 3, local)
    sum_proj = sum_attn[:, 3 * local : 4 * local].T
    quarter, eighth = local // dp_count, units // dp_count
    if pair_first:
        extra = sum_attn[:, 4 * local :]
        plain = extra[:6, :part_rows]
        ours = plain[:2] + lax.ppermute(plain[:2], "mp", [(0, 1), (1, 0)])
        plain = jnp.concatenate([ours, plain[2:]])
        sum_qv = jnp.stack([extra[8, :quarter], extra[16, :quarter]])
        sum_bin = extra[24, :eighth]
    else:
        counts = jnp.where((core == 0) | (jnp.arange(6) < 2), 1.0, 0.0).astype(F32)
        wide = (short[:6] * counts[:, None]).reshape(6, dp_count, 1, part_rows)
        wide = jnp.broadcast_to(wide, (6, dp_count, 2, part_rows)).transpose(1, 2, 0, 3)
        to_half = (jnp.arange(2) == core)[None, :, None]

        def half_terms(vectors):
            terms = vectors.reshape(vectors.shape[0], dp_count, -1).transpose(1, 0, 2)
            return jnp.where(to_half, terms.reshape(dp_count, 1, -1), 0.0)

        short = jnp.concatenate(
            [
                wide.reshape(dp_count, 2, -1),
                half_terms(short[6].reshape(2, local)),
                half_terms(short[7:].reshape(1, units)),
            ],
            axis=-1,
        ).reshape(2 * dp_count, -1)
        short = jnp.sum(lax.all_to_all(short, both, 0, 0, tiled=True), axis=0)
        plain = short[: 6 * part_rows].reshape(6, part_rows)
        sum_qv = short[6 * part_rows : 6 * part_rows + 2 * quarter].reshape(2, -1)
        sum_bin = short[6 * part_rows + 2 * quarter :]
    return (
        block_out,
        grad_tokens,
        plain[0],
        plain[1],
        sum_qkv,
        sum_qv,
        sum_proj,
        plain[4],
        plain[2],
        plain[3],
        sum_in,
        sum_bin,
        sum_out.T,
        plain[5],
    )


def solution(mesh):
    return jax.shard_map(
        shards,
        mesh=mesh,
        in_specs=(
            P("dp", None),
            P("dp"),
            P(),
            P("dp", None),
            P(),
            P(),
            P(None, None, "mp"),
            P(None, "mp"),
            P("mp", None),
            P(),
            P(),
            P(),
            P(None, "mp"),
            P("mp"),
            P("mp", None),
            P(),
            P("dp", None),
        ),
        out_specs=(
            P("dp", None),
            P("dp", None),
            P("dp"),
            P("dp"),
            P("dp", None, "mp"),
            P(None, ("mp", "dp")),
            P("mp", "dp"),
            P("dp"),
            P("dp"),
            P("dp"),
            P("dp", "mp"),
            P(("mp", "dp")),
            P("mp", "dp"),
            P("dp"),
        ),
        check_vma=False,
    )
```

```python
import functools

import jax
import jax.numpy as jnp
from jax import lax
from jax.experimental import pallas as pl
from jax.experimental.pallas import tpu as pltpu
from jax.sharding import PartitionSpec as P

HEAD_DIM = 64
NORM_EPS = 1e-06
NEG_FILL = -1e30
SCORE_SCALE = HEAD_DIM ** (-0.5)
MAX_CLIP = 256
LANES = 128
F32 = jnp.float32
BF16 = jnp.bfloat16
MIB = 1 << 20
SMALL = pl.CostEstimate(flops=1 << 20, bytes_accessed=1 << 20, transcendentals=0)


def nn(left, right):
    return lax.dot_general(left, right, (((1,), (0,)), ((), ())), preferred_element_type=F32)


def nt(left, right):
    return lax.dot_general(left, right, (((1,), (1,)), ((), ())), preferred_element_type=F32)


def vmem():
    return pl.BlockSpec(memory_space=pltpu.VMEM)


def hbm():
    return pl.BlockSpec(memory_space=pltpu.HBM)


def anywhere():
    return pl.BlockSpec(memory_space=pl.ANY)


def smem():
    return pl.BlockSpec(memory_space=pltpu.SMEM)


def params(mib):
    return pltpu.CompilerParams(vmem_limit_bytes=mib * MIB)


def shape(dims, dtype):
    return jax.ShapeDtypeStruct(dims, dtype)


def row_stats(vector):
    mean = jnp.mean(vector, axis=-1, keepdims=True)
    centred = vector - mean
    spread = jnp.mean(centred * centred, axis=-1, keepdims=True)
    return centred, lax.rsqrt(spread + NORM_EPS)


def on_lanes(column):
    return jnp.broadcast_to(column, (column.shape[0], LANES))


def wide_rsqrt(inv, here, width):
    return jnp.concatenate([inv[here, :]] * (width // LANES), axis=1)


def row_sum(block):
    return jnp.sum(block, axis=0, keepdims=True)


def fold_rows(block):
    rows, width = block.shape
    return jnp.sum(block.reshape(rows // 8, 8, width), axis=0)


def pick_kernel(index, source, *refs):
    picked = refs[-1]

    def move(i, carry):
        picked[i] = source[index[i]]
        return carry

    lax.fori_loop(0, picked.shape[0], move, 0, unroll=4)


def pick(source, index, *after):
    dims = index.shape + source.shape[1:]
    return pl.pallas_call(
        pick_kernel,
        out_shape=shape(dims, source.dtype),
        in_specs=[smem(), vmem()] + [hbm()] * len(after),
        out_specs=vmem(),
        compiler_params=params(16),
        cost_estimate=SMALL,
        name="pick",
    )(index, source, *after)


def move(source, target, sem):
    return pltpu.make_async_copy(source, target, sem)


PARTS = 4


def part_move(pairs, sems, c, first=0):
    moves = []
    for n, (source, target) in enumerate(pairs):
        count = source.shape[0] // PARTS
        here = pl.ds(pl.multiple_of(c * count, count), count)
        moves.append(move(source.at[here, :], target.at[here, :], sems.at[first + n, c]))
    return moves


def start_parts(pairs, sems):
    for c in range(PARTS):
        start_all(part_move(pairs, sems, c))


def row_parts(rows, blk, wait, body):
    steps = rows // PARTS // blk

    def part(c, carry):
        wait(c)

        def step(i, carry):
            body(pl.multiple_of((c * steps + i) * blk, blk))
            return carry

        return lax.fori_loop(0, steps, step, carry, unroll=4)

    lax.fori_loop(0, PARTS, part, 0)


def start_all(moves):
    for one in moves:
        one.start()


def wait_all(moves):
    for one in moves:
        one.wait()


def interleave(*streams):
    order = sorted(
        ((n + 0.5) / len(stream), which, n)
        for which, stream in enumerate(streams)
        for n in range(len(stream))
    )
    for _, which, n in order:
        streams[which][n]()


def spread_clips(seg_row, seg_b):
    for i in range(seg_b.shape[0] // LANES):
        here = pl.ds(i * LANES, LANES)
        seg_b[here, :] = jnp.broadcast_to(seg_row[:, here], (LANES, LANES)).T


def key_window(j, rows):
    window = min(rows, LANES + 2 * MAX_CLIP)
    here = pl.ds(pl.multiple_of(j * LANES, LANES), LANES)
    first = pl.multiple_of(jnp.clip(j * LANES - MAX_CLIP, 0, rows - window), LANES)
    return here, pl.ds(first, window)


def set_bias(bias, seg_b, seg_row, here, keys):
    filled = jnp.where(seg_b[keys, :] == seg_row[:, here], 0.0, NEG_FILL)
    bias[:, pl.ds(0, LANES)] = filled
    bias[:, pl.ds(LANES, LANES)] = filled


def two_heads(block):
    lane = lax.broadcasted_iota(jnp.int32, block.shape, 1)
    return jnp.concatenate(
        [block * (lane // HEAD_DIM == e).astype(BF16) for e in range(2)], axis=0
    )


def attention_kernel(
    blend, flags, seg_row, vecs, biases, tok, own, oth, w3, wp, *refs
):
    mixed, n1, normed, inv, q, k, v, att, part, lse = refs[-32:-22]
    (
        tok_v, own_v, oth_v, w3_v, wp_v, mixed_v, n1_v, q_v, k_v, v_v, att_v, part_v,
        vt, att_t, seg_b, bias, ones, normed_v, inv_v, in_sems, half_sems, out_sems,
    ) = refs[-22:]
    rows, width = tok.shape
    local = wp.shape[0]
    half_rows = rows // 2
    ratio = blend[0]
    blk = 32
    big = 256

    loads = [
        move(source, target, in_sems.at[n])
        for n, (source, target) in enumerate([(tok, tok_v), (w3, w3_v), (wp, wp_v)])
    ]
    halves = [(own, own_v), (oth, oth_v)]
    loads[0].start()
    start_parts(halves, half_sems)
    start_all(loads[1:])
    early = [
        move(source, target, out_sems.at[n])
        for n, (source, target) in enumerate(
            [
                (mixed_v, mixed), (n1_v, n1), (normed_v, normed), (inv_v, inv),
                (q_v, q), (k_v, k), (v_v, v),
            ]
        )
    ]
    ones[...] = jnp.ones_like(ones)
    spread_clips(seg_row, seg_b)

    loads[0].wait()
    for n, src, half in ((0, own_v, flags[0]), (1, oth_v, 1 - flags[0])):

        def mix(low, src=src, half=half):
            here = pl.ds(pl.multiple_of(half * half_rows + low, blk), blk)
            there = pl.ds(low, blk)
            mine, other = tok_v[here, :].astype(F32), src[there, :].astype(F32)
            blended = ratio * mine + (1.0 - ratio) * other
            mixed_v[here, :] = blended
            centred, scale = row_stats(blended)
            inv_v[here, :] = on_lanes(scale)
            plain = centred * scale
            normed_v[here, :] = plain.astype(BF16)
            n1_v[here, :] = (plain * vecs[0:1, :] + vecs[1:2, :]).astype(BF16)

        row_parts(
            half_rows, blk, lambda c, n=n: wait_all(part_move([halves[n]], half_sems, c, n)), mix
        )
    start_all(early[:4])

    loads[1].wait()
    for i in range(rows // big):
        here = pl.ds(i * big, big)
        rows_in = n1_v[here, :]
        queries = (nn(rows_in, w3_v[0]) + biases[0:1, :local]).astype(BF16).astype(F32)
        q_v[here, :] = (queries * SCORE_SCALE).astype(BF16)
        k_v[here, :] = nn(rows_in, w3_v[1]).astype(BF16)
        values = (nn(rows_in, w3_v[2]) + biases[0:1, local:]).astype(BF16)
        v_v[here, :] = values
        vt[:, here] = values.T
    start_all(early[4:])

    def attend(j, carry):
        here, keys = key_window(j, rows)
        set_bias(bias, seg_b, seg_row, here, keys)
        for p in range(local // LANES):
            pair = pl.ds(p * LANES, LANES)
            scores = nt(k_v[keys, pair], two_heads(q_v[here, pair])) + bias[...]
            top = jnp.max(scores, axis=0, keepdims=True)
            grown = jnp.exp(scores - top).astype(BF16)
            total = nn(ones[...], grown)[:1]
            out = (nn(vt[pair, keys], grown) / total).astype(BF16)
            logs = top + jnp.log(total)
            for e in range(2):
                lanes = slice(e * LANES, e * LANES + LANES)
                head = slice(e * HEAD_DIM, e * HEAD_DIM + HEAD_DIM)
                att_t[pl.ds(p * LANES + e * HEAD_DIM, HEAD_DIM), here] = out[head, lanes]
                lse[pl.ds(2 * p + e, 1), here] = logs[:, lanes]
        return carry

    lax.fori_loop(0, rows // LANES, attend, 0)

    loads[2].wait()
    last = []
    for i in range(rows // big):
        here = pl.ds(i * big, big)
        block = att_t[:, here].T
        att_v[here, :] = block
        part_v[here, :] = nn(block, wp_v[...]).astype(BF16)
        last.append(move(part_v.at[here, :], part.at[here, :], out_sems.at[8 + i]))
        last[-1].start()
    last.append(move(att_v, att, out_sems.at[7]))
    last[-1].start()
    wait_all(early + last)


def attention(blend, flags, segment, vecs, biases, tok, own, oth, w3, wp, *before):
    rows, width = tok.shape
    local = wp.shape[0]
    window = min(rows, LANES + 2 * MAX_CLIP)
    thin = shape((rows, local), BF16)
    tall = shape((rows, width), BF16)
    return pl.pallas_call(
        attention_kernel,
        out_shape=(
            shape((rows, width), F32), tall, tall, shape((rows, LANES), F32),
            thin, thin, thin, thin, tall, shape((local // HEAD_DIM, rows), F32),
        ),
        in_specs=[smem(), smem()] + [vmem()] * 3 + [anywhere()] * 3 + [hbm()] * (2 + len(before)),
        out_specs=[hbm()] * 9 + [vmem()],
        scratch_shapes=[
            pltpu.VMEM((rows, width), BF16),
            pltpu.VMEM((rows // 2, width), BF16),
            pltpu.VMEM((rows // 2, width), BF16),
            pltpu.VMEM(w3.shape, BF16),
            pltpu.VMEM(wp.shape, BF16),
            pltpu.VMEM((rows, width), F32),
            pltpu.VMEM((rows, width), BF16),
            pltpu.VMEM((rows, local), BF16),
            pltpu.VMEM((rows, local), BF16),
            pltpu.VMEM((rows, local), BF16),
            pltpu.VMEM((rows, local), BF16),
            pltpu.VMEM((rows, width), BF16),
            pltpu.VMEM((local, rows), BF16),
            pltpu.VMEM((local, rows), BF16),
            pltpu.VMEM((rows, LANES), F32),
            pltpu.VMEM((window, 2 * LANES), F32),
            pltpu.VMEM((16, window), BF16),
            pltpu.VMEM((rows, width), BF16),
            pltpu.VMEM((rows, LANES), F32),
            pltpu.SemaphoreType.DMA((3,)),
            pltpu.SemaphoreType.DMA((2, PARTS)),
            pltpu.SemaphoreType.DMA((8 + rows // 256,)),
        ],
        compiler_params=params(60),
        cost_estimate=SMALL,
        name="attention",
    )(
        blend, flags, segment, vecs, biases, tok, own, oth, w3, wp, *before,
    )


ERFC_SLOPE = 0.47
ERFC_COEFFS = (
    0.2663094668265691,
    0.2480096137831850,
    0.3362712657560771,
    -0.1262288063821733,
    0.6076790117752645,
    -0.4204702410368928,
    0.0884296765518492,
)


def gelu_parts(pre):
    bell = jnp.exp(pre * pre * -0.5)
    t = 1.0 / (1.0 + jnp.abs(pre) * (ERFC_SLOPE * 0.5**0.5))
    poly = 0.5 * ERFC_COEFFS[-1]
    for coeff in ERFC_COEFFS[-2::-1]:
        poly = poly * t + 0.5 * coeff
    tail = poly * t * bell
    cdf = jnp.where(pre >= 0, 1.0 - tail, tail)
    return pre * cdf, cdf + pre * bell * 0.3989422804014327


def turn_into(target, source, blocks):
    rows = source.shape[0]
    big = 256
    for i in range(rows // big):
        here = pl.ds(i * big, big)
        turned = source[here, :].T
        for start, place, count in blocks:
            target[pl.ds(place, count), here] = turned[start : start + count]


def lead_blocks(width, lead_rows):
    runs = width // lead_rows
    return [
        (run * lead_rows, ((run % 2) * (runs // 2) + run // 2) * lead_rows, lead_rows)
        for run in range(runs)
    ]


def feed_kernel(
    in_rows, out_rows, flags, vecs, biases, mixed, p_own, p_oth, cot, cot_t,
    w_in, w_out, w_out_one, w_out_two,
    hidden, part, gn_part, in_keep, in_send, out_keep, out_send, normed, inv, g_bin, g_bout,
    mixed_v, own_v, oth_v, cot_v, cot_tv, w_in_v, w_out_v, n2, n2_t, act, gp,
    g_in, g_out, normed_v, inv_v, in_sems, turn_sems, weight_sems, out_sems, grad_sems,
):
    rows, width = mixed.shape
    units = w_in.shape[1]
    blk = 32
    big = 256
    sub = 16
    home = flags[1] == 1
    across = flags[2]
    kept_out = jnp.where(home, flags[0], 1 - flags[0]) if in_rows != out_rows else across
    sides = (across, kept_out)

    loads = [(mixed, mixed_v), (p_own, own_v), (p_oth, oth_v), (cot, cot_v)]
    start_parts(loads, in_sems)

    weights = [move(w_in, w_in_v, weight_sems.at[0])]
    weights[0].start()
    half = w_out.shape[0] // 2
    for n, (got, place) in enumerate([(w_out_one, across), (w_out_two, 1 - across)]):
        spot = pl.ds(pl.multiple_of(place * half, half), half)
        sem = weight_sems.at[1 + n]
        weights.append(move(w_out.at[spot, :], w_out_v.at[spot, :], sem))

        @pl.when(home)
        def _(spot=spot, sem=sem):
            move(w_out.at[spot, :], w_out_v.at[spot, :], sem).start()

        @pl.when(jnp.logical_not(home))
        def _(got=got, spot=spot, sem=sem):
            move(got, w_out_v.at[spot, :], sem).start()

    turns = [
        move(cot_t.at[pl.ds(start, count), :], cot_tv.at[pl.ds(place, count), :], turn_sems.at[n])
        for n, (start, place, count) in enumerate(lead_blocks(width, out_rows))
    ]
    start_all(turns)

    g_bout[...] = jnp.zeros_like(g_bout)

    def norm(low):
        here = pl.ds(low, blk)
        attn = own_v[here, :].astype(F32) + oth_v[here, :].astype(F32)
        total = mixed_v[here, :] + attn + vecs[4:5, :]
        mixed_v[here, :] = total
        centred, scale = row_stats(total)
        inv_v[here, :] = on_lanes(scale)
        plain = centred * scale
        normed_v[here, :] = plain.astype(BF16)
        n2[here, :] = (plain * vecs[2:3, :] + vecs[3:4, :]).astype(BF16)
        g_bout[...] += fold_rows(cot_v[here, :].astype(F32))

    row_parts(rows, blk, lambda c: wait_all(part_move(loads, in_sems, c)), norm)
    stores = [
        move(source, target, out_sems.at[0, n])
        for n, (source, target) in enumerate(
            [(mixed_v, hidden), (normed_v, normed), (inv_v, inv)]
        )
    ]
    start_all(stores)
    turn_into(n2_t, n2, lead_blocks(width, in_rows))
    wait_all(weights)

    g_bin[...] = jnp.zeros_like(g_bin)

    def row_block(i):
        here = pl.ds(pl.multiple_of(i * big, big), big)
        for j in range(units // width):
            cols = pl.ds(j * width, width)
            pre_all = nn(n2[here, :], w_in_v[:, cols])
            grad_all = nt(cot_v[here, :], w_out_v[cols, :])
            sums = jnp.zeros((8, width), F32)
            for s in range(big // sub):
                rng = slice(s * sub, s * sub + sub)
                value, slope = gelu_parts(pre_all[rng] + biases[1 + j : 2 + j, :])
                grad = grad_all[rng] * slope
                sums += fold_rows(grad)
                spot = pl.ds(pl.multiple_of(i * big + s * sub, sub), sub)
                act[spot, cols] = value.astype(BF16)
                gp[spot, cols] = grad.astype(BF16)
            g_bin[:, cols] += sums
        oth_v[here, :] = nt(gp[here, :], w_in_v[...]).astype(BF16)
        own_v[here, :] = nn(act[here, :], w_out_v[...]).astype(BF16)
        for n, (source, target) in enumerate([(oth_v, gn_part), (own_v, part)]):
            move(source.at[here, :], target.at[here, :], out_sems.at[1 + n, i]).start()

    def two_blocks(i, carry):
        row_block(2 * i)
        row_block(2 * i + 1)
        return carry

    lax.fori_loop(0, rows // big // 2, two_blocks, 0)
    for i in range(rows // big):
        here = pl.ds(i * big, big)
        for n, (source, target) in enumerate([(oth_v, gn_part), (own_v, part)]):
            stores.append(move(source.at[here, :], target.at[here, :], out_sems.at[1 + n, i]))

    wait_all(turns)
    half = width // 2
    for n, (turned, right, buf, keep, send) in enumerate(
        [(n2_t, gp, g_in, in_keep, in_send), (cot_tv, act, g_out, out_keep, out_send)]
    ):
        for side in range(2):
            lines = pl.ds(side * half, half)
            for j in range(units // width):
                cols = pl.ds(j * width, width)
                buf[side, :, cols] = nn(turned[lines, :], right[:, cols]).astype(BF16)
        for m, (side, target) in enumerate([(1 - sides[n], send), (sides[n], keep)]):
            stores.append(move(buf.at[side], target, grad_sems.at[n, m]))
            stores[-1].start()
    wait_all(stores)


def feed(
    in_rows, out_rows, flags, vecs, biases, mixed, p_own, p_oth, cot, cot_t,
    w_in, w_out, w_out_one, w_out_two,
):
    rows, width = mixed.shape
    units = w_in.shape[1]
    tall = shape((rows, width), BF16)
    grad = shape((width // 2, units), BF16)
    return pl.pallas_call(
        functools.partial(feed_kernel, in_rows, out_rows),
        out_shape=(
            shape((rows, width), F32), tall, tall, grad, grad, grad, grad,
            tall, shape((rows, LANES), F32), shape((8, units), F32), shape((8, width), F32),
        ),
        in_specs=[smem()] + [vmem()] * 2 + [hbm()] * 2 + [anywhere()] + [hbm()] * 6,
        out_specs=[hbm()] * 9 + [vmem()] * 2,
        scratch_shapes=[
            pltpu.VMEM((rows, width), F32),
            pltpu.VMEM((rows, width), BF16),
            pltpu.VMEM((rows, width), BF16),
            pltpu.VMEM((rows, width), BF16),
            pltpu.VMEM((width, rows), BF16),
            pltpu.VMEM(w_in.shape, BF16),
            pltpu.VMEM(w_out.shape, BF16),
            pltpu.VMEM((rows, width), BF16),
            pltpu.VMEM((width, rows), BF16),
            pltpu.VMEM((rows, units), BF16),
            pltpu.VMEM((rows, units), BF16),
            pltpu.VMEM((2, width // 2, units), BF16),
            pltpu.VMEM((2, width // 2, units), BF16),
            pltpu.VMEM((rows, width), BF16),
            pltpu.VMEM((rows, LANES), F32),
            pltpu.SemaphoreType.DMA((4, PARTS)),
            pltpu.SemaphoreType.DMA((width // out_rows,)),
            pltpu.SemaphoreType.DMA((3,)),
            pltpu.SemaphoreType.DMA((3, rows // 256)),
            pltpu.SemaphoreType.DMA((2, 2)),
        ],
        compiler_params=params(60),
        cost_estimate=SMALL,
        name="feed",
    )(
        flags, vecs, biases, mixed, p_own, p_oth, cot, cot_t,
        w_in, w_out, w_out_one, w_out_two,
    )


def attention_back_kernel(
    lead_rows, part_rows, flags, vecs, seg_row, lse, g_bin, g_bout, g_own, g_oth, cot, normed, inv,
    wp, att, k, q, v, w3, n1, normed_one,
    gh, part, keep, send, short,
    gh_v, own_v, oth_v, cot_v, normed_v, inv_v, wp_v, att_v, k_v, q_v, v_v, w3_v, n1_v, one_v, low_v, part_v,
    sums, tails, d_out, kt, dq_t, dk, dv, delta, seg_b, bias, raw, raw_g, low_p, low_g, n1_t, gh_t, grad_v, out,
    in_sems, row_sems, out_sems, last_sems,
):
    rows, width = cot.shape
    local = wp.shape[0]
    blk = 32
    big = 256
    blocks = lead_blocks(width, lead_rows)
    kept_side = flags[2]
    row_loads = [(g_own, own_v), (g_oth, oth_v), (cot, cot_v), (normed, normed_v), (inv, inv_v)]
    start_parts(row_loads, row_sems)
    loads = [
        move(source, target, in_sems.at[n])
        for n, (source, target) in enumerate(
            [
                (wp, wp_v), (att, att_v), (k, k_v), (q, q_v), (v, v_v), (w3, w3_v), (n1, n1_v),
                (normed_one, one_v),
            ]
        )
    ]
    start_all(loads)
    sums[...] = jnp.zeros_like(sums)
    dk[...] = jnp.zeros_like(dk)
    dv[...] = jnp.zeros_like(dv)
    spread_clips(seg_row, seg_b)

    def norm(low):
        here = pl.ds(low, blk)
        grad = own_v[here, :].astype(F32) + oth_v[here, :].astype(F32)
        plain = normed_v[here, :].astype(F32)
        scaled = grad * vecs[2:3, :]
        mean_one = jnp.mean(scaled, axis=-1, keepdims=True)
        mean_two = jnp.mean(scaled * plain, axis=-1, keepdims=True)
        scale = wide_rsqrt(inv_v, here, width)
        back = cot_v[here, :].astype(F32) + scale * (scaled - mean_one - plain * mean_two)
        gh_v[here, :] = back
        low_v[here, :] = back.astype(BF16)
        sums[0] += fold_rows(grad * plain)
        sums[1] += fold_rows(grad)
        sums[2] += fold_rows(back)

    row_parts(rows, blk, lambda c: wait_all(part_move(row_loads, row_sems, c)), norm)
    stores = [move(gh_v, gh, out_sems.at[0])]
    stores[0].start()

    wait_all(loads[:3])
    heads = local // HEAD_DIM
    lane = lax.broadcasted_iota(jnp.int32, (delta.shape[0], local), 1)
    row = lax.broadcasted_iota(jnp.int32, (delta.shape[0], local), 0)
    of_head = (lane // HEAD_DIM == row).astype(BF16)

    def project(i, carry):
        here = pl.ds(pl.multiple_of(i * big, big), big)
        grad_out = nt(low_v[here, :], wp_v[...]).astype(BF16)
        d_out[here, :] = grad_out
        product = grad_out.astype(F32) * att_v[here, :].astype(F32)
        coarse = product.astype(BF16)
        fine = (product - coarse.astype(F32)).astype(BF16)
        delta[:, here] = nt(of_head, coarse) + nt(of_head, fine)
        kt[:, here] = k_v[here, :].T
        return carry

    lax.fori_loop(0, rows // big, project, 0)
    wait_all(loads[3:])

    pairs = heads // 2
    window = bias.shape[0]
    strip = 128
    strips = window // strip

    def attend(j, carry):
        here, keys = key_window(j, rows)
        first = pl.multiple_of(keys.start, LANES)
        set_bias(bias, seg_b, seg_row, here, keys)
        blocks_two = {}

        def two(p):
            if p not in blocks_two:
                pair = pl.ds(p * LANES, LANES)
                blocks_two[p] = (two_heads(q_v[here, pair]), two_heads(d_out[here, pair]))
            return blocks_two[p]

        def at_strip(n):
            return (
                pl.ds(pl.multiple_of(first + n * strip, strip), strip),
                pl.ds(n * strip, strip),
            )

        def products(p):
            pair = pl.ds(p * LANES, LANES)

            def scores(n):
                def run():
                    some, at = at_strip(n)
                    raw[p % 2, at, :] = nt(k_v[some, pair], two(p)[0])

                return run

            def grads(n):
                def run():
                    some, at = at_strip(n)
                    raw_g[p % 2, at, :] = nt(v_v[some, pair], two(p)[1])

                return run

            return [make(n) for n in range(strips) for make in (scores, grads)]

        def softmax_back(p):
            tops = jnp.concatenate([lse[pl.ds(2 * p + e, 1), here] for e in range(2)], axis=1)
            inner = jnp.concatenate([delta[pl.ds(2 * p + e, 1), here] for e in range(2)], axis=1)
            half = strip // 2

            def run_at(n):
                def run():
                    at = pl.ds(n * half, half)
                    probs = jnp.exp(raw[p % 2, at, :] + bias[at, :] - tops)
                    low_p[p % 2, at, :] = probs.astype(BF16)
                    low_g[p % 2, at, :] = (probs * (raw_g[p % 2, at, :] - inner)).astype(BF16)

                return run

            return [run_at(n) for n in range(2 * strips)]

        def sums_of(p):
            pair = pl.ds(p * LANES, LANES)

            def keys_of(n):
                def run():
                    some, at = at_strip(n)
                    dk[some, pair] += nn(low_g[p % 2, at, :], two(p)[0])

                return run

            def values_of(n):
                def run():
                    some, at = at_strip(n)
                    dv[some, pair] += nn(low_p[p % 2, at, :], two(p)[1])

                return run

            def queries():
                grad_q = nn(kt[pair, keys], low_g[p % 2]) * SCORE_SCALE
                for e in range(2):
                    lanes = slice(e * LANES, e * LANES + LANES)
                    head = slice(e * HEAD_DIM, e * HEAD_DIM + HEAD_DIM)
                    dq_t[pl.ds(p * LANES + e * HEAD_DIM, HEAD_DIM), here] = grad_q[head, lanes]

            return [make(n) for n in range(strips) for make in (keys_of, values_of)] + [queries]

        def turns():
            for target, source in ((n1_t, n1_v), (gh_t, low_v)):
                turned = source[here, :].T
                for start, place, count in blocks:
                    target[pl.ds(place, count), here] = turned[start : start + count]

        interleave(products(0), [turns])
        for p in range(pairs):
            matrix = (products(p + 1) if p + 1 < pairs else []) + (sums_of(p - 1) if p else [])
            interleave(softmax_back(p), matrix)
        interleave(sums_of(pairs - 1))
        return carry

    lax.fori_loop(0, rows // LANES, attend, 0)

    tails[...] = jnp.zeros_like(tails)

    def finish(i, carry):
        here = pl.ds(pl.multiple_of(i * big, big), big)
        grad_q, grad_k, grad_val = dq_t[:, here].T, dk[here, :], dv[here, :]
        tails[2, :, pl.ds(0, local)] += fold_rows(grad_q)
        tails[2, :, pl.ds(local, local)] += fold_rows(grad_val)
        lows = [grad.astype(BF16) for grad in (grad_q, grad_k, grad_val)]
        total = sum(nt(low, w3_v[n]) for n, low in enumerate(lows))
        part_v[here, :] = total.astype(BF16)
        tails[0] += fold_rows(total * one_v[here, :].astype(F32))
        tails[1] += fold_rows(total)
        for n, low in enumerate(lows):
            grad_v[here, pl.ds(n * local, local)] = low
        move(part_v.at[here, :], part.at[here, :], last_sems.at[i]).start()
        return carry

    lax.fori_loop(0, rows // big, finish, 0)
    for i in range(rows // big):
        here = pl.ds(i * big, big)
        stores.append(move(part_v.at[here, :], part.at[here, :], last_sems.at[i]))
    units = g_bin.shape[1]
    listed = [tails[0], tails[1], sums[0], sums[1], sums[2], g_bout[...], tails[2]]
    listed += [g_bin[:, pl.ds(n, width)] for n in range(0, units, width)]
    half = width // 2
    listed = [row_sum(block) for block in listed]
    for n, block in enumerate(listed):
        short[pl.ds(n, 1), :] = block
    if part_rows:
        sources = [
            (jnp.concatenate(listed[:6] + [jnp.zeros((2, width), F32)], axis=0), part_rows),
            (jnp.broadcast_to(listed[6][:, :local], (8, local)), local * part_rows // width),
            (jnp.broadcast_to(listed[6][:, local:], (8, local)), local * part_rows // width),
            (
                jnp.broadcast_to(jnp.concatenate(listed[7:], axis=1), (8, units)),
                units * part_rows // width,
            ),
        ]
        rest = jnp.zeros((part_rows - 8 * len(sources), LANES), F32)
        for start, place, count in blocks:
            for row in range(0, count, part_rows):
                d = (start + row) // part_rows
                parts = [
                    pltpu.roll(source, (source.shape[1] - d * size) % source.shape[1], 1)[:, :LANES]
                    for source, size in sources
                ]
                side, at = divmod(place + row, half)
                out[side, pl.ds(at, part_rows), pl.ds(4 * local, LANES)] = jnp.concatenate(
                    parts + [rest], axis=0
                ).astype(BF16)
    for side in range(2):
        lines = pl.ds(side * half, half)
        for n in range(3):
            cols = pl.ds(n * local, local)
            out[side, :, cols] = nn(n1_t[lines, :], grad_v[:, cols]).astype(BF16)
        out[side, :, pl.ds(3 * local, local)] = nn(gh_t[lines, :], att_v[...]).astype(BF16)
    for n, (side, target) in enumerate([(1 - kept_side, send), (kept_side, keep)]):
        stores.append(move(out.at[side], target, out_sems.at[1 + n]))
        stores[-1].start()
    wait_all(stores)


def attention_back(
    lead_rows, part_rows, flags, vecs, segment, lse, g_bin, g_bout, g_own, g_oth, cot, normed, inv,
    wp, att, k, q, v, w3, n1, normed_one,
):
    rows, width = cot.shape
    local = wp.shape[0]
    window = min(rows, LANES + 2 * MAX_CLIP)
    tall, thin = pltpu.VMEM((rows, width), BF16), pltpu.VMEM((rows, local), BF16)
    turned = pltpu.VMEM((width, rows), BF16)
    half = (width // 2, 4 * local + (LANES if part_rows else 0))
    return pl.pallas_call(
        functools.partial(attention_back_kernel, lead_rows, part_rows),
        out_shape=(
            shape((rows, width), F32),
            shape((rows, width), BF16),
            shape(half, BF16),
            shape(half, BF16),
            shape((7 + g_bin.shape[1] // width, width), F32),
        ),
        in_specs=[smem()] + [vmem()] * 5 + [hbm()] + [anywhere()] + [hbm()] * 11,
        out_specs=[hbm()] * 4 + [vmem()],
        scratch_shapes=[
            pltpu.VMEM((rows, width), F32),
            tall, tall, tall, tall,
            pltpu.VMEM((rows, LANES), F32),
            pltpu.VMEM(wp.shape, BF16),
            thin, thin, thin, thin,
            pltpu.VMEM(w3.shape, BF16),
            tall, tall, tall, tall,
            pltpu.VMEM((3, 8, width), F32),
            pltpu.VMEM((3, 8, width), F32),
            thin,
            pltpu.VMEM((local, rows), BF16),
            pltpu.VMEM((local, rows), F32),
            pltpu.VMEM((rows, local), F32),
            pltpu.VMEM((rows, local), F32),
            pltpu.VMEM((8, rows), F32),
            pltpu.VMEM((rows, LANES), F32),
            pltpu.VMEM((window, 2 * LANES), F32),
            pltpu.VMEM((2, window, 2 * LANES), F32),
            pltpu.VMEM((2, window, 2 * LANES), F32),
            pltpu.VMEM((2, window, 2 * LANES), BF16),
            pltpu.VMEM((2, window, 2 * LANES), BF16),
            turned, turned,
            pltpu.VMEM((rows, 3 * local), BF16),
            pltpu.VMEM((2,) + half, BF16),
            pltpu.SemaphoreType.DMA((8,)),
            pltpu.SemaphoreType.DMA((5, PARTS)),
            pltpu.SemaphoreType.DMA((3,)),
            pltpu.SemaphoreType.DMA((rows // 256,)),
        ],
        compiler_params=params(60),
        cost_estimate=SMALL,
        name="attention_back",
    )(
        flags, vecs, segment, lse, g_bin, g_bout, g_own, g_oth, cot, normed, inv,
        wp, att, k, q, v, w3, n1, normed_one,
    )


def mixed_back_kernel(blend, flags, vecs, gh, g_own, g_oth, normed, inv, outgoing, kept, *refs):
    gh_v, own_v, oth_v, normed_v, inv_v, leave_v, kept_v, in_sems, out_sems, leave_sems = refs
    ratio = blend[0]
    rows, width = gh.shape
    blk = 32
    piece = leave_v.shape[1]
    loads = [(gh, gh_v), (g_own, own_v), (g_oth, oth_v), (normed, normed_v), (inv, inv_v)]
    stores = [(kept_v, kept)]
    start_parts(loads, in_sems)

    def norm(low):
        here = pl.ds(low, blk)
        grad = own_v[here, :].astype(F32) + oth_v[here, :].astype(F32)
        plain = normed_v[here, :].astype(F32)
        scaled = grad * vecs[0:1, :]
        mean_one = jnp.mean(scaled, axis=-1, keepdims=True)
        mean_two = jnp.mean(scaled * plain, axis=-1, keepdims=True)
        scale = wide_rsqrt(inv_v, here, width)
        back = gh_v[here, :] + scale * (scaled - mean_one - plain * mean_two)
        leave = ((1.0 - ratio) * back).astype(BF16)
        leave_v[pl.ds(low // piece, blk // piece)] = leave.reshape(blk // piece, piece, width)
        kept_v[here, :] = (ratio * back).astype(BF16)

    row_parts(rows, blk, lambda c: wait_all(part_move(loads, in_sems, c)), norm)
    start_parts(stores, out_sems)
    if len(outgoing.shape) == 3:
        leaves = [move(leave_v, outgoing, leave_sems.at[0])]
    else:
        count = outgoing.shape[0]
        leaves = [
            move(
                leave_v.at[pl.ds(pl.multiple_of((2 * m + flags[0]) * count, count), count)],
                outgoing.at[:, m],
                leave_sems.at[m],
            )
            for m in range(2)
        ]
    start_all(leaves)
    for c in range(PARTS):
        wait_all(part_move(stores, out_sems, c))
    wait_all(leaves)


def mixed_back(piece, ordered, blend, flags, vecs, gh, g_own, g_oth, normed, inv):
    rows, width = gh.shape
    tall = pltpu.VMEM((rows, width), BF16)
    runs = rows // piece
    dims = (runs // 4, 2, piece, width) if ordered else (runs, piece, width)
    return pl.pallas_call(
        mixed_back_kernel,
        out_shape=(shape(dims, BF16), shape((rows, width), BF16)),
        in_specs=[smem(), smem(), vmem()] + [hbm()] * 2 + [anywhere()] + [hbm()] * 2,
        out_specs=[hbm(), hbm()],
        scratch_shapes=[
            pltpu.VMEM((rows, width), F32),
            tall, tall, tall, pltpu.VMEM((rows, LANES), F32),
            pltpu.VMEM((runs, piece, width), BF16),
            tall,
            pltpu.SemaphoreType.DMA((5, PARTS)),
            pltpu.SemaphoreType.DMA((1, PARTS)),
            pltpu.SemaphoreType.DMA((2,)),
        ],
        compiler_params=params(60),
        cost_estimate=SMALL,
        name="mixed_back",
    )(blend, flags, vecs, gh, g_own, g_oth, normed, inv)


def shards(
    tokens,
    mix_blend,
    partner,
    clip_ids,
    gain_one,
    shift_one,
    qkv_weight,
    qv_bias,
    proj_weight,
    proj_bias,
    gain_two,
    shift_two,
    in_weight,
    in_bias,
    out_weight,
    out_bias,
    cotangent,
):
    rows, width = tokens.shape
    dp_count = lax.axis_size("dp")
    both = ("dp", "mp")
    bits = dp_count.bit_length() - 1
    seq = lax.axis_index("dp")
    mp = lax.axis_index("mp")
    core = lax.rem(seq, 2)
    home = core == mp
    all_dp = range(dp_count)

    def joint(d, m):
        return 2 * d + m

    core_swap = [(d, d ^ 1) for d in all_dp]
    home_to_pair = [(joint(d, d & 1), joint(d, 1 - (d & 1))) for d in all_dp]
    pair_to_home = [(joint(d, 1 - (d & 1)), joint(d, d & 1)) for d in all_dp]
    weight_move = home_to_pair + [
        (joint(d, 1 - (d & 1)), joint(d ^ 1, 1 - (d & 1))) for d in all_dp
    ]

    def swap(value):
        return lax.ppermute(value, "dp", core_swap)

    def chip_value(value):
        return jnp.where(home, value, swap(value))

    def after(value, *others):
        return lax.optimization_barrier((value,) + others)[0]

    def half_weight(value):
        return lax.ppermute(value, both, weight_move)

    part_rows = width // dp_count
    lead = min(n for n in range(1, bits) if (part_rows << n) % 16 == 0)
    lead_rows = part_rows << lead
    across = lax.rem(seq >> lead, 2)
    flags = jnp.stack([core, home.astype(jnp.int32), across]).astype(jnp.int32)

    def taken(value, index, axis):
        return lax.dynamic_index_in_dim(value, index, axis, keepdims=False)

    seq_small = chip_value(jnp.concatenate([mix_blend, clip_ids[0].astype(F32)]))
    blend, segment = seq_small[:1], seq_small[1:].reshape(1, rows)
    local = proj_weight.shape[0]
    units = in_bias.shape[0]
    half_small = jnp.concatenate([qv_bias.reshape(-1), in_bias])
    half_small = jnp.where(home, half_small, half_weight(half_small))
    biases = half_small.reshape(-1, width)
    vecs = jnp.stack([gain_one, shift_one, gain_two, shift_two, proj_bias])

    w3 = half_weight(qkv_weight.transpose(1, 0, 2))
    wp = half_weight(proj_weight)

    def two_way(value):
        halves = value.reshape(2, value.shape[0] // 2, value.shape[1])
        one = half_weight(taken(halves, across, 0))
        moves = [(joint(d, 1 - (d & 1)), joint(d ^ (1 << lead), 1 - (d & 1))) for d in all_dp]
        return value, one, lax.ppermute(one, both, moves)

    ids = jnp.arange(2 * dp_count, dtype=jnp.int32)
    piece = rows // (2 * 2 * dp_count)
    sent = tokens.reshape(2, dp_count, 2, piece, width)
    sent = lax.dynamic_index_in_dim(sent, mp, 2, keepdims=False)
    spread = lax.all_to_all(sent.transpose(1, 0, 2, 3), "dp", 0, 0, tiled=True)
    wanted = partner[(ids // 4) * 2 + ids % 2] * 2 + (ids // 2) % 2
    source_of = jnp.sum(
        jnp.where(partner[:, None] == ids[None, :dp_count], ids[:dp_count, None], 0),
        axis=0,
        dtype=jnp.int32,
    )
    source = source_of[ids // 2]
    wanted_back = (source // 2) * 4 + (ids % 2) * 2 + source % 2
    chosen = pick(spread.reshape(2 * dp_count, piece, width), wanted, w3, wp, half_small)
    partner_own = lax.all_to_all(chosen, both, 0, 0, tiled=True).reshape(rows // 2, width)
    w_out = two_way(out_weight)
    w_in = half_weight(after(in_weight, w_out[1]))

    tok = chip_value(tokens)
    cot = chip_value(cotangent)
    cot_t = cot.T
    partner_oth = swap(after(partner_own, tok, cot, vecs, segment, wanted_back))

    mixed, n1, normed_one, inv_one, q, k, v, att, attn_part, lse = attention(
        blend, flags, segment, vecs, biases, tok, partner_own, partner_oth, w3, wp, w_out[2], cot_t
    )
    pair_first = part_rows % 16 == 0
    fed = feed(
        lead_rows, part_rows if pair_first else lead_rows, flags, vecs, biases,
        mixed, attn_part, swap(attn_part), cot, cot_t, w_in, *w_out,
    )
    hidden, out_part, gn2_part, in_keep, in_send, out_keep, out_send = fed[:7]
    normed_two, inv_two, g_bin, g_bout = fed[7:]
    gn2_oth = swap(gn2_part)

    high, mid = dp_count >> (lead + 1), 1 << (lead - 1)
    pair_and_core = pair_to_home + [(joint(d, d & 1), joint(d ^ 1, d & 1)) for d in all_dp]
    pair_diagonal = [(joint(d, 1 - (d & 1)), joint(d ^ 1, d & 1)) for d in all_dp]

    def total(*terms):
        return sum(term.astype(F32) for term in terms)

    def send_across(value):
        return lax.ppermute(value, "dp", [(d, d ^ (1 << lead)) for d in all_dp])

    def send_pair(value):
        value = value.reshape(high, mid, 2, part_rows, -1)
        one = lax.ppermute(taken(value, jnp.where(home, 1 - core, core), 2), both, pair_and_core)
        two = lax.ppermute(taken(value, 1 - core, 2), both, pair_diagonal)
        held = taken(value, core, 2)
        return jnp.where(home, held, jnp.zeros_like(held)), one, two

    def far(value, *others):
        for shift, left in ((1, mid), (lead + 1, high)):
            while left > 1:
                radix = min(4, left)
                left //= radix
                value = value.reshape((-1, left, radix) + value.shape[-2:]).astype(BF16)
                spot = lax.rem(seq >> shift, radix)
                got = [
                    lax.ppermute(
                        taken(value, spot ^ flip, 2),
                        "dp",
                        [(d, d ^ (flip << shift)) for d in all_dp],
                    )
                    for flip in range(1, radix)
                ]
                value = total(taken(value, spot, 2), *after(got, *others))
                shift += radix.bit_length() - 1
        return value.reshape(value.shape[-2:])

    def send_first(keep, send):
        if not pair_first:
            return [keep, send_across(send)]
        one = lax.ppermute(send, both, pair_and_core)
        two = lax.ppermute(keep, both, pair_diagonal)
        return [jnp.where(home, keep, jnp.zeros_like(keep)), one, two]

    def send_second(value):
        if not pair_first:
            return send_pair(value) + (value,)
        value = value.reshape(high, 2, mid, part_rows, -1)
        away = taken(value, 1 - across, 1)
        return taken(value, across, 1), send_across(away), away

    in_got = send_across(in_send)
    out_first = send_first(out_keep, out_send)
    gh, gn1_part, attn_keep, attn_send, short = attention_back(
        lead_rows, part_rows if pair_first else 0, flags, vecs, segment, lse, g_bin, g_bout,
        gn2_part, gn2_oth, cot, normed_two, inv_two, wp, att, k, q, v, w3, n1, normed_one,
    )
    gn1_oth = swap(after(gn1_part, in_got, *out_first))
    attn_first = [attn_keep, send_across(attn_send)]
    in_terms = send_pair(total(in_keep, in_got).astype(BF16))
    ordered = piece % 16 == 0
    outgoing, kept = mixed_back(
        piece if ordered else 16, ordered, blend, flags, vecs, gh, gn1_part, gn1_oth, normed_one, inv_one
    )

    if ordered:
        leaving = outgoing.reshape(2 * dp_count, piece, width)
    else:
        leaving = taken(outgoing.reshape(2, 2, dp_count, piece, width), core, 1)
        leaving = leaving.transpose(1, 0, 2, 3).reshape(2 * dp_count, piece, width)
    back = lax.all_to_all(leaving, both, 0, 0, tiled=True)

    in_value = total(*after(in_terms, leaving)).astype(BF16)
    sum_in = far(in_value)
    out_oth = swap(after(out_part, leaving))
    out_value = total(*after(out_first, in_value)).astype(BF16)
    *out_terms, out_away = send_second(out_value)
    attn_value = total(*after(attn_first, out_away)).astype(BF16)
    attn_terms = send_pair(attn_value)
    block = hidden + (out_part.astype(F32) + after(out_oth, attn_value).astype(F32)) + out_bias
    block = block.astype(BF16)
    kept = kept.reshape(2, rows // 2, width)
    kept_got = half_weight(taken(kept, 1 - mp, 0))
    block_got = half_weight(block)

    def side_by_side(*groups):
        values = [total(*terms).reshape(high * mid, part_rows, -1) for terms in groups]
        return jnp.concatenate(values, axis=2).astype(BF16)

    returning = pick(back, wanted_back, attn_value, sum_in)
    returned = lax.all_to_all(
        returning.reshape(dp_count, 2, piece, width), "dp", 0, 0, tiled=True
    )
    returned = after(returned, kept_got)
    kept = jnp.where(home, taken(kept, mp, 0), kept_got)
    returned = returned.transpose(1, 0, 2, 3).reshape(rows // 2, width)
    mine = (kept.astype(F32) + returned.astype(F32)).astype(BF16)
    other = lax.ppermute(mine, "mp", [(0, 1), (1, 0)])
    block_out = jnp.where(home, block, after(block_got, mine))
    grad_tokens = jnp.where(
        jnp.arange(2)[:, None, None] == mp, mine[None], other[None]
    ).reshape(rows, width)

    marker = swap(returning[0, :, :LANES])
    summed = far(
        side_by_side(*(after(terms, marker) for terms in (out_terms, attn_terms))),
        block_out,
    )
    sum_out, sum_attn = after(summed[:, :units], other), summed[:, units:]
    sum_qkv = sum_attn[:, : 3 * local].reshape(-1, 3, local)
    sum_proj = sum_attn[:, 3 * local : 4 * local].T
    quarter, eighth = local // dp_count, units // dp_count
    if pair_first:
        extra = sum_attn[:, 4 * local :]
        plain = extra[:6, :part_rows]
        ours = plain[:2] + lax.ppermute(plain[:2], "mp", [(0, 1), (1, 0)])
        plain = jnp.concatenate([ours, plain[2:]])
        sum_qv = jnp.stack([extra[8, :quarter], extra[16, :quarter]])
        sum_bin = extra[24, :eighth]
    else:
        counts = jnp.where((core == 0) | (jnp.arange(6) < 2), 1.0, 0.0).astype(F32)
        wide = (short[:6] * counts[:, None]).reshape(6, dp_count, 1, part_rows)
        wide = jnp.broadcast_to(wide, (6, dp_count, 2, part_rows)).transpose(1, 2, 0, 3)
        to_half = (jnp.arange(2) == core)[None, :, None]

        def half_terms(vectors):
            terms = vectors.reshape(vectors.shape[0], dp_count, -1).transpose(1, 0, 2)
            return jnp.where(to_half, terms.reshape(dp_count, 1, -1), 0.0)

        short = jnp.concatenate(
            [
                wide.reshape(dp_count, 2, -1),
                half_terms(short[6].reshape(2, local)),
                half_terms(short[7:].reshape(1, units)),
            ],
            axis=-1,
        ).reshape(2 * dp_count, -1)
        short = jnp.sum(lax.all_to_all(short, both, 0, 0, tiled=True), axis=0)
        plain = short[: 6 * part_rows].reshape(6, part_rows)
        sum_qv = short[6 * part_rows : 6 * part_rows + 2 * quarter].reshape(2, -1)
        sum_bin = short[6 * part_rows + 2 * quarter :]
    return (
        block_out,
        grad_tokens,
        plain[0],
        plain[1],
        sum_qkv,
        sum_qv,
        sum_proj,
        plain[4],
        plain[2],
        plain[3],
        sum_in,
        sum_bin,
        sum_out.T,
        plain[5],
    )


def solution(mesh):
    return jax.shard_map(
        shards,
        mesh=mesh,
        in_specs=(
            P("dp", None),
            P("dp"),
            P(),
            P("dp", None),
            P(),
            P(),
            P(None, None, "mp"),
            P(None, "mp"),
            P("mp", None),
            P(),
            P(),
            P(),
            P(None, "mp"),
            P("mp"),
            P("mp", None),
            P(),
            P("dp", None),
        ),
        out_specs=(
            P("dp", None),
            P("dp", None),
            P("dp"),
            P("dp"),
            P("dp", None, "mp"),
            P(None, ("mp", "dp")),
            P("mp", "dp"),
            P("dp"),
            P("dp"),
            P("dp"),
            P("dp", "mp"),
            P(("mp", "dp")),
            P("mp", "dp"),
            P("dp"),
        ),
        check_vma=False,
    )
```

```python
import functools

import jax
import jax.numpy as jnp
from jax import lax
from jax.experimental import pallas as pl
from jax.experimental.pallas import tpu as pltpu
from jax.sharding import PartitionSpec as P

HEAD_DIM = 64
NORM_EPS = 1e-06
NEG_FILL = -1e30
SCORE_SCALE = HEAD_DIM ** (-0.5)
MAX_CLIP = 256
LANES = 128
F32 = jnp.float32
BF16 = jnp.bfloat16
MIB = 1 << 20
SMALL = pl.CostEstimate(flops=1 << 20, bytes_accessed=1 << 20, transcendentals=0)


def nn(left, right):
    return lax.dot_general(left, right, (((1,), (0,)), ((), ())), preferred_element_type=F32)


def nt(left, right):
    return lax.dot_general(left, right, (((1,), (1,)), ((), ())), preferred_element_type=F32)


def vmem():
    return pl.BlockSpec(memory_space=pltpu.VMEM)


def hbm():
    return pl.BlockSpec(memory_space=pltpu.HBM)


def anywhere():
    return pl.BlockSpec(memory_space=pl.ANY)


def smem():
    return pl.BlockSpec(memory_space=pltpu.SMEM)


def params(mib):
    return pltpu.CompilerParams(vmem_limit_bytes=mib * MIB)


def shape(dims, dtype):
    return jax.ShapeDtypeStruct(dims, dtype)


def row_stats(vector):
    mean = jnp.mean(vector, axis=-1, keepdims=True)
    centred = vector - mean
    spread = jnp.mean(centred * centred, axis=-1, keepdims=True)
    return centred, lax.rsqrt(spread + NORM_EPS)


def on_lanes(column):
    return jnp.broadcast_to(column, (column.shape[0], LANES))


def wide_rsqrt(inv, here, width):
    return jnp.concatenate([inv[here, :]] * (width // LANES), axis=1)


def row_sum(block):
    return jnp.sum(block, axis=0, keepdims=True)


def fold_rows(block):
    rows, width = block.shape
    return jnp.sum(block.reshape(rows // 8, 8, width), axis=0)


def pick_kernel(index, source, *refs):
    picked = refs[-1]

    def move(i, carry):
        picked[i] = source[index[i]]
        return carry

    lax.fori_loop(0, picked.shape[0], move, 0, unroll=4)


def pick(source, index, *after):
    dims = index.shape + source.shape[1:]
    return pl.pallas_call(
        pick_kernel,
        out_shape=shape(dims, source.dtype),
        in_specs=[smem(), vmem()] + [hbm()] * len(after),
        out_specs=vmem(),
        compiler_params=params(16),
        cost_estimate=SMALL,
        name="pick",
    )(index, source, *after)


def move(source, target, sem):
    return pltpu.make_async_copy(source, target, sem)


PARTS = 4


def part_move(pairs, sems, c, first=0):
    moves = []
    for n, (source, target) in enumerate(pairs):
        count = source.shape[0] // PARTS
        here = pl.ds(pl.multiple_of(c * count, count), count)
        moves.append(move(source.at[here, :], target.at[here, :], sems.at[first + n, c]))
    return moves


def start_parts(pairs, sems):
    for c in range(PARTS):
        start_all(part_move(pairs, sems, c))


def row_parts(rows, blk, wait, body):
    steps = rows // PARTS // blk

    def part(c, carry):
        wait(c)

        def step(i, carry):
            body(pl.multiple_of((c * steps + i) * blk, blk))
            return carry

        return lax.fori_loop(0, steps, step, carry, unroll=4)

    lax.fori_loop(0, PARTS, part, 0)


def start_all(moves):
    for one in moves:
        one.start()


def wait_all(moves):
    for one in moves:
        one.wait()


def interleave(*streams):
    order = sorted(
        ((n + 0.5) / len(stream), which, n)
        for which, stream in enumerate(streams)
        for n in range(len(stream))
    )
    for _, which, n in order:
        streams[which][n]()


def spread_clips(seg_row, seg_b):
    for i in range(seg_b.shape[0] // LANES):
        here = pl.ds(i * LANES, LANES)
        seg_b[here, :] = jnp.broadcast_to(seg_row[:, here], (LANES, LANES)).T


def key_window(j, rows):
    window = min(rows, LANES + 2 * MAX_CLIP)
    here = pl.ds(pl.multiple_of(j * LANES, LANES), LANES)
    first = pl.multiple_of(jnp.clip(j * LANES - MAX_CLIP, 0, rows - window), LANES)
    return here, pl.ds(first, window)


def set_bias(bias, seg_b, seg_row, here, keys):
    filled = jnp.where(seg_b[keys, :] == seg_row[:, here], 0.0, NEG_FILL)
    bias[:, pl.ds(0, LANES)] = filled
    bias[:, pl.ds(LANES, LANES)] = filled


def two_heads(block):
    lane = lax.broadcasted_iota(jnp.int32, block.shape, 1)
    return jnp.concatenate(
        [block * (lane // HEAD_DIM == e).astype(BF16) for e in range(2)], axis=0
    )


def attention_kernel(
    blend, flags, seg_row, vecs, biases, tok, own, oth, w3, wp, *refs
):
    mixed, n1, normed, inv, q, k, v, att, part, lse = refs[-32:-22]
    (
        tok_v, own_v, oth_v, w3_v, wp_v, mixed_v, n1_v, q_v, k_v, v_v, att_v, part_v,
        vt, att_t, seg_b, bias, ones, normed_v, inv_v, in_sems, half_sems, out_sems,
    ) = refs[-22:]
    rows, width = tok.shape
    local = wp.shape[0]
    half_rows = rows // 2
    ratio = blend[0]
    blk = 32
    big = 256

    loads = [
        move(source, target, in_sems.at[n])
        for n, (source, target) in enumerate([(tok, tok_v), (w3, w3_v), (wp, wp_v)])
    ]
    halves = [(own, own_v), (oth, oth_v)]
    loads[0].start()
    start_parts(halves, half_sems)
    start_all(loads[1:])
    early = [
        move(source, target, out_sems.at[n])
        for n, (source, target) in enumerate(
            [
                (mixed_v, mixed), (n1_v, n1), (normed_v, normed), (inv_v, inv),
                (q_v, q), (k_v, k), (v_v, v),
            ]
        )
    ]
    ones[...] = jnp.ones_like(ones)
    spread_clips(seg_row, seg_b)

    loads[0].wait()
    for n, src, half in ((0, own_v, flags[0]), (1, oth_v, 1 - flags[0])):

        def mix(low, src=src, half=half):
            here = pl.ds(pl.multiple_of(half * half_rows + low, blk), blk)
            there = pl.ds(low, blk)
            mine, other = tok_v[here, :].astype(F32), src[there, :].astype(F32)
            blended = ratio * mine + (1.0 - ratio) * other
            mixed_v[here, :] = blended
            centred, scale = row_stats(blended)
            inv_v[here, :] = on_lanes(scale)
            plain = centred * scale
            normed_v[here, :] = plain.astype(BF16)
            n1_v[here, :] = (plain * vecs[0:1, :] + vecs[1:2, :]).astype(BF16)

        row_parts(
            half_rows, blk, lambda c, n=n: wait_all(part_move([halves[n]], half_sems, c, n)), mix
        )
    start_all(early[:4])

    loads[1].wait()
    for i in range(rows // big):
        here = pl.ds(i * big, big)
        rows_in = n1_v[here, :]
        queries = (nn(rows_in, w3_v[0]) + biases[0:1, :local]).astype(BF16).astype(F32)
        q_v[here, :] = (queries * SCORE_SCALE).astype(BF16)
        k_v[here, :] = nn(rows_in, w3_v[1]).astype(BF16)
        values = (nn(rows_in, w3_v[2]) + biases[0:1, local:]).astype(BF16)
        v_v[here, :] = values
        vt[:, here] = values.T
    start_all(early[4:])

    def attend(j, carry):
        here, keys = key_window(j, rows)
        set_bias(bias, seg_b, seg_row, here, keys)
        for p in range(local // LANES):
            pair = pl.ds(p * LANES, LANES)
            scores = nt(k_v[keys, pair], two_heads(q_v[here, pair])) + bias[...]
            top = jnp.max(scores, axis=0, keepdims=True)
            grown = jnp.exp(scores - top).astype(BF16)
            total = nn(ones[...], grown)[:1]
            out = (nn(vt[pair, keys], grown) / total).astype(BF16)
            logs = top + jnp.log(total)
            for e in range(2):
                lanes = slice(e * LANES, e * LANES + LANES)
                head = slice(e * HEAD_DIM, e * HEAD_DIM + HEAD_DIM)
                att_t[pl.ds(p * LANES + e * HEAD_DIM, HEAD_DIM), here] = out[head, lanes]
                lse[pl.ds(2 * p + e, 1), here] = logs[:, lanes]
        return carry

    lax.fori_loop(0, rows // LANES, attend, 0)

    loads[2].wait()
    last = []
    for i in range(rows // big):
        here = pl.ds(i * big, big)
        block = att_t[:, here].T
        att_v[here, :] = block
        part_v[here, :] = nn(block, wp_v[...]).astype(BF16)
        last.append(move(part_v.at[here, :], part.at[here, :], out_sems.at[8 + i]))
        last[-1].start()
    last.append(move(att_v, att, out_sems.at[7]))
    last[-1].start()
    wait_all(early + last)


def attention(blend, flags, segment, vecs, biases, tok, own, oth, w3, wp, *before):
    rows, width = tok.shape
    local = wp.shape[0]
    window = min(rows, LANES + 2 * MAX_CLIP)
    thin = shape((rows, local), BF16)
    tall = shape((rows, width), BF16)
    return pl.pallas_call(
        attention_kernel,
        out_shape=(
            shape((rows, width), F32), tall, tall, shape((rows, LANES), F32),
            thin, thin, thin, thin, tall, shape((local // HEAD_DIM, rows), F32),
        ),
        in_specs=[smem(), smem()] + [vmem()] * 3 + [anywhere()] * 3 + [hbm()] * (2 + len(before)),
        out_specs=[hbm()] * 9 + [vmem()],
        scratch_shapes=[
            pltpu.VMEM((rows, width), BF16),
            pltpu.VMEM((rows // 2, width), BF16),
            pltpu.VMEM((rows // 2, width), BF16),
            pltpu.VMEM(w3.shape, BF16),
            pltpu.VMEM(wp.shape, BF16),
            pltpu.VMEM((rows, width), F32),
            pltpu.VMEM((rows, width), BF16),
            pltpu.VMEM((rows, local), BF16),
            pltpu.VMEM((rows, local), BF16),
            pltpu.VMEM((rows, local), BF16),
            pltpu.VMEM((rows, local), BF16),
            pltpu.VMEM((rows, width), BF16),
            pltpu.VMEM((local, rows), BF16),
            pltpu.VMEM((local, rows), BF16),
            pltpu.VMEM((rows, LANES), F32),
            pltpu.VMEM((window, 2 * LANES), F32),
            pltpu.VMEM((16, window), BF16),
            pltpu.VMEM((rows, width), BF16),
            pltpu.VMEM((rows, LANES), F32),
            pltpu.SemaphoreType.DMA((3,)),
            pltpu.SemaphoreType.DMA((2, PARTS)),
            pltpu.SemaphoreType.DMA((8 + rows // 256,)),
        ],
        compiler_params=params(60),
        cost_estimate=SMALL,
        name="attention",
    )(
        blend, flags, segment, vecs, biases, tok, own, oth, w3, wp, *before,
    )


ERFC_SLOPE = 0.47
ERFC_COEFFS = (
    0.2663094668265691,
    0.2480096137831850,
    0.3362712657560771,
    -0.1262288063821733,
    0.6076790117752645,
    -0.4204702410368928,
    0.0884296765518492,
)


def gelu_parts(pre):
    bell = jnp.exp(pre * pre * -0.5)
    t = 1.0 / (1.0 + jnp.abs(pre) * (ERFC_SLOPE * 0.5**0.5))
    poly = 0.5 * ERFC_COEFFS[-1]
    for coeff in ERFC_COEFFS[-2::-1]:
        poly = poly * t + 0.5 * coeff
    tail = poly * t * bell
    cdf = jnp.where(pre >= 0, 1.0 - tail, tail)
    return pre * cdf, cdf + pre * bell * 0.3989422804014327


def turn_into(target, source, blocks):
    rows = source.shape[0]
    big = 256
    for i in range(rows // big):
        here = pl.ds(i * big, big)
        turned = source[here, :].T
        for start, place, count in blocks:
            target[pl.ds(place, count), here] = turned[start : start + count]


def lead_blocks(width, lead_rows):
    runs = width // lead_rows
    return [
        (run * lead_rows, ((run % 2) * (runs // 2) + run // 2) * lead_rows, lead_rows)
        for run in range(runs)
    ]


def feed_kernel(
    in_rows, out_rows, flags, vecs, biases, mixed, p_own, p_oth, cot, cot_t,
    w_in, w_out, w_out_one, w_out_two,
    hidden, part, gn_part, in_keep, in_send, out_keep, out_send, normed, inv, g_bin, g_bout,
    mixed_v, own_v, oth_v, cot_v, cot_tv, w_in_v, w_out_v, n2, n2_t, act, gp,
    g_in, g_out, normed_v, inv_v, in_sems, turn_sems, weight_sems, out_sems, grad_sems,
):
    rows, width = mixed.shape
    units = w_in.shape[1]
    blk = 32
    big = 256
    sub = 16
    home = flags[1] == 1
    across = flags[2]
    kept_out = jnp.where(home, flags[0], 1 - flags[0]) if in_rows != out_rows else across
    sides = (across, kept_out)

    loads = [(mixed, mixed_v), (p_own, own_v), (p_oth, oth_v), (cot, cot_v)]
    start_parts(loads, in_sems)

    weights = [move(w_in, w_in_v, weight_sems.at[0])]
    weights[0].start()
    half = w_out.shape[0] // 2
    for n, (got, place) in enumerate([(w_out_one, across), (w_out_two, 1 - across)]):
        spot = pl.ds(pl.multiple_of(place * half, half), half)
        sem = weight_sems.at[1 + n]
        weights.append(move(w_out.at[spot, :], w_out_v.at[spot, :], sem))

        @pl.when(home)
        def _(spot=spot, sem=sem):
            move(w_out.at[spot, :], w_out_v.at[spot, :], sem).start()

        @pl.when(jnp.logical_not(home))
        def _(got=got, spot=spot, sem=sem):
            move(got, w_out_v.at[spot, :], sem).start()

    turns = [
        move(cot_t.at[pl.ds(start, count), :], cot_tv.at[pl.ds(place, count), :], turn_sems.at[n])
        for n, (start, place, count) in enumerate(lead_blocks(width, out_rows))
    ]
    start_all(turns)

    g_bout[...] = jnp.zeros_like(g_bout)

    def norm(low):
        here = pl.ds(low, blk)
        attn = own_v[here, :].astype(F32) + oth_v[here, :].astype(F32)
        total = mixed_v[here, :] + attn + vecs[4:5, :]
        mixed_v[here, :] = total
        centred, scale = row_stats(total)
        inv_v[here, :] = on_lanes(scale)
        plain = centred * scale
        normed_v[here, :] = plain.astype(BF16)
        n2[here, :] = (plain * vecs[2:3, :] + vecs[3:4, :]).astype(BF16)
        g_bout[...] += fold_rows(cot_v[here, :].astype(F32))

    row_parts(rows, blk, lambda c: wait_all(part_move(loads, in_sems, c)), norm)
    stores = [
        move(source, target, out_sems.at[0, n])
        for n, (source, target) in enumerate(
            [(mixed_v, hidden), (normed_v, normed), (inv_v, inv)]
        )
    ]
    start_all(stores)
    turn_into(n2_t, n2, lead_blocks(width, in_rows))
    wait_all(weights)

    g_bin[...] = jnp.zeros_like(g_bin)

    def row_block(i):
        here = pl.ds(pl.multiple_of(i * big, big), big)
        for j in range(units // width):
            cols = pl.ds(j * width, width)
            pre_all = nn(n2[here, :], w_in_v[:, cols])
            grad_all = nt(cot_v[here, :], w_out_v[cols, :])
            sums = jnp.zeros((8, width), F32)
            for s in range(big // sub):
                rng = slice(s * sub, s * sub + sub)
                value, slope = gelu_parts(pre_all[rng] + biases[1 + j : 2 + j, :])
                grad = grad_all[rng] * slope
                sums += fold_rows(grad)
                spot = pl.ds(pl.multiple_of(i * big + s * sub, sub), sub)
                act[spot, cols] = value.astype(BF16)
                gp[spot, cols] = grad.astype(BF16)
            g_bin[:, cols] += sums
        oth_v[here, :] = nt(gp[here, :], w_in_v[...]).astype(BF16)
        own_v[here, :] = nn(act[here, :], w_out_v[...]).astype(BF16)
        for n, (source, target) in enumerate([(oth_v, gn_part), (own_v, part)]):
            move(source.at[here, :], target.at[here, :], out_sems.at[1 + n, i]).start()

    for i in range(rows // big):
        row_block(i)
    for i in range(rows // big):
        here = pl.ds(i * big, big)
        for n, (source, target) in enumerate([(oth_v, gn_part), (own_v, part)]):
            stores.append(move(source.at[here, :], target.at[here, :], out_sems.at[1 + n, i]))

    wait_all(turns)
    half = width // 2
    for n, (turned, right, buf, keep, send) in enumerate(
        [(n2_t, gp, g_in, in_keep, in_send), (cot_tv, act, g_out, out_keep, out_send)]
    ):
        for side in range(2):
            lines = pl.ds(side * half, half)
            for j in range(units // width):
                cols = pl.ds(j * width, width)
                buf[side, :, cols] = nn(turned[lines, :], right[:, cols]).astype(BF16)
        for m, (side, target) in enumerate([(1 - sides[n], send), (sides[n], keep)]):
            stores.append(move(buf.at[side], target, grad_sems.at[n, m]))
            stores[-1].start()
    wait_all(stores)


def feed(
    in_rows, out_rows, flags, vecs, biases, mixed, p_own, p_oth, cot, cot_t,
    w_in, w_out, w_out_one, w_out_two,
):
    rows, width = mixed.shape
    units = w_in.shape[1]
    tall = shape((rows, width), BF16)
    grad = shape((width // 2, units), BF16)
    return pl.pallas_call(
        functools.partial(feed_kernel, in_rows, out_rows),
        out_shape=(
            shape((rows, width), F32), tall, tall, grad, grad, grad, grad,
            tall, shape((rows, LANES), F32), shape((8, units), F32), shape((8, width), F32),
        ),
        in_specs=[smem()] + [vmem()] * 2 + [hbm()] * 2 + [anywhere()] + [hbm()] * 6,
        out_specs=[hbm()] * 9 + [vmem()] * 2,
        scratch_shapes=[
            pltpu.VMEM((rows, width), F32),
            pltpu.VMEM((rows, width), BF16),
            pltpu.VMEM((rows, width), BF16),
            pltpu.VMEM((rows, width), BF16),
            pltpu.VMEM((width, rows), BF16),
            pltpu.VMEM(w_in.shape, BF16),
            pltpu.VMEM(w_out.shape, BF16),
            pltpu.VMEM((rows, width), BF16),
            pltpu.VMEM((width, rows), BF16),
            pltpu.VMEM((rows, units), BF16),
            pltpu.VMEM((rows, units), BF16),
            pltpu.VMEM((2, width // 2, units), BF16),
            pltpu.VMEM((2, width // 2, units), BF16),
            pltpu.VMEM((rows, width), BF16),
            pltpu.VMEM((rows, LANES), F32),
            pltpu.SemaphoreType.DMA((4, PARTS)),
            pltpu.SemaphoreType.DMA((width // out_rows,)),
            pltpu.SemaphoreType.DMA((3,)),
            pltpu.SemaphoreType.DMA((3, rows // 256)),
            pltpu.SemaphoreType.DMA((2, 2)),
        ],
        compiler_params=params(60),
        cost_estimate=SMALL,
        name="feed",
    )(
        flags, vecs, biases, mixed, p_own, p_oth, cot, cot_t,
        w_in, w_out, w_out_one, w_out_two,
    )


def attention_back_kernel(
    lead_rows, part_rows, flags, vecs, seg_row, lse, g_bin, g_bout, g_own, g_oth, cot, normed, inv,
    wp, att, k, q, v, w3, n1, normed_one,
    gh, part, keep, send, short,
    gh_v, own_v, oth_v, cot_v, normed_v, inv_v, wp_v, att_v, k_v, q_v, v_v, w3_v, n1_v, one_v, low_v, part_v,
    sums, tails, d_out, kt, dq_t, dk, dv, delta, seg_b, bias, raw, raw_g, low_p, low_g, n1_t, gh_t, grad_v, out,
    in_sems, row_sems, out_sems, last_sems,
):
    rows, width = cot.shape
    local = wp.shape[0]
    blk = 32
    big = 256
    blocks = lead_blocks(width, lead_rows)
    kept_side = flags[2]
    row_loads = [(g_own, own_v), (g_oth, oth_v), (cot, cot_v), (normed, normed_v), (inv, inv_v)]
    start_parts(row_loads, row_sems)
    loads = [
        move(source, target, in_sems.at[n])
        for n, (source, target) in enumerate(
            [
                (wp, wp_v), (att, att_v), (k, k_v), (q, q_v), (v, v_v), (w3, w3_v), (n1, n1_v),
                (normed_one, one_v),
            ]
        )
    ]
    start_all(loads)
    sums[...] = jnp.zeros_like(sums)
    dk[...] = jnp.zeros_like(dk)
    dv[...] = jnp.zeros_like(dv)
    spread_clips(seg_row, seg_b)

    def norm(low):
        here = pl.ds(low, blk)
        grad = own_v[here, :].astype(F32) + oth_v[here, :].astype(F32)
        plain = normed_v[here, :].astype(F32)
        scaled = grad * vecs[2:3, :]
        mean_one = jnp.mean(scaled, axis=-1, keepdims=True)
        mean_two = jnp.mean(scaled * plain, axis=-1, keepdims=True)
        scale = wide_rsqrt(inv_v, here, width)
        back = cot_v[here, :].astype(F32) + scale * (scaled - mean_one - plain * mean_two)
        gh_v[here, :] = back
        low_v[here, :] = back.astype(BF16)
        sums[0] += fold_rows(grad * plain)
        sums[1] += fold_rows(grad)
        sums[2] += fold_rows(back)

    row_parts(rows, blk, lambda c: wait_all(part_move(row_loads, row_sems, c)), norm)
    stores = [move(gh_v, gh, out_sems.at[0])]
    stores[0].start()

    wait_all(loads[:3])
    heads = local // HEAD_DIM
    lane = lax.broadcasted_iota(jnp.int32, (delta.shape[0], local), 1)
    row = lax.broadcasted_iota(jnp.int32, (delta.shape[0], local), 0)
    of_head = (lane // HEAD_DIM == row).astype(BF16)

    def project(i, carry):
        here = pl.ds(pl.multiple_of(i * big, big), big)
        grad_out = nt(low_v[here, :], wp_v[...]).astype(BF16)
        d_out[here, :] = grad_out
        product = grad_out.astype(F32) * att_v[here, :].astype(F32)
        coarse = product.astype(BF16)
        fine = (product - coarse.astype(F32)).astype(BF16)
        delta[:, here] = nt(of_head, coarse) + nt(of_head, fine)
        kt[:, here] = k_v[here, :].T
        return carry

    lax.fori_loop(0, rows // big, project, 0)
    wait_all(loads[3:])

    pairs = heads // 2
    window = bias.shape[0]
    strip = 128
    strips = window // strip

    def attend(j, carry):
        here, keys = key_window(j, rows)
        first = pl.multiple_of(keys.start, LANES)
        set_bias(bias, seg_b, seg_row, here, keys)
        blocks_two = {}

        def two(p):
            if p not in blocks_two:
                pair = pl.ds(p * LANES, LANES)
                blocks_two[p] = (two_heads(q_v[here, pair]), two_heads(d_out[here, pair]))
            return blocks_two[p]

        def at_strip(n):
            return (
                pl.ds(pl.multiple_of(first + n * strip, strip), strip),
                pl.ds(n * strip, strip),
            )

        def products(p):
            pair = pl.ds(p * LANES, LANES)

            def scores(n):
                def run():
                    some, at = at_strip(n)
                    raw[p % 2, at, :] = nt(k_v[some, pair], two(p)[0])

                return run

            def grads(n):
                def run():
                    some, at = at_strip(n)
                    raw_g[p % 2, at, :] = nt(v_v[some, pair], two(p)[1])

                return run

            return [make(n) for n in range(strips) for make in (scores, grads)]

        def softmax_back(p):
            tops = jnp.concatenate([lse[pl.ds(2 * p + e, 1), here] for e in range(2)], axis=1)
            inner = jnp.concatenate([delta[pl.ds(2 * p + e, 1), here] for e in range(2)], axis=1)
            half = strip // 2

            def run_at(n):
                def run():
                    at = pl.ds(n * half, half)
                    probs = jnp.exp(raw[p % 2, at, :] + bias[at, :] - tops)
                    low_p[p % 2, at, :] = probs.astype(BF16)
                    low_g[p % 2, at, :] = (probs * (raw_g[p % 2, at, :] - inner)).astype(BF16)

                return run

            return [run_at(n) for n in range(2 * strips)]

        def sums_of(p):
            pair = pl.ds(p * LANES, LANES)

            def keys_of(n):
                def run():
                    some, at = at_strip(n)
                    dk[some, pair] += nn(low_g[p % 2, at, :], two(p)[0])

                return run

            def values_of(n):
                def run():
                    some, at = at_strip(n)
                    dv[some, pair] += nn(low_p[p % 2, at, :], two(p)[1])

                return run

            def queries():
                grad_q = nn(kt[pair, keys], low_g[p % 2]) * SCORE_SCALE
                for e in range(2):
                    lanes = slice(e * LANES, e * LANES + LANES)
                    head = slice(e * HEAD_DIM, e * HEAD_DIM + HEAD_DIM)
                    dq_t[pl.ds(p * LANES + e * HEAD_DIM, HEAD_DIM), here] = grad_q[head, lanes]

            return [make(n) for n in range(strips) for make in (keys_of, values_of)] + [queries]

        def turns():
            for target, source in ((n1_t, n1_v), (gh_t, low_v)):
                turned = source[here, :].T
                for start, place, count in blocks:
                    target[pl.ds(place, count), here] = turned[start : start + count]

        interleave(products(0), [turns])
        for p in range(pairs):
            matrix = (products(p + 1) if p + 1 < pairs else []) + (sums_of(p - 1) if p else [])
            interleave(softmax_back(p), matrix)
        interleave(sums_of(pairs - 1))
        return carry

    lax.fori_loop(0, rows // LANES, attend, 0)

    tails[...] = jnp.zeros_like(tails)

    def finish(i, carry):
        here = pl.ds(pl.multiple_of(i * big, big), big)
        grad_q, grad_k, grad_val = dq_t[:, here].T, dk[here, :], dv[here, :]
        tails[2, :, pl.ds(0, local)] += fold_rows(grad_q)
        tails[2, :, pl.ds(local, local)] += fold_rows(grad_val)
        lows = [grad.astype(BF16) for grad in (grad_q, grad_k, grad_val)]
        total = sum(nt(low, w3_v[n]) for n, low in enumerate(lows))
        part_v[here, :] = total.astype(BF16)
        tails[0] += fold_rows(total * one_v[here, :].astype(F32))
        tails[1] += fold_rows(total)
        for n, low in enumerate(lows):
            grad_v[here, pl.ds(n * local, local)] = low
        move(part_v.at[here, :], part.at[here, :], last_sems.at[i]).start()
        return carry

    lax.fori_loop(0, rows // big, finish, 0)
    for i in range(rows // big):
        here = pl.ds(i * big, big)
        stores.append(move(part_v.at[here, :], part.at[here, :], last_sems.at[i]))
    units = g_bin.shape[1]
    listed = [tails[0], tails[1], sums[0], sums[1], sums[2], g_bout[...], tails[2]]
    listed += [g_bin[:, pl.ds(n, width)] for n in range(0, units, width)]
    half = width // 2
    listed = [row_sum(block) for block in listed]
    for n, block in enumerate(listed):
        short[pl.ds(n, 1), :] = block
    if part_rows:
        sources = [
            (jnp.concatenate(listed[:6] + [jnp.zeros((2, width), F32)], axis=0), part_rows),
            (jnp.broadcast_to(listed[6][:, :local], (8, local)), local * part_rows // width),
            (jnp.broadcast_to(listed[6][:, local:], (8, local)), local * part_rows // width),
            (
                jnp.broadcast_to(jnp.concatenate(listed[7:], axis=1), (8, units)),
                units * part_rows // width,
            ),
        ]
        rest = jnp.zeros((part_rows - 8 * len(sources), LANES), F32)
        for start, place, count in blocks:
            for row in range(0, count, part_rows):
                d = (start + row) // part_rows
                parts = [
                    pltpu.roll(source, (source.shape[1] - d * size) % source.shape[1], 1)[:, :LANES]
                    for source, size in sources
                ]
                side, at = divmod(place + row, half)
                out[side, pl.ds(at, part_rows), pl.ds(4 * local, LANES)] = jnp.concatenate(
                    parts + [rest], axis=0
                ).astype(BF16)
    for side in range(2):
        lines = pl.ds(side * half, half)
        for n in range(3):
            cols = pl.ds(n * local, local)
            out[side, :, cols] = nn(n1_t[lines, :], grad_v[:, cols]).astype(BF16)
        out[side, :, pl.ds(3 * local, local)] = nn(gh_t[lines, :], att_v[...]).astype(BF16)
    for n, (side, target) in enumerate([(1 - kept_side, send), (kept_side, keep)]):
        stores.append(move(out.at[side], target, out_sems.at[1 + n]))
        stores[-1].start()
    wait_all(stores)


def attention_back(
    lead_rows, part_rows, flags, vecs, segment, lse, g_bin, g_bout, g_own, g_oth, cot, normed, inv,
    wp, att, k, q, v, w3, n1, normed_one,
):
    rows, width = cot.shape
    local = wp.shape[0]
    window = min(rows, LANES + 2 * MAX_CLIP)
    tall, thin = pltpu.VMEM((rows, width), BF16), pltpu.VMEM((rows, local), BF16)
    turned = pltpu.VMEM((width, rows), BF16)
    half = (width // 2, 4 * local + (LANES if part_rows else 0))
    return pl.pallas_call(
        functools.partial(attention_back_kernel, lead_rows, part_rows),
        out_shape=(
            shape((rows, width), F32),
            shape((rows, width), BF16),
            shape(half, BF16),
            shape(half, BF16),
            shape((7 + g_bin.shape[1] // width, width), F32),
        ),
        in_specs=[smem()] + [vmem()] * 5 + [hbm()] + [anywhere()] + [hbm()] * 11,
        out_specs=[hbm()] * 4 + [vmem()],
        scratch_shapes=[
            pltpu.VMEM((rows, width), F32),
            tall, tall, tall, tall,
            pltpu.VMEM((rows, LANES), F32),
            pltpu.VMEM(wp.shape, BF16),
            thin, thin, thin, thin,
            pltpu.VMEM(w3.shape, BF16),
            tall, tall, tall, tall,
            pltpu.VMEM((3, 8, width), F32),
            pltpu.VMEM((3, 8, width), F32),
            thin,
            pltpu.VMEM((local, rows), BF16),
            pltpu.VMEM((local, rows), F32),
            pltpu.VMEM((rows, local), F32),
            pltpu.VMEM((rows, local), F32),
            pltpu.VMEM((8, rows), F32),
            pltpu.VMEM((rows, LANES), F32),
            pltpu.VMEM((window, 2 * LANES), F32),
            pltpu.VMEM((2, window, 2 * LANES), F32),
            pltpu.VMEM((2, window, 2 * LANES), F32),
            pltpu.VMEM((2, window, 2 * LANES), BF16),
            pltpu.VMEM((2, window, 2 * LANES), BF16),
            turned, turned,
            pltpu.VMEM((rows, 3 * local), BF16),
            pltpu.VMEM((2,) + half, BF16),
            pltpu.SemaphoreType.DMA((8,)),
            pltpu.SemaphoreType.DMA((5, PARTS)),
            pltpu.SemaphoreType.DMA((3,)),
            pltpu.SemaphoreType.DMA((rows // 256,)),
        ],
        compiler_params=params(60),
        cost_estimate=SMALL,
        name="attention_back",
    )(
        flags, vecs, segment, lse, g_bin, g_bout, g_own, g_oth, cot, normed, inv,
        wp, att, k, q, v, w3, n1, normed_one,
    )


def mixed_back_kernel(blend, flags, vecs, gh, g_own, g_oth, normed, inv, outgoing, kept, *refs):
    gh_v, own_v, oth_v, normed_v, inv_v, leave_v, kept_v, in_sems, out_sems, leave_sems = refs
    ratio = blend[0]
    rows, width = gh.shape
    blk = 32
    piece = leave_v.shape[1]
    loads = [(gh, gh_v), (g_own, own_v), (g_oth, oth_v), (normed, normed_v), (inv, inv_v)]
    stores = [(kept_v, kept)]
    start_parts(loads, in_sems)

    def norm(low):
        here = pl.ds(low, blk)
        grad = own_v[here, :].astype(F32) + oth_v[here, :].astype(F32)
        plain = normed_v[here, :].astype(F32)
        scaled = grad * vecs[0:1, :]
        mean_one = jnp.mean(scaled, axis=-1, keepdims=True)
        mean_two = jnp.mean(scaled * plain, axis=-1, keepdims=True)
        scale = wide_rsqrt(inv_v, here, width)
        back = gh_v[here, :] + scale * (scaled - mean_one - plain * mean_two)
        leave = ((1.0 - ratio) * back).astype(BF16)
        leave_v[pl.ds(low // piece, blk // piece)] = leave.reshape(blk // piece, piece, width)
        kept_v[here, :] = (ratio * back).astype(BF16)

    row_parts(rows, blk, lambda c: wait_all(part_move(loads, in_sems, c)), norm)
    start_parts(stores, out_sems)
    if len(outgoing.shape) == 3:
        leaves = [move(leave_v, outgoing, leave_sems.at[0])]
    else:
        count = outgoing.shape[0]
        leaves = [
            move(
                leave_v.at[pl.ds(pl.multiple_of((2 * m + flags[0]) * count, count), count)],
                outgoing.at[:, m],
                leave_sems.at[m],
            )
            for m in range(2)
        ]
    start_all(leaves)
    for c in range(PARTS):
        wait_all(part_move(stores, out_sems, c))
    wait_all(leaves)


def mixed_back(piece, ordered, blend, flags, vecs, gh, g_own, g_oth, normed, inv):
    rows, width = gh.shape
    tall = pltpu.VMEM((rows, width), BF16)
    runs = rows // piece
    dims = (runs // 4, 2, piece, width) if ordered else (runs, piece, width)
    return pl.pallas_call(
        mixed_back_kernel,
        out_shape=(shape(dims, BF16), shape((rows, width), BF16)),
        in_specs=[smem(), smem(), vmem()] + [hbm()] * 2 + [anywhere()] + [hbm()] * 2,
        out_specs=[hbm(), hbm()],
        scratch_shapes=[
            pltpu.VMEM((rows, width), F32),
            tall, tall, tall, pltpu.VMEM((rows, LANES), F32),
            pltpu.VMEM((runs, piece, width), BF16),
            tall,
            pltpu.SemaphoreType.DMA((5, PARTS)),
            pltpu.SemaphoreType.DMA((1, PARTS)),
            pltpu.SemaphoreType.DMA((2,)),
        ],
        compiler_params=params(60),
        cost_estimate=SMALL,
        name="mixed_back",
    )(blend, flags, vecs, gh, g_own, g_oth, normed, inv)


def shards(
    tokens,
    mix_blend,
    partner,
    clip_ids,
    gain_one,
    shift_one,
    qkv_weight,
    qv_bias,
    proj_weight,
    proj_bias,
    gain_two,
    shift_two,
    in_weight,
    in_bias,
    out_weight,
    out_bias,
    cotangent,
):
    rows, width = tokens.shape
    dp_count = lax.axis_size("dp")
    both = ("dp", "mp")
    bits = dp_count.bit_length() - 1
    seq = lax.axis_index("dp")
    mp = lax.axis_index("mp")
    core = lax.rem(seq, 2)
    home = core == mp
    all_dp = range(dp_count)

    def joint(d, m):
        return 2 * d + m

    core_swap = [(d, d ^ 1) for d in all_dp]
    home_to_pair = [(joint(d, d & 1), joint(d, 1 - (d & 1))) for d in all_dp]
    pair_to_home = [(joint(d, 1 - (d & 1)), joint(d, d & 1)) for d in all_dp]
    weight_move = home_to_pair + [
        (joint(d, 1 - (d & 1)), joint(d ^ 1, 1 - (d & 1))) for d in all_dp
    ]

    def swap(value):
        return lax.ppermute(value, "dp", core_swap)

    def chip_value(value):
        return jnp.where(home, value, swap(value))

    def after(value, *others):
        return lax.optimization_barrier((value,) + others)[0]

    def half_weight(value):
        return lax.ppermute(value, both, weight_move)

    part_rows = width // dp_count
    lead = min(n for n in range(1, bits) if (part_rows << n) % 16 == 0)
    lead_rows = part_rows << lead
    across = lax.rem(seq >> lead, 2)
    flags = jnp.stack([core, home.astype(jnp.int32), across]).astype(jnp.int32)

    def taken(value, index, axis):
        return lax.dynamic_index_in_dim(value, index, axis, keepdims=False)

    seq_small = chip_value(jnp.concatenate([mix_blend, clip_ids[0].astype(F32)]))
    blend, segment = seq_small[:1], seq_small[1:].reshape(1, rows)
    local = proj_weight.shape[0]
    units = in_bias.shape[0]
    half_small = jnp.concatenate([qv_bias.reshape(-1), in_bias])
    half_small = jnp.where(home, half_small, half_weight(half_small))
    biases = half_small.reshape(-1, width)
    vecs = jnp.stack([gain_one, shift_one, gain_two, shift_two, proj_bias])

    w3 = half_weight(qkv_weight.transpose(1, 0, 2))
    wp = half_weight(proj_weight)

    def two_way(value):
        halves = value.reshape(2, value.shape[0] // 2, value.shape[1])
        one = half_weight(taken(halves, across, 0))
        moves = [(joint(d, 1 - (d & 1)), joint(d ^ (1 << lead), 1 - (d & 1))) for d in all_dp]
        return value, one, lax.ppermute(one, both, moves)

    ids = jnp.arange(2 * dp_count, dtype=jnp.int32)
    piece = rows // (2 * 2 * dp_count)
    sent = tokens.reshape(2, dp_count, 2, piece, width)
    sent = lax.dynamic_index_in_dim(sent, mp, 2, keepdims=False)
    spread = lax.all_to_all(sent.transpose(1, 0, 2, 3), "dp", 0, 0, tiled=True)
    wanted = partner[(ids // 4) * 2 + ids % 2] * 2 + (ids // 2) % 2
    source_of = jnp.sum(
        jnp.where(partner[:, None] == ids[None, :dp_count], ids[:dp_count, None], 0),
        axis=0,
        dtype=jnp.int32,
    )
    source = source_of[ids // 2]
    wanted_back = (source // 2) * 4 + (ids % 2) * 2 + source % 2
    chosen = pick(spread.reshape(2 * dp_count, piece, width), wanted, w3, wp, half_small)
    partner_own = lax.all_to_all(chosen, both, 0, 0, tiled=True).reshape(rows // 2, width)
    w_out = two_way(out_weight)
    w_in = half_weight(after(in_weight, w_out[1]))

    tok = chip_value(tokens)
    cot = chip_value(cotangent)
    cot_t = cot.T
    partner_oth = swap(after(partner_own, tok, cot, vecs, segment, wanted_back))

    mixed, n1, normed_one, inv_one, q, k, v, att, attn_part, lse = attention(
        blend, flags, segment, vecs, biases, tok, partner_own, partner_oth, w3, wp, w_out[2], cot_t
    )
    pair_first = part_rows % 16 == 0
    fed = feed(
        lead_rows, part_rows if pair_first else lead_rows, flags, vecs, biases,
        mixed, attn_part, swap(attn_part), cot, cot_t, w_in, *w_out,
    )
    hidden, out_part, gn2_part, in_keep, in_send, out_keep, out_send = fed[:7]
    normed_two, inv_two, g_bin, g_bout = fed[7:]
    gn2_oth = swap(gn2_part)

    high, mid = dp_count >> (lead + 1), 1 << (lead - 1)
    pair_and_core = pair_to_home + [(joint(d, d & 1), joint(d ^ 1, d & 1)) for d in all_dp]
    pair_diagonal = [(joint(d, 1 - (d & 1)), joint(d ^ 1, d & 1)) for d in all_dp]

    def total(*terms):
        return sum(term.astype(F32) for term in terms)

    def send_across(value):
        return lax.ppermute(value, "dp", [(d, d ^ (1 << lead)) for d in all_dp])

    def send_pair(value):
        value = value.reshape(high, mid, 2, part_rows, -1)
        one = lax.ppermute(taken(value, jnp.where(home, 1 - core, core), 2), both, pair_and_core)
        two = lax.ppermute(taken(value, 1 - core, 2), both, pair_diagonal)
        held = taken(value, core, 2)
        return jnp.where(home, held, jnp.zeros_like(held)), one, two

    def far(value, *others):
        for shift, left in ((1, mid), (lead + 1, high)):
            while left > 1:
                radix = min(4, left)
                left //= radix
                value = value.reshape((-1, left, radix) + value.shape[-2:]).astype(BF16)
                spot = lax.rem(seq >> shift, radix)
                got = [
                    lax.ppermute(
                        taken(value, spot ^ flip, 2),
                        "dp",
                        [(d, d ^ (flip << shift)) for d in all_dp],
                    )
                    for flip in range(1, radix)
                ]
                value = total(taken(value, spot, 2), *after(got, *others))
                shift += radix.bit_length() - 1
        return value.reshape(value.shape[-2:])

    def send_first(keep, send):
        if not pair_first:
            return [keep, send_across(send)]
        one = lax.ppermute(send, both, pair_and_core)
        two = lax.ppermute(keep, both, pair_diagonal)
        return [jnp.where(home, keep, jnp.zeros_like(keep)), one, two]

    def send_second(value):
        if not pair_first:
            return send_pair(value) + (value,)
        value = value.reshape(high, 2, mid, part_rows, -1)
        away = taken(value, 1 - across, 1)
        return taken(value, across, 1), send_across(away), away

    in_got = send_across(in_send)
    out_first = send_first(out_keep, out_send)
    gh, gn1_part, attn_keep, attn_send, short = attention_back(
        lead_rows, part_rows if pair_first else 0, flags, vecs, segment, lse, g_bin, g_bout,
        gn2_part, gn2_oth, cot, normed_two, inv_two, wp, att, k, q, v, w3, n1, normed_one,
    )
    gn1_oth = swap(after(gn1_part, in_got, *out_first))
    attn_first = [attn_keep, send_across(attn_send)]
    in_terms = send_pair(total(in_keep, in_got).astype(BF16))
    ordered = piece % 16 == 0
    outgoing, kept = mixed_back(
        piece if ordered else 16, ordered, blend, flags, vecs, gh, gn1_part, gn1_oth, normed_one, inv_one
    )

    if ordered:
        leaving = outgoing.reshape(2 * dp_count, piece, width)
    else:
        leaving = taken(outgoing.reshape(2, 2, dp_count, piece, width), core, 1)
        leaving = leaving.transpose(1, 0, 2, 3).reshape(2 * dp_count, piece, width)
    back = lax.all_to_all(leaving, both, 0, 0, tiled=True)

    in_value = total(*after(in_terms, leaving)).astype(BF16)
    sum_in = far(in_value)
    out_oth = swap(after(out_part, leaving))
    out_value = total(*after(out_first, in_value)).astype(BF16)
    *out_terms, out_away = send_second(out_value)
    attn_value = total(*after(attn_first, out_away)).astype(BF16)
    attn_terms = send_pair(attn_value)
    block = hidden + (out_part.astype(F32) + after(out_oth, attn_value).astype(F32)) + out_bias
    block = block.astype(BF16)
    kept = kept.reshape(2, rows // 2, width)
    kept_got = half_weight(taken(kept, 1 - mp, 0))
    block_got = half_weight(block)

    def side_by_side(*groups):
        values = [total(*terms).reshape(high * mid, part_rows, -1) for terms in groups]
        return jnp.concatenate(values, axis=2).astype(BF16)

    returning = pick(back, wanted_back, attn_value, sum_in)
    returned = lax.all_to_all(
        returning.reshape(dp_count, 2, piece, width), "dp", 0, 0, tiled=True
    )
    returned = after(returned, kept_got)
    kept = jnp.where(home, taken(kept, mp, 0), kept_got)
    returned = returned.transpose(1, 0, 2, 3).reshape(rows // 2, width)
    mine = (kept.astype(F32) + returned.astype(F32)).astype(BF16)
    other = lax.ppermute(mine, "mp", [(0, 1), (1, 0)])
    block_out = jnp.where(home, block, after(block_got, mine))
    grad_tokens = jnp.where(
        jnp.arange(2)[:, None, None] == mp, mine[None], other[None]
    ).reshape(rows, width)

    marker = swap(returning[0, :, :LANES])
    summed = far(
        side_by_side(*(after(terms, marker) for terms in (out_terms, attn_terms))),
        block_out,
    )
    sum_out, sum_attn = after(summed[:, :units], other), summed[:, units:]
    sum_qkv = sum_attn[:, : 3 * local].reshape(-1, 3, local)
    sum_proj = sum_attn[:, 3 * local : 4 * local].T
    quarter, eighth = local // dp_count, units // dp_count
    if pair_first:
        extra = sum_attn[:, 4 * local :]
        plain = extra[:6, :part_rows]
        ours = plain[:2] + lax.ppermute(plain[:2], "mp", [(0, 1), (1, 0)])
        plain = jnp.concatenate([ours, plain[2:]])
        sum_qv = jnp.stack([extra[8, :quarter], extra[16, :quarter]])
        sum_bin = extra[24, :eighth]
    else:
        counts = jnp.where((core == 0) | (jnp.arange(6) < 2), 1.0, 0.0).astype(F32)
        wide = (short[:6] * counts[:, None]).reshape(6, dp_count, 1, part_rows)
        wide = jnp.broadcast_to(wide, (6, dp_count, 2, part_rows)).transpose(1, 2, 0, 3)
        to_half = (jnp.arange(2) == core)[None, :, None]

        def half_terms(vectors):
            terms = vectors.reshape(vectors.shape[0], dp_count, -1).transpose(1, 0, 2)
            return jnp.where(to_half, terms.reshape(dp_count, 1, -1), 0.0)

        short = jnp.concatenate(
            [
                wide.reshape(dp_count, 2, -1),
                half_terms(short[6].reshape(2, local)),
                half_terms(short[7:].reshape(1, units)),
            ],
            axis=-1,
        ).reshape(2 * dp_count, -1)
        short = jnp.sum(lax.all_to_all(short, both, 0, 0, tiled=True), axis=0)
        plain = short[: 6 * part_rows].reshape(6, part_rows)
        sum_qv = short[6 * part_rows : 6 * part_rows + 2 * quarter].reshape(2, -1)
        sum_bin = short[6 * part_rows + 2 * quarter :]
    return (
        block_out,
        grad_tokens,
        plain[0],
        plain[1],
        sum_qkv,
        sum_qv,
        sum_proj,
        plain[4],
        plain[2],
        plain[3],
        sum_in,
        sum_bin,
        sum_out.T,
        plain[5],
    )


def solution(mesh):
    return jax.shard_map(
        shards,
        mesh=mesh,
        in_specs=(
            P("dp", None),
            P("dp"),
            P(),
            P("dp", None),
            P(),
            P(),
            P(None, None, "mp"),
            P(None, "mp"),
            P("mp", None),
            P(),
            P(),
            P(),
            P(None, "mp"),
            P("mp"),
            P("mp", None),
            P(),
            P("dp", None),
        ),
        out_specs=(
            P("dp", None),
            P("dp", None),
            P("dp"),
            P("dp"),
            P("dp", None, "mp"),
            P(None, ("mp", "dp")),
            P("mp", "dp"),
            P("dp"),
            P("dp"),
            P("dp"),
            P("dp", "mp"),
            P(("mp", "dp")),
            P("mp", "dp"),
            P("dp"),
        ),
        check_vma=False,
    )
```

```python
import functools

import jax
import jax.numpy as jnp
from jax import lax
from jax.experimental import pallas as pl
from jax.experimental.pallas import tpu as pltpu
from jax.sharding import PartitionSpec as P

HEAD_DIM = 64
NORM_EPS = 1e-06
NEG_FILL = -1e30
SCORE_SCALE = HEAD_DIM ** (-0.5)
MAX_CLIP = 256
LANES = 128
F32 = jnp.float32
BF16 = jnp.bfloat16
MIB = 1 << 20
SMALL = pl.CostEstimate(flops=1 << 20, bytes_accessed=1 << 20, transcendentals=0)


def nn(left, right):
    return lax.dot_general(left, right, (((1,), (0,)), ((), ())), preferred_element_type=F32)


def nt(left, right):
    return lax.dot_general(left, right, (((1,), (1,)), ((), ())), preferred_element_type=F32)


def vmem():
    return pl.BlockSpec(memory_space=pltpu.VMEM)


def hbm():
    return pl.BlockSpec(memory_space=pltpu.HBM)


def anywhere():
    return pl.BlockSpec(memory_space=pl.ANY)


def smem():
    return pl.BlockSpec(memory_space=pltpu.SMEM)


def params(mib):
    return pltpu.CompilerParams(vmem_limit_bytes=mib * MIB)


def shape(dims, dtype):
    return jax.ShapeDtypeStruct(dims, dtype)


def row_stats(vector):
    mean = jnp.mean(vector, axis=-1, keepdims=True)
    centred = vector - mean
    spread = jnp.mean(centred * centred, axis=-1, keepdims=True)
    return centred, lax.rsqrt(spread + NORM_EPS)


def on_lanes(column):
    return jnp.broadcast_to(column, (column.shape[0], LANES))


def wide_rsqrt(inv, here, width):
    return jnp.concatenate([inv[here, :]] * (width // LANES), axis=1)


def row_sum(block):
    return jnp.sum(block, axis=0, keepdims=True)


def fold_rows(block):
    rows, width = block.shape
    return jnp.sum(block.reshape(rows // 8, 8, width), axis=0)


def pick_kernel(index, source, *refs):
    picked = refs[-1]

    def move(i, carry):
        picked[i] = source[index[i]]
        return carry

    lax.fori_loop(0, picked.shape[0], move, 0, unroll=4)


def pick(source, index, *after):
    dims = index.shape + source.shape[1:]
    return pl.pallas_call(
        pick_kernel,
        out_shape=shape(dims, source.dtype),
        in_specs=[smem(), vmem()] + [hbm()] * len(after),
        out_specs=vmem(),
        compiler_params=params(16),
        cost_estimate=SMALL,
        name="pick",
    )(index, source, *after)


def move(source, target, sem):
    return pltpu.make_async_copy(source, target, sem)


PARTS = 4


def part_move(pairs, sems, c, first=0):
    moves = []
    for n, (source, target) in enumerate(pairs):
        count = source.shape[0] // PARTS
        here = pl.ds(pl.multiple_of(c * count, count), count)
        moves.append(move(source.at[here, :], target.at[here, :], sems.at[first + n, c]))
    return moves


def start_parts(pairs, sems):
    for c in range(PARTS):
        start_all(part_move(pairs, sems, c))


def row_parts(rows, blk, wait, body):
    steps = rows // PARTS // blk

    def part(c, carry):
        wait(c)

        def step(i, carry):
            body(pl.multiple_of((c * steps + i) * blk, blk))
            return carry

        return lax.fori_loop(0, steps, step, carry, unroll=4)

    lax.fori_loop(0, PARTS, part, 0)


def start_all(moves):
    for one in moves:
        one.start()


def wait_all(moves):
    for one in moves:
        one.wait()


def interleave(*streams):
    order = sorted(
        ((n + 0.5) / len(stream), which, n)
        for which, stream in enumerate(streams)
        for n in range(len(stream))
    )
    for _, which, n in order:
        streams[which][n]()


def spread_clips(seg_row, seg_b):
    for i in range(seg_b.shape[0] // LANES):
        here = pl.ds(i * LANES, LANES)
        seg_b[here, :] = jnp.broadcast_to(seg_row[:, here], (LANES, LANES)).T


def key_window(j, rows):
    window = min(rows, LANES + 2 * MAX_CLIP)
    here = pl.ds(pl.multiple_of(j * LANES, LANES), LANES)
    first = pl.multiple_of(jnp.clip(j * LANES - MAX_CLIP, 0, rows - window), LANES)
    return here, pl.ds(first, window)


def set_bias(bias, seg_b, seg_row, here, keys):
    filled = jnp.where(seg_b[keys, :] == seg_row[:, here], 0.0, NEG_FILL)
    bias[:, pl.ds(0, LANES)] = filled
    bias[:, pl.ds(LANES, LANES)] = filled


def two_heads(block):
    lane = lax.broadcasted_iota(jnp.int32, block.shape, 1)
    return jnp.concatenate(
        [block * (lane // HEAD_DIM == e).astype(BF16) for e in range(2)], axis=0
    )


def attention_kernel(
    blend, flags, seg_row, vecs, biases, tok, own, oth, w3, wp, *refs
):
    mixed, n1, normed, inv, q, k, v, att, part, lse = refs[-32:-22]
    (
        tok_v, own_v, oth_v, w3_v, wp_v, mixed_v, n1_v, q_v, k_v, v_v, att_v, part_v,
        vt, att_t, seg_b, bias, ones, normed_v, inv_v, in_sems, half_sems, out_sems,
    ) = refs[-22:]
    rows, width = tok.shape
    local = wp.shape[0]
    half_rows = rows // 2
    ratio = blend[0]
    blk = 32
    big = 256

    loads = [
        move(source, target, in_sems.at[n])
        for n, (source, target) in enumerate([(tok, tok_v), (w3, w3_v), (wp, wp_v)])
    ]
    halves = [(own, own_v), (oth, oth_v)]
    loads[0].start()
    start_parts(halves, half_sems)
    start_all(loads[1:])
    early = [
        move(source, target, out_sems.at[n])
        for n, (source, target) in enumerate(
            [
                (mixed_v, mixed), (n1_v, n1), (normed_v, normed), (inv_v, inv),
                (q_v, q), (k_v, k), (v_v, v),
            ]
        )
    ]
    ones[...] = jnp.ones_like(ones)
    spread_clips(seg_row, seg_b)

    loads[0].wait()
    for n, src, half in ((0, own_v, flags[0]), (1, oth_v, 1 - flags[0])):

        def mix(low, src=src, half=half):
            here = pl.ds(pl.multiple_of(half * half_rows + low, blk), blk)
            there = pl.ds(low, blk)
            mine, other = tok_v[here, :].astype(F32), src[there, :].astype(F32)
            blended = ratio * mine + (1.0 - ratio) * other
            mixed_v[here, :] = blended
            centred, scale = row_stats(blended)
            inv_v[here, :] = on_lanes(scale)
            plain = centred * scale
            normed_v[here, :] = plain.astype(BF16)
            n1_v[here, :] = (plain * vecs[0:1, :] + vecs[1:2, :]).astype(BF16)

        row_parts(
            half_rows, blk, lambda c, n=n: wait_all(part_move([halves[n]], half_sems, c, n)), mix
        )
    start_all(early[:4])

    loads[1].wait()
    for i in range(rows // big):
        here = pl.ds(i * big, big)
        rows_in = n1_v[here, :]
        queries = (nn(rows_in, w3_v[0]) + biases[0:1, :local]).astype(BF16).astype(F32)
        q_v[here, :] = (queries * SCORE_SCALE).astype(BF16)
        k_v[here, :] = nn(rows_in, w3_v[1]).astype(BF16)
        values = (nn(rows_in, w3_v[2]) + biases[0:1, local:]).astype(BF16)
        v_v[here, :] = values
        vt[:, here] = values.T
    start_all(early[4:])

    def attend(j, carry):
        here, keys = key_window(j, rows)
        set_bias(bias, seg_b, seg_row, here, keys)
        for p in range(local // LANES):
            pair = pl.ds(p * LANES, LANES)
            scores = nt(k_v[keys, pair], two_heads(q_v[here, pair])) + bias[...]
            top = jnp.max(scores, axis=0, keepdims=True)
            grown = jnp.exp(scores - top).astype(BF16)
            total = nn(ones[...], grown)[:1]
            out = (nn(vt[pair, keys], grown) / total).astype(BF16)
            logs = top + jnp.log(total)
            for e in range(2):
                lanes = slice(e * LANES, e * LANES + LANES)
                head = slice(e * HEAD_DIM, e * HEAD_DIM + HEAD_DIM)
                att_t[pl.ds(p * LANES + e * HEAD_DIM, HEAD_DIM), here] = out[head, lanes]
                lse[pl.ds(2 * p + e, 1), here] = logs[:, lanes]
        return carry

    lax.fori_loop(0, rows // LANES, attend, 0)

    loads[2].wait()
    last = []
    for i in range(rows // big):
        here = pl.ds(i * big, big)
        block = att_t[:, here].T
        att_v[here, :] = block
        part_v[here, :] = nn(block, wp_v[...]).astype(BF16)
        last.append(move(part_v.at[here, :], part.at[here, :], out_sems.at[8 + i]))
        last[-1].start()
    last.append(move(att_v, att, out_sems.at[7]))
    last[-1].start()
    wait_all(early + last)


def attention(blend, flags, segment, vecs, biases, tok, own, oth, w3, wp, *before):
    rows, width = tok.shape
    local = wp.shape[0]
    window = min(rows, LANES + 2 * MAX_CLIP)
    thin = shape((rows, local), BF16)
    tall = shape((rows, width), BF16)
    return pl.pallas_call(
        attention_kernel,
        out_shape=(
            shape((rows, width), F32), tall, tall, shape((rows, LANES), F32),
            thin, thin, thin, thin, tall, shape((local // HEAD_DIM, rows), F32),
        ),
        in_specs=[smem(), smem()] + [vmem()] * 3 + [anywhere()] * 3 + [hbm()] * (2 + len(before)),
        out_specs=[hbm()] * 9 + [vmem()],
        scratch_shapes=[
            pltpu.VMEM((rows, width), BF16),
            pltpu.VMEM((rows // 2, width), BF16),
            pltpu.VMEM((rows // 2, width), BF16),
            pltpu.VMEM(w3.shape, BF16),
            pltpu.VMEM(wp.shape, BF16),
            pltpu.VMEM((rows, width), F32),
            pltpu.VMEM((rows, width), BF16),
            pltpu.VMEM((rows, local), BF16),
            pltpu.VMEM((rows, local), BF16),
            pltpu.VMEM((rows, local), BF16),
            pltpu.VMEM((rows, local), BF16),
            pltpu.VMEM((rows, width), BF16),
            pltpu.VMEM((local, rows), BF16),
            pltpu.VMEM((local, rows), BF16),
            pltpu.VMEM((rows, LANES), F32),
            pltpu.VMEM((window, 2 * LANES), F32),
            pltpu.VMEM((16, window), BF16),
            pltpu.VMEM((rows, width), BF16),
            pltpu.VMEM((rows, LANES), F32),
            pltpu.SemaphoreType.DMA((3,)),
            pltpu.SemaphoreType.DMA((2, PARTS)),
            pltpu.SemaphoreType.DMA((8 + rows // 256,)),
        ],
        compiler_params=params(60),
        cost_estimate=SMALL,
        name="attention",
    )(
        blend, flags, segment, vecs, biases, tok, own, oth, w3, wp, *before,
    )


ERFC_SLOPE = 0.47
ERFC_COEFFS = (
    0.2663094668265691,
    0.2480096137831850,
    0.3362712657560771,
    -0.1262288063821733,
    0.6076790117752645,
    -0.4204702410368928,
    0.0884296765518492,
)


def gelu_parts(pre):
    bell = jnp.exp(pre * pre * -0.5)
    t = 1.0 / (1.0 + jnp.abs(pre) * (ERFC_SLOPE * 0.5**0.5))
    poly = 0.5 * ERFC_COEFFS[-1]
    for coeff in ERFC_COEFFS[-2::-1]:
        poly = poly * t + 0.5 * coeff
    tail = poly * t * bell
    cdf = jnp.where(pre >= 0, 1.0 - tail, tail)
    return pre * cdf, cdf + pre * bell * 0.3989422804014327


def turn_into(target, source, blocks):
    rows = source.shape[0]
    big = 256
    for i in range(rows // big):
        here = pl.ds(i * big, big)
        turned = source[here, :].T
        for start, place, count in blocks:
            target[pl.ds(place, count), here] = turned[start : start + count]


def lead_blocks(width, lead_rows):
    runs = width // lead_rows
    return [
        (run * lead_rows, ((run % 2) * (runs // 2) + run // 2) * lead_rows, lead_rows)
        for run in range(runs)
    ]


def feed_kernel(
    in_rows, out_rows, flags, vecs, biases, mixed, p_own, p_oth, cot, cot_t,
    w_in, w_out, w_out_one, w_out_two,
    hidden, part, gn_part, in_keep, in_send, out_keep, out_send, normed, inv, g_bin, g_bout,
    mixed_v, own_v, oth_v, cot_v, cot_tv, w_in_v, w_out_v, n2, n2_t, act, gp,
    g_in, g_out, normed_v, inv_v, in_sems, turn_sems, weight_sems, out_sems, grad_sems,
):
    rows, width = mixed.shape
    units = w_in.shape[1]
    blk = 32
    big = 256
    sub = 16
    home = flags[1] == 1
    across = flags[2]
    kept_out = jnp.where(home, flags[0], 1 - flags[0]) if in_rows != out_rows else across
    sides = (across, kept_out)

    loads = [(mixed, mixed_v), (p_own, own_v), (p_oth, oth_v), (cot, cot_v)]
    start_parts(loads, in_sems)

    weights = [move(w_in, w_in_v, weight_sems.at[0])]
    weights[0].start()
    half = w_out.shape[0] // 2
    for n, (got, place) in enumerate([(w_out_one, across), (w_out_two, 1 - across)]):
        spot = pl.ds(pl.multiple_of(place * half, half), half)
        sem = weight_sems.at[1 + n]
        weights.append(move(w_out.at[spot, :], w_out_v.at[spot, :], sem))

        @pl.when(home)
        def _(spot=spot, sem=sem):
            move(w_out.at[spot, :], w_out_v.at[spot, :], sem).start()

        @pl.when(jnp.logical_not(home))
        def _(got=got, spot=spot, sem=sem):
            move(got, w_out_v.at[spot, :], sem).start()

    turns = [
        move(cot_t.at[pl.ds(start, count), :], cot_tv.at[pl.ds(place, count), :], turn_sems.at[n])
        for n, (start, place, count) in enumerate(lead_blocks(width, out_rows))
    ]
    start_all(turns)

    g_bout[...] = jnp.zeros_like(g_bout)

    def norm(low):
        here = pl.ds(low, blk)
        attn = own_v[here, :].astype(F32) + oth_v[here, :].astype(F32)
        total = mixed_v[here, :] + attn + vecs[4:5, :]
        mixed_v[here, :] = total
        centred, scale = row_stats(total)
        inv_v[here, :] = on_lanes(scale)
        plain = centred * scale
        normed_v[here, :] = plain.astype(BF16)
        n2[here, :] = (plain * vecs[2:3, :] + vecs[3:4, :]).astype(BF16)
        g_bout[...] += fold_rows(cot_v[here, :].astype(F32))

    row_parts(rows, blk, lambda c: wait_all(part_move(loads, in_sems, c)), norm)
    stores = [
        move(source, target, out_sems.at[0, n])
        for n, (source, target) in enumerate(
            [(mixed_v, hidden), (normed_v, normed), (inv_v, inv)]
        )
    ]
    start_all(stores)
    turn_into(n2_t, n2, lead_blocks(width, in_rows))
    wait_all(weights)

    g_bin[...] = jnp.zeros_like(g_bin)

    def row_block(i):
        here = pl.ds(pl.multiple_of(i * big, big), big)
        for j in range(units // width):
            cols = pl.ds(j * width, width)
            pre_all = nn(n2[here, :], w_in_v[:, cols])
            grad_all = nt(cot_v[here, :], w_out_v[cols, :])
            sums = jnp.zeros((8, width), F32)
            for s in range(big // sub):
                rng = slice(s * sub, s * sub + sub)
                value, slope = gelu_parts(pre_all[rng] + biases[1 + j : 2 + j, :])
                grad = grad_all[rng] * slope
                sums += fold_rows(grad)
                spot = pl.ds(pl.multiple_of(i * big + s * sub, sub), sub)
                act[spot, cols] = value.astype(BF16)
                gp[spot, cols] = grad.astype(BF16)
            g_bin[:, cols] += sums
        oth_v[here, :] = nt(gp[here, :], w_in_v[...]).astype(BF16)
        own_v[here, :] = nn(act[here, :], w_out_v[...]).astype(BF16)
        for n, (source, target) in enumerate([(oth_v, gn_part), (own_v, part)]):
            move(source.at[here, :], target.at[here, :], out_sems.at[1 + n, i]).start()

    def two_blocks(i, carry):
        row_block(2 * i)
        row_block(2 * i + 1)
        return carry

    lax.fori_loop(0, rows // big // 2, two_blocks, 0)
    for i in range(rows // big):
        here = pl.ds(i * big, big)
        for n, (source, target) in enumerate([(oth_v, gn_part), (own_v, part)]):
            stores.append(move(source.at[here, :], target.at[here, :], out_sems.at[1 + n, i]))

    wait_all(turns)
    half = width // 2
    for n, (turned, right, buf, keep, send) in enumerate(
        [(n2_t, gp, g_in, in_keep, in_send), (cot_tv, act, g_out, out_keep, out_send)]
    ):
        for side in range(2):
            lines = pl.ds(side * half, half)
            for j in range(units // width):
                cols = pl.ds(j * width, width)
                buf[side, :, cols] = nn(turned[lines, :], right[:, cols]).astype(BF16)
        for m, (side, target) in enumerate([(1 - sides[n], send), (sides[n], keep)]):
            stores.append(move(buf.at[side], target, grad_sems.at[n, m]))
            stores[-1].start()
    wait_all(stores)


def feed(
    in_rows, out_rows, flags, vecs, biases, mixed, p_own, p_oth, cot, cot_t,
    w_in, w_out, w_out_one, w_out_two,
):
    rows, width = mixed.shape
    units = w_in.shape[1]
    tall = shape((rows, width), BF16)
    grad = shape((width // 2, units), BF16)
    return pl.pallas_call(
        functools.partial(feed_kernel, in_rows, out_rows),
        out_shape=(
            shape((rows, width), F32), tall, tall, grad, grad, grad, grad,
            tall, shape((rows, LANES), F32), shape((8, units), F32), shape((8, width), F32),
        ),
        in_specs=[smem()] + [vmem()] * 2 + [hbm()] * 2 + [anywhere()] + [hbm()] * 6,
        out_specs=[hbm()] * 9 + [vmem()] * 2,
        scratch_shapes=[
            pltpu.VMEM((rows, width), F32),
            pltpu.VMEM((rows, width), BF16),
            pltpu.VMEM((rows, width), BF16),
            pltpu.VMEM((rows, width), BF16),
            pltpu.VMEM((width, rows), BF16),
            pltpu.VMEM(w_in.shape, BF16),
            pltpu.VMEM(w_out.shape, BF16),
            pltpu.VMEM((rows, width), BF16),
            pltpu.VMEM((width, rows), BF16),
            pltpu.VMEM((rows, units), BF16),
            pltpu.VMEM((rows, units), BF16),
            pltpu.VMEM((2, width // 2, units), BF16),
            pltpu.VMEM((2, width // 2, units), BF16),
            pltpu.VMEM((rows, width), BF16),
            pltpu.VMEM((rows, LANES), F32),
            pltpu.SemaphoreType.DMA((4, PARTS)),
            pltpu.SemaphoreType.DMA((width // out_rows,)),
            pltpu.SemaphoreType.DMA((3,)),
            pltpu.SemaphoreType.DMA((3, rows // 256)),
            pltpu.SemaphoreType.DMA((2, 2)),
        ],
        compiler_params=params(60),
        cost_estimate=SMALL,
        name="feed",
    )(
        flags, vecs, biases, mixed, p_own, p_oth, cot, cot_t,
        w_in, w_out, w_out_one, w_out_two,
    )


def attention_back_kernel(
    lead_rows, part_rows, flags, vecs, seg_row, lse, g_bin, g_bout, g_own, g_oth, cot, normed, inv,
    wp, att, k, q, v, w3, n1, normed_one,
    gh, part, keep, send, short,
    gh_v, own_v, oth_v, cot_v, normed_v, inv_v, wp_v, att_v, k_v, q_v, v_v, w3_v, n1_v, one_v, low_v, part_v,
    sums, tails, d_out, kt, dq_t, dk, dv, delta, seg_b, bias, raw, raw_g, low_p, low_g, n1_t, gh_t, grad_v, out,
    in_sems, row_sems, out_sems, last_sems,
):
    rows, width = cot.shape
    local = wp.shape[0]
    blk = 32
    big = 256
    blocks = lead_blocks(width, lead_rows)
    kept_side = flags[2]
    row_loads = [(g_own, own_v), (g_oth, oth_v), (cot, cot_v), (normed, normed_v), (inv, inv_v)]
    start_parts(row_loads, row_sems)
    loads = [
        move(source, target, in_sems.at[n])
        for n, (source, target) in enumerate(
            [
                (wp, wp_v), (att, att_v), (k, k_v), (q, q_v), (v, v_v), (w3, w3_v), (n1, n1_v),
                (normed_one, one_v),
            ]
        )
    ]
    start_all(loads)
    sums[...] = jnp.zeros_like(sums)
    dk[...] = jnp.zeros_like(dk)
    dv[...] = jnp.zeros_like(dv)
    spread_clips(seg_row, seg_b)

    def norm(low):
        here = pl.ds(low, blk)
        grad = own_v[here, :].astype(F32) + oth_v[here, :].astype(F32)
        plain = normed_v[here, :].astype(F32)
        scaled = grad * vecs[2:3, :]
        mean_one = jnp.mean(scaled, axis=-1, keepdims=True)
        mean_two = jnp.mean(scaled * plain, axis=-1, keepdims=True)
        scale = wide_rsqrt(inv_v, here, width)
        back = cot_v[here, :].astype(F32) + scale * (scaled - mean_one - plain * mean_two)
        gh_v[here, :] = back
        low_v[here, :] = back.astype(BF16)
        sums[0] += fold_rows(grad * plain)
        sums[1] += fold_rows(grad)
        sums[2] += fold_rows(back)

    row_parts(rows, blk, lambda c: wait_all(part_move(row_loads, row_sems, c)), norm)
    stores = [move(gh_v, gh, out_sems.at[0])]
    stores[0].start()

    wait_all(loads[:3])
    heads = local // HEAD_DIM
    lane = lax.broadcasted_iota(jnp.int32, (delta.shape[0], local), 1)
    row = lax.broadcasted_iota(jnp.int32, (delta.shape[0], local), 0)
    of_head = (lane // HEAD_DIM == row).astype(BF16)

    def project(i, carry):
        here = pl.ds(pl.multiple_of(i * big, big), big)
        grad_out = nt(low_v[here, :], wp_v[...]).astype(BF16)
        d_out[here, :] = grad_out
        product = grad_out.astype(F32) * att_v[here, :].astype(F32)
        coarse = product.astype(BF16)
        fine = (product - coarse.astype(F32)).astype(BF16)
        delta[:, here] = nt(of_head, coarse) + nt(of_head, fine)
        kt[:, here] = k_v[here, :].T
        return carry

    lax.fori_loop(0, rows // big, project, 0)
    wait_all(loads[3:])

    pairs = heads // 2
    window = bias.shape[0]
    strip = 128
    strips = window // strip

    def attend(j, carry):
        here, keys = key_window(j, rows)
        first = pl.multiple_of(keys.start, LANES)
        set_bias(bias, seg_b, seg_row, here, keys)
        blocks_two = {}

        def two(p):
            if p not in blocks_two:
                pair = pl.ds(p * LANES, LANES)
                blocks_two[p] = (two_heads(q_v[here, pair]), two_heads(d_out[here, pair]))
            return blocks_two[p]

        def at_strip(n):
            return (
                pl.ds(pl.multiple_of(first + n * strip, strip), strip),
                pl.ds(n * strip, strip),
            )

        def products(p):
            pair = pl.ds(p * LANES, LANES)

            def scores(n):
                def run():
                    some, at = at_strip(n)
                    raw[p % 2, at, :] = nt(k_v[some, pair], two(p)[0])

                return run

            def grads(n):
                def run():
                    some, at = at_strip(n)
                    raw_g[p % 2, at, :] = nt(v_v[some, pair], two(p)[1])

                return run

            return [make(n) for n in range(strips) for make in (scores, grads)]

        def softmax_back(p):
            tops = jnp.concatenate([lse[pl.ds(2 * p + e, 1), here] for e in range(2)], axis=1)
            inner = jnp.concatenate([delta[pl.ds(2 * p + e, 1), here] for e in range(2)], axis=1)
            half = strip // 2

            def run_at(n):
                def run():
                    at = pl.ds(n * half, half)
                    probs = jnp.exp(raw[p % 2, at, :] + bias[at, :] - tops)
                    low_p[p % 2, at, :] = probs.astype(BF16)
                    low_g[p % 2, at, :] = (probs * (raw_g[p % 2, at, :] - inner)).astype(BF16)

                return run

            return [run_at(n) for n in range(2 * strips)]

        def sums_of(p):
            pair = pl.ds(p * LANES, LANES)

            def keys_of(n):
                def run():
                    some, at = at_strip(n)
                    dk[some, pair] += nn(low_g[p % 2, at, :], two(p)[0])

                return run

            def values_of(n):
                def run():
                    some, at = at_strip(n)
                    dv[some, pair] += nn(low_p[p % 2, at, :], two(p)[1])

                return run

            def queries():
                grad_q = nn(kt[pair, keys], low_g[p % 2]) * SCORE_SCALE
                for e in range(2):
                    lanes = slice(e * LANES, e * LANES + LANES)
                    head = slice(e * HEAD_DIM, e * HEAD_DIM + HEAD_DIM)
                    dq_t[pl.ds(p * LANES + e * HEAD_DIM, HEAD_DIM), here] = grad_q[head, lanes]

            return [make(n) for n in range(strips) for make in (keys_of, values_of)] + [queries]

        def turns():
            for target, source in ((n1_t, n1_v), (gh_t, low_v)):
                turned = source[here, :].T
                for start, place, count in blocks:
                    target[pl.ds(place, count), here] = turned[start : start + count]

        interleave(products(0), [turns])
        for p in range(pairs):
            matrix = (products(p + 1) if p + 1 < pairs else []) + (sums_of(p - 1) if p else [])
            interleave(softmax_back(p), matrix)
        interleave(sums_of(pairs - 1))
        return carry

    lax.fori_loop(0, rows // LANES, attend, 0)

    tails[...] = jnp.zeros_like(tails)

    def finish(i, carry):
        here = pl.ds(pl.multiple_of(i * big, big), big)
        grad_q, grad_k, grad_val = dq_t[:, here].T, dk[here, :], dv[here, :]
        tails[2, :, pl.ds(0, local)] += fold_rows(grad_q)
        tails[2, :, pl.ds(local, local)] += fold_rows(grad_val)
        lows = [grad.astype(BF16) for grad in (grad_q, grad_k, grad_val)]
        total = sum(nt(low, w3_v[n]) for n, low in enumerate(lows))
        part_v[here, :] = total.astype(BF16)
        tails[0] += fold_rows(total * one_v[here, :].astype(F32))
        tails[1] += fold_rows(total)
        for n, low in enumerate(lows):
            grad_v[here, pl.ds(n * local, local)] = low
        move(part_v.at[here, :], part.at[here, :], last_sems.at[i]).start()
        return carry

    lax.fori_loop(0, rows // big, finish, 0, unroll=2)
    for i in range(rows // big):
        here = pl.ds(i * big, big)
        stores.append(move(part_v.at[here, :], part.at[here, :], last_sems.at[i]))
    units = g_bin.shape[1]
    listed = [tails[0], tails[1], sums[0], sums[1], sums[2], g_bout[...], tails[2]]
    listed += [g_bin[:, pl.ds(n, width)] for n in range(0, units, width)]
    half = width // 2
    listed = [row_sum(block) for block in listed]
    for n, block in enumerate(listed):
        short[pl.ds(n, 1), :] = block
    if part_rows:
        sources = [
            (jnp.concatenate(listed[:6] + [jnp.zeros((2, width), F32)], axis=0), part_rows),
            (jnp.broadcast_to(listed[6][:, :local], (8, local)), local * part_rows // width),
            (jnp.broadcast_to(listed[6][:, local:], (8, local)), local * part_rows // width),
            (
                jnp.broadcast_to(jnp.concatenate(listed[7:], axis=1), (8, units)),
                units * part_rows // width,
            ),
        ]
        rest = jnp.zeros((part_rows - 8 * len(sources), LANES), F32)
        for start, place, count in blocks:
            for row in range(0, count, part_rows):
                d = (start + row) // part_rows
                parts = [
                    pltpu.roll(source, (source.shape[1] - d * size) % source.shape[1], 1)[:, :LANES]
                    for source, size in sources
                ]
                side, at = divmod(place + row, half)
                out[side, pl.ds(at, part_rows), pl.ds(4 * local, LANES)] = jnp.concatenate(
                    parts + [rest], axis=0
                ).astype(BF16)
    for side in range(2):
        lines = pl.ds(side * half, half)
        for n in range(3):
            cols = pl.ds(n * local, local)
            out[side, :, cols] = nn(n1_t[lines, :], grad_v[:, cols]).astype(BF16)
        out[side, :, pl.ds(3 * local, local)] = nn(gh_t[lines, :], att_v[...]).astype(BF16)
    for n, (side, target) in enumerate([(1 - kept_side, send), (kept_side, keep)]):
        stores.append(move(out.at[side], target, out_sems.at[1 + n]))
        stores[-1].start()
    wait_all(stores)


def attention_back(
    lead_rows, part_rows, flags, vecs, segment, lse, g_bin, g_bout, g_own, g_oth, cot, normed, inv,
    wp, att, k, q, v, w3, n1, normed_one,
):
    rows, width = cot.shape
    local = wp.shape[0]
    window = min(rows, LANES + 2 * MAX_CLIP)
    tall, thin = pltpu.VMEM((rows, width), BF16), pltpu.VMEM((rows, local), BF16)
    turned = pltpu.VMEM((width, rows), BF16)
    half = (width // 2, 4 * local + (LANES if part_rows else 0))
    return pl.pallas_call(
        functools.partial(attention_back_kernel, lead_rows, part_rows),
        out_shape=(
            shape((rows, width), F32),
            shape((rows, width), BF16),
            shape(half, BF16),
            shape(half, BF16),
            shape((7 + g_bin.shape[1] // width, width), F32),
        ),
        in_specs=[smem()] + [vmem()] * 5 + [hbm()] + [anywhere()] + [hbm()] * 11,
        out_specs=[hbm()] * 4 + [vmem()],
        scratch_shapes=[
            pltpu.VMEM((rows, width), F32),
            tall, tall, tall, tall,
            pltpu.VMEM((rows, LANES), F32),
            pltpu.VMEM(wp.shape, BF16),
            thin, thin, thin, thin,
            pltpu.VMEM(w3.shape, BF16),
            tall, tall, tall, tall,
            pltpu.VMEM((3, 8, width), F32),
            pltpu.VMEM((3, 8, width), F32),
            thin,
            pltpu.VMEM((local, rows), BF16),
            pltpu.VMEM((local, rows), F32),
            pltpu.VMEM((rows, local), F32),
            pltpu.VMEM((rows, local), F32),
            pltpu.VMEM((8, rows), F32),
            pltpu.VMEM((rows, LANES), F32),
            pltpu.VMEM((window, 2 * LANES), F32),
            pltpu.VMEM((2, window, 2 * LANES), F32),
            pltpu.VMEM((2, window, 2 * LANES), F32),
            pltpu.VMEM((2, window, 2 * LANES), BF16),
            pltpu.VMEM((2, window, 2 * LANES), BF16),
            turned, turned,
            pltpu.VMEM((rows, 3 * local), BF16),
            pltpu.VMEM((2,) + half, BF16),
            pltpu.SemaphoreType.DMA((8,)),
            pltpu.SemaphoreType.DMA((5, PARTS)),
            pltpu.SemaphoreType.DMA((3,)),
            pltpu.SemaphoreType.DMA((rows // 256,)),
        ],
        compiler_params=params(60),
        cost_estimate=SMALL,
        name="attention_back",
    )(
        flags, vecs, segment, lse, g_bin, g_bout, g_own, g_oth, cot, normed, inv,
        wp, att, k, q, v, w3, n1, normed_one,
    )


def mixed_back_kernel(blend, flags, vecs, gh, g_own, g_oth, normed, inv, outgoing, kept, *refs):
    gh_v, own_v, oth_v, normed_v, inv_v, leave_v, kept_v, in_sems, out_sems, leave_sems = refs
    ratio = blend[0]
    rows, width = gh.shape
    blk = 32
    piece = leave_v.shape[1]
    loads = [(gh, gh_v), (g_own, own_v), (g_oth, oth_v), (normed, normed_v), (inv, inv_v)]
    stores = [(kept_v, kept)]
    start_parts(loads, in_sems)

    def norm(low):
        here = pl.ds(low, blk)
        grad = own_v[here, :].astype(F32) + oth_v[here, :].astype(F32)
        plain = normed_v[here, :].astype(F32)
        scaled = grad * vecs[0:1, :]
        mean_one = jnp.mean(scaled, axis=-1, keepdims=True)
        mean_two = jnp.mean(scaled * plain, axis=-1, keepdims=True)
        scale = wide_rsqrt(inv_v, here, width)
        back = gh_v[here, :] + scale * (scaled - mean_one - plain * mean_two)
        leave = ((1.0 - ratio) * back).astype(BF16)
        leave_v[pl.ds(low // piece, blk // piece)] = leave.reshape(blk // piece, piece, width)
        kept_v[here, :] = (ratio * back).astype(BF16)

    row_parts(rows, blk, lambda c: wait_all(part_move(loads, in_sems, c)), norm)
    start_parts(stores, out_sems)
    if len(outgoing.shape) == 3:
        leaves = [move(leave_v, outgoing, leave_sems.at[0])]
    else:
        count = outgoing.shape[0]
        leaves = [
            move(
                leave_v.at[pl.ds(pl.multiple_of((2 * m + flags[0]) * count, count), count)],
                outgoing.at[:, m],
                leave_sems.at[m],
            )
            for m in range(2)
        ]
    start_all(leaves)
    for c in range(PARTS):
        wait_all(part_move(stores, out_sems, c))
    wait_all(leaves)


def mixed_back(piece, ordered, blend, flags, vecs, gh, g_own, g_oth, normed, inv):
    rows, width = gh.shape
    tall = pltpu.VMEM((rows, width), BF16)
    runs = rows // piece
    dims = (runs // 4, 2, piece, width) if ordered else (runs, piece, width)
    return pl.pallas_call(
        mixed_back_kernel,
        out_shape=(shape(dims, BF16), shape((rows, width), BF16)),
        in_specs=[smem(), smem(), vmem()] + [hbm()] * 2 + [anywhere()] + [hbm()] * 2,
        out_specs=[hbm(), hbm()],
        scratch_shapes=[
            pltpu.VMEM((rows, width), F32),
            tall, tall, tall, pltpu.VMEM((rows, LANES), F32),
            pltpu.VMEM((runs, piece, width), BF16),
            tall,
            pltpu.SemaphoreType.DMA((5, PARTS)),
            pltpu.SemaphoreType.DMA((1, PARTS)),
            pltpu.SemaphoreType.DMA((2,)),
        ],
        compiler_params=params(60),
        cost_estimate=SMALL,
        name="mixed_back",
    )(blend, flags, vecs, gh, g_own, g_oth, normed, inv)


def shards(
    tokens,
    mix_blend,
    partner,
    clip_ids,
    gain_one,
    shift_one,
    qkv_weight,
    qv_bias,
    proj_weight,
    proj_bias,
    gain_two,
    shift_two,
    in_weight,
    in_bias,
    out_weight,
    out_bias,
    cotangent,
):
    rows, width = tokens.shape
    dp_count = lax.axis_size("dp")
    both = ("dp", "mp")
    bits = dp_count.bit_length() - 1
    seq = lax.axis_index("dp")
    mp = lax.axis_index("mp")
    core = lax.rem(seq, 2)
    home = core == mp
    all_dp = range(dp_count)

    def joint(d, m):
        return 2 * d + m

    core_swap = [(d, d ^ 1) for d in all_dp]
    home_to_pair = [(joint(d, d & 1), joint(d, 1 - (d & 1))) for d in all_dp]
    pair_to_home = [(joint(d, 1 - (d & 1)), joint(d, d & 1)) for d in all_dp]
    weight_move = home_to_pair + [
        (joint(d, 1 - (d & 1)), joint(d ^ 1, 1 - (d & 1))) for d in all_dp
    ]

    def swap(value):
        return lax.ppermute(value, "dp", core_swap)

    def chip_value(value):
        return jnp.where(home, value, swap(value))

    def after(value, *others):
        return lax.optimization_barrier((value,) + others)[0]

    def half_weight(value):
        return lax.ppermute(value, both, weight_move)

    part_rows = width // dp_count
    lead = min(n for n in range(1, bits) if (part_rows << n) % 16 == 0)
    lead_rows = part_rows << lead
    across = lax.rem(seq >> lead, 2)
    flags = jnp.stack([core, home.astype(jnp.int32), across]).astype(jnp.int32)

    def taken(value, index, axis):
        return lax.dynamic_index_in_dim(value, index, axis, keepdims=False)

    seq_small = chip_value(jnp.concatenate([mix_blend, clip_ids[0].astype(F32)]))
    blend, segment = seq_small[:1], seq_small[1:].reshape(1, rows)
    local = proj_weight.shape[0]
    units = in_bias.shape[0]
    half_small = jnp.concatenate([qv_bias.reshape(-1), in_bias])
    half_small = jnp.where(home, half_small, half_weight(half_small))
    biases = half_small.reshape(-1, width)
    vecs = jnp.stack([gain_one, shift_one, gain_two, shift_two, proj_bias])

    w3 = half_weight(qkv_weight.transpose(1, 0, 2))
    wp = half_weight(proj_weight)

    def two_way(value):
        halves = value.reshape(2, value.shape[0] // 2, value.shape[1])
        one = half_weight(taken(halves, across, 0))
        moves = [(joint(d, 1 - (d & 1)), joint(d ^ (1 << lead), 1 - (d & 1))) for d in all_dp]
        return value, one, lax.ppermute(one, both, moves)

    ids = jnp.arange(2 * dp_count, dtype=jnp.int32)
    piece = rows // (2 * 2 * dp_count)
    sent = tokens.reshape(2, dp_count, 2, piece, width)
    sent = lax.dynamic_index_in_dim(sent, mp, 2, keepdims=False)
    spread = lax.all_to_all(sent.transpose(1, 0, 2, 3), "dp", 0, 0, tiled=True)
    wanted = partner[(ids // 4) * 2 + ids % 2] * 2 + (ids // 2) % 2
    source_of = jnp.sum(
        jnp.where(partner[:, None] == ids[None, :dp_count], ids[:dp_count, None], 0),
        axis=0,
        dtype=jnp.int32,
    )
    source = source_of[ids // 2]
    wanted_back = (source // 2) * 4 + (ids % 2) * 2 + source % 2
    chosen = pick(spread.reshape(2 * dp_count, piece, width), wanted, w3, wp, half_small)
    partner_own = lax.all_to_all(chosen, both, 0, 0, tiled=True).reshape(rows // 2, width)
    w_out = two_way(out_weight)
    w_in = half_weight(after(in_weight, w_out[1]))

    tok = chip_value(tokens)
    cot = chip_value(cotangent)
    cot_t = cot.T
    partner_oth = swap(after(partner_own, tok, cot, vecs, segment, wanted_back))

    mixed, n1, normed_one, inv_one, q, k, v, att, attn_part, lse = attention(
        blend, flags, segment, vecs, biases, tok, partner_own, partner_oth, w3, wp, w_out[2], cot_t
    )
    pair_first = part_rows % 16 == 0
    fed = feed(
        lead_rows, part_rows if pair_first else lead_rows, flags, vecs, biases,
        mixed, attn_part, swap(attn_part), cot, cot_t, w_in, *w_out,
    )
    hidden, out_part, gn2_part, in_keep, in_send, out_keep, out_send = fed[:7]
    normed_two, inv_two, g_bin, g_bout = fed[7:]
    gn2_oth = swap(gn2_part)

    high, mid = dp_count >> (lead + 1), 1 << (lead - 1)
    pair_and_core = pair_to_home + [(joint(d, d & 1), joint(d ^ 1, d & 1)) for d in all_dp]
    pair_diagonal = [(joint(d, 1 - (d & 1)), joint(d ^ 1, d & 1)) for d in all_dp]

    def total(*terms):
        return sum(term.astype(F32) for term in terms)

    def send_across(value):
        return lax.ppermute(value, "dp", [(d, d ^ (1 << lead)) for d in all_dp])

    def send_pair(value):
        value = value.reshape(high, mid, 2, part_rows, -1)
        one = lax.ppermute(taken(value, jnp.where(home, 1 - core, core), 2), both, pair_and_core)
        two = lax.ppermute(taken(value, 1 - core, 2), both, pair_diagonal)
        held = taken(value, core, 2)
        return jnp.where(home, held, jnp.zeros_like(held)), one, two

    def far(value, *others):
        for shift, left in ((1, mid), (lead + 1, high)):
            while left > 1:
                radix = min(4, left)
                left //= radix
                value = value.reshape((-1, left, radix) + value.shape[-2:]).astype(BF16)
                spot = lax.rem(seq >> shift, radix)
                got = [
                    lax.ppermute(
                        taken(value, spot ^ flip, 2),
                        "dp",
                        [(d, d ^ (flip << shift)) for d in all_dp],
                    )
                    for flip in range(1, radix)
                ]
                value = total(taken(value, spot, 2), *after(got, *others))
                shift += radix.bit_length() - 1
        return value.reshape(value.shape[-2:])

    def send_first(keep, send):
        if not pair_first:
            return [keep, send_across(send)]
        one = lax.ppermute(send, both, pair_and_core)
        two = lax.ppermute(keep, both, pair_diagonal)
        return [jnp.where(home, keep, jnp.zeros_like(keep)), one, two]

    def send_second(value):
        if not pair_first:
            return send_pair(value) + (value,)
        value = value.reshape(high, 2, mid, part_rows, -1)
        away = taken(value, 1 - across, 1)
        return taken(value, across, 1), send_across(away), away

    in_got = send_across(in_send)
    out_first = send_first(out_keep, out_send)
    gh, gn1_part, attn_keep, attn_send, short = attention_back(
        lead_rows, part_rows if pair_first else 0, flags, vecs, segment, lse, g_bin, g_bout,
        gn2_part, gn2_oth, cot, normed_two, inv_two, wp, att, k, q, v, w3, n1, normed_one,
    )
    gn1_oth = swap(after(gn1_part, in_got, *out_first))
    attn_first = [attn_keep, send_across(attn_send)]
    in_terms = send_pair(total(in_keep, in_got).astype(BF16))
    ordered = piece % 16 == 0
    outgoing, kept = mixed_back(
        piece if ordered else 16, ordered, blend, flags, vecs, gh, gn1_part, gn1_oth, normed_one, inv_one
    )

    if ordered:
        leaving = outgoing.reshape(2 * dp_count, piece, width)
    else:
        leaving = taken(outgoing.reshape(2, 2, dp_count, piece, width), core, 1)
        leaving = leaving.transpose(1, 0, 2, 3).reshape(2 * dp_count, piece, width)
    back = lax.all_to_all(leaving, both, 0, 0, tiled=True)

    in_value = total(*after(in_terms, leaving)).astype(BF16)
    sum_in = far(in_value)
    out_oth = swap(after(out_part, leaving))
    out_value = total(*after(out_first, in_value)).astype(BF16)
    *out_terms, out_away = send_second(out_value)
    attn_value = total(*after(attn_first, out_away)).astype(BF16)
    attn_terms = send_pair(attn_value)
    block = hidden + (out_part.astype(F32) + after(out_oth, attn_value).astype(F32)) + out_bias
    block = block.astype(BF16)
    kept = kept.reshape(2, rows // 2, width)
    kept_got = half_weight(taken(kept, 1 - mp, 0))
    block_got = half_weight(block)

    def side_by_side(*groups):
        values = [total(*terms).reshape(high * mid, part_rows, -1) for terms in groups]
        return jnp.concatenate(values, axis=2).astype(BF16)

    returning = pick(back, wanted_back, attn_value, sum_in)
    returned = lax.all_to_all(
        returning.reshape(dp_count, 2, piece, width), "dp", 0, 0, tiled=True
    )
    returned = after(returned, kept_got)
    kept = jnp.where(home, taken(kept, mp, 0), kept_got)
    returned = returned.transpose(1, 0, 2, 3).reshape(rows // 2, width)
    mine = (kept.astype(F32) + returned.astype(F32)).astype(BF16)
    other = lax.ppermute(mine, "mp", [(0, 1), (1, 0)])
    block_out = jnp.where(home, block, after(block_got, mine))
    grad_tokens = jnp.where(
        jnp.arange(2)[:, None, None] == mp, mine[None], other[None]
    ).reshape(rows, width)

    marker = swap(returning[0, :, :LANES])
    summed = far(
        side_by_side(*(after(terms, marker) for terms in (out_terms, attn_terms))),
        block_out,
    )
    sum_out, sum_attn = after(summed[:, :units], other), summed[:, units:]
    sum_qkv = sum_attn[:, : 3 * local].reshape(-1, 3, local)
    sum_proj = sum_attn[:, 3 * local : 4 * local].T
    quarter, eighth = local // dp_count, units // dp_count
    if pair_first:
        extra = sum_attn[:, 4 * local :]
        plain = extra[:6, :part_rows]
        ours = plain[:2] + lax.ppermute(plain[:2], "mp", [(0, 1), (1, 0)])
        plain = jnp.concatenate([ours, plain[2:]])
        sum_qv = jnp.stack([extra[8, :quarter], extra[16, :quarter]])
        sum_bin = extra[24, :eighth]
    else:
        counts = jnp.where((core == 0) | (jnp.arange(6) < 2), 1.0, 0.0).astype(F32)
        wide = (short[:6] * counts[:, None]).reshape(6, dp_count, 1, part_rows)
        wide = jnp.broadcast_to(wide, (6, dp_count, 2, part_rows)).transpose(1, 2, 0, 3)
        to_half = (jnp.arange(2) == core)[None, :, None]

        def half_terms(vectors):
            terms = vectors.reshape(vectors.shape[0], dp_count, -1).transpose(1, 0, 2)
            return jnp.where(to_half, terms.reshape(dp_count, 1, -1), 0.0)

        short = jnp.concatenate(
            [
                wide.reshape(dp_count, 2, -1),
                half_terms(short[6].reshape(2, local)),
                half_terms(short[7:].reshape(1, units)),
            ],
            axis=-1,
        ).reshape(2 * dp_count, -1)
        short = jnp.sum(lax.all_to_all(short, both, 0, 0, tiled=True), axis=0)
        plain = short[: 6 * part_rows].reshape(6, part_rows)
        sum_qv = short[6 * part_rows : 6 * part_rows + 2 * quarter].reshape(2, -1)
        sum_bin = short[6 * part_rows + 2 * quarter :]
    return (
        block_out,
        grad_tokens,
        plain[0],
        plain[1],
        sum_qkv,
        sum_qv,
        sum_proj,
        plain[4],
        plain[2],
        plain[3],
        sum_in,
        sum_bin,
        sum_out.T,
        plain[5],
    )


def solution(mesh):
    return jax.shard_map(
        shards,
        mesh=mesh,
        in_specs=(
            P("dp", None),
            P("dp"),
            P(),
            P("dp", None),
            P(),
            P(),
            P(None, None, "mp"),
            P(None, "mp"),
            P("mp", None),
            P(),
            P(),
            P(),
            P(None, "mp"),
            P("mp"),
            P("mp", None),
            P(),
            P("dp", None),
        ),
        out_specs=(
            P("dp", None),
            P("dp", None),
            P("dp"),
            P("dp"),
            P("dp", None, "mp"),
            P(None, ("mp", "dp")),
            P("mp", "dp"),
            P("dp"),
            P("dp"),
            P("dp"),
            P("dp", "mp"),
            P(("mp", "dp")),
            P("mp", "dp"),
            P("dp"),
        ),
        check_vma=False,
    )
```
